128 devices in a mesh: seq: 8 (over z_lo, y), fsdp: 16 (over z_hi, x, core).
Axes of the slice: x: 4, y: 4, z: 4 (z_hi: 2, z_lo: 2; z = z_hi * 2 + z_lo), core: 2. Of those that a mesh axis runs over, the one named last changes fastest.
Arguments:
- layer_input: bfloat16 [16, 1024, 2048], P('fsdp', 'seq'), may hold values from -6 to 6
- positions: int32 [16, 1024], P('fsdp', 'seq'), may hold values from 0 to 1023, as said below
- attn_gain: float32 [2048], P('fsdp'), may hold values from 0.1 to 1.9
- w_query: bfloat16 [2048, 2048], P('fsdp'), may hold values from -0.125 to 0.125
- w_key: bfloat16 [2048, 256], P('fsdp'), may hold values from -0.125 to 0.125
- w_value: bfloat16 [2048, 256], P('fsdp'), may hold values from -0.125 to 0.125
- w_output: bfloat16 [2048, 2048], P('fsdp'), may hold values from -3 to 3
- mlp_gain: float32 [2048], P('fsdp'), may hold values from 0.1 to 1.9
- w_gate: bfloat16 [2048, 5632], P('fsdp'), may hold values from -0.125 to 0.125
- w_up: bfloat16 [2048, 5632], P('fsdp'), may hold values from -0.125 to 0.125
- w_down: bfloat16 [5632, 2048], P('fsdp'), may hold values from -0.109375 to 0.109375
- out_grad: bfloat16 [16, 1024, 2048], P('fsdp', 'seq'), may hold values from -6 to 6
Outputs:
- layer_output: bfloat16 [16, 1024, 2048], P('fsdp', 'seq')
- input_grad: bfloat16 [16, 1024, 2048], P('fsdp', 'seq')
- attn_gain_grad: float32 [2048], P('fsdp')
- w_query_grad: float32 [2048, 2048], P('fsdp')
- w_key_grad: float32 [2048, 256], P('fsdp')
- w_value_grad: float32 [2048, 256], P('fsdp')
- w_output_grad: float32 [2048, 2048], P('fsdp')
- mlp_gain_grad: float32 [2048], P('fsdp')
- w_gate_grad: float32 [2048, 5632], P('fsdp')
- w_up_grad: float32 [2048, 5632], P('fsdp')
- w_down_grad: float32 [5632, 2048], P('fsdp')
The draws below stay inside these ranges and needn't reach their ends.
Inputs may be any that keep to these rules, and one draw needn't show every extreme that they name: In each sequence the positions rise by one from token to token and fall back to 0 at some tokens; each sequence's first token has position 0; in one sequence they never fall back and run from 0 to 1023.
All inputs are finite; a program needn't handle non-finite values.
Results may differ from the reference program's by a relative error of at most 0.04.
Values may be sent and summed in bfloat16 or wider, within the bound.
No kernel may reach another device: no remote copies, remote signals or barrier semaphores. Data moves between devices by JAX's collectives and lax.ppermute only.
A program may use at most 320 MiB of HBM per device.

```python
import jax
import jax.numpy as jnp
from jax import lax

D = 2048
H = 32
KV = 4
HD = 64
FF = 5632
LEN = 1024
SEQS = 16
N_SEQ = 8


def draw_positions(key, part):
    key = jax.random.fold_in(key, 7)
    break_key, pick_key = jax.random.split(key)
    breaks_at = jax.random.randint(break_key, (SEQS, LEN), 0, max(4, LEN // 4)) == 0
    unbroken = jax.random.randint(pick_key, (), 0, SEQS)
    seq_ids = jnp.arange(SEQS, dtype=jnp.int32)[:, None]
    breaks_at = jnp.logical_and(breaks_at, seq_ids != unbroken)
    places_all = jnp.broadcast_to(jnp.arange(LEN, dtype=jnp.int32), (SEQS, LEN))
    anchor = lax.cummax(jnp.where(breaks_at, places_all, 0), axis=1)
    return (places_all - anchor).astype(jnp.int32)


def steps_of(stream_key, extent, cuts, low, top_value):
    loudness, own = 1.0, jax.random.fold_in(stream_key, 6)
    for axis_at, blocks in cuts:
        steps = jnp.exp(jax.random.uniform(jax.random.fold_in(own, axis_at), (blocks,), jnp.float32, low / len(cuts), top_value / len(cuts)))
        loudness = loudness * jnp.repeat(steps, extent[axis_at] // blocks).reshape([-1 if axis == axis_at else 1 for axis in range(len(extent))])
    return loudness


def noise(rng, extent, scale, reach, cuts=(), held_as=jnp.bfloat16):
    values = jax.random.normal(rng, extent, jnp.float32) * scale
    if len(cuts) > 0:
        values = steps_of(rng, extent, cuts, -0.22, 0.18) * values
    return jnp.clip(values, min=-reach, max=reach).astype(held_as)


def setup_inputs(seed: int = 0) -> dict:
    key_of = jax.random.split(jax.random.key(seed), 13)
    layer_input = noise(key_of[0], (SEQS, LEN, D), 1.0, 6.0, ((0, 16), (1, 8)))
    positions = draw_positions(jax.random.fold_in(key_of[12], 71), 0)
    attn_gain = jnp.clip(1.0 + 0.18 * jax.random.normal(key_of[2], (D,), jnp.float32), 0.1, 1.9)
    w_query = noise(key_of[3], (D, H * HD), D ** -0.5, 0.125, ((0, 16),))
    w_key = noise(key_of[4], (D, KV * HD), D ** -0.5, 0.125, ((0, 16),))
    w_value = noise(key_of[5], (D, KV * HD), D ** -0.5, 0.125, ((0, 16),))
    w_output = noise(key_of[6], (H * HD, D), (max(1, D * 2 // LEN)) ** -0.5, 3.0, ((0, 16),))
    mlp_gain = jnp.clip(1.0 + 0.18 * jax.random.normal(key_of[7], (D,), jnp.float32), 0.1, 1.9)
    w_gate = noise(key_of[8], (D, FF), D ** -0.5, 0.125, ((0, 16),))
    w_up = noise(key_of[9], (D, FF), D ** -0.5, 0.125, ((0, 16),))
    w_down = noise(key_of[10], (FF, D), (FF // 2) ** -0.5, 0.109375, ((0, 16),))
    out_grad = noise(key_of[11], (SEQS, LEN, D), 1.0, 6.0, ((0, 16), (1, 8)))
    return {"layer_input": layer_input, "positions": positions, "attn_gain": attn_gain, "w_query": w_query, "w_key": w_key, "w_value": w_value, "w_output": w_output, "mlp_gain": mlp_gain, "w_gate": w_gate, "w_up": w_up, "w_down": w_down, "out_grad": out_grad}


@jax.custom_vjp
def low(v):
    return lax.optimization_barrier(v.astype(jnp.bfloat16)).astype(jnp.float32)

@jax.custom_vjp
def low_back(v):
    return v

def low_keep(v):
    return (low(v), None)

def low_pass(kept, grad):
    return (grad,)

def back_keep(v):
    return (v, None)

def back_low(kept, grad):
    return (low(grad),)
low.defvjp(low_keep, low_pass)
low_back.defvjp(back_keep, back_low)
eps = 1e-05
theta = 10000.0
highest = lax.Precision.HIGHEST

def product(left, right):
    return jnp.dot(left, right, precision=highest)

def rms_scale(values):
    return lax.rsqrt(lax.optimization_barrier(jnp.mean(values * values, axis=-1, keepdims=True)) + eps)

def rotate(values, cosine, sine_part):
    half_dim = values.shape[-1] // 2
    turned = jnp.concatenate([-values[..., half_dim:], values[..., :half_dim]], axis=-1)
    return values * cosine + turned * sine_part

def rope_tables(places):
    frequency = theta ** (-jnp.arange(0, HD, 2).astype(jnp.float32) / HD)
    angles = places.astype(jnp.float32)[..., None] * frequency
    angles = jnp.concatenate([angles, angles], axis=-1)
    return (jnp.cos(angles)[..., None, :], jnp.sin(angles)[..., None, :])

def attend_block(query_part, key_grid, value_grid, first_row):
    scores = jnp.einsum('qcgd,kcd->cgqk', query_part, key_grid, precision=highest)
    scores = low_back(scores) * HD ** (-0.5)
    rows_at = first_row + jnp.arange(query_part.shape[0]).astype(jnp.int32)
    cols_at = jnp.arange(key_grid.shape[0]).astype(jnp.int32)
    scores = jnp.where(rows_at[:, None] >= cols_at[None, :], scores, -1e+30)
    row_top = lax.optimization_barrier(jnp.max(scores, axis=-1, keepdims=True))
    weights = jnp.exp(scores - row_top)
    probs = low(weights / lax.optimization_barrier(jnp.sum(weights, axis=-1, keepdims=True)))
    mixed_rows = jnp.einsum('cgqk,kcd->qcgd', probs, value_grid, precision=highest)
    return mixed_rows.reshape(query_part.shape[0], -1)

def attend(query_grid, key_grid, value_grid):
    length = query_grid.shape[0]
    block_rows = min(512, length)
    blocks_q = query_grid.reshape((length // block_rows, block_rows) + query_grid.shape[1:])
    firsts = (jnp.arange(length // block_rows) * block_rows).astype(jnp.int32)

    def one_block(block_pair):
        return attend_block(block_pair[0], key_grid, value_grid, block_pair[1])
    mixed_all = lax.map(jax.checkpoint(one_block), (blocks_q, firsts))
    return mixed_all.reshape(length, -1)

def forward(inputs, places, attn_gain, w_query, w_key, w_value, w_output, mlp_gain, w_gate, w_up, w_down):
    leading = inputs.shape[:2]
    copies_all = max(KV, N_SEQ)
    repeat_by = copies_all // KV
    per_copy = H // copies_all
    normed = low(inputs * rms_scale(inputs) * attn_gain)
    cosine, sine_part = rope_tables(places)
    query_pre = low_back(product(normed, w_query)).reshape(leading + (H, HD))
    key_pre = low_back(product(normed, w_key)).reshape(leading + (KV, HD))
    queries = low_back(low(rotate(query_pre, cosine, sine_part)))
    key_rot = low(rotate(key_pre, cosine, sine_part))
    key_copies = low_back(jnp.repeat(key_rot, repeat_by, axis=2))
    value_low = low_back(low(product(normed, w_value))).reshape(leading + (KV, HD))
    value_copies = low_back(jnp.repeat(value_low, repeat_by, axis=2))
    query_grid = queries.reshape(leading + (copies_all, per_copy, HD))
    attended = jax.vmap(attend)(query_grid, key_copies, value_copies)
    mixed = low_back(low(attended))
    hidden = inputs + low_back(product(mixed, w_output))
    normed_two = low(hidden * rms_scale(hidden) * mlp_gain)
    gate_pre = low_back(product(normed_two, w_gate))
    upward = low_back(product(normed_two, w_up))
    activation = low(jax.nn.silu(gate_pre) * upward)
    return hidden + product(activation, w_down)

def reference(layer_input, positions, attn_gain, w_query, w_key, w_value, w_output, mlp_gain, w_gate, w_up, w_down, out_grad):
    params = (attn_gain.astype(jnp.float32), w_query.astype(jnp.float32), w_key.astype(jnp.float32), w_value.astype(jnp.float32), w_output.astype(jnp.float32), mlp_gain.astype(jnp.float32), w_gate.astype(jnp.float32), w_up.astype(jnp.float32), w_down.astype(jnp.float32))
    per_group = 1
    while per_group * 2 * LEN <= 4096 and SEQS % (per_group * 2) == 0:
        per_group = per_group * 2
    group_count = SEQS // per_group
    all_inputs = layer_input.astype(jnp.float32).reshape(group_count, per_group, LEN, D)
    all_places = positions.reshape(group_count, per_group, LEN)
    all_cotangent = out_grad.astype(jnp.float32).reshape(group_count, per_group, LEN, D)

    def one_group(totals, pieces):
        part_in, part_places, part_cot = pieces

        def run_layer(values, *weights):
            return forward(values, part_places, *weights)
        result, pullback = jax.vjp(run_layer, part_in, *params)
        gradients = pullback(part_cot)
        totals = tuple((total_now + grad_now for total_now, grad_now in zip(totals, gradients[1:])))
        return (totals, (result, gradients[0]))
    zero_grads = tuple((jnp.zeros_like(weight_now) for weight_now in params))
    totals, outputs = lax.scan(one_group, zero_grads, (all_inputs, all_places, all_cotangent))
    results, input_grads = outputs
    layer_output = results.reshape(SEQS, LEN, D).astype(jnp.bfloat16)
    input_grad = input_grads.reshape(SEQS, LEN, D).astype(jnp.bfloat16)
    return (layer_output, input_grad, totals[0], totals[1], totals[2], totals[3], totals[4], totals[5], totals[6], totals[7], totals[8])
```

```python
import jax
import jax.numpy as jnp
from jax import lax
from jax.sharding import Mesh
from jax.sharding import PartitionSpec as P

H = 32
KV = 4
HD = 64
D = 2048
FF = 5632
B = 128
HALF = 512
HEADS = 4
FFL = 704
PIECE = 88

eps = 1e-05
theta = 10000.0
F32 = jnp.float32
BF16 = jnp.bfloat16
AXES = ("zlo", "y", "zhi", "x", "core")
FSDP = ("zhi", "x", "core")
SEQ = ("zlo", "y")


def matmul(left, right):
    return jnp.dot(left, right, preferred_element_type=F32)


def times_transposed(left, right):
    return lax.dot_general(left, right, (((1,), (1,)), ((), ())), preferred_element_type=F32)


def outer_sum(left, right):
    return lax.dot_general(left, right, (((0,), (0,)), ((), ())), preferred_element_type=F32)


def shift(value, axis, by):
    size = lax.axis_size(axis)
    return lax.ppermute(value, axis, [(i, (i + by) % size) for i in range(size)])


def swap_core(value):
    return shift(value, "core", 1)


def ring_gather(block, axis):
    half = block.shape[0] // 2
    before = shift(block, axis, 1)
    after = shift(block, axis, -1)
    far_low = shift(before[:half], axis, 1)
    far_high = shift(after[half:], axis, -1)
    return block, after, jnp.concatenate([far_low, far_high], axis=0), before


def small_gather(block, axis):
    return block, shift(block, axis, -1), shift(block, axis, 2), shift(block, axis, 1)


def ring_scatter(parts, axis):
    half = parts[2].shape[0] // 2
    far = parts[2].astype(BF16)
    low = shift(far[:half], axis, 1)
    high = shift(far[half:], axis, -1)
    after = jnp.concatenate([parts[1][:half] + low.astype(F32), parts[1][half:]], axis=0)
    before = jnp.concatenate([parts[3][:half], parts[3][half:] + high.astype(F32)], axis=0)
    from_before = shift(after.astype(BF16), axis, 1)
    from_after = shift(before.astype(BF16), axis, -1)
    return parts[0] + from_before.astype(F32) + from_after.astype(F32)


def gather_tokens(block):
    own = jnp.concatenate(ring_gather(block, "y"), axis=0)
    return jnp.concatenate([own, swap_core(own)], axis=0)


def scatter_tokens(partial):
    other = swap_core(partial[HALF:].astype(BF16))
    total = partial[:HALF] + other.astype(F32)
    return ring_scatter([total[i * B : (i + 1) * B] for i in range(4)], "y")


def turn(values):
    first, second = values[..., : HD // 2], values[..., HD // 2 :]
    return jnp.concatenate([-second, first], axis=-1)


def turn_back(values):
    first, second = values[..., : HD // 2], values[..., HD // 2 :]
    return jnp.concatenate([second, -first], axis=-1)


def own_rows(rows_all, y, core, per):
    return lax.dynamic_slice_in_dim(rows_all, (2 * y + core) * per, per, 0)


def on_device(
    layer_input,
    positions,
    attn_gain,
    w_query,
    w_key,
    w_value,
    w_output,
    mlp_gain,
    w_gate,
    w_up,
    w_down,
    out_grad,
):
    zlo = lax.axis_index("zlo")
    y = lax.axis_index("y")
    core = lax.axis_index("core")

    x_low = layer_input[0]
    inputs = x_low.astype(F32)
    scale_one = lax.rsqrt(jnp.mean(inputs * inputs, axis=-1, keepdims=True) + eps)
    x_all = gather_tokens(x_low)
    meta = jnp.concatenate([positions.astype(F32), scale_one.reshape(1, B)], axis=0)
    meta_own = jnp.concatenate(small_gather(meta, "y"), axis=1)
    meta_all = jnp.concatenate([meta_own, swap_core(meta_own)], axis=1)
    scale_all = meta_all[1][:, None]
    frequency = theta ** (-jnp.arange(0, HD, 2).astype(F32) / HD)
    angles = meta_all[0][:, None] * frequency
    angles = jnp.concatenate([angles, angles], axis=-1)
    cosine, sine = jnp.cos(angles)[:, None, :], jnp.sin(angles)[:, None, :]

    qkv_rows = jnp.concatenate([w_query, w_key, w_value], axis=1).astype(F32) * attn_gain[:, None]
    qkv_rows = qkv_rows.astype(BF16).T

    def qkv_of(core_index):
        return jnp.concatenate(
            [
                own_rows(qkv_rows, y, core_index, HEADS * HD),
                lax.dynamic_slice_in_dim(qkv_rows, H * HD + y * HD, HD, 0),
                lax.dynamic_slice_in_dim(qkv_rows, (H + KV) * HD + y * HD, HD, 0),
            ],
            axis=0,
        )

    def both_blocks(mine, for_other):
        got = swap_core(for_other)
        return jnp.where(core == 0, jnp.stack([mine, got]), jnp.stack([got, mine]))

    def gather_blocks(pair):
        got = shift(pair, "zhi", 1)
        zhi = lax.axis_index("zhi")
        column = jnp.where(zhi == 0, jnp.stack([pair, got]), jnp.stack([got, pair]))
        ring = jnp.stack(ring_gather(column, "x"))
        ring = jnp.roll(ring, lax.axis_index("x"), axis=0)
        return ring.transpose(3, 1, 0, 2, 4).reshape(pair.shape[1], D)

    qkv_full = gather_blocks(both_blocks(qkv_of(core), qkv_of(1 - core)))
    o_rows = lax.all_to_all(
        w_output.reshape(B, 16, B).transpose(1, 0, 2), FSDP, 0, 0, tiled=True
    ).reshape(D, B)
    o_full = gather_blocks(
        both_blocks(own_rows(o_rows, y, core, HEADS * HD), own_rows(o_rows, y, 1 - core, HEADS * HD))
    )

    def hidden_rows(weight):
        return (weight.astype(F32) * mlp_gain[:, None]).astype(BF16).T

    picked = jnp.where(zlo == 0, w_gate, w_up)
    picked = hidden_rows(picked).reshape(8, 2, 4, PIECE, B)
    picked = lax.dynamic_index_in_dim(picked, y, 2, keepdims=False)
    mine = lax.dynamic_index_in_dim(picked, core, 1, keepdims=False).reshape(FFL, B)
    for_other = lax.dynamic_index_in_dim(picked, 1 - core, 1, keepdims=False).reshape(FFL, B)
    pair = both_blocks(mine, for_other).reshape(2 * FFL, B)
    down_piece = lax.dynamic_slice(w_down, (y * PIECE, zlo * (D // 2)), (PIECE, D // 2))
    down_piece = down_piece.reshape(PIECE, 8, B).transpose(1, 0, 2).reshape(FFL, B)
    ff_piece = jnp.concatenate([pair, down_piece], axis=0)
    ff_all = lax.all_gather(ff_piece, ("zlo", "zhi", "x"), axis=0, tiled=False)
    ff_all = ff_all.reshape(2, 8, 3 * FFL, B)

    def column_blocks(blocks):
        return blocks.reshape(8, 2, FFL, B).transpose(2, 0, 1, 3).reshape(FFL, D)

    gate_full = column_blocks(ff_all[0, :, : 2 * FFL])
    up_full = column_blocks(ff_all[1, :, : 2 * FFL])
    down_full = ff_all[:, :, 2 * FFL :].reshape(2, 8, 8, PIECE, B)
    down_full = down_full.transpose(1, 3, 0, 2, 4).reshape(FFL, D)

    pre = times_transposed(x_all, qkv_full) * scale_all
    query_pre = pre[:, : HEADS * HD].reshape(2 * HALF, HEADS, HD)
    key_pre = pre[:, HEADS * HD : (HEADS + 1) * HD].reshape(2 * HALF, 1, HD)
    query = (query_pre * cosine + turn(query_pre) * sine).astype(BF16)
    key = (key_pre * cosine + turn(key_pre) * sine).astype(BF16)
    value = pre[:, (HEADS + 1) * HD :].astype(BF16).reshape(2 * HALF, 1, HD)
    key_value = jnp.concatenate([key, value], axis=1).reshape(2, HALF, 2, HD)
    earlier = lax.ppermute(key_value, "zlo", [(0, 1)])
    kv_all = jnp.concatenate([earlier, key_value], axis=1)
    key_all, value_all = kv_all[:, :, 0], kv_all[:, :, 1]
    query = query.reshape(2, HALF, HEADS, HD)

    at = jnp.arange(HALF, dtype=jnp.int32)
    at = ((at // B + y) % 4) * B + at % B
    allowed = jnp.concatenate(
        [jnp.broadcast_to(zlo == 1, (HALF, HALF)), at[:, None] >= at[None, :]], axis=1
    )
    score_scale = HD ** (-0.5)

    def scores_of(query_part, key_part):
        scores = jnp.einsum("qhd,kd->hqk", query_part, key_part, preferred_element_type=F32)
        return jnp.where(allowed, scores * score_scale, -1e30)

    def attend(query_part, key_part, value_part):
        scores = scores_of(query_part, key_part)
        top = jnp.max(scores, axis=-1, keepdims=True)
        weights = jnp.exp(scores - top)
        total = jnp.sum(weights, axis=-1, keepdims=True)
        low = (weights / total).astype(BF16)
        mixed = jnp.einsum("hqk,kd->qhd", low, value_part, preferred_element_type=F32)
        return mixed.reshape(HALF, HEADS * HD).astype(BF16), top + jnp.log(total)

    mixed_parts = [attend(query[s], key_all[s], value_all[s]) for s in range(2)]
    mixed = jnp.concatenate([m for m, _ in mixed_parts], axis=0)

    hidden = inputs + scatter_tokens(matmul(mixed, o_full))
    scale_two = lax.rsqrt(jnp.mean(hidden * hidden, axis=-1, keepdims=True) + eps)
    normed_all = gather_tokens((hidden * scale_two).astype(BF16))
    grad_all = gather_tokens(out_grad[0])

    gate_pre = times_transposed(normed_all, gate_full)
    upward = times_transposed(normed_all, up_full)
    sigmoid = 1.0 / (1.0 + jnp.exp(-gate_pre))
    silu = gate_pre * sigmoid
    activation = (silu * upward).astype(BF16)
    grad_act = times_transposed(grad_all, down_full)
    grad_up = (grad_act * silu).astype(BF16)
    grad_gate = (grad_act * upward * (sigmoid * (1.0 + gate_pre * (1.0 - sigmoid)))).astype(BF16)
    grad_normed_two = scatter_tokens(matmul(grad_gate, gate_full) + matmul(grad_up, up_full))
    result = hidden + scatter_tokens(matmul(activation, down_full))

    gate_term = outer_sum(grad_gate, normed_all).astype(BF16)
    up_term = outer_sum(grad_up, normed_all).astype(BF16)
    down_term = outer_sum(activation, grad_all).astype(BF16)

    def blocks_of(term):
        return term.reshape(FFL, 8, 2, B).transpose(1, 2, 0, 3).reshape(8, 2 * FFL, B)

    ff_terms = jnp.stack([blocks_of(gate_term), blocks_of(up_term)])
    down_blocks = down_term.reshape(8, PIECE, 2, 8, B).transpose(2, 0, 3, 1, 4)
    ff_terms = jnp.concatenate([ff_terms, down_blocks.reshape(2, 8, FFL, B)], axis=2)
    ff_sum = lax.psum_scatter(
        ff_terms.reshape(16, 3 * FFL, B), ("zlo", "zhi", "x"), scatter_dimension=0, tiled=True
    ).reshape(3 * FFL, B)

    mean_two = jnp.mean(grad_normed_two * hidden, axis=-1, keepdims=True)
    grad_hidden = (
        out_grad[0].astype(F32)
        + scale_two * grad_normed_two
        - hidden * (scale_two * scale_two * scale_two) * mean_two
    )
    hidden_grad_all = gather_tokens(grad_hidden.astype(BF16))
    grad_mixed = times_transposed(hidden_grad_all, o_full).astype(BF16)
    output_term = outer_sum(mixed, hidden_grad_all).astype(BF16)
    grad_mixed = grad_mixed.reshape(2, HALF, HEADS, HD)

    def attend_back(query_part, key_part, value_part, grad_part, log_total):
        weights = jnp.exp(scores_of(query_part, key_part) - log_total)
        low = weights.astype(BF16)
        grad_value = jnp.einsum("hqk,qhd->kd", low, grad_part, preferred_element_type=F32)
        grad_weights = jnp.einsum("qhd,kd->hqk", grad_part, value_part, preferred_element_type=F32)
        delta = jnp.sum(weights * grad_weights, axis=-1, keepdims=True)
        grad_scores = (weights * (grad_weights - delta) * score_scale).astype(BF16)
        grad_query = jnp.einsum("hqk,kd->qhd", grad_scores, key_part, preferred_element_type=F32)
        grad_key = jnp.einsum("hqk,qhd->kd", grad_scores, query_part, preferred_element_type=F32)
        return grad_query, grad_key, grad_value

    backs = [
        attend_back(query[s], key_all[s], value_all[s], grad_mixed[s], mixed_parts[s][1])
        for s in range(2)
    ]
    grad_query = jnp.concatenate([b[0] for b in backs], axis=0)
    grad_kv = jnp.stack([jnp.stack([b[1], b[2]], axis=1) for b in backs])
    later = lax.ppermute(grad_kv[:, :HALF].astype(BF16), "zlo", [(1, 0)])
    grad_kv = (grad_kv[:, HALF:] + later.astype(F32)).reshape(2 * HALF, 2, HD)
    grad_key, grad_value = grad_kv[:, :1], grad_kv[:, 1]
    grad_query = grad_query * cosine + turn_back(grad_query * sine)
    grad_key = grad_key * cosine + turn_back(grad_key * sine)
    grad_pre = jnp.concatenate(
        [grad_query.reshape(2 * HALF, HEADS * HD), grad_key.reshape(2 * HALF, HD), grad_value], axis=1
    )
    grad_normed = scatter_tokens(matmul(grad_pre.astype(BF16), qkv_full))
    mean_one = jnp.mean(grad_normed * inputs, axis=-1, keepdims=True)
    input_grad = (
        grad_hidden
        + scale_one * grad_normed
        - inputs * (scale_one * scale_one * scale_one) * mean_one
    )
    qkv_term = outer_sum((grad_pre * scale_all).astype(BF16), x_all).astype(BF16)

    attn_terms = jnp.concatenate([qkv_term, output_term], axis=0)
    rows = attn_terms.shape[0]
    attn_terms = attn_terms.reshape(2, rows // 2, 8, 2, B).transpose(0, 2, 3, 1, 4)
    attn_sum = lax.psum_scatter(
        attn_terms.reshape(16, rows, B), ("zlo", "zhi", "x"), scatter_dimension=0, tiled=True
    ).reshape(2, rows // 2, B)

    def own_block(pair):
        keep = lax.dynamic_index_in_dim(pair, core, 0, keepdims=False)
        got = swap_core(lax.dynamic_index_in_dim(pair, 1 - core, 0, keepdims=False))
        return jnp.where(core == 0, jnp.stack([keep, got]), jnp.stack([got, keep]))

    def both_zlo(part):
        got = shift(part, "zlo", 1)
        return jnp.where(zlo == 0, jnp.stack([part, got]), jnp.stack([got, part]))

    def all_y(part):
        ring = jnp.stack(ring_gather(part, "y"))
        return jnp.roll(ring, y, axis=0)

    attn_own = both_zlo(own_block(attn_sum))
    attn_own = attn_own.transpose(1, 0, 2, 3).reshape(2, rows, B)
    attn_own = all_y(attn_own)
    query_grad = attn_own[:, :, : HEADS * HD].reshape(D, B).T.astype(F32)
    key_grad = jnp.sum(attn_own[:, :, HEADS * HD : (HEADS + 1) * HD].astype(F32), axis=1)
    key_grad = key_grad.reshape(KV * HD, B).T
    value_grad = jnp.sum(attn_own[:, :, (HEADS + 1) * HD : (HEADS + 2) * HD].astype(F32), axis=1)
    value_grad = value_grad.reshape(KV * HD, B).T
    output_rows = attn_own[:, :, (HEADS + 2) * HD :].reshape(16, B, B)
    output_grad = lax.all_to_all(output_rows, FSDP, 0, 0, tiled=True)
    output_grad = output_grad.transpose(1, 0, 2).reshape(B, D).astype(F32)

    gu_own = both_zlo(
        jnp.concatenate(
            [own_block(ff_sum[: 2 * FFL].reshape(2, FFL, B)).reshape(2 * FFL, B), ff_sum[2 * FFL :]], axis=0
        )
    )
    ff_own = all_y(gu_own)
    gate_up = ff_own[:, :, : 2 * FFL].reshape(4, 2, 2, 8, PIECE, B)
    gate_up = gate_up.transpose(1, 3, 2, 0, 4, 5).reshape(2, FF, B)
    gate_grad = gate_up[0].T.astype(F32)
    up_grad = gate_up[1].T.astype(F32)
    down_grad = ff_own[:, :, 2 * FFL :].reshape(4, 2, 8, PIECE, B)
    down_grad = down_grad.transpose(0, 3, 1, 2, 4).reshape(4 * PIECE, D).astype(F32)

    attn_gain_grad = (
        jnp.sum(query_grad * w_query.astype(F32), axis=1)
        + jnp.sum(key_grad * w_key.astype(F32), axis=1)
        + jnp.sum(value_grad * w_value.astype(F32), axis=1)
    )
    mlp_gain_grad = jnp.sum(gate_grad * w_gate.astype(F32) + up_grad * w_up.astype(F32), axis=1)
    one, two = attn_gain[:, None], mlp_gain[:, None]
    return (
        result.astype(BF16)[None],
        input_grad.astype(BF16)[None],
        attn_gain_grad,
        query_grad * one,
        key_grad * one,
        value_grad * one,
        output_grad,
        mlp_gain_grad,
        gate_grad * two,
        up_grad * two,
        down_grad,
    )


def solution(mesh):
    split = Mesh(mesh.devices.reshape(2, 4, 2, 4, 2), AXES)
    tokens = P(FSDP, SEQ, None)
    rows = P(FSDP, None)
    gain = P(FSDP)
    in_specs = (
        tokens, P(FSDP, SEQ), gain, rows, rows, rows, rows, gain, rows, rows, rows, tokens,
    )
    out_specs = (tokens, tokens, gain, rows, rows, rows, rows, gain, rows, rows, rows)
    return jax.shard_map(
        on_device, mesh=split, in_specs=in_specs, out_specs=out_specs, check_vma=False
    )
```

```python
import jax
import jax.numpy as jnp
from jax import lax
from jax.experimental import pallas as pl
from jax.experimental.pallas import tpu as pltpu
from jax.sharding import Mesh
from jax.sharding import PartitionSpec as P

H = 32
KV = 4
HD = 64
D = 2048
FF = 5632
B = 128
HALF = 512
HEADS = 4
FFL = 704
PIECE = 88

eps = 1e-05
theta = 10000.0
F32 = jnp.float32
BF16 = jnp.bfloat16
AXES = ("zlo", "y", "zhi", "x", "core")
FSDP = ("zhi", "x", "core")
SEQ = ("zlo", "y")


def matmul(left, right):
    return jnp.dot(left, right, preferred_element_type=F32)


def times_transposed(left, right):
    return lax.dot_general(left, right, (((1,), (1,)), ((), ())), preferred_element_type=F32)


def outer_sum(left, right):
    return lax.dot_general(left, right, (((0,), (0,)), ((), ())), preferred_element_type=F32)


def shift(value, axis, by):
    if axis == "z":
        at = [2 * (z % 2) + z // 2 for z in range(4)]
        return lax.ppermute(value, ("zlo", "zhi"), [(at[z], at[(z + by) % 4]) for z in range(4)])
    size = lax.axis_size(axis)
    return lax.ppermute(value, axis, [(i, (i + by) % size) for i in range(size)])


def swap_core(value):
    return shift(value, "core", 1)


def ring_gather(block, axis):
    half = block.shape[0] // 2
    before = shift(block, axis, 1)
    after = shift(block, axis, -1)
    far_low = shift(before[:half], axis, 1)
    far_high = shift(after[half:], axis, -1)
    return block, after, jnp.concatenate([far_low, far_high], axis=0), before


def small_gather(block, axis):
    return block, shift(block, axis, -1), shift(block, axis, 2), shift(block, axis, 1)


def ring_scatter(parts, axis):
    half = parts[2].shape[0] // 2
    low = shift(parts[2][:half], axis, 1)
    high = shift(parts[2][half:], axis, -1)
    after = jnp.concatenate([add(parts[1][:half], low).astype(BF16), parts[1][half:]], axis=0)
    before = jnp.concatenate([parts[3][:half], add(parts[3][half:], high).astype(BF16)], axis=0)
    from_before = shift(after, axis, 1)
    from_after = shift(before, axis, -1)
    return add(parts[0], from_before) + from_after.astype(F32)


def tie(*values):
    return lax.optimization_barrier(values)


def ring_pieces(block, axis):
    half = block.shape[0] // 2
    before = shift(block, axis, 1)
    after = shift(block, axis, -1)
    return block, after, shift(before[:half], axis, 1), shift(after[half:], axis, -1), before


def add(left, right):
    return left.astype(F32) + right.astype(F32)


def along_y(value):
    pairs = []
    for i in range(4):
        pairs.append((2 * i, 2 * ((i + 1) % 4)))
        pairs.append((2 * i + 1, 2 * ((i + 3) % 4) + 1))
    return lax.ppermute(value, ("y", "core"), pairs)


def send_half(got):
    core = lax.axis_index("core")
    return lax.dynamic_slice_in_dim(got, core * (B // 2), B // 2, 1)


def gather_tokens(block):
    pair = jnp.stack([block, swap_core(block)])
    got = along_y(pair)
    far = along_y(send_half(got))
    return (pair, got, swap_core(got), far, swap_core(far))


FLIPPED = (0, 0, 1, 0, 1)
LENGTHS = (B, B, B, B // 2, B // 2)


def scatter_tokens(parts):
    core = lax.axis_index("core")
    first, behind, ahead, far, far_other = parts
    far = add(far, swap_core(far_other)[::-1]).astype(BF16)
    low = along_y(far)
    ahead = add(ahead, swap_core(behind)[::-1]).astype(BF16)
    own = add(first[0], swap_core(first[1]))
    mine = lax.dynamic_slice_in_dim(ahead, core * (B // 2), B // 2, 1)
    ahead = lax.dynamic_update_slice_in_dim(ahead, add(mine, low).astype(BF16), core * (B // 2), 1)
    got = along_y(ahead)
    return own + got[0].astype(F32) + swap_core(got[1]).astype(F32)


def put_tokens(refs, rows_ref, sems, start):
    copies = []
    row = 0
    for s in range(2):
        for ref, flip, length in zip(refs, FLIPPED, LENGTHS):
            copies.append(
                pltpu.make_async_copy(
                    ref.at[s ^ flip], rows_ref.at[pl.ds(row, length)], sems.at[start + len(copies)]
                )
            )
            row += length
    return copies


TILE = 256
VMEM_LIMIT = 56 * 2**20
ANYWHERE = pl.BlockSpec(memory_space=pl.ANY)


def params(*kinds):
    return pltpu.CompilerParams(dimension_semantics=kinds or None, vmem_limit_bytes=VMEM_LIMIT)


def cost(flops, megabytes):
    return pl.CostEstimate(flops=flops, bytes_accessed=int(megabytes * 2**20), transcendentals=0)


def shaped(*shape, kind=BF16):
    return jax.ShapeDtypeStruct(shape, kind)


PART_SPECS = [pl.BlockSpec((1, n, D), lambda i, *_: (i // 2, 0, 0)) for n in LENGTHS]
PART_SHAPES = [jax.ShapeDtypeStruct((2, n, D), BF16) for n in LENGTHS]


def put_parts(step, tile, refs):
    @pl.when(step % 2 == 0)
    def _():
        refs[0][0] = tile[:B]
        refs[1][0] = tile[B:]

    @pl.when(step % 2 == 1)
    def _():
        refs[2][0] = tile[:B]
        refs[3][0] = tile[B : B + B // 2]
        refs[4][0] = tile[B + B // 2 :]


def turned(values):
    lane = lax.broadcasted_iota(jnp.int32, values.shape, 1) % HD
    return jnp.where(lane < HD // 2, -pltpu.roll(values, 2 * HD - HD // 2, 1), pltpu.roll(values, HD // 2, 1))


def lane_block(zhi, x, core):
    return pl.ds(pl.multiple_of((zhi * 8 + x * 2 + core) * B, B), B)


def put_columns(place, refs, into, sems, start):
    copies = []
    for ref, by, first in zip(refs, (0, 1, 2, 2, 3), (0, 0, 0, 1, 0)):
        for i in range(ref.shape[0]):
            for core in range(2):
                lanes = lane_block(first + i, (place[3] + by) % 4, core)
                copies.append(
                    pltpu.make_async_copy(ref.at[i, core], into.at[:, lanes], sems.at[start + len(copies)])
                )
    return copies


def prepare_qkv_kernel(place, q_mine, q_other, w_key, w_value, gain, mine_ref, other_ref, k_rows, v_rows):
    scale = gain[...]
    k_rows[...] = (w_key[...].astype(F32) * scale).T
    v_rows[...] = (w_value[...].astype(F32) * scale).T
    rows = pl.ds(pl.multiple_of(place[1] * HD, HD), HD)
    for source, out in ((q_mine, mine_ref), (q_other, other_ref)):
        out[: HEADS * HD] = (source[...].astype(F32) * scale).T.astype(BF16)
        out[HEADS * HD : (HEADS + 1) * HD] = k_rows[rows].astype(BF16)
        out[(HEADS + 1) * HD :] = v_rows[rows].astype(BF16)


QKV = (HEADS + 2) * HD


def prepare_qkv(place, w_query, w_key, w_value, gain):
    whole = lambda *shape: pl.BlockSpec(shape, lambda i, p: (0,) * len(shape))
    return pl.pallas_call(
        prepare_qkv_kernel,
        grid_spec=pltpu.PrefetchScalarGridSpec(
            num_scalar_prefetch=1,
            grid=(1,),
            in_specs=[
                pl.BlockSpec((B, HEADS * HD), lambda i, p: (0, 2 * p[1] + p[2])),
                pl.BlockSpec((B, HEADS * HD), lambda i, p: (0, 2 * p[1] + 1 - p[2])),
                whole(B, KV * HD), whole(B, KV * HD), whole(B, 1),
            ],
            out_specs=[whole(QKV, B), whole(QKV, B)],
            scratch_shapes=[pltpu.VMEM((KV * HD, B), F32), pltpu.VMEM((KV * HD, B), F32)],
        ),
        out_shape=[shaped(QKV, B), shaped(QKV, B)],
        compiler_params=params("arbitrary"),
        cost_estimate=cost(0, 1),
        name="prepare_qkv",
    )(place, w_query, w_query, w_key, w_value, gain)


def prepare_ff_kernel(place, w_gate, w_up, w_down, gain, mine_ref, other_ref, down_ref, picked, rows, down_rows, sems):
    zlo, y, core = place[0], place[1], place[2]
    down = pltpu.make_async_copy(
        w_down.at[:, pl.ds(pl.multiple_of(zlo * (D // 2), D // 2), D // 2)], down_rows, sems.at[1]
    )
    down.start()

    @pl.when(zlo == 0)
    def _():
        copy = pltpu.make_async_copy(w_gate, picked, sems.at[0])
        copy.start()
        copy.wait()

    @pl.when(zlo == 1)
    def _():
        copy = pltpu.make_async_copy(w_up, picked, sems.at[0])
        copy.start()
        copy.wait()

    scale = gain[...]
    for i in range(FF // B):
        rows[i * B : (i + 1) * B] = (picked[:, i * B : (i + 1) * B].astype(F32) * scale).T
    for which, out in ((core, mine_ref), (1 - core, other_ref)):
        slabs = []
        for zx in range(8):
            at = pl.multiple_of(zx * 2 * 4 * PIECE + which * 4 * PIECE + y * PIECE, 8)
            slabs.append(rows[pl.ds(at, PIECE)])
        out[...] = jnp.concatenate(slabs, axis=0).astype(BF16)
    down.wait()
    for t in range(8):
        rows[t * 4 * PIECE : (t + 1) * 4 * PIECE] = down_rows[:, t * B : (t + 1) * B].astype(F32)
    slabs = [rows[pl.ds(pl.multiple_of(t * 4 * PIECE + y * PIECE, 8), PIECE)] for t in range(8)]
    down_ref[...] = jnp.concatenate(slabs, axis=0).astype(BF16)


def prepare_ff(place, w_gate, w_up, w_down, gain):
    return pl.pallas_call(
        prepare_ff_kernel,
        grid_spec=pltpu.PrefetchScalarGridSpec(
            num_scalar_prefetch=1,
            grid=(1,),
            in_specs=[ANYWHERE, ANYWHERE, ANYWHERE, pl.BlockSpec((B, 1), lambda i, p: (0, 0))],
            out_specs=[pl.BlockSpec((FFL, B), lambda i, p: (0, 0))] * 3,
            scratch_shapes=[
                pltpu.VMEM((B, FF), BF16),
                pltpu.VMEM((FF, B), F32),
                pltpu.VMEM((4 * PIECE, D // 2), BF16),
                pltpu.SemaphoreType.DMA((2,)),
            ],
        ),
        out_shape=[shaped(FFL, B)] * 3,
        compiler_params=params("arbitrary"),
        cost_estimate=cost(0, 6),
        name="prepare_ff",
    )(place, w_gate, w_up, w_down, gain)


def project_qkv_kernel(*refs):
    place, x_refs, w_refs = refs[0], refs[1:6], refs[6:11]
    scale_ref, cosine_ref, sine_ref, query_ref, kv_ref, w_out, rows, weights, sems = refs[11:]
    step = pl.program_id(0)
    tokens = put_tokens(x_refs, rows, sems, 0)
    columns = put_columns(place, w_refs, weights, sems, 10)
    back = pltpu.make_async_copy(weights, w_out, sems.at[26])

    @pl.when(step == 0)
    def _():
        for copy in columns + tokens:
            copy.start()
        for copy in columns:
            copy.wait()
        back.start()
        for copy in tokens:
            copy.wait()

    tile = rows[pl.ds(pl.multiple_of(step * TILE, TILE), TILE), :]
    pre = times_transposed(tile, weights[...]) * scale_ref[...]
    cosine, sine = cosine_ref[...], sine_ref[...]
    for i in range(2):
        part = pre[:, i * 2 * HD : (i + 1) * 2 * HD]
        part = (part * cosine + turned(part) * sine).astype(BF16) * HD ** (-0.5)
        query_ref[0, 2 * i] = part[:, :HD]
        query_ref[0, 2 * i + 1] = part[:, HD:]
    part = pre[:, HEADS * HD :]
    lane = lax.broadcasted_iota(jnp.int32, part.shape, 1)
    kv_ref[0] = jnp.where(lane < HD, part * cosine + turned(part) * sine, part).astype(BF16)

    @pl.when(step == 3)
    def _():
        back.wait()


def project_qkv(place, x_pieces, w_pieces, scale, cosine, sine):
    tile = lambda lanes: pl.BlockSpec((TILE, lanes), lambda i, p: (i, 0))
    return pl.pallas_call(
        project_qkv_kernel,
        grid_spec=pltpu.PrefetchScalarGridSpec(
            num_scalar_prefetch=1,
            grid=(4,),
            in_specs=[ANYWHERE] * 10 + [tile(1), tile(2 * HD), tile(2 * HD)],
            out_specs=[
                pl.BlockSpec((1, HEADS, TILE, HD), lambda i, p: (i // 2, 0, i % 2, 0)),
                pl.BlockSpec((1, TILE, 2 * HD), lambda i, p: (i // 2, i % 2, 0)),
                ANYWHERE,
            ],
            scratch_shapes=[
                pltpu.VMEM((2 * HALF, D), BF16),
                pltpu.VMEM((QKV, D), BF16),
                pltpu.SemaphoreType.DMA((27,)),
            ],
        ),
        out_shape=[shaped(2, HEADS, HALF, HD), shaped(2, HALF, 2 * HD), shaped(QKV, D)],
        compiler_params=params("arbitrary"),
        cost_estimate=cost(2 * 2 * HALF * QKV * D, 8),
        name="project_qkv",
    )(place, *x_pieces, *w_pieces, scale, cosine, sine)


def project_out_kernel(*refs):
    place, w_refs, left_ref = refs[0], refs[1:6], refs[6]
    parts, w_out, weights, sems = refs[7:12], refs[12], refs[13], refs[14]
    step = pl.program_id(0)
    columns = put_columns(place, w_refs, weights, sems, 0)
    back = pltpu.make_async_copy(weights, w_out, sems.at[16])

    @pl.when(step == 0)
    def _():
        for copy in columns:
            copy.start()
        for copy in columns:
            copy.wait()
        back.start()

    put_parts(step, matmul(left_ref[...], weights[...]).astype(BF16), parts)

    @pl.when(step == 3)
    def _():
        back.wait()


def project_out(place, w_pieces, mixed):
    return pl.pallas_call(
        project_out_kernel,
        grid_spec=pltpu.PrefetchScalarGridSpec(
            num_scalar_prefetch=1,
            grid=(4,),
            in_specs=[ANYWHERE] * 5 + [pl.BlockSpec((TILE, HEADS * HD), lambda i, p: (i, 0))],
            out_specs=PART_SPECS + [ANYWHERE],
            scratch_shapes=[pltpu.VMEM((HEADS * HD, D), BF16), pltpu.SemaphoreType.DMA((17,))],
        ),
        out_shape=PART_SHAPES + [shaped(HEADS * HD, D)],
        compiler_params=params("arbitrary"),
        cost_estimate=cost(2 * 2 * HALF * HEADS * HD * D, 7),
        name="project_out",
    )(place, *w_pieces, mixed)


def project_kernel(left_ref, weight_ref, *parts):
    put_parts(pl.program_id(0), matmul(left_ref[...], weight_ref[...]).astype(BF16), parts)


def project(left, weight):
    depth = left.shape[1]
    return pl.pallas_call(
        project_kernel,
        grid=(4,),
        in_specs=[pl.BlockSpec((TILE, depth), lambda i: (i, 0)), pl.BlockSpec((depth, D), lambda i: (0, 0))],
        out_specs=PART_SPECS,
        out_shape=PART_SHAPES,
        compiler_params=params("arbitrary"),
        cost_estimate=cost(2 * 2 * HALF * depth * D, 8),
        name="project",
    )(left, weight)


def grad_mixed_kernel(*refs):
    place, grad_refs, weight_ref, mixed_ref = refs[0], refs[1:6], refs[6], refs[7]
    grad_mixed_ref, term_ref, rows, sems = refs[8:]
    copies = put_tokens(grad_refs, rows, sems, 0)
    for copy in copies:
        copy.start()
    for copy in copies:
        copy.wait()
    for i in range(4):
        tile = rows[i * TILE : (i + 1) * TILE, :]
        grad_mixed_ref[i * TILE : (i + 1) * TILE, :] = times_transposed(tile, weight_ref[...]).astype(BF16)
    left = mixed_ref[...].astype(F32).T.astype(BF16)
    put_term(place, left, rows, term_ref)


def put_term(place, left, rows, term_ref):
    def one(zx, carry):
        lanes = pl.ds(pl.multiple_of(zx * 2 * B, 2 * B), 2 * B)
        term = matmul(left, rows[:, lanes]).astype(BF16)
        by = (zx % 4 + 4 - place[3]) % 4
        term_ref[by, zx // 4, 0] = term[:, :B]
        term_ref[by, zx // 4, 1] = term[:, B:]
        return carry

    lax.fori_loop(0, 8, one, 0)


def grad_of_mixed(place, grad_pieces, weight, mixed):
    whole = lambda *shape: pl.BlockSpec(shape, lambda i, p: (0,) * len(shape))
    rows = HEADS * HD
    return pl.pallas_call(
        grad_mixed_kernel,
        grid_spec=pltpu.PrefetchScalarGridSpec(
            num_scalar_prefetch=1,
            grid=(1,),
            in_specs=[ANYWHERE] * 5 + [whole(rows, D), whole(2 * HALF, rows)],
            out_specs=[whole(2 * HALF, rows), whole(4, 2, 2, rows, B)],
            scratch_shapes=[pltpu.VMEM((2 * HALF, D), BF16), pltpu.SemaphoreType.DMA((10,))],
        ),
        out_shape=[shaped(2 * HALF, rows), shaped(4, 2, 2, rows, B)],
        compiler_params=params("arbitrary"),
        cost_estimate=cost(4 * 2 * HALF * rows * D, 8),
        name="grad_of_mixed",
    )(place, *grad_pieces, weight, mixed)


def qkv_back_kernel(grad_q_ref, own_ref, later_ref, cosine_ref, sine_ref, scale_ref, weight_ref, *outs):
    parts, turned_ref = outs[:5], outs[5]
    cosine, sine = cosine_ref[...], sine_ref[...]
    lane = lax.broadcasted_iota(jnp.int32, cosine.shape, 1)
    pieces = []
    for i in range(2):
        part = grad_q_ref[0, :, i * 2 * HD : (i + 1) * 2 * HD]
        pieces.append(part * cosine - turned(part * sine))
    part = own_ref[0] + later_ref[0].astype(F32)
    pieces.append(jnp.where(lane < HD, part * cosine - turned(part * sine), part))
    grad_pre = jnp.concatenate(pieces, axis=1)
    put_parts(pl.program_id(0), matmul(grad_pre.astype(BF16), weight_ref[...]).astype(BF16), parts)
    turned_ref[...] = (grad_pre * scale_ref[...]).T.astype(BF16)


def qkv_back(grad_query, own, later, cosine, sine, scale, weight):
    tile = lambda lanes: pl.BlockSpec((TILE, lanes), lambda i: (i, 0))
    half = lambda lanes: pl.BlockSpec((1, TILE, lanes), lambda i: (i // 2, i % 2, 0))
    return pl.pallas_call(
        qkv_back_kernel,
        grid=(4,),
        in_specs=[
            half(HEADS * HD), half(2 * HD), half(2 * HD), tile(2 * HD), tile(2 * HD), tile(1),
            pl.BlockSpec((QKV, D), lambda i: (0, 0)),
        ],
        out_specs=PART_SPECS + [pl.BlockSpec((QKV, TILE), lambda i: (0, i))],
        out_shape=PART_SHAPES + [shaped(QKV, 2 * HALF)],
        compiler_params=params("arbitrary"),
        cost_estimate=cost(2 * 2 * HALF * QKV * D, 9),
        name="qkv_back",
    )(grad_query, own, later, cosine, sine, scale, weight)


def qkv_term_kernel(*refs):
    place, x_refs, left_ref, term_ref, rows, sems = refs[0], refs[1:6], refs[6], refs[7], refs[8], refs[9]
    copies = put_tokens(x_refs, rows, sems, 0)
    for copy in copies:
        copy.start()
    for copy in copies:
        copy.wait()
    put_term(place, left_ref[...], rows, term_ref)


def qkv_terms(place, x_pieces, left):
    whole = lambda *shape: pl.BlockSpec(shape, lambda i, p: (0,) * len(shape))
    return pl.pallas_call(
        qkv_term_kernel,
        grid_spec=pltpu.PrefetchScalarGridSpec(
            num_scalar_prefetch=1,
            grid=(1,),
            in_specs=[ANYWHERE] * 5 + [whole(QKV, 2 * HALF)],
            out_specs=whole(4, 2, 2, QKV, B),
            scratch_shapes=[pltpu.VMEM((2 * HALF, D), BF16), pltpu.SemaphoreType.DMA((10,))],
        ),
        out_shape=shaped(4, 2, 2, QKV, B),
        compiler_params=params("arbitrary"),
        cost_estimate=cost(2 * 2 * HALF * QKV * D, 7),
        name="qkv_terms",
    )(place, *x_pieces, left)


def token_places(at, y, core):
    step = 1 - 2 * core
    block = jnp.where(
        at < B, y, jnp.where(at < 2 * B, y + 4 - step, jnp.where(at < 3 * B, y + 4 + step, y + 2))
    )
    row = at % B
    row = jnp.where(at < 3 * B, row, (row + core * (B // 2)) % B)
    return (block % 4) * B + row


def set_bias(place_ref, bias_ref):
    zlo, y, core = place_ref[0], place_ref[1], place_ref[2]
    key_at = token_places(lax.broadcasted_iota(jnp.int32, (HALF, 1), 0), y, core)
    query_at = token_places(lax.broadcasted_iota(jnp.int32, (1, HALF), 1), y, core)
    bias_ref[:HALF, :] = jnp.broadcast_to(jnp.where(zlo == 1, 0.0, -1e30), (HALF, HALF))
    bias_ref[HALF:, :] = jnp.where(key_at <= query_at, 0.0, -1e30)


def attention_kernel(place_ref, query_ref, kv_ref, mixed_ref, log_ref, bias_ref):
    head = pl.program_id(1)

    @pl.when((pl.program_id(0) == 0) & (head == 0))
    def _():
        set_bias(place_ref, bias_ref)

    key, value = kv_ref[0, :, :HD], kv_ref[0, :, HD:]
    scores = times_transposed(key, query_ref[0, 0]) + bias_ref[...]
    top = jnp.max(scores, axis=0, keepdims=True)
    weights = jnp.exp(scores - top)
    total = jnp.sum(weights, axis=0, keepdims=True)
    low = (weights * (1.0 / total)).astype(BF16)
    mixed = outer_sum(value, low).T.astype(BF16)
    for i in range(HEADS):

        @pl.when(head == i)
        def _():
            mixed_ref[0, :, i * HD : (i + 1) * HD] = mixed

    log_ref[0, 0] = top + jnp.log(total)


def attention_back_kernel(
    place_ref, query_ref, kv_ref, grad_ref, log_ref, grad_query_ref, earlier_ref, own_ref, bias_ref, grad_one, total
):
    head = pl.program_id(1)

    @pl.when((pl.program_id(0) == 0) & (head == 0))
    def _():
        set_bias(place_ref, bias_ref)

    for i in range(HEADS):

        @pl.when(head == i)
        def _():
            grad_one[...] = grad_ref[0, :, i * HD : (i + 1) * HD]

    key, value = kv_ref[0, :, :HD], kv_ref[0, :, HD:]
    query, grad = query_ref[0, 0], grad_one[...]
    weights = jnp.exp(times_transposed(key, query) + bias_ref[...] - log_ref[0, 0])
    grad_weights = times_transposed(value, grad)
    delta = jnp.sum(weights * grad_weights, axis=0, keepdims=True)
    grad_scores = (weights * (grad_weights - delta)).astype(BF16)
    grad_query = outer_sum(key, grad_scores).T * HD ** (-0.5)
    for i in range(HEADS):

        @pl.when(head == i)
        def _():
            grad_query_ref[0, :, i * HD : (i + 1) * HD] = grad_query

    grads = jnp.concatenate([matmul(grad_scores, query), matmul(weights.astype(BF16), grad)], axis=1)

    @pl.when(head == 0)
    def _():
        total[...] = grads

    @pl.when(head > 0)
    def _():
        total[...] += grads

    @pl.when(head == HEADS - 1)
    def _():
        earlier_ref[0] = total[:HALF].astype(BF16)
        own_ref[0] = total[HALF:]


def head_block(*tail):
    return pl.BlockSpec((1, 1) + tail, lambda s, h, place: (s, h, 0, 0))


def sequence_block(*tail):
    return pl.BlockSpec((1,) + tail, lambda s, h, place: (s, 0, 0))


def attention_call(kernel, in_specs, out_specs, out_shape, scratch, flops, name):
    return pl.pallas_call(
        kernel,
        grid_spec=pltpu.PrefetchScalarGridSpec(
            num_scalar_prefetch=1,
            grid=(2, HEADS),
            in_specs=in_specs,
            out_specs=out_specs,
            scratch_shapes=[pltpu.VMEM((2 * HALF, HALF), F32)] + scratch,
        ),
        out_shape=out_shape,
        compiler_params=params("arbitrary", "arbitrary"),
        cost_estimate=cost(flops * 8 * 2 * HALF * HALF * HD * 2, 4),
        name=name,
    )


def attention(place, query, kv):
    return attention_call(
        attention_kernel,
        [head_block(HALF, HD), sequence_block(2 * HALF, 2 * HD)],
        [sequence_block(HALF, HEADS * HD), head_block(1, HALF)],
        [shaped(2, HALF, HEADS * HD), shaped(2, HEADS, 1, HALF, kind=F32)],
        [],
        2,
        "attention",
    )(place, query, kv)


def attention_back(place, query, kv, grad, log_total):
    return attention_call(
        attention_back_kernel,
        [
            head_block(HALF, HD), sequence_block(2 * HALF, 2 * HD),
            sequence_block(HALF, HEADS * HD), head_block(1, HALF),
        ],
        [sequence_block(HALF, HEADS * HD), sequence_block(HALF, 2 * HD), sequence_block(HALF, 2 * HD)],
        [
            shaped(2, HALF, HEADS * HD, kind=F32),
            shaped(2, HALF, 2 * HD),
            shaped(2, HALF, 2 * HD, kind=F32),
        ],
        [pltpu.VMEM((HALF, HD), BF16), pltpu.VMEM((2 * HALF, 2 * HD), F32)],
        5,
        "attention_back",
    )(place, query, kv, grad, log_total)


def own_rows(rows_all, y, core, per):
    return lax.dynamic_slice_in_dim(rows_all, (2 * y + core) * per, per, 0)


def feed_forward_kernel(*refs):
    place, token_refs, grad_refs, ff_ref = refs[0], refs[1:6], refs[6:11], refs[11]
    act_ref, act_t, gate_t, up_t = refs[12:16]
    parts, down_out = refs[16:21], refs[21]
    rows_h, rows_g, gate_up, down, slabs, sems = refs[22:]
    step = pl.program_id(0)
    tokens = put_tokens(token_refs, rows_h, sems, 0)
    grads = put_tokens(grad_refs, rows_g, sems, 10)
    weights, loads = [], []
    for x in range(4):
        for by in range(4):
            z = (2 * place[4] + place[0] + by) % 4
            zhi, zlo = z // 2, z % 2
            for core in range(2):
                weights.append(
                    pltpu.make_async_copy(
                        ff_ref.at[x, by, pl.ds(core * FFL, FFL)],
                        gate_up.at[zlo, :, lane_block(zhi, x, core)],
                        sems.at[20 + len(weights)],
                    )
                )
            loads.append(
                pltpu.make_async_copy(
                    ff_ref.at[x, by, pl.ds(2 * FFL, FFL)], slabs.at[zlo, zhi * 4 + x], sems.at[52 + len(loads)]
                )
            )
    back = pltpu.make_async_copy(down, down_out, sems.at[68])

    @pl.when(step == 0)
    def _():
        for copy in loads + tokens + weights + grads:
            copy.start()
        for copy in loads:
            copy.wait()

        def put(q, carry):
            for half in range(2):
                for p in range(4):
                    one = slabs[half, 2 * q, 2 * p * PIECE : 2 * (p + 1) * PIECE, :].astype(F32)
                    two = slabs[half, 2 * q + 1, 2 * p * PIECE : 2 * (p + 1) * PIECE, :].astype(F32)
                    lane = (half * 8 + 2 * p) * B
                    rows = pl.ds(pl.multiple_of(q * 2 * PIECE, 16), 2 * PIECE)
                    down[rows, lane : lane + B] = jnp.concatenate([one[:PIECE], two[:PIECE]], axis=0).astype(BF16)
                    down[rows, lane + B : lane + 2 * B] = jnp.concatenate(
                        [one[PIECE:], two[PIECE:]], axis=0
                    ).astype(BF16)
            return carry

        lax.fori_loop(0, 4, put, 0)
        back.start()
        for copy in tokens + weights + grads:
            copy.wait()

    rows = pl.ds(pl.multiple_of(step * TILE, TILE), TILE)
    normed = rows_h[rows, :]
    gate_pre = times_transposed(normed, gate_up[0])
    upward = times_transposed(normed, gate_up[1])
    grad_act = times_transposed(rows_g[rows, :], down[...])
    sigmoid = 1.0 / (1.0 + jnp.exp(-gate_pre))
    silu = gate_pre * sigmoid
    activation = silu * upward
    grad_up = grad_act * silu
    grad_gate = grad_act * upward * (sigmoid * (1.0 + gate_pre * (1.0 - sigmoid)))
    part = matmul(grad_gate.astype(BF16), gate_up[0]) + matmul(grad_up.astype(BF16), gate_up[1])
    put_parts(step, part.astype(BF16), parts)
    act_ref[...] = activation.astype(BF16)
    act_t[...] = activation.T.astype(BF16)
    gate_t[...] = grad_gate.T.astype(BF16)
    up_t[...] = grad_up.T.astype(BF16)

    @pl.when(step == 3)
    def _():
        back.wait()


def feed_forward(place, tokens, grads, ff_all):
    turned_spec = pl.BlockSpec((FFL, TILE), lambda i, p: (0, i))
    turned_shape = shaped(FFL, 2 * HALF)
    return pl.pallas_call(
        feed_forward_kernel,
        grid_spec=pltpu.PrefetchScalarGridSpec(
            num_scalar_prefetch=1,
            grid=(4,),
            in_specs=[ANYWHERE] * 11,
            out_specs=[pl.BlockSpec((TILE, FFL), lambda i, p: (i, 0))] + [turned_spec] * 3 + PART_SPECS + [ANYWHERE],
            scratch_shapes=[
                pltpu.VMEM((2 * HALF, D), BF16),
                pltpu.VMEM((2 * HALF, D), BF16),
                pltpu.VMEM((2, FFL, D), BF16),
                pltpu.VMEM((FFL, D), BF16),
                pltpu.VMEM((2, 8, FFL, B), BF16),
                pltpu.SemaphoreType.DMA((69,)),
            ],
        ),
        out_shape=[shaped(2 * HALF, FFL)] + [turned_shape] * 3 + PART_SHAPES + [shaped(FFL, D)],
        compiler_params=params("arbitrary"),
        cost_estimate=cost(2 * 5 * 2 * HALF * FFL * D, 32),
        name="feed_forward",
    )(place, *tokens, *grads, ff_all)


def along_z(place, zhi, zlo):
    return (2 * zhi + zlo + 4 - 2 * place[4] - place[0]) % 4


def gate_up_kernel(*refs):
    place, token_refs, gate_t, up_t, out_ref, rows, sems = refs[0], refs[1:6], *refs[6:]
    step = pl.program_id(0)
    copies = put_tokens(token_refs, rows, sems, 0)

    @pl.when(step == 0)
    def _():
        for copy in copies:
            copy.start()
        for copy in copies:
            copy.wait()

    normed = rows[:, pl.ds(pl.multiple_of(step * 2 * B, 2 * B), 2 * B)]
    for matrix, left in ((0, gate_t), (1, up_t)):
        term = matmul(left[...], normed).astype(BF16)
        by = along_z(place, step // 4, matrix)
        out_ref[step % 4, by, 0:FFL, :] = term[:, :B]
        out_ref[step % 4, by, FFL:, :] = term[:, B:]


def down_kernel(*refs):
    place, grad_refs, act_t, out_ref, rows, sems = refs[0], refs[1:6], *refs[6:]
    step = pl.program_id(0)
    copies = put_tokens(grad_refs, rows, sems, 0)

    @pl.when(step == 0)
    def _():
        for copy in copies:
            copy.start()
        for copy in copies:
            copy.wait()

    term = matmul(act_t[...], rows[:, pl.ds(pl.multiple_of(step * 2 * B, 2 * B), 2 * B)])
    half, p = step // 4, step % 4
    at = pl.ds(pl.multiple_of(p * 2 * PIECE, 16), 2 * PIECE)
    for zx in range(8):
        slab = term[zx * PIECE : (zx + 1) * PIECE]
        slab = jnp.concatenate([slab[:, :B], slab[:, B:]], axis=0).astype(BF16)
        out_ref[zx % 4, along_z(place, zx // 4, half), at, :] = slab


def ff_terms(kernel, place, pieces, lefts, rows, name):
    whole = pl.BlockSpec((FFL, 2 * HALF), lambda i, p: (0, 0))
    return pl.pallas_call(
        kernel,
        grid_spec=pltpu.PrefetchScalarGridSpec(
            num_scalar_prefetch=1,
            grid=(8,),
            in_specs=[ANYWHERE] * 5 + [whole] * len(lefts),
            out_specs=pl.BlockSpec((4, 4, rows, B), lambda i, p: (0, 0, 0, 0)),
            scratch_shapes=[pltpu.VMEM((2 * HALF, D), BF16), pltpu.SemaphoreType.DMA((10,))],
        ),
        out_shape=shaped(4, 4, rows, B),
        compiler_params=params("arbitrary"),
        cost_estimate=cost(2 * len(lefts) * 2 * HALF * FFL * D, 8 + 4 * len(lefts)),
        name=name,
    )(place, *pieces, *lefts)


def finish_hidden_kernel(*refs):
    place, piece_refs, weight_ref, gain_ref, out_ref, gain_out, rows = refs[0], refs[1:5], *refs[5:]
    y = place[1]
    for ref, by in zip(piece_refs, (0, 1, 2, 3)):
        at_y = (y + by) % 4
        for core in range(2):
            slab = ref[core].astype(F32)
            for zx in range(8):
                at = pl.multiple_of((2 * zx + core) * 4 * PIECE + at_y * PIECE, 8)
                rows[pl.ds(at, PIECE)] = slab[zx * PIECE : (zx + 1) * PIECE]
    gain = gain_ref[...]
    total = jnp.zeros((B, 1), F32)
    for i in range(FF // B):
        lanes = slice(i * B, (i + 1) * B)
        block = rows[lanes].T
        total = total + jnp.sum(block * weight_ref[:, lanes].astype(F32), axis=1, keepdims=True)
        out_ref[:, lanes] = block * gain
    gain_out[...] = total


def finish_hidden(place, pieces, weight, gain):
    whole = lambda *shape: pl.BlockSpec(shape, lambda i, p: (0,) * len(shape))
    return pl.pallas_call(
        finish_hidden_kernel,
        grid_spec=pltpu.PrefetchScalarGridSpec(
            num_scalar_prefetch=1,
            grid=(1,),
            in_specs=[whole(2, FFL, B)] * 4 + [whole(B, FF), whole(B, 1)],
            out_specs=[whole(B, FF), whole(B, 1)],
            scratch_shapes=[pltpu.VMEM((FF, B), F32)],
        ),
        out_shape=[shaped(B, FF, kind=F32), shaped(B, 1, kind=F32)],
        compiler_params=params("arbitrary"),
        cost_estimate=cost(0, 6),
        name="finish_hidden",
    )(place, *pieces, weight, gain)


def finish_down_kernel(place, *refs):
    piece_refs, out_ref = refs[:4], refs[4]
    for ref, by in zip(piece_refs, range(4)):
        rows = pl.ds(pl.multiple_of((place[1] + by) % 4 * PIECE, 8), PIECE)
        for half in range(2):
            slab = ref[half].astype(F32)
            for t in range(8):
                lane = (half * 8 + t) * B
                out_ref[rows, lane : lane + B] = slab[t * PIECE : (t + 1) * PIECE]


def finish_down(place, pieces):
    whole = lambda *shape: pl.BlockSpec(shape, lambda i, p: (0,) * len(shape))
    return pl.pallas_call(
        finish_down_kernel,
        grid_spec=pltpu.PrefetchScalarGridSpec(
            num_scalar_prefetch=1,
            grid=(1,),
            in_specs=[whole(2, FFL, B)] * 4,
            out_specs=whole(4 * PIECE, D),
            scratch_shapes=[],
        ),
        out_shape=shaped(4 * PIECE, D, kind=F32),
        compiler_params=params("arbitrary"),
        cost_estimate=cost(0, 5),
        name="finish_down",
    )(place, *pieces)


def on_device(
    layer_input,
    positions,
    attn_gain,
    w_query,
    w_key,
    w_value,
    w_output,
    mlp_gain,
    w_gate,
    w_up,
    w_down,
    out_grad,
):
    zlo, y, zhi, x, core = (lax.axis_index(axis) for axis in AXES)
    place = jnp.stack([zlo, y, core, x, zhi]).astype(jnp.int32)

    def by_core(mine, got):
        return jnp.where(core == 0, jnp.stack([mine, got]), jnp.stack([got, mine]))

    def by_zlo(mine, got):
        return jnp.where(zlo == 0, jnp.stack([mine, got]), jnp.stack([got, mine]))

    def by_zhi(mine, got):
        return jnp.where(zhi == 0, jnp.stack([mine, got]), jnp.stack([got, mine]))

    x_low = layer_input[0]
    x_pair = jnp.stack([x_low, swap_core(x_low)])
    qkv_mine, qkv_other = prepare_qkv(place, w_query, w_key, w_value, attn_gain[:, None])
    qkv_pair = by_core(qkv_mine, swap_core(qkv_other))
    x_pair, qkv_pair = tie(x_pair, qkv_pair)

    x_got = along_y(x_pair)
    qkv_column = by_zhi(qkv_pair, shift(qkv_pair, "zhi", 1))
    inputs = x_low.astype(F32)
    scale_one = lax.rsqrt(jnp.mean(inputs * inputs, axis=-1, keepdims=True) + eps)
    meta = jnp.concatenate([positions.astype(F32), scale_one.reshape(1, B)], axis=0)
    gain_two, meta, _ = tie(mlp_gain[:, None], meta, x_pair)
    ff_mine, ff_other, ff_down = prepare_ff(place, w_gate, w_up, w_down, gain_two)
    ff_piece = jnp.concatenate([by_core(ff_mine, swap_core(ff_other)).reshape(2 * FFL, B), ff_down], axis=0)
    x_got, qkv_column, ff_piece = tie(x_got, qkv_column, ff_piece)

    x_far = along_y(send_half(x_got))
    x_swapped = swap_core(x_got)
    qkv_before, qkv_after = shift(qkv_column, "x", 1), shift(qkv_column, "x", -1)
    ff_before, ff_after = shift(ff_piece, "z", 1), shift(ff_piece, "z", -1)
    meta = jnp.stack(small_gather(meta, "y"))
    x_far, x_swapped, qkv_before, qkv_after, ff_before, ff_after, meta = tie(
        x_far, x_swapped, qkv_before, qkv_after, ff_before, ff_after, meta
    )

    x_pieces = (x_pair, x_got, x_swapped, x_far, swap_core(x_far))
    qkv_pieces = (
        qkv_column, qkv_after, shift(qkv_before[:1], "x", 1), shift(qkv_after[1:], "x", -1), qkv_before,
    )
    half = 3 * FFL // 2
    ff_low, ff_high = shift(ff_before[:half], "z", 1), shift(ff_after[half:], "z", -1)
    ff_ring = jnp.concatenate([ff_piece, ff_after, ff_low, ff_high, ff_before], axis=0).reshape(4, 3 * FFL, B)
    meta = jnp.stack([meta, swap_core(meta)])
    near = jnp.where(core == 0, meta[:, 3], meta[:, 1])
    ahead = jnp.where(core == 0, meta[:, 1], meta[:, 3])
    far = jnp.where(core == 0, meta[:, 2], jnp.roll(meta[:, 2], B // 2, axis=-1))
    meta = jnp.concatenate([meta[:, 0], near, ahead, far], axis=-1)
    scale_all = meta[:, 1].reshape(2 * HALF, 1)
    frequency = theta ** (-jnp.arange(0, HD, 2).astype(F32) / HD)
    angles = meta[:, 0].reshape(2 * HALF, 1) * jnp.tile(frequency, 4)
    cosine, sine = jnp.cos(angles), jnp.sin(angles)
    x_pieces, qkv_pieces, ff_ring, out_low, w_out = tie(x_pieces, qkv_pieces, ff_ring, out_grad[0], w_output)

    ff_all = lax.all_gather(ff_ring, "x", axis=0, tiled=False)
    query, key_value, qkv_full = project_qkv(place, x_pieces, qkv_pieces, scale_all, cosine, sine)
    o_rows = lax.all_to_all(w_out.reshape(B, 16, B).transpose(1, 0, 2), FSDP, 0, 0, tiled=True).reshape(D, B)
    o_pair = by_core(
        own_rows(o_rows, y, core, HEADS * HD), swap_core(own_rows(o_rows, y, 1 - core, HEADS * HD))
    )
    o_column = by_zhi(o_pair, shift(o_pair, "zhi", 1))
    o_pieces = ring_pieces(o_column, "x")
    grad_pieces = gather_tokens(out_low)
    earlier = lax.ppermute(key_value, "zlo", [(0, 1)])
    key_value = jnp.concatenate([earlier, key_value], axis=1)
    mixed, log_total = attention(place, query, key_value)
    mixed = mixed.reshape(2 * HALF, HEADS * HD)
    *parts, o_full = project_out(place, o_pieces, mixed)
    hidden = inputs + scatter_tokens(parts)
    scale_two = lax.rsqrt(jnp.mean(hidden * hidden, axis=-1, keepdims=True) + eps)
    normed_pieces = gather_tokens((hidden * scale_two).astype(BF16))

    activation, act_t, gate_t, up_t, *parts, down_full = feed_forward(place, normed_pieces, grad_pieces, ff_all)
    grad_normed_two = scatter_tokens(parts)
    gate_up_terms = ff_terms(gate_up_kernel, place, normed_pieces, (gate_t, up_t), 2 * FFL, "gate_up_terms")
    down_terms = ff_terms(down_kernel, place, grad_pieces, (act_t,), FFL, "down_terms")
    down_parts = project(activation, down_full)

    mean_two = jnp.mean(grad_normed_two * hidden, axis=-1, keepdims=True)
    grad_hidden = (
        out_grad[0].astype(F32)
        + scale_two * grad_normed_two
        - hidden * (scale_two * scale_two * scale_two) * mean_two
    )
    hidden_low, gate_up_terms, down_terms = tie(grad_hidden.astype(BF16), gate_up_terms, down_terms)
    gate_up_sum = lax.psum_scatter(gate_up_terms, "x", scatter_dimension=0, tiled=True)[0]
    down_sum = lax.psum_scatter(down_terms, "x", scatter_dimension=0, tiled=True)[0]
    hidden_grad_pieces = gather_tokens(hidden_low)
    grad_mixed, output_terms = grad_of_mixed(place, hidden_grad_pieces, o_full, mixed)
    grad_mixed, down_parts = tie(grad_mixed, down_parts)
    result = hidden + scatter_tokens(down_parts)
    grad_query, grad_earlier, grad_own = attention_back(
        place, query, key_value, grad_mixed.reshape(2, HALF, HEADS * HD), log_total
    )
    later = lax.ppermute(grad_earlier, "zlo", [(1, 0)])
    *parts, grad_t = qkv_back(grad_query, grad_own, later, cosine, sine, scale_all, qkv_full)
    grad_normed = scatter_tokens(parts)
    qkv_term = qkv_terms(place, x_pieces, grad_t)
    mean_one = jnp.mean(grad_normed * inputs, axis=-1, keepdims=True)
    input_grad = (
        grad_hidden
        + scale_one * grad_normed
        - inputs * (scale_one * scale_one * scale_one) * mean_one
    )

    def own_block(pair):
        keep = lax.dynamic_index_in_dim(pair, core, 0, keepdims=False)
        return by_core(keep, swap_core(lax.dynamic_index_in_dim(pair, 1 - core, 0, keepdims=False)))

    def attention_sums(terms):
        rows = terms.shape[3]
        column = ring_scatter([terms[i] for i in range(4)], "x").astype(BF16)
        column = column.reshape(2, 2, 2, rows // 2, B).transpose(0, 2, 1, 3, 4).reshape(4, rows, B)
        z = 2 * zhi + zlo
        column = [lax.dynamic_index_in_dim(column, (z + i) % 4, 0, keepdims=False) for i in range(4)]
        own = own_block(ring_scatter(column, "z").astype(BF16).reshape(2, rows // 2, B))
        own = by_zlo(own, shift(own, "zlo", 1)).transpose(1, 0, 2, 3).reshape(2, rows, B)
        return jnp.roll(jnp.stack(ring_gather(own, "y")), y, axis=0)

    output_rows = attention_sums(output_terms).reshape(16, B, B)
    output_grad = lax.all_to_all(output_rows, FSDP, 0, 0, tiled=True)
    output_grad = output_grad.transpose(1, 0, 2).reshape(B, D).astype(F32)
    sums = attention_sums(qkv_term)
    query_grad = sums[:, :, : HEADS * HD].reshape(D, B).T.astype(F32)
    key_grad = jnp.sum(sums[:, :, HEADS * HD : (HEADS + 1) * HD].astype(F32), axis=1)
    key_grad = key_grad.reshape(KV * HD, B).T
    value_grad = jnp.sum(sums[:, :, (HEADS + 1) * HD :].astype(F32), axis=1)
    value_grad = value_grad.reshape(KV * HD, B).T
    attn_gain_grad = (
        jnp.sum(query_grad * w_query.astype(F32), axis=1)
        + jnp.sum(key_grad * w_key.astype(F32), axis=1)
        + jnp.sum(value_grad * w_value.astype(F32), axis=1)
    )

    gate_up = ring_scatter([gate_up_sum[i] for i in range(4)], "z").astype(BF16)
    gate_up = own_block(gate_up.reshape(2, FFL, B))
    gate_up = by_zlo(gate_up, shift(gate_up, "zlo", 1))
    gate_up = ring_gather(gate_up, "y")
    gain_two = mlp_gain[:, None]
    gate_grad, gate_gain = finish_hidden(place, [p[0] for p in gate_up], w_gate, gain_two)
    up_grad, up_gain = finish_hidden(place, [p[1] for p in gate_up], w_up, gain_two)
    down = ring_scatter([down_sum[i] for i in range(4)], "z").astype(BF16)
    down = by_zlo(down, shift(down, "zlo", 1))
    down_grad = finish_down(place, ring_gather(down, "y"))
    one = attn_gain[:, None]
    return (
        result.astype(BF16)[None],
        input_grad.astype(BF16)[None],
        attn_gain_grad,
        query_grad * one,
        key_grad * one,
        value_grad * one,
        output_grad,
        (gate_gain + up_gain)[:, 0],
        gate_grad,
        up_grad,
        down_grad,
    )


def solution(mesh):
    split = Mesh(mesh.devices.reshape(2, 4, 2, 4, 2), AXES)
    tokens = P(FSDP, SEQ, None)
    rows = P(FSDP, None)
    gain = P(FSDP)
    in_specs = (
        tokens, P(FSDP, SEQ), gain, rows, rows, rows, rows, gain, rows, rows, rows, tokens,
    )
    out_specs = (tokens, tokens, gain, rows, rows, rows, rows, gain, rows, rows, rows)
    return jax.shard_map(
        on_device, mesh=split, in_specs=in_specs, out_specs=out_specs, check_vma=False
    )
```

```python
import jax
import jax.numpy as jnp
from jax import lax
from jax.experimental import pallas as pl
from jax.experimental.pallas import tpu as pltpu
from jax.sharding import Mesh
from jax.sharding import PartitionSpec as P

H = 32
KV = 4
HD = 64
D = 2048
FF = 5632
B = 128
HALF = 512
HEADS = 4
FFL = 704
PIECE = 88

eps = 1e-05
theta = 10000.0
F32 = jnp.float32
BF16 = jnp.bfloat16
AXES = ("zlo", "y", "zhi", "x", "core")
FSDP = ("zhi", "x", "core")
SEQ = ("zlo", "y")


def matmul(left, right):
    return jnp.dot(left, right, preferred_element_type=F32)


def times_transposed(left, right):
    return lax.dot_general(left, right, (((1,), (1,)), ((), ())), preferred_element_type=F32)


def outer_sum(left, right):
    return lax.dot_general(left, right, (((0,), (0,)), ((), ())), preferred_element_type=F32)


def shift(value, axis, by):
    if axis == "z":
        at = [2 * (z % 2) + z // 2 for z in range(4)]
        return lax.ppermute(value, ("zlo", "zhi"), [(at[z], at[(z + by) % 4]) for z in range(4)])
    size = lax.axis_size(axis)
    return lax.ppermute(value, axis, [(i, (i + by) % size) for i in range(size)])


def swap_core(value):
    return shift(value, "core", 1)


def small_gather(block, axis):
    return block, shift(block, axis, -1), shift(block, axis, 2), shift(block, axis, 1)


def tie(*values):
    return lax.optimization_barrier(values)


def add(left, right):
    return left.astype(F32) + right.astype(F32)


def along_y(value):
    pairs = []
    for i in range(4):
        pairs.append((2 * i, 2 * ((i + 1) % 4)))
        pairs.append((2 * i + 1, 2 * ((i + 3) % 4) + 1))
    return lax.ppermute(value, ("y", "core"), pairs)


def send_half(got):
    core = lax.axis_index("core")
    return lax.dynamic_slice_in_dim(got, core * (B // 2), B // 2, 1)


FLIPPED = (0, 0, 1, 0, 1)
LENGTHS = (B, B, B, B // 2, B // 2)


def put_tokens(refs, rows_ref, sems, start):
    copies = []
    row = 0
    for s in range(2):
        for ref, flip, length in zip(refs, FLIPPED, LENGTHS):
            copies.append(
                pltpu.make_async_copy(
                    ref.at[s ^ flip], rows_ref.at[pl.ds(row, length)], sems.at[start + len(copies)]
                )
            )
            row += length
    return copies


TILE = 256
VMEM_LIMIT = 56 * 2**20
ANYWHERE = pl.BlockSpec(memory_space=pl.ANY)


def params(*kinds):
    return pltpu.CompilerParams(dimension_semantics=kinds or None, vmem_limit_bytes=VMEM_LIMIT)


def cost(flops, megabytes):
    return pl.CostEstimate(flops=flops, bytes_accessed=int(megabytes * 2**20), transcendentals=0)


def shaped(*shape, kind=BF16):
    return jax.ShapeDtypeStruct(shape, kind)


PART_SPECS = [pl.BlockSpec((1, n, D), lambda i, *_: (i // 2, 0, 0)) for n in LENGTHS]
PART_SHAPES = [jax.ShapeDtypeStruct((2, n, D), BF16) for n in LENGTHS]


def put_parts(step, tile, refs):
    @pl.when(step % 2 == 0)
    def _():
        refs[0][0] = tile[:B]
        refs[1][0] = tile[B:]

    @pl.when(step % 2 == 1)
    def _():
        refs[2][0] = tile[:B]
        refs[3][0] = tile[B : B + B // 2]
        refs[4][0] = tile[B + B // 2 :]


def turned(values):
    lane = lax.broadcasted_iota(jnp.int32, values.shape, 1) % HD
    return jnp.where(lane < HD // 2, -pltpu.roll(values, 2 * HD - HD // 2, 1), pltpu.roll(values, HD // 2, 1))


def lane_block(zhi, x, core):
    return pl.ds(pl.multiple_of((zhi * 8 + x * 2 + core) * B, B), B)


def put_columns(place, refs, into, sems, start):
    copies = []
    for ref, by, first in zip(refs, (0, 1, 2, 2, 3), (0, 0, 0, 1, 0)):
        for i in range(ref.shape[0]):
            for core in range(2):
                lanes = lane_block(first + i, (place[3] + by) % 4, core)
                copies.append(
                    pltpu.make_async_copy(ref.at[i, core], into.at[:, lanes], sems.at[start + len(copies)])
                )
    return copies


def prepare_qkv_kernel(place, q_mine, q_other, w_key, w_value, gain, mine_ref, other_ref, k_rows, v_rows):
    scale = gain[...]
    k_rows[...] = (w_key[...].astype(F32) * scale).T
    v_rows[...] = (w_value[...].astype(F32) * scale).T
    rows = pl.ds(pl.multiple_of(place[1] * HD, HD), HD)
    for source, out in ((q_mine, mine_ref), (q_other, other_ref)):
        out[: HEADS * HD] = (source[...].astype(F32) * scale).T.astype(BF16)
        out[HEADS * HD : (HEADS + 1) * HD] = k_rows[rows].astype(BF16)
        out[(HEADS + 1) * HD :] = v_rows[rows].astype(BF16)


QKV = (HEADS + 2) * HD


def prepare_qkv(place, w_query, w_key, w_value, gain):
    whole = lambda *shape: pl.BlockSpec(shape, lambda i, p: (0,) * len(shape))
    return pl.pallas_call(
        prepare_qkv_kernel,
        grid_spec=pltpu.PrefetchScalarGridSpec(
            num_scalar_prefetch=1,
            grid=(1,),
            in_specs=[
                pl.BlockSpec((B, HEADS * HD), lambda i, p: (0, 2 * p[1] + p[2])),
                pl.BlockSpec((B, HEADS * HD), lambda i, p: (0, 2 * p[1] + 1 - p[2])),
                whole(B, KV * HD), whole(B, KV * HD), whole(B, 1),
            ],
            out_specs=[whole(QKV, B), whole(QKV, B)],
            scratch_shapes=[pltpu.VMEM((KV * HD, B), F32), pltpu.VMEM((KV * HD, B), F32)],
        ),
        out_shape=[shaped(QKV, B), shaped(QKV, B)],
        compiler_params=params("arbitrary"),
        cost_estimate=cost(0, 1),
        name="prepare_qkv",
    )(place, w_query, w_query, w_key, w_value, gain)


def prepare_ff_kernel(place, w_gate, w_up, w_down, gain, mine_ref, other_ref, down_ref, picked, rows, down_rows, sems):
    zlo, y, core = place[0], place[1], place[2]
    down = pltpu.make_async_copy(
        w_down.at[:, pl.ds(pl.multiple_of(zlo * (D // 2), D // 2), D // 2)], down_rows, sems.at[1]
    )
    down.start()

    @pl.when(zlo == 0)
    def _():
        copy = pltpu.make_async_copy(w_gate, picked, sems.at[0])
        copy.start()
        copy.wait()

    @pl.when(zlo == 1)
    def _():
        copy = pltpu.make_async_copy(w_up, picked, sems.at[0])
        copy.start()
        copy.wait()

    scale = gain[...]
    for i in range(FF // B):
        rows[i * B : (i + 1) * B] = (picked[:, i * B : (i + 1) * B].astype(F32) * scale).T
    for which, out in ((core, mine_ref), (1 - core, other_ref)):
        slabs = []
        for zx in range(8):
            at = pl.multiple_of(zx * 2 * 4 * PIECE + which * 4 * PIECE + y * PIECE, 8)
            slabs.append(rows[pl.ds(at, PIECE)])
        out[...] = jnp.concatenate(slabs, axis=0).astype(BF16)
    down.wait()
    for t in range(8):
        rows[t * 4 * PIECE : (t + 1) * 4 * PIECE] = down_rows[:, t * B : (t + 1) * B].astype(F32)
    slabs = [rows[pl.ds(pl.multiple_of(t * 4 * PIECE + y * PIECE, 8), PIECE)] for t in range(8)]
    down_ref[...] = jnp.concatenate(slabs, axis=0).astype(BF16)


def prepare_ff(place, w_gate, w_up, w_down, gain):
    return pl.pallas_call(
        prepare_ff_kernel,
        grid_spec=pltpu.PrefetchScalarGridSpec(
            num_scalar_prefetch=1,
            grid=(1,),
            in_specs=[ANYWHERE, ANYWHERE, ANYWHERE, pl.BlockSpec((B, 1), lambda i, p: (0, 0))],
            out_specs=[pl.BlockSpec((FFL, B), lambda i, p: (0, 0))] * 3,
            scratch_shapes=[
                pltpu.VMEM((B, FF), BF16),
                pltpu.VMEM((FF, B), F32),
                pltpu.VMEM((4 * PIECE, D // 2), BF16),
                pltpu.SemaphoreType.DMA((2,)),
            ],
        ),
        out_shape=[shaped(FFL, B)] * 3,
        compiler_params=params("arbitrary"),
        cost_estimate=cost(0, 6),
        name="prepare_ff",
    )(place, w_gate, w_up, w_down, gain)


def project_qkv_kernel(*refs):
    place, x_refs, w_refs = refs[0], refs[1:6], refs[6:11]
    cosine_ref, sine_ref, query_ref, kv_ref, scale_ref, w_out, rows, weights, sems = refs[11:]
    step = pl.program_id(0)
    tokens = put_tokens(x_refs, rows, sems, 0)
    columns = put_columns(place, w_refs, weights, sems, 10)
    back = pltpu.make_async_copy(weights, w_out, sems.at[26])

    @pl.when(step == 0)
    def _():
        for copy in columns + tokens:
            copy.start()
        for copy in columns:
            copy.wait()
        back.start()
        for copy in tokens:
            copy.wait()

    tile = rows[pl.ds(pl.multiple_of(step * TILE, TILE), TILE), :]
    wide = tile.astype(F32)
    scale = lax.rsqrt(jnp.mean(wide * wide, axis=-1, keepdims=True) + eps)
    scale_ref[...] = scale
    pre = times_transposed(tile, weights[...]) * scale
    cosine, sine = cosine_ref[...], sine_ref[...]
    for i in range(2):
        part = pre[:, i * 2 * HD : (i + 1) * 2 * HD]
        part = (part * cosine + turned(part) * sine).astype(BF16) * HD ** (-0.5)
        query_ref[0, 2 * i] = part[:, :HD]
        query_ref[0, 2 * i + 1] = part[:, HD:]
    part = pre[:, HEADS * HD :]
    lane = lax.broadcasted_iota(jnp.int32, part.shape, 1)
    kv_ref[0] = jnp.where(lane < HD, part * cosine + turned(part) * sine, part).astype(BF16)

    @pl.when(step == 3)
    def _():
        back.wait()


def project_qkv(place, x_pieces, w_pieces, cosine, sine):
    tile = lambda lanes: pl.BlockSpec((TILE, lanes), lambda i, p: (i, 0))
    return pl.pallas_call(
        project_qkv_kernel,
        grid_spec=pltpu.PrefetchScalarGridSpec(
            num_scalar_prefetch=1,
            grid=(4,),
            in_specs=[ANYWHERE] * 10 + [tile(2 * HD), tile(2 * HD)],
            out_specs=[
                pl.BlockSpec((1, HEADS, TILE, HD), lambda i, p: (i // 2, 0, i % 2, 0)),
                pl.BlockSpec((1, TILE, 2 * HD), lambda i, p: (i // 2, i % 2, 0)),
                tile(1),
                ANYWHERE,
            ],
            scratch_shapes=[
                pltpu.VMEM((2 * HALF, D), BF16),
                pltpu.VMEM((QKV, D), BF16),
                pltpu.SemaphoreType.DMA((27,)),
            ],
        ),
        out_shape=[
            shaped(2, HEADS, HALF, HD), shaped(2, HALF, 2 * HD), shaped(2 * HALF, 1, kind=F32), shaped(QKV, D),
        ],
        compiler_params=params("arbitrary"),
        cost_estimate=cost(2 * 2 * HALF * QKV * D, 8),
        name="project_qkv",
    )(place, *x_pieces, *w_pieces, cosine, sine)


def project_out_kernel(*refs):
    place, w_refs, left_ref = refs[0], refs[1:6], refs[6]
    parts, w_out, weights, sems = refs[7:12], refs[12], refs[13], refs[14]
    step = pl.program_id(0)
    columns = put_columns(place, w_refs, weights, sems, 0)
    back = pltpu.make_async_copy(weights, w_out, sems.at[16])

    @pl.when(step == 0)
    def _():
        for copy in columns:
            copy.start()
        for copy in columns:
            copy.wait()
        back.start()

    put_parts(step, matmul(left_ref[...], weights[...]).astype(BF16), parts)

    @pl.when(step == 3)
    def _():
        back.wait()


def project_out(place, w_pieces, mixed):
    return pl.pallas_call(
        project_out_kernel,
        grid_spec=pltpu.PrefetchScalarGridSpec(
            num_scalar_prefetch=1,
            grid=(4,),
            in_specs=[ANYWHERE] * 5 + [pl.BlockSpec((TILE, HEADS * HD), lambda i, p: (i, 0))],
            out_specs=PART_SPECS + [ANYWHERE],
            scratch_shapes=[pltpu.VMEM((HEADS * HD, D), BF16), pltpu.SemaphoreType.DMA((17,))],
        ),
        out_shape=PART_SHAPES + [shaped(HEADS * HD, D)],
        compiler_params=params("arbitrary"),
        cost_estimate=cost(2 * 2 * HALF * HEADS * HD * D, 7),
        name="project_out",
    )(place, *w_pieces, mixed)


def project_kernel(left_ref, weight_ref, *parts):
    put_parts(pl.program_id(0), matmul(left_ref[...], weight_ref[...]).astype(BF16), parts)


def project(left, weight):
    depth = left.shape[1]
    return pl.pallas_call(
        project_kernel,
        grid=(4,),
        in_specs=[pl.BlockSpec((TILE, depth), lambda i: (i, 0)), pl.BlockSpec((depth, D), lambda i: (0, 0))],
        out_specs=PART_SPECS,
        out_shape=PART_SHAPES,
        compiler_params=params("arbitrary"),
        cost_estimate=cost(2 * 2 * HALF * depth * D, 8),
        name="project",
    )(left, weight)


def grad_mixed_kernel(*refs):
    place, grad_refs, weight_ref, mixed_ref = refs[0], refs[1:6], refs[6], refs[7]
    grad_mixed_ref, term_ref, rows, sems = refs[8:]
    copies = put_tokens(grad_refs, rows, sems, 0)
    for copy in copies:
        copy.start()
    for copy in copies:
        copy.wait()
    for i in range(4):
        tile = rows[i * TILE : (i + 1) * TILE, :]
        grad_mixed_ref[i * TILE : (i + 1) * TILE, :] = times_transposed(tile, weight_ref[...]).astype(BF16)
    left = mixed_ref[...].astype(F32).T.astype(BF16)
    put_term(place, left, rows, term_ref)


def put_term(place, left, rows, term_ref):
    def one(zx, carry):
        lanes = pl.ds(pl.multiple_of(zx * 2 * B, 2 * B), 2 * B)
        term = matmul(left, rows[:, lanes]).astype(BF16)
        by = (zx % 4 + 4 - place[3]) % 4
        term_ref[by, zx // 4, 0] = term[:, :B]
        term_ref[by, zx // 4, 1] = term[:, B:]
        return carry

    lax.fori_loop(0, 8, one, 0)


def grad_of_mixed(place, grad_pieces, weight, mixed):
    whole = lambda *shape: pl.BlockSpec(shape, lambda i, p: (0,) * len(shape))
    rows = HEADS * HD
    return pl.pallas_call(
        grad_mixed_kernel,
        grid_spec=pltpu.PrefetchScalarGridSpec(
            num_scalar_prefetch=1,
            grid=(1,),
            in_specs=[ANYWHERE] * 5 + [whole(rows, D), whole(2 * HALF, rows)],
            out_specs=[whole(2 * HALF, rows), whole(4, 2, 2, rows, B)],
            scratch_shapes=[pltpu.VMEM((2 * HALF, D), BF16), pltpu.SemaphoreType.DMA((10,))],
        ),
        out_shape=[shaped(2 * HALF, rows), shaped(4, 2, 2, rows, B)],
        compiler_params=params("arbitrary"),
        cost_estimate=cost(4 * 2 * HALF * rows * D, 8),
        name="grad_of_mixed",
    )(place, *grad_pieces, weight, mixed)


def qkv_back_kernel(grad_q_ref, own_ref, later_ref, cosine_ref, sine_ref, scale_ref, weight_ref, *outs):
    parts, turned_ref = outs[:5], outs[5]
    cosine, sine = cosine_ref[...], sine_ref[...]
    lane = lax.broadcasted_iota(jnp.int32, cosine.shape, 1)
    pieces = []
    for i in range(2):
        part = grad_q_ref[0, :, i * 2 * HD : (i + 1) * 2 * HD]
        pieces.append(part * cosine - turned(part * sine))
    part = own_ref[0] + later_ref[0].astype(F32)
    pieces.append(jnp.where(lane < HD, part * cosine - turned(part * sine), part))
    grad_pre = jnp.concatenate(pieces, axis=1)
    put_parts(pl.program_id(0), matmul(grad_pre.astype(BF16), weight_ref[...]).astype(BF16), parts)
    turned_ref[...] = (grad_pre * scale_ref[...]).T.astype(BF16)


def qkv_back(grad_query, own, later, cosine, sine, scale, weight):
    tile = lambda lanes: pl.BlockSpec((TILE, lanes), lambda i: (i, 0))
    half = lambda lanes: pl.BlockSpec((1, TILE, lanes), lambda i: (i // 2, i % 2, 0))
    return pl.pallas_call(
        qkv_back_kernel,
        grid=(4,),
        in_specs=[
            half(HEADS * HD), half(2 * HD), half(2 * HD), tile(2 * HD), tile(2 * HD), tile(1),
            pl.BlockSpec((QKV, D), lambda i: (0, 0)),
        ],
        out_specs=PART_SPECS + [pl.BlockSpec((QKV, TILE), lambda i: (0, i))],
        out_shape=PART_SHAPES + [shaped(QKV, 2 * HALF)],
        compiler_params=params("arbitrary"),
        cost_estimate=cost(2 * 2 * HALF * QKV * D, 9),
        name="qkv_back",
    )(grad_query, own, later, cosine, sine, scale, weight)


def qkv_term_kernel(*refs):
    place, x_refs, left_ref, term_ref, rows, sems = refs[0], refs[1:6], refs[6], refs[7], refs[8], refs[9]
    copies = put_tokens(x_refs, rows, sems, 0)
    for copy in copies:
        copy.start()
    for copy in copies:
        copy.wait()
    put_term(place, left_ref[...], rows, term_ref)


def qkv_terms(place, x_pieces, left):
    whole = lambda *shape: pl.BlockSpec(shape, lambda i, p: (0,) * len(shape))
    return pl.pallas_call(
        qkv_term_kernel,
        grid_spec=pltpu.PrefetchScalarGridSpec(
            num_scalar_prefetch=1,
            grid=(1,),
            in_specs=[ANYWHERE] * 5 + [whole(QKV, 2 * HALF)],
            out_specs=whole(4, 2, 2, QKV, B),
            scratch_shapes=[pltpu.VMEM((2 * HALF, D), BF16), pltpu.SemaphoreType.DMA((10,))],
        ),
        out_shape=shaped(4, 2, 2, QKV, B),
        compiler_params=params("arbitrary"),
        cost_estimate=cost(2 * 2 * HALF * QKV * D, 7),
        name="qkv_terms",
    )(place, *x_pieces, left)


def token_places(at, y, core):
    step = 1 - 2 * core
    block = jnp.where(
        at < B, y, jnp.where(at < 2 * B, y + 4 - step, jnp.where(at < 3 * B, y + 4 + step, y + 2))
    )
    row = at % B
    row = jnp.where(at < 3 * B, row, (row + core * (B // 2)) % B)
    return (block % 4) * B + row


def set_bias(place_ref, bias_ref):
    zlo, y, core = place_ref[0], place_ref[1], place_ref[2]
    key_at = token_places(lax.broadcasted_iota(jnp.int32, (HALF, 1), 0), y, core)
    query_at = token_places(lax.broadcasted_iota(jnp.int32, (1, HALF), 1), y, core)
    bias_ref[:HALF, :] = jnp.broadcast_to(jnp.where(zlo == 1, 0.0, -1e30), (HALF, HALF))
    bias_ref[HALF:, :] = jnp.where(key_at <= query_at, 0.0, -1e30)


def attention_kernel(place_ref, query_ref, kv_ref, mixed_ref, log_ref, bias_ref):
    @pl.when(pl.program_id(0) == 0)
    def _():
        set_bias(place_ref, bias_ref)

    key, value = kv_ref[0, :, :HD], kv_ref[0, :, HD:]
    for head in range(HEADS):
        scores = times_transposed(key, query_ref[0, head]) + bias_ref[...]
        top = jnp.max(scores, axis=0, keepdims=True)
        weights = jnp.exp(scores - top)
        total = jnp.sum(weights, axis=0, keepdims=True)
        low = (weights * (1.0 / total)).astype(BF16)
        mixed_ref[0, :, head * HD : (head + 1) * HD] = outer_sum(value, low).T.astype(BF16)
        log_ref[0, head] = top + jnp.log(total)


def attention_back_kernel(
    place_ref, query_ref, kv_ref, grad_ref, log_ref, grad_query_ref, earlier_ref, own_ref, bias_ref
):
    @pl.when(pl.program_id(0) == 0)
    def _():
        set_bias(place_ref, bias_ref)

    key, value = kv_ref[0, :, :HD], kv_ref[0, :, HD:]
    grad_key = jnp.zeros((2 * HALF, HD), F32)
    grad_value = jnp.zeros((2 * HALF, HD), F32)
    for head in range(HEADS):
        lanes = slice(head * HD, (head + 1) * HD)
        query, grad = query_ref[0, head], grad_ref[0, :, lanes]
        weights = jnp.exp(times_transposed(key, query) + bias_ref[...] - log_ref[0, head])
        grad_weights = times_transposed(value, grad)
        delta = jnp.sum(weights * grad_weights, axis=0, keepdims=True)
        grad_scores = (weights * (grad_weights - delta)).astype(BF16)
        grad_query_ref[0, :, lanes] = outer_sum(key, grad_scores).T * HD ** (-0.5)
        grad_key += matmul(grad_scores, query)
        grad_value += matmul(weights.astype(BF16), grad)
    total = jnp.concatenate([grad_key, grad_value], axis=1)
    earlier_ref[0] = total[:HALF].astype(BF16)
    own_ref[0] = total[HALF:]


def sequence_block(*tail):
    return pl.BlockSpec((1,) + tail, lambda s, place: (s,) + (0,) * len(tail))


def attention_call(kernel, in_specs, out_specs, out_shape, flops, name):
    return pl.pallas_call(
        kernel,
        grid_spec=pltpu.PrefetchScalarGridSpec(
            num_scalar_prefetch=1,
            grid=(2,),
            in_specs=in_specs,
            out_specs=out_specs,
            scratch_shapes=[pltpu.VMEM((2 * HALF, HALF), F32)],
        ),
        out_shape=out_shape,
        compiler_params=params("arbitrary"),
        cost_estimate=cost(flops * 8 * 2 * HALF * HALF * HD * 2, 4),
        name=name,
    )


def attention(place, query, kv):
    return attention_call(
        attention_kernel,
        [sequence_block(HEADS, HALF, HD), sequence_block(2 * HALF, 2 * HD)],
        [sequence_block(HALF, HEADS * HD), sequence_block(HEADS, 1, HALF)],
        [shaped(2, HALF, HEADS * HD), shaped(2, HEADS, 1, HALF, kind=F32)],
        2,
        "attention",
    )(place, query, kv)


def attention_back(place, query, kv, grad, log_total):
    return attention_call(
        attention_back_kernel,
        [
            sequence_block(HEADS, HALF, HD), sequence_block(2 * HALF, 2 * HD),
            sequence_block(HALF, HEADS * HD), sequence_block(HEADS, 1, HALF),
        ],
        [sequence_block(HALF, HEADS * HD), sequence_block(HALF, 2 * HD), sequence_block(HALF, 2 * HD)],
        [
            shaped(2, HALF, HEADS * HD, kind=F32),
            shaped(2, HALF, 2 * HD),
            shaped(2, HALF, 2 * HD, kind=F32),
        ],
        5,
        "attention_back",
    )(place, query, kv, grad, log_total)


def own_rows(rows_all, y, core, per):
    return lax.dynamic_slice_in_dim(rows_all, (2 * y + core) * per, per, 0)


def feed_forward_kernel(*refs):
    place, token_refs, grad_refs, ff_ref = refs[0], refs[1:6], refs[6:11], refs[11]
    act_ref, act_t, gate_t, up_t = refs[12:16]
    parts, down_out = refs[16:21], refs[21]
    rows_h, rows_g, gate_up, down, slabs, sems = refs[22:]
    step = pl.program_id(0)
    tokens = put_tokens(token_refs, rows_h, sems, 0)
    grads = put_tokens(grad_refs, rows_g, sems, 10)
    weights, loads = [], []
    for x in range(4):
        for by in range(4):
            z = (2 * place[4] + place[0] + by) % 4
            zhi, zlo = z // 2, z % 2
            for core in range(2):
                weights.append(
                    pltpu.make_async_copy(
                        ff_ref.at[x, by, pl.ds(core * FFL, FFL)],
                        gate_up.at[zlo, :, lane_block(zhi, x, core)],
                        sems.at[20 + len(weights)],
                    )
                )
            loads.append(
                pltpu.make_async_copy(
                    ff_ref.at[x, by, pl.ds(2 * FFL, FFL)], slabs.at[zlo, zhi * 4 + x], sems.at[52 + len(loads)]
                )
            )
    back = pltpu.make_async_copy(down, down_out, sems.at[68])

    @pl.when(step == 0)
    def _():
        for copy in loads + tokens + weights + grads:
            copy.start()
        for copy in loads:
            copy.wait()

        def put(q, carry):
            for half in range(2):
                for p in range(4):
                    one = slabs[half, 2 * q, 2 * p * PIECE : 2 * (p + 1) * PIECE, :].astype(F32)
                    two = slabs[half, 2 * q + 1, 2 * p * PIECE : 2 * (p + 1) * PIECE, :].astype(F32)
                    lane = (half * 8 + 2 * p) * B
                    rows = pl.ds(pl.multiple_of(q * 2 * PIECE, 16), 2 * PIECE)
                    down[rows, lane : lane + B] = jnp.concatenate([one[:PIECE], two[:PIECE]], axis=0).astype(BF16)
                    down[rows, lane + B : lane + 2 * B] = jnp.concatenate(
                        [one[PIECE:], two[PIECE:]], axis=0
                    ).astype(BF16)
            return carry

        lax.fori_loop(0, 4, put, 0)
        back.start()
        for copy in tokens + weights + grads:
            copy.wait()

    rows = pl.ds(pl.multiple_of(step * TILE, TILE), TILE)
    normed = rows_h[rows, :]
    gate_pre = times_transposed(normed, gate_up[0])
    upward = times_transposed(normed, gate_up[1])
    grad_act = times_transposed(rows_g[rows, :], down[...])
    sigmoid = 1.0 / (1.0 + jnp.exp(-gate_pre))
    silu = gate_pre * sigmoid
    activation = silu * upward
    grad_up = grad_act * silu
    grad_gate = grad_act * upward * (sigmoid * (1.0 + gate_pre * (1.0 - sigmoid)))
    part = matmul(grad_gate.astype(BF16), gate_up[0]) + matmul(grad_up.astype(BF16), gate_up[1])
    put_parts(step, part.astype(BF16), parts)
    act_ref[...] = activation.astype(BF16)
    act_t[...] = activation.T.astype(BF16)
    gate_t[...] = grad_gate.T.astype(BF16)
    up_t[...] = grad_up.T.astype(BF16)

    @pl.when(step == 3)
    def _():
        back.wait()


def feed_forward(place, tokens, grads, ff_all):
    turned_spec = pl.BlockSpec((FFL, TILE), lambda i, p: (0, i))
    turned_shape = shaped(FFL, 2 * HALF)
    return pl.pallas_call(
        feed_forward_kernel,
        grid_spec=pltpu.PrefetchScalarGridSpec(
            num_scalar_prefetch=1,
            grid=(4,),
            in_specs=[ANYWHERE] * 11,
            out_specs=[pl.BlockSpec((TILE, FFL), lambda i, p: (i, 0))] + [turned_spec] * 3 + PART_SPECS + [ANYWHERE],
            scratch_shapes=[
                pltpu.VMEM((2 * HALF, D), BF16),
                pltpu.VMEM((2 * HALF, D), BF16),
                pltpu.VMEM((2, FFL, D), BF16),
                pltpu.VMEM((FFL, D), BF16),
                pltpu.VMEM((2, 8, FFL, B), BF16),
                pltpu.SemaphoreType.DMA((69,)),
            ],
        ),
        out_shape=[shaped(2 * HALF, FFL)] + [turned_shape] * 3 + PART_SHAPES + [shaped(FFL, D)],
        compiler_params=params("arbitrary"),
        cost_estimate=cost(2 * 5 * 2 * HALF * FFL * D, 32),
        name="feed_forward",
    )(place, *tokens, *grads, ff_all)


def along_z(place, zhi, zlo):
    return (2 * zhi + zlo + 4 - 2 * place[4] - place[0]) % 4


def gate_up_kernel(*refs):
    place, token_refs, gate_t, up_t, out_ref, rows, sems = refs[0], refs[1:6], *refs[6:]
    step = pl.program_id(0)
    copies = put_tokens(token_refs, rows, sems, 0)

    @pl.when(step == 0)
    def _():
        for copy in copies:
            copy.start()
        for copy in copies:
            copy.wait()

    normed = rows[:, pl.ds(pl.multiple_of(step * 2 * B, 2 * B), 2 * B)]
    for matrix, left in ((0, gate_t), (1, up_t)):
        term = matmul(left[...], normed).astype(BF16)
        by = along_z(place, step // 4, matrix)
        out_ref[step % 4, by, 0:FFL, :] = term[:, :B]
        out_ref[step % 4, by, FFL:, :] = term[:, B:]


def down_kernel(*refs):
    place, grad_refs, act_t, out_ref, rows, sems = refs[0], refs[1:6], *refs[6:]
    step = pl.program_id(0)
    copies = put_tokens(grad_refs, rows, sems, 0)

    @pl.when(step == 0)
    def _():
        for copy in copies:
            copy.start()
        for copy in copies:
            copy.wait()

    term = matmul(act_t[...], rows[:, pl.ds(pl.multiple_of(step * 2 * B, 2 * B), 2 * B)])
    half, p = step // 4, step % 4
    at = pl.ds(pl.multiple_of(p * 2 * PIECE, 16), 2 * PIECE)
    for zx in range(8):
        slab = term[zx * PIECE : (zx + 1) * PIECE]
        slab = jnp.concatenate([slab[:, :B], slab[:, B:]], axis=0).astype(BF16)
        out_ref[zx % 4, along_z(place, zx // 4, half), at, :] = slab


def ff_terms(kernel, place, pieces, lefts, rows, name):
    whole = pl.BlockSpec((FFL, 2 * HALF), lambda i, p: (0, 0))
    return pl.pallas_call(
        kernel,
        grid_spec=pltpu.PrefetchScalarGridSpec(
            num_scalar_prefetch=1,
            grid=(8,),
            in_specs=[ANYWHERE] * 5 + [whole] * len(lefts),
            out_specs=pl.BlockSpec((4, 4, rows, B), lambda i, p: (0, 0, 0, 0)),
            scratch_shapes=[pltpu.VMEM((2 * HALF, D), BF16), pltpu.SemaphoreType.DMA((10,))],
        ),
        out_shape=shaped(4, 4, rows, B),
        compiler_params=params("arbitrary"),
        cost_estimate=cost(2 * len(lefts) * 2 * HALF * FFL * D, 8 + 4 * len(lefts)),
        name=name,
    )(place, *pieces, *lefts)


def finish_hidden_kernel(*refs):
    place, piece_refs, weight_ref, gain_ref, out_ref, gain_out, rows = refs[0], refs[1:5], *refs[5:]
    y = place[1]
    for ref, by in zip(piece_refs, (0, 1, 2, 3)):
        at_y = (y + by) % 4
        for core in range(2):
            slab = ref[core].astype(F32)
            for zx in range(8):
                at = pl.multiple_of((2 * zx + core) * 4 * PIECE + at_y * PIECE, 8)
                rows[pl.ds(at, PIECE)] = slab[zx * PIECE : (zx + 1) * PIECE]
    gain = gain_ref[...]
    total = jnp.zeros((B, 1), F32)
    for i in range(FF // B):
        lanes = slice(i * B, (i + 1) * B)
        block = rows[lanes].T
        total = total + jnp.sum(block * weight_ref[:, lanes].astype(F32), axis=1, keepdims=True)
        out_ref[:, lanes] = block * gain
    gain_out[...] = total


def finish_hidden(place, pieces, weight, gain):
    whole = lambda *shape: pl.BlockSpec(shape, lambda i, p: (0,) * len(shape))
    return pl.pallas_call(
        finish_hidden_kernel,
        grid_spec=pltpu.PrefetchScalarGridSpec(
            num_scalar_prefetch=1,
            grid=(1,),
            in_specs=[whole(2, FFL, B)] * 4 + [whole(B, FF), whole(B, 1)],
            out_specs=[whole(B, FF), whole(B, 1)],
            scratch_shapes=[pltpu.VMEM((FF, B), F32)],
        ),
        out_shape=[shaped(B, FF, kind=F32), shaped(B, 1, kind=F32)],
        compiler_params=params("arbitrary"),
        cost_estimate=cost(0, 6),
        name="finish_hidden",
    )(place, *pieces, weight, gain)


def finish_down_kernel(place, *refs):
    piece_refs, out_ref = refs[:4], refs[4]
    for ref, by in zip(piece_refs, range(4)):
        rows = pl.ds(pl.multiple_of((place[1] + by) % 4 * PIECE, 8), PIECE)
        for half in range(2):
            slab = ref[half].astype(F32)
            for t in range(8):
                lane = (half * 8 + t) * B
                out_ref[rows, lane : lane + B] = slab[t * PIECE : (t + 1) * PIECE]


def finish_down(place, pieces):
    whole = lambda *shape: pl.BlockSpec(shape, lambda i, p: (0,) * len(shape))
    return pl.pallas_call(
        finish_down_kernel,
        grid_spec=pltpu.PrefetchScalarGridSpec(
            num_scalar_prefetch=1,
            grid=(1,),
            in_specs=[whole(2, FFL, B)] * 4,
            out_specs=whole(4 * PIECE, D),
            scratch_shapes=[],
        ),
        out_shape=shaped(4 * PIECE, D, kind=F32),
        compiler_params=params("arbitrary"),
        cost_estimate=cost(0, 5),
        name="finish_down",
    )(place, *pieces)


class Flow:
    def __init__(self, steps):
        self.steps, self.result, self.sent = steps, None, None
        self.move(None)

    def move(self, arrived):
        try:
            self.sent = self.steps.send(arrived)
        except StopIteration as end:
            self.sent, self.result = (), end.value


def stage(flows, *values):
    flows = [flow for flow in flows if flow.result is None]
    sizes = [len(flow.sent) for flow in flows]
    leaves, tree = jax.tree.flatten(values)
    tied = tie(*[v for flow in flows for v in flow.sent], *leaves)
    for flow, size in zip(flows, sizes):
        flow.move(tied[:size])
        tied = tied[size:]
    return jax.tree.unflatten(tree, tied)


def gather_steps(block):
    (other,) = yield (swap_core(block),)
    pair = jnp.stack([block, other])
    (got,) = yield (along_y(pair),)
    far, swapped = yield (along_y(send_half(got)), swap_core(got))
    (far_swapped,) = yield (swap_core(far),)
    return pair, got, swapped, far, far_swapped


def scatter_steps(parts):
    core = lax.axis_index("core")
    first, behind, ahead, far, far_other = parts
    far_got, behind_got, first_got = yield (swap_core(far_other), swap_core(behind), swap_core(first[1]))
    far = add(far, far_got[::-1]).astype(BF16)
    (low,) = yield (along_y(far),)
    ahead = add(ahead, behind_got[::-1])
    mine = lax.dynamic_slice_in_dim(ahead, core * (B // 2), B // 2, 1) + low.astype(F32)
    ahead = lax.dynamic_update_slice_in_dim(ahead, mine, core * (B // 2), 1).astype(BF16)
    (got,) = yield (along_y(ahead),)
    (last,) = yield (swap_core(got[1]),)
    return add(first[0], first_got) + got[0].astype(F32) + last.astype(F32)


def ring_gather_steps(block, axis):
    half = block.shape[0] // 2
    before, after = yield (shift(block, axis, 1), shift(block, axis, -1))
    low, high = yield (shift(before[:half], axis, 1), shift(after[half:], axis, -1))
    return block, after, low, high, before


def ring_scatter_steps(parts, axis):
    half = parts[2].shape[0] // 2
    low, high = yield (shift(parts[2][:half], axis, 1), shift(parts[2][half:], axis, -1))
    after = jnp.concatenate([add(parts[1][:half], low).astype(BF16), parts[1][half:]], axis=0)
    before = jnp.concatenate([parts[3][:half], add(parts[3][half:], high).astype(BF16)], axis=0)
    from_before, from_after = yield (shift(after, axis, 1), shift(before, axis, -1))
    return add(parts[0], from_before) + from_after.astype(F32)


def on_device(
    layer_input,
    positions,
    attn_gain,
    w_query,
    w_key,
    w_value,
    w_output,
    mlp_gain,
    w_gate,
    w_up,
    w_down,
    out_grad,
):
    zlo, y, zhi, x, core = (lax.axis_index(axis) for axis in AXES)
    place = jnp.stack([zlo, y, core, x, zhi]).astype(jnp.int32)

    def by_core(mine, got):
        return jnp.where(core == 0, jnp.stack([mine, got]), jnp.stack([got, mine]))

    def by_zlo(mine, got):
        return jnp.where(zlo == 0, jnp.stack([mine, got]), jnp.stack([got, mine]))

    def by_zhi(mine, got):
        return jnp.where(zhi == 0, jnp.stack([mine, got]), jnp.stack([got, mine]))

    def column_steps(mine, other):
        (got,) = yield (swap_core(other),)
        pair = by_core(mine, got)
        (got,) = yield (shift(pair, "zhi", 1),)
        return (yield from ring_gather_steps(by_zhi(pair, got), "x"))

    def hidden_steps(mine, other, down):
        (got,) = yield (swap_core(other),)
        piece = jnp.concatenate([by_core(mine, got).reshape(2 * FFL, B), down], axis=0)
        pieces = yield from ring_gather_steps(piece, "z")
        return jnp.concatenate(pieces, axis=0).reshape(4, 3 * FFL, B)

    def block_steps(pair):
        keep = lax.dynamic_index_in_dim(pair, core, 0, keepdims=False)
        (got,) = yield (swap_core(lax.dynamic_index_in_dim(pair, 1 - core, 0, keepdims=False)),)
        own = by_core(keep, got)
        (got,) = yield (shift(own, "zlo", 1),)
        return (yield from ring_gather_steps(by_zlo(own, got), "y"))

    def whole_ring(pieces):
        own, after, low, high, before = pieces
        return own, after, jnp.concatenate([low, high], axis=0), before

    def attention_steps(terms):
        rows = terms.shape[3]
        column = yield from ring_scatter_steps([terms[i] for i in range(4)], "x")
        column = column.astype(BF16).reshape(2, 2, 2, rows // 2, B).transpose(0, 2, 1, 3, 4).reshape(4, rows, B)
        z = 2 * zhi + zlo
        column = [lax.dynamic_index_in_dim(column, (z + i) % 4, 0, keepdims=False) for i in range(4)]
        own = yield from ring_scatter_steps(column, "z")
        pieces = yield from block_steps(own.astype(BF16).reshape(2, rows // 2, B))
        ring = jnp.roll(jnp.stack(whole_ring(pieces)), y, axis=0)
        return ring.transpose(0, 2, 1, 3, 4).reshape(4, 2, rows, B)

    def gate_up_steps(sums):
        own = yield from ring_scatter_steps([sums[i] for i in range(4)], "z")
        pieces = yield from block_steps(own.astype(BF16).reshape(2, FFL, B))
        return whole_ring(pieces)

    def down_steps(sums):
        own = yield from ring_scatter_steps([sums[i] for i in range(4)], "z")
        own = own.astype(BF16)
        (got,) = yield (shift(own, "zlo", 1),)
        pieces = yield from ring_gather_steps(by_zlo(own, got), "y")
        return whole_ring(pieces)

    def all_to_all_steps(value):
        (got,) = yield (lax.all_to_all(value, FSDP, 0, 0, tiled=True),)
        return got

    x_low = layer_input[0]
    place_rows = positions.astype(F32)
    tokens = Flow(gather_steps(x_low))
    places = small_gather(place_rows, "y")
    qkv = Flow(column_steps(*prepare_qkv(place, w_query, w_key, w_value, attn_gain[:, None])))
    hidden_rows = Flow(hidden_steps(*prepare_ff(place, w_gate, w_up, w_down, mlp_gain[:, None])))
    places, w_out = stage([tokens, qkv, hidden_rows], places, w_output)

    places = jnp.stack(places)
    places_other = swap_core(places)
    output_rows = Flow(all_to_all_steps(w_out.reshape(B, 16, B).transpose(1, 0, 2)))
    places, places_other, x_low = stage([tokens, qkv, hidden_rows], places, places_other, x_low)

    places = jnp.stack([places, places_other])
    near = jnp.where(core == 0, places[:, 3], places[:, 1])
    ahead = jnp.where(core == 0, places[:, 1], places[:, 3])
    far = jnp.where(core == 0, places[:, 2], jnp.roll(places[:, 2], B // 2, axis=-1))
    places = jnp.concatenate([places[:, 0], near, ahead, far], axis=-1).reshape(2 * HALF, 1)
    frequency = theta ** (-jnp.arange(0, HD, 2).astype(F32) / HD)
    angles = places * jnp.tile(frequency, 4)
    cosine, sine = jnp.cos(angles), jnp.sin(angles)
    inputs = x_low.astype(F32)
    scale_one = lax.rsqrt(jnp.mean(inputs * inputs, axis=-1, keepdims=True) + eps)
    cosine, sine, scale_one, grad_low = stage(
        [tokens, qkv, hidden_rows, output_rows], cosine, sine, scale_one, out_grad[0]
    )

    o_rows = output_rows.result.reshape(D, B)
    o_block = Flow(
        column_steps(own_rows(o_rows, y, core, HEADS * HD), own_rows(o_rows, y, 1 - core, HEADS * HD))
    )
    grads = Flow(gather_steps(grad_low))
    stage([tokens, qkv, hidden_rows, o_block, grads])

    x_pieces = tokens.result
    ff_all = lax.all_gather(hidden_rows.result, "x", axis=0, tiled=False)
    query, key_value, scale_all, qkv_full = project_qkv(place, x_pieces, qkv.result, cosine, sine)
    query, key_value = stage([o_block, grads], query, key_value)
    earlier = lax.ppermute(key_value, "zlo", [(0, 1)])
    query, key_value, earlier = stage([o_block, grads], query, key_value, earlier)
    key_value = jnp.concatenate([earlier, key_value], axis=1)
    mixed, log_total = attention(place, query, key_value)
    (mixed,) = stage([o_block, grads], mixed)
    mixed = mixed.reshape(2 * HALF, HEADS * HD)
    *parts, o_full = project_out(place, o_block.result, mixed)
    grad_pieces = grads.result
    sums = Flow(scatter_steps(parts))
    for _ in range(4):
        stage([sums])
    hidden = inputs + sums.result
    scale_two = lax.rsqrt(jnp.mean(hidden * hidden, axis=-1, keepdims=True) + eps)
    normed = Flow(gather_steps((hidden * scale_two).astype(BF16)))
    for _ in range(4):
        stage([normed])
    normed_pieces = normed.result

    activation, act_t, gate_t, up_t, *parts, down_full = feed_forward(place, normed_pieces, grad_pieces, ff_all)
    sums = Flow(scatter_steps(parts))
    (act_t,) = stage([sums], act_t)
    down_terms = ff_terms(down_kernel, place, grad_pieces, (act_t,), FFL, "down_terms")
    down_terms, gate_t = stage([sums], down_terms, gate_t)
    down_sum = lax.psum_scatter(down_terms, "x", scatter_dimension=0, tiled=True)[0]
    gate_up_terms = ff_terms(gate_up_kernel, place, normed_pieces, (gate_t, up_t), 2 * FFL, "gate_up_terms")
    (gate_up_terms,) = stage([sums], gate_up_terms)
    gate_up_sum = lax.psum_scatter(gate_up_terms, "x", scatter_dimension=0, tiled=True)[0]
    stage([sums])

    grad_normed_two = sums.result
    mean_two = jnp.mean(grad_normed_two * hidden, axis=-1, keepdims=True)
    grad_hidden = (
        out_grad[0].astype(F32)
        + scale_two * grad_normed_two
        - hidden * (scale_two * scale_two * scale_two) * mean_two
    )
    hidden_grads = Flow(gather_steps(grad_hidden.astype(BF16)))
    (activation,) = stage([hidden_grads], activation)
    down_parts = project(activation, down_full)
    down_parts = stage([hidden_grads], *down_parts)
    result = Flow(scatter_steps(down_parts))
    stage([hidden_grads, result])
    stage([hidden_grads])

    grad_mixed, output_terms = grad_of_mixed(place, hidden_grads.result, o_full, mixed)
    grad_mixed, output_terms = stage([result], grad_mixed, output_terms)
    output_sums = Flow(attention_steps(output_terms))
    grad_query, grad_earlier, grad_own = attention_back(
        place, query, key_value, grad_mixed.reshape(2, HALF, HEADS * HD), log_total
    )
    grad_query, grad_earlier, grad_own = stage([result, output_sums], grad_query, grad_earlier, grad_own)
    later = lax.ppermute(grad_earlier, "zlo", [(1, 0)])
    later, grad_query = stage([result, output_sums], later, grad_query)
    *parts, grad_t = qkv_back(grad_query, grad_own, later, cosine, sine, scale_all, qkv_full)
    sums = Flow(scatter_steps(parts))
    (grad_t,) = stage([sums, output_sums], grad_t)
    qkv_term = qkv_terms(place, x_pieces, grad_t)
    qkv_term, down_sum = stage([sums, output_sums], qkv_term, down_sum)
    down = Flow(down_steps(down_sum))
    qkv_sums = Flow(attention_steps(qkv_term))
    (gate_up_sum,) = stage([sums, qkv_sums, down, output_sums], gate_up_sum)
    gate_up = Flow(gate_up_steps(gate_up_sum))
    stage([sums, output_sums, qkv_sums, down, gate_up])
    grad_normed = sums.result
    mean_one = jnp.mean(grad_normed * inputs, axis=-1, keepdims=True)
    input_grad = (
        grad_hidden
        + scale_one * grad_normed
        - inputs * (scale_one * scale_one * scale_one) * mean_one
    )
    input_grad = input_grad.astype(BF16)
    rest = [gate_up, qkv_sums, down, output_sums]
    while any(flow.result is None for flow in rest):
        stage(rest)

    output_grad = lax.all_to_all(output_sums.result.reshape(16, B, B), FSDP, 0, 0, tiled=True)
    output_grad = output_grad.transpose(1, 0, 2).reshape(B, D).astype(F32)
    sums = qkv_sums.result
    query_grad = sums[:, :, : HEADS * HD].reshape(D, B).T.astype(F32)
    key_grad = jnp.sum(sums[:, :, HEADS * HD : (HEADS + 1) * HD].astype(F32), axis=1)
    key_grad = key_grad.reshape(KV * HD, B).T
    value_grad = jnp.sum(sums[:, :, (HEADS + 1) * HD :].astype(F32), axis=1)
    value_grad = value_grad.reshape(KV * HD, B).T
    attn_gain_grad = (
        jnp.sum(query_grad * w_query.astype(F32), axis=1)
        + jnp.sum(key_grad * w_key.astype(F32), axis=1)
        + jnp.sum(value_grad * w_value.astype(F32), axis=1)
    )
    gain_two = mlp_gain[:, None]
    gate_grad, gate_gain = finish_hidden(place, [p[0] for p in gate_up.result], w_gate, gain_two)
    up_grad, up_gain = finish_hidden(place, [p[1] for p in gate_up.result], w_up, gain_two)
    down_grad = finish_down(place, down.result)
    one = attn_gain[:, None]
    return (
        (hidden + result.result).astype(BF16)[None],
        input_grad[None],
        attn_gain_grad,
        query_grad * one,
        key_grad * one,
        value_grad * one,
        output_grad,
        (gate_gain + up_gain)[:, 0],
        gate_grad,
        up_grad,
        down_grad,
    )


def solution(mesh):
    split = Mesh(mesh.devices.reshape(2, 4, 2, 4, 2), AXES)
    tokens = P(FSDP, SEQ, None)
    rows = P(FSDP, None)
    gain = P(FSDP)
    in_specs = (
        tokens, P(FSDP, SEQ), gain, rows, rows, rows, rows, gain, rows, rows, rows, tokens,
    )
    out_specs = (tokens, tokens, gain, rows, rows, rows, rows, gain, rows, rows, rows)
    return jax.shard_map(
        on_device, mesh=split, in_specs=in_specs, out_specs=out_specs, check_vma=False
    )
```

```python
import jax
import jax.numpy as jnp
from jax import lax
from jax.experimental import pallas as pl
from jax.experimental.pallas import tpu as pltpu
from jax.sharding import Mesh
from jax.sharding import PartitionSpec as P

H = 32
KV = 4
HD = 64
D = 2048
FF = 5632
B = 128
HALF = 512
HEADS = 4
FFL = 704
PIECE = 88

eps = 1e-05
theta = 10000.0
F32 = jnp.float32
BF16 = jnp.bfloat16
AXES = ("zlo", "y", "zhi", "x", "core")
FSDP = ("zhi", "x", "core")
SEQ = ("zlo", "y")


def matmul(left, right):
    return jnp.dot(left, right, preferred_element_type=F32)


def times_transposed(left, right):
    return lax.dot_general(left, right, (((1,), (1,)), ((), ())), preferred_element_type=F32)


def outer_sum(left, right):
    return lax.dot_general(left, right, (((0,), (0,)), ((), ())), preferred_element_type=F32)


def shift(value, axis, by):
    if axis == "z":
        at = [2 * (z % 2) + z // 2 for z in range(4)]
        return lax.ppermute(value, ("zlo", "zhi"), [(at[z], at[(z + by) % 4]) for z in range(4)])
    size = lax.axis_size(axis)
    return lax.ppermute(value, axis, [(i, (i + by) % size) for i in range(size)])


def swap_core(value):
    return shift(value, "core", 1)


def small_gather(block, axis):
    return shift(block, axis, -1), shift(block, axis, 2), shift(block, axis, 1)


def tie(*values):
    return lax.optimization_barrier(values)


def add(left, right):
    return left.astype(F32) + right.astype(F32)


def along_y(value):
    pairs = []
    for i in range(4):
        pairs.append((2 * i, 2 * ((i + 1) % 4)))
        pairs.append((2 * i + 1, 2 * ((i + 3) % 4) + 1))
    return lax.ppermute(value, ("y", "core"), pairs)


def send_half(got):
    core = lax.axis_index("core")
    return lax.dynamic_slice_in_dim(got, core * (B // 2), B // 2, 1)


FLIPPED = (0, 0, 1, 0, 1)
LENGTHS = (B, B, B, B // 2, B // 2)


def put_tokens(refs, rows_ref, sems, start):
    lanes = pl.ds(0, rows_ref.shape[1])
    copies = []
    row = 0
    for s in range(2):
        for ref, flip, length in zip(refs, FLIPPED, LENGTHS):
            copies.append(
                pltpu.make_async_copy(
                    ref.at[s ^ flip, :, lanes], rows_ref.at[pl.ds(row, length)], sems.at[start + len(copies)]
                )
            )
            row += length
    return copies


TILE = 256
WIDE = D + B
VMEM_LIMIT = 56 * 2**20
ANYWHERE = pl.BlockSpec(memory_space=pl.ANY)


def params(*kinds):
    return pltpu.CompilerParams(dimension_semantics=kinds or None, vmem_limit_bytes=VMEM_LIMIT)


def cost(flops, megabytes):
    return pl.CostEstimate(flops=flops, bytes_accessed=int(megabytes * 2**20), transcendentals=0)


def shaped(*shape, kind=BF16):
    return jax.ShapeDtypeStruct(shape, kind)


PART_SPECS = [pl.BlockSpec((1, n, D), lambda i, *_: (i // 2, 0, 0)) for n in LENGTHS]
PART_SHAPES = [jax.ShapeDtypeStruct((2, n, D), BF16) for n in LENGTHS]


def put_parts(step, tile, refs):
    @pl.when(step % 2 == 0)
    def _():
        refs[0][0] = tile[:B]
        refs[1][0] = tile[B:]

    @pl.when(step % 2 == 1)
    def _():
        refs[2][0] = tile[:B]
        refs[3][0] = tile[B : B + B // 2]
        refs[4][0] = tile[B + B // 2 :]


def turned(values):
    lane = lax.broadcasted_iota(jnp.int32, values.shape, 1) % HD
    return jnp.where(lane < HD // 2, -pltpu.roll(values, 2 * HD - HD // 2, 1), pltpu.roll(values, HD // 2, 1))


def lane_block(zhi, x, core):
    return pl.ds(pl.multiple_of((zhi * 8 + x * 2 + core) * B, B), B)


def put_columns(place, refs, into, sems, start):
    copies = []
    for ref, by, first in zip(refs, (0, 1, 2, 2, 3), (0, 0, 0, 1, 0)):
        for i in range(ref.shape[0]):
            for core in range(2):
                lanes = lane_block(first + i, (place[3] + by) % 4, core)
                copies.append(
                    pltpu.make_async_copy(ref.at[i, core], into.at[:, lanes], sems.at[start + len(copies)])
                )
    return copies


def prepare_qkv_kernel(place, q_mine, q_other, w_key, w_value, gain, mine_ref, other_ref, k_rows, v_rows):
    scale = gain[...]
    k_rows[...] = (w_key[...].astype(F32) * scale).T
    v_rows[...] = (w_value[...].astype(F32) * scale).T
    rows = pl.ds(pl.multiple_of(place[1] * HD, HD), HD)
    for source, out in ((q_mine, mine_ref), (q_other, other_ref)):
        out[: HEADS * HD] = (source[...].astype(F32) * scale).T.astype(BF16)
        out[HEADS * HD : (HEADS + 1) * HD] = k_rows[rows].astype(BF16)
        out[(HEADS + 1) * HD :] = v_rows[rows].astype(BF16)


QKV = (HEADS + 2) * HD


def prepare_qkv(place, w_query, w_key, w_value, gain):
    whole = lambda *shape: pl.BlockSpec(shape, lambda i, p: (0,) * len(shape))
    return pl.pallas_call(
        prepare_qkv_kernel,
        grid_spec=pltpu.PrefetchScalarGridSpec(
            num_scalar_prefetch=1,
            grid=(1,),
            in_specs=[
                pl.BlockSpec((B, HEADS * HD), lambda i, p: (0, 2 * p[1] + p[2])),
                pl.BlockSpec((B, HEADS * HD), lambda i, p: (0, 2 * p[1] + 1 - p[2])),
                whole(B, KV * HD), whole(B, KV * HD), whole(B, 1),
            ],
            out_specs=[whole(QKV, B), whole(QKV, B)],
            scratch_shapes=[pltpu.VMEM((KV * HD, B), F32), pltpu.VMEM((KV * HD, B), F32)],
        ),
        out_shape=[shaped(QKV, B), shaped(QKV, B)],
        compiler_params=params("arbitrary"),
        cost_estimate=cost(0, 1),
        name="prepare_qkv",
    )(place, w_query, w_query, w_key, w_value, gain)


def prepare_ff_kernel(place, w_gate, w_up, w_down, gain, mine_ref, other_ref, down_ref, picked, rows, down_rows, sems):
    zlo, y, core = place[0], place[1], place[2]
    down = pltpu.make_async_copy(
        w_down.at[:, pl.ds(pl.multiple_of(zlo * (D // 2), D // 2), D // 2)], down_rows, sems.at[1]
    )
    down.start()

    @pl.when(zlo == 0)
    def _():
        copy = pltpu.make_async_copy(w_gate, picked, sems.at[0])
        copy.start()
        copy.wait()

    @pl.when(zlo == 1)
    def _():
        copy = pltpu.make_async_copy(w_up, picked, sems.at[0])
        copy.start()
        copy.wait()

    scale = gain[...]
    for i in range(FF // B):
        rows[i * B : (i + 1) * B] = (picked[:, i * B : (i + 1) * B].astype(F32) * scale).T
    for which, out in ((core, mine_ref), (1 - core, other_ref)):
        slabs = []
        for zx in range(8):
            at = pl.multiple_of(zx * 2 * 4 * PIECE + which * 4 * PIECE + y * PIECE, 8)
            slabs.append(rows[pl.ds(at, PIECE)])
        out[...] = jnp.concatenate(slabs, axis=0).astype(BF16)
    down.wait()
    for t in range(8):
        rows[t * 4 * PIECE : (t + 1) * 4 * PIECE] = down_rows[:, t * B : (t + 1) * B].astype(F32)
    slabs = [rows[pl.ds(pl.multiple_of(t * 4 * PIECE + y * PIECE, 8), PIECE)] for t in range(8)]
    down_ref[...] = jnp.concatenate(slabs, axis=0).astype(BF16)


def prepare_ff(place, w_gate, w_up, w_down, gain):
    return pl.pallas_call(
        prepare_ff_kernel,
        grid_spec=pltpu.PrefetchScalarGridSpec(
            num_scalar_prefetch=1,
            grid=(1,),
            in_specs=[ANYWHERE, ANYWHERE, ANYWHERE, pl.BlockSpec((B, 1), lambda i, p: (0, 0))],
            out_specs=[pl.BlockSpec((FFL, B), lambda i, p: (0, 0))] * 3,
            scratch_shapes=[
                pltpu.VMEM((B, FF), BF16),
                pltpu.VMEM((FF, B), F32),
                pltpu.VMEM((4 * PIECE, D // 2), BF16),
                pltpu.SemaphoreType.DMA((2,)),
            ],
        ),
        out_shape=[shaped(FFL, B)] * 3,
        compiler_params=params("arbitrary"),
        cost_estimate=cost(0, 6),
        name="prepare_ff",
    )(place, w_gate, w_up, w_down, gain)


def project_qkv_kernel(*refs):
    place, x_refs, w_refs = refs[0], refs[1:6], refs[6:11]
    query_ref, kv_ref, scale_ref, cosine_ref, sine_ref, w_out, rows, weights, sems = refs[11:]
    step = pl.program_id(0)
    tokens = put_tokens(x_refs, rows, sems, 0)
    columns = put_columns(place, w_refs, weights, sems, 10)
    back = pltpu.make_async_copy(weights, w_out, sems.at[26])

    @pl.when(step == 0)
    def _():
        for copy in columns + tokens:
            copy.start()
        for copy in columns:
            copy.wait()
        back.start()
        for copy in tokens:
            copy.wait()

    at = pl.ds(pl.multiple_of(step * TILE, TILE), TILE)
    tile = rows[at, :D]
    wide = tile.astype(F32)
    scale = lax.rsqrt(jnp.mean(wide * wide, axis=-1, keepdims=True) + eps)
    scale_ref[...] = scale
    pre = times_transposed(tile, weights[...]) * scale
    tables = rows[at, D:].astype(F32)
    tables = tables + pltpu.roll(tables, B - HD // 2, 1)
    cosine = jnp.concatenate([tables[:, : HD // 2]] * 4, axis=1)
    sine = jnp.concatenate([tables[:, HD : HD + HD // 2]] * 4, axis=1)
    cosine_ref[...] = cosine
    sine_ref[...] = sine
    for i in range(2):
        part = pre[:, i * 2 * HD : (i + 1) * 2 * HD]
        part = (part * cosine + turned(part) * sine).astype(BF16) * HD ** (-0.5)
        query_ref[0, 2 * i] = part[:, :HD]
        query_ref[0, 2 * i + 1] = part[:, HD:]
    part = pre[:, HEADS * HD :]
    lane = lax.broadcasted_iota(jnp.int32, part.shape, 1)
    kv_ref[0] = jnp.where(lane < HD, part * cosine + turned(part) * sine, part).astype(BF16)

    @pl.when(step == 3)
    def _():
        back.wait()


def project_qkv(place, x_pieces, w_pieces):
    tile = lambda lanes: pl.BlockSpec((TILE, lanes), lambda i, p: (i, 0))
    return pl.pallas_call(
        project_qkv_kernel,
        grid_spec=pltpu.PrefetchScalarGridSpec(
            num_scalar_prefetch=1,
            grid=(4,),
            in_specs=[ANYWHERE] * 10,
            out_specs=[
                pl.BlockSpec((1, HEADS, TILE, HD), lambda i, p: (i // 2, 0, i % 2, 0)),
                pl.BlockSpec((1, TILE, 2 * HD), lambda i, p: (i // 2, i % 2, 0)),
                tile(1), tile(2 * HD), tile(2 * HD),
                ANYWHERE,
            ],
            scratch_shapes=[
                pltpu.VMEM((2 * HALF, WIDE), BF16),
                pltpu.VMEM((QKV, D), BF16),
                pltpu.SemaphoreType.DMA((27,)),
            ],
        ),
        out_shape=[
            shaped(2, HEADS, HALF, HD), shaped(2, HALF, 2 * HD), shaped(2 * HALF, 1, kind=F32),
            shaped(2 * HALF, 2 * HD, kind=F32), shaped(2 * HALF, 2 * HD, kind=F32), shaped(QKV, D),
        ],
        compiler_params=params("arbitrary"),
        cost_estimate=cost(2 * 2 * HALF * QKV * D, 8),
        name="project_qkv",
    )(place, *x_pieces, *w_pieces)


def project_out_kernel(*refs):
    place, w_refs, left_ref = refs[0], refs[1:6], refs[6]
    parts, w_out, weights, sems = refs[7:12], refs[12], refs[13], refs[14]
    step = pl.program_id(0)
    columns = put_columns(place, w_refs, weights, sems, 0)
    back = pltpu.make_async_copy(weights, w_out, sems.at[16])

    @pl.when(step == 0)
    def _():
        for copy in columns:
            copy.start()
        for copy in columns:
            copy.wait()
        back.start()

    put_parts(step, matmul(left_ref[...], weights[...]).astype(BF16), parts)

    @pl.when(step == 3)
    def _():
        back.wait()


def project_out(place, w_pieces, mixed):
    return pl.pallas_call(
        project_out_kernel,
        grid_spec=pltpu.PrefetchScalarGridSpec(
            num_scalar_prefetch=1,
            grid=(4,),
            in_specs=[ANYWHERE] * 5 + [pl.BlockSpec((TILE, HEADS * HD), lambda i, p: (i, 0))],
            out_specs=PART_SPECS + [ANYWHERE],
            scratch_shapes=[pltpu.VMEM((HEADS * HD, D), BF16), pltpu.SemaphoreType.DMA((17,))],
        ),
        out_shape=PART_SHAPES + [shaped(HEADS * HD, D)],
        compiler_params=params("arbitrary"),
        cost_estimate=cost(2 * 2 * HALF * HEADS * HD * D, 7),
        name="project_out",
    )(place, *w_pieces, mixed)


def project_kernel(left_ref, weight_ref, *parts):
    put_parts(pl.program_id(0), matmul(left_ref[...], weight_ref[...]).astype(BF16), parts)


def project(left, weight):
    depth = left.shape[1]
    return pl.pallas_call(
        project_kernel,
        grid=(4,),
        in_specs=[pl.BlockSpec((TILE, depth), lambda i: (i, 0)), pl.BlockSpec((depth, D), lambda i: (0, 0))],
        out_specs=PART_SPECS,
        out_shape=PART_SHAPES,
        compiler_params=params("arbitrary"),
        cost_estimate=cost(2 * 2 * HALF * depth * D, 8),
        name="project",
    )(left, weight)


def grad_mixed_kernel(*refs):
    grad_refs, weight_ref = refs[1:6], refs[6]
    grad_mixed_ref, rows, sems = refs[7:]
    copies = put_tokens(grad_refs, rows, sems, 0)
    for copy in copies:
        copy.start()
    for copy in copies:
        copy.wait()
    for i in range(4):
        tile = rows[i * TILE : (i + 1) * TILE, :]
        grad_mixed_ref[i * TILE : (i + 1) * TILE, :] = times_transposed(tile, weight_ref[...]).astype(BF16)


def put_term(place, left, rows, term_ref):
    def one(i, carry):
        term = matmul(left, rows[:, pl.ds(pl.multiple_of(i * 4 * B, 4 * B), 4 * B)]).astype(BF16)
        for j in range(2):
            zx = 2 * i + j
            by = (zx % 4 + 4 - place[3]) % 4
            term_ref[by, zx // 4, 0] = term[:, 2 * j * B : (2 * j + 1) * B]
            term_ref[by, zx // 4, 1] = term[:, (2 * j + 1) * B : (2 * j + 2) * B]
        return carry

    lax.fori_loop(0, 4, one, 0)


def grad_of_mixed(place, grad_pieces, weight):
    whole = lambda *shape: pl.BlockSpec(shape, lambda i, p: (0,) * len(shape))
    rows = HEADS * HD
    return pl.pallas_call(
        grad_mixed_kernel,
        grid_spec=pltpu.PrefetchScalarGridSpec(
            num_scalar_prefetch=1,
            grid=(1,),
            in_specs=[ANYWHERE] * 5 + [whole(rows, D)],
            out_specs=whole(2 * HALF, rows),
            scratch_shapes=[pltpu.VMEM((2 * HALF, D), BF16), pltpu.SemaphoreType.DMA((10,))],
        ),
        out_shape=shaped(2 * HALF, rows),
        compiler_params=params("arbitrary"),
        cost_estimate=cost(2 * 2 * HALF * rows * D, 6),
        name="grad_of_mixed",
    )(place, *grad_pieces, weight)


def qkv_back_kernel(grad_q_ref, own_ref, later_ref, cosine_ref, sine_ref, scale_ref, weight_ref, *outs):
    parts, turned_ref = outs[:5], outs[5]
    cosine, sine = cosine_ref[...], sine_ref[...]
    lane = lax.broadcasted_iota(jnp.int32, cosine.shape, 1)
    pieces = []
    for i in range(2):
        part = grad_q_ref[0, :, i * 2 * HD : (i + 1) * 2 * HD]
        pieces.append(part * cosine - turned(part * sine))
    part = own_ref[0] + later_ref[0].astype(F32)
    pieces.append(jnp.where(lane < HD, part * cosine - turned(part * sine), part))
    grad_pre = jnp.concatenate(pieces, axis=1)
    put_parts(pl.program_id(0), matmul(grad_pre.astype(BF16), weight_ref[...]).astype(BF16), parts)
    turned_ref[...] = (grad_pre * scale_ref[...]).T.astype(BF16)


def qkv_back(grad_query, own, later, cosine, sine, scale, weight):
    tile = lambda lanes: pl.BlockSpec((TILE, lanes), lambda i: (i, 0))
    half = lambda lanes: pl.BlockSpec((1, TILE, lanes), lambda i: (i // 2, i % 2, 0))
    return pl.pallas_call(
        qkv_back_kernel,
        grid=(4,),
        in_specs=[
            half(HEADS * HD), half(2 * HD), half(2 * HD), tile(2 * HD), tile(2 * HD), tile(1),
            pl.BlockSpec((QKV, D), lambda i: (0, 0)),
        ],
        out_specs=PART_SPECS + [pl.BlockSpec((QKV, TILE), lambda i: (0, i))],
        out_shape=PART_SHAPES + [shaped(QKV, 2 * HALF)],
        compiler_params=params("arbitrary"),
        cost_estimate=cost(2 * 2 * HALF * QKV * D, 9),
        name="qkv_back",
    )(grad_query, own, later, cosine, sine, scale, weight)


def attention_term_kernel(*refs):
    place, token_refs, left_ref, term_ref, rows, sems = refs[0], refs[1:6], *refs[6:]
    copies = put_tokens(token_refs, rows, sems, 0)
    for copy in copies:
        copy.start()
    left = left_ref[...]
    if left.shape[0] == 2 * HALF:
        left = left.T
    for copy in copies:
        copy.wait()
    put_term(place, left, rows, term_ref)


def attention_terms(place, pieces, left, name):
    whole = lambda *shape: pl.BlockSpec(shape, lambda i, p: (0,) * len(shape))
    rows = min(left.shape)
    return pl.pallas_call(
        attention_term_kernel,
        grid_spec=pltpu.PrefetchScalarGridSpec(
            num_scalar_prefetch=1,
            grid=(1,),
            in_specs=[ANYWHERE] * 5 + [whole(*left.shape)],
            out_specs=whole(4, 2, 2, rows, B),
            scratch_shapes=[pltpu.VMEM((2 * HALF, D), BF16), pltpu.SemaphoreType.DMA((10,))],
        ),
        out_shape=shaped(4, 2, 2, rows, B),
        compiler_params=params("arbitrary"),
        cost_estimate=cost(2 * 2 * HALF * rows * D, 7),
        name=name,
    )(place, *pieces, left)


def token_places(at, y, core):
    step = 1 - 2 * core
    block = jnp.where(
        at < B, y, jnp.where(at < 2 * B, y + 4 - step, jnp.where(at < 3 * B, y + 4 + step, y + 2))
    )
    row = at % B
    row = jnp.where(at < 3 * B, row, (row + core * (B // 2)) % B)
    return (block % 4) * B + row


def set_bias(place_ref, bias_ref):
    zlo, y, core = place_ref[0], place_ref[1], place_ref[2]
    key_at = token_places(lax.broadcasted_iota(jnp.int32, (HALF, 1), 0), y, core)
    query_at = token_places(lax.broadcasted_iota(jnp.int32, (1, HALF), 1), y, core)
    bias_ref[:HALF, :] = jnp.broadcast_to(jnp.where(zlo == 1, 0.0, -1e30), (HALF, HALF))
    bias_ref[HALF:, :] = jnp.where(key_at <= query_at, 0.0, -1e30)


def attention_kernel(place_ref, query_ref, kv_ref, mixed_ref, log_ref, bias_ref):
    @pl.when(pl.program_id(0) == 0)
    def _():
        set_bias(place_ref, bias_ref)

    key, value = kv_ref[0, :, :HD], kv_ref[0, :, HD:]
    for head in range(HEADS):
        scores = times_transposed(key, query_ref[0, head]) + bias_ref[...]
        top = jnp.max(scores, axis=0, keepdims=True)
        weights = jnp.exp(scores - top)
        total = jnp.sum(weights, axis=0, keepdims=True)
        low = (weights * (1.0 / total)).astype(BF16)
        mixed_ref[0, :, head * HD : (head + 1) * HD] = outer_sum(value, low).T.astype(BF16)
        log_ref[0, head] = top + jnp.log(total)


def attention_back_kernel(
    place_ref, query_ref, kv_ref, grad_ref, log_ref, grad_query_ref, earlier_ref, own_ref, bias_ref
):
    @pl.when(pl.program_id(0) == 0)
    def _():
        set_bias(place_ref, bias_ref)

    key, value = kv_ref[0, :, :HD], kv_ref[0, :, HD:]
    grad_key = jnp.zeros((2 * HALF, HD), F32)
    grad_value = jnp.zeros((2 * HALF, HD), F32)
    for head in range(HEADS):
        lanes = slice(head * HD, (head + 1) * HD)
        query, grad = query_ref[0, head], grad_ref[0, :, lanes]
        weights = jnp.exp(times_transposed(key, query) + bias_ref[...] - log_ref[0, head])
        grad_weights = times_transposed(value, grad)
        delta = jnp.sum(weights * grad_weights, axis=0, keepdims=True)
        grad_scores = (weights * (grad_weights - delta)).astype(BF16)
        grad_query_ref[0, :, lanes] = outer_sum(key, grad_scores).T * HD ** (-0.5)
        grad_key += matmul(grad_scores, query)
        grad_value += matmul(weights.astype(BF16), grad)
    total = jnp.concatenate([grad_key, grad_value], axis=1)
    earlier_ref[0] = total[:HALF].astype(BF16)
    own_ref[0] = total[HALF:]


def sequence_block(*tail):
    return pl.BlockSpec((1,) + tail, lambda s, place: (s,) + (0,) * len(tail))


def attention_call(kernel, in_specs, out_specs, out_shape, flops, name):
    return pl.pallas_call(
        kernel,
        grid_spec=pltpu.PrefetchScalarGridSpec(
            num_scalar_prefetch=1,
            grid=(2,),
            in_specs=in_specs,
            out_specs=out_specs,
            scratch_shapes=[pltpu.VMEM((2 * HALF, HALF), F32)],
        ),
        out_shape=out_shape,
        compiler_params=params("arbitrary"),
        cost_estimate=cost(flops * 8 * 2 * HALF * HALF * HD * 2, 4),
        name=name,
    )


def attention(place, query, kv):
    return attention_call(
        attention_kernel,
        [sequence_block(HEADS, HALF, HD), sequence_block(2 * HALF, 2 * HD)],
        [sequence_block(HALF, HEADS * HD), sequence_block(HEADS, 1, HALF)],
        [shaped(2, HALF, HEADS * HD), shaped(2, HEADS, 1, HALF, kind=F32)],
        2,
        "attention",
    )(place, query, kv)


def attention_back(place, query, kv, grad, log_total):
    return attention_call(
        attention_back_kernel,
        [
            sequence_block(HEADS, HALF, HD), sequence_block(2 * HALF, 2 * HD),
            sequence_block(HALF, HEADS * HD), sequence_block(HEADS, 1, HALF),
        ],
        [sequence_block(HALF, HEADS * HD), sequence_block(HALF, 2 * HD), sequence_block(HALF, 2 * HD)],
        [
            shaped(2, HALF, HEADS * HD, kind=F32),
            shaped(2, HALF, 2 * HD),
            shaped(2, HALF, 2 * HD, kind=F32),
        ],
        5,
        "attention_back",
    )(place, query, kv, grad, log_total)


def own_rows(rows_all, y, core, per):
    return lax.dynamic_slice_in_dim(rows_all, (2 * y + core) * per, per, 0)


def feed_forward_kernel(*refs):
    place, token_refs, grad_refs, ff_ref = refs[0], refs[1:6], refs[6:11], refs[11]
    act_ref, act_t, gate_t, up_t = refs[12:16]
    parts, down_out = refs[16:21], refs[21]
    rows_h, rows_g, gate_up, down, slabs, sems = refs[22:]
    step = pl.program_id(0)
    tokens = put_tokens(token_refs, rows_h, sems, 0)
    grads = put_tokens(grad_refs, rows_g, sems, 10)
    weights, loads = [], []
    for x in range(4):
        for by in range(4):
            z = (2 * place[4] + place[0] + by) % 4
            zhi, zlo = z // 2, z % 2
            for core in range(2):
                weights.append(
                    pltpu.make_async_copy(
                        ff_ref.at[x, by, pl.ds(core * FFL, FFL)],
                        gate_up.at[zlo, :, lane_block(zhi, x, core)],
                        sems.at[20 + len(weights)],
                    )
                )
            loads.append(
                pltpu.make_async_copy(
                    ff_ref.at[x, by, pl.ds(2 * FFL, FFL)], slabs.at[zlo, zhi * 4 + x], sems.at[52 + len(loads)]
                )
            )
    back = pltpu.make_async_copy(down, down_out, sems.at[68])

    @pl.when(step == 0)
    def _():
        for copy in tokens + weights + loads + grads:
            copy.start()
        for copy in tokens + weights:
            copy.wait()

    rows = pl.ds(pl.multiple_of(step * TILE, TILE), TILE)
    normed = rows_h[rows, :]
    gate_pre = times_transposed(normed, gate_up[0])
    upward = times_transposed(normed, gate_up[1])

    @pl.when(step == 0)
    def _():
        for copy in loads:
            copy.wait()

        def put(q, carry):
            for half in range(2):
                for p in range(4):
                    one = slabs[half, 2 * q, 2 * p * PIECE : 2 * (p + 1) * PIECE, :].astype(F32)
                    two = slabs[half, 2 * q + 1, 2 * p * PIECE : 2 * (p + 1) * PIECE, :].astype(F32)
                    lane = (half * 8 + 2 * p) * B
                    rows = pl.ds(pl.multiple_of(q * 2 * PIECE, 16), 2 * PIECE)
                    down[rows, lane : lane + B] = jnp.concatenate([one[:PIECE], two[:PIECE]], axis=0).astype(BF16)
                    down[rows, lane + B : lane + 2 * B] = jnp.concatenate(
                        [one[PIECE:], two[PIECE:]], axis=0
                    ).astype(BF16)
            return carry

        lax.fori_loop(0, 4, put, 0)
        back.start()
        for copy in grads:
            copy.wait()

    grad_act = times_transposed(rows_g[rows, :], down[...])
    sigmoid = 1.0 / (1.0 + jnp.exp(-gate_pre))
    silu = gate_pre * sigmoid
    activation = silu * upward
    grad_up = grad_act * silu
    grad_gate = grad_act * upward * (sigmoid * (1.0 + gate_pre * (1.0 - sigmoid)))
    part = matmul(grad_gate.astype(BF16), gate_up[0]) + matmul(grad_up.astype(BF16), gate_up[1])
    put_parts(step, part.astype(BF16), parts)
    act_ref[...] = activation.astype(BF16)
    act_t[...] = activation.T.astype(BF16)
    gate_t[...] = grad_gate.T.astype(BF16)
    up_t[...] = grad_up.T.astype(BF16)

    @pl.when(step == 3)
    def _():
        back.wait()


def feed_forward(place, tokens, grads, ff_all):
    turned_spec = pl.BlockSpec((FFL, TILE), lambda i, p: (0, i))
    turned_shape = shaped(FFL, 2 * HALF)
    return pl.pallas_call(
        feed_forward_kernel,
        grid_spec=pltpu.PrefetchScalarGridSpec(
            num_scalar_prefetch=1,
            grid=(4,),
            in_specs=[ANYWHERE] * 11,
            out_specs=[pl.BlockSpec((TILE, FFL), lambda i, p: (i, 0))] + [turned_spec] * 3 + PART_SPECS + [ANYWHERE],
            scratch_shapes=[
                pltpu.VMEM((2 * HALF, D), BF16),
                pltpu.VMEM((2 * HALF, D), BF16),
                pltpu.VMEM((2, FFL, D), BF16),
                pltpu.VMEM((FFL, D), BF16),
                pltpu.VMEM((2, 8, FFL, B), BF16),
                pltpu.SemaphoreType.DMA((69,)),
            ],
        ),
        out_shape=[shaped(2 * HALF, FFL)] + [turned_shape] * 3 + PART_SHAPES + [shaped(FFL, D)],
        compiler_params=params("arbitrary"),
        cost_estimate=cost(2 * 5 * 2 * HALF * FFL * D, 32),
        name="feed_forward",
    )(place, *tokens, *grads, ff_all)


def along_z(place, zhi, zlo):
    return (2 * zhi + zlo + 4 - 2 * place[4] - place[0]) % 4


def gate_up_kernel(*refs):
    place, token_refs, gate_t, up_t, out_ref, rows, sems = refs[0], refs[1:6], *refs[6:]
    step = pl.program_id(0)
    copies = put_tokens(token_refs, rows, sems, 0)

    @pl.when(step == 0)
    def _():
        for copy in copies:
            copy.start()
        for copy in copies:
            copy.wait()

    normed = rows[:, pl.ds(pl.multiple_of(step * 4 * B, 4 * B), 4 * B)]
    for matrix, left in ((0, gate_t), (1, up_t)):
        term = matmul(left[...], normed).astype(BF16)
        for j in range(2):
            zx = 2 * step + j
            by = along_z(place, zx // 4, matrix)
            out_ref[zx % 4, by, 0:FFL, :] = term[:, 2 * j * B : (2 * j + 1) * B]
            out_ref[zx % 4, by, FFL:, :] = term[:, (2 * j + 1) * B : (2 * j + 2) * B]


def down_kernel(*refs):
    place, grad_refs, act_t, out_ref, rows, sems = refs[0], refs[1:6], *refs[6:]
    step = pl.program_id(0)
    copies = put_tokens(grad_refs, rows, sems, 0)

    @pl.when(step == 0)
    def _():
        for copy in copies:
            copy.start()
        for copy in copies:
            copy.wait()

    term = matmul(act_t[...], rows[:, pl.ds(pl.multiple_of(step * 4 * B, 4 * B), 4 * B)])
    for j in range(2):
        half, p = step // 2, (2 * step + j) % 4
        at = pl.ds(pl.multiple_of(p * 2 * PIECE, 16), 2 * PIECE)
        for zx in range(8):
            slab = term[zx * PIECE : (zx + 1) * PIECE]
            low, high = slab[:, 2 * j * B : (2 * j + 1) * B], slab[:, (2 * j + 1) * B : (2 * j + 2) * B]
            slab = jnp.concatenate([low, high], axis=0).astype(BF16)
            out_ref[zx % 4, along_z(place, zx // 4, half), at, :] = slab


def ff_terms(kernel, place, pieces, lefts, rows, name):
    whole = pl.BlockSpec((FFL, 2 * HALF), lambda i, p: (0, 0))
    return pl.pallas_call(
        kernel,
        grid_spec=pltpu.PrefetchScalarGridSpec(
            num_scalar_prefetch=1,
            grid=(4,),
            in_specs=[ANYWHERE] * 5 + [whole] * len(lefts),
            out_specs=pl.BlockSpec((4, 4, rows, B), lambda i, p: (0, 0, 0, 0)),
            scratch_shapes=[pltpu.VMEM((2 * HALF, D), BF16), pltpu.SemaphoreType.DMA((10,))],
        ),
        out_shape=shaped(4, 4, rows, B),
        compiler_params=params("arbitrary"),
        cost_estimate=cost(2 * len(lefts) * 2 * HALF * FFL * D, 8 + 4 * len(lefts)),
        name=name,
    )(place, *pieces, *lefts)


def finish_hidden_kernel(*refs):
    place, piece_refs, weight_ref, gain_ref, out_ref, gain_out, rows = refs[0], refs[1:5], *refs[5:]
    y = place[1]
    for ref, by in zip(piece_refs, (0, 1, 2, 3)):
        at_y = (y + by) % 4
        for core in range(2):
            slab = ref[core].astype(F32)
            for zx in range(8):
                at = pl.multiple_of((2 * zx + core) * 4 * PIECE + at_y * PIECE, 8)
                rows[pl.ds(at, PIECE)] = slab[zx * PIECE : (zx + 1) * PIECE]
    gain = gain_ref[...]
    total = jnp.zeros((B, 1), F32)
    for i in range(FF // B):
        lanes = slice(i * B, (i + 1) * B)
        block = rows[lanes].T
        total = total + jnp.sum(block * weight_ref[:, lanes].astype(F32), axis=1, keepdims=True)
        out_ref[:, lanes] = block * gain
    gain_out[...] = total


def finish_hidden(place, pieces, weight, gain):
    whole = lambda *shape: pl.BlockSpec(shape, lambda i, p: (0,) * len(shape))
    return pl.pallas_call(
        finish_hidden_kernel,
        grid_spec=pltpu.PrefetchScalarGridSpec(
            num_scalar_prefetch=1,
            grid=(1,),
            in_specs=[whole(2, FFL, B)] * 4 + [whole(B, FF), whole(B, 1)],
            out_specs=[whole(B, FF), whole(B, 1)],
            scratch_shapes=[pltpu.VMEM((FF, B), F32)],
        ),
        out_shape=[shaped(B, FF, kind=F32), shaped(B, 1, kind=F32)],
        compiler_params=params("arbitrary"),
        cost_estimate=cost(0, 6),
        name="finish_hidden",
    )(place, *pieces, weight, gain)


def finish_down_kernel(place, *refs):
    piece_refs, out_ref = refs[:4], refs[4]
    for ref, by in zip(piece_refs, range(4)):
        rows = pl.ds(pl.multiple_of((place[1] + by) % 4 * PIECE, 8), PIECE)
        for half in range(2):
            slab = ref[half].astype(F32)
            for t in range(8):
                lane = (half * 8 + t) * B
                out_ref[rows, lane : lane + B] = slab[t * PIECE : (t + 1) * PIECE]


def finish_down(place, pieces):
    whole = lambda *shape: pl.BlockSpec(shape, lambda i, p: (0,) * len(shape))
    return pl.pallas_call(
        finish_down_kernel,
        grid_spec=pltpu.PrefetchScalarGridSpec(
            num_scalar_prefetch=1,
            grid=(1,),
            in_specs=[whole(2, FFL, B)] * 4,
            out_specs=whole(4 * PIECE, D),
            scratch_shapes=[],
        ),
        out_shape=shaped(4 * PIECE, D, kind=F32),
        compiler_params=params("arbitrary"),
        cost_estimate=cost(0, 5),
        name="finish_down",
    )(place, *pieces)


class Flow:
    def __init__(self, steps):
        self.steps, self.result, self.sent = steps, None, None
        self.move(None)

    def move(self, arrived):
        try:
            self.sent = self.steps.send(arrived)
        except StopIteration as end:
            self.sent, self.result = (), end.value


def stage(flows, *values):
    flows = [flow for flow in flows if flow.result is None]
    sizes = [len(flow.sent) for flow in flows]
    leaves, tree = jax.tree.flatten(values)
    tied = tie(*[v for flow in flows for v in flow.sent], *leaves)
    for flow, size in zip(flows, sizes):
        flow.move(tied[:size])
        tied = tied[size:]
    return jax.tree.unflatten(tree, tied)


def gather_steps(block):
    (other,) = yield (swap_core(block),)
    pair = jnp.stack([block, other])
    (got,) = yield (along_y(pair),)
    far, swapped = yield (along_y(send_half(got)), swap_core(got))
    (far_swapped,) = yield (swap_core(far),)
    return pair, got, swapped, far, far_swapped


def scatter_steps(parts):
    core = lax.axis_index("core")
    first, behind, ahead, far, far_other = parts
    far_got, behind_got, first_got = yield (swap_core(far_other), swap_core(behind), swap_core(first[1]))
    far = add(far, far_got[::-1]).astype(BF16)
    (low,) = yield (along_y(far),)
    ahead = add(ahead, behind_got[::-1])
    mine = lax.dynamic_slice_in_dim(ahead, core * (B // 2), B // 2, 1) + low.astype(F32)
    ahead = lax.dynamic_update_slice_in_dim(ahead, mine, core * (B // 2), 1).astype(BF16)
    (got,) = yield (along_y(ahead),)
    (last,) = yield (swap_core(got[1]),)
    return add(first[0], first_got) + got[0].astype(F32) + last.astype(F32)


def ring_gather_steps(block, axis):
    half = block.shape[0] // 2
    before, after = yield (shift(block, axis, 1), shift(block, axis, -1))
    low, high = yield (shift(before[:half], axis, 1), shift(after[half:], axis, -1))
    return block, after, low, high, before


def ring_scatter_steps(parts, axis):
    half = parts[2].shape[0] // 2
    low, high = yield (shift(parts[2][:half], axis, 1), shift(parts[2][half:], axis, -1))
    after = jnp.concatenate([add(parts[1][:half], low).astype(BF16), parts[1][half:]], axis=0)
    before = jnp.concatenate([parts[3][:half], add(parts[3][half:], high).astype(BF16)], axis=0)
    from_before, from_after = yield (shift(after, axis, 1), shift(before, axis, -1))
    return add(parts[0], from_before) + from_after.astype(F32)


def on_device(
    layer_input,
    positions,
    attn_gain,
    w_query,
    w_key,
    w_value,
    w_output,
    mlp_gain,
    w_gate,
    w_up,
    w_down,
    out_grad,
):
    zlo, y, zhi, x, core = (lax.axis_index(axis) for axis in AXES)
    place = jnp.stack([zlo, y, core, x, zhi]).astype(jnp.int32)

    def by_core(mine, got):
        return jnp.where(core == 0, jnp.stack([mine, got]), jnp.stack([got, mine]))

    def by_zlo(mine, got):
        return jnp.where(zlo == 0, jnp.stack([mine, got]), jnp.stack([got, mine]))

    def by_zhi(mine, got):
        return jnp.where(zhi == 0, jnp.stack([mine, got]), jnp.stack([got, mine]))

    def trio(mine, other, axis):
        across = lax.ppermute(other, (axis, "core"), [(i, 3 - i) for i in range(4)])
        return shift(mine, axis, 1), swap_core(other), across

    def column_steps(mine, other):
        there, here, across = yield trio(mine, other, "zhi")
        column = by_zhi(by_core(mine, here), by_core(there, across))
        return (yield from ring_gather_steps(column, "x"))

    def hidden_steps(mine, got, down):
        piece = jnp.concatenate([by_core(mine, got).reshape(2 * FFL, B), down], axis=0)
        pieces = yield from ring_gather_steps(piece, "z")
        return jnp.concatenate(pieces, axis=0).reshape(4, 3 * FFL, B)

    def of_core(pair, other=False):
        return lax.dynamic_index_in_dim(pair, 1 - core if other else core, 0, keepdims=False)

    def whole_ring(pieces):
        own, after, low, high, before = pieces
        return own, after, jnp.concatenate([low, high], axis=0), before

    def attention_steps(terms):
        column = yield from ring_scatter_steps([terms[i] for i in range(4)], "x")
        keep = lax.dynamic_index_in_dim(column, zhi, 0, keepdims=False)
        send = lax.dynamic_index_in_dim(column, 1 - zhi, 0, keepdims=False).astype(BF16)
        (got,) = yield (shift(send, "zhi", 1),)
        pair = (keep + got.astype(F32)).astype(BF16)
        mine, other = of_core(pair), of_core(pair, True)
        there, here, across = yield trio(mine, other, "zlo")
        own = by_core(add(mine, there), add(here, across)).astype(BF16)
        ring = yield small_gather(own, "y")
        return jnp.roll(jnp.stack([own, *ring]), y, axis=0)

    def gate_up_steps(sums):
        own = yield from ring_scatter_steps([sums[i] for i in range(4)], "z")
        pair = own.astype(BF16).reshape(2, FFL, B)
        mine, other = of_core(pair), of_core(pair, True)
        there, here, across = yield trio(mine, other, "zlo")
        pieces = yield from ring_gather_steps(by_zlo(by_core(mine, here), by_core(there, across)), "y")
        return whole_ring(pieces)

    def down_steps(sums):
        own = yield from ring_scatter_steps([sums[i] for i in range(4)], "z")
        own = own.astype(BF16)
        (got,) = yield (shift(own, "zlo", 1),)
        pieces = yield from ring_gather_steps(by_zlo(own, got), "y")
        return whole_ring(pieces)

    def all_to_all_steps(value):
        (got,) = yield (lax.all_to_all(value, FSDP, 0, 0, tiled=True),)
        return got

    x_low = layer_input[0]
    frequency = theta ** (-jnp.arange(0, HD, 2).astype(F32) / HD)
    angles = positions[0].astype(F32)[:, None] * frequency
    tables = []
    for table in (jnp.cos(angles), jnp.sin(angles)):
        high = lax.reduce_precision(table, 8, 7)
        tables += [high.astype(BF16), (table - high).astype(BF16)]
    tokens = Flow(gather_steps(jnp.concatenate([x_low, *tables], axis=1)))
    grads = Flow(gather_steps(out_grad[0]))
    mine, other = prepare_qkv(place, w_query, w_key, w_value, attn_gain[:, None])
    mine, other, gain_two, w_out = stage([tokens], mine, other, mlp_gain[:, None], w_output)

    qkv = Flow(column_steps(mine, other))
    output_rows = Flow(all_to_all_steps(w_out.reshape(B, 16, B).transpose(1, 0, 2)))
    ff_mine, ff_other, ff_down = prepare_ff(place, w_gate, w_up, w_down, gain_two)
    ff_got = swap_core(ff_other)
    ff_mine, ff_got, ff_down = stage([tokens, qkv], ff_mine, ff_got, ff_down)

    hidden_rows = Flow(hidden_steps(ff_mine, ff_got, ff_down))
    inputs = x_low.astype(F32)
    scale_one = lax.rsqrt(jnp.mean(inputs * inputs, axis=-1, keepdims=True) + eps)
    (scale_one,) = stage([tokens, qkv, hidden_rows, output_rows], scale_one)

    o_rows = output_rows.result.reshape(D, B)
    stage([tokens, qkv, hidden_rows, grads])

    o_block = Flow(
        column_steps(own_rows(o_rows, y, core, HEADS * HD), own_rows(o_rows, y, 1 - core, HEADS * HD))
    )
    x_pieces = tokens.result
    ff_all = lax.all_gather(hidden_rows.result, "x", axis=0, tiled=False)
    query, key_value, scale_all, cosine, sine, qkv_full = project_qkv(place, x_pieces, qkv.result)
    query, key_value = stage([o_block], query, key_value)

    earlier = lax.ppermute(key_value, "zlo", [(0, 1)])
    query, key_value, earlier = stage([grads, o_block], query, key_value, earlier)

    key_value = jnp.concatenate([earlier, key_value], axis=1)
    mixed, log_total = attention(place, query, key_value)
    (mixed,) = stage([o_block, grads], mixed)
    mixed = mixed.reshape(2 * HALF, HEADS * HD)
    *parts, o_full = project_out(place, o_block.result, mixed)
    sums = Flow(scatter_steps(parts))
    stage([sums, grads])
    grad_pieces = grads.result
    for _ in range(3):
        stage([sums])
    hidden = inputs + sums.result
    scale_two = lax.rsqrt(jnp.mean(hidden * hidden, axis=-1, keepdims=True) + eps)
    normed = Flow(gather_steps((hidden * scale_two).astype(BF16)))
    for _ in range(4):
        stage([normed])
    normed_pieces = normed.result

    activation, act_t, gate_t, up_t, *parts, down_full = feed_forward(place, normed_pieces, grad_pieces, ff_all)
    sums = Flow(scatter_steps(parts))
    (act_t,) = stage([sums], act_t)
    down_terms = ff_terms(down_kernel, place, grad_pieces, (act_t,), FFL, "down_terms")
    down_terms, gate_t = stage([sums], down_terms, gate_t)
    down_sum = lax.psum_scatter(down_terms, "x", scatter_dimension=0, tiled=True)[0]
    gate_up_terms = ff_terms(gate_up_kernel, place, normed_pieces, (gate_t, up_t), 2 * FFL, "gate_up_terms")
    (gate_up_terms,) = stage([sums], gate_up_terms)
    gate_up_sum = lax.psum_scatter(gate_up_terms, "x", scatter_dimension=0, tiled=True)[0]
    stage([sums])

    grad_normed_two = sums.result
    mean_two = jnp.mean(grad_normed_two * hidden, axis=-1, keepdims=True)
    grad_hidden = (
        out_grad[0].astype(F32)
        + scale_two * grad_normed_two
        - hidden * (scale_two * scale_two * scale_two) * mean_two
    )
    hidden_grads = Flow(gather_steps(grad_hidden.astype(BF16)))
    (activation,) = stage([hidden_grads], activation)
    down_parts = project(activation, down_full)
    down_parts = stage([hidden_grads], *down_parts)
    result = Flow(scatter_steps(down_parts))
    stage([hidden_grads, result])
    (down_sum,) = stage([hidden_grads], down_sum)

    hidden_grad_pieces = hidden_grads.result
    down = Flow(down_steps(down_sum))
    grad_mixed = grad_of_mixed(place, hidden_grad_pieces, o_full)
    (grad_mixed,) = stage([result, down], grad_mixed)
    grad_query, grad_earlier, grad_own = attention_back(
        place, query, key_value, grad_mixed.reshape(2, HALF, HEADS * HD), log_total
    )
    grad_query, grad_earlier, grad_own, mixed = stage([result, down], grad_query, grad_earlier, grad_own, mixed)
    later = lax.ppermute(grad_earlier, "zlo", [(1, 0)])
    output_terms = attention_terms(place, hidden_grad_pieces, mixed, "output_terms")
    later, grad_query, output_terms = stage([result, down], later, grad_query, output_terms)
    output_sums = Flow(attention_steps(output_terms))
    *parts, grad_t = qkv_back(grad_query, grad_own, later, cosine, sine, scale_all, qkv_full)
    *parts, grad_t = stage([output_sums, down], *parts, grad_t)
    sums = Flow(scatter_steps(parts))
    qkv_term = attention_terms(place, x_pieces, grad_t, "qkv_terms")
    (qkv_term,) = stage([sums, output_sums, down], qkv_term)
    qkv_sums = Flow(attention_steps(qkv_term))
    (gate_up_sum,) = stage([sums, output_sums, qkv_sums], gate_up_sum)
    gate_up = Flow(gate_up_steps(gate_up_sum))
    stage([sums, output_sums, qkv_sums, gate_up])
    stage([sums, output_sums, qkv_sums, gate_up])
    grad_normed = sums.result
    mean_one = jnp.mean(grad_normed * inputs, axis=-1, keepdims=True)
    input_grad = (
        grad_hidden
        + scale_one * grad_normed
        - inputs * (scale_one * scale_one * scale_one) * mean_one
    )
    input_grad = input_grad.astype(BF16)
    output_grad = lax.all_to_all(output_sums.result.reshape(16, B, B), FSDP, 0, 0, tiled=True)
    rest = [gate_up, qkv_sums]
    while any(flow.result is None for flow in rest):
        stage(rest)

    output_grad = output_grad.transpose(1, 0, 2).reshape(B, D).astype(F32)
    sums = qkv_sums.result
    query_grad = sums[:, :, : HEADS * HD].reshape(D, B).T.astype(F32)
    key_grad = jnp.sum(sums[:, :, HEADS * HD : (HEADS + 1) * HD].astype(F32), axis=1)
    key_grad = key_grad.reshape(KV * HD, B).T
    value_grad = jnp.sum(sums[:, :, (HEADS + 1) * HD :].astype(F32), axis=1)
    value_grad = value_grad.reshape(KV * HD, B).T
    attn_gain_grad = (
        jnp.sum(query_grad * w_query.astype(F32), axis=1)
        + jnp.sum(key_grad * w_key.astype(F32), axis=1)
        + jnp.sum(value_grad * w_value.astype(F32), axis=1)
    )
    gain_two = mlp_gain[:, None]
    gate_grad, gate_gain = finish_hidden(place, [p[0] for p in gate_up.result], w_gate, gain_two)
    up_grad, up_gain = finish_hidden(place, [p[1] for p in gate_up.result], w_up, gain_two)
    down_grad = finish_down(place, down.result)
    one = attn_gain[:, None]
    return (
        (hidden + result.result).astype(BF16)[None],
        input_grad[None],
        attn_gain_grad,
        query_grad * one,
        key_grad * one,
        value_grad * one,
        output_grad,
        (gate_gain + up_gain)[:, 0],
        gate_grad,
        up_grad,
        down_grad,
    )


def solution(mesh):
    split = Mesh(mesh.devices.reshape(2, 4, 2, 4, 2), AXES)
    tokens = P(FSDP, SEQ, None)
    rows = P(FSDP, None)
    gain = P(FSDP)
    in_specs = (
        tokens, P(FSDP, SEQ), gain, rows, rows, rows, rows, gain, rows, rows, rows, tokens,
    )
    out_specs = (tokens, tokens, gain, rows, rows, rows, rows, gain, rows, rows, rows)
    return jax.shard_map(
        on_device, mesh=split, in_specs=in_specs, out_specs=out_specs, check_vma=False
    )
```

```python
import jax
import jax.numpy as jnp
from jax import lax
from jax.experimental import pallas as pl
from jax.experimental.pallas import tpu as pltpu
from jax.sharding import Mesh
from jax.sharding import PartitionSpec as P

H = 32
KV = 4
HD = 64
D = 2048
FF = 5632
B = 128
HALF = 512
HEADS = 4
FFL = 704
PIECE = 88

eps = 1e-05
theta = 10000.0
F32 = jnp.float32
BF16 = jnp.bfloat16
AXES = ("zlo", "y", "zhi", "x", "core")
FSDP = ("zhi", "x", "core")
SEQ = ("zlo", "y")


def matmul(left, right):
    return jnp.dot(left, right, preferred_element_type=F32)


def times_transposed(left, right):
    return lax.dot_general(left, right, (((1,), (1,)), ((), ())), preferred_element_type=F32)


def outer_sum(left, right):
    return lax.dot_general(left, right, (((0,), (0,)), ((), ())), preferred_element_type=F32)


def shift(value, axis, by):
    if axis == "z":
        at = [2 * (z % 2) + z // 2 for z in range(4)]
        return lax.ppermute(value, ("zlo", "zhi"), [(at[z], at[(z + by) % 4]) for z in range(4)])
    size = lax.axis_size(axis)
    return lax.ppermute(value, axis, [(i, (i + by) % size) for i in range(size)])


def swap_core(value):
    return shift(value, "core", 1)


def small_gather(block, axis):
    return shift(block, axis, -1), shift(block, axis, 2), shift(block, axis, 1)


def tie(*values):
    return lax.optimization_barrier(values)


def add(left, right):
    return left.astype(F32) + right.astype(F32)


def along_y(value):
    pairs = []
    for i in range(4):
        pairs.append((2 * i, 2 * ((i + 1) % 4)))
        pairs.append((2 * i + 1, 2 * ((i + 3) % 4) + 1))
    return lax.ppermute(value, ("y", "core"), pairs)


def send_half(got):
    core = lax.axis_index("core")
    return lax.dynamic_slice_in_dim(got, core * (B // 2), B // 2, 1)


FLIPPED = (0, 0, 1, 0, 1)
LENGTHS = (B, B, B, B // 2, B // 2)


def put_tokens(refs, rows_ref, sems, start):
    lanes = pl.ds(0, rows_ref.shape[1])
    copies = []
    row = 0
    for s in range(2):
        for ref, flip, length in zip(refs, FLIPPED, LENGTHS):
            copies.append(
                pltpu.make_async_copy(
                    ref.at[s ^ flip, :, lanes], rows_ref.at[pl.ds(row, length)], sems.at[start + len(copies)]
                )
            )
            row += length
    return copies


TILE = 256
WIDE = D + B
VMEM_LIMIT = 56 * 2**20
ANYWHERE = pl.BlockSpec(memory_space=pl.ANY)


def params(*kinds):
    return pltpu.CompilerParams(dimension_semantics=kinds or None, vmem_limit_bytes=VMEM_LIMIT)


def cost(flops, megabytes):
    return pl.CostEstimate(flops=flops, bytes_accessed=int(megabytes * 2**20), transcendentals=0)


def shaped(*shape, kind=BF16):
    return jax.ShapeDtypeStruct(shape, kind)


PART_SPECS = [pl.BlockSpec((1, n, D), lambda i, *_: (i // 2, 0, 0)) for n in LENGTHS]
PART_SHAPES = [jax.ShapeDtypeStruct((2, n, D), BF16) for n in LENGTHS]


def put_parts(step, tile, refs):
    @pl.when(step % 2 == 0)
    def _():
        refs[0][0] = tile[:B]
        refs[1][0] = tile[B:]

    @pl.when(step % 2 == 1)
    def _():
        refs[2][0] = tile[:B]
        refs[3][0] = tile[B : B + B // 2]
        refs[4][0] = tile[B + B // 2 :]


def turned(values):
    lane = lax.broadcasted_iota(jnp.int32, values.shape, 1) % HD
    return jnp.where(lane < HD // 2, -pltpu.roll(values, 2 * HD - HD // 2, 1), pltpu.roll(values, HD // 2, 1))


def lane_block(zhi, x, core):
    return pl.ds(pl.multiple_of((zhi * 8 + x * 2 + core) * B, B), B)


def put_columns(place, refs, at, into, sems, start):
    rows = pl.ds(at, into.shape[0])
    copies = []
    for ref, by, first in zip(refs, (0, 1, 2, 2, 3), (0, 0, 0, 1, 0)):
        for i in range(ref.shape[0]):
            for core in range(2):
                lanes = lane_block(first + i, (place[3] + by) % 4, core)
                copies.append(
                    pltpu.make_async_copy(ref.at[i, core, rows], into.at[:, lanes], sems.at[start + len(copies)])
                )
    return copies


def prepare_qkv_kernel(place, q_mine, q_other, w_key, w_value, gain, mine_ref, other_ref, k_rows, v_rows):
    scale = gain[...]
    k_rows[...] = (w_key[...].astype(F32) * scale).T
    v_rows[...] = (w_value[...].astype(F32) * scale).T
    rows = pl.ds(pl.multiple_of(place[1] * HD, HD), HD)
    for source, out in ((q_mine, mine_ref), (q_other, other_ref)):
        out[: HEADS * HD] = (source[...].astype(F32) * scale).T.astype(BF16)
        out[HEADS * HD : (HEADS + 1) * HD] = k_rows[rows].astype(BF16)
        out[(HEADS + 1) * HD :] = v_rows[rows].astype(BF16)


QKV = (HEADS + 2) * HD


def prepare_qkv(place, w_query, w_key, w_value, gain):
    whole = lambda *shape: pl.BlockSpec(shape, lambda i, p: (0,) * len(shape))
    return pl.pallas_call(
        prepare_qkv_kernel,
        grid_spec=pltpu.PrefetchScalarGridSpec(
            num_scalar_prefetch=1,
            grid=(1,),
            in_specs=[
                pl.BlockSpec((B, HEADS * HD), lambda i, p: (0, 2 * p[1] + p[2])),
                pl.BlockSpec((B, HEADS * HD), lambda i, p: (0, 2 * p[1] + 1 - p[2])),
                whole(B, KV * HD), whole(B, KV * HD), whole(B, 1),
            ],
            out_specs=[whole(QKV, B), whole(QKV, B)],
            scratch_shapes=[pltpu.VMEM((KV * HD, B), F32), pltpu.VMEM((KV * HD, B), F32)],
        ),
        out_shape=[shaped(QKV, B), shaped(QKV, B)],
        compiler_params=params("arbitrary"),
        cost_estimate=cost(0, 1),
        name="prepare_qkv",
    )(place, w_query, w_query, w_key, w_value, gain)


def prepare_ff_kernel(place, w_gate, w_up, w_down, gain, mine_ref, other_ref, down_ref, picked, rows, down_rows, sems):
    zlo, y, core = place[0], place[1], place[2]
    down = pltpu.make_async_copy(
        w_down.at[:, pl.ds(pl.multiple_of(zlo * (D // 2), D // 2), D // 2)], down_rows, sems.at[1]
    )
    down.start()

    @pl.when(zlo == 0)
    def _():
        copy = pltpu.make_async_copy(w_gate, picked, sems.at[0])
        copy.start()
        copy.wait()

    @pl.when(zlo == 1)
    def _():
        copy = pltpu.make_async_copy(w_up, picked, sems.at[0])
        copy.start()
        copy.wait()

    scale = gain[...]
    for i in range(FF // B):
        rows[i * B : (i + 1) * B] = (picked[:, i * B : (i + 1) * B].astype(F32) * scale).T
    for which, out in ((core, mine_ref), (1 - core, other_ref)):
        slabs = []
        for zx in range(8):
            at = pl.multiple_of(zx * 2 * 4 * PIECE + which * 4 * PIECE + y * PIECE, 8)
            slabs.append(rows[pl.ds(at, PIECE)])
        out[...] = jnp.concatenate(slabs, axis=0).astype(BF16)
    down.wait()
    for t in range(8):
        rows[t * 4 * PIECE : (t + 1) * 4 * PIECE] = down_rows[:, t * B : (t + 1) * B].astype(F32)
    slabs = [rows[pl.ds(pl.multiple_of(t * 4 * PIECE + y * PIECE, 8), PIECE)] for t in range(8)]
    down_ref[...] = jnp.concatenate(slabs, axis=0).astype(BF16)


def prepare_ff(place, w_gate, w_up, w_down, gain):
    return pl.pallas_call(
        prepare_ff_kernel,
        grid_spec=pltpu.PrefetchScalarGridSpec(
            num_scalar_prefetch=1,
            grid=(1,),
            in_specs=[ANYWHERE, ANYWHERE, ANYWHERE, pl.BlockSpec((B, 1), lambda i, p: (0, 0))],
            out_specs=[pl.BlockSpec((FFL, B), lambda i, p: (0, 0))] * 3,
            scratch_shapes=[
                pltpu.VMEM((B, FF), BF16),
                pltpu.VMEM((FF, B), F32),
                pltpu.VMEM((4 * PIECE, D // 2), BF16),
                pltpu.SemaphoreType.DMA((2,)),
            ],
        ),
        out_shape=[shaped(FFL, B)] * 3,
        compiler_params=params("arbitrary"),
        cost_estimate=cost(0, 6),
        name="prepare_ff",
    )(place, w_gate, w_up, w_down, gain)


def project_qkv_kernel(*refs):
    place, x_refs, w_refs = refs[0], refs[1:6], refs[6:11]
    query_ref, kv_ref, scale_ref, cosine_ref, sine_ref, w_out, rows, weights, sems = refs[11:]
    step = pl.program_id(0)
    tokens = put_tokens(x_refs, rows, sems, 0)
    columns = put_columns(place, w_refs, 0, weights, sems, 10)
    back = pltpu.make_async_copy(weights, w_out, sems.at[26])

    @pl.when(step == 0)
    def _():
        for copy in columns + tokens:
            copy.start()
        for copy in columns:
            copy.wait()
        back.start()
        for copy in tokens:
            copy.wait()

    at = pl.ds(pl.multiple_of(step * TILE, TILE), TILE)
    tile = rows[at, :D]
    wide = tile.astype(F32)
    scale = lax.rsqrt(jnp.mean(wide * wide, axis=-1, keepdims=True) + eps)
    scale_ref[...] = scale
    pre = times_transposed(tile, weights[...]) * scale
    tables = rows[at, D:].astype(F32)
    tables = tables + pltpu.roll(tables, B - HD // 2, 1)
    cosine = jnp.concatenate([tables[:, : HD // 2]] * 4, axis=1)
    sine = jnp.concatenate([tables[:, HD : HD + HD // 2]] * 4, axis=1)
    cosine_ref[...] = cosine
    sine_ref[...] = sine
    for i in range(2):
        part = pre[:, i * 2 * HD : (i + 1) * 2 * HD]
        part = (part * cosine + turned(part) * sine).astype(BF16) * HD ** (-0.5)
        query_ref[0, 2 * i] = part[:, :HD]
        query_ref[0, 2 * i + 1] = part[:, HD:]
    part = pre[:, HEADS * HD :]
    lane = lax.broadcasted_iota(jnp.int32, part.shape, 1)
    kv_ref[0] = jnp.where(lane < HD, part * cosine + turned(part) * sine, part).astype(BF16)

    @pl.when(step == 3)
    def _():
        back.wait()


def project_qkv(place, x_pieces, w_pieces):
    tile = lambda lanes: pl.BlockSpec((TILE, lanes), lambda i, p: (i, 0))
    return pl.pallas_call(
        project_qkv_kernel,
        grid_spec=pltpu.PrefetchScalarGridSpec(
            num_scalar_prefetch=1,
            grid=(4,),
            in_specs=[ANYWHERE] * 10,
            out_specs=[
                pl.BlockSpec((1, HEADS, TILE, HD), lambda i, p: (i // 2, 0, i % 2, 0)),
                pl.BlockSpec((1, TILE, 2 * HD), lambda i, p: (i // 2, i % 2, 0)),
                tile(1), tile(2 * HD), tile(2 * HD),
                ANYWHERE,
            ],
            scratch_shapes=[
                pltpu.VMEM((2 * HALF, WIDE), BF16),
                pltpu.VMEM((QKV, D), BF16),
                pltpu.SemaphoreType.DMA((27,)),
            ],
        ),
        out_shape=[
            shaped(2, HEADS, HALF, HD), shaped(2, HALF, 2 * HD), shaped(2 * HALF, 1, kind=F32),
            shaped(2 * HALF, 2 * HD, kind=F32), shaped(2 * HALF, 2 * HD, kind=F32), shaped(QKV, D),
        ],
        compiler_params=params("arbitrary"),
        cost_estimate=cost(2 * 2 * HALF * QKV * D, 8),
        name="project_qkv",
    )(place, *x_pieces, *w_pieces)


def project_out_kernel(*refs):
    place, w_refs, left_ref = refs[0], refs[1:6], refs[6]
    parts, w_out, weights, sems = refs[7:12], refs[12], refs[13], refs[14]
    step = pl.program_id(0)
    columns = put_columns(place, w_refs, QKV, weights, sems, 0)
    back = pltpu.make_async_copy(weights, w_out, sems.at[16])

    @pl.when(step == 0)
    def _():
        for copy in columns:
            copy.start()
        for copy in columns:
            copy.wait()
        back.start()

    put_parts(step, matmul(left_ref[...], weights[...]).astype(BF16), parts)

    @pl.when(step == 3)
    def _():
        back.wait()


def project_out(place, w_pieces, mixed):
    return pl.pallas_call(
        project_out_kernel,
        grid_spec=pltpu.PrefetchScalarGridSpec(
            num_scalar_prefetch=1,
            grid=(4,),
            in_specs=[ANYWHERE] * 5 + [pl.BlockSpec((TILE, HEADS * HD), lambda i, p: (i, 0))],
            out_specs=PART_SPECS + [ANYWHERE],
            scratch_shapes=[pltpu.VMEM((HEADS * HD, D), BF16), pltpu.SemaphoreType.DMA((17,))],
        ),
        out_shape=PART_SHAPES + [shaped(HEADS * HD, D)],
        compiler_params=params("arbitrary"),
        cost_estimate=cost(2 * 2 * HALF * HEADS * HD * D, 7),
        name="project_out",
    )(place, *w_pieces, mixed)


def project_kernel(left_ref, weight_ref, *parts):
    put_parts(pl.program_id(0), matmul(left_ref[...], weight_ref[...]).astype(BF16), parts)


def project(left, weight):
    depth = left.shape[1]
    return pl.pallas_call(
        project_kernel,
        grid=(4,),
        in_specs=[pl.BlockSpec((TILE, depth), lambda i: (i, 0)), pl.BlockSpec((depth, D), lambda i: (0, 0))],
        out_specs=PART_SPECS,
        out_shape=PART_SHAPES,
        compiler_params=params("arbitrary"),
        cost_estimate=cost(2 * 2 * HALF * depth * D, 8),
        name="project",
    )(left, weight)


def grad_mixed_kernel(*refs):
    grad_refs, weight_ref = refs[1:6], refs[6]
    grad_mixed_ref, rows, sems = refs[7:]
    copies = put_tokens(grad_refs, rows, sems, 0)
    for copy in copies:
        copy.start()
    for copy in copies:
        copy.wait()
    for i in range(4):
        tile = rows[i * TILE : (i + 1) * TILE, :]
        grad_mixed_ref[i * TILE : (i + 1) * TILE, :] = times_transposed(tile, weight_ref[...]).astype(BF16)


def put_term(place, left, rows, term_ref):
    def one(i, carry):
        term = matmul(left, rows[:, pl.ds(pl.multiple_of(i * 4 * B, 4 * B), 4 * B)]).astype(BF16)
        for j in range(2):
            zx = 2 * i + j
            by = (zx % 4 + 4 - place[3]) % 4
            term_ref[by, zx // 4, 0, : left.shape[0]] = term[:, 2 * j * B : (2 * j + 1) * B]
            term_ref[by, zx // 4, 1, : left.shape[0]] = term[:, (2 * j + 1) * B : (2 * j + 2) * B]
        return carry

    lax.fori_loop(0, 4, one, 0)


def grad_of_mixed(place, grad_pieces, weight):
    whole = lambda *shape: pl.BlockSpec(shape, lambda i, p: (0,) * len(shape))
    rows = HEADS * HD
    return pl.pallas_call(
        grad_mixed_kernel,
        grid_spec=pltpu.PrefetchScalarGridSpec(
            num_scalar_prefetch=1,
            grid=(1,),
            in_specs=[ANYWHERE] * 5 + [whole(rows, D)],
            out_specs=whole(2 * HALF, rows),
            scratch_shapes=[pltpu.VMEM((2 * HALF, D), BF16), pltpu.SemaphoreType.DMA((10,))],
        ),
        out_shape=shaped(2 * HALF, rows),
        compiler_params=params("arbitrary"),
        cost_estimate=cost(2 * 2 * HALF * rows * D, 6),
        name="grad_of_mixed",
    )(place, *grad_pieces, weight)


def qkv_back_kernel(grad_q_ref, own_ref, later_ref, cosine_ref, sine_ref, scale_ref, weight_ref, *outs):
    parts, turned_ref = outs[:5], outs[5]
    cosine, sine = cosine_ref[...], sine_ref[...]
    lane = lax.broadcasted_iota(jnp.int32, cosine.shape, 1)
    pieces = []
    for i in range(2):
        part = grad_q_ref[0, :, i * 2 * HD : (i + 1) * 2 * HD]
        pieces.append(part * cosine - turned(part * sine))
    part = own_ref[0] + later_ref[0].astype(F32)
    pieces.append(jnp.where(lane < HD, part * cosine - turned(part * sine), part))
    grad_pre = jnp.concatenate(pieces, axis=1)
    put_parts(pl.program_id(0), matmul(grad_pre.astype(BF16), weight_ref[...]).astype(BF16), parts)
    turned_ref[...] = (grad_pre * scale_ref[...]).T.astype(BF16)


def qkv_back(grad_query, own, later, cosine, sine, scale, weight):
    tile = lambda lanes: pl.BlockSpec((TILE, lanes), lambda i: (i, 0))
    half = lambda lanes: pl.BlockSpec((1, TILE, lanes), lambda i: (i // 2, i % 2, 0))
    return pl.pallas_call(
        qkv_back_kernel,
        grid=(4,),
        in_specs=[
            half(HEADS * HD), half(2 * HD), half(2 * HD), tile(2 * HD), tile(2 * HD), tile(1),
            pl.BlockSpec((QKV, D), lambda i: (0, 0)),
        ],
        out_specs=PART_SPECS + [pl.BlockSpec((QKV, TILE), lambda i: (0, i))],
        out_shape=PART_SHAPES + [shaped(QKV, 2 * HALF)],
        compiler_params=params("arbitrary"),
        cost_estimate=cost(2 * 2 * HALF * QKV * D, 9),
        name="qkv_back",
    )(grad_query, own, later, cosine, sine, scale, weight)


def attention_term_kernel(*refs):
    place, token_refs, left_ref = refs[0], refs[1:6], refs[6]
    term_ref, rows, sems = refs[-3:]
    copies = put_tokens(token_refs, rows, sems, 0)
    for copy in copies:
        copy.start()
    left = left_ref[...]
    if left.shape[0] == 2 * HALF:
        left = left.T
    if len(refs) == 11:
        term_ref[:, :, :, left.shape[0] :] = refs[7][...]
    for copy in copies:
        copy.wait()
    put_term(place, left, rows, term_ref)


def attention_terms(place, pieces, left, name, *more):
    whole = lambda *shape: pl.BlockSpec(shape, lambda i, p: (0,) * len(shape))
    rows = min(left.shape)
    total = rows + sum(terms.shape[3] for terms in more)
    return pl.pallas_call(
        attention_term_kernel,
        grid_spec=pltpu.PrefetchScalarGridSpec(
            num_scalar_prefetch=1,
            grid=(1,),
            in_specs=[ANYWHERE] * 5 + [whole(*left.shape)] + [whole(*terms.shape) for terms in more],
            out_specs=whole(4, 2, 2, total, B),
            scratch_shapes=[pltpu.VMEM((2 * HALF, D), BF16), pltpu.SemaphoreType.DMA((10,))],
        ),
        out_shape=shaped(4, 2, 2, total, B),
        compiler_params=params("arbitrary"),
        cost_estimate=cost(2 * 2 * HALF * rows * D, 7),
        name=name,
    )(place, *pieces, left, *more)


def token_places(at, y, core):
    step = 1 - 2 * core
    block = jnp.where(
        at < B, y, jnp.where(at < 2 * B, y + 4 - step, jnp.where(at < 3 * B, y + 4 + step, y + 2))
    )
    row = at % B
    row = jnp.where(at < 3 * B, row, (row + core * (B // 2)) % B)
    return (block % 4) * B + row


def set_bias(place_ref, bias_ref):
    zlo, y, core = place_ref[0], place_ref[1], place_ref[2]
    key_at = token_places(lax.broadcasted_iota(jnp.int32, (HALF, 1), 0), y, core)
    query_at = token_places(lax.broadcasted_iota(jnp.int32, (1, HALF), 1), y, core)
    bias_ref[:HALF, :] = jnp.broadcast_to(jnp.where(zlo == 1, 0.0, -1e30), (HALF, HALF))
    bias_ref[HALF:, :] = jnp.where(key_at <= query_at, 0.0, -1e30)


def attention_kernel(place_ref, query_ref, kv_ref, mixed_ref, log_ref, bias_ref):
    @pl.when(pl.program_id(0) == 0)
    def _():
        set_bias(place_ref, bias_ref)

    key, value = kv_ref[0, :, :HD], kv_ref[0, :, HD:]
    for head in range(HEADS):
        scores = times_transposed(key, query_ref[0, head]) + bias_ref[...]
        top = jnp.max(scores, axis=0, keepdims=True)
        weights = jnp.exp(scores - top)
        total = jnp.sum(weights, axis=0, keepdims=True)
        low = (weights * (1.0 / total)).astype(BF16)
        mixed_ref[0, :, head * HD : (head + 1) * HD] = outer_sum(value, low).T.astype(BF16)
        log_ref[0, head] = top + jnp.log(total)


def attention_back_kernel(
    place_ref, query_ref, kv_ref, grad_ref, log_ref, grad_query_ref, earlier_ref, own_ref, bias_ref
):
    @pl.when(pl.program_id(0) == 0)
    def _():
        set_bias(place_ref, bias_ref)

    key, value = kv_ref[0, :, :HD], kv_ref[0, :, HD:]
    grad_key = jnp.zeros((2 * HALF, HD), F32)
    grad_value = jnp.zeros((2 * HALF, HD), F32)
    for head in range(HEADS):
        lanes = slice(head * HD, (head + 1) * HD)
        query, grad = query_ref[0, head], grad_ref[0, :, lanes]
        weights = jnp.exp(times_transposed(key, query) + bias_ref[...] - log_ref[0, head])
        grad_weights = times_transposed(value, grad)
        delta = jnp.sum(weights * grad_weights, axis=0, keepdims=True)
        grad_scores = (weights * (grad_weights - delta)).astype(BF16)
        grad_query_ref[0, :, lanes] = outer_sum(key, grad_scores).T * HD ** (-0.5)
        grad_key += matmul(grad_scores, query)
        grad_value += matmul(weights.astype(BF16), grad)
    total = jnp.concatenate([grad_key, grad_value], axis=1)
    earlier_ref[0] = total[:HALF].astype(BF16)
    own_ref[0] = total[HALF:]


def sequence_block(*tail):
    return pl.BlockSpec((1,) + tail, lambda s, place: (s,) + (0,) * len(tail))


def attention_call(kernel, in_specs, out_specs, out_shape, flops, name):
    return pl.pallas_call(
        kernel,
        grid_spec=pltpu.PrefetchScalarGridSpec(
            num_scalar_prefetch=1,
            grid=(2,),
            in_specs=in_specs,
            out_specs=out_specs,
            scratch_shapes=[pltpu.VMEM((2 * HALF, HALF), F32)],
        ),
        out_shape=out_shape,
        compiler_params=params("arbitrary"),
        cost_estimate=cost(flops * 8 * 2 * HALF * HALF * HD * 2, 4),
        name=name,
    )


def attention(place, query, kv):
    return attention_call(
        attention_kernel,
        [sequence_block(HEADS, HALF, HD), sequence_block(2 * HALF, 2 * HD)],
        [sequence_block(HALF, HEADS * HD), sequence_block(HEADS, 1, HALF)],
        [shaped(2, HALF, HEADS * HD), shaped(2, HEADS, 1, HALF, kind=F32)],
        2,
        "attention",
    )(place, query, kv)


def attention_back(place, query, kv, grad, log_total):
    return attention_call(
        attention_back_kernel,
        [
            sequence_block(HEADS, HALF, HD), sequence_block(2 * HALF, 2 * HD),
            sequence_block(HALF, HEADS * HD), sequence_block(HEADS, 1, HALF),
        ],
        [sequence_block(HALF, HEADS * HD), sequence_block(HALF, 2 * HD), sequence_block(HALF, 2 * HD)],
        [
            shaped(2, HALF, HEADS * HD, kind=F32),
            shaped(2, HALF, 2 * HD),
            shaped(2, HALF, 2 * HD, kind=F32),
        ],
        5,
        "attention_back",
    )(place, query, kv, grad, log_total)


def own_rows(rows_all, y, core, per):
    return lax.dynamic_slice_in_dim(rows_all, (2 * y + core) * per, per, 0)


def feed_forward_kernel(*refs):
    place, token_refs, grad_refs, ff_ref = refs[0], refs[1:6], refs[6:11], refs[11]
    act_ref, act_t, gate_t, up_t = refs[12:16]
    parts, down_out = refs[16:21], refs[21]
    rows_h, rows_g, gate_up, down, slabs, sems = refs[22:]
    step = pl.program_id(0)
    tokens = put_tokens(token_refs, rows_h, sems, 0)
    grads = put_tokens(grad_refs, rows_g, sems, 10)
    weights, loads = [], []
    for x in range(4):
        for by in range(4):
            z = (2 * place[4] + place[0] + by) % 4
            zhi, zlo = z // 2, z % 2
            for core in range(2):
                weights.append(
                    pltpu.make_async_copy(
                        ff_ref.at[x, by, pl.ds(core * FFL, FFL)],
                        gate_up.at[zlo, :, lane_block(zhi, x, core)],
                        sems.at[20 + len(weights)],
                    )
                )
            loads.append(
                pltpu.make_async_copy(
                    ff_ref.at[x, by, pl.ds(2 * FFL, FFL)], slabs.at[zlo, zhi * 4 + x], sems.at[52 + len(loads)]
                )
            )
    back = pltpu.make_async_copy(down, down_out, sems.at[68])

    @pl.when(step == 0)
    def _():
        for copy in tokens + weights + loads + grads:
            copy.start()
        for copy in tokens + weights:
            copy.wait()

    rows = pl.ds(pl.multiple_of(step * HALF, HALF), HALF)
    normed = rows_h[rows, :]
    gate_pre = times_transposed(normed, gate_up[0])
    upward = times_transposed(normed, gate_up[1])

    @pl.when(step == 0)
    def _():
        for copy in loads:
            copy.wait()

        def put(q, carry):
            for half in range(2):
                for p in range(4):
                    one = slabs[half, 2 * q, 2 * p * PIECE : 2 * (p + 1) * PIECE, :].astype(F32)
                    two = slabs[half, 2 * q + 1, 2 * p * PIECE : 2 * (p + 1) * PIECE, :].astype(F32)
                    lane = (half * 8 + 2 * p) * B
                    rows = pl.ds(pl.multiple_of(q * 2 * PIECE, 16), 2 * PIECE)
                    down[rows, lane : lane + B] = jnp.concatenate([one[:PIECE], two[:PIECE]], axis=0).astype(BF16)
                    down[rows, lane + B : lane + 2 * B] = jnp.concatenate(
                        [one[PIECE:], two[PIECE:]], axis=0
                    ).astype(BF16)
            return carry

        lax.fori_loop(0, 4, put, 0)
        back.start()
        for copy in grads:
            copy.wait()

    grad_act = times_transposed(rows_g[rows, :], down[...])
    sigmoid = 1.0 / (1.0 + jnp.exp(-gate_pre))
    silu = gate_pre * sigmoid
    activation = silu * upward
    grad_up = grad_act * silu
    grad_gate = grad_act * upward * (sigmoid * (1.0 + gate_pre * (1.0 - sigmoid)))
    part = matmul(grad_gate.astype(BF16), gate_up[0]) + matmul(grad_up.astype(BF16), gate_up[1])
    part = part.astype(BF16)
    row = 0
    for ref, length in zip(parts, LENGTHS):
        ref[0] = part[row : row + length]
        row += length
    act_ref[...] = activation.astype(BF16)
    act_t[...] = activation.T.astype(BF16)
    gate_t[...] = grad_gate.T.astype(BF16)
    up_t[...] = grad_up.T.astype(BF16)

    @pl.when(step == 1)
    def _():
        back.wait()


def feed_forward(place, tokens, grads, ff_all):
    turned_spec = pl.BlockSpec((FFL, HALF), lambda i, p: (0, i))
    turned_shape = shaped(FFL, 2 * HALF)
    return pl.pallas_call(
        feed_forward_kernel,
        grid_spec=pltpu.PrefetchScalarGridSpec(
            num_scalar_prefetch=1,
            grid=(2,),
            in_specs=[ANYWHERE] * 11,
            out_specs=[pl.BlockSpec((HALF, FFL), lambda i, p: (i, 0))]
            + [turned_spec] * 3
            + [pl.BlockSpec((1, n, D), lambda i, p: (i, 0, 0)) for n in LENGTHS]
            + [ANYWHERE],
            scratch_shapes=[
                pltpu.VMEM((2 * HALF, D), BF16),
                pltpu.VMEM((2 * HALF, D), BF16),
                pltpu.VMEM((2, FFL, D), BF16),
                pltpu.VMEM((FFL, D), BF16),
                pltpu.VMEM((2, 8, FFL, B), BF16),
                pltpu.SemaphoreType.DMA((69,)),
            ],
        ),
        out_shape=[shaped(2 * HALF, FFL)] + [turned_shape] * 3 + PART_SHAPES + [shaped(FFL, D)],
        compiler_params=params("arbitrary"),
        cost_estimate=cost(2 * 5 * 2 * HALF * FFL * D, 32),
        name="feed_forward",
    )(place, *tokens, *grads, ff_all)


def along_z(place, zhi, zlo):
    return (2 * zhi + zlo + 4 - 2 * place[4] - place[0]) % 4


def gate_up_kernel(*refs):
    place, token_refs, gate_t, up_t, out_ref, rows, sems = refs[0], refs[1:6], *refs[6:]
    step = pl.program_id(0)
    copies = put_tokens(token_refs, rows, sems, 0)

    @pl.when(step == 0)
    def _():
        for copy in copies:
            copy.start()
        for copy in copies:
            copy.wait()

    normed = rows[:, pl.ds(pl.multiple_of(step * 4 * B, 4 * B), 4 * B)]
    for matrix, left in ((0, gate_t), (1, up_t)):
        term = matmul(left[...], normed).astype(BF16)
        for j in range(2):
            zx = 2 * step + j
            by = along_z(place, zx // 4, matrix)
            out_ref[zx % 4, by, 0:FFL, :] = term[:, 2 * j * B : (2 * j + 1) * B]
            out_ref[zx % 4, by, FFL:, :] = term[:, (2 * j + 1) * B : (2 * j + 2) * B]


def down_kernel(*refs):
    place, grad_refs, act_t, out_ref, rows, sems = refs[0], refs[1:6], *refs[6:]
    step = pl.program_id(0)
    copies = put_tokens(grad_refs, rows, sems, 0)

    @pl.when(step == 0)
    def _():
        for copy in copies:
            copy.start()
        for copy in copies:
            copy.wait()

    term = matmul(act_t[...], rows[:, pl.ds(pl.multiple_of(step * 4 * B, 4 * B), 4 * B)])
    for j in range(2):
        half, p = step // 2, (2 * step + j) % 4
        at = pl.ds(pl.multiple_of(p * 2 * PIECE, 16), 2 * PIECE)
        for zx in range(8):
            slab = term[zx * PIECE : (zx + 1) * PIECE]
            low, high = slab[:, 2 * j * B : (2 * j + 1) * B], slab[:, (2 * j + 1) * B : (2 * j + 2) * B]
            slab = jnp.concatenate([low, high], axis=0).astype(BF16)
            out_ref[zx % 4, along_z(place, zx // 4, half), at, :] = slab


def ff_terms(kernel, place, pieces, lefts, rows, name):
    whole = pl.BlockSpec((FFL, 2 * HALF), lambda i, p: (0, 0))
    return pl.pallas_call(
        kernel,
        grid_spec=pltpu.PrefetchScalarGridSpec(
            num_scalar_prefetch=1,
            grid=(4,),
            in_specs=[ANYWHERE] * 5 + [whole] * len(lefts),
            out_specs=pl.BlockSpec((4, 4, rows, B), lambda i, p: (0, 0, 0, 0)),
            scratch_shapes=[pltpu.VMEM((2 * HALF, D), BF16), pltpu.SemaphoreType.DMA((10,))],
        ),
        out_shape=shaped(4, 4, rows, B),
        compiler_params=params("arbitrary"),
        cost_estimate=cost(2 * len(lefts) * 2 * HALF * FFL * D, 8 + 4 * len(lefts)),
        name=name,
    )(place, *pieces, *lefts)


def finish_hidden_kernel(*refs):
    place, piece_refs, weight_ref, gain_ref, out_ref, gain_out, rows = refs[0], refs[1:5], *refs[5:]
    y = place[1]
    for ref, by in zip(piece_refs, (0, 1, 2, 3)):
        at_y = (y + by) % 4
        for core in range(2):
            slab = ref[core].astype(F32)
            for zx in range(8):
                at = pl.multiple_of((2 * zx + core) * 4 * PIECE + at_y * PIECE, 8)
                rows[pl.ds(at, PIECE)] = slab[zx * PIECE : (zx + 1) * PIECE]
    gain = gain_ref[...]
    total = jnp.zeros((B, 1), F32)
    for i in range(FF // B):
        lanes = slice(i * B, (i + 1) * B)
        block = rows[lanes].T
        total = total + jnp.sum(block * weight_ref[:, lanes].astype(F32), axis=1, keepdims=True)
        out_ref[:, lanes] = block * gain
    gain_out[...] = total


def finish_hidden(place, pieces, weight, gain):
    whole = lambda *shape: pl.BlockSpec(shape, lambda i, p: (0,) * len(shape))
    return pl.pallas_call(
        finish_hidden_kernel,
        grid_spec=pltpu.PrefetchScalarGridSpec(
            num_scalar_prefetch=1,
            grid=(1,),
            in_specs=[whole(2, FFL, B)] * 4 + [whole(B, FF), whole(B, 1)],
            out_specs=[whole(B, FF), whole(B, 1)],
            scratch_shapes=[pltpu.VMEM((FF, B), F32)],
        ),
        out_shape=[shaped(B, FF, kind=F32), shaped(B, 1, kind=F32)],
        compiler_params=params("arbitrary"),
        cost_estimate=cost(0, 6),
        name="finish_hidden",
    )(place, *pieces, weight, gain)


def finish_down_kernel(place, *refs):
    piece_refs, out_ref = refs[:4], refs[4]
    for ref, by in zip(piece_refs, range(4)):
        rows = pl.ds(pl.multiple_of((place[1] + by) % 4 * PIECE, 8), PIECE)
        for half in range(2):
            slab = ref[half].astype(F32)
            for t in range(8):
                lane = (half * 8 + t) * B
                out_ref[rows, lane : lane + B] = slab[t * PIECE : (t + 1) * PIECE]


def finish_down(place, pieces):
    whole = lambda *shape: pl.BlockSpec(shape, lambda i, p: (0,) * len(shape))
    return pl.pallas_call(
        finish_down_kernel,
        grid_spec=pltpu.PrefetchScalarGridSpec(
            num_scalar_prefetch=1,
            grid=(1,),
            in_specs=[whole(2, FFL, B)] * 4,
            out_specs=whole(4 * PIECE, D),
            scratch_shapes=[],
        ),
        out_shape=shaped(4 * PIECE, D, kind=F32),
        compiler_params=params("arbitrary"),
        cost_estimate=cost(0, 5),
        name="finish_down",
    )(place, *pieces)


class Flow:
    def __init__(self, steps):
        self.steps, self.result, self.sent = steps, None, None
        self.move(None)

    def move(self, arrived):
        try:
            self.sent = self.steps.send(arrived)
        except StopIteration as end:
            self.sent, self.result = (), end.value


def stage(flows, *values):
    flows = [flow for flow in flows if flow.result is None]
    sizes = [len(flow.sent) for flow in flows]
    leaves, tree = jax.tree.flatten(values)
    tied = tie(*[v for flow in flows for v in flow.sent], *leaves)
    for flow, size in zip(flows, sizes):
        flow.move(tied[:size])
        tied = tied[size:]
    return jax.tree.unflatten(tree, tied)


def gather_steps(block):
    (other,) = yield (swap_core(block),)
    pair = jnp.stack([block, other])
    (got,) = yield (along_y(pair),)
    far, swapped = yield (along_y(send_half(got)), swap_core(got))
    (far_swapped,) = yield (swap_core(far),)
    return pair, got, swapped, far, far_swapped


def scatter_steps(parts):
    core = lax.axis_index("core")
    first, behind, ahead, far, far_other = parts
    (far_got,) = yield (swap_core(far_other),)
    far = add(far, far_got[::-1]).astype(BF16)
    low, behind_got, first_got = yield (along_y(far), swap_core(behind), swap_core(first[1]))
    ahead = add(ahead, behind_got[::-1])
    mine = lax.dynamic_slice_in_dim(ahead, core * (B // 2), B // 2, 1) + low.astype(F32)
    ahead = lax.dynamic_update_slice_in_dim(ahead, mine, core * (B // 2), 1).astype(BF16)
    (got,) = yield (along_y(ahead),)
    (last,) = yield (swap_core(got[1]),)
    return add(first[0], first_got) + got[0].astype(F32) + last.astype(F32)


def ring_gather_steps(block, axis):
    half = block.shape[0] // 2
    before, after = yield (shift(block, axis, 1), shift(block, axis, -1))
    low, high = yield (shift(before[:half], axis, 1), shift(after[half:], axis, -1))
    return block, after, low, high, before


def ring_scatter_steps(parts, axis):
    half = parts[2].shape[0] // 2
    low, high = yield (shift(parts[2][:half], axis, 1), shift(parts[2][half:], axis, -1))
    after = jnp.concatenate([add(parts[1][:half], low).astype(BF16), parts[1][half:]], axis=0)
    before = jnp.concatenate([parts[3][:half], add(parts[3][half:], high).astype(BF16)], axis=0)
    from_before, from_after = yield (shift(after, axis, 1), shift(before, axis, -1))
    return add(parts[0], from_before) + from_after.astype(F32)


def on_device(
    layer_input,
    positions,
    attn_gain,
    w_query,
    w_key,
    w_value,
    w_output,
    mlp_gain,
    w_gate,
    w_up,
    w_down,
    out_grad,
):
    zlo, y, zhi, x, core = (lax.axis_index(axis) for axis in AXES)
    place = jnp.stack([zlo, y, core, x, zhi]).astype(jnp.int32)

    def by_core(mine, got):
        return jnp.where(core == 0, jnp.stack([mine, got]), jnp.stack([got, mine]))

    def by_zlo(mine, got):
        return jnp.where(zlo == 0, jnp.stack([mine, got]), jnp.stack([got, mine]))

    def by_zhi(mine, got):
        return jnp.where(zhi == 0, jnp.stack([mine, got]), jnp.stack([got, mine]))

    def trio(mine, other, axis):
        across = lax.ppermute(other, (axis, "core"), [(i, 3 - i) for i in range(4)])
        return shift(mine, axis, 1), swap_core(other), across

    def column_steps(mine, got):
        pair = by_core(mine, got)
        (got,) = yield (shift(pair, "zhi", 1),)
        return (yield from ring_gather_steps(by_zhi(pair, got), "x"))

    def hidden_steps(mine, got, down):
        piece = jnp.concatenate([by_core(mine, got).reshape(2 * FFL, B), down], axis=0)
        pieces = yield from ring_gather_steps(piece, "z")
        return jnp.concatenate(pieces, axis=0).reshape(4, 3 * FFL, B)

    def of_core(pair, other=False):
        return lax.dynamic_index_in_dim(pair, 1 - core if other else core, 0, keepdims=False)

    def whole_ring(pieces):
        own, after, low, high, before = pieces
        return own, after, jnp.concatenate([low, high], axis=0), before

    def attention_steps(terms):
        column = yield from ring_scatter_steps([terms[i] for i in range(4)], "x")
        keep = lax.dynamic_index_in_dim(column, zhi, 0, keepdims=False)
        send = lax.dynamic_index_in_dim(column, 1 - zhi, 0, keepdims=False).astype(BF16)
        (got,) = yield (shift(send, "zhi", 1),)
        pair = (keep + got.astype(F32)).astype(BF16)
        mine, other = of_core(pair), of_core(pair, True)
        there, here, across = yield trio(mine, other, "zlo")
        own = by_core(add(mine, there), add(here, across)).astype(BF16)
        ring = yield small_gather(own, "y")
        return jnp.roll(jnp.stack([own, *ring]), y, axis=0)

    def ff_steps(sums):
        own = yield from ring_scatter_steps([sums[i] for i in range(4)], "z")
        own = own.astype(BF16)
        pair, down = own[: 2 * FFL].reshape(2, FFL, B), own[2 * FFL :]
        mine, other = of_core(pair), of_core(pair, True)
        there, here, across = yield trio(jnp.concatenate([mine, down], axis=0), other, "zlo")
        both = by_zlo(by_core(mine, here), by_core(there[:FFL], across))
        both = jnp.concatenate([both, by_zlo(down, there[FFL:])[:, None]], axis=1)
        ring = whole_ring((yield from ring_gather_steps(both, "y")))
        return [piece[:, :2] for piece in ring], [piece[:, 2] for piece in ring]

    def all_to_all_steps(value):
        (got,) = yield (lax.all_to_all(value, FSDP, 0, 0, tiled=True),)
        return got

    x_low = layer_input[0]
    frequency = theta ** (-jnp.arange(0, HD, 2).astype(F32) / HD)
    angles = positions[0].astype(F32)[:, None] * frequency
    tables = []
    for table in (jnp.cos(angles), jnp.sin(angles)):
        high = lax.reduce_precision(table, 8, 7)
        tables += [high.astype(BF16), (table - high).astype(BF16)]
    tokens = Flow(gather_steps(jnp.concatenate([x_low, *tables], axis=1)))
    grads = Flow(gather_steps(out_grad[0]))
    output_rows = Flow(all_to_all_steps(w_output.reshape(B, 16, B).transpose(1, 0, 2)))
    (gain_one,) = stage([tokens], attn_gain[:, None])

    qkv_mine, qkv_other = prepare_qkv(place, w_query, w_key, w_value, gain_one)
    ff_mine, ff_other, ff_down = prepare_ff(place, w_gate, w_up, w_down, mlp_gain[:, None])
    ff_got = swap_core(ff_other)
    qkv_mine, qkv_other, ff_mine, ff_got, ff_down = stage(
        [tokens, output_rows], qkv_mine, qkv_other, ff_mine, ff_got, ff_down
    )

    o_rows = output_rows.result.reshape(D, B)
    mine = jnp.concatenate([qkv_mine, own_rows(o_rows, y, core, HEADS * HD)], axis=0)
    other = jnp.concatenate([qkv_other, own_rows(o_rows, y, 1 - core, HEADS * HD)], axis=0)
    columns = Flow(column_steps(mine, swap_core(other)))
    inputs = x_low.astype(F32)
    scale_one = lax.rsqrt(jnp.mean(inputs * inputs, axis=-1, keepdims=True) + eps)
    scale_one, ff_mine, ff_got, ff_down = stage([tokens, columns], scale_one, ff_mine, ff_got, ff_down)

    hidden_rows = Flow(hidden_steps(ff_mine, ff_got, ff_down))
    stage([tokens, columns, hidden_rows, grads])
    stage([columns, hidden_rows])

    x_pieces = tokens.result
    ff_all = lax.all_gather(hidden_rows.result, "x", axis=0, tiled=False)
    query, key_value, scale_all, cosine, sine, qkv_full = project_qkv(place, x_pieces, columns.result)
    query, key_value = stage([], query, key_value)

    earlier = lax.ppermute(key_value, "zlo", [(0, 1)])
    query, key_value, earlier = stage([grads], query, key_value, earlier)

    key_value = jnp.concatenate([earlier, key_value], axis=1)
    mixed, log_total = attention(place, query, key_value)
    (mixed,) = stage([grads], mixed)
    mixed = mixed.reshape(2 * HALF, HEADS * HD)
    *parts, o_full = project_out(place, columns.result, mixed)
    sums = Flow(scatter_steps(parts))
    stage([sums, grads])
    grad_pieces = grads.result
    for _ in range(3):
        stage([sums])
    hidden = inputs + sums.result
    scale_two = lax.rsqrt(jnp.mean(hidden * hidden, axis=-1, keepdims=True) + eps)
    normed = Flow(gather_steps((hidden * scale_two).astype(BF16)))
    for _ in range(4):
        stage([normed])
    normed_pieces = normed.result

    activation, act_t, gate_t, up_t, *parts, down_full = feed_forward(place, normed_pieces, grad_pieces, ff_all)
    sums = Flow(scatter_steps(parts))
    (act_t,) = stage([sums], act_t)
    down_terms = ff_terms(down_kernel, place, grad_pieces, (act_t,), FFL, "down_terms")
    down_terms, gate_t = stage([sums], down_terms, gate_t)
    down_sum = lax.psum_scatter(down_terms, "x", scatter_dimension=0, tiled=True)[0]
    gate_up_terms = ff_terms(gate_up_kernel, place, normed_pieces, (gate_t, up_t), 2 * FFL, "gate_up_terms")
    (gate_up_terms,) = stage([sums], gate_up_terms)
    gate_up_sum = lax.psum_scatter(gate_up_terms, "x", scatter_dimension=0, tiled=True)[0]
    stage([sums])

    grad_normed_two = sums.result
    mean_two = jnp.mean(grad_normed_two * hidden, axis=-1, keepdims=True)
    grad_hidden = (
        out_grad[0].astype(F32)
        + scale_two * grad_normed_two
        - hidden * (scale_two * scale_two * scale_two) * mean_two
    )
    hidden_grads = Flow(gather_steps(grad_hidden.astype(BF16)))
    (activation,) = stage([hidden_grads], activation)
    down_parts = project(activation, down_full)
    down_parts = stage([hidden_grads], *down_parts)
    result = Flow(scatter_steps(down_parts))
    stage([hidden_grads, result])
    stage([hidden_grads])

    hidden_grad_pieces = hidden_grads.result
    grad_mixed = grad_of_mixed(place, hidden_grad_pieces, o_full)
    (grad_mixed,) = stage([result], grad_mixed)
    grad_query, grad_earlier, grad_own = attention_back(
        place, query, key_value, grad_mixed.reshape(2, HALF, HEADS * HD), log_total
    )
    grad_query, grad_earlier, grad_own, mixed = stage([result], grad_query, grad_earlier, grad_own, mixed)
    later = lax.ppermute(grad_earlier, "zlo", [(1, 0)])
    output_terms = attention_terms(place, hidden_grad_pieces, mixed, "output_terms")
    later, grad_query, output_terms, down_sum, gate_up_sum = stage(
        [result], later, grad_query, output_terms, down_sum, gate_up_sum
    )
    ff_sums = Flow(ff_steps(jnp.concatenate([gate_up_sum, down_sum], axis=1)))
    *parts, grad_t = qkv_back(grad_query, grad_own, later, cosine, sine, scale_all, qkv_full)
    *parts, grad_t = stage([ff_sums], *parts, grad_t)
    sums = Flow(scatter_steps(parts))
    terms = attention_terms(place, x_pieces, grad_t, "qkv_terms", output_terms)
    (terms,) = stage([sums, ff_sums], terms)
    attention_sums = Flow(attention_steps(terms))
    stage([sums, attention_sums, ff_sums])
    stage([sums, attention_sums])
    stage([sums, attention_sums])
    grad_normed = sums.result
    mean_one = jnp.mean(grad_normed * inputs, axis=-1, keepdims=True)
    input_grad = (
        grad_hidden
        + scale_one * grad_normed
        - inputs * (scale_one * scale_one * scale_one) * mean_one
    )
    input_grad = input_grad.astype(BF16)
    while attention_sums.result is None or ff_sums.result is None:
        stage([attention_sums, ff_sums])
    output_rows = attention_sums.result[:, :, QKV:].reshape(16, B, B)
    output_grad = lax.all_to_all(output_rows, FSDP, 0, 0, tiled=True)
    gate_up, down = ff_sums.result

    output_grad = output_grad.transpose(1, 0, 2).reshape(B, D).astype(F32)
    sums = attention_sums.result
    query_grad = sums[:, :, : HEADS * HD].reshape(D, B).T.astype(F32)
    key_grad = jnp.sum(sums[:, :, HEADS * HD : (HEADS + 1) * HD].astype(F32), axis=1)
    key_grad = key_grad.reshape(KV * HD, B).T
    value_grad = jnp.sum(sums[:, :, (HEADS + 1) * HD : QKV].astype(F32), axis=1)
    value_grad = value_grad.reshape(KV * HD, B).T
    attn_gain_grad = (
        jnp.sum(query_grad * w_query.astype(F32), axis=1)
        + jnp.sum(key_grad * w_key.astype(F32), axis=1)
        + jnp.sum(value_grad * w_value.astype(F32), axis=1)
    )
    gain_two = mlp_gain[:, None]
    gate_grad, gate_gain = finish_hidden(place, [p[0] for p in gate_up], w_gate, gain_two)
    up_grad, up_gain = finish_hidden(place, [p[1] for p in gate_up], w_up, gain_two)
    down_grad = finish_down(place, down)
    one = attn_gain[:, None]
    return (
        (hidden + result.result).astype(BF16)[None],
        input_grad[None],
        attn_gain_grad,
        query_grad * one,
        key_grad * one,
        value_grad * one,
        output_grad,
        (gate_gain + up_gain)[:, 0],
        gate_grad,
        up_grad,
        down_grad,
    )


def solution(mesh):
    split = Mesh(mesh.devices.reshape(2, 4, 2, 4, 2), AXES)
    tokens = P(FSDP, SEQ, None)
    rows = P(FSDP, None)
    gain = P(FSDP)
    in_specs = (
        tokens, P(FSDP, SEQ), gain, rows, rows, rows, rows, gain, rows, rows, rows, tokens,
    )
    out_specs = (tokens, tokens, gain, rows, rows, rows, rows, gain, rows, rows, rows)
    return jax.shard_map(
        on_device, mesh=split, in_specs=in_specs, out_specs=out_specs, check_vma=False
    )
```

```python
import jax
import jax.numpy as jnp
from jax import lax
from jax.experimental import pallas as pl
from jax.experimental.pallas import tpu as pltpu
from jax.sharding import Mesh
from jax.sharding import PartitionSpec as P

H = 32
KV = 4
HD = 64
D = 2048
FF = 5632
B = 128
HALF = 512
HEADS = 4
FFL = 704
PIECE = 88

eps = 1e-05
theta = 10000.0
F32 = jnp.float32
BF16 = jnp.bfloat16
AXES = ("zlo", "y", "zhi", "x", "core")
FSDP = ("zhi", "x", "core")
SEQ = ("zlo", "y")


def matmul(left, right):
    return jnp.dot(left, right, preferred_element_type=F32)


def times_transposed(left, right):
    return lax.dot_general(left, right, (((1,), (1,)), ((), ())), preferred_element_type=F32)


def outer_sum(left, right):
    return lax.dot_general(left, right, (((0,), (0,)), ((), ())), preferred_element_type=F32)


def shift(value, axis, by):
    if axis == "z":
        at = [2 * (z % 2) + z // 2 for z in range(4)]
        return lax.ppermute(value, ("zlo", "zhi"), [(at[z], at[(z + by) % 4]) for z in range(4)])
    size = lax.axis_size(axis)
    return lax.ppermute(value, axis, [(i, (i + by) % size) for i in range(size)])


def swap_core(value):
    return shift(value, "core", 1)


def small_gather(block, axis):
    return shift(block, axis, -1), shift(block, axis, 2), shift(block, axis, 1)


def tie(*values):
    return lax.optimization_barrier(values)


def add(left, right):
    return left.astype(F32) + right.astype(F32)


def along_y(value):
    pairs = []
    for i in range(4):
        pairs.append((2 * i, 2 * ((i + 1) % 4)))
        pairs.append((2 * i + 1, 2 * ((i + 3) % 4) + 1))
    return lax.ppermute(value, ("y", "core"), pairs)


def send_half(got):
    core = lax.axis_index("core")
    return lax.dynamic_slice_in_dim(got, core * (B // 2), B // 2, 1)


FLIPPED = (0, 0, 1, 0, 1)
LENGTHS = (B, B, B, B // 2, B // 2)


def put_tokens(refs, rows_ref, sems, start):
    lanes = pl.ds(0, rows_ref.shape[1])
    copies = []
    row = 0
    for s in range(2):
        for ref, flip, length in zip(refs, FLIPPED, LENGTHS):
            copies.append(
                pltpu.make_async_copy(
                    ref.at[s ^ flip, :, lanes], rows_ref.at[pl.ds(row, length)], sems.at[start + len(copies)]
                )
            )
            row += length
    return copies


TILE = 256
WIDE = D + B
VMEM_LIMIT = 56 * 2**20
ANYWHERE = pl.BlockSpec(memory_space=pl.ANY)


def params(*kinds):
    return pltpu.CompilerParams(dimension_semantics=kinds or None, vmem_limit_bytes=VMEM_LIMIT)


def cost(flops, megabytes):
    return pl.CostEstimate(flops=flops, bytes_accessed=int(megabytes * 2**20), transcendentals=0)


def shaped(*shape, kind=BF16):
    return jax.ShapeDtypeStruct(shape, kind)


PART_SPECS = [pl.BlockSpec((1, n, D), lambda i, *_: (i // 2, 0, 0)) for n in LENGTHS]
PART_SHAPES = [jax.ShapeDtypeStruct((2, n, D), BF16) for n in LENGTHS]


def put_parts(step, tile, refs):
    @pl.when(step % 2 == 0)
    def _():
        refs[0][0] = tile[:B]
        refs[1][0] = tile[B:]

    @pl.when(step % 2 == 1)
    def _():
        refs[2][0] = tile[:B]
        refs[3][0] = tile[B : B + B // 2]
        refs[4][0] = tile[B + B // 2 :]


def turned(values):
    lane = lax.broadcasted_iota(jnp.int32, values.shape, 1) % HD
    return jnp.where(lane < HD // 2, -pltpu.roll(values, 2 * HD - HD // 2, 1), pltpu.roll(values, HD // 2, 1))


def lane_block(zhi, x, core):
    return pl.ds(pl.multiple_of((zhi * 8 + x * 2 + core) * B, B), B)


def put_columns(place, refs, at, into, sems, start):
    rows = pl.ds(at, into.shape[0])
    copies = []
    for ref, by, first in zip(refs, (0, 1, 2, 2, 3), (0, 0, 0, 1, 0)):
        for i in range(ref.shape[0]):
            for core in range(2):
                lanes = lane_block(first + i, (place[3] + by) % 4, core)
                copies.append(
                    pltpu.make_async_copy(ref.at[i, core, rows], into.at[:, lanes], sems.at[start + len(copies)])
                )
    return copies


def prepare_qkv_kernel(place, q_mine, q_other, w_key, w_value, gain, mine_ref, other_ref, k_rows, v_rows):
    scale = gain[...]
    k_rows[...] = (w_key[...].astype(F32) * scale).T
    v_rows[...] = (w_value[...].astype(F32) * scale).T
    rows = pl.ds(pl.multiple_of(place[1] * HD, HD), HD)
    for source, out in ((q_mine, mine_ref), (q_other, other_ref)):
        out[: HEADS * HD] = (source[...].astype(F32) * scale).T.astype(BF16)
        out[HEADS * HD : (HEADS + 1) * HD] = k_rows[rows].astype(BF16)
        out[(HEADS + 1) * HD :] = v_rows[rows].astype(BF16)


QKV = (HEADS + 2) * HD


def prepare_qkv(place, w_query, w_key, w_value, gain):
    whole = lambda *shape: pl.BlockSpec(shape, lambda i, p: (0,) * len(shape))
    return pl.pallas_call(
        prepare_qkv_kernel,
        grid_spec=pltpu.PrefetchScalarGridSpec(
            num_scalar_prefetch=1,
            grid=(1,),
            in_specs=[
                pl.BlockSpec((B, HEADS * HD), lambda i, p: (0, 2 * p[1] + p[2])),
                pl.BlockSpec((B, HEADS * HD), lambda i, p: (0, 2 * p[1] + 1 - p[2])),
                whole(B, KV * HD), whole(B, KV * HD), whole(B, 1),
            ],
            out_specs=[whole(QKV, B), whole(QKV, B)],
            scratch_shapes=[pltpu.VMEM((KV * HD, B), F32), pltpu.VMEM((KV * HD, B), F32)],
        ),
        out_shape=[shaped(QKV, B), shaped(QKV, B)],
        compiler_params=params("arbitrary"),
        cost_estimate=cost(0, 1),
        name="prepare_qkv",
    )(place, w_query, w_query, w_key, w_value, gain)


def prepare_ff_kernel(place, w_gate, w_up, w_down, gain, mine_ref, other_ref, down_ref, picked, rows, down_rows, sems):
    zlo, y, core = place[0], place[1], place[2]
    down = pltpu.make_async_copy(
        w_down.at[:, pl.ds(pl.multiple_of(zlo * (D // 2), D // 2), D // 2)], down_rows, sems.at[1]
    )
    down.start()

    @pl.when(zlo == 0)
    def _():
        copy = pltpu.make_async_copy(w_gate, picked, sems.at[0])
        copy.start()
        copy.wait()

    @pl.when(zlo == 1)
    def _():
        copy = pltpu.make_async_copy(w_up, picked, sems.at[0])
        copy.start()
        copy.wait()

    scale = gain[...]
    for i in range(FF // B):
        rows[i * B : (i + 1) * B] = (picked[:, i * B : (i + 1) * B].astype(F32) * scale).T
    for which, out in ((core, mine_ref), (1 - core, other_ref)):
        slabs = []
        for zx in range(8):
            at = pl.multiple_of(zx * 2 * 4 * PIECE + which * 4 * PIECE + y * PIECE, 8)
            slabs.append(rows[pl.ds(at, PIECE)])
        out[...] = jnp.concatenate(slabs, axis=0).astype(BF16)
    down.wait()
    for t in range(8):
        rows[t * 4 * PIECE : (t + 1) * 4 * PIECE] = down_rows[:, t * B : (t + 1) * B].astype(F32)
    slabs = [rows[pl.ds(pl.multiple_of(t * 4 * PIECE + y * PIECE, 8), PIECE)] for t in range(8)]
    down_ref[...] = jnp.concatenate(slabs, axis=0).astype(BF16)


def prepare_ff(place, w_gate, w_up, w_down, gain):
    return pl.pallas_call(
        prepare_ff_kernel,
        grid_spec=pltpu.PrefetchScalarGridSpec(
            num_scalar_prefetch=1,
            grid=(1,),
            in_specs=[ANYWHERE, ANYWHERE, ANYWHERE, pl.BlockSpec((B, 1), lambda i, p: (0, 0))],
            out_specs=[pl.BlockSpec((FFL, B), lambda i, p: (0, 0))] * 3,
            scratch_shapes=[
                pltpu.VMEM((B, FF), BF16),
                pltpu.VMEM((FF, B), F32),
                pltpu.VMEM((4 * PIECE, D // 2), BF16),
                pltpu.SemaphoreType.DMA((2,)),
            ],
        ),
        out_shape=[shaped(FFL, B)] * 3,
        compiler_params=params("arbitrary"),
        cost_estimate=cost(0, 6),
        name="prepare_ff",
    )(place, w_gate, w_up, w_down, gain)


def project_qkv_kernel(*refs):
    place, x_refs, w_refs = refs[0], refs[1:6], refs[6:11]
    query_ref, kv_ref, scale_ref, cosine_ref, sine_ref, w_out, rows, weights, sems = refs[11:]
    step = pl.program_id(0)
    tokens = put_tokens(x_refs, rows, sems, 0)
    columns = put_columns(place, w_refs, 0, weights, sems, 10)
    back = pltpu.make_async_copy(weights, w_out, sems.at[26])

    @pl.when(step == 0)
    def _():
        for copy in columns + tokens:
            copy.start()
        for copy in columns:
            copy.wait()
        back.start()
        for copy in tokens:
            copy.wait()

    at = pl.ds(pl.multiple_of(step * TILE, TILE), TILE)
    tile = rows[at, :D]
    wide = tile.astype(F32)
    scale = lax.rsqrt(jnp.mean(wide * wide, axis=-1, keepdims=True) + eps)
    scale_ref[...] = scale
    pre = times_transposed(tile, weights[...]) * scale
    tables = rows[at, D:].astype(F32)
    tables = tables + pltpu.roll(tables, B - HD // 2, 1)
    cosine = jnp.concatenate([tables[:, : HD // 2]] * 4, axis=1)
    sine = jnp.concatenate([tables[:, HD : HD + HD // 2]] * 4, axis=1)
    cosine_ref[...] = cosine
    sine_ref[...] = sine
    for i in range(2):
        part = pre[:, i * 2 * HD : (i + 1) * 2 * HD]
        part = (part * cosine + turned(part) * sine).astype(BF16) * HD ** (-0.5)
        query_ref[0, 2 * i] = part[:, :HD]
        query_ref[0, 2 * i + 1] = part[:, HD:]
    part = pre[:, HEADS * HD :]
    lane = lax.broadcasted_iota(jnp.int32, part.shape, 1)
    kv_ref[0] = jnp.where(lane < HD, part * cosine + turned(part) * sine, part).astype(BF16)

    @pl.when(step == 3)
    def _():
        back.wait()


def project_qkv(place, x_pieces, w_pieces):
    tile = lambda lanes: pl.BlockSpec((TILE, lanes), lambda i, p: (i, 0))
    return pl.pallas_call(
        project_qkv_kernel,
        grid_spec=pltpu.PrefetchScalarGridSpec(
            num_scalar_prefetch=1,
            grid=(4,),
            in_specs=[ANYWHERE] * 10,
            out_specs=[
                pl.BlockSpec((1, HEADS, TILE, HD), lambda i, p: (i // 2, 0, i % 2, 0)),
                pl.BlockSpec((1, TILE, 2 * HD), lambda i, p: (i // 2, i % 2, 0)),
                tile(1), tile(2 * HD), tile(2 * HD),
                ANYWHERE,
            ],
            scratch_shapes=[
                pltpu.VMEM((2 * HALF, WIDE), BF16),
                pltpu.VMEM((QKV, D), BF16),
                pltpu.SemaphoreType.DMA((27,)),
            ],
        ),
        out_shape=[
            shaped(2, HEADS, HALF, HD), shaped(2, HALF, 2 * HD), shaped(2 * HALF, 1, kind=F32),
            shaped(2 * HALF, 2 * HD, kind=F32), shaped(2 * HALF, 2 * HD, kind=F32), shaped(QKV, D),
        ],
        compiler_params=params("arbitrary"),
        cost_estimate=cost(2 * 2 * HALF * QKV * D, 8),
        name="project_qkv",
    )(place, *x_pieces, *w_pieces)


def project_kernel(left_ref, weight_ref, *parts):
    put_parts(pl.program_id(0), matmul(left_ref[...], weight_ref[...]).astype(BF16), parts)


def project(left, weight):
    depth = left.shape[1]
    return pl.pallas_call(
        project_kernel,
        grid=(4,),
        in_specs=[pl.BlockSpec((TILE, depth), lambda i: (i, 0)), pl.BlockSpec((depth, D), lambda i: (0, 0))],
        out_specs=PART_SPECS,
        out_shape=PART_SHAPES,
        compiler_params=params("arbitrary"),
        cost_estimate=cost(2 * 2 * HALF * depth * D, 8),
        name="project",
    )(left, weight)


def put_term(place, left, rows, term_ref):
    def one(i, carry):
        term = matmul(left, rows[:, pl.ds(pl.multiple_of(i * 4 * B, 4 * B), 4 * B)]).astype(BF16)
        for j in range(2):
            zx = 2 * i + j
            by = (zx % 4 + 4 - place[3]) % 4
            term_ref[by, zx // 4, 0, : left.shape[0]] = term[:, 2 * j * B : (2 * j + 1) * B]
            term_ref[by, zx // 4, 1, : left.shape[0]] = term[:, (2 * j + 1) * B : (2 * j + 2) * B]
        return carry

    lax.fori_loop(0, 4, one, 0)


def qkv_back_kernel(grad_q_ref, own_ref, later_ref, cosine_ref, sine_ref, scale_ref, weight_ref, *outs):
    parts, turned_ref = outs[:5], outs[5]
    cosine, sine = cosine_ref[...], sine_ref[...]
    lane = lax.broadcasted_iota(jnp.int32, cosine.shape, 1)
    pieces = []
    for i in range(2):
        part = grad_q_ref[0, :, i * 2 * HD : (i + 1) * 2 * HD]
        pieces.append(part * cosine - turned(part * sine))
    part = own_ref[0] + later_ref[0].astype(F32)
    pieces.append(jnp.where(lane < HD, part * cosine - turned(part * sine), part))
    grad_pre = jnp.concatenate(pieces, axis=1)
    put_parts(pl.program_id(0), matmul(grad_pre.astype(BF16), weight_ref[...]).astype(BF16), parts)
    turned_ref[...] = (grad_pre * scale_ref[...]).T.astype(BF16)


def qkv_back(grad_query, own, later, cosine, sine, scale, weight):
    tile = lambda lanes: pl.BlockSpec((TILE, lanes), lambda i: (i, 0))
    half = lambda lanes: pl.BlockSpec((1, TILE, lanes), lambda i: (i // 2, i % 2, 0))
    return pl.pallas_call(
        qkv_back_kernel,
        grid=(4,),
        in_specs=[
            half(HEADS * HD), half(2 * HD), half(2 * HD), tile(2 * HD), tile(2 * HD), tile(1),
            pl.BlockSpec((QKV, D), lambda i: (0, 0)),
        ],
        out_specs=PART_SPECS + [pl.BlockSpec((QKV, TILE), lambda i: (0, i))],
        out_shape=PART_SHAPES + [shaped(QKV, 2 * HALF)],
        compiler_params=params("arbitrary"),
        cost_estimate=cost(2 * 2 * HALF * QKV * D, 9),
        name="qkv_back",
    )(grad_query, own, later, cosine, sine, scale, weight)


def attention_term_kernel(*refs):
    place, token_refs, left_ref = refs[0], refs[1:6], refs[6]
    term_ref, rows, sems = refs[-3:]
    copies = put_tokens(token_refs, rows, sems, 0)
    for copy in copies:
        copy.start()
    left = left_ref[...]
    if left.shape[0] == 2 * HALF:
        left = left.T
    if len(refs) == 11:
        term_ref[:, :, :, left.shape[0] :] = refs[7][...]
    for copy in copies:
        copy.wait()
    put_term(place, left, rows, term_ref)


def attention_terms(place, pieces, left, name, *more):
    whole = lambda *shape: pl.BlockSpec(shape, lambda i, p: (0,) * len(shape))
    rows = min(left.shape)
    total = rows + sum(terms.shape[3] for terms in more)
    return pl.pallas_call(
        attention_term_kernel,
        grid_spec=pltpu.PrefetchScalarGridSpec(
            num_scalar_prefetch=1,
            grid=(1,),
            in_specs=[ANYWHERE] * 5 + [whole(*left.shape)] + [whole(*terms.shape) for terms in more],
            out_specs=whole(4, 2, 2, total, B),
            scratch_shapes=[pltpu.VMEM((2 * HALF, D), BF16), pltpu.SemaphoreType.DMA((10,))],
        ),
        out_shape=shaped(4, 2, 2, total, B),
        compiler_params=params("arbitrary"),
        cost_estimate=cost(2 * 2 * HALF * rows * D, 7),
        name=name,
    )(place, *pieces, left, *more)


def token_places(at, y, core):
    step = 1 - 2 * core
    block = jnp.where(
        at < B, y, jnp.where(at < 2 * B, y + 4 - step, jnp.where(at < 3 * B, y + 4 + step, y + 2))
    )
    row = at % B
    row = jnp.where(at < 3 * B, row, (row + core * (B // 2)) % B)
    return (block % 4) * B + row


def set_bias(place_ref, bias_ref):
    zlo, y, core = place_ref[0], place_ref[1], place_ref[2]
    key_at = token_places(lax.broadcasted_iota(jnp.int32, (HALF, 1), 0), y, core)
    query_at = token_places(lax.broadcasted_iota(jnp.int32, (1, HALF), 1), y, core)
    bias_ref[:HALF, :] = jnp.broadcast_to(jnp.where(zlo == 1, 0.0, -1e30), (HALF, HALF))
    bias_ref[HALF:, :] = jnp.where(key_at <= query_at, 0.0, -1e30)


def attention_kernel(place_ref, query_ref, kv_ref, weight_ref, mixed_ref, log_ref, *rest):
    parts, bias_ref = rest[:5], rest[5]

    @pl.when(pl.program_id(0) == 0)
    def _():
        set_bias(place_ref, bias_ref)

    key, value = kv_ref[0, :, :HD], kv_ref[0, :, HD:]
    for head in range(HEADS):
        scores = times_transposed(key, query_ref[0, head]) + bias_ref[...]
        top = jnp.max(scores, axis=0, keepdims=True)
        weights = jnp.exp(scores - top)
        total = jnp.sum(weights, axis=0, keepdims=True)
        low = (weights * (1.0 / total)).astype(BF16)
        mixed_ref[0, :, head * HD : (head + 1) * HD] = outer_sum(value, low).T.astype(BF16)
        log_ref[0, head] = top + jnp.log(total)
    put_rows(parts, matmul(mixed_ref[0], weight_ref[...]).astype(BF16))


def put_rows(parts, rows):
    row = 0
    for ref, length in zip(parts, LENGTHS):
        ref[0] = rows[row : row + length]
        row += length


def attention_back_kernel(place_ref, *refs):
    grad_refs, query_ref, kv_ref, log_ref, weight_ref = refs[:5], *refs[5:9]
    grad_query_ref, earlier_ref, own_ref, bias_ref, rows, sems = refs[9:]
    step = pl.program_id(0)
    copies = put_tokens(grad_refs, rows, sems, 0)

    @pl.when(step == 0)
    def _():
        for copy in copies:
            copy.start()
        set_bias(place_ref, bias_ref)
        for copy in copies:
            copy.wait()

    hidden = rows[pl.ds(pl.multiple_of(step * HALF, HALF), HALF), :]
    grads = times_transposed(hidden, weight_ref[...]).astype(BF16)
    key, value = kv_ref[0, :, :HD], kv_ref[0, :, HD:]
    grad_key = jnp.zeros((2 * HALF, HD), F32)
    grad_value = jnp.zeros((2 * HALF, HD), F32)
    for head in range(HEADS):
        lanes = slice(head * HD, (head + 1) * HD)
        query, grad = query_ref[0, head], grads[:, lanes]
        weights = jnp.exp(times_transposed(key, query) + bias_ref[...] - log_ref[0, head])
        grad_weights = times_transposed(value, grad)
        delta = jnp.sum(weights * grad_weights, axis=0, keepdims=True)
        grad_scores = (weights * (grad_weights - delta)).astype(BF16)
        grad_query_ref[0, :, lanes] = outer_sum(key, grad_scores).T * HD ** (-0.5)
        grad_key += matmul(grad_scores, query)
        grad_value += matmul(weights.astype(BF16), grad)
    total = jnp.concatenate([grad_key, grad_value], axis=1)
    earlier_ref[0] = total[:HALF].astype(BF16)
    own_ref[0] = total[HALF:]


def sequence_block(*tail):
    return pl.BlockSpec((1,) + tail, lambda s, place: (s,) + (0,) * len(tail))


HEAD_ROWS = pl.BlockSpec((HEADS * HD, D), lambda s, place: (2 * place[1] + place[2], 0))


def attention_call(kernel, in_specs, out_specs, out_shape, scratch, flops, name):
    return pl.pallas_call(
        kernel,
        grid_spec=pltpu.PrefetchScalarGridSpec(
            num_scalar_prefetch=1,
            grid=(2,),
            in_specs=in_specs,
            out_specs=out_specs,
            scratch_shapes=[pltpu.VMEM((2 * HALF, HALF), F32)] + scratch,
        ),
        out_shape=out_shape,
        compiler_params=params("arbitrary"),
        cost_estimate=cost(flops * 8 * 2 * HALF * HALF * HD * 2, 8),
        name=name,
    )


def attention(place, query, kv, weight):
    return attention_call(
        attention_kernel,
        [sequence_block(HEADS, HALF, HD), sequence_block(2 * HALF, 2 * HD), HEAD_ROWS],
        [sequence_block(HALF, HEADS * HD), sequence_block(HEADS, 1, HALF)] + [sequence_block(n, D) for n in LENGTHS],
        [shaped(2, HALF, HEADS * HD), shaped(2, HEADS, 1, HALF, kind=F32)] + PART_SHAPES,
        [],
        3,
        "attention",
    )(place, query, kv, weight)


def attention_back(place, grad_pieces, query, kv, log_total, weight):
    return attention_call(
        attention_back_kernel,
        [ANYWHERE] * 5
        + [
            sequence_block(HEADS, HALF, HD), sequence_block(2 * HALF, 2 * HD),
            sequence_block(HEADS, 1, HALF), HEAD_ROWS,
        ],
        [sequence_block(HALF, HEADS * HD), sequence_block(HALF, 2 * HD), sequence_block(HALF, 2 * HD)],
        [
            shaped(2, HALF, HEADS * HD, kind=F32),
            shaped(2, HALF, 2 * HD),
            shaped(2, HALF, 2 * HD, kind=F32),
        ],
        [pltpu.VMEM((2 * HALF, D), BF16), pltpu.SemaphoreType.DMA((10,))],
        6,
        "attention_back",
    )(place, *grad_pieces, query, kv, log_total, weight)


def finish_attention_kernel(place, *refs):
    piece_refs, w_query, w_key, w_value, gain_ref = refs[:4], *refs[4:8]
    query_out, key_out, value_out, gain_out, send_out, rows = refs[8:]
    for ref, by in zip(piece_refs, range(4)):
        at_y = (place[1] + by) % 4
        for c in range(2):
            piece = ref[c].astype(F32)
            rows[pl.ds(pl.multiple_of((2 * at_y + c) * HEADS * HD, HEADS * HD), HEADS * HD)] = piece[: HEADS * HD]
            for i in range(2):
                send_out[2 * (2 * at_y + c) + i] = piece[QKV + i * B : QKV + (i + 1) * B].astype(BF16)
        both = ref[0].astype(F32) + ref[1].astype(F32)
        at = pl.multiple_of(H * HD + at_y * HD, HD)
        rows[pl.ds(at, HD)] = both[HEADS * HD : (HEADS + 1) * HD]
        rows[pl.ds(at + KV * HD, HD)] = both[(HEADS + 1) * HD : QKV]
    gain = gain_ref[...]
    total = jnp.zeros((B, 1), F32)
    row = 0
    for weight, out in ((w_query, query_out), (w_key, key_out), (w_value, value_out)):
        for i in range(out.shape[1] // B):
            lanes = slice(i * B, (i + 1) * B)
            block = rows[row : row + B].T
            total = total + jnp.sum(block * weight[:, lanes].astype(F32), axis=1, keepdims=True)
            out[:, lanes] = block * gain
            row += B
    gain_out[...] = total


def finish_attention(place, pieces, w_query, w_key, w_value, gain):
    whole = lambda *shape: pl.BlockSpec(shape, lambda i, p: (0,) * len(shape))
    kv = KV * HD
    return pl.pallas_call(
        finish_attention_kernel,
        grid_spec=pltpu.PrefetchScalarGridSpec(
            num_scalar_prefetch=1,
            grid=(1,),
            in_specs=[whole(2, QKV + HEADS * HD, B)] * 4 + [whole(B, D), whole(B, kv), whole(B, kv), whole(B, 1)],
            out_specs=[whole(B, D), whole(B, kv), whole(B, kv), whole(B, 1), whole(16, B, B)],
            scratch_shapes=[pltpu.VMEM((D + 2 * kv, B), F32)],
        ),
        out_shape=[
            shaped(B, D, kind=F32), shaped(B, kv, kind=F32), shaped(B, kv, kind=F32), shaped(B, 1, kind=F32),
            shaped(16, B, B),
        ],
        compiler_params=params("arbitrary"),
        cost_estimate=cost(0, 4),
        name="finish_attention",
    )(place, *pieces, w_query, w_key, w_value, gain)


def finish_output_kernel(blocks, out):
    for i in range(16):
        out[:, i * B : (i + 1) * B] = blocks[i].astype(F32)


def finish_output(blocks):
    return pl.pallas_call(
        finish_output_kernel,
        out_shape=shaped(B, D, kind=F32),
        compiler_params=params(),
        cost_estimate=cost(0, 2),
        name="finish_output",
    )(blocks)


def feed_forward_kernel(*refs):
    place, token_refs, grad_refs, ff_ref = refs[0], refs[1:6], refs[6:11], refs[11]
    act_ref, act_t, gate_t, up_t = refs[12:16]
    parts, down_out = refs[16:21], refs[21]
    rows_h, rows_g, gate_up, down, slabs, sems = refs[22:]
    step = pl.program_id(0)
    tokens = put_tokens(token_refs, rows_h, sems, 0)
    grads = put_tokens(grad_refs, rows_g, sems, 10)
    weights, loads = [], []
    for x in range(4):
        for by in range(4):
            z = (2 * place[4] + place[0] + by) % 4
            zhi, zlo = z // 2, z % 2
            for core in range(2):
                weights.append(
                    pltpu.make_async_copy(
                        ff_ref.at[x, by, pl.ds(core * FFL, FFL)],
                        gate_up.at[zlo, :, lane_block(zhi, x, core)],
                        sems.at[20 + len(weights)],
                    )
                )
            loads.append(
                pltpu.make_async_copy(
                    ff_ref.at[x, by, pl.ds(2 * FFL, FFL)], slabs.at[zlo, zhi * 4 + x], sems.at[52 + len(loads)]
                )
            )
    back = pltpu.make_async_copy(down, down_out, sems.at[68])

    @pl.when(step == 0)
    def _():
        for copy in tokens + weights + loads + grads:
            copy.start()
        for copy in tokens + weights:
            copy.wait()

    rows = pl.ds(pl.multiple_of(step * HALF, HALF), HALF)
    normed = rows_h[rows, :]
    gate_pre = times_transposed(normed, gate_up[0])
    upward = times_transposed(normed, gate_up[1])

    @pl.when(step == 0)
    def _():
        for copy in loads:
            copy.wait()

        def put(q, carry):
            for half in range(2):
                for p in range(4):
                    one = slabs[half, 2 * q, 2 * p * PIECE : 2 * (p + 1) * PIECE, :].astype(F32)
                    two = slabs[half, 2 * q + 1, 2 * p * PIECE : 2 * (p + 1) * PIECE, :].astype(F32)
                    lane = (half * 8 + 2 * p) * B
                    rows = pl.ds(pl.multiple_of(q * 2 * PIECE, 16), 2 * PIECE)
                    down[rows, lane : lane + B] = jnp.concatenate([one[:PIECE], two[:PIECE]], axis=0).astype(BF16)
                    down[rows, lane + B : lane + 2 * B] = jnp.concatenate(
                        [one[PIECE:], two[PIECE:]], axis=0
                    ).astype(BF16)
            return carry

        lax.fori_loop(0, 4, put, 0)
        back.start()
        for copy in grads:
            copy.wait()

    grad_act = times_transposed(rows_g[rows, :], down[...])
    sigmoid = 1.0 / (1.0 + jnp.exp(-gate_pre))
    silu = gate_pre * sigmoid
    activation = silu * upward
    grad_up = grad_act * silu
    grad_gate = grad_act * upward * (sigmoid * (1.0 + gate_pre * (1.0 - sigmoid)))
    part = matmul(grad_gate.astype(BF16), gate_up[0]) + matmul(grad_up.astype(BF16), gate_up[1])
    part = part.astype(BF16)
    row = 0
    for ref, length in zip(parts, LENGTHS):
        ref[0] = part[row : row + length]
        row += length
    act_ref[...] = activation.astype(BF16)
    act_t[...] = activation.T.astype(BF16)
    gate_t[...] = grad_gate.T.astype(BF16)
    up_t[...] = grad_up.T.astype(BF16)

    @pl.when(step == 1)
    def _():
        back.wait()


def feed_forward(place, tokens, grads, ff_all):
    turned_spec = pl.BlockSpec((FFL, HALF), lambda i, p: (0, i))
    turned_shape = shaped(FFL, 2 * HALF)
    return pl.pallas_call(
        feed_forward_kernel,
        grid_spec=pltpu.PrefetchScalarGridSpec(
            num_scalar_prefetch=1,
            grid=(2,),
            in_specs=[ANYWHERE] * 11,
            out_specs=[pl.BlockSpec((HALF, FFL), lambda i, p: (i, 0))]
            + [turned_spec] * 3
            + [pl.BlockSpec((1, n, D), lambda i, p: (i, 0, 0)) for n in LENGTHS]
            + [ANYWHERE],
            scratch_shapes=[
                pltpu.VMEM((2 * HALF, D), BF16),
                pltpu.VMEM((2 * HALF, D), BF16),
                pltpu.VMEM((2, FFL, D), BF16),
                pltpu.VMEM((FFL, D), BF16),
                pltpu.VMEM((2, 8, FFL, B), BF16),
                pltpu.SemaphoreType.DMA((69,)),
            ],
        ),
        out_shape=[shaped(2 * HALF, FFL)] + [turned_shape] * 3 + PART_SHAPES + [shaped(FFL, D)],
        compiler_params=params("arbitrary"),
        cost_estimate=cost(2 * 5 * 2 * HALF * FFL * D, 32),
        name="feed_forward",
    )(place, *tokens, *grads, ff_all)


def along_z(place, zhi, zlo):
    return (2 * zhi + zlo + 4 - 2 * place[4] - place[0]) % 4


def gate_up_kernel(*refs):
    place, token_refs, gate_t, up_t, out_ref, rows, sems = refs[0], refs[1:6], *refs[6:]
    step = pl.program_id(0)
    copies = put_tokens(token_refs, rows, sems, 0)

    @pl.when(step == 0)
    def _():
        for copy in copies:
            copy.start()
        for copy in copies:
            copy.wait()

    normed = rows[:, pl.ds(pl.multiple_of(step * 4 * B, 4 * B), 4 * B)]
    for matrix, left in ((0, gate_t), (1, up_t)):
        term = matmul(left[...], normed).astype(BF16)
        for j in range(2):
            zx = 2 * step + j
            by = along_z(place, zx // 4, matrix)
            out_ref[zx % 4, by, 0:FFL, :] = term[:, 2 * j * B : (2 * j + 1) * B]
            out_ref[zx % 4, by, FFL:, :] = term[:, (2 * j + 1) * B : (2 * j + 2) * B]


def down_kernel(*refs):
    place, grad_refs, act_t, out_ref, rows, sems = refs[0], refs[1:6], *refs[6:]
    step = pl.program_id(0)
    copies = put_tokens(grad_refs, rows, sems, 0)

    @pl.when(step == 0)
    def _():
        for copy in copies:
            copy.start()
        for copy in copies:
            copy.wait()

    term = matmul(act_t[...], rows[:, pl.ds(pl.multiple_of(step * 4 * B, 4 * B), 4 * B)])
    for j in range(2):
        half, p = step // 2, (2 * step + j) % 4
        at = pl.ds(pl.multiple_of(p * 2 * PIECE, 16), 2 * PIECE)
        for zx in range(8):
            slab = term[zx * PIECE : (zx + 1) * PIECE]
            low, high = slab[:, 2 * j * B : (2 * j + 1) * B], slab[:, (2 * j + 1) * B : (2 * j + 2) * B]
            slab = jnp.concatenate([low, high], axis=0).astype(BF16)
            out_ref[zx % 4, along_z(place, zx // 4, half), at, :] = slab


def ff_terms(kernel, place, pieces, lefts, rows, name):
    whole = pl.BlockSpec((FFL, 2 * HALF), lambda i, p: (0, 0))
    return pl.pallas_call(
        kernel,
        grid_spec=pltpu.PrefetchScalarGridSpec(
            num_scalar_prefetch=1,
            grid=(4,),
            in_specs=[ANYWHERE] * 5 + [whole] * len(lefts),
            out_specs=pl.BlockSpec((4, 4, rows, B), lambda i, p: (0, 0, 0, 0)),
            scratch_shapes=[pltpu.VMEM((2 * HALF, D), BF16), pltpu.SemaphoreType.DMA((10,))],
        ),
        out_shape=shaped(4, 4, rows, B),
        compiler_params=params("arbitrary"),
        cost_estimate=cost(2 * len(lefts) * 2 * HALF * FFL * D, 8 + 4 * len(lefts)),
        name=name,
    )(place, *pieces, *lefts)


def finish_hidden_kernel(*refs):
    place, piece_refs, weight_ref, gain_ref, out_ref, gain_out, rows = refs[0], refs[1:5], *refs[5:]
    y = place[1]
    for ref, by in zip(piece_refs, (0, 1, 2, 3)):
        at_y = (y + by) % 4
        for core in range(2):
            slab = ref[core].astype(F32)
            for zx in range(8):
                at = pl.multiple_of((2 * zx + core) * 4 * PIECE + at_y * PIECE, 8)
                rows[pl.ds(at, PIECE)] = slab[zx * PIECE : (zx + 1) * PIECE]
    gain = gain_ref[...]
    total = jnp.zeros((B, 1), F32)
    for i in range(FF // B):
        lanes = slice(i * B, (i + 1) * B)
        block = rows[lanes].T
        total = total + jnp.sum(block * weight_ref[:, lanes].astype(F32), axis=1, keepdims=True)
        out_ref[:, lanes] = block * gain
    gain_out[...] = total


def finish_hidden(place, pieces, weight, gain):
    whole = lambda *shape: pl.BlockSpec(shape, lambda i, p: (0,) * len(shape))
    return pl.pallas_call(
        finish_hidden_kernel,
        grid_spec=pltpu.PrefetchScalarGridSpec(
            num_scalar_prefetch=1,
            grid=(1,),
            in_specs=[whole(2, FFL, B)] * 4 + [whole(B, FF), whole(B, 1)],
            out_specs=[whole(B, FF), whole(B, 1)],
            scratch_shapes=[pltpu.VMEM((FF, B), F32)],
        ),
        out_shape=[shaped(B, FF, kind=F32), shaped(B, 1, kind=F32)],
        compiler_params=params("arbitrary"),
        cost_estimate=cost(0, 6),
        name="finish_hidden",
    )(place, *pieces, weight, gain)


def finish_down_kernel(place, *refs):
    piece_refs, out_ref = refs[:4], refs[4]
    for ref, by in zip(piece_refs, range(4)):
        rows = pl.ds(pl.multiple_of((place[1] + by) % 4 * PIECE, 8), PIECE)
        for half in range(2):
            slab = ref[half].astype(F32)
            for t in range(8):
                lane = (half * 8 + t) * B
                out_ref[rows, lane : lane + B] = slab[t * PIECE : (t + 1) * PIECE]


def finish_down(place, pieces):
    whole = lambda *shape: pl.BlockSpec(shape, lambda i, p: (0,) * len(shape))
    return pl.pallas_call(
        finish_down_kernel,
        grid_spec=pltpu.PrefetchScalarGridSpec(
            num_scalar_prefetch=1,
            grid=(1,),
            in_specs=[whole(2, FFL, B)] * 4,
            out_specs=whole(4 * PIECE, D),
            scratch_shapes=[],
        ),
        out_shape=shaped(4 * PIECE, D, kind=F32),
        compiler_params=params("arbitrary"),
        cost_estimate=cost(0, 5),
        name="finish_down",
    )(place, *pieces)


class Flow:
    def __init__(self, steps):
        self.steps, self.result, self.sent = steps, None, None
        self.move(None)

    def move(self, arrived):
        try:
            self.sent = self.steps.send(arrived)
        except StopIteration as end:
            self.sent, self.result = (), end.value


def stage(flows, *values):
    flows = [flow for flow in flows if flow.result is None]
    sizes = [len(flow.sent) for flow in flows]
    leaves, tree = jax.tree.flatten(values)
    tied = tie(*[v for flow in flows for v in flow.sent], *leaves)
    for flow, size in zip(flows, sizes):
        flow.move(tied[:size])
        tied = tied[size:]
    return jax.tree.unflatten(tree, tied)


def gather_steps(block):
    (other,) = yield (swap_core(block),)
    pair = jnp.stack([block, other])
    (got,) = yield (along_y(pair),)
    far, swapped = yield (along_y(send_half(got)), swap_core(got))
    (far_swapped,) = yield (swap_core(far),)
    return pair, got, swapped, far, far_swapped


def scatter_steps(parts):
    core = lax.axis_index("core")
    first, behind, ahead, far, far_other = parts
    (far_got,) = yield (swap_core(far_other),)
    far = add(far, far_got[::-1]).astype(BF16)
    low, behind_got, first_got = yield (along_y(far), swap_core(behind), swap_core(first[1]))
    ahead = add(ahead, behind_got[::-1])
    mine = lax.dynamic_slice_in_dim(ahead, core * (B // 2), B // 2, 1) + low.astype(F32)
    ahead = lax.dynamic_update_slice_in_dim(ahead, mine, core * (B // 2), 1).astype(BF16)
    (got,) = yield (along_y(ahead),)
    (last,) = yield (swap_core(got[1]),)
    return add(first[0], first_got) + got[0].astype(F32) + last.astype(F32)


def ring_gather_steps(block, axis):
    half = block.shape[0] // 2
    before, after = yield (shift(block, axis, 1), shift(block, axis, -1))
    low, high = yield (shift(before[:half], axis, 1), shift(after[half:], axis, -1))
    return block, after, low, high, before


def ring_scatter_steps(parts, axis):
    half = parts[2].shape[0] // 2
    low, high = yield (shift(parts[2][:half], axis, 1), shift(parts[2][half:], axis, -1))
    after = jnp.concatenate([add(parts[1][:half], low).astype(BF16), parts[1][half:]], axis=0)
    before = jnp.concatenate([parts[3][:half], add(parts[3][half:], high).astype(BF16)], axis=0)
    from_before, from_after = yield (shift(after, axis, 1), shift(before, axis, -1))
    return add(parts[0], from_before) + from_after.astype(F32)


def on_device(
    layer_input,
    positions,
    attn_gain,
    w_query,
    w_key,
    w_value,
    w_output,
    mlp_gain,
    w_gate,
    w_up,
    w_down,
    out_grad,
):
    zlo, y, zhi, x, core = (lax.axis_index(axis) for axis in AXES)
    place = jnp.stack([zlo, y, core, x, zhi]).astype(jnp.int32)

    def by_core(mine, got):
        return jnp.where(core == 0, jnp.stack([mine, got]), jnp.stack([got, mine]))

    def by_zlo(mine, got):
        return jnp.where(zlo == 0, jnp.stack([mine, got]), jnp.stack([got, mine]))

    def by_zhi(mine, got):
        return jnp.where(zhi == 0, jnp.stack([mine, got]), jnp.stack([got, mine]))

    def trio(mine, other, axis):
        across = lax.ppermute(other, (axis, "core"), [(i, 3 - i) for i in range(4)])
        return shift(mine, axis, 1), swap_core(other), across

    def column_steps(mine, got):
        pair = by_core(mine, got)
        (got,) = yield (shift(pair, "zhi", 1),)
        return (yield from ring_gather_steps(by_zhi(pair, got), "x"))

    def hidden_steps(mine, got, down):
        piece = jnp.concatenate([by_core(mine, got).reshape(2 * FFL, B), down], axis=0)
        pieces = yield from ring_gather_steps(piece, "z")
        return jnp.concatenate(pieces, axis=0).reshape(4, 3 * FFL, B)

    def of_core(pair, other=False):
        return lax.dynamic_index_in_dim(pair, 1 - core if other else core, 0, keepdims=False)

    def whole_ring(pieces):
        own, after, low, high, before = pieces
        return own, after, jnp.concatenate([low, high], axis=0), before

    def attention_steps(terms):
        column = yield from ring_scatter_steps([terms[i] for i in range(4)], "x")
        keep = lax.dynamic_index_in_dim(column, zhi, 0, keepdims=False)
        send = lax.dynamic_index_in_dim(column, 1 - zhi, 0, keepdims=False).astype(BF16)
        (got,) = yield (shift(send, "zhi", 1),)
        pair = (keep + got.astype(F32)).astype(BF16)
        mine, other = of_core(pair), of_core(pair, True)
        there, here, across = yield trio(mine, other, "zlo")
        own = by_core(add(mine, there), add(here, across)).astype(BF16)
        return whole_ring((yield from ring_gather_steps(own, "y")))

    def ff_steps(sums):
        own = yield from ring_scatter_steps([sums[i] for i in range(4)], "z")
        own = own.astype(BF16)
        pair, down = own[: 2 * FFL].reshape(2, FFL, B), own[2 * FFL :]
        mine, other = of_core(pair), of_core(pair, True)
        there, here, across = yield trio(jnp.concatenate([mine, down], axis=0), other, "zlo")
        both = by_zlo(by_core(mine, here), by_core(there[:FFL], across))
        both = jnp.concatenate([both, by_zlo(down, there[FFL:])[:, None]], axis=1)
        ring = whole_ring((yield from ring_gather_steps(both, "y")))
        return [piece[:, :2] for piece in ring], [piece[:, 2] for piece in ring]

    x_low = layer_input[0]
    frequency = theta ** (-jnp.arange(0, HD, 2).astype(F32) / HD)
    angles = positions[0].astype(F32)[:, None] * frequency
    tables = []
    for table in (jnp.cos(angles), jnp.sin(angles)):
        high = lax.reduce_precision(table, 8, 7)
        tables += [high.astype(BF16), (table - high).astype(BF16)]
    tokens = Flow(gather_steps(jnp.concatenate([x_low, *tables], axis=1)))
    grads = Flow(gather_steps(out_grad[0]))
    o_all = lax.all_gather(w_output, FSDP, axis=0, tiled=True)
    qkv_mine, qkv_other = prepare_qkv(place, w_query, w_key, w_value, attn_gain[:, None])
    qkv_mine, qkv_got, gain_two = stage([tokens], qkv_mine, swap_core(qkv_other), mlp_gain[:, None])

    columns = Flow(column_steps(qkv_mine, qkv_got))
    ff_mine, ff_other, ff_down = prepare_ff(place, w_gate, w_up, w_down, gain_two)
    ff_mine, ff_got, ff_down, x_low = stage([tokens, columns], ff_mine, swap_core(ff_other), ff_down, x_low)

    inputs = x_low.astype(F32)
    scale_one = lax.rsqrt(jnp.mean(inputs * inputs, axis=-1, keepdims=True) + eps)
    scale_one, ff_mine, ff_got, ff_down = stage([tokens, columns, grads], scale_one, ff_mine, ff_got, ff_down)

    hidden_rows = Flow(hidden_steps(ff_mine, ff_got, ff_down))
    stage([tokens, columns])

    x_pieces = tokens.result
    query, key_value, scale_all, cosine, sine, qkv_full = project_qkv(place, x_pieces, columns.result)
    query, key_value = stage([hidden_rows, grads], query, key_value)

    earlier = lax.ppermute(key_value, "zlo", [(0, 1)])
    query, key_value, earlier = stage([grads, hidden_rows], query, key_value, earlier)

    ff_all = lax.all_gather(hidden_rows.result, "x", axis=0, tiled=False)
    key_value = jnp.concatenate([earlier, key_value], axis=1)
    mixed, log_total, *parts = attention(place, query, key_value, o_all)
    parts = stage([grads], *parts)
    grad_pieces = grads.result
    sums = Flow(scatter_steps(parts))
    for _ in range(4):
        stage([sums])
    hidden = inputs + sums.result
    scale_two = lax.rsqrt(jnp.mean(hidden * hidden, axis=-1, keepdims=True) + eps)
    normed = Flow(gather_steps((hidden * scale_two).astype(BF16)))
    for _ in range(4):
        stage([normed])
    normed_pieces = normed.result

    activation, act_t, gate_t, up_t, *parts, down_full = feed_forward(place, normed_pieces, grad_pieces, ff_all)
    sums = Flow(scatter_steps(parts))
    (gate_t,) = stage([sums], gate_t)
    gate_up_terms = ff_terms(gate_up_kernel, place, normed_pieces, (gate_t, up_t), 2 * FFL, "gate_up_terms")
    gate_up_terms, act_t = stage([sums], gate_up_terms, act_t)
    gate_up_sum = lax.psum_scatter(gate_up_terms, "x", scatter_dimension=0, tiled=True)[0]
    down_terms = ff_terms(down_kernel, place, grad_pieces, (act_t,), FFL, "down_terms")
    (down_terms,) = stage([sums], down_terms)
    down_sum = lax.psum_scatter(down_terms, "x", scatter_dimension=0, tiled=True)[0]
    stage([sums])

    grad_normed_two = sums.result
    mean_two = jnp.mean(grad_normed_two * hidden, axis=-1, keepdims=True)
    grad_hidden = (
        out_grad[0].astype(F32)
        + scale_two * grad_normed_two
        - hidden * (scale_two * scale_two * scale_two) * mean_two
    )
    hidden_grads = Flow(gather_steps(grad_hidden.astype(BF16)))
    (activation,) = stage([hidden_grads], activation)
    down_parts = project(activation, down_full)
    down_parts = stage([hidden_grads], *down_parts)
    result = Flow(scatter_steps(down_parts))
    stage([hidden_grads, result])
    stage([hidden_grads])

    hidden_grad_pieces = hidden_grads.result
    grad_query, grad_earlier, grad_own = attention_back(
        place, hidden_grad_pieces, query, key_value, log_total, o_all
    )
    grad_query, grad_earlier, grad_own, mixed = stage([result], grad_query, grad_earlier, grad_own, mixed)
    later = lax.ppermute(grad_earlier, "zlo", [(1, 0)])
    output_terms = attention_terms(place, hidden_grad_pieces, mixed.reshape(2 * HALF, HEADS * HD), "output_terms")
    later, grad_query, output_terms, down_sum, gate_up_sum = stage(
        [result], later, grad_query, output_terms, down_sum, gate_up_sum
    )
    ff_sums = Flow(ff_steps(jnp.concatenate([gate_up_sum, down_sum], axis=1)))
    *parts, grad_t = qkv_back(grad_query, grad_own, later, cosine, sine, scale_all, qkv_full)
    *parts, grad_t = stage([ff_sums, result], *parts, grad_t)
    sums = Flow(scatter_steps(parts))
    terms = attention_terms(place, x_pieces, grad_t, "qkv_terms", output_terms)
    (terms,) = stage([sums, ff_sums], terms)
    attention_sums = Flow(attention_steps(terms))
    stage([sums, attention_sums])
    stage([attention_sums])
    stage([sums, attention_sums, ff_sums])
    stage([sums, attention_sums])
    grad_normed = sums.result
    mean_one = jnp.mean(grad_normed * inputs, axis=-1, keepdims=True)
    input_grad = (
        grad_hidden
        + scale_one * grad_normed
        - inputs * (scale_one * scale_one * scale_one) * mean_one
    )
    input_grad = input_grad.astype(BF16)
    stage([attention_sums, ff_sums])
    stage([attention_sums, ff_sums])

    query_grad, key_grad, value_grad, attn_gain_grad, output_send = finish_attention(
        place, attention_sums.result, w_query, w_key, w_value, attn_gain[:, None]
    )
    output_grad = finish_output(lax.all_to_all(output_send, FSDP, 0, 0, tiled=True))
    gate_up, down = ff_sums.result
    gain_two = mlp_gain[:, None]
    gate_grad, gate_gain = finish_hidden(place, [p[0] for p in gate_up], w_gate, gain_two)
    up_grad, up_gain = finish_hidden(place, [p[1] for p in gate_up], w_up, gain_two)
    down_grad = finish_down(place, down)
    assert attention_sums.result is not None and ff_sums.result is not None
    return (
        (hidden + result.result).astype(BF16)[None],
        input_grad[None],
        attn_gain_grad[:, 0],
        query_grad,
        key_grad,
        value_grad,
        output_grad,
        (gate_gain + up_gain)[:, 0],
        gate_grad,
        up_grad,
        down_grad,
    )


def solution(mesh):
    split = Mesh(mesh.devices.reshape(2, 4, 2, 4, 2), AXES)
    tokens = P(FSDP, SEQ, None)
    rows = P(FSDP, None)
    gain = P(FSDP)
    in_specs = (
        tokens, P(FSDP, SEQ), gain, rows, rows, rows, rows, gain, rows, rows, rows, tokens,
    )
    out_specs = (tokens, tokens, gain, rows, rows, rows, rows, gain, rows, rows, rows)
    return jax.shard_map(
        on_device, mesh=split, in_specs=in_specs, out_specs=out_specs, check_vma=False
    )
```

```python
import jax
import jax.numpy as jnp
from jax import lax
from jax.experimental import pallas as pl
from jax.experimental.pallas import tpu as pltpu
from jax.sharding import Mesh
from jax.sharding import PartitionSpec as P

H = 32
KV = 4
HD = 64
D = 2048
FF = 5632
B = 128
HALF = 512
HEADS = 4
FFL = 704
PIECE = 88

eps = 1e-05
theta = 10000.0
F32 = jnp.float32
BF16 = jnp.bfloat16
AXES = ("zlo", "y", "zhi", "x", "core")
FSDP = ("zhi", "x", "core")
SEQ = ("zlo", "y")


def matmul(left, right):
    return jnp.dot(left, right, preferred_element_type=F32)


def times_transposed(left, right):
    return lax.dot_general(left, right, (((1,), (1,)), ((), ())), preferred_element_type=F32)


def outer_sum(left, right):
    return lax.dot_general(left, right, (((0,), (0,)), ((), ())), preferred_element_type=F32)


def shift(value, axis, by):
    if axis == "z":
        at = [2 * (z % 2) + z // 2 for z in range(4)]
        return lax.ppermute(value, ("zlo", "zhi"), [(at[z], at[(z + by) % 4]) for z in range(4)])
    size = lax.axis_size(axis)
    return lax.ppermute(value, axis, [(i, (i + by) % size) for i in range(size)])


def swap_core(value):
    return shift(value, "core", 1)


def small_gather(block, axis):
    return shift(block, axis, -1), shift(block, axis, 2), shift(block, axis, 1)


def tie(*values):
    return lax.optimization_barrier(values)


def add(left, right):
    return left.astype(F32) + right.astype(F32)


def along_y(value):
    pairs = []
    for i in range(4):
        pairs.append((2 * i, 2 * ((i + 1) % 4)))
        pairs.append((2 * i + 1, 2 * ((i + 3) % 4) + 1))
    return lax.ppermute(value, ("y", "core"), pairs)


def send_half(got):
    core = lax.axis_index("core")
    return lax.dynamic_slice_in_dim(got, core * (B // 2), B // 2, 1)


FLIPPED = (0, 0, 1, 0, 1)
LENGTHS = (B, B, B, B // 2, B // 2)


def put_tokens(refs, rows_ref, sems, start):
    lanes = pl.ds(0, rows_ref.shape[1])
    copies = []
    row = 0
    for s in range(2):
        for ref, flip, length in zip(refs, FLIPPED, LENGTHS):
            copies.append(
                pltpu.make_async_copy(
                    ref.at[s ^ flip, :, lanes], rows_ref.at[pl.ds(row, length)], sems.at[start + len(copies)]
                )
            )
            row += length
    return copies


TILE = 256
WIDE = D + B
VMEM_LIMIT = 56 * 2**20
ANYWHERE = pl.BlockSpec(memory_space=pl.ANY)


def params(*kinds):
    return pltpu.CompilerParams(dimension_semantics=kinds or None, vmem_limit_bytes=VMEM_LIMIT)


def cost(flops, megabytes):
    return pl.CostEstimate(flops=flops, bytes_accessed=int(megabytes * 2**20), transcendentals=0)


def shaped(*shape, kind=BF16):
    return jax.ShapeDtypeStruct(shape, kind)


PART_SPECS = [pl.BlockSpec((1, n, D), lambda i, *_: (i // 2, 0, 0)) for n in LENGTHS]
PART_SHAPES = [jax.ShapeDtypeStruct((2, n, D), BF16) for n in LENGTHS]


def put_parts(step, tile, refs):
    @pl.when(step % 2 == 0)
    def _():
        refs[0][0] = tile[:B]
        refs[1][0] = tile[B:]

    @pl.when(step % 2 == 1)
    def _():
        refs[2][0] = tile[:B]
        refs[3][0] = tile[B : B + B // 2]
        refs[4][0] = tile[B + B // 2 :]


def turned(values):
    lane = lax.broadcasted_iota(jnp.int32, values.shape, 1) % HD
    return jnp.where(lane < HD // 2, -pltpu.roll(values, 2 * HD - HD // 2, 1), pltpu.roll(values, HD // 2, 1))


def lane_block(zhi, x, core):
    return pl.ds(pl.multiple_of((zhi * 8 + x * 2 + core) * B, B), B)


def put_columns(place, refs, into, sems, start):
    copies = []
    for ref, by, first in zip(refs, (0, 1, 2, 2, 3), (0, 0, 0, 1, 0)):
        for i in range(ref.shape[0]):
            for core in range(2):
                lanes = lane_block(first + i, (place[3] + by) % 4, core)
                copies.append(
                    pltpu.make_async_copy(ref.at[i, core], into.at[:, lanes], sems.at[start + len(copies)])
                )
    return copies


def prepare_qkv_kernel(place, q_mine, q_other, w_key, w_value, gain, mine_ref, other_ref, k_rows, v_rows):
    scale = gain[...]
    k_rows[...] = (w_key[...].astype(F32) * scale).T
    v_rows[...] = (w_value[...].astype(F32) * scale).T
    rows = pl.ds(pl.multiple_of(place[1] * HD, HD), HD)
    for source, out in ((q_mine, mine_ref), (q_other, other_ref)):
        out[: HEADS * HD] = (source[...].astype(F32) * scale).T.astype(BF16)
        out[HEADS * HD : (HEADS + 1) * HD] = k_rows[rows].astype(BF16)
        out[(HEADS + 1) * HD :] = v_rows[rows].astype(BF16)


QKV = (HEADS + 2) * HD


def prepare_qkv(place, w_query, w_key, w_value, gain):
    whole = lambda *shape: pl.BlockSpec(shape, lambda i, p: (0,) * len(shape))
    return pl.pallas_call(
        prepare_qkv_kernel,
        grid_spec=pltpu.PrefetchScalarGridSpec(
            num_scalar_prefetch=1,
            grid=(1,),
            in_specs=[
                pl.BlockSpec((B, HEADS * HD), lambda i, p: (0, 2 * p[1] + p[2])),
                pl.BlockSpec((B, HEADS * HD), lambda i, p: (0, 2 * p[1] + 1 - p[2])),
                whole(B, KV * HD), whole(B, KV * HD), whole(B, 1),
            ],
            out_specs=[whole(QKV, B), whole(QKV, B)],
            scratch_shapes=[pltpu.VMEM((KV * HD, B), F32), pltpu.VMEM((KV * HD, B), F32)],
        ),
        out_shape=[shaped(QKV, B), shaped(QKV, B)],
        compiler_params=params("arbitrary"),
        cost_estimate=cost(0, 1),
        name="prepare_qkv",
    )(place, w_query, w_query, w_key, w_value, gain)


def prepare_ff_kernel(place, w_gate, w_up, w_down, gain, mine_ref, other_ref, down_ref, picked, rows, down_rows, sems):
    zlo, y, core = place[0], place[1], place[2]
    down = pltpu.make_async_copy(
        w_down.at[:, pl.ds(pl.multiple_of(zlo * (D // 2), D // 2), D // 2)], down_rows, sems.at[1]
    )
    down.start()

    @pl.when(zlo == 0)
    def _():
        copy = pltpu.make_async_copy(w_gate, picked, sems.at[0])
        copy.start()
        copy.wait()

    @pl.when(zlo == 1)
    def _():
        copy = pltpu.make_async_copy(w_up, picked, sems.at[0])
        copy.start()
        copy.wait()

    scale = gain[...]
    for i in range(FF // B):
        rows[i * B : (i + 1) * B] = (picked[:, i * B : (i + 1) * B].astype(F32) * scale).T
    for which, out in ((core, mine_ref), (1 - core, other_ref)):
        slabs = []
        for zx in range(8):
            at = pl.multiple_of(zx * 2 * 4 * PIECE + which * 4 * PIECE + y * PIECE, 8)
            slabs.append(rows[pl.ds(at, PIECE)])
        out[...] = jnp.concatenate(slabs, axis=0).astype(BF16)
    down.wait()
    for t in range(8):
        rows[t * 4 * PIECE : (t + 1) * 4 * PIECE] = down_rows[:, t * B : (t + 1) * B].astype(F32)
    slabs = [rows[pl.ds(pl.multiple_of(t * 4 * PIECE + y * PIECE, 8), PIECE)] for t in range(8)]
    down_ref[...] = jnp.concatenate(slabs, axis=0).astype(BF16)


def prepare_ff(place, w_gate, w_up, w_down, gain):
    return pl.pallas_call(
        prepare_ff_kernel,
        grid_spec=pltpu.PrefetchScalarGridSpec(
            num_scalar_prefetch=1,
            grid=(1,),
            in_specs=[ANYWHERE, ANYWHERE, ANYWHERE, pl.BlockSpec((B, 1), lambda i, p: (0, 0))],
            out_specs=[pl.BlockSpec((FFL, B), lambda i, p: (0, 0))] * 3,
            scratch_shapes=[
                pltpu.VMEM((B, FF), BF16),
                pltpu.VMEM((FF, B), F32),
                pltpu.VMEM((4 * PIECE, D // 2), BF16),
                pltpu.SemaphoreType.DMA((2,)),
            ],
        ),
        out_shape=[shaped(FFL, B)] * 3,
        compiler_params=params("arbitrary"),
        cost_estimate=cost(0, 6),
        name="prepare_ff",
    )(place, w_gate, w_up, w_down, gain)


def project_qkv_kernel(*refs):
    place, x_refs, w_refs = refs[0], refs[1:6], refs[6:11]
    query_ref, kv_ref, scale_ref, cosine_ref, sine_ref, w_out, rows, weights, sems = refs[11:]
    step = pl.program_id(0)
    tokens = put_tokens(x_refs, rows, sems, 0)
    columns = put_columns(place, w_refs, weights, sems, 10)
    back = pltpu.make_async_copy(weights, w_out, sems.at[26])

    @pl.when(step == 0)
    def _():
        for copy in columns + tokens:
            copy.start()
        for copy in columns:
            copy.wait()
        back.start()
        for copy in tokens:
            copy.wait()

    at = pl.ds(pl.multiple_of(step * TILE, TILE), TILE)
    tile = rows[at, :D]
    wide = tile.astype(F32)
    scale = lax.rsqrt(jnp.mean(wide * wide, axis=-1, keepdims=True) + eps)
    scale_ref[...] = scale
    pre = times_transposed(tile, weights[...]) * scale
    tables = rows[at, D:].astype(F32)
    tables = tables + pltpu.roll(tables, B - HD // 2, 1)
    cosine = jnp.concatenate([tables[:, : HD // 2]] * 4, axis=1)
    sine = jnp.concatenate([tables[:, HD : HD + HD // 2]] * 4, axis=1)
    cosine_ref[...] = cosine
    sine_ref[...] = sine
    for i in range(2):
        part = pre[:, i * 2 * HD : (i + 1) * 2 * HD]
        part = (part * cosine + turned(part) * sine).astype(BF16) * HD ** (-0.5)
        query_ref[0, 2 * i] = part[:, :HD]
        query_ref[0, 2 * i + 1] = part[:, HD:]
    part = pre[:, HEADS * HD :]
    lane = lax.broadcasted_iota(jnp.int32, part.shape, 1)
    kv_ref[0] = jnp.where(lane < HD, part * cosine + turned(part) * sine, part).astype(BF16)

    @pl.when(step == 3)
    def _():
        back.wait()


def project_qkv(place, x_pieces, w_pieces):
    tile = lambda lanes: pl.BlockSpec((TILE, lanes), lambda i, p: (i, 0))
    return pl.pallas_call(
        project_qkv_kernel,
        grid_spec=pltpu.PrefetchScalarGridSpec(
            num_scalar_prefetch=1,
            grid=(4,),
            in_specs=[ANYWHERE] * 10,
            out_specs=[
                pl.BlockSpec((1, HEADS, TILE, HD), lambda i, p: (i // 2, 0, i % 2, 0)),
                pl.BlockSpec((1, TILE, 2 * HD), lambda i, p: (i // 2, i % 2, 0)),
                tile(1), tile(2 * HD), tile(2 * HD),
                ANYWHERE,
            ],
            scratch_shapes=[
                pltpu.VMEM((2 * HALF, WIDE), BF16),
                pltpu.VMEM((QKV, D), BF16),
                pltpu.SemaphoreType.DMA((27,)),
            ],
        ),
        out_shape=[
            shaped(2, HEADS, HALF, HD), shaped(2, HALF, 2 * HD), shaped(2 * HALF, 1, kind=F32),
            shaped(2 * HALF, 2 * HD, kind=F32), shaped(2 * HALF, 2 * HD, kind=F32), shaped(QKV, D),
        ],
        compiler_params=params("arbitrary"),
        cost_estimate=cost(2 * 2 * HALF * QKV * D, 8),
        name="project_qkv",
    )(place, *x_pieces, *w_pieces)


def project_kernel(left_ref, weight_ref, *parts):
    put_parts(pl.program_id(0), matmul(left_ref[...], weight_ref[...]).astype(BF16), parts)


def project(left, weight):
    depth = left.shape[1]
    return pl.pallas_call(
        project_kernel,
        grid=(4,),
        in_specs=[pl.BlockSpec((TILE, depth), lambda i: (i, 0)), pl.BlockSpec((depth, D), lambda i: (0, 0))],
        out_specs=PART_SPECS,
        out_shape=PART_SHAPES,
        compiler_params=params("arbitrary"),
        cost_estimate=cost(2 * 2 * HALF * depth * D, 8),
        name="project",
    )(left, weight)


def put_term(place, left, rows, term_ref):
    def one(i, carry):
        term = matmul(left, rows[:, pl.ds(pl.multiple_of(i * 4 * B, 4 * B), 4 * B)]).astype(BF16)
        for j in range(2):
            zx = 2 * i + j
            by = (zx % 4 + 4 - place[3]) % 4
            term_ref[by, zx // 4, 0] = term[:, 2 * j * B : (2 * j + 1) * B]
            term_ref[by, zx // 4, 1] = term[:, (2 * j + 1) * B : (2 * j + 2) * B]
        return carry

    lax.fori_loop(0, 4, one, 0)


def qkv_back_kernel(grad_q_ref, own_ref, later_ref, cosine_ref, sine_ref, scale_ref, weight_ref, *outs):
    parts, turned_ref = outs[:5], outs[5]
    cosine, sine = cosine_ref[...], sine_ref[...]
    lane = lax.broadcasted_iota(jnp.int32, cosine.shape, 1)
    pieces = []
    for i in range(2):
        part = grad_q_ref[0, :, i * 2 * HD : (i + 1) * 2 * HD]
        pieces.append(part * cosine - turned(part * sine))
    part = own_ref[0] + later_ref[0].astype(F32)
    pieces.append(jnp.where(lane < HD, part * cosine - turned(part * sine), part))
    grad_pre = jnp.concatenate(pieces, axis=1)
    put_parts(pl.program_id(0), matmul(grad_pre.astype(BF16), weight_ref[...]).astype(BF16), parts)
    turned_ref[...] = (grad_pre * scale_ref[...]).T.astype(BF16)


def qkv_back(grad_query, own, later, cosine, sine, scale, weight):
    tile = lambda lanes: pl.BlockSpec((TILE, lanes), lambda i: (i, 0))
    half = lambda lanes: pl.BlockSpec((1, TILE, lanes), lambda i: (i // 2, i % 2, 0))
    return pl.pallas_call(
        qkv_back_kernel,
        grid=(4,),
        in_specs=[
            half(HEADS * HD), half(2 * HD), half(2 * HD), tile(2 * HD), tile(2 * HD), tile(1),
            pl.BlockSpec((QKV, D), lambda i: (0, 0)),
        ],
        out_specs=PART_SPECS + [pl.BlockSpec((QKV, TILE), lambda i: (0, i))],
        out_shape=PART_SHAPES + [shaped(QKV, 2 * HALF)],
        compiler_params=params("arbitrary"),
        cost_estimate=cost(2 * 2 * HALF * QKV * D, 9),
        name="qkv_back",
    )(grad_query, own, later, cosine, sine, scale, weight)


def attention_term_kernel(*refs):
    place, token_refs, left_ref = refs[0], refs[1:6], refs[6]
    term_ref, rows, sems = refs[-3:]
    copies = put_tokens(token_refs, rows, sems, 0)
    for copy in copies:
        copy.start()
    left = left_ref[...]
    if left.shape[0] == 2 * HALF:
        left = left.T
    for copy in copies:
        copy.wait()
    put_term(place, left, rows, term_ref)


def attention_terms(place, pieces, left, name):
    whole = lambda *shape: pl.BlockSpec(shape, lambda i, p: (0,) * len(shape))
    rows = min(left.shape)
    return pl.pallas_call(
        attention_term_kernel,
        grid_spec=pltpu.PrefetchScalarGridSpec(
            num_scalar_prefetch=1,
            grid=(1,),
            in_specs=[ANYWHERE] * 5 + [whole(*left.shape)],
            out_specs=whole(4, 2, 2, rows, B),
            scratch_shapes=[pltpu.VMEM((2 * HALF, D), BF16), pltpu.SemaphoreType.DMA((10,))],
        ),
        out_shape=shaped(4, 2, 2, rows, B),
        compiler_params=params("arbitrary"),
        cost_estimate=cost(2 * 2 * HALF * rows * D, 7),
        name=name,
    )(place, *pieces, left)


def token_places(at, y, core):
    step = 1 - 2 * core
    block = jnp.where(
        at < B, y, jnp.where(at < 2 * B, y + 4 - step, jnp.where(at < 3 * B, y + 4 + step, y + 2))
    )
    row = at % B
    row = jnp.where(at < 3 * B, row, (row + core * (B // 2)) % B)
    return (block % 4) * B + row


def set_bias(place_ref, bias_ref):
    zlo, y, core = place_ref[0], place_ref[1], place_ref[2]
    key_at = token_places(lax.broadcasted_iota(jnp.int32, (HALF, 1), 0), y, core)
    query_at = token_places(lax.broadcasted_iota(jnp.int32, (1, HALF), 1), y, core)
    bias_ref[:HALF, :] = jnp.broadcast_to(jnp.where(zlo == 1, 0.0, -1e30), (HALF, HALF))
    bias_ref[HALF:, :] = jnp.where(key_at <= query_at, 0.0, -1e30)


def attention_kernel(place_ref, *refs):
    w_refs, query_ref, kv_ref, mixed_ref, log_ref = refs[:5], *refs[5:9]
    parts, w_out, bias_ref, weight, sems = refs[9:14], *refs[14:]
    columns = put_columns(place_ref, w_refs, weight, sems, 0)
    back = pltpu.make_async_copy(weight, w_out, sems.at[16])

    @pl.when(pl.program_id(0) == 0)
    def _():
        for copy in columns:
            copy.start()
        set_bias(place_ref, bias_ref)
        for copy in columns:
            copy.wait()
        back.start()

    key, value = kv_ref[0, :, :HD], kv_ref[0, :, HD:]
    for head in range(HEADS):
        scores = times_transposed(key, query_ref[0, head]) + bias_ref[...]
        top = jnp.max(scores, axis=0, keepdims=True)
        weights = jnp.exp(scores - top)
        total = jnp.sum(weights, axis=0, keepdims=True)
        low = (weights * (1.0 / total)).astype(BF16)
        mixed_ref[0, :, head * HD : (head + 1) * HD] = outer_sum(value, low).T.astype(BF16)
        log_ref[0, head] = top + jnp.log(total)
    put_rows(parts, matmul(mixed_ref[0], weight[...]).astype(BF16))

    @pl.when(pl.program_id(0) == 1)
    def _():
        back.wait()


def put_rows(parts, rows):
    row = 0
    for ref, length in zip(parts, LENGTHS):
        ref[0] = rows[row : row + length]
        row += length


def attention_back_kernel(place_ref, *refs):
    grad_refs, query_ref, kv_ref, log_ref, weight_ref = refs[:5], *refs[5:9]
    grad_query_ref, earlier_ref, own_ref, bias_ref, rows, sems = refs[9:]
    step = pl.program_id(0)
    copies = put_tokens(grad_refs, rows, sems, 0)

    @pl.when(step == 0)
    def _():
        for copy in copies:
            copy.start()
        set_bias(place_ref, bias_ref)
        for copy in copies:
            copy.wait()

    hidden = rows[pl.ds(pl.multiple_of(step * HALF, HALF), HALF), :]
    grads = times_transposed(hidden, weight_ref[...]).astype(BF16)
    key, value = kv_ref[0, :, :HD], kv_ref[0, :, HD:]
    grad_key = jnp.zeros((2 * HALF, HD), F32)
    grad_value = jnp.zeros((2 * HALF, HD), F32)
    for head in range(HEADS):
        lanes = slice(head * HD, (head + 1) * HD)
        query, grad = query_ref[0, head], grads[:, lanes]
        weights = jnp.exp(times_transposed(key, query) + bias_ref[...] - log_ref[0, head])
        grad_weights = times_transposed(value, grad)
        delta = jnp.sum(weights * grad_weights, axis=0, keepdims=True)
        grad_scores = (weights * (grad_weights - delta)).astype(BF16)
        grad_query_ref[0, :, lanes] = outer_sum(key, grad_scores).T * HD ** (-0.5)
        grad_key += matmul(grad_scores, query)
        grad_value += matmul(weights.astype(BF16), grad)
    total = jnp.concatenate([grad_key, grad_value], axis=1)
    earlier_ref[0] = total[:HALF].astype(BF16)
    own_ref[0] = total[HALF:]


def sequence_block(*tail):
    return pl.BlockSpec((1,) + tail, lambda s, place: (s,) + (0,) * len(tail))


def attention_call(kernel, in_specs, out_specs, out_shape, scratch, flops, name):
    return pl.pallas_call(
        kernel,
        grid_spec=pltpu.PrefetchScalarGridSpec(
            num_scalar_prefetch=1,
            grid=(2,),
            in_specs=in_specs,
            out_specs=out_specs,
            scratch_shapes=[pltpu.VMEM((2 * HALF, HALF), F32)] + scratch,
        ),
        out_shape=out_shape,
        compiler_params=params("arbitrary"),
        cost_estimate=cost(flops * 8 * 2 * HALF * HALF * HD * 2, 8),
        name=name,
    )


def attention(place, w_pieces, query, kv):
    return attention_call(
        attention_kernel,
        [ANYWHERE] * 5 + [sequence_block(HEADS, HALF, HD), sequence_block(2 * HALF, 2 * HD)],
        [sequence_block(HALF, HEADS * HD), sequence_block(HEADS, 1, HALF)]
        + [sequence_block(n, D) for n in LENGTHS]
        + [ANYWHERE],
        [shaped(2, HALF, HEADS * HD), shaped(2, HEADS, 1, HALF, kind=F32)] + PART_SHAPES + [shaped(HEADS * HD, D)],
        [pltpu.VMEM((HEADS * HD, D), BF16), pltpu.SemaphoreType.DMA((17,))],
        3,
        "attention",
    )(place, *w_pieces, query, kv)


def attention_back(place, grad_pieces, query, kv, log_total, weight):
    return attention_call(
        attention_back_kernel,
        [ANYWHERE] * 5
        + [
            sequence_block(HEADS, HALF, HD), sequence_block(2 * HALF, 2 * HD),
            sequence_block(HEADS, 1, HALF), pl.BlockSpec((HEADS * HD, D), lambda s, place: (0, 0)),
        ],
        [sequence_block(HALF, HEADS * HD), sequence_block(HALF, 2 * HD), sequence_block(HALF, 2 * HD)],
        [
            shaped(2, HALF, HEADS * HD, kind=F32),
            shaped(2, HALF, 2 * HD),
            shaped(2, HALF, 2 * HD, kind=F32),
        ],
        [pltpu.VMEM((2 * HALF, D), BF16), pltpu.SemaphoreType.DMA((10,))],
        6,
        "attention_back",
    )(place, *grad_pieces, query, kv, log_total, weight)


def finish_attention_kernel(place, *refs):
    piece_refs, w_query, w_key, w_value, gain_ref = refs[:4], *refs[4:8]
    query_out, key_out, value_out, gain_out, rows = refs[8:]
    for ref, by in zip(piece_refs, range(4)):
        at_y = (place[1] + by) % 4
        for c in range(2):
            piece = ref[c].astype(F32)
            rows[pl.ds(pl.multiple_of((2 * at_y + c) * HEADS * HD, HEADS * HD), HEADS * HD)] = piece[: HEADS * HD]
        both = ref[0].astype(F32) + ref[1].astype(F32)
        at = pl.multiple_of(H * HD + at_y * HD, HD)
        rows[pl.ds(at, HD)] = both[HEADS * HD : (HEADS + 1) * HD]
        rows[pl.ds(at + KV * HD, HD)] = both[(HEADS + 1) * HD :]
    gain = gain_ref[...]
    total = jnp.zeros((B, 1), F32)
    row = 0
    for weight, out in ((w_query, query_out), (w_key, key_out), (w_value, value_out)):
        for i in range(out.shape[1] // B):
            lanes = slice(i * B, (i + 1) * B)
            block = rows[row : row + B].T
            total = total + jnp.sum(block * weight[:, lanes].astype(F32), axis=1, keepdims=True)
            out[:, lanes] = block * gain
            row += B
    gain_out[...] = total


def finish_attention(place, pieces, w_query, w_key, w_value, gain):
    whole = lambda *shape: pl.BlockSpec(shape, lambda i, p: (0,) * len(shape))
    kv = KV * HD
    return pl.pallas_call(
        finish_attention_kernel,
        grid_spec=pltpu.PrefetchScalarGridSpec(
            num_scalar_prefetch=1,
            grid=(1,),
            in_specs=[whole(2, QKV, B)] * 4 + [whole(B, D), whole(B, kv), whole(B, kv), whole(B, 1)],
            out_specs=[whole(B, D), whole(B, kv), whole(B, kv), whole(B, 1)],
            scratch_shapes=[pltpu.VMEM((D + 2 * kv, B), F32)],
        ),
        out_shape=[
            shaped(B, D, kind=F32), shaped(B, kv, kind=F32), shaped(B, kv, kind=F32), shaped(B, 1, kind=F32),
        ],
        compiler_params=params("arbitrary"),
        cost_estimate=cost(0, 4),
        name="finish_attention",
    )(place, *pieces, w_query, w_key, w_value, gain)


def finish_output_kernel(blocks, out):
    for i in range(16):
        out[:, i * B : (i + 1) * B] = blocks[i].astype(F32)


def finish_output(blocks):
    return pl.pallas_call(
        finish_output_kernel,
        out_shape=shaped(B, D, kind=F32),
        compiler_params=params(),
        cost_estimate=cost(0, 2),
        name="finish_output",
    )(blocks)


def feed_forward_kernel(*refs):
    place, token_refs, grad_refs, ff_ref = refs[0], refs[1:6], refs[6:11], refs[11]
    act_ref, act_t, gate_t, up_t = refs[12:16]
    parts, down_out = refs[16:21], refs[21]
    rows_h, rows_g, gate_up, down, slabs, sems = refs[22:]
    step = pl.program_id(0)
    tokens = put_tokens(token_refs, rows_h, sems, 0)
    grads = put_tokens(grad_refs, rows_g, sems, 10)
    weights, loads = [], []
    for x in range(4):
        for by in range(4):
            z = (2 * place[4] + place[0] + by) % 4
            zhi, zlo = z // 2, z % 2
            for core in range(2):
                weights.append(
                    pltpu.make_async_copy(
                        ff_ref.at[x, by, pl.ds(core * FFL, FFL)],
                        gate_up.at[zlo, :, lane_block(zhi, x, core)],
                        sems.at[20 + len(weights)],
                    )
                )
            loads.append(
                pltpu.make_async_copy(
                    ff_ref.at[x, by, pl.ds(2 * FFL, FFL)], slabs.at[zlo, zhi * 4 + x], sems.at[52 + len(loads)]
                )
            )
    back = pltpu.make_async_copy(down, down_out, sems.at[68])

    @pl.when(step == 0)
    def _():
        for copy in tokens + weights + loads + grads:
            copy.start()
        for copy in tokens + weights:
            copy.wait()

    rows = pl.ds(pl.multiple_of(step * HALF, HALF), HALF)
    normed = rows_h[rows, :]
    gate_pre = times_transposed(normed, gate_up[0])
    upward = times_transposed(normed, gate_up[1])

    @pl.when(step == 0)
    def _():
        for copy in loads:
            copy.wait()

        def put(q, carry):
            for half in range(2):
                for p in range(4):
                    one = slabs[half, 2 * q, 2 * p * PIECE : 2 * (p + 1) * PIECE, :].astype(F32)
                    two = slabs[half, 2 * q + 1, 2 * p * PIECE : 2 * (p + 1) * PIECE, :].astype(F32)
                    lane = (half * 8 + 2 * p) * B
                    rows = pl.ds(pl.multiple_of(q * 2 * PIECE, 16), 2 * PIECE)
                    down[rows, lane : lane + B] = jnp.concatenate([one[:PIECE], two[:PIECE]], axis=0).astype(BF16)
                    down[rows, lane + B : lane + 2 * B] = jnp.concatenate(
                        [one[PIECE:], two[PIECE:]], axis=0
                    ).astype(BF16)
            return carry

        lax.fori_loop(0, 4, put, 0)
        back.start()
        for copy in grads:
            copy.wait()

    grad_act = times_transposed(rows_g[rows, :], down[...])
    sigmoid = 1.0 / (1.0 + jnp.exp(-gate_pre))
    silu = gate_pre * sigmoid
    activation = silu * upward
    grad_up = grad_act * silu
    grad_gate = grad_act * upward * (sigmoid * (1.0 + gate_pre * (1.0 - sigmoid)))
    part = matmul(grad_gate.astype(BF16), gate_up[0]) + matmul(grad_up.astype(BF16), gate_up[1])
    part = part.astype(BF16)
    row = 0
    for ref, length in zip(parts, LENGTHS):
        ref[0] = part[row : row + length]
        row += length
    act_ref[...] = activation.astype(BF16)
    act_t[...] = activation.T.astype(BF16)
    gate_t[...] = grad_gate.T.astype(BF16)
    up_t[...] = grad_up.T.astype(BF16)

    @pl.when(step == 1)
    def _():
        back.wait()


def feed_forward(place, tokens, grads, ff_all):
    turned_spec = pl.BlockSpec((FFL, HALF), lambda i, p: (0, i))
    turned_shape = shaped(FFL, 2 * HALF)
    return pl.pallas_call(
        feed_forward_kernel,
        grid_spec=pltpu.PrefetchScalarGridSpec(
            num_scalar_prefetch=1,
            grid=(2,),
            in_specs=[ANYWHERE] * 11,
            out_specs=[pl.BlockSpec((HALF, FFL), lambda i, p: (i, 0))]
            + [turned_spec] * 3
            + [pl.BlockSpec((1, n, D), lambda i, p: (i, 0, 0)) for n in LENGTHS]
            + [ANYWHERE],
            scratch_shapes=[
                pltpu.VMEM((2 * HALF, D), BF16),
                pltpu.VMEM((2 * HALF, D), BF16),
                pltpu.VMEM((2, FFL, D), BF16),
                pltpu.VMEM((FFL, D), BF16),
                pltpu.VMEM((2, 8, FFL, B), BF16),
                pltpu.SemaphoreType.DMA((69,)),
            ],
        ),
        out_shape=[shaped(2 * HALF, FFL)] + [turned_shape] * 3 + PART_SHAPES + [shaped(FFL, D)],
        compiler_params=params("arbitrary"),
        cost_estimate=cost(2 * 5 * 2 * HALF * FFL * D, 32),
        name="feed_forward",
    )(place, *tokens, *grads, ff_all)


def along_z(place, zhi, zlo):
    return (2 * zhi + zlo + 4 - 2 * place[4] - place[0]) % 4


def gate_up_kernel(*refs):
    place, token_refs, gate_t, up_t, out_ref, rows, sems = refs[0], refs[1:6], *refs[6:]
    step = pl.program_id(0)
    copies = put_tokens(token_refs, rows, sems, 0)

    @pl.when(step == 0)
    def _():
        for copy in copies:
            copy.start()
        for copy in copies:
            copy.wait()

    normed = rows[:, pl.ds(pl.multiple_of(step * 4 * B, 4 * B), 4 * B)]
    for matrix, left in ((0, gate_t), (1, up_t)):
        term = matmul(left[...], normed).astype(BF16)
        for j in range(2):
            zx = 2 * step + j
            by = along_z(place, zx // 4, matrix)
            out_ref[zx % 4, by, 0:FFL, :] = term[:, 2 * j * B : (2 * j + 1) * B]
            out_ref[zx % 4, by, FFL:, :] = term[:, (2 * j + 1) * B : (2 * j + 2) * B]


def down_kernel(*refs):
    place, grad_refs, act_t, out_ref, rows, sems = refs[0], refs[1:6], *refs[6:]
    step = pl.program_id(0)
    copies = put_tokens(grad_refs, rows, sems, 0)

    @pl.when(step == 0)
    def _():
        for copy in copies:
            copy.start()
        for copy in copies:
            copy.wait()

    term = matmul(act_t[...], rows[:, pl.ds(pl.multiple_of(step * 4 * B, 4 * B), 4 * B)])
    for j in range(2):
        half, p = step // 2, (2 * step + j) % 4
        at = pl.ds(pl.multiple_of(p * 2 * PIECE, 16), 2 * PIECE)
        for zx in range(8):
            slab = term[zx * PIECE : (zx + 1) * PIECE]
            low, high = slab[:, 2 * j * B : (2 * j + 1) * B], slab[:, (2 * j + 1) * B : (2 * j + 2) * B]
            slab = jnp.concatenate([low, high], axis=0).astype(BF16)
            out_ref[zx % 4, along_z(place, zx // 4, half), at, :] = slab


def ff_terms(kernel, place, pieces, lefts, rows, name):
    whole = pl.BlockSpec((FFL, 2 * HALF), lambda i, p: (0, 0))
    return pl.pallas_call(
        kernel,
        grid_spec=pltpu.PrefetchScalarGridSpec(
            num_scalar_prefetch=1,
            grid=(4,),
            in_specs=[ANYWHERE] * 5 + [whole] * len(lefts),
            out_specs=pl.BlockSpec((4, 4, rows, B), lambda i, p: (0, 0, 0, 0)),
            scratch_shapes=[pltpu.VMEM((2 * HALF, D), BF16), pltpu.SemaphoreType.DMA((10,))],
        ),
        out_shape=shaped(4, 4, rows, B),
        compiler_params=params("arbitrary"),
        cost_estimate=cost(2 * len(lefts) * 2 * HALF * FFL * D, 8 + 4 * len(lefts)),
        name=name,
    )(place, *pieces, *lefts)


def finish_hidden_kernel(*refs):
    place, piece_refs, weight_ref, gain_ref, out_ref, gain_out, rows = refs[0], refs[1:5], *refs[5:]
    y = place[1]
    for ref, by in zip(piece_refs, (0, 1, 2, 3)):
        at_y = (y + by) % 4
        for core in range(2):
            slab = ref[core].astype(F32)
            for zx in range(8):
                at = pl.multiple_of((2 * zx + core) * 4 * PIECE + at_y * PIECE, 8)
                rows[pl.ds(at, PIECE)] = slab[zx * PIECE : (zx + 1) * PIECE]
    gain = gain_ref[...]
    total = jnp.zeros((B, 1), F32)
    for i in range(FF // B):
        lanes = slice(i * B, (i + 1) * B)
        block = rows[lanes].T
        total = total + jnp.sum(block * weight_ref[:, lanes].astype(F32), axis=1, keepdims=True)
        out_ref[:, lanes] = block * gain
    gain_out[...] = total


def finish_hidden(place, pieces, weight, gain):
    whole = lambda *shape: pl.BlockSpec(shape, lambda i, p: (0,) * len(shape))
    return pl.pallas_call(
        finish_hidden_kernel,
        grid_spec=pltpu.PrefetchScalarGridSpec(
            num_scalar_prefetch=1,
            grid=(1,),
            in_specs=[whole(2, FFL, B)] * 4 + [whole(B, FF), whole(B, 1)],
            out_specs=[whole(B, FF), whole(B, 1)],
            scratch_shapes=[pltpu.VMEM((FF, B), F32)],
        ),
        out_shape=[shaped(B, FF, kind=F32), shaped(B, 1, kind=F32)],
        compiler_params=params("arbitrary"),
        cost_estimate=cost(0, 6),
        name="finish_hidden",
    )(place, *pieces, weight, gain)


def finish_down_kernel(place, *refs):
    piece_refs, out_ref = refs[:4], refs[4]
    for ref, by in zip(piece_refs, range(4)):
        rows = pl.ds(pl.multiple_of((place[1] + by) % 4 * PIECE, 8), PIECE)
        for half in range(2):
            slab = ref[half].astype(F32)
            for t in range(8):
                lane = (half * 8 + t) * B
                out_ref[rows, lane : lane + B] = slab[t * PIECE : (t + 1) * PIECE]


def finish_down(place, pieces):
    whole = lambda *shape: pl.BlockSpec(shape, lambda i, p: (0,) * len(shape))
    return pl.pallas_call(
        finish_down_kernel,
        grid_spec=pltpu.PrefetchScalarGridSpec(
            num_scalar_prefetch=1,
            grid=(1,),
            in_specs=[whole(2, FFL, B)] * 4,
            out_specs=whole(4 * PIECE, D),
            scratch_shapes=[],
        ),
        out_shape=shaped(4 * PIECE, D, kind=F32),
        compiler_params=params("arbitrary"),
        cost_estimate=cost(0, 5),
        name="finish_down",
    )(place, *pieces)


def own_rows(rows_all, y, core, per):
    return lax.dynamic_slice_in_dim(rows_all, (2 * y + core) * per, per, 0)


class Flow:
    def __init__(self, steps):
        self.steps, self.result, self.sent = steps, None, None
        self.move(None)

    def move(self, arrived):
        try:
            self.sent = self.steps.send(arrived)
        except StopIteration as end:
            self.sent, self.result = (), end.value


def stage(flows, *values):
    flows = [flow for flow in flows if flow.result is None]
    sizes = [len(flow.sent) for flow in flows]
    leaves, tree = jax.tree.flatten(values)
    tied = tie(*[v for flow in flows for v in flow.sent], *leaves)
    for flow, size in zip(flows, sizes):
        flow.move(tied[:size])
        tied = tied[size:]
    return jax.tree.unflatten(tree, tied)


def gather_steps(block):
    (other,) = yield (swap_core(block),)
    pair = jnp.stack([block, other])
    (got,) = yield (along_y(pair),)
    far, swapped = yield (along_y(send_half(got)), swap_core(got))
    (far_swapped,) = yield (swap_core(far),)
    return pair, got, swapped, far, far_swapped


def scatter_steps(parts):
    core = lax.axis_index("core")
    first, behind, ahead, far, far_other = parts
    (far_got,) = yield (swap_core(far_other),)
    far = add(far, far_got[::-1]).astype(BF16)
    low, behind_got, first_got = yield (along_y(far), swap_core(behind), swap_core(first[1]))
    ahead = add(ahead, behind_got[::-1])
    mine = lax.dynamic_slice_in_dim(ahead, core * (B // 2), B // 2, 1) + low.astype(F32)
    ahead = lax.dynamic_update_slice_in_dim(ahead, mine, core * (B // 2), 1).astype(BF16)
    (got,) = yield (along_y(ahead),)
    (last,) = yield (swap_core(got[1]),)
    return add(first[0], first_got) + got[0].astype(F32) + last.astype(F32)


def ring_gather_steps(block, axis):
    half = block.shape[0] // 2
    before, after = yield (shift(block, axis, 1), shift(block, axis, -1))
    low, high = yield (shift(before[:half], axis, 1), shift(after[half:], axis, -1))
    return block, after, low, high, before


def ring_scatter_steps(parts, axis):
    half = parts[2].shape[0] // 2
    low, high = yield (shift(parts[2][:half], axis, 1), shift(parts[2][half:], axis, -1))
    after = jnp.concatenate([add(parts[1][:half], low).astype(BF16), parts[1][half:]], axis=0)
    before = jnp.concatenate([parts[3][:half], add(parts[3][half:], high).astype(BF16)], axis=0)
    from_before, from_after = yield (shift(after, axis, 1), shift(before, axis, -1))
    return add(parts[0], from_before) + from_after.astype(F32)


def on_device(
    layer_input,
    positions,
    attn_gain,
    w_query,
    w_key,
    w_value,
    w_output,
    mlp_gain,
    w_gate,
    w_up,
    w_down,
    out_grad,
):
    zlo, y, zhi, x, core = (lax.axis_index(axis) for axis in AXES)
    place = jnp.stack([zlo, y, core, x, zhi]).astype(jnp.int32)

    def by_core(mine, got):
        return jnp.where(core == 0, jnp.stack([mine, got]), jnp.stack([got, mine]))

    def by_zlo(mine, got):
        return jnp.where(zlo == 0, jnp.stack([mine, got]), jnp.stack([got, mine]))

    def by_zhi(mine, got):
        return jnp.where(zhi == 0, jnp.stack([mine, got]), jnp.stack([got, mine]))

    def trio(mine, other, axis):
        across = lax.ppermute(other, (axis, "core"), [(i, 3 - i) for i in range(4)])
        return shift(mine, axis, 1), swap_core(other), across

    def column_steps(mine, got):
        pair = by_core(mine, got)
        (got,) = yield (shift(pair, "zhi", 1),)
        return (yield from ring_gather_steps(by_zhi(pair, got), "x"))

    def output_steps(mine, other):
        there, here, across = yield trio(mine, other, "zhi")
        column = by_zhi(by_core(mine, here), by_core(there, across))
        return (yield from ring_gather_steps(column, "x"))

    def hidden_steps(mine, got, down):
        piece = jnp.concatenate([by_core(mine, got).reshape(2 * FFL, B), down], axis=0)
        pieces = yield from ring_gather_steps(piece, "z")
        return jnp.concatenate(pieces, axis=0).reshape(4, 3 * FFL, B)

    def of_core(pair, other=False):
        return lax.dynamic_index_in_dim(pair, 1 - core if other else core, 0, keepdims=False)

    def whole_ring(pieces):
        own, after, low, high, before = pieces
        return own, after, jnp.concatenate([low, high], axis=0), before

    def attention_steps(terms):
        column = yield from ring_scatter_steps([terms[i] for i in range(4)], "x")
        keep = lax.dynamic_index_in_dim(column, zhi, 0, keepdims=False)
        send = lax.dynamic_index_in_dim(column, 1 - zhi, 0, keepdims=False).astype(BF16)
        (got,) = yield (shift(send, "zhi", 1),)
        pair = (keep + got.astype(F32)).astype(BF16)
        mine, other = of_core(pair), of_core(pair, True)
        there, here, across = yield trio(mine, other, "zlo")
        own = by_core(add(mine, there), add(here, across)).astype(BF16)
        return whole_ring((yield from ring_gather_steps(own, "y")))

    def ff_steps(sums):
        own = yield from ring_scatter_steps([sums[i] for i in range(4)], "z")
        own = own.astype(BF16)
        pair, down = own[: 2 * FFL].reshape(2, FFL, B), own[2 * FFL :]
        mine, other = of_core(pair), of_core(pair, True)
        there, here, across = yield trio(jnp.concatenate([mine, down], axis=0), other, "zlo")
        both = by_zlo(by_core(mine, here), by_core(there[:FFL], across))
        both = jnp.concatenate([both, by_zlo(down, there[FFL:])[:, None]], axis=1)
        ring = whole_ring((yield from ring_gather_steps(both, "y")))
        return [piece[:, :2] for piece in ring], [piece[:, 2] for piece in ring]

    x_low = layer_input[0]
    frequency = theta ** (-jnp.arange(0, HD, 2).astype(F32) / HD)
    angles = positions[0].astype(F32)[:, None] * frequency
    tables = []
    for table in (jnp.cos(angles), jnp.sin(angles)):
        high = lax.reduce_precision(table, 8, 7)
        tables += [high.astype(BF16), (table - high).astype(BF16)]
    tokens = Flow(gather_steps(jnp.concatenate([x_low, *tables], axis=1)))
    grads = Flow(gather_steps(out_grad[0]))
    qkv_mine, qkv_other = prepare_qkv(place, w_query, w_key, w_value, attn_gain[:, None])
    qkv_mine, qkv_got, gain_two, w_out = stage([tokens], qkv_mine, swap_core(qkv_other), mlp_gain[:, None], w_output)

    columns = Flow(column_steps(qkv_mine, qkv_got))
    o_rows = lax.all_to_all(w_out.reshape(B, 16, B).transpose(1, 0, 2), FSDP, 0, 0, tiled=True)
    ff_mine, ff_other, ff_down = prepare_ff(place, w_gate, w_up, w_down, gain_two)
    ff_mine, ff_got, ff_down, x_low = stage([tokens, columns], ff_mine, swap_core(ff_other), ff_down, x_low)

    hidden_rows = Flow(hidden_steps(ff_mine, ff_got, ff_down))
    inputs = x_low.astype(F32)
    scale_one = lax.rsqrt(jnp.mean(inputs * inputs, axis=-1, keepdims=True) + eps)
    scale_one, o_rows = stage([tokens, columns, grads, hidden_rows], scale_one, o_rows)

    o_rows = o_rows.reshape(D, B)
    mine, other = own_rows(o_rows, y, core, HEADS * HD), own_rows(o_rows, y, 1 - core, HEADS * HD)
    outputs = Flow(output_steps(mine, other))
    stage([tokens, columns, outputs])

    x_pieces = tokens.result
    query, key_value, scale_all, cosine, sine, qkv_full = project_qkv(place, x_pieces, columns.result)
    query, key_value = stage([hidden_rows, outputs], query, key_value)

    ff_all = lax.all_gather(hidden_rows.result, "x", axis=0, tiled=False)
    earlier = lax.ppermute(key_value, "zlo", [(0, 1)])
    query, key_value, earlier = stage([grads, outputs], query, key_value, earlier)

    key_value = jnp.concatenate([earlier, key_value], axis=1)
    mixed, log_total, *parts, o_full = attention(place, outputs.result, query, key_value)
    parts = stage([grads], *parts)
    sums = Flow(scatter_steps(parts))
    stage([sums, grads])
    grad_pieces = grads.result
    for _ in range(3):
        stage([sums])
    hidden = inputs + sums.result
    scale_two = lax.rsqrt(jnp.mean(hidden * hidden, axis=-1, keepdims=True) + eps)
    normed = Flow(gather_steps((hidden * scale_two).astype(BF16)))
    for _ in range(4):
        stage([normed])
    normed_pieces = normed.result

    activation, act_t, gate_t, up_t, *parts, down_full = feed_forward(place, normed_pieces, grad_pieces, ff_all)
    sums = Flow(scatter_steps(parts))
    (act_t,) = stage([sums], act_t)
    down_terms = ff_terms(down_kernel, place, grad_pieces, (act_t,), FFL, "down_terms")
    down_terms, gate_t = stage([sums], down_terms, gate_t)
    down_sum = lax.psum_scatter(down_terms, "x", scatter_dimension=0, tiled=True)[0]
    gate_up_terms = ff_terms(gate_up_kernel, place, normed_pieces, (gate_t, up_t), 2 * FFL, "gate_up_terms")
    (gate_up_terms,) = stage([sums], gate_up_terms)
    gate_up_sum = lax.psum_scatter(gate_up_terms, "x", scatter_dimension=0, tiled=True)[0]
    stage([sums])

    grad_normed_two = sums.result
    mean_two = jnp.mean(grad_normed_two * hidden, axis=-1, keepdims=True)
    grad_hidden = (
        out_grad[0].astype(F32)
        + scale_two * grad_normed_two
        - hidden * (scale_two * scale_two * scale_two) * mean_two
    )
    hidden_grads = Flow(gather_steps(grad_hidden.astype(BF16)))
    (activation,) = stage([hidden_grads], activation)
    down_parts = project(activation, down_full)
    down_parts = stage([hidden_grads], *down_parts)
    result = Flow(scatter_steps(down_parts))
    stage([hidden_grads, result])
    stage([hidden_grads])

    hidden_grad_pieces = hidden_grads.result
    grad_query, grad_earlier, grad_own = attention_back(
        place, hidden_grad_pieces, query, key_value, log_total, o_full
    )
    grad_query, grad_earlier, grad_own, mixed = stage([result], grad_query, grad_earlier, grad_own, mixed)
    later = lax.ppermute(grad_earlier, "zlo", [(1, 0)])
    output_terms = attention_terms(place, hidden_grad_pieces, mixed.reshape(2 * HALF, HEADS * HD), "output_terms")
    later, grad_query, output_terms, down_sum, gate_up_sum = stage(
        [result], later, grad_query, output_terms, down_sum, gate_up_sum
    )
    ff_sums = Flow(ff_steps(jnp.concatenate([gate_up_sum, down_sum], axis=1)))
    output_sums = Flow(attention_steps(output_terms))
    *parts, grad_t = qkv_back(grad_query, grad_own, later, cosine, sine, scale_all, qkv_full)
    *parts, grad_t = stage([ff_sums, output_sums, result], *parts, grad_t)

    sums = Flow(scatter_steps(parts))
    terms = attention_terms(place, x_pieces, grad_t, "qkv_terms")
    (terms,) = stage([sums, ff_sums, output_sums], terms)
    attention_sums = Flow(attention_steps(terms))
    stage([sums, attention_sums, ff_sums, output_sums])
    stage([sums, attention_sums, output_sums])
    stage([sums, attention_sums])
    grad_normed = sums.result
    mean_one = jnp.mean(grad_normed * inputs, axis=-1, keepdims=True)
    input_grad = (
        grad_hidden
        + scale_one * grad_normed
        - inputs * (scale_one * scale_one * scale_one) * mean_one
    )
    input_grad = input_grad.astype(BF16)
    stage([attention_sums, output_sums, ff_sums])
    stage([attention_sums, output_sums])

    ring = jnp.roll(jnp.stack(output_sums.result), y, axis=0).reshape(16, B, B)
    output_grad = lax.all_to_all(ring, FSDP, 0, 0, tiled=True)
    stage([attention_sums, ff_sums])

    gate_up, down = ff_sums.result
    gain_two = mlp_gain[:, None]
    query_grad, key_grad, value_grad, attn_gain_grad = finish_attention(
        place, attention_sums.result, w_query, w_key, w_value, attn_gain[:, None]
    )
    gate_grad, gate_gain = finish_hidden(place, [p[0] for p in gate_up], w_gate, gain_two)
    up_grad, up_gain = finish_hidden(place, [p[1] for p in gate_up], w_up, gain_two)
    down_grad = finish_down(place, down)
    output_grad = finish_output(output_grad)
    return (
        (hidden + result.result).astype(BF16)[None],
        input_grad[None],
        attn_gain_grad[:, 0],
        query_grad,
        key_grad,
        value_grad,
        output_grad,
        (gate_gain + up_gain)[:, 0],
        gate_grad,
        up_grad,
        down_grad,
    )


def solution(mesh):
    split = Mesh(mesh.devices.reshape(2, 4, 2, 4, 2), AXES)
    tokens = P(FSDP, SEQ, None)
    rows = P(FSDP, None)
    gain = P(FSDP)
    in_specs = (
        tokens, P(FSDP, SEQ), gain, rows, rows, rows, rows, gain, rows, rows, rows, tokens,
    )
    out_specs = (tokens, tokens, gain, rows, rows, rows, rows, gain, rows, rows, rows)
    return jax.shard_map(
        on_device, mesh=split, in_specs=in_specs, out_specs=out_specs, check_vma=False
    )
```

```python
import jax
import jax.numpy as jnp
from jax import lax
from jax.experimental import pallas as pl
from jax.experimental.pallas import tpu as pltpu
from jax.sharding import Mesh
from jax.sharding import PartitionSpec as P

H = 32
KV = 4
HD = 64
D = 2048
FF = 5632
B = 128
HALF = 512
HEADS = 4
FFL = 704
PIECE = 88

eps = 1e-05
theta = 10000.0
F32 = jnp.float32
BF16 = jnp.bfloat16
AXES = ("zlo", "y", "zhi", "x", "core")
FSDP = ("zhi", "x", "core")
SEQ = ("zlo", "y")


def matmul(left, right):
    return jnp.dot(left, right, preferred_element_type=F32)


def times_transposed(left, right):
    return lax.dot_general(left, right, (((1,), (1,)), ((), ())), preferred_element_type=F32)


def outer_sum(left, right):
    return lax.dot_general(left, right, (((0,), (0,)), ((), ())), preferred_element_type=F32)


def shift(value, axis, by):
    if axis == "z":
        at = [2 * (z % 2) + z // 2 for z in range(4)]
        return lax.ppermute(value, ("zlo", "zhi"), [(at[z], at[(z + by) % 4]) for z in range(4)])
    size = lax.axis_size(axis)
    return lax.ppermute(value, axis, [(i, (i + by) % size) for i in range(size)])


def swap_core(value):
    return shift(value, "core", 1)


def small_gather(block, axis):
    return shift(block, axis, -1), shift(block, axis, 2), shift(block, axis, 1)


def tie(*values):
    return lax.optimization_barrier(values)


def add(left, right):
    return left.astype(F32) + right.astype(F32)


def along_y(value):
    pairs = []
    for i in range(4):
        pairs.append((2 * i, 2 * ((i + 1) % 4)))
        pairs.append((2 * i + 1, 2 * ((i + 3) % 4) + 1))
    return lax.ppermute(value, ("y", "core"), pairs)


def send_half(got):
    core = lax.axis_index("core")
    return lax.dynamic_slice_in_dim(got, core * (B // 2), B // 2, 1)


FLIPPED = (0, 0, 1, 0, 1)
LENGTHS = (B, B, B, B // 2, B // 2)


def put_tokens(refs, rows_ref, sems, start):
    lanes = pl.ds(0, rows_ref.shape[1])
    copies = []
    row = 0
    for s in range(2):
        for ref, flip, length in zip(refs, FLIPPED, LENGTHS):
            copies.append(
                pltpu.make_async_copy(
                    ref.at[s ^ flip, :, lanes], rows_ref.at[pl.ds(row, length)], sems.at[start + len(copies)]
                )
            )
            row += length
    return copies


TILE = 256
WIDE = D + B
VMEM_LIMIT = 56 * 2**20
ANYWHERE = pl.BlockSpec(memory_space=pl.ANY)


def params(*kinds):
    return pltpu.CompilerParams(dimension_semantics=kinds or None, vmem_limit_bytes=VMEM_LIMIT)


def cost(flops, megabytes):
    return pl.CostEstimate(flops=flops, bytes_accessed=int(megabytes * 2**20), transcendentals=0)


def shaped(*shape, kind=BF16):
    return jax.ShapeDtypeStruct(shape, kind)


PART_SPECS = [pl.BlockSpec((1, n, D), lambda i, *_: (i // 2, 0, 0)) for n in LENGTHS]
PART_SHAPES = [jax.ShapeDtypeStruct((2, n, D), BF16) for n in LENGTHS]


def put_parts(step, tile, refs):
    @pl.when(step % 2 == 0)
    def _():
        refs[0][0] = tile[:B]
        refs[1][0] = tile[B:]

    @pl.when(step % 2 == 1)
    def _():
        refs[2][0] = tile[:B]
        refs[3][0] = tile[B : B + B // 2]
        refs[4][0] = tile[B + B // 2 :]


def turned(values):
    lane = lax.broadcasted_iota(jnp.int32, values.shape, 1) % HD
    return jnp.where(lane < HD // 2, -pltpu.roll(values, 2 * HD - HD // 2, 1), pltpu.roll(values, HD // 2, 1))


def lane_block(zhi, x, core):
    return pl.ds(pl.multiple_of((zhi * 8 + x * 2 + core) * B, B), B)


def put_columns(place, refs, into, sems, start):
    copies = []
    for ref, by, first in zip(refs, (0, 1, 2, 2, 3), (0, 0, 0, 1, 0)):
        for i in range(ref.shape[0]):
            for core in range(2):
                lanes = lane_block(first + i, (place[3] + by) % 4, core)
                copies.append(
                    pltpu.make_async_copy(ref.at[i, core], into.at[:, lanes], sems.at[start + len(copies)])
                )
    return copies


def prepare_qkv_kernel(place, q_mine, q_other, w_key, w_value, gain, mine_ref, other_ref, k_rows, v_rows):
    scale = gain[...]
    k_rows[...] = (w_key[...].astype(F32) * scale).T
    v_rows[...] = (w_value[...].astype(F32) * scale).T
    rows = pl.ds(pl.multiple_of(place[1] * HD, HD), HD)
    for source, out in ((q_mine, mine_ref), (q_other, other_ref)):
        out[: HEADS * HD] = (source[...].astype(F32) * scale).T.astype(BF16)
        out[HEADS * HD : (HEADS + 1) * HD] = k_rows[rows].astype(BF16)
        out[(HEADS + 1) * HD :] = v_rows[rows].astype(BF16)


QKV = (HEADS + 2) * HD


def prepare_qkv(place, w_query, w_key, w_value, gain):
    whole = lambda *shape: pl.BlockSpec(shape, lambda i, p: (0,) * len(shape))
    return pl.pallas_call(
        prepare_qkv_kernel,
        grid_spec=pltpu.PrefetchScalarGridSpec(
            num_scalar_prefetch=1,
            grid=(1,),
            in_specs=[
                pl.BlockSpec((B, HEADS * HD), lambda i, p: (0, 2 * p[1] + p[2])),
                pl.BlockSpec((B, HEADS * HD), lambda i, p: (0, 2 * p[1] + 1 - p[2])),
                whole(B, KV * HD), whole(B, KV * HD), whole(B, 1),
            ],
            out_specs=[whole(QKV, B), whole(QKV, B)],
            scratch_shapes=[pltpu.VMEM((KV * HD, B), F32), pltpu.VMEM((KV * HD, B), F32)],
        ),
        out_shape=[shaped(QKV, B), shaped(QKV, B)],
        compiler_params=params("arbitrary"),
        cost_estimate=cost(0, 1),
        name="prepare_qkv",
    )(place, w_query, w_query, w_key, w_value, gain)


def prepare_ff_kernel(place, w_gate, w_up, w_down, gain, mine_ref, other_ref, down_ref, picked, rows, down_rows, sems):
    zlo, y, core = place[0], place[1], place[2]
    down = pltpu.make_async_copy(
        w_down.at[:, pl.ds(pl.multiple_of(zlo * (D // 2), D // 2), D // 2)], down_rows, sems.at[1]
    )
    down.start()

    @pl.when(zlo == 0)
    def _():
        copy = pltpu.make_async_copy(w_gate, picked, sems.at[0])
        copy.start()
        copy.wait()

    @pl.when(zlo == 1)
    def _():
        copy = pltpu.make_async_copy(w_up, picked, sems.at[0])
        copy.start()
        copy.wait()

    scale = gain[...]
    for i in range(FF // B):
        rows[i * B : (i + 1) * B] = (picked[:, i * B : (i + 1) * B].astype(F32) * scale).T
    for which, out in ((core, mine_ref), (1 - core, other_ref)):
        slabs = []
        for zx in range(8):
            at = pl.multiple_of(zx * 2 * 4 * PIECE + which * 4 * PIECE + y * PIECE, 8)
            slabs.append(rows[pl.ds(at, PIECE)])
        out[...] = jnp.concatenate(slabs, axis=0).astype(BF16)
    down.wait()
    for t in range(8):
        rows[t * 4 * PIECE : (t + 1) * 4 * PIECE] = down_rows[:, t * B : (t + 1) * B].astype(F32)
    slabs = [rows[pl.ds(pl.multiple_of(t * 4 * PIECE + y * PIECE, 8), PIECE)] for t in range(8)]
    down_ref[...] = jnp.concatenate(slabs, axis=0).astype(BF16)


def prepare_ff(place, w_gate, w_up, w_down, gain):
    return pl.pallas_call(
        prepare_ff_kernel,
        grid_spec=pltpu.PrefetchScalarGridSpec(
            num_scalar_prefetch=1,
            grid=(1,),
            in_specs=[ANYWHERE, ANYWHERE, ANYWHERE, pl.BlockSpec((B, 1), lambda i, p: (0, 0))],
            out_specs=[pl.BlockSpec((FFL, B), lambda i, p: (0, 0))] * 3,
            scratch_shapes=[
                pltpu.VMEM((B, FF), BF16),
                pltpu.VMEM((FF, B), F32),
                pltpu.VMEM((4 * PIECE, D // 2), BF16),
                pltpu.SemaphoreType.DMA((2,)),
            ],
        ),
        out_shape=[shaped(FFL, B)] * 3,
        compiler_params=params("arbitrary"),
        cost_estimate=cost(0, 6),
        name="prepare_ff",
    )(place, w_gate, w_up, w_down, gain)


def project_qkv_kernel(*refs):
    place, x_refs, w_refs = refs[0], refs[1:6], refs[6:11]
    query_ref, kv_ref, scale_ref, cosine_ref, sine_ref, w_out, rows, weights, sems = refs[11:]
    step = pl.program_id(0)
    tokens = put_tokens(x_refs, rows, sems, 0)
    columns = put_columns(place, w_refs, weights, sems, 10)
    back = pltpu.make_async_copy(weights, w_out, sems.at[26])

    @pl.when(step == 0)
    def _():
        for copy in columns + tokens:
            copy.start()
        for copy in columns:
            copy.wait()
        back.start()
        for copy in tokens:
            copy.wait()

    at = pl.ds(pl.multiple_of(step * TILE, TILE), TILE)
    tile = rows[at, :D]
    wide = tile.astype(F32)
    scale = lax.rsqrt(jnp.mean(wide * wide, axis=-1, keepdims=True) + eps)
    scale_ref[...] = scale
    pre = times_transposed(tile, weights[...]) * scale
    tables = rows[at, D:].astype(F32)
    tables = tables + pltpu.roll(tables, B - HD // 2, 1)
    cosine = jnp.concatenate([tables[:, : HD // 2]] * 4, axis=1)
    sine = jnp.concatenate([tables[:, HD : HD + HD // 2]] * 4, axis=1)
    cosine_ref[...] = cosine
    sine_ref[...] = sine
    for i in range(2):
        part = pre[:, i * 2 * HD : (i + 1) * 2 * HD]
        part = (part * cosine + turned(part) * sine).astype(BF16) * HD ** (-0.5)
        query_ref[0, 2 * i] = part[:, :HD]
        query_ref[0, 2 * i + 1] = part[:, HD:]
    part = pre[:, HEADS * HD :]
    lane = lax.broadcasted_iota(jnp.int32, part.shape, 1)
    kv_ref[0] = jnp.where(lane < HD, part * cosine + turned(part) * sine, part).astype(BF16)

    @pl.when(step == 3)
    def _():
        back.wait()


def project_qkv(place, x_pieces, w_pieces):
    tile = lambda lanes: pl.BlockSpec((TILE, lanes), lambda i, p: (i, 0))
    return pl.pallas_call(
        project_qkv_kernel,
        grid_spec=pltpu.PrefetchScalarGridSpec(
            num_scalar_prefetch=1,
            grid=(4,),
            in_specs=[ANYWHERE] * 10,
            out_specs=[
                pl.BlockSpec((1, HEADS, TILE, HD), lambda i, p: (i // 2, 0, i % 2, 0)),
                pl.BlockSpec((1, TILE, 2 * HD), lambda i, p: (i // 2, i % 2, 0)),
                tile(1), tile(2 * HD), tile(2 * HD),
                ANYWHERE,
            ],
            scratch_shapes=[
                pltpu.VMEM((2 * HALF, WIDE), BF16),
                pltpu.VMEM((QKV, D), BF16),
                pltpu.SemaphoreType.DMA((27,)),
            ],
        ),
        out_shape=[
            shaped(2, HEADS, HALF, HD), shaped(2, HALF, 2 * HD), shaped(2 * HALF, 1, kind=F32),
            shaped(2 * HALF, 2 * HD, kind=F32), shaped(2 * HALF, 2 * HD, kind=F32), shaped(QKV, D),
        ],
        compiler_params=params("arbitrary"),
        cost_estimate=cost(2 * 2 * HALF * QKV * D, 8),
        name="project_qkv",
    )(place, *x_pieces, *w_pieces)


def project_kernel(left_ref, weight_ref, *parts):
    put_parts(pl.program_id(0), matmul(left_ref[...], weight_ref[...]).astype(BF16), parts)


def project(left, weight):
    depth = left.shape[1]
    return pl.pallas_call(
        project_kernel,
        grid=(4,),
        in_specs=[pl.BlockSpec((TILE, depth), lambda i: (i, 0)), pl.BlockSpec((depth, D), lambda i: (0, 0))],
        out_specs=PART_SPECS,
        out_shape=PART_SHAPES,
        compiler_params=params("arbitrary"),
        cost_estimate=cost(2 * 2 * HALF * depth * D, 8),
        name="project",
    )(left, weight)


def put_term(place, left, rows, term_ref):
    def one(i, carry):
        term = matmul(left, rows[:, pl.ds(pl.multiple_of(i * 4 * B, 4 * B), 4 * B)]).astype(BF16)
        for j in range(2):
            zx = 2 * i + j
            by = (zx % 4 + 4 - place[3]) % 4
            term_ref[by, zx // 4, 0] = term[:, 2 * j * B : (2 * j + 1) * B]
            term_ref[by, zx // 4, 1] = term[:, (2 * j + 1) * B : (2 * j + 2) * B]
        return carry

    lax.fori_loop(0, 4, one, 0)


def qkv_back_kernel(grad_q_ref, own_ref, later_ref, cosine_ref, sine_ref, scale_ref, weight_ref, *outs):
    parts, turned_ref = outs[:5], outs[5]
    cosine, sine = cosine_ref[...], sine_ref[...]
    lane = lax.broadcasted_iota(jnp.int32, cosine.shape, 1)
    pieces = []
    for i in range(2):
        part = grad_q_ref[0, :, i * 2 * HD : (i + 1) * 2 * HD]
        pieces.append(part * cosine - turned(part * sine))
    part = own_ref[0] + later_ref[0].astype(F32)
    pieces.append(jnp.where(lane < HD, part * cosine - turned(part * sine), part))
    grad_pre = jnp.concatenate(pieces, axis=1)
    put_parts(pl.program_id(0), matmul(grad_pre.astype(BF16), weight_ref[...]).astype(BF16), parts)
    turned_ref[...] = (grad_pre * scale_ref[...]).T.astype(BF16)


def qkv_back(grad_query, own, later, cosine, sine, scale, weight):
    tile = lambda lanes: pl.BlockSpec((TILE, lanes), lambda i: (i, 0))
    half = lambda lanes: pl.BlockSpec((1, TILE, lanes), lambda i: (i // 2, i % 2, 0))
    return pl.pallas_call(
        qkv_back_kernel,
        grid=(4,),
        in_specs=[
            half(HEADS * HD), half(2 * HD), half(2 * HD), tile(2 * HD), tile(2 * HD), tile(1),
            pl.BlockSpec((QKV, D), lambda i: (0, 0)),
        ],
        out_specs=PART_SPECS + [pl.BlockSpec((QKV, TILE), lambda i: (0, i))],
        out_shape=PART_SHAPES + [shaped(QKV, 2 * HALF)],
        compiler_params=params("arbitrary"),
        cost_estimate=cost(2 * 2 * HALF * QKV * D, 9),
        name="qkv_back",
    )(grad_query, own, later, cosine, sine, scale, weight)


def attention_term_kernel(*refs):
    place, token_refs, left_ref = refs[0], refs[1:6], refs[6]
    term_ref, rows, sems = refs[-3:]
    copies = put_tokens(token_refs, rows, sems, 0)
    for copy in copies:
        copy.start()
    left = left_ref[...]
    if left.shape[0] == 2 * HALF:
        left = left.T
    for copy in copies:
        copy.wait()
    put_term(place, left, rows, term_ref)


def attention_terms(place, pieces, left, name):
    whole = lambda *shape: pl.BlockSpec(shape, lambda i, p: (0,) * len(shape))
    rows = min(left.shape)
    return pl.pallas_call(
        attention_term_kernel,
        grid_spec=pltpu.PrefetchScalarGridSpec(
            num_scalar_prefetch=1,
            grid=(1,),
            in_specs=[ANYWHERE] * 5 + [whole(*left.shape)],
            out_specs=whole(4, 2, 2, rows, B),
            scratch_shapes=[pltpu.VMEM((2 * HALF, D), BF16), pltpu.SemaphoreType.DMA((10,))],
        ),
        out_shape=shaped(4, 2, 2, rows, B),
        compiler_params=params("arbitrary"),
        cost_estimate=cost(2 * 2 * HALF * rows * D, 7),
        name=name,
    )(place, *pieces, left)


def token_places(at, y, core):
    step = 1 - 2 * core
    block = jnp.where(
        at < B, y, jnp.where(at < 2 * B, y + 4 - step, jnp.where(at < 3 * B, y + 4 + step, y + 2))
    )
    row = at % B
    row = jnp.where(at < 3 * B, row, (row + core * (B // 2)) % B)
    return (block % 4) * B + row


def set_bias(place_ref, bias_ref):
    zlo, y, core = place_ref[0], place_ref[1], place_ref[2]
    key_at = token_places(lax.broadcasted_iota(jnp.int32, (HALF, 1), 0), y, core)
    query_at = token_places(lax.broadcasted_iota(jnp.int32, (1, HALF), 1), y, core)
    bias_ref[:HALF, :] = jnp.broadcast_to(jnp.where(zlo == 1, 0.0, -1e30), (HALF, HALF))
    bias_ref[HALF:, :] = jnp.where(key_at <= query_at, 0.0, -1e30)


def attention_kernel(place_ref, query_ref, kv_ref, weight_ref, mixed_ref, log_ref, *rest):
    parts, bias_ref = rest[:5], rest[5]

    @pl.when(pl.program_id(0) == 0)
    def _():
        set_bias(place_ref, bias_ref)

    key, value = kv_ref[0, :, :HD], kv_ref[0, :, HD:]
    for head in range(HEADS):
        scores = times_transposed(key, query_ref[0, head]) + bias_ref[...]
        top = jnp.max(scores, axis=0, keepdims=True)
        weights = jnp.exp(scores - top)
        total = jnp.sum(weights, axis=0, keepdims=True)
        low = (weights * (1.0 / total)).astype(BF16)
        mixed_ref[0, :, head * HD : (head + 1) * HD] = outer_sum(value, low).T.astype(BF16)
        log_ref[0, head] = top + jnp.log(total)
    put_rows(parts, matmul(mixed_ref[0], weight_ref[...]).astype(BF16))


def put_rows(parts, rows):
    row = 0
    for ref, length in zip(parts, LENGTHS):
        ref[0] = rows[row : row + length]
        row += length


def attention_back_kernel(place_ref, *refs):
    grad_refs, query_ref, kv_ref, log_ref, weight_ref = refs[:5], *refs[5:9]
    grad_query_ref, earlier_ref, own_ref, bias_ref, rows, sems = refs[9:]
    step = pl.program_id(0)
    copies = put_tokens(grad_refs, rows, sems, 0)

    @pl.when(step == 0)
    def _():
        for copy in copies:
            copy.start()
        set_bias(place_ref, bias_ref)
        for copy in copies:
            copy.wait()

    hidden = rows[pl.ds(pl.multiple_of(step * HALF, HALF), HALF), :]
    grads = times_transposed(hidden, weight_ref[...]).astype(BF16)
    key, value = kv_ref[0, :, :HD], kv_ref[0, :, HD:]
    grad_key = jnp.zeros((2 * HALF, HD), F32)
    grad_value = jnp.zeros((2 * HALF, HD), F32)
    for head in range(HEADS):
        lanes = slice(head * HD, (head + 1) * HD)
        query, grad = query_ref[0, head], grads[:, lanes]
        weights = jnp.exp(times_transposed(key, query) + bias_ref[...] - log_ref[0, head])
        grad_weights = times_transposed(value, grad)
        delta = jnp.sum(weights * grad_weights, axis=0, keepdims=True)
        grad_scores = (weights * (grad_weights - delta)).astype(BF16)
        grad_query_ref[0, :, lanes] = outer_sum(key, grad_scores).T * HD ** (-0.5)
        grad_key += matmul(grad_scores, query)
        grad_value += matmul(weights.astype(BF16), grad)
    total = jnp.concatenate([grad_key, grad_value], axis=1)
    earlier_ref[0] = total[:HALF].astype(BF16)
    own_ref[0] = total[HALF:]


def sequence_block(*tail):
    return pl.BlockSpec((1,) + tail, lambda s, place: (s,) + (0,) * len(tail))


def attention_call(kernel, in_specs, out_specs, out_shape, scratch, flops, name):
    return pl.pallas_call(
        kernel,
        grid_spec=pltpu.PrefetchScalarGridSpec(
            num_scalar_prefetch=1,
            grid=(2,),
            in_specs=in_specs,
            out_specs=out_specs,
            scratch_shapes=[pltpu.VMEM((2 * HALF, HALF), F32)] + scratch,
        ),
        out_shape=out_shape,
        compiler_params=params("arbitrary"),
        cost_estimate=cost(flops * 8 * 2 * HALF * HALF * HD * 2, 8),
        name=name,
    )


WHOLE_ROWS = pl.BlockSpec((HEADS * HD, D), lambda s, place: (0, 0))


def attention(place, query, kv, weight):
    return attention_call(
        attention_kernel,
        [sequence_block(HEADS, HALF, HD), sequence_block(2 * HALF, 2 * HD), WHOLE_ROWS],
        [sequence_block(HALF, HEADS * HD), sequence_block(HEADS, 1, HALF)] + [sequence_block(n, D) for n in LENGTHS],
        [shaped(2, HALF, HEADS * HD), shaped(2, HEADS, 1, HALF, kind=F32)] + PART_SHAPES,
        [],
        3,
        "attention",
    )(place, query, kv, weight)


def attention_back(place, grad_pieces, query, kv, log_total, weight):
    return attention_call(
        attention_back_kernel,
        [ANYWHERE] * 5
        + [
            sequence_block(HEADS, HALF, HD), sequence_block(2 * HALF, 2 * HD),
            sequence_block(HEADS, 1, HALF), WHOLE_ROWS,
        ],
        [sequence_block(HALF, HEADS * HD), sequence_block(HALF, 2 * HD), sequence_block(HALF, 2 * HD)],
        [
            shaped(2, HALF, HEADS * HD, kind=F32),
            shaped(2, HALF, 2 * HD),
            shaped(2, HALF, 2 * HD, kind=F32),
        ],
        [pltpu.VMEM((2 * HALF, D), BF16), pltpu.SemaphoreType.DMA((10,))],
        6,
        "attention_back",
    )(place, *grad_pieces, query, kv, log_total, weight)


def finish_attention_kernel(place, *refs):
    piece_refs, w_query, w_key, w_value, gain_ref = refs[:4], *refs[4:8]
    query_out, key_out, value_out, gain_out, rows = refs[8:]
    for ref, by in zip(piece_refs, range(4)):
        at_y = (place[1] + by) % 4
        for c in range(2):
            piece = ref[c].astype(F32)
            rows[pl.ds(pl.multiple_of((2 * at_y + c) * HEADS * HD, HEADS * HD), HEADS * HD)] = piece[: HEADS * HD]
        both = ref[0].astype(F32) + ref[1].astype(F32)
        at = pl.multiple_of(H * HD + at_y * HD, HD)
        rows[pl.ds(at, HD)] = both[HEADS * HD : (HEADS + 1) * HD]
        rows[pl.ds(at + KV * HD, HD)] = both[(HEADS + 1) * HD :]
    gain = gain_ref[...]
    total = jnp.zeros((B, 1), F32)
    row = 0
    for weight, out in ((w_query, query_out), (w_key, key_out), (w_value, value_out)):
        for i in range(out.shape[1] // B):
            lanes = slice(i * B, (i + 1) * B)
            block = rows[row : row + B].T
            total = total + jnp.sum(block * weight[:, lanes].astype(F32), axis=1, keepdims=True)
            out[:, lanes] = block * gain
            row += B
    gain_out[...] = total


def finish_attention(place, pieces, w_query, w_key, w_value, gain):
    whole = lambda *shape: pl.BlockSpec(shape, lambda i, p: (0,) * len(shape))
    kv = KV * HD
    return pl.pallas_call(
        finish_attention_kernel,
        grid_spec=pltpu.PrefetchScalarGridSpec(
            num_scalar_prefetch=1,
            grid=(1,),
            in_specs=[whole(2, QKV, B)] * 4 + [whole(B, D), whole(B, kv), whole(B, kv), whole(B, 1)],
            out_specs=[whole(B, D), whole(B, kv), whole(B, kv), whole(B, 1)],
            scratch_shapes=[pltpu.VMEM((D + 2 * kv, B), F32)],
        ),
        out_shape=[
            shaped(B, D, kind=F32), shaped(B, kv, kind=F32), shaped(B, kv, kind=F32), shaped(B, 1, kind=F32),
        ],
        compiler_params=params("arbitrary"),
        cost_estimate=cost(0, 4),
        name="finish_attention",
    )(place, *pieces, w_query, w_key, w_value, gain)


def finish_output_kernel(blocks, out):
    for i in range(16):
        out[:, i * B : (i + 1) * B] = blocks[i].astype(F32)


def finish_output(blocks):
    return pl.pallas_call(
        finish_output_kernel,
        out_shape=shaped(B, D, kind=F32),
        compiler_params=params(),
        cost_estimate=cost(0, 2),
        name="finish_output",
    )(blocks)


def feed_forward_kernel(*refs):
    place, token_refs, grad_refs, ff_ref = refs[0], refs[1:6], refs[6:11], refs[11]
    act_ref, act_t, gate_t, up_t = refs[12:16]
    parts, down_out = refs[16:21], refs[21]
    rows_h, rows_g, gate_up, down, slabs, sems = refs[22:]
    step = pl.program_id(0)
    tokens = put_tokens(token_refs, rows_h, sems, 0)
    grads = put_tokens(grad_refs, rows_g, sems, 10)
    weights, loads = [], []
    for x in range(4):
        for by in range(4):
            z = (2 * place[4] + place[0] + by) % 4
            zhi, zlo = z // 2, z % 2
            for core in range(2):
                weights.append(
                    pltpu.make_async_copy(
                        ff_ref.at[x, by, pl.ds(core * FFL, FFL)],
                        gate_up.at[zlo, :, lane_block(zhi, x, core)],
                        sems.at[20 + len(weights)],
                    )
                )
            loads.append(
                pltpu.make_async_copy(
                    ff_ref.at[x, by, pl.ds(2 * FFL, FFL)], slabs.at[zlo, zhi * 4 + x], sems.at[52 + len(loads)]
                )
            )
    back = pltpu.make_async_copy(down, down_out, sems.at[68])

    @pl.when(step == 0)
    def _():
        for copy in tokens + weights + loads + grads:
            copy.start()
        for copy in tokens + weights:
            copy.wait()

    rows = pl.ds(pl.multiple_of(step * HALF, HALF), HALF)
    normed = rows_h[rows, :]
    gate_pre = times_transposed(normed, gate_up[0])
    upward = times_transposed(normed, gate_up[1])

    @pl.when(step == 0)
    def _():
        for copy in loads:
            copy.wait()

        def put(q, carry):
            for half in range(2):
                for p in range(4):
                    one = slabs[half, 2 * q, 2 * p * PIECE : 2 * (p + 1) * PIECE, :].astype(F32)
                    two = slabs[half, 2 * q + 1, 2 * p * PIECE : 2 * (p + 1) * PIECE, :].astype(F32)
                    lane = (half * 8 + 2 * p) * B
                    rows = pl.ds(pl.multiple_of(q * 2 * PIECE, 16), 2 * PIECE)
                    down[rows, lane : lane + B] = jnp.concatenate([one[:PIECE], two[:PIECE]], axis=0).astype(BF16)
                    down[rows, lane + B : lane + 2 * B] = jnp.concatenate(
                        [one[PIECE:], two[PIECE:]], axis=0
                    ).astype(BF16)
            return carry

        lax.fori_loop(0, 4, put, 0)
        back.start()
        for copy in grads:
            copy.wait()

    grad_act = times_transposed(rows_g[rows, :], down[...])
    sigmoid = 1.0 / (1.0 + jnp.exp(-gate_pre))
    silu = gate_pre * sigmoid
    activation = silu * upward
    grad_up = grad_act * silu
    grad_gate = grad_act * upward * (sigmoid * (1.0 + gate_pre * (1.0 - sigmoid)))
    part = matmul(grad_gate.astype(BF16), gate_up[0]) + matmul(grad_up.astype(BF16), gate_up[1])
    part = part.astype(BF16)
    row = 0
    for ref, length in zip(parts, LENGTHS):
        ref[0] = part[row : row + length]
        row += length
    act_ref[...] = activation.astype(BF16)
    act_t[...] = activation.T.astype(BF16)
    gate_t[...] = grad_gate.T.astype(BF16)
    up_t[...] = grad_up.T.astype(BF16)

    @pl.when(step == 1)
    def _():
        back.wait()


def feed_forward(place, tokens, grads, ff_all):
    turned_spec = pl.BlockSpec((FFL, HALF), lambda i, p: (0, i))
    turned_shape = shaped(FFL, 2 * HALF)
    return pl.pallas_call(
        feed_forward_kernel,
        grid_spec=pltpu.PrefetchScalarGridSpec(
            num_scalar_prefetch=1,
            grid=(2,),
            in_specs=[ANYWHERE] * 11,
            out_specs=[pl.BlockSpec((HALF, FFL), lambda i, p: (i, 0))]
            + [turned_spec] * 3
            + [pl.BlockSpec((1, n, D), lambda i, p: (i, 0, 0)) for n in LENGTHS]
            + [ANYWHERE],
            scratch_shapes=[
                pltpu.VMEM((2 * HALF, D), BF16),
                pltpu.VMEM((2 * HALF, D), BF16),
                pltpu.VMEM((2, FFL, D), BF16),
                pltpu.VMEM((FFL, D), BF16),
                pltpu.VMEM((2, 8, FFL, B), BF16),
                pltpu.SemaphoreType.DMA((69,)),
            ],
        ),
        out_shape=[shaped(2 * HALF, FFL)] + [turned_shape] * 3 + PART_SHAPES + [shaped(FFL, D)],
        compiler_params=params("arbitrary"),
        cost_estimate=cost(2 * 5 * 2 * HALF * FFL * D, 32),
        name="feed_forward",
    )(place, *tokens, *grads, ff_all)


FF_TERMS = (2, 2, 4, 3 * FFL, B)


def load_tokens(step, refs, rows, sems):
    copies = put_tokens(refs, rows, sems, 0)

    @pl.when(step == 0)
    def _():
        for copy in copies:
            copy.start()
        for copy in copies:
            copy.wait()


def down_kernel(*refs):
    grad_refs, act_t, out_ref, rows, terms, sems = refs[:5], *refs[5:]
    step = pl.program_id(0)
    load_tokens(step, grad_refs, rows, sems)
    term = matmul(act_t[...], rows[:, pl.ds(pl.multiple_of(step * 4 * B, 4 * B), 4 * B)])
    for j in range(2):
        p = (2 * step + j) % 4
        at = pl.ds(pl.multiple_of(p * 2 * PIECE, 16), 2 * PIECE)
        for zx in range(8):
            slab = term[zx * PIECE : (zx + 1) * PIECE]
            low, high = slab[:, 2 * j * B : (2 * j + 1) * B], slab[:, (2 * j + 1) * B : (2 * j + 2) * B]
            terms[step // 2, zx // 4, zx % 4, at, :] = jnp.concatenate([low, high], axis=0).astype(BF16)
    half = step // 2
    out = pltpu.make_async_copy(
        terms.at[half], out_ref.at[half, :, :, pl.ds(2 * FFL, FFL)], sems.at[10 + half]
    )

    @pl.when(step % 2 == 1)
    def _():
        out.start()

    @pl.when(step == 3)
    def _():
        for i in range(2):
            pltpu.make_async_copy(
                terms.at[i], out_ref.at[i, :, :, pl.ds(2 * FFL, FFL)], sems.at[10 + i]
            ).wait()


def gate_up_kernel(*refs):
    token_refs, gate_t, up_t, out_ref, rows, terms, sems = refs[:5], *refs[5:7], *refs[8:]
    step = pl.program_id(0)
    load_tokens(step, token_refs, rows, sems)
    normed = rows[:, pl.ds(pl.multiple_of(step * 4 * B, 4 * B), 4 * B)]
    zhi, x = step // 2, step % 2
    for matrix, left in ((0, gate_t), (1, up_t)):
        term = matmul(left[...], normed).astype(BF16)
        for j in range(2):
            terms[matrix, zhi, 2 * x + j, 0:FFL, :] = term[:, 2 * j * B : (2 * j + 1) * B]
            terms[matrix, zhi, 2 * x + j, FFL:, :] = term[:, (2 * j + 1) * B : (2 * j + 2) * B]

    def out(i):
        at = pl.ds(i % 2 * 2, 2)
        return pltpu.make_async_copy(
            terms.at[:, i // 2, at], out_ref.at[:, i // 2, at, pl.ds(0, 2 * FFL)], sems.at[10 + i]
        )

    out(step).start()

    @pl.when(step == 3)
    def _():
        for i in range(4):
            out(i).wait()


def ff_terms(kernel, pieces, lefts, rows, name, *more):
    whole = pl.BlockSpec((FFL, 2 * HALF), lambda i: (0, 0))
    return pl.pallas_call(
        kernel,
        grid=(4,),
        in_specs=[ANYWHERE] * 5 + [whole] * len(lefts) + [ANYWHERE] * len(more),
        out_specs=ANYWHERE,
        out_shape=shaped(*FF_TERMS),
        scratch_shapes=[
            pltpu.VMEM((2 * HALF, D), BF16),
            pltpu.VMEM((2, 2, 4, rows, B), BF16),
            pltpu.SemaphoreType.DMA((14,)),
        ],
        input_output_aliases={7: 0} if more else {},
        compiler_params=params("arbitrary"),
        cost_estimate=cost(2 * len(lefts) * 2 * HALF * FFL * D, 8 + 4 * len(lefts)),
        name=name,
    )(*pieces, *lefts, *more)


def finish_hidden_kernel(sums_ref, weight_ref, gain_ref, out_ref, gain_out, rows):
    for y in range(4):
        for core in range(2):
            slab = sums_ref[y, 0, core].astype(F32)
            for zx in range(8):
                at = (2 * zx + core) * 4 * PIECE + y * PIECE
                rows[at : at + PIECE] = slab[zx * PIECE : (zx + 1) * PIECE]
    gain = gain_ref[...]
    total = jnp.zeros((B, 1), F32)
    for i in range(FF // B):
        lanes = slice(i * B, (i + 1) * B)
        block = rows[lanes].T
        total = total + jnp.sum(block * weight_ref[:, lanes].astype(F32), axis=1, keepdims=True)
        out_ref[:, lanes] = block * gain
    gain_out[...] = total


def finish_hidden(sums, matrix, weight, gain):
    return pl.pallas_call(
        finish_hidden_kernel,
        grid=(1,),
        in_specs=[
            pl.BlockSpec((4, 1, 2, FFL, B), lambda i: (0, matrix, 0, 0, 0)),
            pl.BlockSpec((B, FF), lambda i: (0, 0)),
            pl.BlockSpec((B, 1), lambda i: (0, 0)),
        ],
        out_specs=[pl.BlockSpec((B, FF), lambda i: (0, 0)), pl.BlockSpec((B, 1), lambda i: (0, 0))],
        out_shape=[shaped(B, FF, kind=F32), shaped(B, 1, kind=F32)],
        scratch_shapes=[pltpu.VMEM((FF, B), F32)],
        compiler_params=params("arbitrary"),
        cost_estimate=cost(0, 6),
        name="finish_hidden",
    )(sums, weight, gain)


def finish_down_kernel(sums_ref, out_ref):
    for y in range(4):
        for half in range(2):
            slab = sums_ref[y, half, 0].astype(F32)
            for t in range(8):
                lane = (half * 8 + t) * B
                out_ref[y * PIECE : (y + 1) * PIECE, lane : lane + B] = slab[t * PIECE : (t + 1) * PIECE]


def finish_down(sums):
    return pl.pallas_call(
        finish_down_kernel,
        grid=(1,),
        in_specs=[pl.BlockSpec((4, 2, 1, FFL, B), lambda i: (0, 0, 2, 0, 0))],
        out_specs=pl.BlockSpec((4 * PIECE, D), lambda i: (0, 0)),
        out_shape=shaped(4 * PIECE, D, kind=F32),
        compiler_params=params("arbitrary"),
        cost_estimate=cost(0, 5),
        name="finish_down",
    )(sums)


def own_rows(rows_all, y, core, per):
    return lax.dynamic_slice_in_dim(rows_all, (2 * y + core) * per, per, 0)


class Flow:
    def __init__(self, steps):
        self.steps, self.result, self.sent = steps, None, None
        self.move(None)

    def move(self, arrived):
        try:
            self.sent = self.steps.send(arrived)
        except StopIteration as end:
            self.sent, self.result = (), end.value


def stage(flows, *values):
    flows = [flow for flow in flows if flow.result is None]
    sizes = [len(flow.sent) for flow in flows]
    leaves, tree = jax.tree.flatten(values)
    tied = tie(*[v for flow in flows for v in flow.sent], *leaves)
    for flow, size in zip(flows, sizes):
        flow.move(tied[:size])
        tied = tied[size:]
    return jax.tree.unflatten(tree, tied)


def gather_steps(block):
    (other,) = yield (swap_core(block),)
    pair = jnp.stack([block, other])
    (got,) = yield (along_y(pair),)
    far, swapped = yield (along_y(send_half(got)), swap_core(got))
    (far_swapped,) = yield (swap_core(far),)
    return pair, got, swapped, far, far_swapped


def scatter_steps(parts):
    core = lax.axis_index("core")
    first, behind, ahead, far, far_other = parts
    (far_got,) = yield (swap_core(far_other),)
    far = add(far, far_got[::-1]).astype(BF16)
    low, behind_got, first_got = yield (along_y(far), swap_core(behind), swap_core(first[1]))
    ahead = add(ahead, behind_got[::-1])
    mine = lax.dynamic_slice_in_dim(ahead, core * (B // 2), B // 2, 1) + low.astype(F32)
    ahead = lax.dynamic_update_slice_in_dim(ahead, mine, core * (B // 2), 1).astype(BF16)
    (got,) = yield (along_y(ahead),)
    (last,) = yield (swap_core(got[1]),)
    return add(first[0], first_got) + got[0].astype(F32) + last.astype(F32)


def ring_gather_steps(block, axis):
    half = block.shape[0] // 2
    before, after = yield (shift(block, axis, 1), shift(block, axis, -1))
    low, high = yield (shift(before[:half], axis, 1), shift(after[half:], axis, -1))
    return block, after, low, high, before


def ring_scatter_steps(parts, axis):
    half = parts[2].shape[0] // 2
    low, high = yield (shift(parts[2][:half], axis, 1), shift(parts[2][half:], axis, -1))
    after = jnp.concatenate([add(parts[1][:half], low).astype(BF16), parts[1][half:]], axis=0)
    before = jnp.concatenate([parts[3][:half], add(parts[3][half:], high).astype(BF16)], axis=0)
    from_before, from_after = yield (shift(after, axis, 1), shift(before, axis, -1))
    return add(parts[0], from_before) + from_after.astype(F32)


def on_device(
    layer_input,
    positions,
    attn_gain,
    w_query,
    w_key,
    w_value,
    w_output,
    mlp_gain,
    w_gate,
    w_up,
    w_down,
    out_grad,
):
    zlo, y, zhi, x, core = (lax.axis_index(axis) for axis in AXES)
    place = jnp.stack([zlo, y, core, x, zhi]).astype(jnp.int32)

    def by_core(mine, got):
        return jnp.where(core == 0, jnp.stack([mine, got]), jnp.stack([got, mine]))

    def by_zlo(mine, got):
        return jnp.where(zlo == 0, jnp.stack([mine, got]), jnp.stack([got, mine]))

    def by_zhi(mine, got):
        return jnp.where(zhi == 0, jnp.stack([mine, got]), jnp.stack([got, mine]))

    def trio(mine, other, axis):
        across = lax.ppermute(other, (axis, "core"), [(i, 3 - i) for i in range(4)])
        return shift(mine, axis, 1), swap_core(other), across

    def column_steps(mine, got):
        pair = by_core(mine, got)
        (got,) = yield (shift(pair, "zhi", 1),)
        return (yield from ring_gather_steps(by_zhi(pair, got), "x"))

    def output_steps(rows):
        mine = lax.dynamic_index_in_dim(rows, (2 * y + core) % 4, 0, keepdims=False)
        other = lax.dynamic_index_in_dim(rows, (2 * y + 1 - core) % 4, 0, keepdims=False)
        (got,) = yield (swap_core(other),)
        pair = by_core(mine, got)
        pairs = [(2 * i + i // 2, 2 * i + 1 - i // 2) for i in range(4)]
        (got,) = yield (lax.ppermute(pair, ("y", "zhi"), pairs),)
        return jnp.where(zhi == y // 2, pair, got).reshape(HEADS * HD, D)

    def hidden_steps(mine, got, down):
        piece = jnp.concatenate([by_core(mine, got).reshape(2 * FFL, B), down], axis=0)
        pieces = yield from ring_gather_steps(piece, "z")
        return jnp.concatenate(pieces, axis=0).reshape(4, 3 * FFL, B)

    def of_core(pair, other=False):
        return lax.dynamic_index_in_dim(pair, 1 - core if other else core, 0, keepdims=False)

    def whole_ring(pieces):
        own, after, low, high, before = pieces
        return own, after, jnp.concatenate([low, high], axis=0), before

    def attention_steps(terms):
        column = yield from ring_scatter_steps([terms[i] for i in range(4)], "x")
        keep = lax.dynamic_index_in_dim(column, zhi, 0, keepdims=False)
        send = lax.dynamic_index_in_dim(column, 1 - zhi, 0, keepdims=False).astype(BF16)
        (got,) = yield (shift(send, "zhi", 1),)
        pair = (keep + got.astype(F32)).astype(BF16)
        mine, other = of_core(pair), of_core(pair, True)
        there, here, across = yield trio(mine, other, "zlo")
        own = by_core(add(mine, there), add(here, across)).astype(BF16)
        return whole_ring((yield from ring_gather_steps(own, "y")))

    def ff_steps(own):
        pair, down = own[: 2 * FFL].reshape(2, FFL, B), own[2 * FFL :]
        mine, other = of_core(pair), of_core(pair, True)
        there, here, across = yield trio(jnp.concatenate([mine, down], axis=0), other, "zlo")
        both = by_zlo(by_core(mine, here), by_core(there[:FFL], across))
        return jnp.concatenate([both, by_zlo(down, there[FFL:])[:, None]], axis=1)

    x_low = layer_input[0]
    frequency = theta ** (-jnp.arange(0, HD, 2).astype(F32) / HD)
    angles = positions[0].astype(F32)[:, None] * frequency
    tables = []
    for table in (jnp.cos(angles), jnp.sin(angles)):
        high = lax.reduce_precision(table, 8, 7)
        tables += [high.astype(BF16), (table - high).astype(BF16)]
    tokens = Flow(gather_steps(jnp.concatenate([x_low, *tables], axis=1)))
    grads = Flow(gather_steps(out_grad[0]))
    o_rows = lax.all_gather(w_output, "x", axis=0, tiled=False)
    qkv_mine, qkv_other = prepare_qkv(place, w_query, w_key, w_value, attn_gain[:, None])
    qkv_mine, qkv_got, gain_two = stage([tokens], qkv_mine, swap_core(qkv_other), mlp_gain[:, None])

    columns = Flow(column_steps(qkv_mine, qkv_got))
    ff_mine, ff_other, ff_down = prepare_ff(place, w_gate, w_up, w_down, gain_two)
    ff_mine, ff_got, ff_down, x_low = stage([tokens, columns], ff_mine, swap_core(ff_other), ff_down, x_low)

    hidden_rows = Flow(hidden_steps(ff_mine, ff_got, ff_down))
    inputs = x_low.astype(F32)
    scale_one = lax.rsqrt(jnp.mean(inputs * inputs, axis=-1, keepdims=True) + eps)
    (scale_one,) = stage([tokens, columns, grads, hidden_rows], scale_one)

    (o_rows,) = stage([tokens, columns, hidden_rows], o_rows)

    ff_all = lax.all_gather(hidden_rows.result, "x", axis=0, tiled=False)
    outputs = Flow(output_steps(o_rows))
    x_pieces = tokens.result
    query, key_value, scale_all, cosine, sine, qkv_full = project_qkv(place, x_pieces, columns.result)
    query, key_value = stage([outputs, grads], query, key_value)

    earlier = lax.ppermute(key_value, "zlo", [(0, 1)])
    query, key_value, earlier = stage([outputs], query, key_value, earlier)

    key_value = jnp.concatenate([earlier, key_value], axis=1)
    o_full = outputs.result
    mixed, log_total, *parts = attention(place, query, key_value, o_full)
    parts = stage([grads], *parts)
    sums = Flow(scatter_steps(parts))
    stage([sums, grads])
    grad_pieces = grads.result
    for _ in range(3):
        stage([sums])
    hidden = inputs + sums.result
    scale_two = lax.rsqrt(jnp.mean(hidden * hidden, axis=-1, keepdims=True) + eps)
    normed = Flow(gather_steps((hidden * scale_two).astype(BF16)))
    for _ in range(4):
        stage([normed])
    normed_pieces = normed.result

    activation, act_t, gate_t, up_t, *parts, down_full = feed_forward(place, normed_pieces, grad_pieces, ff_all)
    sums = Flow(scatter_steps(parts))
    (act_t,) = stage([sums], act_t)
    terms = ff_terms(down_kernel, grad_pieces, (act_t,), FFL, "down_terms")
    terms, gate_t = stage([sums], terms, gate_t)
    terms = ff_terms(gate_up_kernel, normed_pieces, (gate_t, up_t), 2 * FFL, "gate_up_terms", terms)
    (terms,) = stage([sums], terms)
    ff_sum = lax.psum_scatter(
        terms.reshape(16, 3 * FFL, B), ("zlo", "zhi", "x"), scatter_dimension=0, tiled=True
    ).reshape(3 * FFL, B)
    stage([sums])

    grad_normed_two = sums.result
    mean_two = jnp.mean(grad_normed_two * hidden, axis=-1, keepdims=True)
    grad_hidden = (
        out_grad[0].astype(F32)
        + scale_two * grad_normed_two
        - hidden * (scale_two * scale_two * scale_two) * mean_two
    )
    hidden_grads = Flow(gather_steps(grad_hidden.astype(BF16)))
    (activation,) = stage([hidden_grads], activation)
    down_parts = project(activation, down_full)
    down_parts = stage([hidden_grads], *down_parts)
    result = Flow(scatter_steps(down_parts))
    stage([hidden_grads, result])
    stage([hidden_grads])

    hidden_grad_pieces = hidden_grads.result
    grad_query, grad_earlier, grad_own = attention_back(
        place, hidden_grad_pieces, query, key_value, log_total, o_full
    )
    grad_query, grad_earlier, grad_own, mixed = stage([result], grad_query, grad_earlier, grad_own, mixed)
    later = lax.ppermute(grad_earlier, "zlo", [(1, 0)])
    output_terms = attention_terms(place, hidden_grad_pieces, mixed.reshape(2 * HALF, HEADS * HD), "output_terms")
    later, grad_query, output_terms = stage([result], later, grad_query, output_terms)
    output_sums = Flow(attention_steps(output_terms))
    *parts, grad_t = qkv_back(grad_query, grad_own, later, cosine, sine, scale_all, qkv_full)
    *parts, grad_t = stage([output_sums, result], *parts, grad_t)

    sums = Flow(scatter_steps(parts))
    terms = attention_terms(place, x_pieces, grad_t, "qkv_terms")
    terms, ff_sum = stage([sums, output_sums], terms, ff_sum)
    ff_sums = Flow(ff_steps(ff_sum))
    attention_sums = Flow(attention_steps(terms))
    stage([sums, attention_sums, ff_sums, output_sums])
    ff_sums = lax.all_gather(ff_sums.result, "y", axis=0, tiled=False)
    stage([sums, attention_sums, output_sums])
    stage([sums, attention_sums, output_sums])
    grad_normed = sums.result
    mean_one = jnp.mean(grad_normed * inputs, axis=-1, keepdims=True)
    input_grad = (
        grad_hidden
        + scale_one * grad_normed
        - inputs * (scale_one * scale_one * scale_one) * mean_one
    )
    input_grad = input_grad.astype(BF16)
    stage([attention_sums, output_sums])

    ring = jnp.roll(jnp.stack(output_sums.result), y, axis=0).reshape(16, B, B)
    output_grad = lax.all_to_all(ring, FSDP, 0, 0, tiled=True)
    stage([attention_sums])
    stage([attention_sums])

    gain_two = mlp_gain[:, None]
    query_grad, key_grad, value_grad, attn_gain_grad = finish_attention(
        place, attention_sums.result, w_query, w_key, w_value, attn_gain[:, None]
    )
    gate_grad, gate_gain = finish_hidden(ff_sums, 0, w_gate, gain_two)
    up_grad, up_gain = finish_hidden(ff_sums, 1, w_up, gain_two)
    down_grad = finish_down(ff_sums)
    output_grad = finish_output(output_grad)
    return (
        (hidden + result.result).astype(BF16)[None],
        input_grad[None],
        attn_gain_grad[:, 0],
        query_grad,
        key_grad,
        value_grad,
        output_grad,
        (gate_gain + up_gain)[:, 0],
        gate_grad,
        up_grad,
        down_grad,
    )


def solution(mesh):
    split = Mesh(mesh.devices.reshape(2, 4, 2, 4, 2), AXES)
    tokens = P(FSDP, SEQ, None)
    rows = P(FSDP, None)
    gain = P(FSDP)
    in_specs = (
        tokens, P(FSDP, SEQ), gain, rows, rows, rows, rows, gain, rows, rows, rows, tokens,
    )
    out_specs = (tokens, tokens, gain, rows, rows, rows, rows, gain, rows, rows, rows)
    return jax.shard_map(
        on_device, mesh=split, in_specs=in_specs, out_specs=out_specs, check_vma=False
    )
```

```python
import jax
import jax.numpy as jnp
from jax import lax
from jax.experimental import pallas as pl
from jax.experimental.pallas import tpu as pltpu
from jax.sharding import Mesh
from jax.sharding import PartitionSpec as P

H = 32
KV = 4
HD = 64
D = 2048
FF = 5632
B = 128
HALF = 512
HEADS = 4
FFL = 704
PIECE = 88

eps = 1e-05
theta = 10000.0
F32 = jnp.float32
BF16 = jnp.bfloat16
AXES = ("zlo", "y", "zhi", "x", "core")
FSDP = ("zhi", "x", "core")
SEQ = ("zlo", "y")


def matmul(left, right):
    return jnp.dot(left, right, preferred_element_type=F32)


def times_transposed(left, right):
    return lax.dot_general(left, right, (((1,), (1,)), ((), ())), preferred_element_type=F32)


def outer_sum(left, right):
    return lax.dot_general(left, right, (((0,), (0,)), ((), ())), preferred_element_type=F32)


def shift(value, axis, by):
    if axis == "z":
        at = [2 * (z % 2) + z // 2 for z in range(4)]
        return lax.ppermute(value, ("zlo", "zhi"), [(at[z], at[(z + by) % 4]) for z in range(4)])
    size = lax.axis_size(axis)
    return lax.ppermute(value, axis, [(i, (i + by) % size) for i in range(size)])


def swap_core(value):
    return shift(value, "core", 1)


def small_gather(block, axis):
    return shift(block, axis, -1), shift(block, axis, 2), shift(block, axis, 1)


def tie(*values):
    return lax.optimization_barrier(values)


def add(left, right):
    return left.astype(F32) + right.astype(F32)


def along_y(value):
    pairs = []
    for i in range(4):
        pairs.append((2 * i, 2 * ((i + 1) % 4)))
        pairs.append((2 * i + 1, 2 * ((i + 3) % 4) + 1))
    return lax.ppermute(value, ("y", "core"), pairs)


def send_half(got):
    core = lax.axis_index("core")
    return lax.dynamic_slice_in_dim(got, core * (B // 2), B // 2, 1)


FLIPPED = (0, 0, 1, 0, 1)
LENGTHS = (B, B, B, B // 2, B // 2)


def put_tokens(refs, rows_ref, sems, start):
    lanes = pl.ds(0, rows_ref.shape[1])
    copies = []
    row = 0
    for s in range(2):
        for ref, flip, length in zip(refs, FLIPPED, LENGTHS):
            copies.append(
                pltpu.make_async_copy(
                    ref.at[s ^ flip, :, lanes], rows_ref.at[pl.ds(row, length)], sems.at[start + len(copies)]
                )
            )
            row += length
    return copies


TILE = 256
WIDE = D + B
VMEM_LIMIT = 56 * 2**20
ANYWHERE = pl.BlockSpec(memory_space=pl.ANY)


def params(*kinds):
    return pltpu.CompilerParams(dimension_semantics=kinds or None, vmem_limit_bytes=VMEM_LIMIT)


def cost(flops, megabytes):
    return pl.CostEstimate(flops=flops, bytes_accessed=int(megabytes * 2**20), transcendentals=0)


def shaped(*shape, kind=BF16):
    return jax.ShapeDtypeStruct(shape, kind)


PART_SPECS = [pl.BlockSpec((1, n, D), lambda i, *_: (i // 2, 0, 0)) for n in LENGTHS]
PART_SHAPES = [jax.ShapeDtypeStruct((2, n, D), BF16) for n in LENGTHS]


def put_parts(step, tile, refs):
    @pl.when(step % 2 == 0)
    def _():
        refs[0][0] = tile[:B]
        refs[1][0] = tile[B:]

    @pl.when(step % 2 == 1)
    def _():
        refs[2][0] = tile[:B]
        refs[3][0] = tile[B : B + B // 2]
        refs[4][0] = tile[B + B // 2 :]


def turned(values):
    lane = lax.broadcasted_iota(jnp.int32, values.shape, 1) % HD
    return jnp.where(lane < HD // 2, -pltpu.roll(values, 2 * HD - HD // 2, 1), pltpu.roll(values, HD // 2, 1))


def lane_block(zhi, x, core):
    return pl.ds(pl.multiple_of((zhi * 8 + x * 2 + core) * B, B), B)


def put_columns(place, refs, into, sems, start):
    copies = []
    for ref, by, first in zip(refs, (0, 1, 2, 2, 3), (0, 0, 0, 1, 0)):
        for i in range(ref.shape[0]):
            for core in range(2):
                lanes = lane_block(first + i, (place[3] + by) % 4, core)
                copies.append(
                    pltpu.make_async_copy(ref.at[i, core], into.at[:, lanes], sems.at[start + len(copies)])
                )
    return copies


def prepare_qkv_kernel(place, q_mine, q_other, w_key, w_value, gain, mine_ref, other_ref, k_rows, v_rows):
    scale = gain[...]
    k_rows[...] = (w_key[...].astype(F32) * scale).T
    v_rows[...] = (w_value[...].astype(F32) * scale).T
    rows = pl.ds(pl.multiple_of(place[1] * HD, HD), HD)
    for source, out in ((q_mine, mine_ref), (q_other, other_ref)):
        out[: HEADS * HD] = (source[...].astype(F32) * scale).T.astype(BF16)
        out[HEADS * HD : (HEADS + 1) * HD] = k_rows[rows].astype(BF16)
        out[(HEADS + 1) * HD :] = v_rows[rows].astype(BF16)


QKV = (HEADS + 2) * HD


def prepare_qkv(place, w_query, w_key, w_value, gain):
    whole = lambda *shape: pl.BlockSpec(shape, lambda i, p: (0,) * len(shape))
    return pl.pallas_call(
        prepare_qkv_kernel,
        grid_spec=pltpu.PrefetchScalarGridSpec(
            num_scalar_prefetch=1,
            grid=(1,),
            in_specs=[
                pl.BlockSpec((B, HEADS * HD), lambda i, p: (0, 2 * p[1] + p[2])),
                pl.BlockSpec((B, HEADS * HD), lambda i, p: (0, 2 * p[1] + 1 - p[2])),
                whole(B, KV * HD), whole(B, KV * HD), whole(B, 1),
            ],
            out_specs=[whole(QKV, B), whole(QKV, B)],
            scratch_shapes=[pltpu.VMEM((KV * HD, B), F32), pltpu.VMEM((KV * HD, B), F32)],
        ),
        out_shape=[shaped(QKV, B), shaped(QKV, B)],
        compiler_params=params("arbitrary"),
        cost_estimate=cost(0, 1),
        name="prepare_qkv",
    )(place, w_query, w_query, w_key, w_value, gain)


def prepare_ff_kernel(place, w_gate, w_up, w_down, gain, mine_ref, other_ref, down_ref, picked, rows, down_rows, sems):
    zlo, y, core = place[0], place[1], place[2]
    down = pltpu.make_async_copy(
        w_down.at[:, pl.ds(pl.multiple_of(zlo * (D // 2), D // 2), D // 2)], down_rows, sems.at[1]
    )
    down.start()

    @pl.when(zlo == 0)
    def _():
        copy = pltpu.make_async_copy(w_gate, picked, sems.at[0])
        copy.start()
        copy.wait()

    @pl.when(zlo == 1)
    def _():
        copy = pltpu.make_async_copy(w_up, picked, sems.at[0])
        copy.start()
        copy.wait()

    scale = gain[...]
    for i in range(FF // B):
        rows[i * B : (i + 1) * B] = (picked[:, i * B : (i + 1) * B].astype(F32) * scale).T
    for which, out in ((core, mine_ref), (1 - core, other_ref)):
        slabs = []
        for zx in range(8):
            at = pl.multiple_of(zx * 2 * 4 * PIECE + which * 4 * PIECE + y * PIECE, 8)
            slabs.append(rows[pl.ds(at, PIECE)])
        out[...] = jnp.concatenate(slabs, axis=0).astype(BF16)
    down.wait()
    for t in range(8):
        rows[t * 4 * PIECE : (t + 1) * 4 * PIECE] = down_rows[:, t * B : (t + 1) * B].astype(F32)
    slabs = [rows[pl.ds(pl.multiple_of(t * 4 * PIECE + y * PIECE, 8), PIECE)] for t in range(8)]
    down_ref[...] = jnp.concatenate(slabs, axis=0).astype(BF16)


def prepare_ff(place, w_gate, w_up, w_down, gain):
    return pl.pallas_call(
        prepare_ff_kernel,
        grid_spec=pltpu.PrefetchScalarGridSpec(
            num_scalar_prefetch=1,
            grid=(1,),
            in_specs=[ANYWHERE, ANYWHERE, ANYWHERE, pl.BlockSpec((B, 1), lambda i, p: (0, 0))],
            out_specs=[pl.BlockSpec((FFL, B), lambda i, p: (0, 0))] * 3,
            scratch_shapes=[
                pltpu.VMEM((B, FF), BF16),
                pltpu.VMEM((FF, B), F32),
                pltpu.VMEM((4 * PIECE, D // 2), BF16),
                pltpu.SemaphoreType.DMA((2,)),
            ],
        ),
        out_shape=[shaped(FFL, B)] * 3,
        compiler_params=params("arbitrary"),
        cost_estimate=cost(0, 6),
        name="prepare_ff",
    )(place, w_gate, w_up, w_down, gain)


def project_qkv_kernel(*refs):
    place, x_refs, w_refs = refs[0], refs[1:6], refs[6:11]
    query_ref, kv_ref, scale_ref, cosine_ref, sine_ref, w_out, rows, weights, sems = refs[11:]
    step = pl.program_id(0)
    tokens = put_tokens(x_refs, rows, sems, 0)
    columns = put_columns(place, w_refs, weights, sems, 10)
    back = pltpu.make_async_copy(weights, w_out, sems.at[26])

    @pl.when(step == 0)
    def _():
        for copy in columns + tokens:
            copy.start()
        for copy in columns:
            copy.wait()
        back.start()
        for copy in tokens:
            copy.wait()

    at = pl.ds(pl.multiple_of(step * TILE, TILE), TILE)
    tile = rows[at, :D]
    wide = tile.astype(F32)
    scale = lax.rsqrt(jnp.mean(wide * wide, axis=-1, keepdims=True) + eps)
    scale_ref[...] = scale
    pre = times_transposed(tile, weights[...]) * scale
    tables = rows[at, D:].astype(F32)
    tables = tables + pltpu.roll(tables, B - HD // 2, 1)
    cosine = jnp.concatenate([tables[:, : HD // 2]] * 4, axis=1)
    sine = jnp.concatenate([tables[:, HD : HD + HD // 2]] * 4, axis=1)
    cosine_ref[...] = cosine
    sine_ref[...] = sine
    for i in range(2):
        part = pre[:, i * 2 * HD : (i + 1) * 2 * HD]
        part = (part * cosine + turned(part) * sine).astype(BF16) * HD ** (-0.5)
        query_ref[0, 2 * i] = part[:, :HD]
        query_ref[0, 2 * i + 1] = part[:, HD:]
    part = pre[:, HEADS * HD :]
    lane = lax.broadcasted_iota(jnp.int32, part.shape, 1)
    kv_ref[0] = jnp.where(lane < HD, part * cosine + turned(part) * sine, part).astype(BF16)

    @pl.when(step == 3)
    def _():
        back.wait()


def project_qkv(place, x_pieces, w_pieces):
    tile = lambda lanes: pl.BlockSpec((TILE, lanes), lambda i, p: (i, 0))
    return pl.pallas_call(
        project_qkv_kernel,
        grid_spec=pltpu.PrefetchScalarGridSpec(
            num_scalar_prefetch=1,
            grid=(4,),
            in_specs=[ANYWHERE] * 10,
            out_specs=[
                pl.BlockSpec((1, HEADS, TILE, HD), lambda i, p: (i // 2, 0, i % 2, 0)),
                pl.BlockSpec((1, TILE, 2 * HD), lambda i, p: (i // 2, i % 2, 0)),
                tile(1), tile(2 * HD), tile(2 * HD),
                ANYWHERE,
            ],
            scratch_shapes=[
                pltpu.VMEM((2 * HALF, WIDE), BF16),
                pltpu.VMEM((QKV, D), BF16),
                pltpu.SemaphoreType.DMA((27,)),
            ],
        ),
        out_shape=[
            shaped(2, HEADS, HALF, HD), shaped(2, HALF, 2 * HD), shaped(2 * HALF, 1, kind=F32),
            shaped(2 * HALF, 2 * HD, kind=F32), shaped(2 * HALF, 2 * HD, kind=F32), shaped(QKV, D),
        ],
        compiler_params=params("arbitrary"),
        cost_estimate=cost(2 * 2 * HALF * QKV * D, 8),
        name="project_qkv",
    )(place, *x_pieces, *w_pieces)


def project_kernel(left_ref, weight_ref, *parts):
    put_parts(pl.program_id(0), matmul(left_ref[...], weight_ref[...]).astype(BF16), parts)


def project(left, weight):
    depth = left.shape[1]
    return pl.pallas_call(
        project_kernel,
        grid=(4,),
        in_specs=[pl.BlockSpec((TILE, depth), lambda i: (i, 0)), pl.BlockSpec((depth, D), lambda i: (0, 0))],
        out_specs=PART_SPECS,
        out_shape=PART_SHAPES,
        compiler_params=params("arbitrary"),
        cost_estimate=cost(2 * 2 * HALF * depth * D, 8),
        name="project",
    )(left, weight)


def put_term(place, left, rows, term_ref):
    def one(i, carry):
        term = matmul(left, rows[:, pl.ds(pl.multiple_of(i * 4 * B, 4 * B), 4 * B)]).astype(BF16)
        for j in range(2):
            zx = 2 * i + j
            by = (zx % 4 + 4 - place[3]) % 4
            term_ref[by, zx // 4, 0] = term[:, 2 * j * B : (2 * j + 1) * B]
            term_ref[by, zx // 4, 1] = term[:, (2 * j + 1) * B : (2 * j + 2) * B]
        return carry

    lax.fori_loop(0, 4, one, 0)


def qkv_back_kernel(grad_q_ref, own_ref, later_ref, cosine_ref, sine_ref, scale_ref, weight_ref, *outs):
    parts, turned_ref = outs[:5], outs[5]
    cosine, sine = cosine_ref[...], sine_ref[...]
    lane = lax.broadcasted_iota(jnp.int32, cosine.shape, 1)
    pieces = []
    for i in range(2):
        part = grad_q_ref[0, :, i * 2 * HD : (i + 1) * 2 * HD]
        pieces.append(part * cosine - turned(part * sine))
    part = own_ref[0] + later_ref[0].astype(F32)
    pieces.append(jnp.where(lane < HD, part * cosine - turned(part * sine), part))
    grad_pre = jnp.concatenate(pieces, axis=1)
    put_parts(pl.program_id(0), matmul(grad_pre.astype(BF16), weight_ref[...]).astype(BF16), parts)
    turned_ref[...] = (grad_pre * scale_ref[...]).T.astype(BF16)


def qkv_back(grad_query, own, later, cosine, sine, scale, weight):
    tile = lambda lanes: pl.BlockSpec((TILE, lanes), lambda i: (i, 0))
    half = lambda lanes: pl.BlockSpec((1, TILE, lanes), lambda i: (i // 2, i % 2, 0))
    return pl.pallas_call(
        qkv_back_kernel,
        grid=(4,),
        in_specs=[
            half(HEADS * HD), half(2 * HD), half(2 * HD), tile(2 * HD), tile(2 * HD), tile(1),
            pl.BlockSpec((QKV, D), lambda i: (0, 0)),
        ],
        out_specs=PART_SPECS + [pl.BlockSpec((QKV, TILE), lambda i: (0, i))],
        out_shape=PART_SHAPES + [shaped(QKV, 2 * HALF)],
        compiler_params=params("arbitrary"),
        cost_estimate=cost(2 * 2 * HALF * QKV * D, 9),
        name="qkv_back",
    )(grad_query, own, later, cosine, sine, scale, weight)


def attention_term_kernel(*refs):
    place, token_refs, left_ref = refs[0], refs[1:6], refs[6]
    term_ref, rows, sems = refs[-3:]
    copies = put_tokens(token_refs, rows, sems, 0)
    for copy in copies:
        copy.start()
    left = left_ref[...]
    if left.shape[0] == 2 * HALF:
        left = left.T
    for copy in copies:
        copy.wait()
    put_term(place, left, rows, term_ref)


def attention_terms(place, pieces, left, name):
    whole = lambda *shape: pl.BlockSpec(shape, lambda i, p: (0,) * len(shape))
    rows = min(left.shape)
    return pl.pallas_call(
        attention_term_kernel,
        grid_spec=pltpu.PrefetchScalarGridSpec(
            num_scalar_prefetch=1,
            grid=(1,),
            in_specs=[ANYWHERE] * 5 + [whole(*left.shape)],
            out_specs=whole(4, 2, 2, rows, B),
            scratch_shapes=[pltpu.VMEM((2 * HALF, D), BF16), pltpu.SemaphoreType.DMA((10,))],
        ),
        out_shape=shaped(4, 2, 2, rows, B),
        compiler_params=params("arbitrary"),
        cost_estimate=cost(2 * 2 * HALF * rows * D, 7),
        name=name,
    )(place, *pieces, left)


def token_places(at, y, core):
    step = 1 - 2 * core
    block = jnp.where(
        at < B, y, jnp.where(at < 2 * B, y + 4 - step, jnp.where(at < 3 * B, y + 4 + step, y + 2))
    )
    row = at % B
    row = jnp.where(at < 3 * B, row, (row + core * (B // 2)) % B)
    return (block % 4) * B + row


def set_bias(place_ref, bias_ref):
    zlo, y, core = place_ref[0], place_ref[1], place_ref[2]
    key_at = token_places(lax.broadcasted_iota(jnp.int32, (HALF, 1), 0), y, core)
    query_at = token_places(lax.broadcasted_iota(jnp.int32, (1, HALF), 1), y, core)
    bias_ref[:HALF, :] = jnp.broadcast_to(jnp.where(zlo == 1, 0.0, -1e30), (HALF, HALF))
    bias_ref[HALF:, :] = jnp.where(key_at <= query_at, 0.0, -1e30)


def attention_kernel(place_ref, *refs):
    w_refs, query_ref, kv_ref, mixed_ref, log_ref = refs[:5], *refs[5:9]
    parts, w_out, bias_ref, weight, sems = refs[9:14], *refs[14:]
    columns = put_columns(place_ref, w_refs, weight, sems, 0)
    back = pltpu.make_async_copy(weight, w_out, sems.at[16])

    @pl.when(pl.program_id(0) == 0)
    def _():
        for copy in columns:
            copy.start()
        set_bias(place_ref, bias_ref)
        for copy in columns:
            copy.wait()
        back.start()

    key, value = kv_ref[0, :, :HD], kv_ref[0, :, HD:]
    for head in range(HEADS):
        scores = times_transposed(key, query_ref[0, head]) + bias_ref[...]
        top = jnp.max(scores, axis=0, keepdims=True)
        weights = jnp.exp(scores - top)
        total = jnp.sum(weights, axis=0, keepdims=True)
        low = (weights * (1.0 / total)).astype(BF16)
        mixed_ref[0, :, head * HD : (head + 1) * HD] = outer_sum(value, low).T.astype(BF16)
        log_ref[0, head] = top + jnp.log(total)
    put_rows(parts, matmul(mixed_ref[0], weight[...]).astype(BF16))

    @pl.when(pl.program_id(0) == 1)
    def _():
        back.wait()


def put_rows(parts, rows):
    row = 0
    for ref, length in zip(parts, LENGTHS):
        ref[0] = rows[row : row + length]
        row += length


def attention_back_kernel(place_ref, *refs):
    grad_refs, query_ref, kv_ref, log_ref, weight_ref = refs[:5], *refs[5:9]
    grad_query_ref, earlier_ref, own_ref, bias_ref, rows, sems = refs[9:]
    step = pl.program_id(0)
    copies = put_tokens(grad_refs, rows, sems, 0)

    @pl.when(step == 0)
    def _():
        for copy in copies:
            copy.start()
        set_bias(place_ref, bias_ref)
        for copy in copies:
            copy.wait()

    hidden = rows[pl.ds(pl.multiple_of(step * HALF, HALF), HALF), :]
    grads = times_transposed(hidden, weight_ref[...]).astype(BF16)
    key, value = kv_ref[0, :, :HD], kv_ref[0, :, HD:]
    grad_key = jnp.zeros((2 * HALF, HD), F32)
    grad_value = jnp.zeros((2 * HALF, HD), F32)
    for head in range(HEADS):
        lanes = slice(head * HD, (head + 1) * HD)
        query, grad = query_ref[0, head], grads[:, lanes]
        weights = jnp.exp(times_transposed(key, query) + bias_ref[...] - log_ref[0, head])
        grad_weights = times_transposed(value, grad)
        delta = jnp.sum(weights * grad_weights, axis=0, keepdims=True)
        grad_scores = (weights * (grad_weights - delta)).astype(BF16)
        grad_query_ref[0, :, lanes] = outer_sum(key, grad_scores).T * HD ** (-0.5)
        grad_key += matmul(grad_scores, query)
        grad_value += matmul(weights.astype(BF16), grad)
    total = jnp.concatenate([grad_key, grad_value], axis=1)
    earlier_ref[0] = total[:HALF].astype(BF16)
    own_ref[0] = total[HALF:]


def sequence_block(*tail):
    return pl.BlockSpec((1,) + tail, lambda s, place: (s,) + (0,) * len(tail))


def attention_call(kernel, in_specs, out_specs, out_shape, scratch, flops, name):
    return pl.pallas_call(
        kernel,
        grid_spec=pltpu.PrefetchScalarGridSpec(
            num_scalar_prefetch=1,
            grid=(2,),
            in_specs=in_specs,
            out_specs=out_specs,
            scratch_shapes=[pltpu.VMEM((2 * HALF, HALF), F32)] + scratch,
        ),
        out_shape=out_shape,
        compiler_params=params("arbitrary"),
        cost_estimate=cost(flops * 8 * 2 * HALF * HALF * HD * 2, 8),
        name=name,
    )


def attention(place, w_pieces, query, kv):
    return attention_call(
        attention_kernel,
        [ANYWHERE] * 5 + [sequence_block(HEADS, HALF, HD), sequence_block(2 * HALF, 2 * HD)],
        [sequence_block(HALF, HEADS * HD), sequence_block(HEADS, 1, HALF)]
        + [sequence_block(n, D) for n in LENGTHS]
        + [ANYWHERE],
        [shaped(2, HALF, HEADS * HD), shaped(2, HEADS, 1, HALF, kind=F32)] + PART_SHAPES + [shaped(HEADS * HD, D)],
        [pltpu.VMEM((HEADS * HD, D), BF16), pltpu.SemaphoreType.DMA((17,))],
        3,
        "attention",
    )(place, *w_pieces, query, kv)


def attention_back(place, grad_pieces, query, kv, log_total, weight):
    return attention_call(
        attention_back_kernel,
        [ANYWHERE] * 5
        + [
            sequence_block(HEADS, HALF, HD), sequence_block(2 * HALF, 2 * HD),
            sequence_block(HEADS, 1, HALF), pl.BlockSpec((HEADS * HD, D), lambda s, place: (0, 0)),
        ],
        [sequence_block(HALF, HEADS * HD), sequence_block(HALF, 2 * HD), sequence_block(HALF, 2 * HD)],
        [
            shaped(2, HALF, HEADS * HD, kind=F32),
            shaped(2, HALF, 2 * HD),
            shaped(2, HALF, 2 * HD, kind=F32),
        ],
        [pltpu.VMEM((2 * HALF, D), BF16), pltpu.SemaphoreType.DMA((10,))],
        6,
        "attention_back",
    )(place, *grad_pieces, query, kv, log_total, weight)


def finish_attention_kernel(place, *refs):
    piece_refs, w_query, w_key, w_value, gain_ref = refs[:4], *refs[4:8]
    query_out, key_out, value_out, gain_out, rows = refs[8:]
    for ref, by in zip(piece_refs, range(4)):
        at_y = (place[1] + by) % 4
        for c in range(2):
            piece = ref[c].astype(F32)
            rows[pl.ds(pl.multiple_of((2 * at_y + c) * HEADS * HD, HEADS * HD), HEADS * HD)] = piece[: HEADS * HD]
        both = ref[0].astype(F32) + ref[1].astype(F32)
        at = pl.multiple_of(H * HD + at_y * HD, HD)
        rows[pl.ds(at, HD)] = both[HEADS * HD : (HEADS + 1) * HD]
        rows[pl.ds(at + KV * HD, HD)] = both[(HEADS + 1) * HD :]
    gain = gain_ref[...]
    total = jnp.zeros((B, 1), F32)
    row = 0
    for weight, out in ((w_query, query_out), (w_key, key_out), (w_value, value_out)):
        for i in range(out.shape[1] // B):
            lanes = slice(i * B, (i + 1) * B)
            block = rows[row : row + B].T
            total = total + jnp.sum(block * weight[:, lanes].astype(F32), axis=1, keepdims=True)
            out[:, lanes] = block * gain
            row += B
    gain_out[...] = total


def finish_attention(place, pieces, w_query, w_key, w_value, gain):
    whole = lambda *shape: pl.BlockSpec(shape, lambda i, p: (0,) * len(shape))
    kv = KV * HD
    return pl.pallas_call(
        finish_attention_kernel,
        grid_spec=pltpu.PrefetchScalarGridSpec(
            num_scalar_prefetch=1,
            grid=(1,),
            in_specs=[whole(2, QKV, B)] * 4 + [whole(B, D), whole(B, kv), whole(B, kv), whole(B, 1)],
            out_specs=[whole(B, D), whole(B, kv), whole(B, kv), whole(B, 1)],
            scratch_shapes=[pltpu.VMEM((D + 2 * kv, B), F32)],
        ),
        out_shape=[
            shaped(B, D, kind=F32), shaped(B, kv, kind=F32), shaped(B, kv, kind=F32), shaped(B, 1, kind=F32),
        ],
        compiler_params=params("arbitrary"),
        cost_estimate=cost(0, 4),
        name="finish_attention",
    )(place, *pieces, w_query, w_key, w_value, gain)


def finish_output_kernel(blocks, out):
    for i in range(16):
        out[:, i * B : (i + 1) * B] = blocks[i].astype(F32)


def finish_output(blocks):
    return pl.pallas_call(
        finish_output_kernel,
        out_shape=shaped(B, D, kind=F32),
        compiler_params=params(),
        cost_estimate=cost(0, 2),
        name="finish_output",
    )(blocks)


def feed_forward_kernel(*refs):
    place, token_refs, grad_refs, ff_ref = refs[0], refs[1:6], refs[6:11], refs[11]
    act_ref, act_t, gate_t, up_t = refs[12:16]
    parts, down_out = refs[16:21], refs[21]
    rows_h, rows_g, gate_up, down, slabs, sems = refs[22:]
    step = pl.program_id(0)
    tokens = put_tokens(token_refs, rows_h, sems, 0)
    grads = put_tokens(grad_refs, rows_g, sems, 10)
    weights, loads = [], []
    for x in range(4):
        for by in range(4):
            z = (2 * place[4] + place[0] + by) % 4
            zhi, zlo = z // 2, z % 2
            for core in range(2):
                weights.append(
                    pltpu.make_async_copy(
                        ff_ref.at[x, by, pl.ds(core * FFL, FFL)],
                        gate_up.at[zlo, :, lane_block(zhi, x, core)],
                        sems.at[20 + len(weights)],
                    )
                )
            loads.append(
                pltpu.make_async_copy(
                    ff_ref.at[x, by, pl.ds(2 * FFL, FFL)], slabs.at[zlo, zhi * 4 + x], sems.at[52 + len(loads)]
                )
            )
    back = pltpu.make_async_copy(down, down_out, sems.at[68])

    @pl.when(step == 0)
    def _():
        for copy in tokens + weights + loads + grads:
            copy.start()
        for copy in tokens + weights:
            copy.wait()

    rows = pl.ds(pl.multiple_of(step * HALF, HALF), HALF)
    normed = rows_h[rows, :]
    gate_pre = times_transposed(normed, gate_up[0])
    upward = times_transposed(normed, gate_up[1])

    @pl.when(step == 0)
    def _():
        for copy in loads:
            copy.wait()

        def put(q, carry):
            for half in range(2):
                for p in range(4):
                    one = slabs[half, 2 * q, 2 * p * PIECE : 2 * (p + 1) * PIECE, :].astype(F32)
                    two = slabs[half, 2 * q + 1, 2 * p * PIECE : 2 * (p + 1) * PIECE, :].astype(F32)
                    lane = (half * 8 + 2 * p) * B
                    rows = pl.ds(pl.multiple_of(q * 2 * PIECE, 16), 2 * PIECE)
                    down[rows, lane : lane + B] = jnp.concatenate([one[:PIECE], two[:PIECE]], axis=0).astype(BF16)
                    down[rows, lane + B : lane + 2 * B] = jnp.concatenate(
                        [one[PIECE:], two[PIECE:]], axis=0
                    ).astype(BF16)
            return carry

        lax.fori_loop(0, 4, put, 0)
        back.start()
        for copy in grads:
            copy.wait()

    grad_act = times_transposed(rows_g[rows, :], down[...])
    sigmoid = 1.0 / (1.0 + jnp.exp(-gate_pre))
    silu = gate_pre * sigmoid
    activation = silu * upward
    grad_up = grad_act * silu
    grad_gate = grad_act * upward * (sigmoid * (1.0 + gate_pre * (1.0 - sigmoid)))
    part = matmul(grad_gate.astype(BF16), gate_up[0]) + matmul(grad_up.astype(BF16), gate_up[1])
    part = part.astype(BF16)
    row = 0
    for ref, length in zip(parts, LENGTHS):
        ref[0] = part[row : row + length]
        row += length
    act_ref[...] = activation.astype(BF16)
    act_t[...] = activation.T.astype(BF16)
    gate_t[...] = grad_gate.T.astype(BF16)
    up_t[...] = grad_up.T.astype(BF16)

    @pl.when(step == 1)
    def _():
        back.wait()


def feed_forward(place, tokens, grads, ff_all):
    turned_spec = pl.BlockSpec((FFL, HALF), lambda i, p: (0, i))
    turned_shape = shaped(FFL, 2 * HALF)
    return pl.pallas_call(
        feed_forward_kernel,
        grid_spec=pltpu.PrefetchScalarGridSpec(
            num_scalar_prefetch=1,
            grid=(2,),
            in_specs=[ANYWHERE] * 11,
            out_specs=[pl.BlockSpec((HALF, FFL), lambda i, p: (i, 0))]
            + [turned_spec] * 3
            + [pl.BlockSpec((1, n, D), lambda i, p: (i, 0, 0)) for n in LENGTHS]
            + [ANYWHERE],
            scratch_shapes=[
                pltpu.VMEM((2 * HALF, D), BF16),
                pltpu.VMEM((2 * HALF, D), BF16),
                pltpu.VMEM((2, FFL, D), BF16),
                pltpu.VMEM((FFL, D), BF16),
                pltpu.VMEM((2, 8, FFL, B), BF16),
                pltpu.SemaphoreType.DMA((69,)),
            ],
        ),
        out_shape=[shaped(2 * HALF, FFL)] + [turned_shape] * 3 + PART_SHAPES + [shaped(FFL, D)],
        compiler_params=params("arbitrary"),
        cost_estimate=cost(2 * 5 * 2 * HALF * FFL * D, 32),
        name="feed_forward",
    )(place, *tokens, *grads, ff_all)


def along_z(place, zhi, zlo):
    return (2 * zhi + zlo + 4 - 2 * place[4] - place[0]) % 4


def load_tokens(step, refs, rows, sems):
    copies = put_tokens(refs, rows, sems, 0)

    @pl.when(step == 0)
    def _():
        for copy in copies:
            copy.start()
        for copy in copies:
            copy.wait()


def gate_up_kernel(*refs):
    place, token_refs, gate_t, up_t, out_ref, rows, terms, sems = refs[0], refs[1:6], *refs[6:]
    step = pl.program_id(0)
    load_tokens(step, token_refs, rows, sems)
    normed = rows[:, pl.ds(pl.multiple_of(step * 4 * B, 4 * B), 4 * B)]

    def out(i, matrix):
        xs, by = pl.ds(i % 2 * 2, 2), along_z(place, i // 2, matrix)
        return pltpu.make_async_copy(terms.at[xs, by], out_ref.at[xs, by], sems.at[10 + 2 * i + matrix])

    for matrix, left in ((0, gate_t), (1, up_t)):
        term = matmul(left[...], normed).astype(BF16)
        by = along_z(place, step // 2, matrix)
        for j in range(2):
            terms[step % 2 * 2 + j, by, 0:FFL, :] = term[:, 2 * j * B : (2 * j + 1) * B]
            terms[step % 2 * 2 + j, by, FFL:, :] = term[:, (2 * j + 1) * B : (2 * j + 2) * B]
        out(step, matrix).start()

    @pl.when(step == 3)
    def _():
        for i in range(4):
            for matrix in range(2):
                out(i, matrix).wait()


def down_kernel(*refs):
    place, grad_refs, act_t, out_ref, rows, terms, sems = refs[0], refs[1:6], *refs[6:]
    step = pl.program_id(0)
    load_tokens(step, grad_refs, rows, sems)
    term = matmul(act_t[...], rows[:, pl.ds(pl.multiple_of(step * 4 * B, 4 * B), 4 * B)])
    for j in range(2):
        p = (2 * step + j) % 4
        at = pl.ds(pl.multiple_of(p * 2 * PIECE, 16), 2 * PIECE)
        for zx in range(8):
            slab = term[zx * PIECE : (zx + 1) * PIECE]
            low, high = slab[:, 2 * j * B : (2 * j + 1) * B], slab[:, (2 * j + 1) * B : (2 * j + 2) * B]
            by = along_z(place, zx // 4, step // 2)
            terms[zx % 4, by, at, :] = jnp.concatenate([low, high], axis=0).astype(BF16)

    def out(half, zhi):
        by = along_z(place, zhi, half)
        return pltpu.make_async_copy(terms.at[:, by], out_ref.at[:, by], sems.at[10 + 2 * half + zhi])

    @pl.when(step % 2 == 1)
    def _():
        for zhi in range(2):
            out(step // 2, zhi).start()

    @pl.when(step == 3)
    def _():
        for half in range(2):
            for zhi in range(2):
                out(half, zhi).wait()


def ff_terms(kernel, place, pieces, lefts, rows, name):
    whole = pl.BlockSpec((FFL, 2 * HALF), lambda i, p: (0, 0))
    return pl.pallas_call(
        kernel,
        grid_spec=pltpu.PrefetchScalarGridSpec(
            num_scalar_prefetch=1,
            grid=(4,),
            in_specs=[ANYWHERE] * 5 + [whole] * len(lefts),
            out_specs=ANYWHERE,
            scratch_shapes=[
                pltpu.VMEM((2 * HALF, D), BF16),
                pltpu.VMEM((4, 4, rows, B), BF16),
                pltpu.SemaphoreType.DMA((18,)),
            ],
        ),
        out_shape=shaped(4, 4, rows, B),
        compiler_params=params("arbitrary"),
        cost_estimate=cost(2 * len(lefts) * 2 * HALF * FFL * D, 8 + 4 * len(lefts)),
        name=name,
    )(place, *pieces, *lefts)


def stack_ring_kernel(own, after, low, high, before, out, sems):
    half = low.shape[0]
    parts = ((own, out.at[0]), (after, out.at[1]), (low, out.at[2, pl.ds(0, half)]),
             (high, out.at[2, pl.ds(half, half)]), (before, out.at[3]))
    copies = [pltpu.make_async_copy(ref, to, sems.at[i]) for i, (ref, to) in enumerate(parts)]
    for copy in copies:
        copy.start()
    for copy in copies:
        copy.wait()


def stack_ring(pieces):
    rows = pieces[0].shape[0]
    return pl.pallas_call(
        stack_ring_kernel,
        in_specs=[ANYWHERE] * 5,
        out_specs=ANYWHERE,
        out_shape=shaped(4, rows, B),
        scratch_shapes=[pltpu.SemaphoreType.DMA((5,))],
        compiler_params=params(),
        cost_estimate=cost(0, 4),
        name="stack_ring",
    )(*pieces)


def finish_hidden_kernel(sums_ref, weight_ref, gain_ref, out_ref, gain_out, rows):
    for y in range(4):
        for core in range(2):
            slab = sums_ref[y, 0, core].astype(F32)
            for zx in range(8):
                at = (2 * zx + core) * 4 * PIECE + y * PIECE
                rows[at : at + PIECE] = slab[zx * PIECE : (zx + 1) * PIECE]
    gain = gain_ref[...]
    total = jnp.zeros((B, 1), F32)
    for i in range(FF // B):
        lanes = slice(i * B, (i + 1) * B)
        block = rows[lanes].T
        total = total + jnp.sum(block * weight_ref[:, lanes].astype(F32), axis=1, keepdims=True)
        out_ref[:, lanes] = block * gain
    gain_out[...] = total


def finish_hidden(sums, matrix, weight, gain):
    return pl.pallas_call(
        finish_hidden_kernel,
        grid=(1,),
        in_specs=[
            pl.BlockSpec((4, 1, 2, FFL, B), lambda i: (0, matrix, 0, 0, 0)),
            pl.BlockSpec((B, FF), lambda i: (0, 0)),
            pl.BlockSpec((B, 1), lambda i: (0, 0)),
        ],
        out_specs=[pl.BlockSpec((B, FF), lambda i: (0, 0)), pl.BlockSpec((B, 1), lambda i: (0, 0))],
        out_shape=[shaped(B, FF, kind=F32), shaped(B, 1, kind=F32)],
        scratch_shapes=[pltpu.VMEM((FF, B), F32)],
        compiler_params=params("arbitrary"),
        cost_estimate=cost(0, 6),
        name="finish_hidden",
    )(sums, weight, gain)


def finish_down_kernel(sums_ref, out_ref):
    for y in range(4):
        for half in range(2):
            slab = sums_ref[y, half, 0].astype(F32)
            for t in range(8):
                lane = (half * 8 + t) * B
                out_ref[y * PIECE : (y + 1) * PIECE, lane : lane + B] = slab[t * PIECE : (t + 1) * PIECE]


def finish_down(sums):
    return pl.pallas_call(
        finish_down_kernel,
        grid=(1,),
        in_specs=[pl.BlockSpec((4, 2, 1, FFL, B), lambda i: (0, 0, 2, 0, 0))],
        out_specs=pl.BlockSpec((4 * PIECE, D), lambda i: (0, 0)),
        out_shape=shaped(4 * PIECE, D, kind=F32),
        compiler_params=params("arbitrary"),
        cost_estimate=cost(0, 5),
        name="finish_down",
    )(sums)


def own_rows(rows_all, y, core, per):
    return lax.dynamic_slice_in_dim(rows_all, (2 * y + core) * per, per, 0)


class Flow:
    def __init__(self, steps):
        self.steps, self.result, self.sent = steps, None, None
        self.move(None)

    def move(self, arrived):
        try:
            self.sent = self.steps.send(arrived)
        except StopIteration as end:
            self.sent, self.result = (), end.value


def stage(flows, *values):
    flows = [flow for flow in flows if flow.result is None]
    sizes = [len(flow.sent) for flow in flows]
    leaves, tree = jax.tree.flatten(values)
    tied = tie(*[v for flow in flows for v in flow.sent], *leaves)
    for flow, size in zip(flows, sizes):
        flow.move(tied[:size])
        tied = tied[size:]
    return jax.tree.unflatten(tree, tied)


def gather_steps(block):
    (other,) = yield (swap_core(block),)
    pair = jnp.stack([block, other])
    (got,) = yield (along_y(pair),)
    far, swapped = yield (along_y(send_half(got)), swap_core(got))
    (far_swapped,) = yield (swap_core(far),)
    return pair, got, swapped, far, far_swapped


def scatter_steps(parts):
    core = lax.axis_index("core")
    first, behind, ahead, far, far_other = parts
    (far_got,) = yield (swap_core(far_other),)
    far = add(far, far_got[::-1]).astype(BF16)
    low, behind_got, first_got = yield (along_y(far), swap_core(behind), swap_core(first[1]))
    ahead = add(ahead, behind_got[::-1])
    mine = lax.dynamic_slice_in_dim(ahead, core * (B // 2), B // 2, 1) + low.astype(F32)
    ahead = lax.dynamic_update_slice_in_dim(ahead, mine, core * (B // 2), 1).astype(BF16)
    (got,) = yield (along_y(ahead),)
    (last,) = yield (swap_core(got[1]),)
    return add(first[0], first_got) + got[0].astype(F32) + last.astype(F32)


def ring_gather_steps(block, axis):
    half = block.shape[0] // 2
    before, after = yield (shift(block, axis, 1), shift(block, axis, -1))
    low, high = yield (shift(before[:half], axis, 1), shift(after[half:], axis, -1))
    return block, after, low, high, before


def ring_scatter_steps(parts, axis):
    half = parts[2].shape[0] // 2
    low, high = yield (shift(parts[2][:half], axis, 1), shift(parts[2][half:], axis, -1))
    after = jnp.concatenate([add(parts[1][:half], low).astype(BF16), parts[1][half:]], axis=0)
    before = jnp.concatenate([parts[3][:half], add(parts[3][half:], high).astype(BF16)], axis=0)
    from_before, from_after = yield (shift(after, axis, 1), shift(before, axis, -1))
    return add(parts[0], from_before) + from_after.astype(F32)


def on_device(
    layer_input,
    positions,
    attn_gain,
    w_query,
    w_key,
    w_value,
    w_output,
    mlp_gain,
    w_gate,
    w_up,
    w_down,
    out_grad,
):
    zlo, y, zhi, x, core = (lax.axis_index(axis) for axis in AXES)
    place = jnp.stack([zlo, y, core, x, zhi]).astype(jnp.int32)

    def by_core(mine, got):
        return jnp.where(core == 0, jnp.stack([mine, got]), jnp.stack([got, mine]))

    def by_zlo(mine, got):
        return jnp.where(zlo == 0, jnp.stack([mine, got]), jnp.stack([got, mine]))

    def by_zhi(mine, got):
        return jnp.where(zhi == 0, jnp.stack([mine, got]), jnp.stack([got, mine]))

    def trio(mine, other, axis):
        across = lax.ppermute(other, (axis, "core"), [(i, 3 - i) for i in range(4)])
        return shift(mine, axis, 1), swap_core(other), across

    def column_steps(mine, got):
        pair = by_core(mine, got)
        (got,) = yield (shift(pair, "zhi", 1),)
        return (yield from ring_gather_steps(by_zhi(pair, got), "x"))

    def output_steps(mine, other):
        there, here, across = yield trio(mine, other, "zhi")
        column = by_zhi(by_core(mine, here), by_core(there, across))
        return (yield from ring_gather_steps(column, "x"))

    def hidden_steps(mine, got, down):
        piece = jnp.concatenate([by_core(mine, got).reshape(2 * FFL, B), down], axis=0)
        return stack_ring((yield from ring_gather_steps(piece, "z")))

    def of_core(pair, other=False):
        return lax.dynamic_index_in_dim(pair, 1 - core if other else core, 0, keepdims=False)

    def whole_ring(pieces):
        own, after, low, high, before = pieces
        return own, after, jnp.concatenate([low, high], axis=0), before

    def attention_steps(terms):
        column = yield from ring_scatter_steps([terms[i] for i in range(4)], "x")
        keep = lax.dynamic_index_in_dim(column, zhi, 0, keepdims=False)
        send = lax.dynamic_index_in_dim(column, 1 - zhi, 0, keepdims=False).astype(BF16)
        (got,) = yield (shift(send, "zhi", 1),)
        pair = (keep + got.astype(F32)).astype(BF16)
        mine, other = of_core(pair), of_core(pair, True)
        there, here, across = yield trio(mine, other, "zlo")
        own = by_core(add(mine, there), add(here, across)).astype(BF16)
        return whole_ring((yield from ring_gather_steps(own, "y")))

    def ff_steps(sums):
        own = yield from ring_scatter_steps([sums[i] for i in range(4)], "z")
        own = own.astype(BF16)
        pair, down = own[: 2 * FFL].reshape(2, FFL, B), own[2 * FFL :]
        mine, other = of_core(pair), of_core(pair, True)
        there, here, across = yield trio(jnp.concatenate([mine, down], axis=0), other, "zlo")
        both = by_zlo(by_core(mine, here), by_core(there[:FFL], across))
        return jnp.concatenate([both, by_zlo(down, there[FFL:])[:, None]], axis=1)

    x_low = layer_input[0]
    frequency = theta ** (-jnp.arange(0, HD, 2).astype(F32) / HD)
    angles = positions[0].astype(F32)[:, None] * frequency
    tables = []
    for table in (jnp.cos(angles), jnp.sin(angles)):
        high = lax.reduce_precision(table, 8, 7)
        tables += [high.astype(BF16), (table - high).astype(BF16)]
    tokens = Flow(gather_steps(jnp.concatenate([x_low, *tables], axis=1)))
    grads = Flow(gather_steps(out_grad[0]))
    qkv_mine, qkv_other = prepare_qkv(place, w_query, w_key, w_value, attn_gain[:, None])
    qkv_mine, qkv_got, gain_two, w_out = stage([tokens], qkv_mine, swap_core(qkv_other), mlp_gain[:, None], w_output)

    columns = Flow(column_steps(qkv_mine, qkv_got))
    o_rows = lax.all_to_all(w_out.reshape(B, 16, B).transpose(1, 0, 2), FSDP, 0, 0, tiled=True)
    ff_mine, ff_other, ff_down = prepare_ff(place, w_gate, w_up, w_down, gain_two)
    ff_mine, ff_got, ff_down, x_low, o_rows = stage(
        [tokens, columns], ff_mine, swap_core(ff_other), ff_down, x_low, o_rows
    )

    inputs = x_low.astype(F32)
    scale_one = lax.rsqrt(jnp.mean(inputs * inputs, axis=-1, keepdims=True) + eps)
    o_rows = o_rows.reshape(D, B)
    mine, other = own_rows(o_rows, y, core, HEADS * HD), own_rows(o_rows, y, 1 - core, HEADS * HD)
    scale_one, mine, other, ff_mine, ff_got, ff_down = stage(
        [tokens, columns, grads], scale_one, mine, other, ff_mine, ff_got, ff_down
    )

    outputs = Flow(output_steps(mine, other))
    ff_mine, ff_got, ff_down = stage([tokens, columns, outputs], ff_mine, ff_got, ff_down)

    hidden_rows = Flow(hidden_steps(ff_mine, ff_got, ff_down))
    x_pieces = tokens.result
    query, key_value, scale_all, cosine, sine, qkv_full = project_qkv(place, x_pieces, columns.result)
    query, key_value = stage([hidden_rows, outputs, grads], query, key_value)

    earlier = lax.ppermute(key_value, "zlo", [(0, 1)])
    query, key_value, earlier = stage([outputs, hidden_rows], query, key_value, earlier)
    ff_all = lax.all_gather(hidden_rows.result, "x", axis=0, tiled=False)

    key_value = jnp.concatenate([earlier, key_value], axis=1)
    mixed, log_total, *parts, o_full = attention(place, outputs.result, query, key_value)
    parts = stage([grads], *parts)
    sums = Flow(scatter_steps(parts))
    stage([sums, grads])
    grad_pieces = grads.result
    for _ in range(3):
        stage([sums])
    hidden = inputs + sums.result
    scale_two = lax.rsqrt(jnp.mean(hidden * hidden, axis=-1, keepdims=True) + eps)
    normed = Flow(gather_steps((hidden * scale_two).astype(BF16)))
    for _ in range(4):
        stage([normed])
    normed_pieces = normed.result

    activation, act_t, gate_t, up_t, *parts, down_full = feed_forward(place, normed_pieces, grad_pieces, ff_all)
    sums = Flow(scatter_steps(parts))
    (act_t,) = stage([sums], act_t)
    down_terms = ff_terms(down_kernel, place, grad_pieces, (act_t,), FFL, "down_terms")
    down_terms, gate_t = stage([sums], down_terms, gate_t)
    down_sum = lax.psum_scatter(down_terms, "x", scatter_dimension=0, tiled=True)[0]
    gate_up_terms = ff_terms(gate_up_kernel, place, normed_pieces, (gate_t, up_t), 2 * FFL, "gate_up_terms")
    (gate_up_terms,) = stage([sums], gate_up_terms)
    gate_up_sum = lax.psum_scatter(gate_up_terms, "x", scatter_dimension=0, tiled=True)[0]
    stage([sums])

    grad_normed_two = sums.result
    mean_two = jnp.mean(grad_normed_two * hidden, axis=-1, keepdims=True)
    grad_hidden = (
        out_grad[0].astype(F32)
        + scale_two * grad_normed_two
        - hidden * (scale_two * scale_two * scale_two) * mean_two
    )
    hidden_grads = Flow(gather_steps(grad_hidden.astype(BF16)))
    (activation,) = stage([hidden_grads], activation)
    down_parts = project(activation, down_full)
    down_parts = stage([hidden_grads], *down_parts)
    result = Flow(scatter_steps(down_parts))
    stage([hidden_grads, result])
    stage([hidden_grads])

    hidden_grad_pieces = hidden_grads.result
    grad_query, grad_earlier, grad_own = attention_back(
        place, hidden_grad_pieces, query, key_value, log_total, o_full
    )
    grad_query, grad_earlier, grad_own, mixed = stage([result], grad_query, grad_earlier, grad_own, mixed)
    later = lax.ppermute(grad_earlier, "zlo", [(1, 0)])
    output_terms = attention_terms(place, hidden_grad_pieces, mixed.reshape(2 * HALF, HEADS * HD), "output_terms")
    later, grad_query, output_terms, down_sum, gate_up_sum = stage(
        [result], later, grad_query, output_terms, down_sum, gate_up_sum
    )
    ff_sums = Flow(ff_steps(jnp.concatenate([gate_up_sum, down_sum], axis=1)))
    output_sums = Flow(attention_steps(output_terms))
    *parts, grad_t = qkv_back(grad_query, grad_own, later, cosine, sine, scale_all, qkv_full)
    *parts, grad_t = stage([ff_sums, output_sums, result], *parts, grad_t)

    sums = Flow(scatter_steps(parts))
    terms = attention_terms(place, x_pieces, grad_t, "qkv_terms")
    (terms,) = stage([sums, ff_sums, output_sums], terms)
    attention_sums = Flow(attention_steps(terms))
    stage([sums, attention_sums, ff_sums, output_sums])
    ff_sums = lax.all_gather(ff_sums.result, "y", axis=0, tiled=False)
    stage([sums, attention_sums, output_sums])
    stage([sums, attention_sums, output_sums])
    grad_normed = sums.result
    mean_one = jnp.mean(grad_normed * inputs, axis=-1, keepdims=True)
    input_grad = (
        grad_hidden
        + scale_one * grad_normed
        - inputs * (scale_one * scale_one * scale_one) * mean_one
    )
    input_grad = input_grad.astype(BF16)
    stage([attention_sums, output_sums])

    ring = jnp.roll(jnp.stack(output_sums.result), y, axis=0).reshape(16, B, B)
    output_grad = lax.all_to_all(ring, FSDP, 0, 0, tiled=True)
    stage([attention_sums])
    stage([attention_sums])

    gain_two = mlp_gain[:, None]
    query_grad, key_grad, value_grad, attn_gain_grad = finish_attention(
        place, attention_sums.result, w_query, w_key, w_value, attn_gain[:, None]
    )
    gate_grad, gate_gain = finish_hidden(ff_sums, 0, w_gate, gain_two)
    up_grad, up_gain = finish_hidden(ff_sums, 1, w_up, gain_two)
    down_grad = finish_down(ff_sums)
    output_grad = finish_output(output_grad)
    return (
        (hidden + result.result).astype(BF16)[None],
        input_grad[None],
        attn_gain_grad[:, 0],
        query_grad,
        key_grad,
        value_grad,
        output_grad,
        (gate_gain + up_gain)[:, 0],
        gate_grad,
        up_grad,
        down_grad,
    )


def solution(mesh):
    split = Mesh(mesh.devices.reshape(2, 4, 2, 4, 2), AXES)
    tokens = P(FSDP, SEQ, None)
    rows = P(FSDP, None)
    gain = P(FSDP)
    in_specs = (
        tokens, P(FSDP, SEQ), gain, rows, rows, rows, rows, gain, rows, rows, rows, tokens,
    )
    out_specs = (tokens, tokens, gain, rows, rows, rows, rows, gain, rows, rows, rows)
    return jax.shard_map(
        on_device, mesh=split, in_specs=in_specs, out_specs=out_specs, check_vma=False
    )
```

```python
import jax
import jax.numpy as jnp
from jax import lax
from jax.experimental import pallas as pl
from jax.experimental.pallas import tpu as pltpu
from jax.sharding import Mesh
from jax.sharding import PartitionSpec as P

H = 32
KV = 4
HD = 64
D = 2048
FF = 5632
B = 128
HALF = 512
HEADS = 4
FFL = 704
PIECE = 88

eps = 1e-05
theta = 10000.0
F32 = jnp.float32
BF16 = jnp.bfloat16
AXES = ("zlo", "y", "zhi", "x", "core")
FSDP = ("zhi", "x", "core")
SEQ = ("zlo", "y")


def matmul(left, right):
    return jnp.dot(left, right, preferred_element_type=F32)


def times_transposed(left, right):
    return lax.dot_general(left, right, (((1,), (1,)), ((), ())), preferred_element_type=F32)


def outer_sum(left, right):
    return lax.dot_general(left, right, (((0,), (0,)), ((), ())), preferred_element_type=F32)


def shift(value, axis, by):
    if axis == "z":
        at = [2 * (z % 2) + z // 2 for z in range(4)]
        return lax.ppermute(value, ("zlo", "zhi"), [(at[z], at[(z + by) % 4]) for z in range(4)])
    size = lax.axis_size(axis)
    return lax.ppermute(value, axis, [(i, (i + by) % size) for i in range(size)])


def swap_core(value):
    return shift(value, "core", 1)


def small_gather(block, axis):
    return shift(block, axis, -1), shift(block, axis, 2), shift(block, axis, 1)


def tie(*values):
    return lax.optimization_barrier(values)


def add(left, right):
    return left.astype(F32) + right.astype(F32)


def along_y(value):
    pairs = []
    for i in range(4):
        pairs.append((2 * i, 2 * ((i + 1) % 4)))
        pairs.append((2 * i + 1, 2 * ((i + 3) % 4) + 1))
    return lax.ppermute(value, ("y", "core"), pairs)


def send_half(got):
    core = lax.axis_index("core")
    return lax.dynamic_slice_in_dim(got, core * (B // 2), B // 2, 1)


FLIPPED = (0, 0, 1, 0, 1)
LENGTHS = (B, B, B, B // 2, B // 2)


def put_tokens(refs, rows_ref, sems, start):
    lanes = pl.ds(0, rows_ref.shape[1])
    copies = []
    row = 0
    for s in range(2):
        for ref, flip, length in zip(refs, FLIPPED, LENGTHS):
            copies.append(
                pltpu.make_async_copy(
                    ref.at[s ^ flip, :, lanes], rows_ref.at[pl.ds(row, length)], sems.at[start + len(copies)]
                )
            )
            row += length
    return copies


TILE = 256
WIDE = D + B
VMEM_LIMIT = 56 * 2**20
ANYWHERE = pl.BlockSpec(memory_space=pl.ANY)


def params(*kinds):
    return pltpu.CompilerParams(dimension_semantics=kinds or None, vmem_limit_bytes=VMEM_LIMIT)


def cost(flops, megabytes):
    return pl.CostEstimate(flops=flops, bytes_accessed=int(megabytes * 2**20), transcendentals=0)


def shaped(*shape, kind=BF16):
    return jax.ShapeDtypeStruct(shape, kind)


PART_SPECS = [pl.BlockSpec((1, n, D), lambda i, *_: (i // 2, 0, 0)) for n in LENGTHS]
PART_SHAPES = [jax.ShapeDtypeStruct((2, n, D), BF16) for n in LENGTHS]


def put_parts(step, tile, refs):
    @pl.when(step % 2 == 0)
    def _():
        refs[0][0] = tile[:B]
        refs[1][0] = tile[B:]

    @pl.when(step % 2 == 1)
    def _():
        refs[2][0] = tile[:B]
        refs[3][0] = tile[B : B + B // 2]
        refs[4][0] = tile[B + B // 2 :]


def turned(values):
    lane = lax.broadcasted_iota(jnp.int32, values.shape, 1) % HD
    return jnp.where(lane < HD // 2, -pltpu.roll(values, 2 * HD - HD // 2, 1), pltpu.roll(values, HD // 2, 1))


def lane_block(zhi, x, core):
    return pl.ds(pl.multiple_of((zhi * 8 + x * 2 + core) * B, B), B)


def put_columns(place, refs, into, sems, start):
    copies = []
    for ref, by, first in zip(refs, (0, 1, 2, 2, 3), (0, 0, 0, 1, 0)):
        for i in range(ref.shape[0]):
            for core in range(2):
                lanes = lane_block(first + i, (place[3] + by) % 4, core)
                copies.append(
                    pltpu.make_async_copy(ref.at[i, core], into.at[:, lanes], sems.at[start + len(copies)])
                )
    return copies


def prepare_qkv_kernel(place, q_mine, q_other, w_key, w_value, gain, mine_ref, other_ref, k_rows, v_rows):
    scale = gain[...]
    k_rows[...] = (w_key[...].astype(F32) * scale).T
    v_rows[...] = (w_value[...].astype(F32) * scale).T
    rows = pl.ds(pl.multiple_of(place[1] * HD, HD), HD)
    for source, out in ((q_mine, mine_ref), (q_other, other_ref)):
        out[: HEADS * HD] = (source[...].astype(F32) * scale).T.astype(BF16)
        out[HEADS * HD : (HEADS + 1) * HD] = k_rows[rows].astype(BF16)
        out[(HEADS + 1) * HD :] = v_rows[rows].astype(BF16)


QKV = (HEADS + 2) * HD


def prepare_qkv(place, w_query, w_key, w_value, gain):
    whole = lambda *shape: pl.BlockSpec(shape, lambda i, p: (0,) * len(shape))
    return pl.pallas_call(
        prepare_qkv_kernel,
        grid_spec=pltpu.PrefetchScalarGridSpec(
            num_scalar_prefetch=1,
            grid=(1,),
            in_specs=[
                pl.BlockSpec((B, HEADS * HD), lambda i, p: (0, 2 * p[1] + p[2])),
                pl.BlockSpec((B, HEADS * HD), lambda i, p: (0, 2 * p[1] + 1 - p[2])),
                whole(B, KV * HD), whole(B, KV * HD), whole(B, 1),
            ],
            out_specs=[whole(QKV, B), whole(QKV, B)],
            scratch_shapes=[pltpu.VMEM((KV * HD, B), F32), pltpu.VMEM((KV * HD, B), F32)],
        ),
        out_shape=[shaped(QKV, B), shaped(QKV, B)],
        compiler_params=params("arbitrary"),
        cost_estimate=cost(0, 1),
        name="prepare_qkv",
    )(place, w_query, w_query, w_key, w_value, gain)


def prepare_ff_kernel(place, w_gate, w_up, w_down, gain, mine_ref, other_ref, down_ref, picked, rows, down_rows, sems):
    zlo, y, core = place[0], place[1], place[2]
    down = pltpu.make_async_copy(
        w_down.at[:, pl.ds(pl.multiple_of(zlo * (D // 2), D // 2), D // 2)], down_rows, sems.at[1]
    )
    down.start()

    @pl.when(zlo == 0)
    def _():
        copy = pltpu.make_async_copy(w_gate, picked, sems.at[0])
        copy.start()
        copy.wait()

    @pl.when(zlo == 1)
    def _():
        copy = pltpu.make_async_copy(w_up, picked, sems.at[0])
        copy.start()
        copy.wait()

    scale = gain[...]
    for i in range(FF // B):
        rows[i * B : (i + 1) * B] = (picked[:, i * B : (i + 1) * B].astype(F32) * scale).T
    for which, out in ((core, mine_ref), (1 - core, other_ref)):
        slabs = []
        for zx in range(8):
            at = pl.multiple_of(zx * 2 * 4 * PIECE + which * 4 * PIECE + y * PIECE, 8)
            slabs.append(rows[pl.ds(at, PIECE)])
        out[...] = jnp.concatenate(slabs, axis=0).astype(BF16)
    down.wait()
    for t in range(8):
        rows[t * 4 * PIECE : (t + 1) * 4 * PIECE] = down_rows[:, t * B : (t + 1) * B].astype(F32)
    slabs = [rows[pl.ds(pl.multiple_of(t * 4 * PIECE + y * PIECE, 8), PIECE)] for t in range(8)]
    down_ref[...] = jnp.concatenate(slabs, axis=0).astype(BF16)


def prepare_ff(place, w_gate, w_up, w_down, gain):
    return pl.pallas_call(
        prepare_ff_kernel,
        grid_spec=pltpu.PrefetchScalarGridSpec(
            num_scalar_prefetch=1,
            grid=(1,),
            in_specs=[ANYWHERE, ANYWHERE, ANYWHERE, pl.BlockSpec((B, 1), lambda i, p: (0, 0))],
            out_specs=[pl.BlockSpec((FFL, B), lambda i, p: (0, 0))] * 3,
            scratch_shapes=[
                pltpu.VMEM((B, FF), BF16),
                pltpu.VMEM((FF, B), F32),
                pltpu.VMEM((4 * PIECE, D // 2), BF16),
                pltpu.SemaphoreType.DMA((2,)),
            ],
        ),
        out_shape=[shaped(FFL, B)] * 3,
        compiler_params=params("arbitrary"),
        cost_estimate=cost(0, 6),
        name="prepare_ff",
    )(place, w_gate, w_up, w_down, gain)


def project_qkv_kernel(*refs):
    place, x_refs, w_refs = refs[0], refs[1:6], refs[6:11]
    query_ref, kv_ref, scale_ref, cosine_ref, sine_ref, w_out, rows, weights, sems = refs[11:]
    step = pl.program_id(0)
    tokens = put_tokens(x_refs, rows, sems, 0)
    columns = put_columns(place, w_refs, weights, sems, 10)
    back = pltpu.make_async_copy(weights, w_out, sems.at[26])

    @pl.when(step == 0)
    def _():
        for copy in columns + tokens:
            copy.start()
        for copy in columns:
            copy.wait()
        back.start()
        for copy in tokens:
            copy.wait()

    at = pl.ds(pl.multiple_of(step * TILE, TILE), TILE)
    tile = rows[at, :D]
    wide = tile.astype(F32)
    scale = lax.rsqrt(jnp.mean(wide * wide, axis=-1, keepdims=True) + eps)
    scale_ref[...] = scale
    pre = times_transposed(tile, weights[...]) * scale
    tables = rows[at, D:].astype(F32)
    tables = tables + pltpu.roll(tables, B - HD // 2, 1)
    cosine = jnp.concatenate([tables[:, : HD // 2]] * 4, axis=1)
    sine = jnp.concatenate([tables[:, HD : HD + HD // 2]] * 4, axis=1)
    cosine_ref[...] = cosine
    sine_ref[...] = sine
    for i in range(2):
        part = pre[:, i * 2 * HD : (i + 1) * 2 * HD]
        part = (part * cosine + turned(part) * sine).astype(BF16) * HD ** (-0.5)
        query_ref[0, 2 * i] = part[:, :HD]
        query_ref[0, 2 * i + 1] = part[:, HD:]
    part = pre[:, HEADS * HD :]
    lane = lax.broadcasted_iota(jnp.int32, part.shape, 1)
    kv_ref[0] = jnp.where(lane < HD, part * cosine + turned(part) * sine, part).astype(BF16)

    @pl.when(step == 3)
    def _():
        back.wait()


def project_qkv(place, x_pieces, w_pieces):
    tile = lambda lanes: pl.BlockSpec((TILE, lanes), lambda i, p: (i, 0))
    return pl.pallas_call(
        project_qkv_kernel,
        grid_spec=pltpu.PrefetchScalarGridSpec(
            num_scalar_prefetch=1,
            grid=(4,),
            in_specs=[ANYWHERE] * 10,
            out_specs=[
                pl.BlockSpec((1, HEADS, TILE, HD), lambda i, p: (i // 2, 0, i % 2, 0)),
                pl.BlockSpec((1, TILE, 2 * HD), lambda i, p: (i // 2, i % 2, 0)),
                tile(1), tile(2 * HD), tile(2 * HD),
                ANYWHERE,
            ],
            scratch_shapes=[
                pltpu.VMEM((2 * HALF, WIDE), BF16),
                pltpu.VMEM((QKV, D), BF16),
                pltpu.SemaphoreType.DMA((27,)),
            ],
        ),
        out_shape=[
            shaped(2, HEADS, HALF, HD), shaped(2, HALF, 2 * HD), shaped(2 * HALF, 1, kind=F32),
            shaped(2 * HALF, 2 * HD, kind=F32), shaped(2 * HALF, 2 * HD, kind=F32), shaped(QKV, D),
        ],
        compiler_params=params("arbitrary"),
        cost_estimate=cost(2 * 2 * HALF * QKV * D, 8),
        name="project_qkv",
    )(place, *x_pieces, *w_pieces)


def project_kernel(left_ref, weight_ref, *parts):
    put_parts(pl.program_id(0), matmul(left_ref[...], weight_ref[...]).astype(BF16), parts)


def project(left, weight):
    depth = left.shape[1]
    return pl.pallas_call(
        project_kernel,
        grid=(4,),
        in_specs=[pl.BlockSpec((TILE, depth), lambda i: (i, 0)), pl.BlockSpec((depth, D), lambda i: (0, 0))],
        out_specs=PART_SPECS,
        out_shape=PART_SHAPES,
        compiler_params=params("arbitrary"),
        cost_estimate=cost(2 * 2 * HALF * depth * D, 8),
        name="project",
    )(left, weight)


def put_term(left, rows, term_ref):
    def one(i, carry):
        term = matmul(left, rows[:, pl.ds(pl.multiple_of(i * 4 * B, 4 * B), 4 * B)]).astype(BF16)
        for j in range(2):
            zx = 2 * i + j
            term_ref[zx % 4, zx // 4, 0] = term[:, 2 * j * B : (2 * j + 1) * B]
            term_ref[zx % 4, zx // 4, 1] = term[:, (2 * j + 1) * B : (2 * j + 2) * B]
        return carry

    lax.fori_loop(0, 4, one, 0)


def qkv_back_kernel(grad_q_ref, own_ref, later_ref, cosine_ref, sine_ref, scale_ref, weight_ref, *outs):
    parts, turned_ref = outs[:5], outs[5]
    cosine, sine = cosine_ref[...], sine_ref[...]
    lane = lax.broadcasted_iota(jnp.int32, cosine.shape, 1)
    pieces = []
    for i in range(2):
        part = grad_q_ref[0, :, i * 2 * HD : (i + 1) * 2 * HD]
        pieces.append(part * cosine - turned(part * sine))
    part = own_ref[0] + later_ref[0].astype(F32)
    pieces.append(jnp.where(lane < HD, part * cosine - turned(part * sine), part))
    grad_pre = jnp.concatenate(pieces, axis=1)
    put_parts(pl.program_id(0), matmul(grad_pre.astype(BF16), weight_ref[...]).astype(BF16), parts)
    turned_ref[...] = (grad_pre * scale_ref[...]).T.astype(BF16)


def qkv_back(grad_query, own, later, cosine, sine, scale, weight):
    tile = lambda lanes: pl.BlockSpec((TILE, lanes), lambda i: (i, 0))
    half = lambda lanes: pl.BlockSpec((1, TILE, lanes), lambda i: (i // 2, i % 2, 0))
    return pl.pallas_call(
        qkv_back_kernel,
        grid=(4,),
        in_specs=[
            half(HEADS * HD), half(2 * HD), half(2 * HD), tile(2 * HD), tile(2 * HD), tile(1),
            pl.BlockSpec((QKV, D), lambda i: (0, 0)),
        ],
        out_specs=PART_SPECS + [pl.BlockSpec((QKV, TILE), lambda i: (0, i))],
        out_shape=PART_SHAPES + [shaped(QKV, 2 * HALF)],
        compiler_params=params("arbitrary"),
        cost_estimate=cost(2 * 2 * HALF * QKV * D, 9),
        name="qkv_back",
    )(grad_query, own, later, cosine, sine, scale, weight)


def attention_term_kernel(*refs):
    token_refs, left_ref = refs[1:6], refs[6]
    term_ref, rows, sems = refs[-3:]
    copies = put_tokens(token_refs, rows, sems, 0)
    for copy in copies:
        copy.start()
    left = left_ref[...]
    if left.shape[0] == 2 * HALF:
        left = left.T
    for copy in copies:
        copy.wait()
    put_term(left, rows, term_ref)


def attention_terms(place, pieces, left, name):
    whole = lambda *shape: pl.BlockSpec(shape, lambda i, p: (0,) * len(shape))
    rows = min(left.shape)
    return pl.pallas_call(
        attention_term_kernel,
        grid_spec=pltpu.PrefetchScalarGridSpec(
            num_scalar_prefetch=1,
            grid=(1,),
            in_specs=[ANYWHERE] * 5 + [whole(*left.shape)],
            out_specs=whole(4, 2, 2, rows, B),
            scratch_shapes=[pltpu.VMEM((2 * HALF, D), BF16), pltpu.SemaphoreType.DMA((10,))],
        ),
        out_shape=shaped(4, 2, 2, rows, B),
        compiler_params=params("arbitrary"),
        cost_estimate=cost(2 * 2 * HALF * rows * D, 7),
        name=name,
    )(place, *pieces, left)


def token_places(at, y, core):
    step = 1 - 2 * core
    block = jnp.where(
        at < B, y, jnp.where(at < 2 * B, y + 4 - step, jnp.where(at < 3 * B, y + 4 + step, y + 2))
    )
    row = at % B
    row = jnp.where(at < 3 * B, row, (row + core * (B // 2)) % B)
    return (block % 4) * B + row


def set_bias(place_ref, bias_ref):
    zlo, y, core = place_ref[0], place_ref[1], place_ref[2]
    key_at = token_places(lax.broadcasted_iota(jnp.int32, (HALF, 1), 0), y, core)
    query_at = token_places(lax.broadcasted_iota(jnp.int32, (1, HALF), 1), y, core)
    bias_ref[:HALF, :] = jnp.broadcast_to(jnp.where(zlo == 1, 0.0, -1e30), (HALF, HALF))
    bias_ref[HALF:, :] = jnp.where(key_at <= query_at, 0.0, -1e30)


def attention_kernel(place_ref, *refs):
    w_refs, query_ref, kv_ref, mixed_ref, log_ref = refs[:5], *refs[5:9]
    parts, w_out, bias_ref, weight, sems = refs[9:14], *refs[14:]
    columns = put_columns(place_ref, w_refs, weight, sems, 0)
    back = pltpu.make_async_copy(weight, w_out, sems.at[16])

    @pl.when(pl.program_id(0) == 0)
    def _():
        for copy in columns:
            copy.start()
        set_bias(place_ref, bias_ref)
        for copy in columns:
            copy.wait()
        back.start()

    key, value = kv_ref[0, :, :HD], kv_ref[0, :, HD:]
    for head in range(HEADS):
        scores = times_transposed(key, query_ref[0, head]) + bias_ref[...]
        top = jnp.max(scores, axis=0, keepdims=True)
        weights = jnp.exp(scores - top)
        total = jnp.sum(weights, axis=0, keepdims=True)
        low = (weights * (1.0 / total)).astype(BF16)
        mixed_ref[0, :, head * HD : (head + 1) * HD] = outer_sum(value, low).T.astype(BF16)
        log_ref[0, head] = top + jnp.log(total)
    put_rows(parts, matmul(mixed_ref[0], weight[...]).astype(BF16))

    @pl.when(pl.program_id(0) == 1)
    def _():
        back.wait()


def put_rows(parts, rows):
    row = 0
    for ref, length in zip(parts, LENGTHS):
        ref[0] = rows[row : row + length]
        row += length


def attention_back_kernel(place_ref, *refs):
    grad_refs, query_ref, kv_ref, log_ref, weight_ref = refs[:5], *refs[5:9]
    grad_query_ref, earlier_ref, own_ref, bias_ref, rows, sems = refs[9:]
    step = pl.program_id(0)
    copies = put_tokens(grad_refs, rows, sems, 0)

    @pl.when(step == 0)
    def _():
        for copy in copies:
            copy.start()
        set_bias(place_ref, bias_ref)
        for copy in copies:
            copy.wait()

    hidden = rows[pl.ds(pl.multiple_of(step * HALF, HALF), HALF), :]
    grads = times_transposed(hidden, weight_ref[...]).astype(BF16)
    key, value = kv_ref[0, :, :HD], kv_ref[0, :, HD:]
    grad_key = jnp.zeros((2 * HALF, HD), F32)
    grad_value = jnp.zeros((2 * HALF, HD), F32)
    for head in range(HEADS):
        lanes = slice(head * HD, (head + 1) * HD)
        query, grad = query_ref[0, head], grads[:, lanes]
        weights = jnp.exp(times_transposed(key, query) + bias_ref[...] - log_ref[0, head])
        grad_weights = times_transposed(value, grad)
        delta = jnp.sum(weights * grad_weights, axis=0, keepdims=True)
        grad_scores = (weights * (grad_weights - delta)).astype(BF16)
        grad_query_ref[0, :, lanes] = outer_sum(key, grad_scores).T * HD ** (-0.5)
        grad_key += matmul(grad_scores, query)
        grad_value += matmul(weights.astype(BF16), grad)
    total = jnp.concatenate([grad_key, grad_value], axis=1)
    earlier_ref[0] = total[:HALF].astype(BF16)
    own_ref[0] = total[HALF:]


def sequence_block(*tail):
    return pl.BlockSpec((1,) + tail, lambda s, place: (s,) + (0,) * len(tail))


def attention_call(kernel, in_specs, out_specs, out_shape, scratch, flops, name):
    return pl.pallas_call(
        kernel,
        grid_spec=pltpu.PrefetchScalarGridSpec(
            num_scalar_prefetch=1,
            grid=(2,),
            in_specs=in_specs,
            out_specs=out_specs,
            scratch_shapes=[pltpu.VMEM((2 * HALF, HALF), F32)] + scratch,
        ),
        out_shape=out_shape,
        compiler_params=params("arbitrary"),
        cost_estimate=cost(flops * 8 * 2 * HALF * HALF * HD * 2, 8),
        name=name,
    )


def attention(place, w_pieces, query, kv):
    return attention_call(
        attention_kernel,
        [ANYWHERE] * 5 + [sequence_block(HEADS, HALF, HD), sequence_block(2 * HALF, 2 * HD)],
        [sequence_block(HALF, HEADS * HD), sequence_block(HEADS, 1, HALF)]
        + [sequence_block(n, D) for n in LENGTHS]
        + [ANYWHERE],
        [shaped(2, HALF, HEADS * HD), shaped(2, HEADS, 1, HALF, kind=F32)] + PART_SHAPES + [shaped(HEADS * HD, D)],
        [pltpu.VMEM((HEADS * HD, D), BF16), pltpu.SemaphoreType.DMA((17,))],
        3,
        "attention",
    )(place, *w_pieces, query, kv)


def attention_back(place, grad_pieces, query, kv, log_total, weight):
    return attention_call(
        attention_back_kernel,
        [ANYWHERE] * 5
        + [
            sequence_block(HEADS, HALF, HD), sequence_block(2 * HALF, 2 * HD),
            sequence_block(HEADS, 1, HALF), pl.BlockSpec((HEADS * HD, D), lambda s, place: (0, 0)),
        ],
        [sequence_block(HALF, HEADS * HD), sequence_block(HALF, 2 * HD), sequence_block(HALF, 2 * HD)],
        [
            shaped(2, HALF, HEADS * HD, kind=F32),
            shaped(2, HALF, 2 * HD),
            shaped(2, HALF, 2 * HD, kind=F32),
        ],
        [pltpu.VMEM((2 * HALF, D), BF16), pltpu.SemaphoreType.DMA((10,))],
        6,
        "attention_back",
    )(place, *grad_pieces, query, kv, log_total, weight)


def finish_attention_kernel(place, *refs):
    piece_refs, w_query, w_key, w_value, gain_ref = refs[:4], *refs[4:8]
    query_out, key_out, value_out, gain_out, rows = refs[8:]
    for ref, by in zip(piece_refs, range(4)):
        at_y = (place[1] + by) % 4
        for c in range(2):
            piece = ref[c].astype(F32)
            rows[pl.ds(pl.multiple_of((2 * at_y + c) * HEADS * HD, HEADS * HD), HEADS * HD)] = piece[: HEADS * HD]
        both = ref[0].astype(F32) + ref[1].astype(F32)
        at = pl.multiple_of(H * HD + at_y * HD, HD)
        rows[pl.ds(at, HD)] = both[HEADS * HD : (HEADS + 1) * HD]
        rows[pl.ds(at + KV * HD, HD)] = both[(HEADS + 1) * HD :]
    gain = gain_ref[...]
    total = jnp.zeros((B, 1), F32)
    row = 0
    for weight, out in ((w_query, query_out), (w_key, key_out), (w_value, value_out)):
        for i in range(out.shape[1] // B):
            lanes = slice(i * B, (i + 1) * B)
            block = rows[row : row + B].T
            total = total + jnp.sum(block * weight[:, lanes].astype(F32), axis=1, keepdims=True)
            out[:, lanes] = block * gain
            row += B
    gain_out[...] = total


def finish_attention(place, pieces, w_query, w_key, w_value, gain):
    whole = lambda *shape: pl.BlockSpec(shape, lambda i, p: (0,) * len(shape))
    kv = KV * HD
    return pl.pallas_call(
        finish_attention_kernel,
        grid_spec=pltpu.PrefetchScalarGridSpec(
            num_scalar_prefetch=1,
            grid=(1,),
            in_specs=[whole(2, QKV, B)] * 4 + [whole(B, D), whole(B, kv), whole(B, kv), whole(B, 1)],
            out_specs=[whole(B, D), whole(B, kv), whole(B, kv), whole(B, 1)],
            scratch_shapes=[pltpu.VMEM((D + 2 * kv, B), F32)],
        ),
        out_shape=[
            shaped(B, D, kind=F32), shaped(B, kv, kind=F32), shaped(B, kv, kind=F32), shaped(B, 1, kind=F32),
        ],
        compiler_params=params("arbitrary"),
        cost_estimate=cost(0, 4),
        name="finish_attention",
    )(place, *pieces, w_query, w_key, w_value, gain)


def finish_output_kernel(blocks, out):
    for i in range(16):
        out[:, i * B : (i + 1) * B] = blocks[i].astype(F32)


def finish_output(blocks):
    return pl.pallas_call(
        finish_output_kernel,
        out_shape=shaped(B, D, kind=F32),
        compiler_params=params(),
        cost_estimate=cost(0, 2),
        name="finish_output",
    )(blocks)


def feed_forward_kernel(*refs):
    place, token_refs, grad_refs, ff_ref = refs[0], refs[1:6], refs[6:11], refs[11]
    act_ref, act_t, gate_t, up_t = refs[12:16]
    parts, down_out = refs[16:21], refs[21]
    rows_h, rows_g, gate_up, down, slabs, sems = refs[22:]
    step = pl.program_id(0)
    tokens = put_tokens(token_refs, rows_h, sems, 0)
    grads = put_tokens(grad_refs, rows_g, sems, 10)
    weights, loads = [], []
    for x in range(4):
        for by in range(4):
            z = (2 * place[4] + place[0] + by) % 4
            zhi, zlo = z // 2, z % 2
            for core in range(2):
                weights.append(
                    pltpu.make_async_copy(
                        ff_ref.at[x, by, pl.ds(core * FFL, FFL)],
                        gate_up.at[zlo, :, lane_block(zhi, x, core)],
                        sems.at[20 + len(weights)],
                    )
                )
            loads.append(
                pltpu.make_async_copy(
                    ff_ref.at[x, by, pl.ds(2 * FFL, FFL)], slabs.at[zlo, zhi * 4 + x], sems.at[52 + len(loads)]
                )
            )
    back = pltpu.make_async_copy(down, down_out, sems.at[68])

    @pl.when(step == 0)
    def _():
        for copy in tokens + weights + loads + grads:
            copy.start()
        for copy in tokens + weights:
            copy.wait()

    rows = pl.ds(pl.multiple_of(step * HALF, HALF), HALF)
    normed = rows_h[rows, :]
    gate_pre = times_transposed(normed, gate_up[0])
    upward = times_transposed(normed, gate_up[1])

    @pl.when(step == 0)
    def _():
        for copy in loads:
            copy.wait()

        def put(q, carry):
            for half in range(2):
                for p in range(4):
                    one = slabs[half, 2 * q, 2 * p * PIECE : 2 * (p + 1) * PIECE, :].astype(F32)
                    two = slabs[half, 2 * q + 1, 2 * p * PIECE : 2 * (p + 1) * PIECE, :].astype(F32)
                    lane = (half * 8 + 2 * p) * B
                    rows = pl.ds(pl.multiple_of(q * 2 * PIECE, 16), 2 * PIECE)
                    down[rows, lane : lane + B] = jnp.concatenate([one[:PIECE], two[:PIECE]], axis=0).astype(BF16)
                    down[rows, lane + B : lane + 2 * B] = jnp.concatenate(
                        [one[PIECE:], two[PIECE:]], axis=0
                    ).astype(BF16)
            return carry

        lax.fori_loop(0, 4, put, 0)
        back.start()
        for copy in grads:
            copy.wait()

    grad_act = times_transposed(rows_g[rows, :], down[...])
    sigmoid = 1.0 / (1.0 + jnp.exp(-gate_pre))
    silu = gate_pre * sigmoid
    activation = silu * upward
    grad_up = grad_act * silu
    grad_gate = grad_act * upward * (sigmoid * (1.0 + gate_pre * (1.0 - sigmoid)))
    part = matmul(grad_gate.astype(BF16), gate_up[0]) + matmul(grad_up.astype(BF16), gate_up[1])
    part = part.astype(BF16)
    row = 0
    for ref, length in zip(parts, LENGTHS):
        ref[0] = part[row : row + length]
        row += length
    act_ref[...] = activation.astype(BF16)
    act_t[...] = activation.T.astype(BF16)
    gate_t[...] = grad_gate.T.astype(BF16)
    up_t[...] = grad_up.T.astype(BF16)

    @pl.when(step == 1)
    def _():
        back.wait()


def feed_forward(place, tokens, grads, ff_all):
    turned_spec = pl.BlockSpec((FFL, HALF), lambda i, p: (0, i))
    turned_shape = shaped(FFL, 2 * HALF)
    return pl.pallas_call(
        feed_forward_kernel,
        grid_spec=pltpu.PrefetchScalarGridSpec(
            num_scalar_prefetch=1,
            grid=(2,),
            in_specs=[ANYWHERE] * 11,
            out_specs=[pl.BlockSpec((HALF, FFL), lambda i, p: (i, 0))]
            + [turned_spec] * 3
            + [pl.BlockSpec((1, n, D), lambda i, p: (i, 0, 0)) for n in LENGTHS]
            + [ANYWHERE],
            scratch_shapes=[
                pltpu.VMEM((2 * HALF, D), BF16),
                pltpu.VMEM((2 * HALF, D), BF16),
                pltpu.VMEM((2, FFL, D), BF16),
                pltpu.VMEM((FFL, D), BF16),
                pltpu.VMEM((2, 8, FFL, B), BF16),
                pltpu.SemaphoreType.DMA((69,)),
            ],
        ),
        out_shape=[shaped(2 * HALF, FFL)] + [turned_shape] * 3 + PART_SHAPES + [shaped(FFL, D)],
        compiler_params=params("arbitrary"),
        cost_estimate=cost(2 * 5 * 2 * HALF * FFL * D, 32),
        name="feed_forward",
    )(place, *tokens, *grads, ff_all)


def along_z(place, zhi, zlo):
    return (2 * zhi + zlo + 4 - 2 * place[4] - place[0]) % 4


def load_tokens(step, refs, rows, sems):
    copies = put_tokens(refs, rows, sems, 0)

    @pl.when(step == 0)
    def _():
        for copy in copies:
            copy.start()
        for copy in copies:
            copy.wait()


def gate_up_kernel(*refs):
    place, token_refs, gate_t, up_t, out_ref, rows, terms, sems = refs[0], refs[1:6], *refs[6:]
    step = pl.program_id(0)
    load_tokens(step, token_refs, rows, sems)
    normed = rows[:, pl.ds(pl.multiple_of(step * 4 * B, 4 * B), 4 * B)]

    def out(i, matrix):
        xs, by = pl.ds(i % 2 * 2, 2), along_z(place, i // 2, matrix)
        return pltpu.make_async_copy(terms.at[xs, by], out_ref.at[xs, by], sems.at[10 + 2 * i + matrix])

    for matrix, left in ((0, gate_t), (1, up_t)):
        term = matmul(left[...], normed).astype(BF16)
        by = along_z(place, step // 2, matrix)
        for j in range(2):
            terms[step % 2 * 2 + j, by, 0:FFL, :] = term[:, 2 * j * B : (2 * j + 1) * B]
            terms[step % 2 * 2 + j, by, FFL:, :] = term[:, (2 * j + 1) * B : (2 * j + 2) * B]
        out(step, matrix).start()

    @pl.when(step == 3)
    def _():
        for i in range(4):
            for matrix in range(2):
                out(i, matrix).wait()


def down_kernel(*refs):
    place, grad_refs, act_t, out_ref, rows, terms, sems = refs[0], refs[1:6], *refs[6:]
    step = pl.program_id(0)
    load_tokens(step, grad_refs, rows, sems)
    term = matmul(act_t[...], rows[:, pl.ds(pl.multiple_of(step * 4 * B, 4 * B), 4 * B)])
    for j in range(2):
        p = (2 * step + j) % 4
        at = pl.ds(pl.multiple_of(p * 2 * PIECE, 16), 2 * PIECE)
        for zx in range(8):
            slab = term[zx * PIECE : (zx + 1) * PIECE]
            low, high = slab[:, 2 * j * B : (2 * j + 1) * B], slab[:, (2 * j + 1) * B : (2 * j + 2) * B]
            by = along_z(place, zx // 4, step // 2)
            terms[zx % 4, by, at, :] = jnp.concatenate([low, high], axis=0).astype(BF16)

    def out(half, zhi):
        by = along_z(place, zhi, half)
        return pltpu.make_async_copy(terms.at[:, by], out_ref.at[:, by], sems.at[10 + 2 * half + zhi])

    @pl.when(step % 2 == 1)
    def _():
        for zhi in range(2):
            out(step // 2, zhi).start()

    @pl.when(step == 3)
    def _():
        for half in range(2):
            for zhi in range(2):
                out(half, zhi).wait()


def ff_terms(kernel, place, pieces, lefts, rows, name):
    whole = pl.BlockSpec((FFL, 2 * HALF), lambda i, p: (0, 0))
    return pl.pallas_call(
        kernel,
        grid_spec=pltpu.PrefetchScalarGridSpec(
            num_scalar_prefetch=1,
            grid=(4,),
            in_specs=[ANYWHERE] * 5 + [whole] * len(lefts),
            out_specs=ANYWHERE,
            scratch_shapes=[
                pltpu.VMEM((2 * HALF, D), BF16),
                pltpu.VMEM((4, 4, rows, B), BF16),
                pltpu.SemaphoreType.DMA((18,)),
            ],
        ),
        out_shape=shaped(4, 4, rows, B),
        compiler_params=params("arbitrary"),
        cost_estimate=cost(2 * len(lefts) * 2 * HALF * FFL * D, 8 + 4 * len(lefts)),
        name=name,
    )(place, *pieces, *lefts)


def finish_hidden_kernel(*refs):
    place, piece_refs, weight_ref, gain_ref, out_ref, gain_out, rows = refs[0], refs[1:5], *refs[5:]
    for ref, by in zip(piece_refs, range(4)):
        at_y = (place[1] + by) % 4
        for core in range(2):
            slab = ref[0, core].astype(F32)
            for zx in range(8):
                at = pl.multiple_of((2 * zx + core) * 4 * PIECE + at_y * PIECE, 8)
                rows[pl.ds(at, PIECE)] = slab[zx * PIECE : (zx + 1) * PIECE]
    gain = gain_ref[...]
    total = jnp.zeros((B, 1), F32)
    for i in range(FF // B):
        lanes = slice(i * B, (i + 1) * B)
        block = rows[lanes].T
        total = total + jnp.sum(block * weight_ref[:, lanes].astype(F32), axis=1, keepdims=True)
        out_ref[:, lanes] = block * gain
    gain_out[...] = total


def finish_hidden(place, pieces, matrix, weight, gain):
    own, after, low, high, before = pieces
    at = lambda m: pl.BlockSpec((1, 2, FFL, B), lambda i, p: (m, 0, 0, 0))
    whole = lambda *shape: pl.BlockSpec(shape, lambda i, p: (0,) * len(shape))
    return pl.pallas_call(
        finish_hidden_kernel,
        grid_spec=pltpu.PrefetchScalarGridSpec(
            num_scalar_prefetch=1,
            grid=(1,),
            in_specs=[at(matrix), at(matrix), at(0), at(matrix), whole(B, FF), whole(B, 1)],
            out_specs=[whole(B, FF), whole(B, 1)],
            scratch_shapes=[pltpu.VMEM((FF, B), F32)],
        ),
        out_shape=[shaped(B, FF, kind=F32), shaped(B, 1, kind=F32)],
        compiler_params=params("arbitrary"),
        cost_estimate=cost(0, 6),
        name="finish_hidden",
    )(place, own, after, (low, high)[matrix], before, weight, gain)


def finish_down_kernel(place, own, after, low, high, before, out_ref):
    for refs, by in (((own, own), 0), ((after, after), 1), ((low, high), 2), ((before, before), 3)):
        rows = pl.ds(pl.multiple_of((place[1] + by) % 4 * PIECE, 8), PIECE)
        for half in range(2):
            slab = refs[half][half if by != 2 else 0, 0].astype(F32)
            for t in range(8):
                lane = (half * 8 + t) * B
                out_ref[rows, lane : lane + B] = slab[t * PIECE : (t + 1) * PIECE]


def finish_down(place, pieces):
    halves = lambda n: pl.BlockSpec((n, 1, FFL, B), lambda i, p: (0, 2, 0, 0))
    return pl.pallas_call(
        finish_down_kernel,
        grid_spec=pltpu.PrefetchScalarGridSpec(
            num_scalar_prefetch=1,
            grid=(1,),
            in_specs=[halves(2), halves(2), halves(1), halves(1), halves(2)],
            out_specs=pl.BlockSpec((4 * PIECE, D), lambda i, p: (0, 0)),
        ),
        out_shape=shaped(4 * PIECE, D, kind=F32),
        compiler_params=params("arbitrary"),
        cost_estimate=cost(0, 5),
        name="finish_down",
    )(place, *pieces)


def own_rows(rows_all, y, core, per):
    return lax.dynamic_slice_in_dim(rows_all, (2 * y + core) * per, per, 0)


class Flow:
    def __init__(self, steps):
        self.steps, self.result, self.sent = steps, None, None
        self.move(None)

    def move(self, arrived):
        try:
            self.sent = self.steps.send(arrived)
        except StopIteration as end:
            self.sent, self.result = (), end.value


def stage(flows, *values):
    flows = [flow for flow in flows if flow.result is None]
    sizes = [len(flow.sent) for flow in flows]
    leaves, tree = jax.tree.flatten(values)
    tied = tie(*[v for flow in flows for v in flow.sent], *leaves)
    for flow, size in zip(flows, sizes):
        flow.move(tied[:size])
        tied = tied[size:]
    return jax.tree.unflatten(tree, tied)


def gather_steps(block):
    (other,) = yield (swap_core(block),)
    pair = jnp.stack([block, other])
    (got,) = yield (along_y(pair),)
    far, swapped = yield (along_y(send_half(got)), swap_core(got))
    (far_swapped,) = yield (swap_core(far),)
    return pair, got, swapped, far, far_swapped


def scatter_steps(parts):
    core = lax.axis_index("core")
    first, behind, ahead, far, far_other = parts
    (far_got,) = yield (swap_core(far_other),)
    far = add(far, far_got[::-1]).astype(BF16)
    low, behind_got, first_got = yield (along_y(far), swap_core(behind), swap_core(first[1]))
    ahead = add(ahead, behind_got[::-1])
    mine = lax.dynamic_slice_in_dim(ahead, core * (B // 2), B // 2, 1) + low.astype(F32)
    ahead = lax.dynamic_update_slice_in_dim(ahead, mine, core * (B // 2), 1).astype(BF16)
    (got,) = yield (along_y(ahead),)
    (last,) = yield (swap_core(got[1]),)
    return add(first[0], first_got) + got[0].astype(F32) + last.astype(F32)


def ring_gather_steps(block, axis):
    half = block.shape[0] // 2
    before, after = yield (shift(block, axis, 1), shift(block, axis, -1))
    low, high = yield (shift(before[:half], axis, 1), shift(after[half:], axis, -1))
    return block, after, low, high, before


def ring_scatter_steps(parts, axis):
    half = parts[2].shape[0] // 2
    low, high = yield (shift(parts[2][:half], axis, 1), shift(parts[2][half:], axis, -1))
    after = jnp.concatenate([add(parts[1][:half], low).astype(BF16), parts[1][half:]], axis=0)
    before = jnp.concatenate([parts[3][:half], add(parts[3][half:], high).astype(BF16)], axis=0)
    from_before, from_after = yield (shift(after, axis, 1), shift(before, axis, -1))
    return add(parts[0], from_before) + from_after.astype(F32)


def on_device(
    layer_input,
    positions,
    attn_gain,
    w_query,
    w_key,
    w_value,
    w_output,
    mlp_gain,
    w_gate,
    w_up,
    w_down,
    out_grad,
):
    zlo, y, zhi, x, core = (lax.axis_index(axis) for axis in AXES)
    place = jnp.stack([zlo, y, core, x, zhi]).astype(jnp.int32)

    def by_core(mine, got):
        return jnp.where(core == 0, jnp.stack([mine, got]), jnp.stack([got, mine]))

    def by_zlo(mine, got):
        return jnp.where(zlo == 0, jnp.stack([mine, got]), jnp.stack([got, mine]))

    def by_zhi(mine, got):
        return jnp.where(zhi == 0, jnp.stack([mine, got]), jnp.stack([got, mine]))

    def trio(mine, other, axis):
        across = lax.ppermute(other, (axis, "core"), [(i, 3 - i) for i in range(4)])
        return shift(mine, axis, 1), swap_core(other), across

    def column_steps(mine, got):
        pair = by_core(mine, got)
        (got,) = yield (shift(pair, "zhi", 1),)
        return (yield from ring_gather_steps(by_zhi(pair, got), "x"))

    def output_steps(mine, other):
        there, here, across = yield trio(mine, other, "zhi")
        column = by_zhi(by_core(mine, here), by_core(there, across))
        return (yield from ring_gather_steps(column, "x"))

    def hidden_steps(mine, got, down):
        piece = jnp.concatenate([by_core(mine, got).reshape(2 * FFL, B), down], axis=0)
        pieces = yield from ring_gather_steps(piece, "z")
        return jnp.concatenate(pieces, axis=0).reshape(4, 3 * FFL, B)

    def of_core(pair, other=False):
        return lax.dynamic_index_in_dim(pair, 1 - core if other else core, 0, keepdims=False)

    def whole_ring(pieces):
        own, after, low, high, before = pieces
        return own, after, jnp.concatenate([low, high], axis=0), before

    def attention_steps(column):
        keep = lax.dynamic_index_in_dim(column, zhi, 0, keepdims=False)
        send = lax.dynamic_index_in_dim(column, 1 - zhi, 0, keepdims=False)
        (got,) = yield (shift(send, "zhi", 1),)
        pair = add(keep, got).astype(BF16)
        mine, other = of_core(pair), of_core(pair, True)
        there, here, across = yield trio(mine, other, "zlo")
        own = by_core(add(mine, there), add(here, across)).astype(BF16)
        return (yield from ring_gather_steps(own, "y"))

    def ff_steps(sums):
        own = yield from ring_scatter_steps([sums[i] for i in range(4)], "z")
        own = own.astype(BF16)
        pair, down = own[: 2 * FFL].reshape(2, FFL, B), own[2 * FFL :]
        mine, other = of_core(pair), of_core(pair, True)
        there, here, across = yield trio(jnp.concatenate([mine, down], axis=0), other, "zlo")
        both = by_zlo(by_core(mine, here), by_core(there[:FFL], across))
        both = jnp.concatenate([both, by_zlo(down, there[FFL:])[:, None]], axis=1)
        return (yield from ring_gather_steps(both, "y"))

    x_low = layer_input[0]
    frequency = theta ** (-jnp.arange(0, HD, 2).astype(F32) / HD)
    angles = positions[0].astype(F32)[:, None] * frequency
    tables = []
    for table in (jnp.cos(angles), jnp.sin(angles)):
        high = lax.reduce_precision(table, 8, 7)
        tables += [high.astype(BF16), (table - high).astype(BF16)]
    tokens = Flow(gather_steps(jnp.concatenate([x_low, *tables], axis=1)))
    grads = Flow(gather_steps(out_grad[0]))
    qkv_mine, qkv_other = prepare_qkv(place, w_query, w_key, w_value, attn_gain[:, None])
    qkv_mine, qkv_got, gain_two, w_out = stage([tokens], qkv_mine, swap_core(qkv_other), mlp_gain[:, None], w_output)

    columns = Flow(column_steps(qkv_mine, qkv_got))
    o_rows = lax.all_to_all(w_out.reshape(B, 16, B).transpose(1, 0, 2), FSDP, 0, 0, tiled=True)
    ff_mine, ff_other, ff_down = prepare_ff(place, w_gate, w_up, w_down, gain_two)
    ff_mine, ff_got, ff_down, x_low, o_rows = stage(
        [tokens, columns], ff_mine, swap_core(ff_other), ff_down, x_low, o_rows
    )

    inputs = x_low.astype(F32)
    scale_one = lax.rsqrt(jnp.mean(inputs * inputs, axis=-1, keepdims=True) + eps)
    o_rows = o_rows.reshape(D, B)
    mine, other = own_rows(o_rows, y, core, HEADS * HD), own_rows(o_rows, y, 1 - core, HEADS * HD)
    scale_one, mine, other, ff_mine, ff_got, ff_down = stage(
        [tokens, columns, grads], scale_one, mine, other, ff_mine, ff_got, ff_down
    )

    outputs = Flow(output_steps(mine, other))
    ff_mine, ff_got, ff_down = stage([tokens, columns, outputs], ff_mine, ff_got, ff_down)

    hidden_rows = Flow(hidden_steps(ff_mine, ff_got, ff_down))
    x_pieces = tokens.result
    query, key_value, scale_all, cosine, sine, qkv_full = project_qkv(place, x_pieces, columns.result)
    query, key_value = stage([hidden_rows, outputs, grads], query, key_value)

    earlier = lax.ppermute(key_value, "zlo", [(0, 1)])
    query, key_value, earlier = stage([outputs, hidden_rows], query, key_value, earlier)
    ff_all = lax.all_gather(hidden_rows.result, "x", axis=0, tiled=False)

    key_value = jnp.concatenate([earlier, key_value], axis=1)
    mixed, log_total, *parts, o_full = attention(place, outputs.result, query, key_value)
    parts = stage([grads], *parts)
    sums = Flow(scatter_steps(parts))
    stage([sums, grads])
    grad_pieces = grads.result
    for _ in range(3):
        stage([sums])
    hidden = inputs + sums.result
    scale_two = lax.rsqrt(jnp.mean(hidden * hidden, axis=-1, keepdims=True) + eps)
    normed = Flow(gather_steps((hidden * scale_two).astype(BF16)))
    for _ in range(4):
        stage([normed])
    normed_pieces = normed.result

    activation, act_t, gate_t, up_t, *parts, down_full = feed_forward(place, normed_pieces, grad_pieces, ff_all)
    sums = Flow(scatter_steps(parts))
    (act_t,) = stage([sums], act_t)
    down_terms = ff_terms(down_kernel, place, grad_pieces, (act_t,), FFL, "down_terms")
    down_terms, gate_t = stage([sums], down_terms, gate_t)
    down_sum = lax.psum_scatter(down_terms, "x", scatter_dimension=0, tiled=True)[0]
    gate_up_terms = ff_terms(gate_up_kernel, place, normed_pieces, (gate_t, up_t), 2 * FFL, "gate_up_terms")
    (gate_up_terms,) = stage([sums], gate_up_terms)
    gate_up_sum = lax.psum_scatter(gate_up_terms, "x", scatter_dimension=0, tiled=True)[0]
    stage([sums])

    grad_normed_two = sums.result
    mean_two = jnp.mean(grad_normed_two * hidden, axis=-1, keepdims=True)
    grad_hidden = (
        out_grad[0].astype(F32)
        + scale_two * grad_normed_two
        - hidden * (scale_two * scale_two * scale_two) * mean_two
    )
    hidden_grads = Flow(gather_steps(grad_hidden.astype(BF16)))
    (activation,) = stage([hidden_grads], activation)
    down_parts = project(activation, down_full)
    down_parts = stage([hidden_grads], *down_parts)
    result = Flow(scatter_steps(down_parts))
    stage([hidden_grads, result])
    stage([hidden_grads])

    hidden_grad_pieces = hidden_grads.result
    grad_query, grad_earlier, grad_own = attention_back(
        place, hidden_grad_pieces, query, key_value, log_total, o_full
    )
    grad_query, grad_earlier, grad_own, mixed = stage([result], grad_query, grad_earlier, grad_own, mixed)
    later = lax.ppermute(grad_earlier, "zlo", [(1, 0)])
    output_terms = attention_terms(place, hidden_grad_pieces, mixed.reshape(2 * HALF, HEADS * HD), "output_terms")
    later, grad_query, output_terms, down_sum, gate_up_sum = stage(
        [result], later, grad_query, output_terms, down_sum, gate_up_sum
    )
    output_sum = lax.psum_scatter(output_terms, "x", scatter_dimension=0, tiled=True)[0]
    ff_sums = Flow(ff_steps(jnp.concatenate([gate_up_sum, down_sum], axis=1)))
    *parts, grad_t = qkv_back(grad_query, grad_own, later, cosine, sine, scale_all, qkv_full)
    *parts, grad_t = stage([ff_sums, result], *parts, grad_t)

    sums = Flow(scatter_steps(parts))
    terms = attention_terms(place, x_pieces, grad_t, "qkv_terms")
    terms, output_sum = stage([sums, ff_sums], terms, output_sum)
    attention_sum = lax.psum_scatter(terms, "x", scatter_dimension=0, tiled=True)[0]
    output_sums = Flow(attention_steps(output_sum))
    stage([sums, ff_sums, output_sums])
    (attention_sum,) = stage([sums, output_sums], attention_sum)
    attention_sums = Flow(attention_steps(attention_sum))
    stage([sums, attention_sums, ff_sums, output_sums])
    grad_normed = sums.result
    mean_one = jnp.mean(grad_normed * inputs, axis=-1, keepdims=True)
    input_grad = (
        grad_hidden
        + scale_one * grad_normed
        - inputs * (scale_one * scale_one * scale_one) * mean_one
    )
    input_grad = input_grad.astype(BF16)
    stage([attention_sums, output_sums, ff_sums])

    ring = jnp.roll(jnp.stack(whole_ring(output_sums.result)), y, axis=0).reshape(16, B, B)
    output_grad = lax.all_to_all(ring, FSDP, 0, 0, tiled=True)
    gain_two = mlp_gain[:, None]
    pieces = ff_sums.result
    gate_grad, gate_gain = finish_hidden(place, pieces, 0, w_gate, gain_two)
    up_grad, up_gain = finish_hidden(place, pieces, 1, w_up, gain_two)
    down_grad = finish_down(place, pieces)
    gate_grad, up_grad, down_grad = stage([attention_sums], gate_grad, up_grad, down_grad)
    stage([attention_sums])

    query_grad, key_grad, value_grad, attn_gain_grad = finish_attention(
        place, whole_ring(attention_sums.result), w_query, w_key, w_value, attn_gain[:, None]
    )
    output_grad = finish_output(output_grad)
    return (
        (hidden + result.result).astype(BF16)[None],
        input_grad[None],
        attn_gain_grad[:, 0],
        query_grad,
        key_grad,
        value_grad,
        output_grad,
        (gate_gain + up_gain)[:, 0],
        gate_grad,
        up_grad,
        down_grad,
    )


def solution(mesh):
    split = Mesh(mesh.devices.reshape(2, 4, 2, 4, 2), AXES)
    tokens = P(FSDP, SEQ, None)
    rows = P(FSDP, None)
    gain = P(FSDP)
    in_specs = (
        tokens, P(FSDP, SEQ), gain, rows, rows, rows, rows, gain, rows, rows, rows, tokens,
    )
    out_specs = (tokens, tokens, gain, rows, rows, rows, rows, gain, rows, rows, rows)
    return jax.shard_map(
        on_device, mesh=split, in_specs=in_specs, out_specs=out_specs, check_vma=False
    )
```

```python
import jax
import jax.numpy as jnp
from jax import lax
from jax.experimental import pallas as pl
from jax.experimental.pallas import tpu as pltpu
from jax.sharding import Mesh
from jax.sharding import PartitionSpec as P

H = 32
KV = 4
HD = 64
D = 2048
FF = 5632
B = 128
HALF = 512
HEADS = 4
FFL = 704
PIECE = 88

eps = 1e-05
theta = 10000.0
F32 = jnp.float32
BF16 = jnp.bfloat16
AXES = ("zlo", "y", "zhi", "x", "core")
FSDP = ("zhi", "x", "core")
SEQ = ("zlo", "y")


def matmul(left, right):
    return jnp.dot(left, right, preferred_element_type=F32)


def times_transposed(left, right):
    return lax.dot_general(left, right, (((1,), (1,)), ((), ())), preferred_element_type=F32)


def outer_sum(left, right):
    return lax.dot_general(left, right, (((0,), (0,)), ((), ())), preferred_element_type=F32)


def shift(value, axis, by):
    if axis == "z":
        at = [2 * (z % 2) + z // 2 for z in range(4)]
        return lax.ppermute(value, ("zlo", "zhi"), [(at[z], at[(z + by) % 4]) for z in range(4)])
    size = lax.axis_size(axis)
    return lax.ppermute(value, axis, [(i, (i + by) % size) for i in range(size)])


def swap_core(value):
    return shift(value, "core", 1)


def small_gather(block, axis):
    return shift(block, axis, -1), shift(block, axis, 2), shift(block, axis, 1)


def tie(*values):
    return lax.optimization_barrier(values)


def add(left, right):
    return left.astype(F32) + right.astype(F32)


def along_y(value):
    pairs = []
    for i in range(4):
        pairs.append((2 * i, 2 * ((i + 1) % 4)))
        pairs.append((2 * i + 1, 2 * ((i + 3) % 4) + 1))
    return lax.ppermute(value, ("y", "core"), pairs)


def send_half(got):
    core = lax.axis_index("core")
    return lax.dynamic_slice_in_dim(got, core * (B // 2), B // 2, 1)


FLIPPED = (0, 0, 1, 0, 1)
LENGTHS = (B, B, B, B // 2, B // 2)


def put_tokens(refs, rows_ref, sems, start):
    lanes = pl.ds(0, rows_ref.shape[1])
    copies = []
    row = 0
    for s in range(2):
        for ref, flip, length in zip(refs, FLIPPED, LENGTHS):
            copies.append(
                pltpu.make_async_copy(
                    ref.at[s ^ flip, :, lanes], rows_ref.at[pl.ds(row, length)], sems.at[start + len(copies)]
                )
            )
            row += length
    return copies


TILE = 256
WIDE = D + B
VMEM_LIMIT = 56 * 2**20
ANYWHERE = pl.BlockSpec(memory_space=pl.ANY)


def params(*kinds):
    return pltpu.CompilerParams(dimension_semantics=kinds or None, vmem_limit_bytes=VMEM_LIMIT)


def cost(flops, megabytes):
    return pl.CostEstimate(flops=flops, bytes_accessed=int(megabytes * 2**20), transcendentals=0)


def shaped(*shape, kind=BF16):
    return jax.ShapeDtypeStruct(shape, kind)


PART_SPECS = [pl.BlockSpec((1, n, D), lambda i, *_: (i // 2, 0, 0)) for n in LENGTHS]
PART_SHAPES = [jax.ShapeDtypeStruct((2, n, D), BF16) for n in LENGTHS]


def put_parts(step, tile, refs):
    @pl.when(step % 2 == 0)
    def _():
        refs[0][0] = tile[:B]
        refs[1][0] = tile[B:]

    @pl.when(step % 2 == 1)
    def _():
        refs[2][0] = tile[:B]
        refs[3][0] = tile[B : B + B // 2]
        refs[4][0] = tile[B + B // 2 :]


def turned(values):
    lane = lax.broadcasted_iota(jnp.int32, values.shape, 1) % HD
    return jnp.where(lane < HD // 2, -pltpu.roll(values, 2 * HD - HD // 2, 1), pltpu.roll(values, HD // 2, 1))


def lane_block(zhi, x, core):
    return pl.ds(pl.multiple_of((zhi * 8 + x * 2 + core) * B, B), B)


def put_columns(place, refs, into, sems, start):
    copies = []
    for ref, by, first in zip(refs, (0, 1, 2, 2, 3), (0, 0, 0, 1, 0)):
        for i in range(ref.shape[0]):
            for core in range(2):
                lanes = lane_block(first + i, (place[3] + by) % 4, core)
                copies.append(
                    pltpu.make_async_copy(ref.at[i, core], into.at[:, lanes], sems.at[start + len(copies)])
                )
    return copies


def prepare_qkv_kernel(place, q_mine, q_other, w_key, w_value, gain, mine_ref, other_ref, k_rows, v_rows):
    scale = gain[...]
    k_rows[...] = (w_key[...].astype(F32) * scale).T
    v_rows[...] = (w_value[...].astype(F32) * scale).T
    rows = pl.ds(pl.multiple_of(place[1] * HD, HD), HD)
    for source, out in ((q_mine, mine_ref), (q_other, other_ref)):
        out[: HEADS * HD] = (source[...].astype(F32) * scale).T.astype(BF16)
        out[HEADS * HD : (HEADS + 1) * HD] = k_rows[rows].astype(BF16)
        out[(HEADS + 1) * HD :] = v_rows[rows].astype(BF16)


QKV = (HEADS + 2) * HD


def prepare_qkv(place, w_query, w_key, w_value, gain):
    whole = lambda *shape: pl.BlockSpec(shape, lambda i, p: (0,) * len(shape))
    return pl.pallas_call(
        prepare_qkv_kernel,
        grid_spec=pltpu.PrefetchScalarGridSpec(
            num_scalar_prefetch=1,
            grid=(1,),
            in_specs=[
                pl.BlockSpec((B, HEADS * HD), lambda i, p: (0, 2 * p[1] + p[2])),
                pl.BlockSpec((B, HEADS * HD), lambda i, p: (0, 2 * p[1] + 1 - p[2])),
                whole(B, KV * HD), whole(B, KV * HD), whole(B, 1),
            ],
            out_specs=[whole(QKV, B), whole(QKV, B)],
            scratch_shapes=[pltpu.VMEM((KV * HD, B), F32), pltpu.VMEM((KV * HD, B), F32)],
        ),
        out_shape=[shaped(QKV, B), shaped(QKV, B)],
        compiler_params=params("arbitrary"),
        cost_estimate=cost(0, 1),
        name="prepare_qkv",
    )(place, w_query, w_query, w_key, w_value, gain)


def prepare_ff_kernel(place, w_gate, w_up, w_down, gain, mine_ref, other_ref, down_ref, picked, rows, down_rows, sems):
    zlo, y, core = place[0], place[1], place[2]
    down = pltpu.make_async_copy(
        w_down.at[:, pl.ds(pl.multiple_of(zlo * (D // 2), D // 2), D // 2)], down_rows, sems.at[1]
    )
    down.start()

    @pl.when(zlo == 0)
    def _():
        copy = pltpu.make_async_copy(w_gate, picked, sems.at[0])
        copy.start()
        copy.wait()

    @pl.when(zlo == 1)
    def _():
        copy = pltpu.make_async_copy(w_up, picked, sems.at[0])
        copy.start()
        copy.wait()

    scale = gain[...]
    for i in range(FF // B):
        rows[i * B : (i + 1) * B] = (picked[:, i * B : (i + 1) * B].astype(F32) * scale).T
    for which, out in ((core, mine_ref), (1 - core, other_ref)):
        slabs = []
        for zx in range(8):
            at = pl.multiple_of(zx * 2 * 4 * PIECE + which * 4 * PIECE + y * PIECE, 8)
            slabs.append(rows[pl.ds(at, PIECE)])
        out[...] = jnp.concatenate(slabs, axis=0).astype(BF16)
    down.wait()
    for t in range(8):
        rows[t * 4 * PIECE : (t + 1) * 4 * PIECE] = down_rows[:, t * B : (t + 1) * B].astype(F32)
    slabs = [rows[pl.ds(pl.multiple_of(t * 4 * PIECE + y * PIECE, 8), PIECE)] for t in range(8)]
    down_ref[...] = jnp.concatenate(slabs, axis=0).astype(BF16)


def prepare_ff(place, w_gate, w_up, w_down, gain):
    return pl.pallas_call(
        prepare_ff_kernel,
        grid_spec=pltpu.PrefetchScalarGridSpec(
            num_scalar_prefetch=1,
            grid=(1,),
            in_specs=[ANYWHERE, ANYWHERE, ANYWHERE, pl.BlockSpec((B, 1), lambda i, p: (0, 0))],
            out_specs=[pl.BlockSpec((FFL, B), lambda i, p: (0, 0))] * 3,
            scratch_shapes=[
                pltpu.VMEM((B, FF), BF16),
                pltpu.VMEM((FF, B), F32),
                pltpu.VMEM((4 * PIECE, D // 2), BF16),
                pltpu.SemaphoreType.DMA((2,)),
            ],
        ),
        out_shape=[shaped(FFL, B)] * 3,
        compiler_params=params("arbitrary"),
        cost_estimate=cost(0, 6),
        name="prepare_ff",
    )(place, w_gate, w_up, w_down, gain)


def project_qkv_kernel(*refs):
    place, x_refs, w_refs = refs[0], refs[1:6], refs[6:11]
    query_ref, kv_ref, scale_ref, cosine_ref, sine_ref, w_out, rows, weights, sems = refs[11:]
    step = pl.program_id(0)
    tokens = put_tokens(x_refs, rows, sems, 0)
    columns = put_columns(place, w_refs, weights, sems, 10)
    back = pltpu.make_async_copy(weights, w_out, sems.at[26])

    @pl.when(step == 0)
    def _():
        for copy in columns + tokens:
            copy.start()
        for copy in columns:
            copy.wait()
        back.start()
        for copy in tokens:
            copy.wait()

    at = pl.ds(pl.multiple_of(step * TILE, TILE), TILE)
    tile = rows[at, :D]
    wide = tile.astype(F32)
    scale = lax.rsqrt(jnp.mean(wide * wide, axis=-1, keepdims=True) + eps)
    scale_ref[...] = scale
    pre = times_transposed(tile, weights[...]) * scale
    tables = rows[at, D:].astype(F32)
    tables = tables + pltpu.roll(tables, B - HD // 2, 1)
    cosine = jnp.concatenate([tables[:, : HD // 2]] * 4, axis=1)
    sine = jnp.concatenate([tables[:, HD : HD + HD // 2]] * 4, axis=1)
    cosine_ref[...] = cosine
    sine_ref[...] = sine
    for i in range(2):
        part = pre[:, i * 2 * HD : (i + 1) * 2 * HD]
        part = (part * cosine + turned(part) * sine).astype(BF16) * HD ** (-0.5)
        query_ref[0, 2 * i] = part[:, :HD]
        query_ref[0, 2 * i + 1] = part[:, HD:]
    part = pre[:, HEADS * HD :]
    lane = lax.broadcasted_iota(jnp.int32, part.shape, 1)
    kv_ref[0] = jnp.where(lane < HD, part * cosine + turned(part) * sine, part).astype(BF16)

    @pl.when(step == 3)
    def _():
        back.wait()


def project_qkv(place, x_pieces, w_pieces):
    tile = lambda lanes: pl.BlockSpec((TILE, lanes), lambda i, p: (i, 0))
    return pl.pallas_call(
        project_qkv_kernel,
        grid_spec=pltpu.PrefetchScalarGridSpec(
            num_scalar_prefetch=1,
            grid=(4,),
            in_specs=[ANYWHERE] * 10,
            out_specs=[
                pl.BlockSpec((1, HEADS, TILE, HD), lambda i, p: (i // 2, 0, i % 2, 0)),
                pl.BlockSpec((1, TILE, 2 * HD), lambda i, p: (i // 2, i % 2, 0)),
                tile(1), tile(2 * HD), tile(2 * HD),
                ANYWHERE,
            ],
            scratch_shapes=[
                pltpu.VMEM((2 * HALF, WIDE), BF16),
                pltpu.VMEM((QKV, D), BF16),
                pltpu.SemaphoreType.DMA((27,)),
            ],
        ),
        out_shape=[
            shaped(2, HEADS, HALF, HD), shaped(2, HALF, 2 * HD), shaped(2 * HALF, 1, kind=F32),
            shaped(2 * HALF, 2 * HD, kind=F32), shaped(2 * HALF, 2 * HD, kind=F32), shaped(QKV, D),
        ],
        compiler_params=params("arbitrary"),
        cost_estimate=cost(2 * 2 * HALF * QKV * D, 8),
        name="project_qkv",
    )(place, *x_pieces, *w_pieces)


def project_kernel(left_ref, weight_ref, *parts):
    put_parts(pl.program_id(0), matmul(left_ref[...], weight_ref[...]).astype(BF16), parts)


def project(left, weight):
    depth = left.shape[1]
    return pl.pallas_call(
        project_kernel,
        grid=(4,),
        in_specs=[pl.BlockSpec((TILE, depth), lambda i: (i, 0)), pl.BlockSpec((depth, D), lambda i: (0, 0))],
        out_specs=PART_SPECS,
        out_shape=PART_SHAPES,
        compiler_params=params("arbitrary"),
        cost_estimate=cost(2 * 2 * HALF * depth * D, 8),
        name="project",
    )(left, weight)


def put_term(left, rows, term_ref):
    def one(i, carry):
        term = matmul(left, rows[:, pl.ds(pl.multiple_of(i * 4 * B, 4 * B), 4 * B)]).astype(BF16)
        for j in range(2):
            zx = 2 * i + j
            term_ref[zx % 4, zx // 4, 0] = term[:, 2 * j * B : (2 * j + 1) * B]
            term_ref[zx % 4, zx // 4, 1] = term[:, (2 * j + 1) * B : (2 * j + 2) * B]
        return carry

    lax.fori_loop(0, 4, one, 0)


def qkv_back_kernel(grad_q_ref, own_ref, later_ref, cosine_ref, sine_ref, scale_ref, weight_ref, *outs):
    parts, turned_ref = outs[:5], outs[5]
    cosine, sine = cosine_ref[...], sine_ref[...]
    lane = lax.broadcasted_iota(jnp.int32, cosine.shape, 1)
    pieces = []
    for i in range(2):
        part = grad_q_ref[0, :, i * 2 * HD : (i + 1) * 2 * HD]
        pieces.append(part * cosine - turned(part * sine))
    part = own_ref[0] + later_ref[0].astype(F32)
    pieces.append(jnp.where(lane < HD, part * cosine - turned(part * sine), part))
    grad_pre = jnp.concatenate(pieces, axis=1)
    put_parts(pl.program_id(0), matmul(grad_pre.astype(BF16), weight_ref[...]).astype(BF16), parts)
    turned_ref[...] = (grad_pre * scale_ref[...]).T.astype(BF16)


def qkv_back(grad_query, own, later, cosine, sine, scale, weight):
    tile = lambda lanes: pl.BlockSpec((TILE, lanes), lambda i: (i, 0))
    half = lambda lanes: pl.BlockSpec((1, TILE, lanes), lambda i: (i // 2, i % 2, 0))
    return pl.pallas_call(
        qkv_back_kernel,
        grid=(4,),
        in_specs=[
            half(HEADS * HD), half(2 * HD), half(2 * HD), tile(2 * HD), tile(2 * HD), tile(1),
            pl.BlockSpec((QKV, D), lambda i: (0, 0)),
        ],
        out_specs=PART_SPECS + [pl.BlockSpec((QKV, TILE), lambda i: (0, i))],
        out_shape=PART_SHAPES + [shaped(QKV, 2 * HALF)],
        compiler_params=params("arbitrary"),
        cost_estimate=cost(2 * 2 * HALF * QKV * D, 9),
        name="qkv_back",
    )(grad_query, own, later, cosine, sine, scale, weight)


def attention_term_kernel(*refs):
    token_refs, left_ref = refs[1:6], refs[6]
    term_ref, rows, sems = refs[-3:]
    copies = put_tokens(token_refs, rows, sems, 0)
    for copy in copies:
        copy.start()
    left = left_ref[...]
    if left.shape[0] == 2 * HALF:
        left = left.T
    for copy in copies:
        copy.wait()
    put_term(left, rows, term_ref)


def attention_terms(place, pieces, left, name):
    whole = lambda *shape: pl.BlockSpec(shape, lambda i, p: (0,) * len(shape))
    rows = min(left.shape)
    return pl.pallas_call(
        attention_term_kernel,
        grid_spec=pltpu.PrefetchScalarGridSpec(
            num_scalar_prefetch=1,
            grid=(1,),
            in_specs=[ANYWHERE] * 5 + [whole(*left.shape)],
            out_specs=whole(4, 2, 2, rows, B),
            scratch_shapes=[pltpu.VMEM((2 * HALF, D), BF16), pltpu.SemaphoreType.DMA((10,))],
        ),
        out_shape=shaped(4, 2, 2, rows, B),
        compiler_params=params("arbitrary"),
        cost_estimate=cost(2 * 2 * HALF * rows * D, 7),
        name=name,
    )(place, *pieces, left)


def token_places(at, y, core):
    step = 1 - 2 * core
    block = jnp.where(
        at < B, y, jnp.where(at < 2 * B, y + 4 - step, jnp.where(at < 3 * B, y + 4 + step, y + 2))
    )
    row = at % B
    row = jnp.where(at < 3 * B, row, (row + core * (B // 2)) % B)
    return (block % 4) * B + row


def set_bias(place_ref, bias_ref):
    zlo, y, core = place_ref[0], place_ref[1], place_ref[2]
    key_at = token_places(lax.broadcasted_iota(jnp.int32, (HALF, 1), 0), y, core)
    query_at = token_places(lax.broadcasted_iota(jnp.int32, (1, HALF), 1), y, core)
    bias_ref[:HALF, :] = jnp.broadcast_to(jnp.where(zlo == 1, 0.0, -1e30), (HALF, HALF))
    bias_ref[HALF:, :] = jnp.where(key_at <= query_at, 0.0, -1e30)


def attention_kernel(place_ref, *refs):
    w_refs, query_ref, kv_ref, mixed_ref, log_ref = refs[:5], *refs[5:9]
    parts, w_out, bias_ref, weight, sems = refs[9:14], *refs[14:]
    columns = put_columns(place_ref, w_refs, weight, sems, 0)
    back = pltpu.make_async_copy(weight, w_out, sems.at[16])

    @pl.when(pl.program_id(0) == 0)
    def _():
        for copy in columns:
            copy.start()
        set_bias(place_ref, bias_ref)
        for copy in columns:
            copy.wait()
        back.start()

    key, value = kv_ref[0, :, :HD], kv_ref[0, :, HD:]
    for head in range(HEADS):
        scores = times_transposed(key, query_ref[0, head]) + bias_ref[...]
        top = jnp.max(scores, axis=0, keepdims=True)
        weights = jnp.exp(scores - top)
        total = jnp.sum(weights, axis=0, keepdims=True)
        low = (weights * (1.0 / total)).astype(BF16)
        mixed_ref[0, :, head * HD : (head + 1) * HD] = outer_sum(value, low).T.astype(BF16)
        log_ref[0, head] = top + jnp.log(total)
    put_rows(parts, matmul(mixed_ref[0], weight[...]).astype(BF16))

    @pl.when(pl.program_id(0) == 1)
    def _():
        back.wait()


def put_rows(parts, rows):
    row = 0
    for ref, length in zip(parts, LENGTHS):
        ref[0] = rows[row : row + length]
        row += length


def attention_back_kernel(place_ref, *refs):
    grad_refs, query_ref, kv_ref, log_ref, weight_ref = refs[:5], *refs[5:9]
    grad_query_ref, earlier_ref, own_ref, bias_ref, rows, sems = refs[9:]
    step = pl.program_id(0)
    copies = put_tokens(grad_refs, rows, sems, 0)

    @pl.when(step == 0)
    def _():
        for copy in copies:
            copy.start()
        set_bias(place_ref, bias_ref)
        for copy in copies:
            copy.wait()

    hidden = rows[pl.ds(pl.multiple_of(step * HALF, HALF), HALF), :]
    grads = times_transposed(hidden, weight_ref[...]).astype(BF16)
    key, value = kv_ref[0, :, :HD], kv_ref[0, :, HD:]
    grad_key = jnp.zeros((2 * HALF, HD), F32)
    grad_value = jnp.zeros((2 * HALF, HD), F32)
    for head in range(HEADS):
        lanes = slice(head * HD, (head + 1) * HD)
        query, grad = query_ref[0, head], grads[:, lanes]
        weights = jnp.exp(times_transposed(key, query) + bias_ref[...] - log_ref[0, head])
        grad_weights = times_transposed(value, grad)
        delta = jnp.sum(weights * grad_weights, axis=0, keepdims=True)
        grad_scores = (weights * (grad_weights - delta)).astype(BF16)
        grad_query_ref[0, :, lanes] = outer_sum(key, grad_scores).T * HD ** (-0.5)
        grad_key += matmul(grad_scores, query)
        grad_value += matmul(weights.astype(BF16), grad)
    total = jnp.concatenate([grad_key, grad_value], axis=1)
    earlier_ref[0] = total[:HALF].astype(BF16)
    own_ref[0] = total[HALF:]


def sequence_block(*tail):
    return pl.BlockSpec((1,) + tail, lambda s, place: (s,) + (0,) * len(tail))


def attention_call(kernel, in_specs, out_specs, out_shape, scratch, flops, name):
    return pl.pallas_call(
        kernel,
        grid_spec=pltpu.PrefetchScalarGridSpec(
            num_scalar_prefetch=1,
            grid=(2,),
            in_specs=in_specs,
            out_specs=out_specs,
            scratch_shapes=[pltpu.VMEM((2 * HALF, HALF), F32)] + scratch,
        ),
        out_shape=out_shape,
        compiler_params=params("arbitrary"),
        cost_estimate=cost(flops * 8 * 2 * HALF * HALF * HD * 2, 8),
        name=name,
    )


def attention(place, w_pieces, query, kv):
    return attention_call(
        attention_kernel,
        [ANYWHERE] * 5 + [sequence_block(HEADS, HALF, HD), sequence_block(2 * HALF, 2 * HD)],
        [sequence_block(HALF, HEADS * HD), sequence_block(HEADS, 1, HALF)]
        + [sequence_block(n, D) for n in LENGTHS]
        + [ANYWHERE],
        [shaped(2, HALF, HEADS * HD), shaped(2, HEADS, 1, HALF, kind=F32)] + PART_SHAPES + [shaped(HEADS * HD, D)],
        [pltpu.VMEM((HEADS * HD, D), BF16), pltpu.SemaphoreType.DMA((17,))],
        3,
        "attention",
    )(place, *w_pieces, query, kv)


def attention_back(place, grad_pieces, query, kv, log_total, weight):
    return attention_call(
        attention_back_kernel,
        [ANYWHERE] * 5
        + [
            sequence_block(HEADS, HALF, HD), sequence_block(2 * HALF, 2 * HD),
            sequence_block(HEADS, 1, HALF), pl.BlockSpec((HEADS * HD, D), lambda s, place: (0, 0)),
        ],
        [sequence_block(HALF, HEADS * HD), sequence_block(HALF, 2 * HD), sequence_block(HALF, 2 * HD)],
        [
            shaped(2, HALF, HEADS * HD, kind=F32),
            shaped(2, HALF, 2 * HD),
            shaped(2, HALF, 2 * HD, kind=F32),
        ],
        [pltpu.VMEM((2 * HALF, D), BF16), pltpu.SemaphoreType.DMA((10,))],
        6,
        "attention_back",
    )(place, *grad_pieces, query, kv, log_total, weight)


def finish_attention_kernel(place, *refs):
    piece_refs, w_query, w_key, w_value, gain_ref = refs[:4], *refs[4:8]
    query_out, key_out, value_out, gain_out, rows = refs[8:]
    for ref, by in zip(piece_refs, range(4)):
        at_y = (place[1] + by) % 4
        for c in range(2):
            piece = ref[c].astype(F32)
            rows[pl.ds(pl.multiple_of((2 * at_y + c) * HEADS * HD, HEADS * HD), HEADS * HD)] = piece[: HEADS * HD]
        both = ref[0].astype(F32) + ref[1].astype(F32)
        at = pl.multiple_of(H * HD + at_y * HD, HD)
        rows[pl.ds(at, HD)] = both[HEADS * HD : (HEADS + 1) * HD]
        rows[pl.ds(at + KV * HD, HD)] = both[(HEADS + 1) * HD :]
    gain = gain_ref[...]
    total = jnp.zeros((B, 1), F32)
    row = 0
    for weight, out in ((w_query, query_out), (w_key, key_out), (w_value, value_out)):
        for i in range(out.shape[1] // B):
            lanes = slice(i * B, (i + 1) * B)
            block = rows[row : row + B].T
            total = total + jnp.sum(block * weight[:, lanes].astype(F32), axis=1, keepdims=True)
            out[:, lanes] = block * gain
            row += B
    gain_out[...] = total


def finish_attention(place, pieces, w_query, w_key, w_value, gain):
    whole = lambda *shape: pl.BlockSpec(shape, lambda i, p: (0,) * len(shape))
    kv = KV * HD
    return pl.pallas_call(
        finish_attention_kernel,
        grid_spec=pltpu.PrefetchScalarGridSpec(
            num_scalar_prefetch=1,
            grid=(1,),
            in_specs=[whole(2, QKV, B)] * 4 + [whole(B, D), whole(B, kv), whole(B, kv), whole(B, 1)],
            out_specs=[whole(B, D), whole(B, kv), whole(B, kv), whole(B, 1)],
            scratch_shapes=[pltpu.VMEM((D + 2 * kv, B), F32)],
        ),
        out_shape=[
            shaped(B, D, kind=F32), shaped(B, kv, kind=F32), shaped(B, kv, kind=F32), shaped(B, 1, kind=F32),
        ],
        compiler_params=params("arbitrary"),
        cost_estimate=cost(0, 4),
        name="finish_attention",
    )(place, *pieces, w_query, w_key, w_value, gain)


def finish_output_kernel(blocks, out):
    for i in range(16):
        out[:, i * B : (i + 1) * B] = blocks[i].astype(F32)


def finish_output(blocks):
    return pl.pallas_call(
        finish_output_kernel,
        out_shape=shaped(B, D, kind=F32),
        compiler_params=params(),
        cost_estimate=cost(0, 2),
        name="finish_output",
    )(blocks)


def feed_forward_kernel(*refs):
    place, token_refs, grad_refs, ff_refs = refs[0], refs[1:6], refs[6:11], refs[11:16]
    act_ref, act_t, gate_t, up_t = refs[16:20]
    parts, down_out = refs[20:25], refs[25]
    rows_h, rows_g, gate_up, down, slabs, sems = refs[26:]
    step = pl.program_id(0)
    tokens = put_tokens(token_refs, rows_h, sems, 0)
    grads = put_tokens(grad_refs, rows_g, sems, 10)
    weights, loads = [], []
    for x in range(4):
        own, after, low, high, before = ff_refs
        far = low.at[x] if x < 2 else high.at[x - 2]
        for by, piece in enumerate((own.at[x], after.at[x], far, before.at[x])):
            z = (2 * place[4] + place[0] + by) % 4
            zhi, zlo = z // 2, z % 2
            for core in range(2):
                weights.append(
                    pltpu.make_async_copy(
                        piece.at[pl.ds(core * FFL, FFL)],
                        gate_up.at[zlo, :, lane_block(zhi, x, core)],
                        sems.at[20 + len(weights)],
                    )
                )
            loads.append(
                pltpu.make_async_copy(
                    piece.at[pl.ds(2 * FFL, FFL)], slabs.at[zlo, zhi * 4 + x], sems.at[52 + len(loads)]
                )
            )
    back = pltpu.make_async_copy(down, down_out, sems.at[68])

    @pl.when(step == 0)
    def _():
        for copy in tokens + weights + loads + grads:
            copy.start()
        for copy in tokens + weights:
            copy.wait()

    rows = pl.ds(pl.multiple_of(step * HALF, HALF), HALF)
    normed = rows_h[rows, :]
    gate_pre = times_transposed(normed, gate_up[0])
    upward = times_transposed(normed, gate_up[1])

    @pl.when(step == 0)
    def _():
        for copy in loads:
            copy.wait()

        def put(q, carry):
            for half in range(2):
                for p in range(4):
                    one = slabs[half, 2 * q, 2 * p * PIECE : 2 * (p + 1) * PIECE, :].astype(F32)
                    two = slabs[half, 2 * q + 1, 2 * p * PIECE : 2 * (p + 1) * PIECE, :].astype(F32)
                    lane = (half * 8 + 2 * p) * B
                    rows = pl.ds(pl.multiple_of(q * 2 * PIECE, 16), 2 * PIECE)
                    down[rows, lane : lane + B] = jnp.concatenate([one[:PIECE], two[:PIECE]], axis=0).astype(BF16)
                    down[rows, lane + B : lane + 2 * B] = jnp.concatenate(
                        [one[PIECE:], two[PIECE:]], axis=0
                    ).astype(BF16)
            return carry

        lax.fori_loop(0, 4, put, 0)
        back.start()
        for copy in grads:
            copy.wait()

    grad_act = times_transposed(rows_g[rows, :], down[...])
    sigmoid = 1.0 / (1.0 + jnp.exp(-gate_pre))
    silu = gate_pre * sigmoid
    activation = silu * upward
    grad_up = grad_act * silu
    grad_gate = grad_act * upward * (sigmoid * (1.0 + gate_pre * (1.0 - sigmoid)))
    part = matmul(grad_gate.astype(BF16), gate_up[0]) + matmul(grad_up.astype(BF16), gate_up[1])
    part = part.astype(BF16)
    row = 0
    for ref, length in zip(parts, LENGTHS):
        ref[0] = part[row : row + length]
        row += length
    act_ref[...] = activation.astype(BF16)
    act_t[...] = activation.T.astype(BF16)
    gate_t[...] = grad_gate.T.astype(BF16)
    up_t[...] = grad_up.T.astype(BF16)

    @pl.when(step == 1)
    def _():
        back.wait()


def feed_forward(place, tokens, grads, ff_pieces):
    turned_spec = pl.BlockSpec((FFL, HALF), lambda i, p: (0, i))
    turned_shape = shaped(FFL, 2 * HALF)
    return pl.pallas_call(
        feed_forward_kernel,
        grid_spec=pltpu.PrefetchScalarGridSpec(
            num_scalar_prefetch=1,
            grid=(2,),
            in_specs=[ANYWHERE] * 15,
            out_specs=[pl.BlockSpec((HALF, FFL), lambda i, p: (i, 0))]
            + [turned_spec] * 3
            + [pl.BlockSpec((1, n, D), lambda i, p: (i, 0, 0)) for n in LENGTHS]
            + [ANYWHERE],
            scratch_shapes=[
                pltpu.VMEM((2 * HALF, D), BF16),
                pltpu.VMEM((2 * HALF, D), BF16),
                pltpu.VMEM((2, FFL, D), BF16),
                pltpu.VMEM((FFL, D), BF16),
                pltpu.VMEM((2, 8, FFL, B), BF16),
                pltpu.SemaphoreType.DMA((69,)),
            ],
        ),
        out_shape=[shaped(2 * HALF, FFL)] + [turned_shape] * 3 + PART_SHAPES + [shaped(FFL, D)],
        compiler_params=params("arbitrary"),
        cost_estimate=cost(2 * 5 * 2 * HALF * FFL * D, 32),
        name="feed_forward",
    )(place, *tokens, *grads, *ff_pieces)


def along_z(place, zhi, zlo):
    return (2 * zhi + zlo + 4 - 2 * place[4] - place[0]) % 4


def load_tokens(step, refs, rows, sems):
    copies = put_tokens(refs, rows, sems, 0)

    @pl.when(step == 0)
    def _():
        for copy in copies:
            copy.start()
        for copy in copies:
            copy.wait()


def gate_up_kernel(*refs):
    place, token_refs, gate_t, up_t, out_ref, rows, terms, sems = refs[0], refs[1:6], *refs[6:]
    step = pl.program_id(0)
    load_tokens(step, token_refs, rows, sems)
    normed = rows[:, pl.ds(pl.multiple_of(step * 4 * B, 4 * B), 4 * B)]

    def out(i, matrix):
        xs, by = pl.ds(i % 2 * 2, 2), along_z(place, i // 2, matrix)
        return pltpu.make_async_copy(terms.at[xs, by], out_ref.at[xs, by], sems.at[10 + 2 * i + matrix])

    for matrix, left in ((0, gate_t), (1, up_t)):
        term = matmul(left[...], normed).astype(BF16)
        by = along_z(place, step // 2, matrix)
        for j in range(2):
            terms[step % 2 * 2 + j, by, 0:FFL, :] = term[:, 2 * j * B : (2 * j + 1) * B]
            terms[step % 2 * 2 + j, by, FFL:, :] = term[:, (2 * j + 1) * B : (2 * j + 2) * B]
        out(step, matrix).start()

    @pl.when(step == 3)
    def _():
        for i in range(4):
            for matrix in range(2):
                out(i, matrix).wait()


def down_kernel(*refs):
    place, grad_refs, act_t, out_ref, rows, terms, sems = refs[0], refs[1:6], *refs[6:]
    step = pl.program_id(0)
    load_tokens(step, grad_refs, rows, sems)
    term = matmul(act_t[...], rows[:, pl.ds(pl.multiple_of(step * 4 * B, 4 * B), 4 * B)])
    for j in range(2):
        p = (2 * step + j) % 4
        at = pl.ds(pl.multiple_of(p * 2 * PIECE, 16), 2 * PIECE)
        for zx in range(8):
            slab = term[zx * PIECE : (zx + 1) * PIECE]
            low, high = slab[:, 2 * j * B : (2 * j + 1) * B], slab[:, (2 * j + 1) * B : (2 * j + 2) * B]
            by = along_z(place, zx // 4, step // 2)
            terms[zx % 4, by, at, :] = jnp.concatenate([low, high], axis=0).astype(BF16)

    def out(half, zhi):
        by = along_z(place, zhi, half)
        return pltpu.make_async_copy(terms.at[:, by], out_ref.at[:, by], sems.at[10 + 2 * half + zhi])

    @pl.when(step % 2 == 1)
    def _():
        for zhi in range(2):
            out(step // 2, zhi).start()

    @pl.when(step == 3)
    def _():
        for half in range(2):
            for zhi in range(2):
                out(half, zhi).wait()


def ff_terms(kernel, place, pieces, lefts, rows, name):
    whole = pl.BlockSpec((FFL, 2 * HALF), lambda i, p: (0, 0))
    return pl.pallas_call(
        kernel,
        grid_spec=pltpu.PrefetchScalarGridSpec(
            num_scalar_prefetch=1,
            grid=(4,),
            in_specs=[ANYWHERE] * 5 + [whole] * len(lefts),
            out_specs=ANYWHERE,
            scratch_shapes=[
                pltpu.VMEM((2 * HALF, D), BF16),
                pltpu.VMEM((4, 4, rows, B), BF16),
                pltpu.SemaphoreType.DMA((18,)),
            ],
        ),
        out_shape=shaped(4, 4, rows, B),
        compiler_params=params("arbitrary"),
        cost_estimate=cost(2 * len(lefts) * 2 * HALF * FFL * D, 8 + 4 * len(lefts)),
        name=name,
    )(place, *pieces, *lefts)


def finish_hidden_kernel(*refs):
    place, piece_refs, weight_ref, gain_ref, out_ref, gain_out, rows = refs[0], refs[1:5], *refs[5:]
    for ref, by in zip(piece_refs, range(4)):
        at_y = (place[1] + by) % 4
        for core in range(2):
            slab = ref[0, core].astype(F32)
            for zx in range(8):
                at = pl.multiple_of((2 * zx + core) * 4 * PIECE + at_y * PIECE, 8)
                rows[pl.ds(at, PIECE)] = slab[zx * PIECE : (zx + 1) * PIECE]
    gain = gain_ref[...]
    total = jnp.zeros((B, 1), F32)
    for i in range(FF // B):
        lanes = slice(i * B, (i + 1) * B)
        block = rows[lanes].T
        total = total + jnp.sum(block * weight_ref[:, lanes].astype(F32), axis=1, keepdims=True)
        out_ref[:, lanes] = block * gain
    gain_out[...] = total


def finish_hidden(place, pieces, matrix, weight, gain):
    own, after, low, high, before = pieces
    at = lambda m: pl.BlockSpec((1, 2, FFL, B), lambda i, p: (m, 0, 0, 0))
    whole = lambda *shape: pl.BlockSpec(shape, lambda i, p: (0,) * len(shape))
    return pl.pallas_call(
        finish_hidden_kernel,
        grid_spec=pltpu.PrefetchScalarGridSpec(
            num_scalar_prefetch=1,
            grid=(1,),
            in_specs=[at(matrix), at(matrix), at(0), at(matrix), whole(B, FF), whole(B, 1)],
            out_specs=[whole(B, FF), whole(B, 1)],
            scratch_shapes=[pltpu.VMEM((FF, B), F32)],
        ),
        out_shape=[shaped(B, FF, kind=F32), shaped(B, 1, kind=F32)],
        compiler_params=params("arbitrary"),
        cost_estimate=cost(0, 6),
        name="finish_hidden",
    )(place, own, after, (low, high)[matrix], before, weight, gain)


def finish_down_kernel(place, own, after, low, high, before, out_ref):
    for refs, by in (((own, own), 0), ((after, after), 1), ((low, high), 2), ((before, before), 3)):
        rows = pl.ds(pl.multiple_of((place[1] + by) % 4 * PIECE, 8), PIECE)
        for half in range(2):
            slab = refs[half][half if by != 2 else 0, 0].astype(F32)
            for t in range(8):
                lane = (half * 8 + t) * B
                out_ref[rows, lane : lane + B] = slab[t * PIECE : (t + 1) * PIECE]


def finish_down(place, pieces):
    halves = lambda n: pl.BlockSpec((n, 1, FFL, B), lambda i, p: (0, 2, 0, 0))
    return pl.pallas_call(
        finish_down_kernel,
        grid_spec=pltpu.PrefetchScalarGridSpec(
            num_scalar_prefetch=1,
            grid=(1,),
            in_specs=[halves(2), halves(2), halves(1), halves(1), halves(2)],
            out_specs=pl.BlockSpec((4 * PIECE, D), lambda i, p: (0, 0)),
        ),
        out_shape=shaped(4 * PIECE, D, kind=F32),
        compiler_params=params("arbitrary"),
        cost_estimate=cost(0, 5),
        name="finish_down",
    )(place, *pieces)


def own_rows(rows_all, y, core, per):
    return lax.dynamic_slice_in_dim(rows_all, (2 * y + core) * per, per, 0)


class Flow:
    def __init__(self, steps):
        self.steps, self.result, self.sent = steps, None, None
        self.move(None)

    def move(self, arrived):
        try:
            self.sent = self.steps.send(arrived)
        except StopIteration as end:
            self.sent, self.result = (), end.value


def stage(flows, *values):
    flows = [flow for flow in flows if flow.result is None]
    sizes = [len(flow.sent) for flow in flows]
    leaves, tree = jax.tree.flatten(values)
    tied = tie(*[v for flow in flows for v in flow.sent], *leaves)
    for flow, size in zip(flows, sizes):
        flow.move(tied[:size])
        tied = tied[size:]
    return jax.tree.unflatten(tree, tied)


def gather_steps(block):
    (other,) = yield (swap_core(block),)
    pair = jnp.stack([block, other])
    (got,) = yield (along_y(pair),)
    far, swapped = yield (along_y(send_half(got)), swap_core(got))
    (far_swapped,) = yield (swap_core(far),)
    return pair, got, swapped, far, far_swapped


def scatter_steps(parts):
    core = lax.axis_index("core")
    first, behind, ahead, far, far_other = parts
    (far_got,) = yield (swap_core(far_other),)
    far = add(far, far_got[::-1]).astype(BF16)
    low, behind_got, first_got = yield (along_y(far), swap_core(behind), swap_core(first[1]))
    ahead = add(ahead, behind_got[::-1])
    mine = lax.dynamic_slice_in_dim(ahead, core * (B // 2), B // 2, 1) + low.astype(F32)
    ahead = lax.dynamic_update_slice_in_dim(ahead, mine, core * (B // 2), 1).astype(BF16)
    (got,) = yield (along_y(ahead),)
    (last,) = yield (swap_core(got[1]),)
    return add(first[0], first_got) + got[0].astype(F32) + last.astype(F32)


def ring_gather_steps(block, axis):
    half = block.shape[0] // 2
    before, after = yield (shift(block, axis, 1), shift(block, axis, -1))
    low, high = yield (shift(before[:half], axis, 1), shift(after[half:], axis, -1))
    return block, after, low, high, before


def ring_scatter_steps(parts, axis):
    half = parts[2].shape[0] // 2
    low, high = yield (shift(parts[2][:half], axis, 1), shift(parts[2][half:], axis, -1))
    after = jnp.concatenate([add(parts[1][:half], low).astype(BF16), parts[1][half:]], axis=0)
    before = jnp.concatenate([parts[3][:half], add(parts[3][half:], high).astype(BF16)], axis=0)
    from_before, from_after = yield (shift(after, axis, 1), shift(before, axis, -1))
    return add(parts[0], from_before) + from_after.astype(F32)


def on_device(
    layer_input,
    positions,
    attn_gain,
    w_query,
    w_key,
    w_value,
    w_output,
    mlp_gain,
    w_gate,
    w_up,
    w_down,
    out_grad,
):
    zlo, y, zhi, x, core = (lax.axis_index(axis) for axis in AXES)
    place = jnp.stack([zlo, y, core, x, zhi]).astype(jnp.int32)

    def by_core(mine, got):
        return jnp.where(core == 0, jnp.stack([mine, got]), jnp.stack([got, mine]))

    def by_zlo(mine, got):
        return jnp.where(zlo == 0, jnp.stack([mine, got]), jnp.stack([got, mine]))

    def by_zhi(mine, got):
        return jnp.where(zhi == 0, jnp.stack([mine, got]), jnp.stack([got, mine]))

    def trio(mine, other, axis):
        across = lax.ppermute(other, (axis, "core"), [(i, 3 - i) for i in range(4)])
        return shift(mine, axis, 1), swap_core(other), across

    def column_steps(mine, got):
        pair = by_core(mine, got)
        (got,) = yield (shift(pair, "zhi", 1),)
        return (yield from ring_gather_steps(by_zhi(pair, got), "x"))

    def output_steps(mine, other):
        there, here, across = yield trio(mine, other, "zhi")
        column = by_zhi(by_core(mine, here), by_core(there, across))
        return (yield from ring_gather_steps(column, "x"))

    def of_core(pair, other=False):
        return lax.dynamic_index_in_dim(pair, 1 - core if other else core, 0, keepdims=False)

    def whole_ring(pieces):
        own, after, low, high, before = pieces
        return own, after, jnp.concatenate([low, high], axis=0), before

    def attention_steps(column):
        keep = lax.dynamic_index_in_dim(column, zhi, 0, keepdims=False)
        send = lax.dynamic_index_in_dim(column, 1 - zhi, 0, keepdims=False)
        (got,) = yield (shift(send, "zhi", 1),)
        pair = add(keep, got).astype(BF16)
        mine, other = of_core(pair), of_core(pair, True)
        there, here, across = yield trio(mine, other, "zlo")
        own = by_core(add(mine, there), add(here, across)).astype(BF16)
        return (yield from ring_gather_steps(own, "y"))

    def ff_steps(sums):
        own = yield from ring_scatter_steps([sums[i] for i in range(4)], "z")
        own = own.astype(BF16)
        pair, down = own[: 2 * FFL].reshape(2, FFL, B), own[2 * FFL :]
        mine, other = of_core(pair), of_core(pair, True)
        there, here, across = yield trio(jnp.concatenate([mine, down], axis=0), other, "zlo")
        both = by_zlo(by_core(mine, here), by_core(there[:FFL], across))
        both = jnp.concatenate([both, by_zlo(down, there[FFL:])[:, None]], axis=1)
        return (yield from ring_gather_steps(both, "y"))

    x_low = layer_input[0]
    frequency = theta ** (-jnp.arange(0, HD, 2).astype(F32) / HD)
    angles = positions[0].astype(F32)[:, None] * frequency
    tables = []
    for table in (jnp.cos(angles), jnp.sin(angles)):
        high = lax.reduce_precision(table, 8, 7)
        tables += [high.astype(BF16), (table - high).astype(BF16)]
    tokens = Flow(gather_steps(jnp.concatenate([x_low, *tables], axis=1)))
    grads = Flow(gather_steps(out_grad[0]))
    qkv_mine, qkv_other = prepare_qkv(place, w_query, w_key, w_value, attn_gain[:, None])
    qkv_mine, qkv_got, gain_two, w_out = stage([tokens], qkv_mine, swap_core(qkv_other), mlp_gain[:, None], w_output)

    columns = Flow(column_steps(qkv_mine, qkv_got))
    o_rows = lax.all_to_all(w_out.reshape(B, 16, B).transpose(1, 0, 2), FSDP, 0, 0, tiled=True)
    ff_mine, ff_other, ff_down = prepare_ff(place, w_gate, w_up, w_down, gain_two)
    ff_mine, ff_got, ff_down, x_low, o_rows = stage(
        [tokens, columns], ff_mine, swap_core(ff_other), ff_down, x_low, o_rows
    )

    ff_piece = jnp.concatenate([by_core(ff_mine, ff_got).reshape(2 * FFL, B), ff_down], axis=0)
    ff_column = lax.all_gather(ff_piece, "x", axis=0, tiled=False)
    inputs = x_low.astype(F32)
    scale_one = lax.rsqrt(jnp.mean(inputs * inputs, axis=-1, keepdims=True) + eps)
    o_rows = o_rows.reshape(D, B)
    mine, other = own_rows(o_rows, y, core, HEADS * HD), own_rows(o_rows, y, 1 - core, HEADS * HD)
    scale_one, mine, other = stage([tokens, columns, grads], scale_one, mine, other)

    outputs = Flow(output_steps(mine, other))
    stage([tokens, columns, outputs])

    x_pieces = tokens.result
    query, key_value, scale_all, cosine, sine, qkv_full = project_qkv(place, x_pieces, columns.result)
    query, key_value = stage([outputs, grads], query, key_value)

    earlier = lax.ppermute(key_value, "zlo", [(0, 1)])
    query, key_value, earlier, ff_column = stage([outputs], query, key_value, earlier, ff_column)

    hidden_rows = Flow(ring_gather_steps(ff_column, "z"))
    key_value = jnp.concatenate([earlier, key_value], axis=1)
    mixed, log_total, *parts, o_full = attention(place, outputs.result, query, key_value)
    parts = stage([grads], *parts)
    sums = Flow(scatter_steps(parts))
    stage([sums, grads])
    grad_pieces = grads.result
    stage([sums])
    stage([sums])
    stage([sums, hidden_rows])
    hidden = inputs + sums.result
    scale_two = lax.rsqrt(jnp.mean(hidden * hidden, axis=-1, keepdims=True) + eps)
    normed = Flow(gather_steps((hidden * scale_two).astype(BF16)))
    stage([normed])
    stage([normed])
    stage([normed])
    stage([normed, hidden_rows])
    normed_pieces = normed.result

    activation, act_t, gate_t, up_t, *parts, down_full = feed_forward(
        place, normed_pieces, grad_pieces, hidden_rows.result
    )
    sums = Flow(scatter_steps(parts))
    (act_t,) = stage([sums], act_t)
    down_terms = ff_terms(down_kernel, place, grad_pieces, (act_t,), FFL, "down_terms")
    down_terms, gate_t = stage([sums], down_terms, gate_t)
    down_sum = lax.psum_scatter(down_terms, "x", scatter_dimension=0, tiled=True)[0]
    gate_up_terms = ff_terms(gate_up_kernel, place, normed_pieces, (gate_t, up_t), 2 * FFL, "gate_up_terms")
    (gate_up_terms,) = stage([sums], gate_up_terms)
    gate_up_sum = lax.psum_scatter(gate_up_terms, "x", scatter_dimension=0, tiled=True)[0]
    stage([sums])

    grad_normed_two = sums.result
    mean_two = jnp.mean(grad_normed_two * hidden, axis=-1, keepdims=True)
    grad_hidden = (
        out_grad[0].astype(F32)
        + scale_two * grad_normed_two
        - hidden * (scale_two * scale_two * scale_two) * mean_two
    )
    hidden_grads = Flow(gather_steps(grad_hidden.astype(BF16)))
    (activation,) = stage([hidden_grads], activation)
    down_parts = project(activation, down_full)
    down_parts = stage([hidden_grads], *down_parts)
    result = Flow(scatter_steps(down_parts))
    stage([hidden_grads, result])
    stage([hidden_grads])

    hidden_grad_pieces = hidden_grads.result
    grad_query, grad_earlier, grad_own = attention_back(
        place, hidden_grad_pieces, query, key_value, log_total, o_full
    )
    grad_query, grad_earlier, grad_own, mixed = stage([result], grad_query, grad_earlier, grad_own, mixed)
    later = lax.ppermute(grad_earlier, "zlo", [(1, 0)])
    output_terms = attention_terms(place, hidden_grad_pieces, mixed.reshape(2 * HALF, HEADS * HD), "output_terms")
    later, grad_query, output_terms, down_sum, gate_up_sum = stage(
        [result], later, grad_query, output_terms, down_sum, gate_up_sum
    )
    output_sum = lax.psum_scatter(output_terms, "x", scatter_dimension=0, tiled=True)[0]
    ff_sums = Flow(ff_steps(jnp.concatenate([gate_up_sum, down_sum], axis=1)))
    *parts, grad_t = qkv_back(grad_query, grad_own, later, cosine, sine, scale_all, qkv_full)
    *parts, grad_t = stage([ff_sums, result], *parts, grad_t)

    sums = Flow(scatter_steps(parts))
    terms = attention_terms(place, x_pieces, grad_t, "qkv_terms")
    terms, output_sum = stage([sums, ff_sums], terms, output_sum)
    attention_sum = lax.psum_scatter(terms, "x", scatter_dimension=0, tiled=True)[0]
    output_sums = Flow(attention_steps(output_sum))
    (attention_sum,) = stage([sums, output_sums], attention_sum)
    attention_sums = Flow(attention_steps(attention_sum))
    stage([sums, output_sums, attention_sums, ff_sums])
    stage([sums, output_sums, attention_sums])
    grad_normed = sums.result
    mean_one = jnp.mean(grad_normed * inputs, axis=-1, keepdims=True)
    input_grad = (
        grad_hidden
        + scale_one * grad_normed
        - inputs * (scale_one * scale_one * scale_one) * mean_one
    )
    input_grad = input_grad.astype(BF16)
    stage([attention_sums, output_sums, ff_sums])

    ring = jnp.roll(jnp.stack(whole_ring(output_sums.result)), y, axis=0).reshape(16, B, B)
    output_grad = lax.all_to_all(ring, FSDP, 0, 0, tiled=True)
    stage([attention_sums, ff_sums])

    gain_two = mlp_gain[:, None]
    pieces = ff_sums.result
    gate_grad, gate_gain = finish_hidden(place, pieces, 0, w_gate, gain_two)
    up_grad, up_gain = finish_hidden(place, pieces, 1, w_up, gain_two)
    down_grad = finish_down(place, pieces)
    query_grad, key_grad, value_grad, attn_gain_grad = finish_attention(
        place, whole_ring(attention_sums.result), w_query, w_key, w_value, attn_gain[:, None]
    )
    output_grad = finish_output(output_grad)
    return (
        (hidden + result.result).astype(BF16)[None],
        input_grad[None],
        attn_gain_grad[:, 0],
        query_grad,
        key_grad,
        value_grad,
        output_grad,
        (gate_gain + up_gain)[:, 0],
        gate_grad,
        up_grad,
        down_grad,
    )


def solution(mesh):
    split = Mesh(mesh.devices.reshape(2, 4, 2, 4, 2), AXES)
    tokens = P(FSDP, SEQ, None)
    rows = P(FSDP, None)
    gain = P(FSDP)
    in_specs = (
        tokens, P(FSDP, SEQ), gain, rows, rows, rows, rows, gain, rows, rows, rows, tokens,
    )
    out_specs = (tokens, tokens, gain, rows, rows, rows, rows, gain, rows, rows, rows)
    return jax.shard_map(
        on_device, mesh=split, in_specs=in_specs, out_specs=out_specs, check_vma=False
    )
```

```python
import jax
import jax.numpy as jnp
from jax import lax
from jax.experimental import pallas as pl
from jax.experimental.pallas import tpu as pltpu
from jax.sharding import Mesh
from jax.sharding import PartitionSpec as P

H = 32
KV = 4
HD = 64
D = 2048
FF = 5632
B = 128
HALF = 512
HEADS = 4
FFL = 704
PIECE = 88

eps = 1e-05
theta = 10000.0
F32 = jnp.float32
BF16 = jnp.bfloat16
AXES = ("zlo", "y", "zhi", "x", "core")
FSDP = ("zhi", "x", "core")
SEQ = ("zlo", "y")


def matmul(left, right):
    return jnp.dot(left, right, preferred_element_type=F32)


def times_transposed(left, right):
    return lax.dot_general(left, right, (((1,), (1,)), ((), ())), preferred_element_type=F32)


def outer_sum(left, right):
    return lax.dot_general(left, right, (((0,), (0,)), ((), ())), preferred_element_type=F32)


def shift(value, axis, by):
    if axis == "z":
        at = [2 * (z % 2) + z // 2 for z in range(4)]
        return lax.ppermute(value, ("zlo", "zhi"), [(at[z], at[(z + by) % 4]) for z in range(4)])
    size = lax.axis_size(axis)
    return lax.ppermute(value, axis, [(i, (i + by) % size) for i in range(size)])


def swap_core(value):
    return shift(value, "core", 1)


def small_gather(block, axis):
    return shift(block, axis, -1), shift(block, axis, 2), shift(block, axis, 1)


def tie(*values):
    return lax.optimization_barrier(values)


def add(left, right):
    return left.astype(F32) + right.astype(F32)


def along_y(value):
    pairs = []
    for i in range(4):
        pairs.append((2 * i, 2 * ((i + 1) % 4)))
        pairs.append((2 * i + 1, 2 * ((i + 3) % 4) + 1))
    return lax.ppermute(value, ("y", "core"), pairs)


def send_half(got):
    core = lax.axis_index("core")
    return lax.dynamic_slice_in_dim(got, core * (B // 2), B // 2, 1)


FLIPPED = (0, 0, 1, 0, 1)
LENGTHS = (B, B, B, B // 2, B // 2)


def put_tokens(refs, rows_ref, sems, start):
    lanes = pl.ds(0, rows_ref.shape[1])
    copies = []
    row = 0
    for s in range(2):
        for ref, flip, length in zip(refs, FLIPPED, LENGTHS):
            copies.append(
                pltpu.make_async_copy(
                    ref.at[s ^ flip, :, lanes], rows_ref.at[pl.ds(row, length)], sems.at[start + len(copies)]
                )
            )
            row += length
    return copies


TILE = 256
WIDE = D + B
VMEM_LIMIT = 56 * 2**20
ANYWHERE = pl.BlockSpec(memory_space=pl.ANY)


def params(*kinds):
    return pltpu.CompilerParams(dimension_semantics=kinds or None, vmem_limit_bytes=VMEM_LIMIT)


def cost(flops, megabytes):
    return pl.CostEstimate(flops=flops, bytes_accessed=int(megabytes * 2**20), transcendentals=0)


def shaped(*shape, kind=BF16):
    return jax.ShapeDtypeStruct(shape, kind)


PARTS = ((B, True), (B, False), (B // 2, False), (B // 2, True))
PART_SHAPES = [jax.ShapeDtypeStruct((B, D), BF16)] * 2 + [jax.ShapeDtypeStruct((2, n, D), BF16) for n, _ in PARTS]


def part_specs(steps):
    def of(turn):
        return lambda i, *_: (1 - i // steps if turn else i // steps, 0, 0)

    return [pl.BlockSpec((B, D), lambda i, *_: (0, 0))] * 2 + [pl.BlockSpec((1, n, D), of(turn)) for n, turn in PARTS]


def put_first(sequence, rows, refs):
    for s in range(2):

        @pl.when(sequence == s)
        def _():
            refs[s][...] = rows


def put_parts(step, tile, refs):
    @pl.when(step % 2 == 0)
    def _():
        put_first(step // 2, tile[:B], refs)
        refs[2][0] = tile[B:]

    @pl.when(step % 2 == 1)
    def _():
        refs[3][0] = tile[:B]
        refs[4][0] = tile[B : B + B // 2]
        refs[5][0] = tile[B + B // 2 :]


def put_rows(sequence, rows, refs):
    put_first(sequence, rows[:B], refs)
    row = B
    for ref, (length, _) in zip(refs[2:], PARTS):
        ref[0] = rows[row : row + length]
        row += length


def turned(values):
    lane = lax.broadcasted_iota(jnp.int32, values.shape, 1) % HD
    return jnp.where(lane < HD // 2, -pltpu.roll(values, 2 * HD - HD // 2, 1), pltpu.roll(values, HD // 2, 1))


def lane_block(zhi, x, core):
    return pl.ds(pl.multiple_of((zhi * 8 + x * 2 + core) * B, B), B)


def put_columns(place, refs, into, sems, start):
    copies = []
    for ref, by, first in zip(refs, (0, 1, 2, 2, 3), (0, 0, 0, 1, 0)):
        for i in range(ref.shape[0]):
            for core in range(2):
                lanes = lane_block(first + i, (place[3] + by) % 4, core)
                copies.append(
                    pltpu.make_async_copy(ref.at[i, core], into.at[:, lanes], sems.at[start + len(copies)])
                )
    return copies


def prepare_qkv_kernel(place, q_mine, q_other, w_key, w_value, gain, mine_ref, other_ref, k_rows, v_rows):
    scale = gain[...]
    k_rows[...] = (w_key[...].astype(F32) * scale).T
    v_rows[...] = (w_value[...].astype(F32) * scale).T
    rows = pl.ds(pl.multiple_of(place[1] * HD, HD), HD)
    for source, out in ((q_mine, mine_ref), (q_other, other_ref)):
        out[: HEADS * HD] = (source[...].astype(F32) * scale).T.astype(BF16)
        out[HEADS * HD : (HEADS + 1) * HD] = k_rows[rows].astype(BF16)
        out[(HEADS + 1) * HD :] = v_rows[rows].astype(BF16)


QKV = (HEADS + 2) * HD


def prepare_qkv(place, w_query, w_key, w_value, gain):
    whole = lambda *shape: pl.BlockSpec(shape, lambda i, p: (0,) * len(shape))
    return pl.pallas_call(
        prepare_qkv_kernel,
        grid_spec=pltpu.PrefetchScalarGridSpec(
            num_scalar_prefetch=1,
            grid=(1,),
            in_specs=[
                pl.BlockSpec((B, HEADS * HD), lambda i, p: (0, 2 * p[1] + p[2])),
                pl.BlockSpec((B, HEADS * HD), lambda i, p: (0, 2 * p[1] + 1 - p[2])),
                whole(B, KV * HD), whole(B, KV * HD), whole(B, 1),
            ],
            out_specs=[whole(QKV, B), whole(QKV, B)],
            scratch_shapes=[pltpu.VMEM((KV * HD, B), F32), pltpu.VMEM((KV * HD, B), F32)],
        ),
        out_shape=[shaped(QKV, B), shaped(QKV, B)],
        compiler_params=params("arbitrary"),
        cost_estimate=cost(0, 1),
        name="prepare_qkv",
    )(place, w_query, w_query, w_key, w_value, gain)


def prepare_ff_kernel(place, w_gate, w_up, w_down, gain, mine_ref, other_ref, down_ref, picked, rows, down_rows, sems):
    zlo, y, core = place[0], place[1], place[2]
    down = pltpu.make_async_copy(
        w_down.at[:, pl.ds(pl.multiple_of(zlo * (D // 2), D // 2), D // 2)], down_rows, sems.at[1]
    )
    down.start()

    @pl.when(zlo == 0)
    def _():
        copy = pltpu.make_async_copy(w_gate, picked, sems.at[0])
        copy.start()
        copy.wait()

    @pl.when(zlo == 1)
    def _():
        copy = pltpu.make_async_copy(w_up, picked, sems.at[0])
        copy.start()
        copy.wait()

    scale = gain[...]
    for i in range(FF // B):
        rows[i * B : (i + 1) * B] = (picked[:, i * B : (i + 1) * B].astype(F32) * scale).T
    for which, out in ((core, mine_ref), (1 - core, other_ref)):
        slabs = []
        for zx in range(8):
            at = pl.multiple_of(zx * 2 * 4 * PIECE + which * 4 * PIECE + y * PIECE, 8)
            slabs.append(rows[pl.ds(at, PIECE)])
        out[...] = jnp.concatenate(slabs, axis=0).astype(BF16)
    down.wait()
    for t in range(8):
        rows[t * 4 * PIECE : (t + 1) * 4 * PIECE] = down_rows[:, t * B : (t + 1) * B].astype(F32)
    slabs = [rows[pl.ds(pl.multiple_of(t * 4 * PIECE + y * PIECE, 8), PIECE)] for t in range(8)]
    down_ref[...] = jnp.concatenate(slabs, axis=0).astype(BF16)


def prepare_ff(place, w_gate, w_up, w_down, gain):
    return pl.pallas_call(
        prepare_ff_kernel,
        grid_spec=pltpu.PrefetchScalarGridSpec(
            num_scalar_prefetch=1,
            grid=(1,),
            in_specs=[ANYWHERE, ANYWHERE, ANYWHERE, pl.BlockSpec((B, 1), lambda i, p: (0, 0))],
            out_specs=[pl.BlockSpec((FFL, B), lambda i, p: (0, 0))] * 3,
            scratch_shapes=[
                pltpu.VMEM((B, FF), BF16),
                pltpu.VMEM((FF, B), F32),
                pltpu.VMEM((4 * PIECE, D // 2), BF16),
                pltpu.SemaphoreType.DMA((2,)),
            ],
        ),
        out_shape=[shaped(FFL, B)] * 3,
        compiler_params=params("arbitrary"),
        cost_estimate=cost(0, 6),
        name="prepare_ff",
    )(place, w_gate, w_up, w_down, gain)


def project_qkv_kernel(*refs):
    place, x_refs, w_refs = refs[0], refs[1:6], refs[6:11]
    query_ref, kv_ref, scale_ref, cosine_ref, sine_ref, w_out, rows, weights, sems = refs[11:]
    step = pl.program_id(0)
    tokens = put_tokens(x_refs, rows, sems, 0)
    columns = put_columns(place, w_refs, weights, sems, 10)
    back = pltpu.make_async_copy(weights, w_out, sems.at[26])

    @pl.when(step == 0)
    def _():
        for copy in columns + tokens:
            copy.start()
        for copy in columns:
            copy.wait()
        back.start()
        for copy in tokens:
            copy.wait()

    at = pl.ds(pl.multiple_of(step * TILE, TILE), TILE)
    tile = rows[at, :D]
    wide = tile.astype(F32)
    scale = lax.rsqrt(jnp.mean(wide * wide, axis=-1, keepdims=True) + eps)
    scale_ref[...] = scale
    pre = times_transposed(tile, weights[...]) * scale
    tables = rows[at, D:].astype(F32)
    tables = tables + pltpu.roll(tables, B - HD // 2, 1)
    cosine = jnp.concatenate([tables[:, : HD // 2]] * 4, axis=1)
    sine = jnp.concatenate([tables[:, HD : HD + HD // 2]] * 4, axis=1)
    cosine_ref[...] = cosine
    sine_ref[...] = sine
    for i in range(2):
        part = pre[:, i * 2 * HD : (i + 1) * 2 * HD]
        part = (part * cosine + turned(part) * sine).astype(BF16) * HD ** (-0.5)
        query_ref[0, 2 * i] = part[:, :HD]
        query_ref[0, 2 * i + 1] = part[:, HD:]
    part = pre[:, HEADS * HD :]
    lane = lax.broadcasted_iota(jnp.int32, part.shape, 1)
    kv_ref[0] = jnp.where(lane < HD, part * cosine + turned(part) * sine, part).astype(BF16)

    @pl.when(step == 3)
    def _():
        back.wait()


def project_qkv(place, x_pieces, w_pieces):
    tile = lambda lanes: pl.BlockSpec((TILE, lanes), lambda i, p: (i, 0))
    return pl.pallas_call(
        project_qkv_kernel,
        grid_spec=pltpu.PrefetchScalarGridSpec(
            num_scalar_prefetch=1,
            grid=(4,),
            in_specs=[ANYWHERE] * 10,
            out_specs=[
                pl.BlockSpec((1, HEADS, TILE, HD), lambda i, p: (i // 2, 0, i % 2, 0)),
                pl.BlockSpec((1, TILE, 2 * HD), lambda i, p: (i // 2, i % 2, 0)),
                tile(1), tile(2 * HD), tile(2 * HD),
                ANYWHERE,
            ],
            scratch_shapes=[
                pltpu.VMEM((2 * HALF, WIDE), BF16),
                pltpu.VMEM((QKV, D), BF16),
                pltpu.SemaphoreType.DMA((27,)),
            ],
        ),
        out_shape=[
            shaped(2, HEADS, HALF, HD), shaped(2, HALF, 2 * HD), shaped(2 * HALF, 1, kind=F32),
            shaped(2 * HALF, 2 * HD, kind=F32), shaped(2 * HALF, 2 * HD, kind=F32), shaped(QKV, D),
        ],
        compiler_params=params("arbitrary"),
        cost_estimate=cost(2 * 2 * HALF * QKV * D, 8),
        name="project_qkv",
    )(place, *x_pieces, *w_pieces)


def project_kernel(left_ref, weight_ref, *parts):
    put_parts(pl.program_id(0), matmul(left_ref[...], weight_ref[...]).astype(BF16), parts)


def project(left, weight):
    depth = left.shape[1]
    return pl.pallas_call(
        project_kernel,
        grid=(4,),
        in_specs=[pl.BlockSpec((TILE, depth), lambda i: (i, 0)), pl.BlockSpec((depth, D), lambda i: (0, 0))],
        out_specs=part_specs(2),
        out_shape=PART_SHAPES,
        compiler_params=params("arbitrary"),
        cost_estimate=cost(2 * 2 * HALF * depth * D, 8),
        name="project",
    )(left, weight)


def put_term(left, rows, term_ref):
    def one(i, carry):
        term = matmul(left, rows[:, pl.ds(pl.multiple_of(i * 4 * B, 4 * B), 4 * B)]).astype(BF16)
        for j in range(2):
            zx = 2 * i + j
            term_ref[zx % 4, zx // 4, 0] = term[:, 2 * j * B : (2 * j + 1) * B]
            term_ref[zx % 4, zx // 4, 1] = term[:, (2 * j + 1) * B : (2 * j + 2) * B]
        return carry

    lax.fori_loop(0, 4, one, 0)


def qkv_back_kernel(grad_q_ref, own_ref, later_ref, cosine_ref, sine_ref, scale_ref, weight_ref, *outs):
    parts, turned_ref = outs[:6], outs[6]
    cosine, sine = cosine_ref[...], sine_ref[...]
    lane = lax.broadcasted_iota(jnp.int32, cosine.shape, 1)
    pieces = []
    for i in range(2):
        part = grad_q_ref[0, :, i * 2 * HD : (i + 1) * 2 * HD]
        pieces.append(part * cosine - turned(part * sine))
    part = own_ref[0] + later_ref[0].astype(F32)
    pieces.append(jnp.where(lane < HD, part * cosine - turned(part * sine), part))
    grad_pre = jnp.concatenate(pieces, axis=1)
    put_parts(pl.program_id(0), matmul(grad_pre.astype(BF16), weight_ref[...]).astype(BF16), parts)
    turned_ref[...] = (grad_pre * scale_ref[...]).T.astype(BF16)


def qkv_back(grad_query, own, later, cosine, sine, scale, weight):
    tile = lambda lanes: pl.BlockSpec((TILE, lanes), lambda i: (i, 0))
    half = lambda lanes: pl.BlockSpec((1, TILE, lanes), lambda i: (i // 2, i % 2, 0))
    return pl.pallas_call(
        qkv_back_kernel,
        grid=(4,),
        in_specs=[
            half(HEADS * HD), half(2 * HD), half(2 * HD), tile(2 * HD), tile(2 * HD), tile(1),
            pl.BlockSpec((QKV, D), lambda i: (0, 0)),
        ],
        out_specs=part_specs(2) + [pl.BlockSpec((QKV, TILE), lambda i: (0, i))],
        out_shape=PART_SHAPES + [shaped(QKV, 2 * HALF)],
        compiler_params=params("arbitrary"),
        cost_estimate=cost(2 * 2 * HALF * QKV * D, 9),
        name="qkv_back",
    )(grad_query, own, later, cosine, sine, scale, weight)


def attention_term_kernel(*refs):
    token_refs, left_ref = refs[1:6], refs[6]
    term_ref, rows, sems = refs[-3:]
    copies = put_tokens(token_refs, rows, sems, 0)
    for copy in copies:
        copy.start()
    left = left_ref[...]
    if left.shape[0] == 2 * HALF:
        left = left.T
    for copy in copies:
        copy.wait()
    put_term(left, rows, term_ref)


def attention_terms(place, pieces, left, name):
    whole = lambda *shape: pl.BlockSpec(shape, lambda i, p: (0,) * len(shape))
    rows = min(left.shape)
    return pl.pallas_call(
        attention_term_kernel,
        grid_spec=pltpu.PrefetchScalarGridSpec(
            num_scalar_prefetch=1,
            grid=(1,),
            in_specs=[ANYWHERE] * 5 + [whole(*left.shape)],
            out_specs=whole(4, 2, 2, rows, B),
            scratch_shapes=[pltpu.VMEM((2 * HALF, D), BF16), pltpu.SemaphoreType.DMA((10,))],
        ),
        out_shape=shaped(4, 2, 2, rows, B),
        compiler_params=params("arbitrary"),
        cost_estimate=cost(2 * 2 * HALF * rows * D, 7),
        name=name,
    )(place, *pieces, left)


def token_places(at, y, core):
    step = 1 - 2 * core
    block = jnp.where(
        at < B, y, jnp.where(at < 2 * B, y + 4 - step, jnp.where(at < 3 * B, y + 4 + step, y + 2))
    )
    row = at % B
    row = jnp.where(at < 3 * B, row, (row + core * (B // 2)) % B)
    return (block % 4) * B + row


def set_bias(place_ref, bias_ref):
    zlo, y, core = place_ref[0], place_ref[1], place_ref[2]
    key_at = token_places(lax.broadcasted_iota(jnp.int32, (HALF, 1), 0), y, core)
    query_at = token_places(lax.broadcasted_iota(jnp.int32, (1, HALF), 1), y, core)
    bias_ref[:HALF, :] = jnp.broadcast_to(jnp.where(zlo == 1, 0.0, -1e30), (HALF, HALF))
    bias_ref[HALF:, :] = jnp.where(key_at <= query_at, 0.0, -1e30)


def attention_kernel(place_ref, *refs):
    w_refs, query_ref, kv_ref, mixed_ref, log_ref = refs[:5], *refs[5:9]
    parts, w_out, bias_ref, weight, sems = refs[9:15], *refs[15:]
    columns = put_columns(place_ref, w_refs, weight, sems, 0)
    back = pltpu.make_async_copy(weight, w_out, sems.at[16])

    @pl.when(pl.program_id(0) == 0)
    def _():
        for copy in columns:
            copy.start()
        set_bias(place_ref, bias_ref)
        for copy in columns:
            copy.wait()
        back.start()

    key, value = kv_ref[0, :, :HD], kv_ref[0, :, HD:]
    for head in range(HEADS):
        scores = times_transposed(key, query_ref[0, head]) + bias_ref[...]
        top = jnp.max(scores, axis=0, keepdims=True)
        weights = jnp.exp(scores - top)
        total = jnp.sum(weights, axis=0, keepdims=True)
        low = (weights * (1.0 / total)).astype(BF16)
        mixed_ref[0, :, head * HD : (head + 1) * HD] = outer_sum(value, low).T.astype(BF16)
        log_ref[0, head] = top + jnp.log(total)
    put_rows(pl.program_id(0), matmul(mixed_ref[0], weight[...]).astype(BF16), parts)

    @pl.when(pl.program_id(0) == 1)
    def _():
        back.wait()


def attention_back_kernel(place_ref, *refs):
    grad_refs, query_ref, kv_ref, log_ref, weight_ref = refs[:5], *refs[5:9]
    grad_query_ref, earlier_ref, own_ref, bias_ref, rows, sems = refs[9:]
    step = pl.program_id(0)
    copies = put_tokens(grad_refs, rows, sems, 0)

    @pl.when(step == 0)
    def _():
        for copy in copies:
            copy.start()
        set_bias(place_ref, bias_ref)
        for copy in copies:
            copy.wait()

    hidden = rows[pl.ds(pl.multiple_of(step * HALF, HALF), HALF), :]
    grads = times_transposed(hidden, weight_ref[...]).astype(BF16)
    key, value = kv_ref[0, :, :HD], kv_ref[0, :, HD:]
    grad_key = jnp.zeros((2 * HALF, HD), F32)
    grad_value = jnp.zeros((2 * HALF, HD), F32)
    for head in range(HEADS):
        lanes = slice(head * HD, (head + 1) * HD)
        query, grad = query_ref[0, head], grads[:, lanes]
        weights = jnp.exp(times_transposed(key, query) + bias_ref[...] - log_ref[0, head])
        grad_weights = times_transposed(value, grad)
        delta = jnp.sum(weights * grad_weights, axis=0, keepdims=True)
        grad_scores = (weights * (grad_weights - delta)).astype(BF16)
        grad_query_ref[0, :, lanes] = outer_sum(key, grad_scores).T * HD ** (-0.5)
        grad_key += matmul(grad_scores, query)
        grad_value += matmul(weights.astype(BF16), grad)
    total = jnp.concatenate([grad_key, grad_value], axis=1)
    earlier_ref[0] = total[:HALF].astype(BF16)
    own_ref[0] = total[HALF:]


def sequence_block(*tail):
    return pl.BlockSpec((1,) + tail, lambda s, place: (s,) + (0,) * len(tail))


def attention_call(kernel, in_specs, out_specs, out_shape, scratch, flops, name):
    return pl.pallas_call(
        kernel,
        grid_spec=pltpu.PrefetchScalarGridSpec(
            num_scalar_prefetch=1,
            grid=(2,),
            in_specs=in_specs,
            out_specs=out_specs,
            scratch_shapes=[pltpu.VMEM((2 * HALF, HALF), F32)] + scratch,
        ),
        out_shape=out_shape,
        compiler_params=params("arbitrary"),
        cost_estimate=cost(flops * 8 * 2 * HALF * HALF * HD * 2, 8),
        name=name,
    )


def attention(place, w_pieces, query, kv):
    return attention_call(
        attention_kernel,
        [ANYWHERE] * 5 + [sequence_block(HEADS, HALF, HD), sequence_block(2 * HALF, 2 * HD)],
        [sequence_block(HALF, HEADS * HD), sequence_block(HEADS, 1, HALF)]
        + part_specs(1)
        + [ANYWHERE],
        [shaped(2, HALF, HEADS * HD), shaped(2, HEADS, 1, HALF, kind=F32)] + PART_SHAPES + [shaped(HEADS * HD, D)],
        [pltpu.VMEM((HEADS * HD, D), BF16), pltpu.SemaphoreType.DMA((17,))],
        3,
        "attention",
    )(place, *w_pieces, query, kv)


def attention_back(place, grad_pieces, query, kv, log_total, weight):
    return attention_call(
        attention_back_kernel,
        [ANYWHERE] * 5
        + [
            sequence_block(HEADS, HALF, HD), sequence_block(2 * HALF, 2 * HD),
            sequence_block(HEADS, 1, HALF), pl.BlockSpec((HEADS * HD, D), lambda s, place: (0, 0)),
        ],
        [sequence_block(HALF, HEADS * HD), sequence_block(HALF, 2 * HD), sequence_block(HALF, 2 * HD)],
        [
            shaped(2, HALF, HEADS * HD, kind=F32),
            shaped(2, HALF, 2 * HD),
            shaped(2, HALF, 2 * HD, kind=F32),
        ],
        [pltpu.VMEM((2 * HALF, D), BF16), pltpu.SemaphoreType.DMA((10,))],
        6,
        "attention_back",
    )(place, *grad_pieces, query, kv, log_total, weight)


def finish_attention_kernel(place, *refs):
    piece_refs, w_query, w_key, w_value, gain_ref = refs[:4], *refs[4:8]
    query_out, key_out, value_out, gain_out, rows = refs[8:]
    for ref, by in zip(piece_refs, range(4)):
        at_y = (place[1] + by) % 4
        for c in range(2):
            piece = ref[c].astype(F32)
            rows[pl.ds(pl.multiple_of((2 * at_y + c) * HEADS * HD, HEADS * HD), HEADS * HD)] = piece[: HEADS * HD]
        both = ref[0].astype(F32) + ref[1].astype(F32)
        at = pl.multiple_of(H * HD + at_y * HD, HD)
        rows[pl.ds(at, HD)] = both[HEADS * HD : (HEADS + 1) * HD]
        rows[pl.ds(at + KV * HD, HD)] = both[(HEADS + 1) * HD :]
    gain = gain_ref[...]
    total = jnp.zeros((B, 1), F32)
    row = 0
    for weight, out in ((w_query, query_out), (w_key, key_out), (w_value, value_out)):
        for i in range(out.shape[1] // B):
            lanes = slice(i * B, (i + 1) * B)
            block = rows[row : row + B].T
            total = total + jnp.sum(block * weight[:, lanes].astype(F32), axis=1, keepdims=True)
            out[:, lanes] = block * gain
            row += B
    gain_out[...] = total


def finish_attention(place, pieces, w_query, w_key, w_value, gain):
    whole = lambda *shape: pl.BlockSpec(shape, lambda i, p: (0,) * len(shape))
    kv = KV * HD
    return pl.pallas_call(
        finish_attention_kernel,
        grid_spec=pltpu.PrefetchScalarGridSpec(
            num_scalar_prefetch=1,
            grid=(1,),
            in_specs=[whole(2, QKV, B)] * 4 + [whole(B, D), whole(B, kv), whole(B, kv), whole(B, 1)],
            out_specs=[whole(B, D), whole(B, kv), whole(B, kv), whole(B, 1)],
            scratch_shapes=[pltpu.VMEM((D + 2 * kv, B), F32)],
        ),
        out_shape=[
            shaped(B, D, kind=F32), shaped(B, kv, kind=F32), shaped(B, kv, kind=F32), shaped(B, 1, kind=F32),
        ],
        compiler_params=params("arbitrary"),
        cost_estimate=cost(0, 4),
        name="finish_attention",
    )(place, *pieces, w_query, w_key, w_value, gain)


def finish_output_kernel(blocks, out):
    for i in range(16):
        out[:, i * B : (i + 1) * B] = blocks[i].astype(F32)


def finish_output(blocks):
    return pl.pallas_call(
        finish_output_kernel,
        out_shape=shaped(B, D, kind=F32),
        compiler_params=params(),
        cost_estimate=cost(0, 2),
        name="finish_output",
    )(blocks)


def feed_forward_kernel(*refs):
    place, token_refs, grad_refs, ff_ref = refs[0], refs[1:6], refs[6:11], refs[11]
    act_ref, act_t, gate_t, up_t = refs[12:16]
    parts, down_out = refs[16:22], refs[22]
    rows_h, rows_g, gate_up, down, slabs, sems = refs[23:]
    step = pl.program_id(0)
    tokens = put_tokens(token_refs, rows_h, sems, 0)
    grads = put_tokens(grad_refs, rows_g, sems, 10)
    weights, loads = [], []
    for x in range(4):
        for by in range(4):
            z = (2 * place[4] + place[0] + by) % 4
            zhi, zlo = z // 2, z % 2
            for core in range(2):
                weights.append(
                    pltpu.make_async_copy(
                        ff_ref.at[x, by, pl.ds(core * FFL, FFL)],
                        gate_up.at[zlo, :, lane_block(zhi, x, core)],
                        sems.at[20 + len(weights)],
                    )
                )
            loads.append(
                pltpu.make_async_copy(
                    ff_ref.at[x, by, pl.ds(2 * FFL, FFL)], slabs.at[zlo, zhi * 4 + x], sems.at[52 + len(loads)]
                )
            )
    back = pltpu.make_async_copy(down, down_out, sems.at[68])

    @pl.when(step == 0)
    def _():
        for copy in tokens + weights + loads + grads:
            copy.start()
        for copy in tokens + weights:
            copy.wait()

    rows = pl.ds(pl.multiple_of(step * HALF, HALF), HALF)
    normed = rows_h[rows, :]
    gate_pre = times_transposed(normed, gate_up[0])
    upward = times_transposed(normed, gate_up[1])

    @pl.when(step == 0)
    def _():
        for copy in loads:
            copy.wait()

        def put(q, carry):
            for half in range(2):
                for p in range(4):
                    one = slabs[half, 2 * q, 2 * p * PIECE : 2 * (p + 1) * PIECE, :].astype(F32)
                    two = slabs[half, 2 * q + 1, 2 * p * PIECE : 2 * (p + 1) * PIECE, :].astype(F32)
                    lane = (half * 8 + 2 * p) * B
                    rows = pl.ds(pl.multiple_of(q * 2 * PIECE, 16), 2 * PIECE)
                    down[rows, lane : lane + B] = jnp.concatenate([one[:PIECE], two[:PIECE]], axis=0).astype(BF16)
                    down[rows, lane + B : lane + 2 * B] = jnp.concatenate(
                        [one[PIECE:], two[PIECE:]], axis=0
                    ).astype(BF16)
            return carry

        lax.fori_loop(0, 4, put, 0)
        back.start()
        for copy in grads:
            copy.wait()

    grad_act = times_transposed(rows_g[rows, :], down[...])
    sigmoid = 1.0 / (1.0 + jnp.exp(-gate_pre))
    silu = gate_pre * sigmoid
    activation = silu * upward
    grad_up = grad_act * silu
    grad_gate = grad_act * upward * (sigmoid * (1.0 + gate_pre * (1.0 - sigmoid)))
    part = matmul(grad_gate.astype(BF16), gate_up[0]) + matmul(grad_up.astype(BF16), gate_up[1])
    put_rows(step, part.astype(BF16), parts)
    act_ref[...] = activation.astype(BF16)
    act_t[...] = activation.T.astype(BF16)
    gate_t[...] = grad_gate.T.astype(BF16)
    up_t[...] = grad_up.T.astype(BF16)

    @pl.when(step == 1)
    def _():
        back.wait()


def feed_forward(place, tokens, grads, ff_all):
    turned_spec = pl.BlockSpec((FFL, HALF), lambda i, p: (0, i))
    turned_shape = shaped(FFL, 2 * HALF)
    return pl.pallas_call(
        feed_forward_kernel,
        grid_spec=pltpu.PrefetchScalarGridSpec(
            num_scalar_prefetch=1,
            grid=(2,),
            in_specs=[ANYWHERE] * 11,
            out_specs=[pl.BlockSpec((HALF, FFL), lambda i, p: (i, 0))]
            + [turned_spec] * 3
            + part_specs(1)
            + [ANYWHERE],
            scratch_shapes=[
                pltpu.VMEM((2 * HALF, D), BF16),
                pltpu.VMEM((2 * HALF, D), BF16),
                pltpu.VMEM((2, FFL, D), BF16),
                pltpu.VMEM((FFL, D), BF16),
                pltpu.VMEM((2, 8, FFL, B), BF16),
                pltpu.SemaphoreType.DMA((69,)),
            ],
        ),
        out_shape=[shaped(2 * HALF, FFL)] + [turned_shape] * 3 + PART_SHAPES + [shaped(FFL, D)],
        compiler_params=params("arbitrary"),
        cost_estimate=cost(2 * 5 * 2 * HALF * FFL * D, 32),
        name="feed_forward",
    )(place, *tokens, *grads, ff_all)


def along_z(place, zhi, zlo):
    return (2 * zhi + zlo + 4 - 2 * place[4] - place[0]) % 4


def load_tokens(step, refs, rows, sems):
    copies = put_tokens(refs, rows, sems, 0)

    @pl.when(step == 0)
    def _():
        for copy in copies:
            copy.start()
        for copy in copies:
            copy.wait()


def gate_up_kernel(*refs):
    place, token_refs, gate_t, up_t, out_ref, rows, terms, sems = refs[0], refs[1:6], *refs[6:]
    step = pl.program_id(0)
    load_tokens(step, token_refs, rows, sems)
    normed = rows[:, pl.ds(pl.multiple_of(step * 4 * B, 4 * B), 4 * B)]

    def out(i, matrix):
        xs, by = pl.ds(i % 2 * 2, 2), along_z(place, i // 2, matrix)
        return pltpu.make_async_copy(terms.at[xs, by], out_ref.at[xs, by], sems.at[10 + 2 * i + matrix])

    for matrix, left in ((0, gate_t), (1, up_t)):
        term = matmul(left[...], normed).astype(BF16)
        by = along_z(place, step // 2, matrix)
        for j in range(2):
            terms[step % 2 * 2 + j, by, 0:FFL, :] = term[:, 2 * j * B : (2 * j + 1) * B]
            terms[step % 2 * 2 + j, by, FFL:, :] = term[:, (2 * j + 1) * B : (2 * j + 2) * B]
        out(step, matrix).start()

    @pl.when(step == 3)
    def _():
        for i in range(4):
            for matrix in range(2):
                out(i, matrix).wait()


def down_kernel(*refs):
    place, grad_refs, act_t, out_ref, rows, terms, sems = refs[0], refs[1:6], *refs[6:]
    step = pl.program_id(0)
    load_tokens(step, grad_refs, rows, sems)
    term = matmul(act_t[...], rows[:, pl.ds(pl.multiple_of(step * 4 * B, 4 * B), 4 * B)])
    for j in range(2):
        p = (2 * step + j) % 4
        at = pl.ds(pl.multiple_of(p * 2 * PIECE, 16), 2 * PIECE)
        for zx in range(8):
            slab = term[zx * PIECE : (zx + 1) * PIECE]
            low, high = slab[:, 2 * j * B : (2 * j + 1) * B], slab[:, (2 * j + 1) * B : (2 * j + 2) * B]
            by = along_z(place, zx // 4, step // 2)
            terms[zx % 4, by, at, :] = jnp.concatenate([low, high], axis=0).astype(BF16)

    def out(half, zhi):
        by = along_z(place, zhi, half)
        return pltpu.make_async_copy(terms.at[:, by], out_ref.at[:, by], sems.at[10 + 2 * half + zhi])

    @pl.when(step % 2 == 1)
    def _():
        for zhi in range(2):
            out(step // 2, zhi).start()

    @pl.when(step == 3)
    def _():
        for half in range(2):
            for zhi in range(2):
                out(half, zhi).wait()


def ff_terms(kernel, place, pieces, lefts, rows, name):
    whole = pl.BlockSpec((FFL, 2 * HALF), lambda i, p: (0, 0))
    return pl.pallas_call(
        kernel,
        grid_spec=pltpu.PrefetchScalarGridSpec(
            num_scalar_prefetch=1,
            grid=(4,),
            in_specs=[ANYWHERE] * 5 + [whole] * len(lefts),
            out_specs=ANYWHERE,
            scratch_shapes=[
                pltpu.VMEM((2 * HALF, D), BF16),
                pltpu.VMEM((4, 4, rows, B), BF16),
                pltpu.SemaphoreType.DMA((18,)),
            ],
        ),
        out_shape=shaped(4, 4, rows, B),
        compiler_params=params("arbitrary"),
        cost_estimate=cost(2 * len(lefts) * 2 * HALF * FFL * D, 8 + 4 * len(lefts)),
        name=name,
    )(place, *pieces, *lefts)


def finish_hidden_kernel(*refs):
    place, piece_refs, weight_ref, gain_ref, out_ref, gain_out, rows = refs[0], refs[1:5], *refs[5:]
    for ref, by in zip(piece_refs, range(4)):
        at_y = (place[1] + by) % 4
        for core in range(2):
            slab = ref[0, core].astype(F32)
            for zx in range(8):
                at = pl.multiple_of((2 * zx + core) * 4 * PIECE + at_y * PIECE, 8)
                rows[pl.ds(at, PIECE)] = slab[zx * PIECE : (zx + 1) * PIECE]
    gain = gain_ref[...]
    total = jnp.zeros((B, 1), F32)
    for i in range(FF // B):
        lanes = slice(i * B, (i + 1) * B)
        block = rows[lanes].T
        total = total + jnp.sum(block * weight_ref[:, lanes].astype(F32), axis=1, keepdims=True)
        out_ref[:, lanes] = block * gain
    gain_out[...] = total


def finish_hidden(place, pieces, matrix, weight, gain):
    own, after, low, high, before = pieces
    at = lambda m: pl.BlockSpec((1, 2, FFL, B), lambda i, p: (m, 0, 0, 0))
    whole = lambda *shape: pl.BlockSpec(shape, lambda i, p: (0,) * len(shape))
    return pl.pallas_call(
        finish_hidden_kernel,
        grid_spec=pltpu.PrefetchScalarGridSpec(
            num_scalar_prefetch=1,
            grid=(1,),
            in_specs=[at(matrix), at(matrix), at(0), at(matrix), whole(B, FF), whole(B, 1)],
            out_specs=[whole(B, FF), whole(B, 1)],
            scratch_shapes=[pltpu.VMEM((FF, B), F32)],
        ),
        out_shape=[shaped(B, FF, kind=F32), shaped(B, 1, kind=F32)],
        compiler_params=params("arbitrary"),
        cost_estimate=cost(0, 6),
        name="finish_hidden",
    )(place, own, after, (low, high)[matrix], before, weight, gain)


def finish_down_kernel(place, own, after, low, high, before, out_ref):
    for refs, by in (((own, own), 0), ((after, after), 1), ((low, high), 2), ((before, before), 3)):
        rows = pl.ds(pl.multiple_of((place[1] + by) % 4 * PIECE, 8), PIECE)
        for half in range(2):
            slab = refs[half][half if by != 2 else 0, 0].astype(F32)
            for t in range(8):
                lane = (half * 8 + t) * B
                out_ref[rows, lane : lane + B] = slab[t * PIECE : (t + 1) * PIECE]


def finish_down(place, pieces):
    halves = lambda n: pl.BlockSpec((n, 1, FFL, B), lambda i, p: (0, 2, 0, 0))
    return pl.pallas_call(
        finish_down_kernel,
        grid_spec=pltpu.PrefetchScalarGridSpec(
            num_scalar_prefetch=1,
            grid=(1,),
            in_specs=[halves(2), halves(2), halves(1), halves(1), halves(2)],
            out_specs=pl.BlockSpec((4 * PIECE, D), lambda i, p: (0, 0)),
        ),
        out_shape=shaped(4 * PIECE, D, kind=F32),
        compiler_params=params("arbitrary"),
        cost_estimate=cost(0, 5),
        name="finish_down",
    )(place, *pieces)


def own_rows(rows_all, y, core, per):
    return lax.dynamic_slice_in_dim(rows_all, (2 * y + core) * per, per, 0)


class Flow:
    def __init__(self, steps):
        self.steps, self.result, self.sent = steps, None, None
        self.move(None)

    def move(self, arrived):
        try:
            self.sent = self.steps.send(arrived)
        except StopIteration as end:
            self.sent, self.result = (), end.value


def stage(flows, *values):
    flows = [flow for flow in flows if flow.result is None]
    sizes = [len(flow.sent) for flow in flows]
    leaves, tree = jax.tree.flatten(values)
    tied = tie(*[v for flow in flows for v in flow.sent], *leaves)
    for flow, size in zip(flows, sizes):
        flow.move(tied[:size])
        tied = tied[size:]
    return jax.tree.unflatten(tree, tied)


def gather_steps(block):
    (other,) = yield (swap_core(block),)
    pair = jnp.stack([block, other])
    (got,) = yield (along_y(pair),)
    far, swapped = yield (along_y(send_half(got)), swap_core(got))
    (far_swapped,) = yield (swap_core(far),)
    return pair, got, swapped, far, far_swapped


def scatter_steps(parts):
    core = lax.axis_index("core")
    first, first_other, behind, ahead, far, far_other = parts
    (far_got,) = yield (swap_core(far_other),)
    far = add(far, far_got).astype(BF16)
    low, behind_got, first_got = yield (along_y(far), swap_core(behind), swap_core(first_other))
    ahead = add(ahead, behind_got).astype(BF16)
    mine = add(lax.dynamic_slice_in_dim(ahead, core * (B // 2), B // 2, 1), low).astype(BF16)
    ahead = lax.dynamic_update_slice_in_dim(ahead, mine, core * (B // 2), 1)
    (got,) = yield (along_y(ahead),)
    (last,) = yield (swap_core(got[1]),)
    return add(first, first_got) + got[0].astype(F32) + last.astype(F32)


def ring_gather_steps(block, axis):
    half = block.shape[0] // 2
    before, after = yield (shift(block, axis, 1), shift(block, axis, -1))
    low, high = yield (shift(before[:half], axis, 1), shift(after[half:], axis, -1))
    return block, after, low, high, before


def ring_scatter_steps(parts, axis):
    half = parts[2].shape[0] // 2
    low, high = yield (shift(parts[2][:half], axis, 1), shift(parts[2][half:], axis, -1))
    after = jnp.concatenate([add(parts[1][:half], low).astype(BF16), parts[1][half:]], axis=0)
    before = jnp.concatenate([parts[3][:half], add(parts[3][half:], high).astype(BF16)], axis=0)
    from_before, from_after = yield (shift(after, axis, 1), shift(before, axis, -1))
    return add(parts[0], from_before) + from_after.astype(F32)


def on_device(
    layer_input,
    positions,
    attn_gain,
    w_query,
    w_key,
    w_value,
    w_output,
    mlp_gain,
    w_gate,
    w_up,
    w_down,
    out_grad,
):
    zlo, y, zhi, x, core = (lax.axis_index(axis) for axis in AXES)
    place = jnp.stack([zlo, y, core, x, zhi]).astype(jnp.int32)

    def by_core(mine, got):
        return jnp.where(core == 0, jnp.stack([mine, got]), jnp.stack([got, mine]))

    def by_zlo(mine, got):
        return jnp.where(zlo == 0, jnp.stack([mine, got]), jnp.stack([got, mine]))

    def by_zhi(mine, got):
        return jnp.where(zhi == 0, jnp.stack([mine, got]), jnp.stack([got, mine]))

    def trio(mine, other, axis):
        across = lax.ppermute(other, (axis, "core"), [(i, 3 - i) for i in range(4)])
        return shift(mine, axis, 1), swap_core(other), across

    def column_steps(mine, got):
        pair = by_core(mine, got)
        (got,) = yield (shift(pair, "zhi", 1),)
        return (yield from ring_gather_steps(by_zhi(pair, got), "x"))

    def output_steps(mine, other):
        there, here, across = yield trio(mine, other, "zhi")
        column = by_zhi(by_core(mine, here), by_core(there, across))
        return (yield from ring_gather_steps(column, "x"))

    def hidden_steps(mine, got, down):
        piece = jnp.concatenate([by_core(mine, got).reshape(2 * FFL, B), down], axis=0)
        pieces = yield from ring_gather_steps(piece, "z")
        return jnp.concatenate(pieces, axis=0).reshape(4, 3 * FFL, B)

    def of_core(pair, other=False):
        return lax.dynamic_index_in_dim(pair, 1 - core if other else core, 0, keepdims=False)

    def whole_ring(pieces):
        own, after, low, high, before = pieces
        return own, after, jnp.concatenate([low, high], axis=0), before

    def attention_steps(column):
        keep = lax.dynamic_index_in_dim(column, zhi, 0, keepdims=False)
        send = lax.dynamic_index_in_dim(column, 1 - zhi, 0, keepdims=False)
        (got,) = yield (shift(send, "zhi", 1),)
        pair = add(keep, got).astype(BF16)
        mine, other = of_core(pair), of_core(pair, True)
        there, here, across = yield trio(mine, other, "zlo")
        own = by_core(add(mine, there), add(here, across)).astype(BF16)
        return (yield from ring_gather_steps(own, "y"))

    def ff_steps(sums):
        own = yield from ring_scatter_steps([sums[i] for i in range(4)], "z")
        own = own.astype(BF16)
        pair, down = own[: 2 * FFL].reshape(2, FFL, B), own[2 * FFL :]
        mine, other = of_core(pair), of_core(pair, True)
        there, here, across = yield trio(jnp.concatenate([mine, down], axis=0), other, "zlo")
        both = by_zlo(by_core(mine, here), by_core(there[:FFL], across))
        both = jnp.concatenate([both, by_zlo(down, there[FFL:])[:, None]], axis=1)
        return (yield from ring_gather_steps(both, "y"))

    x_low = layer_input[0]
    frequency = theta ** (-jnp.arange(0, HD, 2).astype(F32) / HD)
    angles = positions[0].astype(F32)[:, None] * frequency
    tables = []
    for table in (jnp.cos(angles), jnp.sin(angles)):
        high = lax.reduce_precision(table, 8, 7)
        tables += [high.astype(BF16), (table - high).astype(BF16)]
    tokens = Flow(gather_steps(jnp.concatenate([x_low, *tables], axis=1)))
    grads = Flow(gather_steps(out_grad[0]))
    qkv_mine, qkv_other = prepare_qkv(place, w_query, w_key, w_value, attn_gain[:, None])
    qkv_mine, qkv_got, gain_two, w_out = stage([tokens], qkv_mine, swap_core(qkv_other), mlp_gain[:, None], w_output)

    columns = Flow(column_steps(qkv_mine, qkv_got))
    o_rows = lax.all_to_all(w_out.reshape(B, 16, B).transpose(1, 0, 2), FSDP, 0, 0, tiled=True)
    gain_two, x_low, o_rows = stage([tokens, columns], gain_two, x_low, o_rows)

    ff_mine, ff_other, ff_down = prepare_ff(place, w_gate, w_up, w_down, gain_two)
    inputs = x_low.astype(F32)
    scale_one = lax.rsqrt(jnp.mean(inputs * inputs, axis=-1, keepdims=True) + eps)
    o_rows = o_rows.reshape(D, B)
    mine, other = own_rows(o_rows, y, core, HEADS * HD), own_rows(o_rows, y, 1 - core, HEADS * HD)
    scale_one, mine, other, ff_mine, ff_got, ff_down = stage(
        [tokens, columns, grads], scale_one, mine, other, ff_mine, swap_core(ff_other), ff_down
    )

    outputs = Flow(output_steps(mine, other))
    ff_mine, ff_got, ff_down = stage([tokens, columns, outputs], ff_mine, ff_got, ff_down)

    hidden_rows = Flow(hidden_steps(ff_mine, ff_got, ff_down))
    x_pieces = tokens.result
    query, key_value, scale_all, cosine, sine, qkv_full = project_qkv(place, x_pieces, columns.result)
    query, key_value = stage([hidden_rows, outputs, grads], query, key_value)

    earlier = lax.ppermute(key_value, "zlo", [(0, 1)])
    query, key_value, earlier = stage([outputs, hidden_rows], query, key_value, earlier)
    ff_all = lax.all_gather(hidden_rows.result, "x", axis=0, tiled=False)

    key_value = jnp.concatenate([earlier, key_value], axis=1)
    mixed, log_total, *parts, o_full = attention(place, outputs.result, query, key_value)
    parts = stage([grads], *parts)
    sums = Flow(scatter_steps(parts))
    stage([sums, grads])
    grad_pieces = grads.result
    for _ in range(3):
        stage([sums])
    hidden = inputs + sums.result
    scale_two = lax.rsqrt(jnp.mean(hidden * hidden, axis=-1, keepdims=True) + eps)
    normed = Flow(gather_steps((hidden * scale_two).astype(BF16)))
    for _ in range(4):
        stage([normed])
    normed_pieces = normed.result

    activation, act_t, gate_t, up_t, *parts, down_full = feed_forward(place, normed_pieces, grad_pieces, ff_all)
    sums = Flow(scatter_steps(parts))
    (act_t,) = stage([sums], act_t)
    down_terms = ff_terms(down_kernel, place, grad_pieces, (act_t,), FFL, "down_terms")
    down_terms, gate_t = stage([sums], down_terms, gate_t)
    down_sum = lax.psum_scatter(down_terms, "x", scatter_dimension=0, tiled=True)[0]
    gate_up_terms = ff_terms(gate_up_kernel, place, normed_pieces, (gate_t, up_t), 2 * FFL, "gate_up_terms")
    (gate_up_terms,) = stage([sums], gate_up_terms)
    gate_up_sum = lax.psum_scatter(gate_up_terms, "x", scatter_dimension=0, tiled=True)[0]
    stage([sums])

    grad_normed_two = sums.result
    mean_two = jnp.mean(grad_normed_two * hidden, axis=-1, keepdims=True)
    grad_hidden = (
        out_grad[0].astype(F32)
        + scale_two * grad_normed_two
        - hidden * (scale_two * scale_two * scale_two) * mean_two
    )
    hidden_grads = Flow(gather_steps(grad_hidden.astype(BF16)))
    (activation,) = stage([hidden_grads], activation)
    down_parts = project(activation, down_full)
    down_parts = stage([hidden_grads], *down_parts)
    result = Flow(scatter_steps(down_parts))
    stage([hidden_grads, result])
    stage([hidden_grads])

    hidden_grad_pieces = hidden_grads.result
    grad_query, grad_earlier, grad_own = attention_back(
        place, hidden_grad_pieces, query, key_value, log_total, o_full
    )
    grad_query, grad_earlier, grad_own, mixed = stage([result], grad_query, grad_earlier, grad_own, mixed)
    later = lax.ppermute(grad_earlier, "zlo", [(1, 0)])
    output_terms = attention_terms(place, hidden_grad_pieces, mixed.reshape(2 * HALF, HEADS * HD), "output_terms")
    later, grad_query, output_terms, down_sum, gate_up_sum = stage(
        [result], later, grad_query, output_terms, down_sum, gate_up_sum
    )
    output_sum = lax.psum_scatter(output_terms, "x", scatter_dimension=0, tiled=True)[0]
    ff_sums = Flow(ff_steps(jnp.concatenate([gate_up_sum, down_sum], axis=1)))
    *parts, grad_t = qkv_back(grad_query, grad_own, later, cosine, sine, scale_all, qkv_full)
    *parts, grad_t = stage([ff_sums, result], *parts, grad_t)

    sums = Flow(scatter_steps(parts))
    terms = attention_terms(place, x_pieces, grad_t, "qkv_terms")
    terms, output_sum = stage([sums, ff_sums], terms, output_sum)
    attention_sum = lax.psum_scatter(terms, "x", scatter_dimension=0, tiled=True)[0]
    output_sums = Flow(attention_steps(output_sum))
    (attention_sum,) = stage([sums, ff_sums, output_sums], attention_sum)
    attention_sums = Flow(attention_steps(attention_sum))
    stage([sums, output_sums, attention_sums])
    stage([sums, output_sums, attention_sums, ff_sums])
    grad_normed = sums.result
    mean_one = jnp.mean(grad_normed * inputs, axis=-1, keepdims=True)
    input_grad = (
        grad_hidden
        + scale_one * grad_normed
        - inputs * (scale_one * scale_one * scale_one) * mean_one
    )
    input_grad = input_grad.astype(BF16)
    stage([attention_sums, output_sums, ff_sums])

    ring = jnp.roll(jnp.stack(whole_ring(output_sums.result)), y, axis=0).reshape(16, B, B)
    output_grad = lax.all_to_all(ring, FSDP, 0, 0, tiled=True)
    gain_two = mlp_gain[:, None]
    pieces = ff_sums.result
    gate_grad, gate_gain = finish_hidden(place, pieces, 0, w_gate, gain_two)
    up_grad, up_gain = finish_hidden(place, pieces, 1, w_up, gain_two)
    down_grad = finish_down(place, pieces)
    gate_grad, up_grad, down_grad = stage([attention_sums], gate_grad, up_grad, down_grad)

    query_grad, key_grad, value_grad, attn_gain_grad = finish_attention(
        place, whole_ring(attention_sums.result), w_query, w_key, w_value, attn_gain[:, None]
    )
    output_grad = finish_output(output_grad)
    return (
        (hidden + result.result).astype(BF16)[None],
        input_grad[None],
        attn_gain_grad[:, 0],
        query_grad,
        key_grad,
        value_grad,
        output_grad,
        (gate_gain + up_gain)[:, 0],
        gate_grad,
        up_grad,
        down_grad,
    )


def solution(mesh):
    split = Mesh(mesh.devices.reshape(2, 4, 2, 4, 2), AXES)
    tokens = P(FSDP, SEQ, None)
    rows = P(FSDP, None)
    gain = P(FSDP)
    in_specs = (
        tokens, P(FSDP, SEQ), gain, rows, rows, rows, rows, gain, rows, rows, rows, tokens,
    )
    out_specs = (tokens, tokens, gain, rows, rows, rows, rows, gain, rows, rows, rows)
    return jax.shard_map(
        on_device, mesh=split, in_specs=in_specs, out_specs=out_specs, check_vma=False
    )
```

```python
import jax
import jax.numpy as jnp
from jax import lax
from jax.experimental import pallas as pl
from jax.experimental.pallas import tpu as pltpu
from jax.sharding import Mesh
from jax.sharding import PartitionSpec as P

H = 32
KV = 4
HD = 64
D = 2048
FF = 5632
B = 128
HALF = 512
HEADS = 4
FFL = 704
PIECE = 88

eps = 1e-05
theta = 10000.0
F32 = jnp.float32
BF16 = jnp.bfloat16
AXES = ("zlo", "y", "zhi", "x", "core")
FSDP = ("zhi", "x", "core")
SEQ = ("zlo", "y")


def matmul(left, right):
    return jnp.dot(left, right, preferred_element_type=F32)


def times_transposed(left, right):
    return lax.dot_general(left, right, (((1,), (1,)), ((), ())), preferred_element_type=F32)


def outer_sum(left, right):
    return lax.dot_general(left, right, (((0,), (0,)), ((), ())), preferred_element_type=F32)


def shift(value, axis, by):
    if axis == "z":
        at = [2 * (z % 2) + z // 2 for z in range(4)]
        return lax.ppermute(value, ("zlo", "zhi"), [(at[z], at[(z + by) % 4]) for z in range(4)])
    size = lax.axis_size(axis)
    return lax.ppermute(value, axis, [(i, (i + by) % size) for i in range(size)])


def swap_core(value):
    return shift(value, "core", 1)


def small_gather(block, axis):
    return shift(block, axis, -1), shift(block, axis, 2), shift(block, axis, 1)


def tie(*values):
    return lax.optimization_barrier(values)


def add(left, right):
    return left.astype(F32) + right.astype(F32)


def along_y(value):
    pairs = []
    for i in range(4):
        pairs.append((2 * i, 2 * ((i + 1) % 4)))
        pairs.append((2 * i + 1, 2 * ((i + 3) % 4) + 1))
    return lax.ppermute(value, ("y", "core"), pairs)


def send_half(got):
    core = lax.axis_index("core")
    return lax.dynamic_slice_in_dim(got, core * (B // 2), B // 2, 1)


FLIPPED = (0, 0, 1, 0, 1)
LENGTHS = (B, B, B, B // 2, B // 2)


def put_tokens(refs, rows_ref, sems, start):
    lanes = pl.ds(0, rows_ref.shape[1])
    copies = []
    row = 0
    for s in range(2):
        for ref, flip, length in zip(refs, FLIPPED, LENGTHS):
            copies.append(
                pltpu.make_async_copy(
                    ref.at[s ^ flip, :, lanes], rows_ref.at[pl.ds(row, length)], sems.at[start + len(copies)]
                )
            )
            row += length
    return copies


TILE = 256
WIDE = D + B
VMEM_LIMIT = 56 * 2**20
ANYWHERE = pl.BlockSpec(memory_space=pl.ANY)


def params(*kinds):
    return pltpu.CompilerParams(dimension_semantics=kinds or None, vmem_limit_bytes=VMEM_LIMIT)


def cost(flops, megabytes):
    return pl.CostEstimate(flops=flops, bytes_accessed=int(megabytes * 2**20), transcendentals=0)


def shaped(*shape, kind=BF16):
    return jax.ShapeDtypeStruct(shape, kind)


PARTS = ((B, False), (B, True), (B, False), (B // 2, False), (B // 2, True))
PART_SHAPES = [jax.ShapeDtypeStruct((2, n, D), BF16) for n, _ in PARTS]


def part_specs(steps):
    def of(turn):
        return lambda i, *_: (1 - i // steps if turn else i // steps, 0, 0)

    return [pl.BlockSpec((1, n, D), of(turn)) for n, turn in PARTS]


def put_parts(step, tile, refs):
    @pl.when(step % 2 == 0)
    def _():
        refs[0][0] = tile[:B]
        refs[1][0] = tile[B:]

    @pl.when(step % 2 == 1)
    def _():
        refs[2][0] = tile[:B]
        refs[3][0] = tile[B : B + B // 2]
        refs[4][0] = tile[B + B // 2 :]


def put_rows(rows, refs):
    row = 0
    for ref, (length, _) in zip(refs, PARTS):
        ref[0] = rows[row : row + length]
        row += length


def turned(values):
    lane = lax.broadcasted_iota(jnp.int32, values.shape, 1) % HD
    return jnp.where(lane < HD // 2, -pltpu.roll(values, 2 * HD - HD // 2, 1), pltpu.roll(values, HD // 2, 1))


def lane_block(zhi, x, core):
    return pl.ds(pl.multiple_of((zhi * 8 + x * 2 + core) * B, B), B)


def put_columns(place, refs, into, sems, start):
    copies = []
    for ref, by, first in zip(refs, (0, 1, 2, 2, 3), (0, 0, 0, 1, 0)):
        for i in range(ref.shape[0]):
            for core in range(2):
                lanes = lane_block(first + i, (place[3] + by) % 4, core)
                copies.append(
                    pltpu.make_async_copy(ref.at[i, core], into.at[:, lanes], sems.at[start + len(copies)])
                )
    return copies


def prepare_qkv_kernel(place, q_mine, q_other, w_key, w_value, gain, mine_ref, other_ref, k_rows, v_rows):
    scale = gain[...]
    k_rows[...] = (w_key[...].astype(F32) * scale).T
    v_rows[...] = (w_value[...].astype(F32) * scale).T
    rows = pl.ds(pl.multiple_of(place[1] * HD, HD), HD)
    for source, out in ((q_mine, mine_ref), (q_other, other_ref)):
        out[: HEADS * HD] = (source[...].astype(F32) * scale).T.astype(BF16)
        out[HEADS * HD : (HEADS + 1) * HD] = k_rows[rows].astype(BF16)
        out[(HEADS + 1) * HD :] = v_rows[rows].astype(BF16)


QKV = (HEADS + 2) * HD


def prepare_qkv(place, w_query, w_key, w_value, gain):
    whole = lambda *shape: pl.BlockSpec(shape, lambda i, p: (0,) * len(shape))
    return pl.pallas_call(
        prepare_qkv_kernel,
        grid_spec=pltpu.PrefetchScalarGridSpec(
            num_scalar_prefetch=1,
            grid=(1,),
            in_specs=[
                pl.BlockSpec((B, HEADS * HD), lambda i, p: (0, 2 * p[1] + p[2])),
                pl.BlockSpec((B, HEADS * HD), lambda i, p: (0, 2 * p[1] + 1 - p[2])),
                whole(B, KV * HD), whole(B, KV * HD), whole(B, 1),
            ],
            out_specs=[whole(QKV, B), whole(QKV, B)],
            scratch_shapes=[pltpu.VMEM((KV * HD, B), F32), pltpu.VMEM((KV * HD, B), F32)],
        ),
        out_shape=[shaped(QKV, B), shaped(QKV, B)],
        compiler_params=params("arbitrary"),
        cost_estimate=cost(0, 1),
        name="prepare_qkv",
    )(place, w_query, w_query, w_key, w_value, gain)


def prepare_ff_kernel(place, w_gate, w_up, w_down, gain, mine_ref, other_ref, down_ref, picked, rows, down_rows, sems):
    zlo, y, core = place[0], place[1], place[2]
    down = pltpu.make_async_copy(
        w_down.at[:, pl.ds(pl.multiple_of(zlo * (D // 2), D // 2), D // 2)], down_rows, sems.at[1]
    )
    down.start()

    @pl.when(zlo == 0)
    def _():
        copy = pltpu.make_async_copy(w_gate, picked, sems.at[0])
        copy.start()
        copy.wait()

    @pl.when(zlo == 1)
    def _():
        copy = pltpu.make_async_copy(w_up, picked, sems.at[0])
        copy.start()
        copy.wait()

    scale = gain[...]
    for i in range(FF // B):
        rows[i * B : (i + 1) * B] = (picked[:, i * B : (i + 1) * B].astype(F32) * scale).T
    for which, out in ((core, mine_ref), (1 - core, other_ref)):
        slabs = []
        for zx in range(8):
            at = pl.multiple_of(zx * 2 * 4 * PIECE + which * 4 * PIECE + y * PIECE, 8)
            slabs.append(rows[pl.ds(at, PIECE)])
        out[...] = jnp.concatenate(slabs, axis=0).astype(BF16)
    down.wait()
    for t in range(8):
        rows[t * 4 * PIECE : (t + 1) * 4 * PIECE] = down_rows[:, t * B : (t + 1) * B].astype(F32)
    slabs = [rows[pl.ds(pl.multiple_of(t * 4 * PIECE + y * PIECE, 8), PIECE)] for t in range(8)]
    down_ref[...] = jnp.concatenate(slabs, axis=0).astype(BF16)


def prepare_ff(place, w_gate, w_up, w_down, gain):
    return pl.pallas_call(
        prepare_ff_kernel,
        grid_spec=pltpu.PrefetchScalarGridSpec(
            num_scalar_prefetch=1,
            grid=(1,),
            in_specs=[ANYWHERE, ANYWHERE, ANYWHERE, pl.BlockSpec((B, 1), lambda i, p: (0, 0))],
            out_specs=[pl.BlockSpec((FFL, B), lambda i, p: (0, 0))] * 3,
            scratch_shapes=[
                pltpu.VMEM((B, FF), BF16),
                pltpu.VMEM((FF, B), F32),
                pltpu.VMEM((4 * PIECE, D // 2), BF16),
                pltpu.SemaphoreType.DMA((2,)),
            ],
        ),
        out_shape=[shaped(FFL, B)] * 3,
        compiler_params=params("arbitrary"),
        cost_estimate=cost(0, 6),
        name="prepare_ff",
    )(place, w_gate, w_up, w_down, gain)


def project_qkv_kernel(*refs):
    place, x_refs, w_refs = refs[0], refs[1:6], refs[6:11]
    query_ref, kv_ref, scale_ref, cosine_ref, sine_ref, w_out, rows, weights, sems = refs[11:]
    step = pl.program_id(0)
    tokens = put_tokens(x_refs, rows, sems, 0)
    columns = put_columns(place, w_refs, weights, sems, 10)
    back = pltpu.make_async_copy(weights, w_out, sems.at[26])

    @pl.when(step == 0)
    def _():
        for copy in columns + tokens:
            copy.start()
        for copy in columns:
            copy.wait()
        back.start()
        for copy in tokens:
            copy.wait()

    at = pl.ds(pl.multiple_of(step * TILE, TILE), TILE)
    tile = rows[at, :D]
    wide = tile.astype(F32)
    scale = lax.rsqrt(jnp.mean(wide * wide, axis=-1, keepdims=True) + eps)
    scale_ref[...] = scale
    pre = times_transposed(tile, weights[...]) * scale
    tables = rows[at, D:].astype(F32)
    tables = tables + pltpu.roll(tables, B - HD // 2, 1)
    cosine = jnp.concatenate([tables[:, : HD // 2]] * 4, axis=1)
    sine = jnp.concatenate([tables[:, HD : HD + HD // 2]] * 4, axis=1)
    cosine_ref[...] = cosine
    sine_ref[...] = sine
    for i in range(2):
        part = pre[:, i * 2 * HD : (i + 1) * 2 * HD]
        part = (part * cosine + turned(part) * sine).astype(BF16) * HD ** (-0.5)
        query_ref[0, 2 * i] = part[:, :HD]
        query_ref[0, 2 * i + 1] = part[:, HD:]
    part = pre[:, HEADS * HD :]
    lane = lax.broadcasted_iota(jnp.int32, part.shape, 1)
    kv_ref[0] = jnp.where(lane < HD, part * cosine + turned(part) * sine, part).astype(BF16)

    @pl.when(step == 3)
    def _():
        back.wait()


def project_qkv(place, x_pieces, w_pieces):
    tile = lambda lanes: pl.BlockSpec((TILE, lanes), lambda i, p: (i, 0))
    return pl.pallas_call(
        project_qkv_kernel,
        grid_spec=pltpu.PrefetchScalarGridSpec(
            num_scalar_prefetch=1,
            grid=(4,),
            in_specs=[ANYWHERE] * 10,
            out_specs=[
                pl.BlockSpec((1, HEADS, TILE, HD), lambda i, p: (i // 2, 0, i % 2, 0)),
                pl.BlockSpec((1, TILE, 2 * HD), lambda i, p: (i // 2, i % 2, 0)),
                tile(1), tile(2 * HD), tile(2 * HD),
                ANYWHERE,
            ],
            scratch_shapes=[
                pltpu.VMEM((2 * HALF, WIDE), BF16),
                pltpu.VMEM((QKV, D), BF16),
                pltpu.SemaphoreType.DMA((27,)),
            ],
        ),
        out_shape=[
            shaped(2, HEADS, HALF, HD), shaped(2, HALF, 2 * HD), shaped(2 * HALF, 1, kind=F32),
            shaped(2 * HALF, 2 * HD, kind=F32), shaped(2 * HALF, 2 * HD, kind=F32), shaped(QKV, D),
        ],
        compiler_params=params("arbitrary"),
        cost_estimate=cost(2 * 2 * HALF * QKV * D, 8),
        name="project_qkv",
    )(place, *x_pieces, *w_pieces)


def project_kernel(left_ref, weight_ref, *parts):
    put_parts(pl.program_id(0), matmul(left_ref[...], weight_ref[...]).astype(BF16), parts)


def project(left, weight):
    depth = left.shape[1]
    return pl.pallas_call(
        project_kernel,
        grid=(4,),
        in_specs=[pl.BlockSpec((TILE, depth), lambda i: (i, 0)), pl.BlockSpec((depth, D), lambda i: (0, 0))],
        out_specs=part_specs(2),
        out_shape=PART_SHAPES,
        compiler_params=params("arbitrary"),
        cost_estimate=cost(2 * 2 * HALF * depth * D, 8),
        name="project",
    )(left, weight)


def put_term(left, rows, term_ref):
    def one(i, carry):
        term = matmul(left, rows[:, pl.ds(pl.multiple_of(i * 4 * B, 4 * B), 4 * B)]).astype(BF16)
        for j in range(2):
            zx = 2 * i + j
            term_ref[zx % 4, zx // 4, 0] = term[:, 2 * j * B : (2 * j + 1) * B]
            term_ref[zx % 4, zx // 4, 1] = term[:, (2 * j + 1) * B : (2 * j + 2) * B]
        return carry

    lax.fori_loop(0, 4, one, 0)


def qkv_back_kernel(grad_q_ref, own_ref, later_ref, cosine_ref, sine_ref, scale_ref, weight_ref, *outs):
    parts, turned_ref = outs[:5], outs[5]
    cosine, sine = cosine_ref[...], sine_ref[...]
    lane = lax.broadcasted_iota(jnp.int32, cosine.shape, 1)
    pieces = []
    for i in range(2):
        part = grad_q_ref[0, :, i * 2 * HD : (i + 1) * 2 * HD]
        pieces.append(part * cosine - turned(part * sine))
    part = own_ref[0] + later_ref[0].astype(F32)
    pieces.append(jnp.where(lane < HD, part * cosine - turned(part * sine), part))
    grad_pre = jnp.concatenate(pieces, axis=1)
    put_parts(pl.program_id(0), matmul(grad_pre.astype(BF16), weight_ref[...]).astype(BF16), parts)
    turned_ref[...] = (grad_pre * scale_ref[...]).T.astype(BF16)


def qkv_back(grad_query, own, later, cosine, sine, scale, weight):
    tile = lambda lanes: pl.BlockSpec((TILE, lanes), lambda i: (i, 0))
    half = lambda lanes: pl.BlockSpec((1, TILE, lanes), lambda i: (i // 2, i % 2, 0))
    return pl.pallas_call(
        qkv_back_kernel,
        grid=(4,),
        in_specs=[
            half(HEADS * HD), half(2 * HD), half(2 * HD), tile(2 * HD), tile(2 * HD), tile(1),
            pl.BlockSpec((QKV, D), lambda i: (0, 0)),
        ],
        out_specs=part_specs(2) + [pl.BlockSpec((QKV, TILE), lambda i: (0, i))],
        out_shape=PART_SHAPES + [shaped(QKV, 2 * HALF)],
        compiler_params=params("arbitrary"),
        cost_estimate=cost(2 * 2 * HALF * QKV * D, 9),
        name="qkv_back",
    )(grad_query, own, later, cosine, sine, scale, weight)


def attention_term_kernel(*refs):
    token_refs, left_ref = refs[1:6], refs[6]
    term_ref, rows, sems = refs[-3:]
    copies = put_tokens(token_refs, rows, sems, 0)
    for copy in copies:
        copy.start()
    left = left_ref[...]
    if left.shape[0] == 2 * HALF:
        left = left.T
    for copy in copies:
        copy.wait()
    put_term(left, rows, term_ref)


def attention_terms(place, pieces, left, name):
    whole = lambda *shape: pl.BlockSpec(shape, lambda i, p: (0,) * len(shape))
    rows = min(left.shape)
    return pl.pallas_call(
        attention_term_kernel,
        grid_spec=pltpu.PrefetchScalarGridSpec(
            num_scalar_prefetch=1,
            grid=(1,),
            in_specs=[ANYWHERE] * 5 + [whole(*left.shape)],
            out_specs=whole(4, 2, 2, rows, B),
            scratch_shapes=[pltpu.VMEM((2 * HALF, D), BF16), pltpu.SemaphoreType.DMA((10,))],
        ),
        out_shape=shaped(4, 2, 2, rows, B),
        compiler_params=params("arbitrary"),
        cost_estimate=cost(2 * 2 * HALF * rows * D, 7),
        name=name,
    )(place, *pieces, left)


def token_places(at, y, core):
    step = 1 - 2 * core
    block = jnp.where(
        at < B, y, jnp.where(at < 2 * B, y + 4 - step, jnp.where(at < 3 * B, y + 4 + step, y + 2))
    )
    row = at % B
    row = jnp.where(at < 3 * B, row, (row + core * (B // 2)) % B)
    return (block % 4) * B + row


def set_bias(place_ref, bias_ref):
    zlo, y, core = place_ref[0], place_ref[1], place_ref[2]
    key_at = token_places(lax.broadcasted_iota(jnp.int32, (HALF, 1), 0), y, core)
    query_at = token_places(lax.broadcasted_iota(jnp.int32, (1, HALF), 1), y, core)
    bias_ref[:HALF, :] = jnp.broadcast_to(jnp.where(zlo == 1, 0.0, -1e30), (HALF, HALF))
    bias_ref[HALF:, :] = jnp.where(key_at <= query_at, 0.0, -1e30)


def attention_kernel(place_ref, *refs):
    w_refs, query_ref, kv_ref, mixed_ref, log_ref = refs[:5], *refs[5:9]
    parts, w_out, bias_ref, weight, sems = refs[9:14], *refs[14:]
    columns = put_columns(place_ref, w_refs, weight, sems, 0)
    back = pltpu.make_async_copy(weight, w_out, sems.at[16])

    @pl.when(pl.program_id(0) == 0)
    def _():
        for copy in columns:
            copy.start()
        set_bias(place_ref, bias_ref)
        for copy in columns:
            copy.wait()
        back.start()

    key, value = kv_ref[0, :, :HD], kv_ref[0, :, HD:]
    for head in range(HEADS):
        scores = times_transposed(key, query_ref[0, head]) + bias_ref[...]
        top = jnp.max(scores, axis=0, keepdims=True)
        weights = jnp.exp(scores - top)
        total = jnp.sum(weights, axis=0, keepdims=True)
        low = (weights * (1.0 / total)).astype(BF16)
        mixed_ref[0, :, head * HD : (head + 1) * HD] = outer_sum(value, low).T.astype(BF16)
        log_ref[0, head] = top + jnp.log(total)
    put_rows(matmul(mixed_ref[0], weight[...]).astype(BF16), parts)

    @pl.when(pl.program_id(0) == 1)
    def _():
        back.wait()


def attention_back_kernel(place_ref, *refs):
    grad_refs, query_ref, kv_ref, log_ref, weight_ref = refs[:5], *refs[5:9]
    grad_query_ref, earlier_ref, own_ref, bias_ref, rows, sems = refs[9:]
    step = pl.program_id(0)
    copies = put_tokens(grad_refs, rows, sems, 0)

    @pl.when(step == 0)
    def _():
        for copy in copies:
            copy.start()
        set_bias(place_ref, bias_ref)
        for copy in copies:
            copy.wait()

    hidden = rows[pl.ds(pl.multiple_of(step * HALF, HALF), HALF), :]
    grads = times_transposed(hidden, weight_ref[...]).astype(BF16)
    key, value = kv_ref[0, :, :HD], kv_ref[0, :, HD:]
    grad_key = jnp.zeros((2 * HALF, HD), F32)
    grad_value = jnp.zeros((2 * HALF, HD), F32)
    for head in range(HEADS):
        lanes = slice(head * HD, (head + 1) * HD)
        query, grad = query_ref[0, head], grads[:, lanes]
        weights = jnp.exp(times_transposed(key, query) + bias_ref[...] - log_ref[0, head])
        grad_weights = times_transposed(value, grad)
        delta = jnp.sum(weights * grad_weights, axis=0, keepdims=True)
        grad_scores = (weights * (grad_weights - delta)).astype(BF16)
        grad_query_ref[0, :, lanes] = outer_sum(key, grad_scores).T * HD ** (-0.5)
        grad_key += matmul(grad_scores, query)
        grad_value += matmul(weights.astype(BF16), grad)
    total = jnp.concatenate([grad_key, grad_value], axis=1)
    earlier_ref[0] = total[:HALF].astype(BF16)
    own_ref[0] = total[HALF:]


def sequence_block(*tail):
    return pl.BlockSpec((1,) + tail, lambda s, place: (s,) + (0,) * len(tail))


def attention_call(kernel, in_specs, out_specs, out_shape, scratch, flops, name):
    return pl.pallas_call(
        kernel,
        grid_spec=pltpu.PrefetchScalarGridSpec(
            num_scalar_prefetch=1,
            grid=(2,),
            in_specs=in_specs,
            out_specs=out_specs,
            scratch_shapes=[pltpu.VMEM((2 * HALF, HALF), F32)] + scratch,
        ),
        out_shape=out_shape,
        compiler_params=params("arbitrary"),
        cost_estimate=cost(flops * 8 * 2 * HALF * HALF * HD * 2, 8),
        name=name,
    )


def attention(place, w_pieces, query, kv):
    return attention_call(
        attention_kernel,
        [ANYWHERE] * 5 + [sequence_block(HEADS, HALF, HD), sequence_block(2 * HALF, 2 * HD)],
        [sequence_block(HALF, HEADS * HD), sequence_block(HEADS, 1, HALF)]
        + part_specs(1)
        + [ANYWHERE],
        [shaped(2, HALF, HEADS * HD), shaped(2, HEADS, 1, HALF, kind=F32)] + PART_SHAPES + [shaped(HEADS * HD, D)],
        [pltpu.VMEM((HEADS * HD, D), BF16), pltpu.SemaphoreType.DMA((17,))],
        3,
        "attention",
    )(place, *w_pieces, query, kv)


def attention_back(place, grad_pieces, query, kv, log_total, weight):
    return attention_call(
        attention_back_kernel,
        [ANYWHERE] * 5
        + [
            sequence_block(HEADS, HALF, HD), sequence_block(2 * HALF, 2 * HD),
            sequence_block(HEADS, 1, HALF), pl.BlockSpec((HEADS * HD, D), lambda s, place: (0, 0)),
        ],
        [sequence_block(HALF, HEADS * HD), sequence_block(HALF, 2 * HD), sequence_block(HALF, 2 * HD)],
        [
            shaped(2, HALF, HEADS * HD, kind=F32),
            shaped(2, HALF, 2 * HD),
            shaped(2, HALF, 2 * HD, kind=F32),
        ],
        [pltpu.VMEM((2 * HALF, D), BF16), pltpu.SemaphoreType.DMA((10,))],
        6,
        "attention_back",
    )(place, *grad_pieces, query, kv, log_total, weight)


def finish_attention_kernel(place, *refs):
    piece_refs, w_query, w_key, w_value, gain_ref = refs[:4], *refs[4:8]
    query_out, key_out, value_out, gain_out, rows = refs[8:]
    for ref, by in zip(piece_refs, range(4)):
        at_y = (place[1] + by) % 4
        for c in range(2):
            piece = ref[c].astype(F32)
            rows[pl.ds(pl.multiple_of((2 * at_y + c) * HEADS * HD, HEADS * HD), HEADS * HD)] = piece[: HEADS * HD]
        both = ref[0].astype(F32) + ref[1].astype(F32)
        at = pl.multiple_of(H * HD + at_y * HD, HD)
        rows[pl.ds(at, HD)] = both[HEADS * HD : (HEADS + 1) * HD]
        rows[pl.ds(at + KV * HD, HD)] = both[(HEADS + 1) * HD :]
    gain = gain_ref[...]
    total = jnp.zeros((B, 1), F32)
    row = 0
    for weight, out in ((w_query, query_out), (w_key, key_out), (w_value, value_out)):
        for i in range(out.shape[1] // B):
            lanes = slice(i * B, (i + 1) * B)
            block = rows[row : row + B].T
            total = total + jnp.sum(block * weight[:, lanes].astype(F32), axis=1, keepdims=True)
            out[:, lanes] = block * gain
            row += B
    gain_out[...] = total


def finish_attention(place, pieces, w_query, w_key, w_value, gain):
    whole = lambda *shape: pl.BlockSpec(shape, lambda i, p: (0,) * len(shape))
    kv = KV * HD
    return pl.pallas_call(
        finish_attention_kernel,
        grid_spec=pltpu.PrefetchScalarGridSpec(
            num_scalar_prefetch=1,
            grid=(1,),
            in_specs=[whole(2, QKV, B)] * 4 + [whole(B, D), whole(B, kv), whole(B, kv), whole(B, 1)],
            out_specs=[whole(B, D), whole(B, kv), whole(B, kv), whole(B, 1)],
            scratch_shapes=[pltpu.VMEM((D + 2 * kv, B), F32)],
        ),
        out_shape=[
            shaped(B, D, kind=F32), shaped(B, kv, kind=F32), shaped(B, kv, kind=F32), shaped(B, 1, kind=F32),
        ],
        compiler_params=params("arbitrary"),
        cost_estimate=cost(0, 4),
        name="finish_attention",
    )(place, *pieces, w_query, w_key, w_value, gain)


def finish_output_kernel(blocks, out):
    for i in range(16):
        out[:, i * B : (i + 1) * B] = blocks[i].astype(F32)


def finish_output(blocks):
    return pl.pallas_call(
        finish_output_kernel,
        out_shape=shaped(B, D, kind=F32),
        compiler_params=params(),
        cost_estimate=cost(0, 2),
        name="finish_output",
    )(blocks)


def feed_forward_kernel(*refs):
    place, token_refs, grad_refs, ff_ref = refs[0], refs[1:6], refs[6:11], refs[11]
    act_ref, act_t, gate_t, up_t = refs[12:16]
    parts, down_out = refs[16:21], refs[21]
    rows_h, rows_g, gate_up, down, slabs, sems = refs[22:]
    step = pl.program_id(0)
    tokens = put_tokens(token_refs, rows_h, sems, 0)
    grads = put_tokens(grad_refs, rows_g, sems, 10)
    weights, loads = [], []
    for x in range(4):
        for by in range(4):
            z = (2 * place[4] + place[0] + by) % 4
            zhi, zlo = z // 2, z % 2
            for core in range(2):
                weights.append(
                    pltpu.make_async_copy(
                        ff_ref.at[x, by, pl.ds(core * FFL, FFL)],
                        gate_up.at[zlo, :, lane_block(zhi, x, core)],
                        sems.at[20 + len(weights)],
                    )
                )
            loads.append(
                pltpu.make_async_copy(
                    ff_ref.at[x, by, pl.ds(2 * FFL, FFL)], slabs.at[zlo, zhi * 4 + x], sems.at[52 + len(loads)]
                )
            )
    back = pltpu.make_async_copy(down, down_out, sems.at[68])

    @pl.when(step == 0)
    def _():
        for copy in tokens + weights + loads + grads:
            copy.start()
        for copy in tokens + weights:
            copy.wait()

    rows = pl.ds(pl.multiple_of(step * HALF, HALF), HALF)
    normed = rows_h[rows, :]
    gate_pre = times_transposed(normed, gate_up[0])
    upward = times_transposed(normed, gate_up[1])

    @pl.when(step == 0)
    def _():
        for copy in loads:
            copy.wait()

        def put(q, carry):
            for half in range(2):
                for p in range(4):
                    one = slabs[half, 2 * q, 2 * p * PIECE : 2 * (p + 1) * PIECE, :].astype(F32)
                    two = slabs[half, 2 * q + 1, 2 * p * PIECE : 2 * (p + 1) * PIECE, :].astype(F32)
                    lane = (half * 8 + 2 * p) * B
                    rows = pl.ds(pl.multiple_of(q * 2 * PIECE, 16), 2 * PIECE)
                    down[rows, lane : lane + B] = jnp.concatenate([one[:PIECE], two[:PIECE]], axis=0).astype(BF16)
                    down[rows, lane + B : lane + 2 * B] = jnp.concatenate(
                        [one[PIECE:], two[PIECE:]], axis=0
                    ).astype(BF16)
            return carry

        lax.fori_loop(0, 4, put, 0)
        back.start()
        for copy in grads:
            copy.wait()

    grad_act = times_transposed(rows_g[rows, :], down[...])
    sigmoid = 1.0 / (1.0 + jnp.exp(-gate_pre))
    silu = gate_pre * sigmoid
    activation = silu * upward
    grad_up = grad_act * silu
    grad_gate = grad_act * upward * (sigmoid * (1.0 + gate_pre * (1.0 - sigmoid)))
    part = matmul(grad_gate.astype(BF16), gate_up[0]) + matmul(grad_up.astype(BF16), gate_up[1])
    put_rows(part.astype(BF16), parts)
    act_ref[...] = activation.astype(BF16)
    act_t[...] = activation.T.astype(BF16)
    gate_t[...] = grad_gate.T.astype(BF16)
    up_t[...] = grad_up.T.astype(BF16)

    @pl.when(step == 1)
    def _():
        back.wait()


def feed_forward(place, tokens, grads, ff_all):
    turned_spec = pl.BlockSpec((FFL, HALF), lambda i, p: (0, i))
    turned_shape = shaped(FFL, 2 * HALF)
    return pl.pallas_call(
        feed_forward_kernel,
        grid_spec=pltpu.PrefetchScalarGridSpec(
            num_scalar_prefetch=1,
            grid=(2,),
            in_specs=[ANYWHERE] * 11,
            out_specs=[pl.BlockSpec((HALF, FFL), lambda i, p: (i, 0))]
            + [turned_spec] * 3
            + part_specs(1)
            + [ANYWHERE],
            scratch_shapes=[
                pltpu.VMEM((2 * HALF, D), BF16),
                pltpu.VMEM((2 * HALF, D), BF16),
                pltpu.VMEM((2, FFL, D), BF16),
                pltpu.VMEM((FFL, D), BF16),
                pltpu.VMEM((2, 8, FFL, B), BF16),
                pltpu.SemaphoreType.DMA((69,)),
            ],
        ),
        out_shape=[shaped(2 * HALF, FFL)] + [turned_shape] * 3 + PART_SHAPES + [shaped(FFL, D)],
        compiler_params=params("arbitrary"),
        cost_estimate=cost(2 * 5 * 2 * HALF * FFL * D, 32),
        name="feed_forward",
    )(place, *tokens, *grads, ff_all)


def along_z(place, zhi, zlo):
    return (2 * zhi + zlo + 4 - 2 * place[4] - place[0]) % 4


def load_tokens(step, refs, rows, sems):
    copies = put_tokens(refs, rows, sems, 0)

    @pl.when(step == 0)
    def _():
        for copy in copies:
            copy.start()
        for copy in copies:
            copy.wait()


def gate_up_kernel(*refs):
    place, token_refs, gate_t, up_t, out_ref, rows, terms, sems = refs[0], refs[1:6], *refs[6:]
    step = pl.program_id(0)
    load_tokens(step, token_refs, rows, sems)
    normed = rows[:, pl.ds(pl.multiple_of(step * 4 * B, 4 * B), 4 * B)]

    def out(i, matrix):
        xs, by = pl.ds(i % 2 * 2, 2), along_z(place, i // 2, matrix)
        return pltpu.make_async_copy(terms.at[xs, by], out_ref.at[xs, by], sems.at[10 + 2 * i + matrix])

    for matrix, left in ((0, gate_t), (1, up_t)):
        term = matmul(left[...], normed).astype(BF16)
        by = along_z(place, step // 2, matrix)
        for j in range(2):
            terms[step % 2 * 2 + j, by, 0:FFL, :] = term[:, 2 * j * B : (2 * j + 1) * B]
            terms[step % 2 * 2 + j, by, FFL:, :] = term[:, (2 * j + 1) * B : (2 * j + 2) * B]
        out(step, matrix).start()

    @pl.when(step == 3)
    def _():
        for i in range(4):
            for matrix in range(2):
                out(i, matrix).wait()


def down_kernel(*refs):
    place, grad_refs, act_t, out_ref, rows, terms, sems = refs[0], refs[1:6], *refs[6:]
    step = pl.program_id(0)
    load_tokens(step, grad_refs, rows, sems)
    term = matmul(act_t[...], rows[:, pl.ds(pl.multiple_of(step * 4 * B, 4 * B), 4 * B)])
    for j in range(2):
        p = (2 * step + j) % 4
        at = pl.ds(pl.multiple_of(p * 2 * PIECE, 16), 2 * PIECE)
        for zx in range(8):
            slab = term[zx * PIECE : (zx + 1) * PIECE]
            low, high = slab[:, 2 * j * B : (2 * j + 1) * B], slab[:, (2 * j + 1) * B : (2 * j + 2) * B]
            by = along_z(place, zx // 4, step // 2)
            terms[zx % 4, by, at, :] = jnp.concatenate([low, high], axis=0).astype(BF16)

    def out(half, zhi):
        by = along_z(place, zhi, half)
        return pltpu.make_async_copy(terms.at[:, by], out_ref.at[:, by], sems.at[10 + 2 * half + zhi])

    @pl.when(step % 2 == 1)
    def _():
        for zhi in range(2):
            out(step // 2, zhi).start()

    @pl.when(step == 3)
    def _():
        for half in range(2):
            for zhi in range(2):
                out(half, zhi).wait()


def ff_terms(kernel, place, pieces, lefts, rows, name):
    whole = pl.BlockSpec((FFL, 2 * HALF), lambda i, p: (0, 0))
    return pl.pallas_call(
        kernel,
        grid_spec=pltpu.PrefetchScalarGridSpec(
            num_scalar_prefetch=1,
            grid=(4,),
            in_specs=[ANYWHERE] * 5 + [whole] * len(lefts),
            out_specs=ANYWHERE,
            scratch_shapes=[
                pltpu.VMEM((2 * HALF, D), BF16),
                pltpu.VMEM((4, 4, rows, B), BF16),
                pltpu.SemaphoreType.DMA((18,)),
            ],
        ),
        out_shape=shaped(4, 4, rows, B),
        compiler_params=params("arbitrary"),
        cost_estimate=cost(2 * len(lefts) * 2 * HALF * FFL * D, 8 + 4 * len(lefts)),
        name=name,
    )(place, *pieces, *lefts)


def finish_hidden_kernel(sums_ref, weight_ref, gain_ref, out_ref, gain_out, rows):
    for y in range(4):
        for core in range(2):
            slab = sums_ref[y, 0, core].astype(F32)
            for zx in range(8):
                at = (2 * zx + core) * 4 * PIECE + y * PIECE
                rows[at : at + PIECE] = slab[zx * PIECE : (zx + 1) * PIECE]
    gain = gain_ref[...]
    total = jnp.zeros((B, 1), F32)
    for i in range(FF // B):
        lanes = slice(i * B, (i + 1) * B)
        block = rows[lanes].T
        total = total + jnp.sum(block * weight_ref[:, lanes].astype(F32), axis=1, keepdims=True)
        out_ref[:, lanes] = block * gain
    gain_out[...] = total


def finish_hidden(sums, matrix, weight, gain):
    return pl.pallas_call(
        finish_hidden_kernel,
        grid=(1,),
        in_specs=[
            pl.BlockSpec((4, 1, 2, FFL, B), lambda i: (0, matrix, 0, 0, 0)),
            pl.BlockSpec((B, FF), lambda i: (0, 0)),
            pl.BlockSpec((B, 1), lambda i: (0, 0)),
        ],
        out_specs=[pl.BlockSpec((B, FF), lambda i: (0, 0)), pl.BlockSpec((B, 1), lambda i: (0, 0))],
        out_shape=[shaped(B, FF, kind=F32), shaped(B, 1, kind=F32)],
        scratch_shapes=[pltpu.VMEM((FF, B), F32)],
        compiler_params=params("arbitrary"),
        cost_estimate=cost(0, 6),
        name="finish_hidden",
    )(sums, weight, gain)


def finish_down_kernel(sums_ref, out_ref):
    for y in range(4):
        for half in range(2):
            slab = sums_ref[y, half, 0].astype(F32)
            for t in range(8):
                lane = (half * 8 + t) * B
                out_ref[y * PIECE : (y + 1) * PIECE, lane : lane + B] = slab[t * PIECE : (t + 1) * PIECE]


def finish_down(sums):
    return pl.pallas_call(
        finish_down_kernel,
        grid=(1,),
        in_specs=[pl.BlockSpec((4, 2, 1, FFL, B), lambda i: (0, 0, 2, 0, 0))],
        out_specs=pl.BlockSpec((4 * PIECE, D), lambda i: (0, 0)),
        out_shape=shaped(4 * PIECE, D, kind=F32),
        compiler_params=params("arbitrary"),
        cost_estimate=cost(0, 5),
        name="finish_down",
    )(sums)


def own_rows(rows_all, y, core, per):
    return lax.dynamic_slice_in_dim(rows_all, (2 * y + core) * per, per, 0)


class Flow:
    def __init__(self, steps):
        self.steps, self.result, self.sent = steps, None, None
        self.move(None)

    def move(self, arrived):
        try:
            self.sent = self.steps.send(arrived)
        except StopIteration as end:
            self.sent, self.result = (), end.value


def stage(flows, *values):
    flows = [flow for flow in flows if flow.result is None]
    sizes = [len(flow.sent) for flow in flows]
    leaves, tree = jax.tree.flatten(values)
    tied = tie(*[v for flow in flows for v in flow.sent], *leaves)
    for flow, size in zip(flows, sizes):
        flow.move(tied[:size])
        tied = tied[size:]
    return jax.tree.unflatten(tree, tied)


def gather_steps(block):
    (other,) = yield (swap_core(block),)
    pair = jnp.stack([block, other])
    (got,) = yield (along_y(pair),)
    far, swapped = yield (along_y(send_half(got)), swap_core(got))
    (far_swapped,) = yield (swap_core(far),)
    return pair, got, swapped, far, far_swapped


def scatter_steps(parts):
    core = lax.axis_index("core")
    first, behind, ahead, far, far_other = parts
    (far_got,) = yield (swap_core(far_other),)
    far = add(far, far_got).astype(BF16)
    low, behind_got, first_got = yield (along_y(far), swap_core(behind), swap_core(first[1]))
    ahead = add(ahead, behind_got).astype(BF16)
    mine = add(lax.dynamic_slice_in_dim(ahead, core * (B // 2), B // 2, 1), low).astype(BF16)
    ahead = lax.dynamic_update_slice_in_dim(ahead, mine, core * (B // 2), 1)
    (got,) = yield (along_y(ahead),)
    (last,) = yield (swap_core(got[1]),)
    return add(first[0], first_got) + got[0].astype(F32) + last.astype(F32)


def ring_gather_steps(block, axis):
    half = block.shape[0] // 2
    before, after = yield (shift(block, axis, 1), shift(block, axis, -1))
    low, high = yield (shift(before[:half], axis, 1), shift(after[half:], axis, -1))
    return block, after, low, high, before


def ring_scatter_steps(parts, axis):
    half = parts[2].shape[0] // 2
    low, high = yield (shift(parts[2][:half], axis, 1), shift(parts[2][half:], axis, -1))
    after = jnp.concatenate([add(parts[1][:half], low).astype(BF16), parts[1][half:]], axis=0)
    before = jnp.concatenate([parts[3][:half], add(parts[3][half:], high).astype(BF16)], axis=0)
    from_before, from_after = yield (shift(after, axis, 1), shift(before, axis, -1))
    return add(parts[0], from_before) + from_after.astype(F32)


def on_device(
    layer_input,
    positions,
    attn_gain,
    w_query,
    w_key,
    w_value,
    w_output,
    mlp_gain,
    w_gate,
    w_up,
    w_down,
    out_grad,
):
    zlo, y, zhi, x, core = (lax.axis_index(axis) for axis in AXES)
    place = jnp.stack([zlo, y, core, x, zhi]).astype(jnp.int32)

    def by_core(mine, got):
        return jnp.where(core == 0, jnp.stack([mine, got]), jnp.stack([got, mine]))

    def by_zlo(mine, got):
        return jnp.where(zlo == 0, jnp.stack([mine, got]), jnp.stack([got, mine]))

    def by_zhi(mine, got):
        return jnp.where(zhi == 0, jnp.stack([mine, got]), jnp.stack([got, mine]))

    def trio(mine, other, axis):
        across = lax.ppermute(other, (axis, "core"), [(i, 3 - i) for i in range(4)])
        return shift(mine, axis, 1), swap_core(other), across

    def column_steps(mine, got):
        pair = by_core(mine, got)
        (got,) = yield (shift(pair, "zhi", 1),)
        return (yield from ring_gather_steps(by_zhi(pair, got), "x"))

    def output_steps(mine, other):
        there, here, across = yield trio(mine, other, "zhi")
        column = by_zhi(by_core(mine, here), by_core(there, across))
        return (yield from ring_gather_steps(column, "x"))

    def hidden_steps(mine, got, down):
        piece = jnp.concatenate([by_core(mine, got).reshape(2 * FFL, B), down], axis=0)
        pieces = yield from ring_gather_steps(piece, "z")
        return jnp.concatenate(pieces, axis=0).reshape(4, 3 * FFL, B)

    def of_core(pair, other=False):
        return lax.dynamic_index_in_dim(pair, 1 - core if other else core, 0, keepdims=False)

    def whole_ring(pieces):
        own, after, low, high, before = pieces
        return own, after, jnp.concatenate([low, high], axis=0), before

    def attention_steps(column):
        keep = lax.dynamic_index_in_dim(column, zhi, 0, keepdims=False)
        send = lax.dynamic_index_in_dim(column, 1 - zhi, 0, keepdims=False)
        (got,) = yield (shift(send, "zhi", 1),)
        pair = add(keep, got).astype(BF16)
        mine, other = of_core(pair), of_core(pair, True)
        there, here, across = yield trio(mine, other, "zlo")
        own = by_core(add(mine, there), add(here, across)).astype(BF16)
        return (yield from ring_gather_steps(own, "y"))

    def ff_steps(sums):
        own = yield from ring_scatter_steps([sums[i] for i in range(4)], "z")
        own = own.astype(BF16)
        pair, down = own[: 2 * FFL].reshape(2, FFL, B), own[2 * FFL :]
        mine, other = of_core(pair), of_core(pair, True)
        there, here, across = yield trio(jnp.concatenate([mine, down], axis=0), other, "zlo")
        both = by_zlo(by_core(mine, here), by_core(there[:FFL], across))
        return jnp.concatenate([both, by_zlo(down, there[FFL:])[:, None]], axis=1)

    x_low = layer_input[0]
    frequency = theta ** (-jnp.arange(0, HD, 2).astype(F32) / HD)
    angles = positions[0].astype(F32)[:, None] * frequency
    tables = []
    for table in (jnp.cos(angles), jnp.sin(angles)):
        high = lax.reduce_precision(table, 8, 7)
        tables += [high.astype(BF16), (table - high).astype(BF16)]
    tokens = Flow(gather_steps(jnp.concatenate([x_low, *tables], axis=1)))
    grads = Flow(gather_steps(out_grad[0]))
    qkv_mine, qkv_other = prepare_qkv(place, w_query, w_key, w_value, attn_gain[:, None])
    qkv_mine, qkv_got, gain_two, w_out = stage([tokens], qkv_mine, swap_core(qkv_other), mlp_gain[:, None], w_output)

    columns = Flow(column_steps(qkv_mine, qkv_got))
    o_rows = lax.all_to_all(w_out.reshape(B, 16, B).transpose(1, 0, 2), FSDP, 0, 0, tiled=True)
    ff_mine, ff_other, ff_down = prepare_ff(place, w_gate, w_up, w_down, gain_two)
    ff_mine, ff_got, ff_down, x_low, o_rows = stage(
        [tokens, columns], ff_mine, swap_core(ff_other), ff_down, x_low, o_rows
    )

    inputs = x_low.astype(F32)
    scale_one = lax.rsqrt(jnp.mean(inputs * inputs, axis=-1, keepdims=True) + eps)
    o_rows = o_rows.reshape(D, B)
    mine, other = own_rows(o_rows, y, core, HEADS * HD), own_rows(o_rows, y, 1 - core, HEADS * HD)
    scale_one, mine, other, ff_mine, ff_got, ff_down = stage(
        [tokens, columns, grads], scale_one, mine, other, ff_mine, ff_got, ff_down
    )

    outputs = Flow(output_steps(mine, other))
    ff_mine, ff_got, ff_down = stage([tokens, columns, outputs], ff_mine, ff_got, ff_down)

    hidden_rows = Flow(hidden_steps(ff_mine, ff_got, ff_down))
    x_pieces = tokens.result
    query, key_value, scale_all, cosine, sine, qkv_full = project_qkv(place, x_pieces, columns.result)
    query, key_value = stage([hidden_rows, outputs, grads], query, key_value)

    earlier = lax.ppermute(key_value, "zlo", [(0, 1)])
    query, key_value, earlier = stage([outputs, hidden_rows], query, key_value, earlier)
    ff_all = lax.all_gather(hidden_rows.result, "x", axis=0, tiled=False)

    key_value = jnp.concatenate([earlier, key_value], axis=1)
    mixed, log_total, *parts, o_full = attention(place, outputs.result, query, key_value)
    parts = stage([grads], *parts)
    sums = Flow(scatter_steps(parts))
    stage([sums, grads])
    grad_pieces = grads.result
    for _ in range(3):
        stage([sums])
    hidden = inputs + sums.result
    scale_two = lax.rsqrt(jnp.mean(hidden * hidden, axis=-1, keepdims=True) + eps)
    normed = Flow(gather_steps((hidden * scale_two).astype(BF16)))
    for _ in range(4):
        stage([normed])
    normed_pieces = normed.result

    activation, act_t, gate_t, up_t, *parts, down_full = feed_forward(place, normed_pieces, grad_pieces, ff_all)
    sums = Flow(scatter_steps(parts))
    (act_t,) = stage([sums], act_t)
    down_terms = ff_terms(down_kernel, place, grad_pieces, (act_t,), FFL, "down_terms")
    down_terms, gate_t = stage([sums], down_terms, gate_t)
    down_sum = lax.psum_scatter(down_terms, "x", scatter_dimension=0, tiled=True)[0]
    gate_up_terms = ff_terms(gate_up_kernel, place, normed_pieces, (gate_t, up_t), 2 * FFL, "gate_up_terms")
    (gate_up_terms,) = stage([sums], gate_up_terms)
    gate_up_sum = lax.psum_scatter(gate_up_terms, "x", scatter_dimension=0, tiled=True)[0]
    stage([sums])

    grad_normed_two = sums.result
    mean_two = jnp.mean(grad_normed_two * hidden, axis=-1, keepdims=True)
    grad_hidden = (
        out_grad[0].astype(F32)
        + scale_two * grad_normed_two
        - hidden * (scale_two * scale_two * scale_two) * mean_two
    )
    hidden_grads = Flow(gather_steps(grad_hidden.astype(BF16)))
    (activation,) = stage([hidden_grads], activation)
    down_parts = project(activation, down_full)
    down_parts = stage([hidden_grads], *down_parts)
    result = Flow(scatter_steps(down_parts))
    stage([hidden_grads, result])
    stage([hidden_grads])

    hidden_grad_pieces = hidden_grads.result
    grad_query, grad_earlier, grad_own = attention_back(
        place, hidden_grad_pieces, query, key_value, log_total, o_full
    )
    grad_query, grad_earlier, grad_own, mixed = stage([result], grad_query, grad_earlier, grad_own, mixed)
    later = lax.ppermute(grad_earlier, "zlo", [(1, 0)])
    output_terms = attention_terms(place, hidden_grad_pieces, mixed.reshape(2 * HALF, HEADS * HD), "output_terms")
    later, grad_query, output_terms, down_sum, gate_up_sum = stage(
        [result], later, grad_query, output_terms, down_sum, gate_up_sum
    )
    output_sum = lax.psum_scatter(output_terms, "x", scatter_dimension=0, tiled=True)[0]
    ff_sums = Flow(ff_steps(jnp.concatenate([gate_up_sum, down_sum], axis=1)))
    *parts, grad_t = qkv_back(grad_query, grad_own, later, cosine, sine, scale_all, qkv_full)
    *parts, grad_t = stage([ff_sums, result], *parts, grad_t)

    sums = Flow(scatter_steps(parts))
    terms = attention_terms(place, x_pieces, grad_t, "qkv_terms")
    terms, output_sum = stage([sums, ff_sums], terms, output_sum)
    attention_sum = lax.psum_scatter(terms, "x", scatter_dimension=0, tiled=True)[0]
    output_sums = Flow(attention_steps(output_sum))
    (attention_sum,) = stage([sums, ff_sums, output_sums], attention_sum)
    ff_sums = lax.all_gather(ff_sums.result, "y", axis=0, tiled=False)
    attention_sums = Flow(attention_steps(attention_sum))
    stage([sums, output_sums, attention_sums])
    stage([sums, output_sums, attention_sums])
    grad_normed = sums.result
    mean_one = jnp.mean(grad_normed * inputs, axis=-1, keepdims=True)
    input_grad = (
        grad_hidden
        + scale_one * grad_normed
        - inputs * (scale_one * scale_one * scale_one) * mean_one
    )
    input_grad = input_grad.astype(BF16)
    stage([attention_sums, output_sums])
    ring = jnp.roll(jnp.stack(whole_ring(output_sums.result)), y, axis=0).reshape(16, B, B)
    (ring,) = stage([attention_sums], ring)

    output_grad = lax.all_to_all(ring, FSDP, 0, 0, tiled=True)

    gain_two = mlp_gain[:, None]
    gate_grad, gate_gain = finish_hidden(ff_sums, 0, w_gate, gain_two)
    up_grad, up_gain = finish_hidden(ff_sums, 1, w_up, gain_two)
    down_grad = finish_down(ff_sums)
    query_grad, key_grad, value_grad, attn_gain_grad = finish_attention(
        place, whole_ring(attention_sums.result), w_query, w_key, w_value, attn_gain[:, None]
    )
    output_grad = finish_output(output_grad)
    return (
        (hidden + result.result).astype(BF16)[None],
        input_grad[None],
        attn_gain_grad[:, 0],
        query_grad,
        key_grad,
        value_grad,
        output_grad,
        (gate_gain + up_gain)[:, 0],
        gate_grad,
        up_grad,
        down_grad,
    )


def solution(mesh):
    split = Mesh(mesh.devices.reshape(2, 4, 2, 4, 2), AXES)
    tokens = P(FSDP, SEQ, None)
    rows = P(FSDP, None)
    gain = P(FSDP)
    in_specs = (
        tokens, P(FSDP, SEQ), gain, rows, rows, rows, rows, gain, rows, rows, rows, tokens,
    )
    out_specs = (tokens, tokens, gain, rows, rows, rows, rows, gain, rows, rows, rows)
    return jax.shard_map(
        on_device, mesh=split, in_specs=in_specs, out_specs=out_specs, check_vma=False
    )
```

```python
import jax
import jax.numpy as jnp
from jax import lax
from jax.experimental import pallas as pl
from jax.experimental.pallas import tpu as pltpu
from jax.sharding import Mesh
from jax.sharding import PartitionSpec as P

H = 32
KV = 4
HD = 64
D = 2048
FF = 5632
B = 128
HALF = 512
HEADS = 4
FFL = 704
PIECE = 88

eps = 1e-05
theta = 10000.0
F32 = jnp.float32
BF16 = jnp.bfloat16
AXES = ("zlo", "y", "zhi", "x", "core")
FSDP = ("zhi", "x", "core")
SEQ = ("zlo", "y")


def matmul(left, right):
    return jnp.dot(left, right, preferred_element_type=F32)


def times_transposed(left, right):
    return lax.dot_general(left, right, (((1,), (1,)), ((), ())), preferred_element_type=F32)


def outer_sum(left, right):
    return lax.dot_general(left, right, (((0,), (0,)), ((), ())), preferred_element_type=F32)


def shift(value, axis, by):
    if axis == "z":
        at = [2 * (z % 2) + z // 2 for z in range(4)]
        return lax.ppermute(value, ("zlo", "zhi"), [(at[z], at[(z + by) % 4]) for z in range(4)])
    size = lax.axis_size(axis)
    return lax.ppermute(value, axis, [(i, (i + by) % size) for i in range(size)])


def swap_core(value):
    return shift(value, "core", 1)


def small_gather(block, axis):
    return shift(block, axis, -1), shift(block, axis, 2), shift(block, axis, 1)


def tie(*values):
    return lax.optimization_barrier(values)


def add(left, right):
    return left.astype(F32) + right.astype(F32)


def along_y(value):
    pairs = []
    for i in range(4):
        pairs.append((2 * i, 2 * ((i + 1) % 4)))
        pairs.append((2 * i + 1, 2 * ((i + 3) % 4) + 1))
    return lax.ppermute(value, ("y", "core"), pairs)


def send_half(got):
    core = lax.axis_index("core")
    return lax.dynamic_slice_in_dim(got, core * (B // 2), B // 2, 1)


FLIPPED = (0, 0, 1, 0, 1)
LENGTHS = (B, B, B, B // 2, B // 2)


def put_tokens(refs, rows_ref, sems, start):
    lanes = pl.ds(0, rows_ref.shape[1])
    copies = []
    row = 0
    for s in range(2):
        for ref, flip, length in zip(refs, FLIPPED, LENGTHS):
            copies.append(
                pltpu.make_async_copy(
                    ref.at[s ^ flip, :, lanes], rows_ref.at[pl.ds(row, length)], sems.at[start + len(copies)]
                )
            )
            row += length
    return copies


TILE = 256
WIDE = D + B
VMEM_LIMIT = 56 * 2**20
ANYWHERE = pl.BlockSpec(memory_space=pl.ANY)


def params(*kinds):
    return pltpu.CompilerParams(dimension_semantics=kinds or None, vmem_limit_bytes=VMEM_LIMIT)


def cost(flops, megabytes):
    return pl.CostEstimate(flops=flops, bytes_accessed=int(megabytes * 2**20), transcendentals=0)


def shaped(*shape, kind=BF16):
    return jax.ShapeDtypeStruct(shape, kind)


PARTS = ((B, False), (B, True), (B, False), (B // 2, False), (B // 2, True))
PART_SHAPES = [jax.ShapeDtypeStruct((2, n, D), BF16) for n, _ in PARTS]


def part_specs(steps):
    def of(turn):
        return lambda i, *_: (1 - i // steps if turn else i // steps, 0, 0)

    return [pl.BlockSpec((1, n, D), of(turn)) for n, turn in PARTS]


def put_parts(step, tile, refs):
    @pl.when(step % 2 == 0)
    def _():
        refs[0][0] = tile[:B]
        refs[1][0] = tile[B:]

    @pl.when(step % 2 == 1)
    def _():
        refs[2][0] = tile[:B]
        refs[3][0] = tile[B : B + B // 2]
        refs[4][0] = tile[B + B // 2 :]


def put_rows(rows, refs):
    row = 0
    for ref, (length, _) in zip(refs, PARTS):
        ref[0] = rows[row : row + length]
        row += length


def turned(values):
    lane = lax.broadcasted_iota(jnp.int32, values.shape, 1) % HD
    return jnp.where(lane < HD // 2, -pltpu.roll(values, 2 * HD - HD // 2, 1), pltpu.roll(values, HD // 2, 1))


def lane_block(zhi, x, core):
    return pl.ds(pl.multiple_of((zhi * 8 + x * 2 + core) * B, B), B)


def put_columns(place, refs, into, sems, start):
    copies = []
    for ref, by, first in zip(refs, (0, 1, 2, 2, 3), (0, 0, 0, 1, 0)):
        for i in range(ref.shape[0]):
            for core in range(2):
                lanes = lane_block(first + i, (place[3] + by) % 4, core)
                copies.append(
                    pltpu.make_async_copy(ref.at[i, core], into.at[:, lanes], sems.at[start + len(copies)])
                )
    return copies


def prepare_qkv_kernel(place, q_mine, q_other, w_key, w_value, gain, mine_ref, other_ref, k_rows, v_rows):
    scale = gain[...]
    k_rows[...] = (w_key[...].astype(F32) * scale).T
    v_rows[...] = (w_value[...].astype(F32) * scale).T
    rows = pl.ds(pl.multiple_of(place[1] * HD, HD), HD)
    for source, out in ((q_mine, mine_ref), (q_other, other_ref)):
        out[: HEADS * HD] = (source[...].astype(F32) * scale).T.astype(BF16)
        out[HEADS * HD : (HEADS + 1) * HD] = k_rows[rows].astype(BF16)
        out[(HEADS + 1) * HD :] = v_rows[rows].astype(BF16)


QKV = (HEADS + 2) * HD


def prepare_qkv(place, w_query, w_key, w_value, gain):
    whole = lambda *shape: pl.BlockSpec(shape, lambda i, p: (0,) * len(shape))
    return pl.pallas_call(
        prepare_qkv_kernel,
        grid_spec=pltpu.PrefetchScalarGridSpec(
            num_scalar_prefetch=1,
            grid=(1,),
            in_specs=[
                pl.BlockSpec((B, HEADS * HD), lambda i, p: (0, 2 * p[1] + p[2])),
                pl.BlockSpec((B, HEADS * HD), lambda i, p: (0, 2 * p[1] + 1 - p[2])),
                whole(B, KV * HD), whole(B, KV * HD), whole(B, 1),
            ],
            out_specs=[whole(QKV, B), whole(QKV, B)],
            scratch_shapes=[pltpu.VMEM((KV * HD, B), F32), pltpu.VMEM((KV * HD, B), F32)],
        ),
        out_shape=[shaped(QKV, B), shaped(QKV, B)],
        compiler_params=params("arbitrary"),
        cost_estimate=cost(0, 1),
        name="prepare_qkv",
    )(place, w_query, w_query, w_key, w_value, gain)


def prepare_ff_kernel(place, w_gate, w_up, w_down, gain, mine_ref, other_ref, down_ref, picked, rows, down_rows, sems):
    zlo, y, core = place[0], place[1], place[2]
    down = pltpu.make_async_copy(
        w_down.at[:, pl.ds(pl.multiple_of(zlo * (D // 2), D // 2), D // 2)], down_rows, sems.at[1]
    )
    down.start()

    @pl.when(zlo == 0)
    def _():
        copy = pltpu.make_async_copy(w_gate, picked, sems.at[0])
        copy.start()
        copy.wait()

    @pl.when(zlo == 1)
    def _():
        copy = pltpu.make_async_copy(w_up, picked, sems.at[0])
        copy.start()
        copy.wait()

    scale = gain[...]
    for i in range(FF // B):
        rows[i * B : (i + 1) * B] = (picked[:, i * B : (i + 1) * B].astype(F32) * scale).T
    for which, out in ((core, mine_ref), (1 - core, other_ref)):
        slabs = []
        for zx in range(8):
            at = pl.multiple_of(zx * 2 * 4 * PIECE + which * 4 * PIECE + y * PIECE, 8)
            slabs.append(rows[pl.ds(at, PIECE)])
        out[...] = jnp.concatenate(slabs, axis=0).astype(BF16)
    down.wait()
    for t in range(8):
        rows[t * 4 * PIECE : (t + 1) * 4 * PIECE] = down_rows[:, t * B : (t + 1) * B].astype(F32)
    slabs = [rows[pl.ds(pl.multiple_of(t * 4 * PIECE + y * PIECE, 8), PIECE)] for t in range(8)]
    down_ref[...] = jnp.concatenate(slabs, axis=0).astype(BF16)


def prepare_ff(place, w_gate, w_up, w_down, gain):
    return pl.pallas_call(
        prepare_ff_kernel,
        grid_spec=pltpu.PrefetchScalarGridSpec(
            num_scalar_prefetch=1,
            grid=(1,),
            in_specs=[ANYWHERE, ANYWHERE, ANYWHERE, pl.BlockSpec((B, 1), lambda i, p: (0, 0))],
            out_specs=[pl.BlockSpec((FFL, B), lambda i, p: (0, 0))] * 3,
            scratch_shapes=[
                pltpu.VMEM((B, FF), BF16),
                pltpu.VMEM((FF, B), F32),
                pltpu.VMEM((4 * PIECE, D // 2), BF16),
                pltpu.SemaphoreType.DMA((2,)),
            ],
        ),
        out_shape=[shaped(FFL, B)] * 3,
        compiler_params=params("arbitrary"),
        cost_estimate=cost(0, 6),
        name="prepare_ff",
    )(place, w_gate, w_up, w_down, gain)


def project_qkv_kernel(*refs):
    place, x_refs, w_refs = refs[0], refs[1:6], refs[6:11]
    query_ref, kv_ref, scale_ref, cosine_ref, sine_ref, w_out, rows, weights, sems = refs[11:]
    step = pl.program_id(0)
    tokens = put_tokens(x_refs, rows, sems, 0)
    columns = put_columns(place, w_refs, weights, sems, 10)
    back = pltpu.make_async_copy(weights, w_out, sems.at[26])

    @pl.when(step == 0)
    def _():
        for copy in columns + tokens:
            copy.start()
        for copy in columns:
            copy.wait()
        back.start()
        for copy in tokens:
            copy.wait()

    at = pl.ds(pl.multiple_of(step * TILE, TILE), TILE)
    tile = rows[at, :D]
    wide = tile.astype(F32)
    scale = lax.rsqrt(jnp.mean(wide * wide, axis=-1, keepdims=True) + eps)
    scale_ref[...] = scale
    pre = times_transposed(tile, weights[...]) * scale
    tables = rows[at, D:].astype(F32)
    tables = tables + pltpu.roll(tables, B - HD // 2, 1)
    cosine = jnp.concatenate([tables[:, : HD // 2]] * 4, axis=1)
    sine = jnp.concatenate([tables[:, HD : HD + HD // 2]] * 4, axis=1)
    cosine_ref[...] = cosine
    sine_ref[...] = sine
    for i in range(2):
        part = pre[:, i * 2 * HD : (i + 1) * 2 * HD]
        part = (part * cosine + turned(part) * sine).astype(BF16) * HD ** (-0.5)
        query_ref[0, 2 * i] = part[:, :HD]
        query_ref[0, 2 * i + 1] = part[:, HD:]
    part = pre[:, HEADS * HD :]
    lane = lax.broadcasted_iota(jnp.int32, part.shape, 1)
    kv_ref[0] = jnp.where(lane < HD, part * cosine + turned(part) * sine, part).astype(BF16)

    @pl.when(step == 3)
    def _():
        back.wait()


def project_qkv(place, x_pieces, w_pieces):
    tile = lambda lanes: pl.BlockSpec((TILE, lanes), lambda i, p: (i, 0))
    return pl.pallas_call(
        project_qkv_kernel,
        grid_spec=pltpu.PrefetchScalarGridSpec(
            num_scalar_prefetch=1,
            grid=(4,),
            in_specs=[ANYWHERE] * 10,
            out_specs=[
                pl.BlockSpec((1, HEADS, TILE, HD), lambda i, p: (i // 2, 0, i % 2, 0)),
                pl.BlockSpec((1, TILE, 2 * HD), lambda i, p: (i // 2, i % 2, 0)),
                tile(1), tile(2 * HD), tile(2 * HD),
                ANYWHERE,
            ],
            scratch_shapes=[
                pltpu.VMEM((2 * HALF, WIDE), BF16),
                pltpu.VMEM((QKV, D), BF16),
                pltpu.SemaphoreType.DMA((27,)),
            ],
        ),
        out_shape=[
            shaped(2, HEADS, HALF, HD), shaped(2, HALF, 2 * HD), shaped(2 * HALF, 1, kind=F32),
            shaped(2 * HALF, 2 * HD, kind=F32), shaped(2 * HALF, 2 * HD, kind=F32), shaped(QKV, D),
        ],
        compiler_params=params("arbitrary"),
        cost_estimate=cost(2 * 2 * HALF * QKV * D, 8),
        name="project_qkv",
    )(place, *x_pieces, *w_pieces)


def project_kernel(left_ref, weight_ref, *parts):
    put_parts(pl.program_id(0), matmul(left_ref[...], weight_ref[...]).astype(BF16), parts)


def project(left, weight):
    depth = left.shape[1]
    return pl.pallas_call(
        project_kernel,
        grid=(4,),
        in_specs=[pl.BlockSpec((TILE, depth), lambda i: (i, 0)), pl.BlockSpec((depth, D), lambda i: (0, 0))],
        out_specs=part_specs(2),
        out_shape=PART_SHAPES,
        compiler_params=params("arbitrary"),
        cost_estimate=cost(2 * 2 * HALF * depth * D, 8),
        name="project",
    )(left, weight)


def put_term(left, rows, term_ref):
    def one(i, carry):
        term = matmul(left, rows[:, pl.ds(pl.multiple_of(i * 4 * B, 4 * B), 4 * B)]).astype(BF16)
        for j in range(2):
            zx = 2 * i + j
            term_ref[zx % 4, zx // 4, 0] = term[:, 2 * j * B : (2 * j + 1) * B]
            term_ref[zx % 4, zx // 4, 1] = term[:, (2 * j + 1) * B : (2 * j + 2) * B]
        return carry

    lax.fori_loop(0, 4, one, 0)


def qkv_back_kernel(*refs):
    x_refs, grad_q, own, later, cosine_ref, sine_ref, scale_ref = refs[1:6], *refs[6:12]
    grad_ref, term_ref, rows, left, sems = refs[12:]
    copies = put_tokens(x_refs, rows, sems, 0)
    for copy in copies:
        copy.start()
    for step in range(4):
        at, s = slice(step * TILE, (step + 1) * TILE), step // 2
        inner = slice(step % 2 * TILE, (step % 2 + 1) * TILE)
        cosine, sine = cosine_ref[at], sine_ref[at]
        pieces = []
        for i in range(2):
            part = grad_q[s, inner, i * 2 * HD : (i + 1) * 2 * HD]
            pieces.append(part * cosine - turned(part * sine))
        lane = lax.broadcasted_iota(jnp.int32, cosine.shape, 1)
        part = own[s, inner] + later[s, inner].astype(F32)
        pieces.append(jnp.where(lane < HD, part * cosine - turned(part * sine), part))
        grad_pre = jnp.concatenate(pieces, axis=1)
        grad_ref[at] = grad_pre.astype(BF16)
        left[:, at] = (grad_pre * scale_ref[at]).T.astype(BF16)
    for copy in copies:
        copy.wait()
    put_term(left[...], rows, term_ref)


def qkv_back(place, x_pieces, grad_query, own, later, cosine, sine, scale):
    whole = lambda *shape: pl.BlockSpec(shape, lambda i, p: (0,) * len(shape))
    tokens = 2 * HALF
    return pl.pallas_call(
        qkv_back_kernel,
        grid_spec=pltpu.PrefetchScalarGridSpec(
            num_scalar_prefetch=1,
            grid=(1,),
            in_specs=[ANYWHERE] * 5
            + [
                whole(2, HALF, HEADS * HD), whole(2, HALF, 2 * HD), whole(2, HALF, 2 * HD),
                whole(tokens, 2 * HD), whole(tokens, 2 * HD), whole(tokens, 1),
            ],
            out_specs=[whole(tokens, QKV), whole(4, 2, 2, QKV, B)],
            scratch_shapes=[
                pltpu.VMEM((tokens, D), BF16), pltpu.VMEM((QKV, tokens), BF16), pltpu.SemaphoreType.DMA((10,)),
            ],
        ),
        out_shape=[shaped(tokens, QKV), shaped(4, 2, 2, QKV, B)],
        compiler_params=params("arbitrary"),
        cost_estimate=cost(2 * tokens * QKV * D, 9),
        name="qkv_back",
    )(place, *x_pieces, grad_query, own, later, cosine, sine, scale)


def attention_term_kernel(*refs):
    token_refs, left_ref = refs[1:6], refs[6]
    term_ref, rows, sems = refs[-3:]
    copies = put_tokens(token_refs, rows, sems, 0)
    for copy in copies:
        copy.start()
    left = left_ref[...]
    if left.shape[0] == 2 * HALF:
        left = left.T
    for copy in copies:
        copy.wait()
    put_term(left, rows, term_ref)


def attention_terms(place, pieces, left, name):
    whole = lambda *shape: pl.BlockSpec(shape, lambda i, p: (0,) * len(shape))
    rows = min(left.shape)
    return pl.pallas_call(
        attention_term_kernel,
        grid_spec=pltpu.PrefetchScalarGridSpec(
            num_scalar_prefetch=1,
            grid=(1,),
            in_specs=[ANYWHERE] * 5 + [whole(*left.shape)],
            out_specs=whole(4, 2, 2, rows, B),
            scratch_shapes=[pltpu.VMEM((2 * HALF, D), BF16), pltpu.SemaphoreType.DMA((10,))],
        ),
        out_shape=shaped(4, 2, 2, rows, B),
        compiler_params=params("arbitrary"),
        cost_estimate=cost(2 * 2 * HALF * rows * D, 7),
        name=name,
    )(place, *pieces, left)


def token_places(at, y, core):
    step = 1 - 2 * core
    block = jnp.where(
        at < B, y, jnp.where(at < 2 * B, y + 4 - step, jnp.where(at < 3 * B, y + 4 + step, y + 2))
    )
    row = at % B
    row = jnp.where(at < 3 * B, row, (row + core * (B // 2)) % B)
    return (block % 4) * B + row


def set_bias(place_ref, bias_ref):
    zlo, y, core = place_ref[0], place_ref[1], place_ref[2]
    key_at = token_places(lax.broadcasted_iota(jnp.int32, (HALF, 1), 0), y, core)
    query_at = token_places(lax.broadcasted_iota(jnp.int32, (1, HALF), 1), y, core)
    bias_ref[:HALF, :] = jnp.broadcast_to(jnp.where(zlo == 1, 0.0, -1e30), (HALF, HALF))
    bias_ref[HALF:, :] = jnp.where(key_at <= query_at, 0.0, -1e30)


def attention_kernel(place_ref, *refs):
    w_refs, query_ref, kv_ref, mixed_ref, log_ref = refs[:5], *refs[5:9]
    parts, w_out, bias_ref, weight, sems = refs[9:14], *refs[14:]
    columns = put_columns(place_ref, w_refs, weight, sems, 0)
    back = pltpu.make_async_copy(weight, w_out, sems.at[16])

    @pl.when(pl.program_id(0) == 0)
    def _():
        for copy in columns:
            copy.start()
        set_bias(place_ref, bias_ref)
        for copy in columns:
            copy.wait()
        back.start()

    key, value = kv_ref[0, :, :HD], kv_ref[0, :, HD:]
    for head in range(HEADS):
        scores = times_transposed(key, query_ref[0, head]) + bias_ref[...]
        top = jnp.max(scores, axis=0, keepdims=True)
        weights = jnp.exp(scores - top)
        total = jnp.sum(weights, axis=0, keepdims=True)
        low = (weights * (1.0 / total)).astype(BF16)
        mixed_ref[0, :, head * HD : (head + 1) * HD] = outer_sum(value, low).T.astype(BF16)
        log_ref[0, head] = top + jnp.log(total)
    put_rows(matmul(mixed_ref[0], weight[...]).astype(BF16), parts)

    @pl.when(pl.program_id(0) == 1)
    def _():
        back.wait()


def attention_back_kernel(place_ref, *refs):
    grad_refs, query_ref, kv_ref, log_ref, weight_ref = refs[:5], *refs[5:9]
    grad_query_ref, earlier_ref, own_ref, bias_ref, rows, sems = refs[9:]
    step = pl.program_id(0)
    copies = put_tokens(grad_refs, rows, sems, 0)

    @pl.when(step == 0)
    def _():
        for copy in copies:
            copy.start()
        set_bias(place_ref, bias_ref)
        for copy in copies:
            copy.wait()

    hidden = rows[pl.ds(pl.multiple_of(step * HALF, HALF), HALF), :]
    grads = times_transposed(hidden, weight_ref[...]).astype(BF16)
    key, value = kv_ref[0, :, :HD], kv_ref[0, :, HD:]
    grad_key = jnp.zeros((2 * HALF, HD), F32)
    grad_value = jnp.zeros((2 * HALF, HD), F32)
    for head in range(HEADS):
        lanes = slice(head * HD, (head + 1) * HD)
        query, grad = query_ref[0, head], grads[:, lanes]
        weights = jnp.exp(times_transposed(key, query) + bias_ref[...] - log_ref[0, head])
        grad_weights = times_transposed(value, grad)
        delta = jnp.sum(weights * grad_weights, axis=0, keepdims=True)
        grad_scores = (weights * (grad_weights - delta)).astype(BF16)
        grad_query_ref[0, :, lanes] = outer_sum(key, grad_scores).T * HD ** (-0.5)
        grad_key += matmul(grad_scores, query)
        grad_value += matmul(weights.astype(BF16), grad)
    total = jnp.concatenate([grad_key, grad_value], axis=1)
    earlier_ref[0] = total[:HALF].astype(BF16)
    own_ref[0] = total[HALF:]


def sequence_block(*tail):
    return pl.BlockSpec((1,) + tail, lambda s, place: (s,) + (0,) * len(tail))


def attention_call(kernel, in_specs, out_specs, out_shape, scratch, flops, name):
    return pl.pallas_call(
        kernel,
        grid_spec=pltpu.PrefetchScalarGridSpec(
            num_scalar_prefetch=1,
            grid=(2,),
            in_specs=in_specs,
            out_specs=out_specs,
            scratch_shapes=[pltpu.VMEM((2 * HALF, HALF), F32)] + scratch,
        ),
        out_shape=out_shape,
        compiler_params=params("arbitrary"),
        cost_estimate=cost(flops * 8 * 2 * HALF * HALF * HD * 2, 8),
        name=name,
    )


def attention(place, w_pieces, query, kv):
    return attention_call(
        attention_kernel,
        [ANYWHERE] * 5 + [sequence_block(HEADS, HALF, HD), sequence_block(2 * HALF, 2 * HD)],
        [sequence_block(HALF, HEADS * HD), sequence_block(HEADS, 1, HALF)]
        + part_specs(1)
        + [ANYWHERE],
        [shaped(2, HALF, HEADS * HD), shaped(2, HEADS, 1, HALF, kind=F32)] + PART_SHAPES + [shaped(HEADS * HD, D)],
        [pltpu.VMEM((HEADS * HD, D), BF16), pltpu.SemaphoreType.DMA((17,))],
        3,
        "attention",
    )(place, *w_pieces, query, kv)


def attention_back(place, grad_pieces, query, kv, log_total, weight):
    return attention_call(
        attention_back_kernel,
        [ANYWHERE] * 5
        + [
            sequence_block(HEADS, HALF, HD), sequence_block(2 * HALF, 2 * HD),
            sequence_block(HEADS, 1, HALF), pl.BlockSpec((HEADS * HD, D), lambda s, place: (0, 0)),
        ],
        [sequence_block(HALF, HEADS * HD), sequence_block(HALF, 2 * HD), sequence_block(HALF, 2 * HD)],
        [
            shaped(2, HALF, HEADS * HD, kind=F32),
            shaped(2, HALF, 2 * HD),
            shaped(2, HALF, 2 * HD, kind=F32),
        ],
        [pltpu.VMEM((2 * HALF, D), BF16), pltpu.SemaphoreType.DMA((10,))],
        6,
        "attention_back",
    )(place, *grad_pieces, query, kv, log_total, weight)


def finish_attention_kernel(place, *refs):
    piece_refs, w_query, w_key, w_value, gain_ref = refs[:4], *refs[4:8]
    query_out, key_out, value_out, gain_out, rows = refs[8:]
    for ref, by in zip(piece_refs, range(4)):
        at_y = (place[1] + by) % 4
        for c in range(2):
            piece = ref[c].astype(F32)
            rows[pl.ds(pl.multiple_of((2 * at_y + c) * HEADS * HD, HEADS * HD), HEADS * HD)] = piece[: HEADS * HD]
        both = ref[0].astype(F32) + ref[1].astype(F32)
        at = pl.multiple_of(H * HD + at_y * HD, HD)
        rows[pl.ds(at, HD)] = both[HEADS * HD : (HEADS + 1) * HD]
        rows[pl.ds(at + KV * HD, HD)] = both[(HEADS + 1) * HD :]
    gain = gain_ref[...]
    total = jnp.zeros((B, 1), F32)
    row = 0
    for weight, out in ((w_query, query_out), (w_key, key_out), (w_value, value_out)):
        for i in range(out.shape[1] // B):
            lanes = slice(i * B, (i + 1) * B)
            block = rows[row : row + B].T
            total = total + jnp.sum(block * weight[:, lanes].astype(F32), axis=1, keepdims=True)
            out[:, lanes] = block * gain
            row += B
    gain_out[...] = total


def finish_attention(place, pieces, w_query, w_key, w_value, gain):
    whole = lambda *shape: pl.BlockSpec(shape, lambda i, p: (0,) * len(shape))
    kv = KV * HD
    return pl.pallas_call(
        finish_attention_kernel,
        grid_spec=pltpu.PrefetchScalarGridSpec(
            num_scalar_prefetch=1,
            grid=(1,),
            in_specs=[whole(2, QKV, B)] * 4 + [whole(B, D), whole(B, kv), whole(B, kv), whole(B, 1)],
            out_specs=[whole(B, D), whole(B, kv), whole(B, kv), whole(B, 1)],
            scratch_shapes=[pltpu.VMEM((D + 2 * kv, B), F32)],
        ),
        out_shape=[
            shaped(B, D, kind=F32), shaped(B, kv, kind=F32), shaped(B, kv, kind=F32), shaped(B, 1, kind=F32),
        ],
        compiler_params=params("arbitrary"),
        cost_estimate=cost(0, 4),
        name="finish_attention",
    )(place, *pieces, w_query, w_key, w_value, gain)


def finish_output_kernel(blocks, out):
    for i in range(16):
        out[:, i * B : (i + 1) * B] = blocks[i].astype(F32)


def finish_output(blocks):
    return pl.pallas_call(
        finish_output_kernel,
        out_shape=shaped(B, D, kind=F32),
        compiler_params=params(),
        cost_estimate=cost(0, 2),
        name="finish_output",
    )(blocks)


def feed_forward_kernel(*refs):
    place, token_refs, grad_refs, ff_ref = refs[0], refs[1:6], refs[6:11], refs[11]
    act_ref, act_t, gate_t, up_t = refs[12:16]
    parts, down_out = refs[16:21], refs[21]
    rows_h, rows_g, gate_up, down, slabs, sems = refs[22:]
    step = pl.program_id(0)
    tokens = put_tokens(token_refs, rows_h, sems, 0)
    grads = put_tokens(grad_refs, rows_g, sems, 10)
    weights, loads = [], []
    for x in range(4):
        for by in range(4):
            z = (2 * place[4] + place[0] + by) % 4
            zhi, zlo = z // 2, z % 2
            for core in range(2):
                weights.append(
                    pltpu.make_async_copy(
                        ff_ref.at[x, by, pl.ds(core * FFL, FFL)],
                        gate_up.at[zlo, :, lane_block(zhi, x, core)],
                        sems.at[20 + len(weights)],
                    )
                )
            loads.append(
                pltpu.make_async_copy(
                    ff_ref.at[x, by, pl.ds(2 * FFL, FFL)], slabs.at[zlo, zhi * 4 + x], sems.at[52 + len(loads)]
                )
            )
    back = pltpu.make_async_copy(down, down_out, sems.at[68])

    @pl.when(step == 0)
    def _():
        for copy in tokens + weights + loads + grads:
            copy.start()
        for copy in tokens + weights:
            copy.wait()

    rows = pl.ds(pl.multiple_of(step * HALF, HALF), HALF)
    normed = rows_h[rows, :]
    gate_pre = times_transposed(normed, gate_up[0])
    upward = times_transposed(normed, gate_up[1])

    @pl.when(step == 0)
    def _():
        for copy in loads:
            copy.wait()

        def put(q, carry):
            for half in range(2):
                for p in range(4):
                    one = slabs[half, 2 * q, 2 * p * PIECE : 2 * (p + 1) * PIECE, :].astype(F32)
                    two = slabs[half, 2 * q + 1, 2 * p * PIECE : 2 * (p + 1) * PIECE, :].astype(F32)
                    lane = (half * 8 + 2 * p) * B
                    rows = pl.ds(pl.multiple_of(q * 2 * PIECE, 16), 2 * PIECE)
                    down[rows, lane : lane + B] = jnp.concatenate([one[:PIECE], two[:PIECE]], axis=0).astype(BF16)
                    down[rows, lane + B : lane + 2 * B] = jnp.concatenate(
                        [one[PIECE:], two[PIECE:]], axis=0
                    ).astype(BF16)
            return carry

        lax.fori_loop(0, 4, put, 0)
        back.start()
        for copy in grads:
            copy.wait()

    grad_act = times_transposed(rows_g[rows, :], down[...])
    sigmoid = 1.0 / (1.0 + jnp.exp(-gate_pre))
    silu = gate_pre * sigmoid
    activation = silu * upward
    grad_up = grad_act * silu
    grad_gate = grad_act * upward * (sigmoid * (1.0 + gate_pre * (1.0 - sigmoid)))
    part = matmul(grad_gate.astype(BF16), gate_up[0]) + matmul(grad_up.astype(BF16), gate_up[1])
    put_rows(part.astype(BF16), parts)
    act_ref[...] = activation.astype(BF16)
    act_t[...] = activation.T.astype(BF16)
    gate_t[...] = grad_gate.T.astype(BF16)
    up_t[...] = grad_up.T.astype(BF16)

    @pl.when(step == 1)
    def _():
        back.wait()


def feed_forward(place, tokens, grads, ff_all):
    turned_spec = pl.BlockSpec((FFL, HALF), lambda i, p: (0, i))
    turned_shape = shaped(FFL, 2 * HALF)
    return pl.pallas_call(
        feed_forward_kernel,
        grid_spec=pltpu.PrefetchScalarGridSpec(
            num_scalar_prefetch=1,
            grid=(2,),
            in_specs=[ANYWHERE] * 11,
            out_specs=[pl.BlockSpec((HALF, FFL), lambda i, p: (i, 0))]
            + [turned_spec] * 3
            + part_specs(1)
            + [ANYWHERE],
            scratch_shapes=[
                pltpu.VMEM((2 * HALF, D), BF16),
                pltpu.VMEM((2 * HALF, D), BF16),
                pltpu.VMEM((2, FFL, D), BF16),
                pltpu.VMEM((FFL, D), BF16),
                pltpu.VMEM((2, 8, FFL, B), BF16),
                pltpu.SemaphoreType.DMA((69,)),
            ],
        ),
        out_shape=[shaped(2 * HALF, FFL)] + [turned_shape] * 3 + PART_SHAPES + [shaped(FFL, D)],
        compiler_params=params("arbitrary"),
        cost_estimate=cost(2 * 5 * 2 * HALF * FFL * D, 32),
        name="feed_forward",
    )(place, *tokens, *grads, ff_all)


def along_z(place, zhi, zlo):
    return (2 * zhi + zlo + 4 - 2 * place[4] - place[0]) % 4


def load_tokens(step, refs, rows, sems):
    copies = put_tokens(refs, rows, sems, 0)

    @pl.when(step == 0)
    def _():
        for copy in copies:
            copy.start()
        for copy in copies:
            copy.wait()


def gate_up_kernel(*refs):
    place, token_refs, gate_t, up_t, out_ref, rows, terms, sems = refs[0], refs[1:6], *refs[6:]
    step = pl.program_id(0)
    load_tokens(step, token_refs, rows, sems)
    normed = rows[:, pl.ds(pl.multiple_of(step * 4 * B, 4 * B), 4 * B)]

    def out(i, matrix):
        xs, by = pl.ds(i % 2 * 2, 2), along_z(place, i // 2, matrix)
        return pltpu.make_async_copy(terms.at[xs, by], out_ref.at[xs, by], sems.at[10 + 2 * i + matrix])

    for matrix, left in ((0, gate_t), (1, up_t)):
        term = matmul(left[...], normed).astype(BF16)
        by = along_z(place, step // 2, matrix)
        for j in range(2):
            terms[step % 2 * 2 + j, by, 0:FFL, :] = term[:, 2 * j * B : (2 * j + 1) * B]
            terms[step % 2 * 2 + j, by, FFL:, :] = term[:, (2 * j + 1) * B : (2 * j + 2) * B]
        out(step, matrix).start()

    @pl.when(step == 3)
    def _():
        for i in range(4):
            for matrix in range(2):
                out(i, matrix).wait()


def down_kernel(*refs):
    place, grad_refs, act_t, out_ref, rows, terms, sems = refs[0], refs[1:6], *refs[6:]
    step = pl.program_id(0)
    load_tokens(step, grad_refs, rows, sems)
    term = matmul(act_t[...], rows[:, pl.ds(pl.multiple_of(step * 4 * B, 4 * B), 4 * B)])
    for j in range(2):
        p = (2 * step + j) % 4
        at = pl.ds(pl.multiple_of(p * 2 * PIECE, 16), 2 * PIECE)
        for zx in range(8):
            slab = term[zx * PIECE : (zx + 1) * PIECE]
            low, high = slab[:, 2 * j * B : (2 * j + 1) * B], slab[:, (2 * j + 1) * B : (2 * j + 2) * B]
            by = along_z(place, zx // 4, step // 2)
            terms[zx % 4, by, at, :] = jnp.concatenate([low, high], axis=0).astype(BF16)

    def out(half, zhi):
        by = along_z(place, zhi, half)
        return pltpu.make_async_copy(terms.at[:, by], out_ref.at[:, by], sems.at[10 + 2 * half + zhi])

    @pl.when(step % 2 == 1)
    def _():
        for zhi in range(2):
            out(step // 2, zhi).start()

    @pl.when(step == 3)
    def _():
        for half in range(2):
            for zhi in range(2):
                out(half, zhi).wait()


def ff_terms(kernel, place, pieces, lefts, rows, name):
    whole = pl.BlockSpec((FFL, 2 * HALF), lambda i, p: (0, 0))
    return pl.pallas_call(
        kernel,
        grid_spec=pltpu.PrefetchScalarGridSpec(
            num_scalar_prefetch=1,
            grid=(4,),
            in_specs=[ANYWHERE] * 5 + [whole] * len(lefts),
            out_specs=ANYWHERE,
            scratch_shapes=[
                pltpu.VMEM((2 * HALF, D), BF16),
                pltpu.VMEM((4, 4, rows, B), BF16),
                pltpu.SemaphoreType.DMA((18,)),
            ],
        ),
        out_shape=shaped(4, 4, rows, B),
        compiler_params=params("arbitrary"),
        cost_estimate=cost(2 * len(lefts) * 2 * HALF * FFL * D, 8 + 4 * len(lefts)),
        name=name,
    )(place, *pieces, *lefts)


def finish_hidden_kernel(sums_ref, weight_ref, gain_ref, out_ref, gain_out, rows):
    for y in range(4):
        for core in range(2):
            slab = sums_ref[y, 0, core].astype(F32)
            for zx in range(8):
                at = (2 * zx + core) * 4 * PIECE + y * PIECE
                rows[at : at + PIECE] = slab[zx * PIECE : (zx + 1) * PIECE]
    gain = gain_ref[...]
    total = jnp.zeros((B, 1), F32)
    for i in range(FF // B):
        lanes = slice(i * B, (i + 1) * B)
        block = rows[lanes].T
        total = total + jnp.sum(block * weight_ref[:, lanes].astype(F32), axis=1, keepdims=True)
        out_ref[:, lanes] = block * gain
    gain_out[...] = total


def finish_hidden(sums, matrix, weight, gain):
    return pl.pallas_call(
        finish_hidden_kernel,
        grid=(1,),
        in_specs=[
            pl.BlockSpec((4, 1, 2, FFL, B), lambda i: (0, matrix, 0, 0, 0)),
            pl.BlockSpec((B, FF), lambda i: (0, 0)),
            pl.BlockSpec((B, 1), lambda i: (0, 0)),
        ],
        out_specs=[pl.BlockSpec((B, FF), lambda i: (0, 0)), pl.BlockSpec((B, 1), lambda i: (0, 0))],
        out_shape=[shaped(B, FF, kind=F32), shaped(B, 1, kind=F32)],
        scratch_shapes=[pltpu.VMEM((FF, B), F32)],
        compiler_params=params("arbitrary"),
        cost_estimate=cost(0, 6),
        name="finish_hidden",
    )(sums, weight, gain)


def finish_down_kernel(sums_ref, out_ref):
    for y in range(4):
        for half in range(2):
            slab = sums_ref[y, half, 0].astype(F32)
            for t in range(8):
                lane = (half * 8 + t) * B
                out_ref[y * PIECE : (y + 1) * PIECE, lane : lane + B] = slab[t * PIECE : (t + 1) * PIECE]


def finish_down(sums):
    return pl.pallas_call(
        finish_down_kernel,
        grid=(1,),
        in_specs=[pl.BlockSpec((4, 2, 1, FFL, B), lambda i: (0, 0, 2, 0, 0))],
        out_specs=pl.BlockSpec((4 * PIECE, D), lambda i: (0, 0)),
        out_shape=shaped(4 * PIECE, D, kind=F32),
        compiler_params=params("arbitrary"),
        cost_estimate=cost(0, 5),
        name="finish_down",
    )(sums)


def own_rows(rows_all, y, core, per):
    return lax.dynamic_slice_in_dim(rows_all, (2 * y + core) * per, per, 0)


class Flow:
    def __init__(self, steps):
        self.steps, self.result, self.sent = steps, None, None
        self.move(None)

    def move(self, arrived):
        try:
            self.sent = self.steps.send(arrived)
        except StopIteration as end:
            self.sent, self.result = (), end.value


def stage(flows, *values):
    flows = [flow for flow in flows if flow.result is None]
    sizes = [len(flow.sent) for flow in flows]
    leaves, tree = jax.tree.flatten(values)
    tied = tie(*[v for flow in flows for v in flow.sent], *leaves)
    for flow, size in zip(flows, sizes):
        flow.move(tied[:size])
        tied = tied[size:]
    return jax.tree.unflatten(tree, tied)


def gather_steps(block):
    (other,) = yield (swap_core(block),)
    pair = jnp.stack([block, other])
    (got,) = yield (along_y(pair),)
    far, swapped = yield (along_y(send_half(got)), swap_core(got))
    (far_swapped,) = yield (swap_core(far),)
    return pair, got, swapped, far, far_swapped


def scatter_steps(parts):
    core = lax.axis_index("core")
    first, behind, ahead, far, far_other = parts
    (far_got,) = yield (swap_core(far_other),)
    far = add(far, far_got).astype(BF16)
    low, behind_got, first_got = yield (along_y(far), swap_core(behind), swap_core(first[1]))
    ahead = add(ahead, behind_got).astype(BF16)
    mine = add(lax.dynamic_slice_in_dim(ahead, core * (B // 2), B // 2, 1), low).astype(BF16)
    ahead = lax.dynamic_update_slice_in_dim(ahead, mine, core * (B // 2), 1)
    (got,) = yield (along_y(ahead),)
    (last,) = yield (swap_core(got[1]),)
    return add(first[0], first_got) + got[0].astype(F32) + last.astype(F32)


def ring_gather_steps(block, axis):
    half = block.shape[0] // 2
    before, after = yield (shift(block, axis, 1), shift(block, axis, -1))
    low, high = yield (shift(before[:half], axis, 1), shift(after[half:], axis, -1))
    return block, after, low, high, before


def ring_scatter_steps(parts, axis):
    half = parts[2].shape[0] // 2
    low, high = yield (shift(parts[2][:half], axis, 1), shift(parts[2][half:], axis, -1))
    after = jnp.concatenate([add(parts[1][:half], low).astype(BF16), parts[1][half:]], axis=0)
    before = jnp.concatenate([parts[3][:half], add(parts[3][half:], high).astype(BF16)], axis=0)
    from_before, from_after = yield (shift(after, axis, 1), shift(before, axis, -1))
    return add(parts[0], from_before) + from_after.astype(F32)


def on_device(
    layer_input,
    positions,
    attn_gain,
    w_query,
    w_key,
    w_value,
    w_output,
    mlp_gain,
    w_gate,
    w_up,
    w_down,
    out_grad,
):
    zlo, y, zhi, x, core = (lax.axis_index(axis) for axis in AXES)
    place = jnp.stack([zlo, y, core, x, zhi]).astype(jnp.int32)

    def by_core(mine, got):
        return jnp.where(core == 0, jnp.stack([mine, got]), jnp.stack([got, mine]))

    def by_zlo(mine, got):
        return jnp.where(zlo == 0, jnp.stack([mine, got]), jnp.stack([got, mine]))

    def by_zhi(mine, got):
        return jnp.where(zhi == 0, jnp.stack([mine, got]), jnp.stack([got, mine]))

    def trio(mine, other, axis):
        across = lax.ppermute(other, (axis, "core"), [(i, 3 - i) for i in range(4)])
        return shift(mine, axis, 1), swap_core(other), across

    def column_steps(mine, got):
        pair = by_core(mine, got)
        (got,) = yield (shift(pair, "zhi", 1),)
        return (yield from ring_gather_steps(by_zhi(pair, got), "x"))

    def output_steps(mine, other):
        there, here, across = yield trio(mine, other, "zhi")
        column = by_zhi(by_core(mine, here), by_core(there, across))
        return (yield from ring_gather_steps(column, "x"))

    def hidden_steps(mine, got, down):
        piece = jnp.concatenate([by_core(mine, got).reshape(2 * FFL, B), down], axis=0)
        pieces = yield from ring_gather_steps(piece, "z")
        return jnp.concatenate(pieces, axis=0).reshape(4, 3 * FFL, B)

    def of_core(pair, other=False):
        return lax.dynamic_index_in_dim(pair, 1 - core if other else core, 0, keepdims=False)

    def whole_ring(pieces):
        own, after, low, high, before = pieces
        return own, after, jnp.concatenate([low, high], axis=0), before

    def attention_steps(column):
        keep = lax.dynamic_index_in_dim(column, zhi, 0, keepdims=False)
        send = lax.dynamic_index_in_dim(column, 1 - zhi, 0, keepdims=False)
        (got,) = yield (shift(send, "zhi", 1),)
        pair = add(keep, got).astype(BF16)
        mine, other = of_core(pair), of_core(pair, True)
        there, here, across = yield trio(mine, other, "zlo")
        own = by_core(add(mine, there), add(here, across)).astype(BF16)
        return (yield from ring_gather_steps(own, "y"))

    def ff_steps(sums):
        own = yield from ring_scatter_steps([sums[i] for i in range(4)], "z")
        own = own.astype(BF16)
        pair, down = own[: 2 * FFL].reshape(2, FFL, B), own[2 * FFL :]
        mine, other = of_core(pair), of_core(pair, True)
        there, here, across = yield trio(jnp.concatenate([mine, down], axis=0), other, "zlo")
        both = by_zlo(by_core(mine, here), by_core(there[:FFL], across))
        return jnp.concatenate([both, by_zlo(down, there[FFL:])[:, None]], axis=1)

    x_low = layer_input[0]
    frequency = theta ** (-jnp.arange(0, HD, 2).astype(F32) / HD)
    angles = positions[0].astype(F32)[:, None] * frequency
    tables = []
    for table in (jnp.cos(angles), jnp.sin(angles)):
        high = lax.reduce_precision(table, 8, 7)
        tables += [high.astype(BF16), (table - high).astype(BF16)]
    tokens = Flow(gather_steps(jnp.concatenate([x_low, *tables], axis=1)))
    grads = Flow(gather_steps(out_grad[0]))
    qkv_mine, qkv_other = prepare_qkv(place, w_query, w_key, w_value, attn_gain[:, None])
    qkv_mine, qkv_got, gain_two, w_out = stage([tokens], qkv_mine, swap_core(qkv_other), mlp_gain[:, None], w_output)

    columns = Flow(column_steps(qkv_mine, qkv_got))
    o_rows = lax.all_to_all(w_out.reshape(B, 16, B).transpose(1, 0, 2), FSDP, 0, 0, tiled=True)
    ff_mine, ff_other, ff_down = prepare_ff(place, w_gate, w_up, w_down, gain_two)
    ff_mine, ff_got, ff_down, x_low, o_rows = stage(
        [tokens, columns], ff_mine, swap_core(ff_other), ff_down, x_low, o_rows
    )

    inputs = x_low.astype(F32)
    scale_one = lax.rsqrt(jnp.mean(inputs * inputs, axis=-1, keepdims=True) + eps)
    o_rows = o_rows.reshape(D, B)
    mine, other = own_rows(o_rows, y, core, HEADS * HD), own_rows(o_rows, y, 1 - core, HEADS * HD)
    scale_one, mine, other, ff_mine, ff_got, ff_down = stage(
        [tokens, columns, grads], scale_one, mine, other, ff_mine, ff_got, ff_down
    )

    outputs = Flow(output_steps(mine, other))
    ff_mine, ff_got, ff_down = stage([tokens, columns, outputs], ff_mine, ff_got, ff_down)

    hidden_rows = Flow(hidden_steps(ff_mine, ff_got, ff_down))
    x_pieces = tokens.result
    query, key_value, scale_all, cosine, sine, qkv_full = project_qkv(place, x_pieces, columns.result)
    query, key_value = stage([hidden_rows, outputs, grads], query, key_value)

    earlier = lax.ppermute(key_value, "zlo", [(0, 1)])
    query, key_value, earlier = stage([outputs, hidden_rows], query, key_value, earlier)
    ff_all = lax.all_gather(hidden_rows.result, "x", axis=0, tiled=False)

    key_value = jnp.concatenate([earlier, key_value], axis=1)
    mixed, log_total, *parts, o_full = attention(place, outputs.result, query, key_value)
    parts = stage([grads], *parts)
    sums = Flow(scatter_steps(parts))
    stage([sums, grads])
    grad_pieces = grads.result
    for _ in range(3):
        stage([sums])
    hidden = inputs + sums.result
    scale_two = lax.rsqrt(jnp.mean(hidden * hidden, axis=-1, keepdims=True) + eps)
    normed = Flow(gather_steps((hidden * scale_two).astype(BF16)))
    for _ in range(4):
        stage([normed])
    normed_pieces = normed.result

    activation, act_t, gate_t, up_t, *parts, down_full = feed_forward(place, normed_pieces, grad_pieces, ff_all)
    sums = Flow(scatter_steps(parts))
    (act_t,) = stage([sums], act_t)
    down_terms = ff_terms(down_kernel, place, grad_pieces, (act_t,), FFL, "down_terms")
    down_terms, gate_t = stage([sums], down_terms, gate_t)
    down_sum = lax.psum_scatter(down_terms, "x", scatter_dimension=0, tiled=True)[0]
    gate_up_terms = ff_terms(gate_up_kernel, place, normed_pieces, (gate_t, up_t), 2 * FFL, "gate_up_terms")
    (gate_up_terms,) = stage([sums], gate_up_terms)
    gate_up_sum = lax.psum_scatter(gate_up_terms, "x", scatter_dimension=0, tiled=True)[0]
    stage([sums])

    grad_normed_two = sums.result
    mean_two = jnp.mean(grad_normed_two * hidden, axis=-1, keepdims=True)
    grad_hidden = (
        out_grad[0].astype(F32)
        + scale_two * grad_normed_two
        - hidden * (scale_two * scale_two * scale_two) * mean_two
    )
    hidden_grads = Flow(gather_steps(grad_hidden.astype(BF16)))
    (activation,) = stage([hidden_grads], activation)
    down_parts = project(activation, down_full)
    down_parts = stage([hidden_grads], *down_parts)
    result = Flow(scatter_steps(down_parts))
    stage([hidden_grads, result])
    stage([hidden_grads])

    hidden_grad_pieces = hidden_grads.result
    grad_query, grad_earlier, grad_own = attention_back(
        place, hidden_grad_pieces, query, key_value, log_total, o_full
    )
    grad_query, grad_earlier, grad_own, mixed = stage([result], grad_query, grad_earlier, grad_own, mixed)
    later = lax.ppermute(grad_earlier, "zlo", [(1, 0)])
    output_terms = attention_terms(place, hidden_grad_pieces, mixed.reshape(2 * HALF, HEADS * HD), "output_terms")
    later, grad_query, output_terms, down_sum, gate_up_sum = stage(
        [result], later, grad_query, output_terms, down_sum, gate_up_sum
    )
    output_sum = lax.psum_scatter(output_terms, "x", scatter_dimension=0, tiled=True)[0]
    ff_sums = Flow(ff_steps(jnp.concatenate([gate_up_sum, down_sum], axis=1)))
    grad_pre, terms = qkv_back(place, x_pieces, grad_query, grad_own, later, cosine, sine, scale_all)
    grad_pre, terms = stage([ff_sums, result], grad_pre, terms)

    attention_sum = lax.psum_scatter(terms, "x", scatter_dimension=0, tiled=True)[0]
    parts = project(grad_pre, qkv_full)
    *parts, output_sum, attention_sum = stage([ff_sums], *parts, output_sum, attention_sum)

    sums = Flow(scatter_steps(parts))
    output_sums = Flow(attention_steps(output_sum))
    attention_sums = Flow(attention_steps(attention_sum))
    stage([sums, ff_sums, output_sums, attention_sums])
    ff_sums = lax.all_gather(ff_sums.result, "y", axis=0, tiled=False)
    stage([sums, output_sums, attention_sums])
    stage([output_sums, attention_sums])
    stage([sums, output_sums, attention_sums])

    ring = jnp.roll(jnp.stack(whole_ring(output_sums.result)), y, axis=0).reshape(16, B, B)
    output_grad = lax.all_to_all(ring, FSDP, 0, 0, tiled=True)
    stage([sums])
    grad_normed = sums.result
    mean_one = jnp.mean(grad_normed * inputs, axis=-1, keepdims=True)
    input_grad = (
        grad_hidden
        + scale_one * grad_normed
        - inputs * (scale_one * scale_one * scale_one) * mean_one
    )
    input_grad = input_grad.astype(BF16)
    gain_two = mlp_gain[:, None]
    gate_grad, gate_gain = finish_hidden(ff_sums, 0, w_gate, gain_two)
    up_grad, up_gain = finish_hidden(ff_sums, 1, w_up, gain_two)
    down_grad = finish_down(ff_sums)
    query_grad, key_grad, value_grad, attn_gain_grad = finish_attention(
        place, whole_ring(attention_sums.result), w_query, w_key, w_value, attn_gain[:, None]
    )
    output_grad, gate_grad, up_grad, down_grad, query_grad = tie(output_grad, gate_grad, up_grad, down_grad, query_grad)
    output_grad = finish_output(output_grad)
    return (
        (hidden + result.result).astype(BF16)[None],
        input_grad[None],
        attn_gain_grad[:, 0],
        query_grad,
        key_grad,
        value_grad,
        output_grad,
        (gate_gain + up_gain)[:, 0],
        gate_grad,
        up_grad,
        down_grad,
    )


def solution(mesh):
    split = Mesh(mesh.devices.reshape(2, 4, 2, 4, 2), AXES)
    tokens = P(FSDP, SEQ, None)
    rows = P(FSDP, None)
    gain = P(FSDP)
    in_specs = (
        tokens, P(FSDP, SEQ), gain, rows, rows, rows, rows, gain, rows, rows, rows, tokens,
    )
    out_specs = (tokens, tokens, gain, rows, rows, rows, rows, gain, rows, rows, rows)
    return jax.shard_map(
        on_device, mesh=split, in_specs=in_specs, out_specs=out_specs, check_vma=False
    )
```

```python
import jax
import jax.numpy as jnp
from jax import lax
from jax.experimental import pallas as pl
from jax.experimental.pallas import tpu as pltpu
from jax.sharding import Mesh
from jax.sharding import PartitionSpec as P

H = 32
KV = 4
HD = 64
D = 2048
FF = 5632
B = 128
HALF = 512
HEADS = 4
FFL = 704
PIECE = 88

eps = 1e-05
theta = 10000.0
F32 = jnp.float32
BF16 = jnp.bfloat16
AXES = ("zlo", "y", "zhi", "x", "core")
FSDP = ("zhi", "x", "core")
SEQ = ("zlo", "y")


def matmul(left, right):
    return jnp.dot(left, right, preferred_element_type=F32)


def times_transposed(left, right):
    return lax.dot_general(left, right, (((1,), (1,)), ((), ())), preferred_element_type=F32)


def outer_sum(left, right):
    return lax.dot_general(left, right, (((0,), (0,)), ((), ())), preferred_element_type=F32)


def shift(value, axis, by):
    if axis == "z":
        at = [2 * (z % 2) + z // 2 for z in range(4)]
        return lax.ppermute(value, ("zlo", "zhi"), [(at[z], at[(z + by) % 4]) for z in range(4)])
    size = lax.axis_size(axis)
    return lax.ppermute(value, axis, [(i, (i + by) % size) for i in range(size)])


def swap_core(value):
    return shift(value, "core", 1)


def small_gather(block, axis):
    return shift(block, axis, -1), shift(block, axis, 2), shift(block, axis, 1)


def tie(*values):
    return lax.optimization_barrier(values)


def add(left, right):
    return left.astype(F32) + right.astype(F32)


def along_y(value):
    pairs = []
    for i in range(4):
        pairs.append((2 * i, 2 * ((i + 1) % 4)))
        pairs.append((2 * i + 1, 2 * ((i + 3) % 4) + 1))
    return lax.ppermute(value, ("y", "core"), pairs)


def send_half(got):
    core = lax.axis_index("core")
    return lax.dynamic_slice_in_dim(got, core * (B // 2), B // 2, 1)


FLIPPED = (0, 0, 1, 0, 1)
LENGTHS = (B, B, B, B // 2, B // 2)


def put_tokens(refs, rows_ref, sems, start):
    lanes = pl.ds(0, rows_ref.shape[1])
    copies = []
    row = 0
    for s in range(2):
        for ref, flip, length in zip(refs, FLIPPED, LENGTHS):
            copies.append(
                pltpu.make_async_copy(
                    ref.at[s ^ flip, :, lanes], rows_ref.at[pl.ds(row, length)], sems.at[start + len(copies)]
                )
            )
            row += length
    return copies


TILE = 256
WIDE = D + B
VMEM_LIMIT = 56 * 2**20
ANYWHERE = pl.BlockSpec(memory_space=pl.ANY)


def params(*kinds):
    return pltpu.CompilerParams(dimension_semantics=kinds or None, vmem_limit_bytes=VMEM_LIMIT)


def cost(flops, megabytes):
    return pl.CostEstimate(flops=flops, bytes_accessed=int(megabytes * 2**20), transcendentals=0)


def shaped(*shape, kind=BF16):
    return jax.ShapeDtypeStruct(shape, kind)


PARTS = ((B, False), (B, True), (B, False), (B // 2, False), (B // 2, True))
PART_SHAPES = [jax.ShapeDtypeStruct((2, n, D), BF16) for n, _ in PARTS]


def part_specs(steps):
    def of(turn):
        return lambda i, *_: (1 - i // steps if turn else i // steps, 0, 0)

    return [pl.BlockSpec((1, n, D), of(turn)) for n, turn in PARTS]


def put_parts(step, tile, refs):
    @pl.when(step % 2 == 0)
    def _():
        refs[0][0] = tile[:B]
        refs[1][0] = tile[B:]

    @pl.when(step % 2 == 1)
    def _():
        refs[2][0] = tile[:B]
        refs[3][0] = tile[B : B + B // 2]
        refs[4][0] = tile[B + B // 2 :]


def put_rows(rows, refs):
    row = 0
    for ref, (length, _) in zip(refs, PARTS):
        ref[0] = rows[row : row + length]
        row += length


def turned(values):
    lane = lax.broadcasted_iota(jnp.int32, values.shape, 1) % HD
    return jnp.where(lane < HD // 2, -pltpu.roll(values, 2 * HD - HD // 2, 1), pltpu.roll(values, HD // 2, 1))


def lane_block(zhi, x, core):
    return pl.ds(pl.multiple_of((zhi * 8 + x * 2 + core) * B, B), B)


def put_columns(place, refs, into, sems, start):
    copies = []
    for ref, by, first in zip(refs, (0, 1, 2, 2, 3), (0, 0, 0, 1, 0)):
        for i in range(ref.shape[0]):
            for core in range(2):
                lanes = lane_block(first + i, (place[3] + by) % 4, core)
                copies.append(
                    pltpu.make_async_copy(ref.at[i, core], into.at[:, lanes], sems.at[start + len(copies)])
                )
    return copies


def prepare_qkv_kernel(place, q_mine, q_other, w_key, w_value, gain, mine_ref, other_ref, k_rows, v_rows):
    scale = gain[...]
    k_rows[...] = (w_key[...].astype(F32) * scale).T
    v_rows[...] = (w_value[...].astype(F32) * scale).T
    rows = pl.ds(pl.multiple_of(place[1] * HD, HD), HD)
    for source, out in ((q_mine, mine_ref), (q_other, other_ref)):
        out[: HEADS * HD] = (source[...].astype(F32) * scale).T.astype(BF16)
        out[HEADS * HD : (HEADS + 1) * HD] = k_rows[rows].astype(BF16)
        out[(HEADS + 1) * HD :] = v_rows[rows].astype(BF16)


QKV = (HEADS + 2) * HD


def prepare_qkv(place, w_query, w_key, w_value, gain):
    whole = lambda *shape: pl.BlockSpec(shape, lambda i, p: (0,) * len(shape))
    return pl.pallas_call(
        prepare_qkv_kernel,
        grid_spec=pltpu.PrefetchScalarGridSpec(
            num_scalar_prefetch=1,
            grid=(1,),
            in_specs=[
                pl.BlockSpec((B, HEADS * HD), lambda i, p: (0, 2 * p[1] + p[2])),
                pl.BlockSpec((B, HEADS * HD), lambda i, p: (0, 2 * p[1] + 1 - p[2])),
                whole(B, KV * HD), whole(B, KV * HD), whole(B, 1),
            ],
            out_specs=[whole(QKV, B), whole(QKV, B)],
            scratch_shapes=[pltpu.VMEM((KV * HD, B), F32), pltpu.VMEM((KV * HD, B), F32)],
        ),
        out_shape=[shaped(QKV, B), shaped(QKV, B)],
        compiler_params=params("arbitrary"),
        cost_estimate=cost(0, 1),
        name="prepare_qkv",
    )(place, w_query, w_query, w_key, w_value, gain)


def prepare_ff_kernel(place, w_gate, w_up, w_down, gain, mine_ref, other_ref, down_ref, picked, rows, down_rows, sems):
    zlo, y, core = place[0], place[1], place[2]
    down = pltpu.make_async_copy(
        w_down.at[:, pl.ds(pl.multiple_of(zlo * (D // 2), D // 2), D // 2)], down_rows, sems.at[1]
    )
    down.start()

    @pl.when(zlo == 0)
    def _():
        copy = pltpu.make_async_copy(w_gate, picked, sems.at[0])
        copy.start()
        copy.wait()

    @pl.when(zlo == 1)
    def _():
        copy = pltpu.make_async_copy(w_up, picked, sems.at[0])
        copy.start()
        copy.wait()

    scale = gain[...]
    for i in range(FF // B):
        rows[i * B : (i + 1) * B] = (picked[:, i * B : (i + 1) * B].astype(F32) * scale).T
    for which, out in ((core, mine_ref), (1 - core, other_ref)):
        slabs = []
        for zx in range(8):
            at = pl.multiple_of(zx * 2 * 4 * PIECE + which * 4 * PIECE + y * PIECE, 8)
            slabs.append(rows[pl.ds(at, PIECE)])
        out[...] = jnp.concatenate(slabs, axis=0).astype(BF16)
    down.wait()
    for t in range(8):
        rows[t * 4 * PIECE : (t + 1) * 4 * PIECE] = down_rows[:, t * B : (t + 1) * B].astype(F32)
    slabs = [rows[pl.ds(pl.multiple_of(t * 4 * PIECE + y * PIECE, 8), PIECE)] for t in range(8)]
    down_ref[...] = jnp.concatenate(slabs, axis=0).astype(BF16)


def prepare_ff(place, w_gate, w_up, w_down, gain):
    return pl.pallas_call(
        prepare_ff_kernel,
        grid_spec=pltpu.PrefetchScalarGridSpec(
            num_scalar_prefetch=1,
            grid=(1,),
            in_specs=[ANYWHERE, ANYWHERE, ANYWHERE, pl.BlockSpec((B, 1), lambda i, p: (0, 0))],
            out_specs=[pl.BlockSpec((FFL, B), lambda i, p: (0, 0))] * 3,
            scratch_shapes=[
                pltpu.VMEM((B, FF), BF16),
                pltpu.VMEM((FF, B), F32),
                pltpu.VMEM((4 * PIECE, D // 2), BF16),
                pltpu.SemaphoreType.DMA((2,)),
            ],
        ),
        out_shape=[shaped(FFL, B)] * 3,
        compiler_params=params("arbitrary"),
        cost_estimate=cost(0, 6),
        name="prepare_ff",
    )(place, w_gate, w_up, w_down, gain)


def project_qkv_kernel(*refs):
    place, x_refs, w_refs = refs[0], refs[1:6], refs[6:11]
    query_ref, kv_ref, scale_ref, cosine_ref, sine_ref, w_out, rows, weights, sems = refs[11:]
    step = pl.program_id(0)
    tokens = put_tokens(x_refs, rows, sems, 0)
    columns = put_columns(place, w_refs, weights, sems, 10)
    back = pltpu.make_async_copy(weights, w_out, sems.at[26])

    @pl.when(step == 0)
    def _():
        for copy in columns + tokens:
            copy.start()
        for copy in columns:
            copy.wait()
        back.start()
        for copy in tokens:
            copy.wait()

    at = pl.ds(pl.multiple_of(step * TILE, TILE), TILE)
    tile = rows[at, :D]
    wide = tile.astype(F32)
    scale = lax.rsqrt(jnp.mean(wide * wide, axis=-1, keepdims=True) + eps)
    scale_ref[...] = scale
    pre = times_transposed(tile, weights[...]) * scale
    tables = rows[at, D:].astype(F32)
    tables = tables + pltpu.roll(tables, B - HD // 2, 1)
    cosine = jnp.concatenate([tables[:, : HD // 2]] * 4, axis=1)
    sine = jnp.concatenate([tables[:, HD : HD + HD // 2]] * 4, axis=1)
    cosine_ref[...] = cosine
    sine_ref[...] = sine
    for i in range(2):
        part = pre[:, i * 2 * HD : (i + 1) * 2 * HD]
        part = (part * cosine + turned(part) * sine).astype(BF16) * HD ** (-0.5)
        query_ref[0, 2 * i] = part[:, :HD]
        query_ref[0, 2 * i + 1] = part[:, HD:]
    part = pre[:, HEADS * HD :]
    lane = lax.broadcasted_iota(jnp.int32, part.shape, 1)
    kv_ref[0] = jnp.where(lane < HD, part * cosine + turned(part) * sine, part).astype(BF16)

    @pl.when(step == 3)
    def _():
        back.wait()


def project_qkv(place, x_pieces, w_pieces):
    tile = lambda lanes: pl.BlockSpec((TILE, lanes), lambda i, p: (i, 0))
    return pl.pallas_call(
        project_qkv_kernel,
        grid_spec=pltpu.PrefetchScalarGridSpec(
            num_scalar_prefetch=1,
            grid=(4,),
            in_specs=[ANYWHERE] * 10,
            out_specs=[
                pl.BlockSpec((1, HEADS, TILE, HD), lambda i, p: (i // 2, 0, i % 2, 0)),
                pl.BlockSpec((1, TILE, 2 * HD), lambda i, p: (i // 2, i % 2, 0)),
                tile(1), tile(2 * HD), tile(2 * HD),
                ANYWHERE,
            ],
            scratch_shapes=[
                pltpu.VMEM((2 * HALF, WIDE), BF16),
                pltpu.VMEM((QKV, D), BF16),
                pltpu.SemaphoreType.DMA((27,)),
            ],
        ),
        out_shape=[
            shaped(2, HEADS, HALF, HD), shaped(2, HALF, 2 * HD), shaped(2 * HALF, 1, kind=F32),
            shaped(2 * HALF, 2 * HD, kind=F32), shaped(2 * HALF, 2 * HD, kind=F32), shaped(QKV, D),
        ],
        compiler_params=params("arbitrary"),
        cost_estimate=cost(2 * 2 * HALF * QKV * D, 8),
        name="project_qkv",
    )(place, *x_pieces, *w_pieces)


def project_kernel(left_ref, weight_ref, *parts):
    put_parts(pl.program_id(0), matmul(left_ref[...], weight_ref[...]).astype(BF16), parts)


def project(left, weight):
    depth = left.shape[1]
    return pl.pallas_call(
        project_kernel,
        grid=(4,),
        in_specs=[pl.BlockSpec((TILE, depth), lambda i: (i, 0)), pl.BlockSpec((depth, D), lambda i: (0, 0))],
        out_specs=part_specs(2),
        out_shape=PART_SHAPES,
        compiler_params=params("arbitrary"),
        cost_estimate=cost(2 * 2 * HALF * depth * D, 8),
        name="project",
    )(left, weight)


def put_term(left, rows, term_ref):
    def one(i, carry):
        term = matmul(left, rows[:, pl.ds(pl.multiple_of(i * 4 * B, 4 * B), 4 * B)]).astype(BF16)
        for j in range(2):
            zx = 2 * i + j
            term_ref[zx % 4, zx // 4, 0] = term[:, 2 * j * B : (2 * j + 1) * B]
            term_ref[zx % 4, zx // 4, 1] = term[:, (2 * j + 1) * B : (2 * j + 2) * B]
        return carry

    lax.fori_loop(0, 4, one, 0)


def qkv_back_kernel(*refs):
    x_refs, grad_q, own, later, cosine_ref, sine_ref, scale_ref = refs[1:6], *refs[6:12]
    grad_ref, term_ref, rows, left, sems = refs[12:]
    copies = put_tokens(x_refs, rows, sems, 0)
    for copy in copies:
        copy.start()
    for step in range(4):
        at, s = slice(step * TILE, (step + 1) * TILE), step // 2
        inner = slice(step % 2 * TILE, (step % 2 + 1) * TILE)
        cosine, sine = cosine_ref[at], sine_ref[at]
        pieces = []
        for i in range(2):
            part = grad_q[s, inner, i * 2 * HD : (i + 1) * 2 * HD]
            pieces.append(part * cosine - turned(part * sine))
        lane = lax.broadcasted_iota(jnp.int32, cosine.shape, 1)
        part = own[s, inner] + later[s, inner].astype(F32)
        pieces.append(jnp.where(lane < HD, part * cosine - turned(part * sine), part))
        grad_pre = jnp.concatenate(pieces, axis=1)
        grad_ref[at] = grad_pre.astype(BF16)
        left[:, at] = (grad_pre * scale_ref[at]).T.astype(BF16)
    for copy in copies:
        copy.wait()
    put_term(left[...], rows, term_ref)


def qkv_back(place, x_pieces, grad_query, own, later, cosine, sine, scale):
    whole = lambda *shape: pl.BlockSpec(shape, lambda i, p: (0,) * len(shape))
    tokens = 2 * HALF
    return pl.pallas_call(
        qkv_back_kernel,
        grid_spec=pltpu.PrefetchScalarGridSpec(
            num_scalar_prefetch=1,
            grid=(1,),
            in_specs=[ANYWHERE] * 5
            + [
                whole(2, HALF, HEADS * HD), whole(2, HALF, 2 * HD), whole(2, HALF, 2 * HD),
                whole(tokens, 2 * HD), whole(tokens, 2 * HD), whole(tokens, 1),
            ],
            out_specs=[whole(tokens, QKV), whole(4, 2, 2, QKV, B)],
            scratch_shapes=[
                pltpu.VMEM((tokens, D), BF16), pltpu.VMEM((QKV, tokens), BF16), pltpu.SemaphoreType.DMA((10,)),
            ],
        ),
        out_shape=[shaped(tokens, QKV), shaped(4, 2, 2, QKV, B)],
        compiler_params=params("arbitrary"),
        cost_estimate=cost(2 * tokens * QKV * D, 9),
        name="qkv_back",
    )(place, *x_pieces, grad_query, own, later, cosine, sine, scale)


def attention_term_kernel(*refs):
    token_refs, left_ref = refs[1:6], refs[6]
    term_ref, rows, sems = refs[-3:]
    copies = put_tokens(token_refs, rows, sems, 0)
    for copy in copies:
        copy.start()
    left = left_ref[...]
    if left.shape[0] == 2 * HALF:
        left = left.T
    for copy in copies:
        copy.wait()
    put_term(left, rows, term_ref)


def attention_terms(place, pieces, left, name):
    whole = lambda *shape: pl.BlockSpec(shape, lambda i, p: (0,) * len(shape))
    rows = min(left.shape)
    return pl.pallas_call(
        attention_term_kernel,
        grid_spec=pltpu.PrefetchScalarGridSpec(
            num_scalar_prefetch=1,
            grid=(1,),
            in_specs=[ANYWHERE] * 5 + [whole(*left.shape)],
            out_specs=whole(4, 2, 2, rows, B),
            scratch_shapes=[pltpu.VMEM((2 * HALF, D), BF16), pltpu.SemaphoreType.DMA((10,))],
        ),
        out_shape=shaped(4, 2, 2, rows, B),
        compiler_params=params("arbitrary"),
        cost_estimate=cost(2 * 2 * HALF * rows * D, 7),
        name=name,
    )(place, *pieces, left)


def token_places(at, y, core):
    step = 1 - 2 * core
    block = jnp.where(
        at < B, y, jnp.where(at < 2 * B, y + 4 - step, jnp.where(at < 3 * B, y + 4 + step, y + 2))
    )
    row = at % B
    row = jnp.where(at < 3 * B, row, (row + core * (B // 2)) % B)
    return (block % 4) * B + row


def set_bias(place_ref, bias_ref):
    zlo, y, core = place_ref[0], place_ref[1], place_ref[2]
    key_at = token_places(lax.broadcasted_iota(jnp.int32, (HALF, 1), 0), y, core)
    query_at = token_places(lax.broadcasted_iota(jnp.int32, (1, HALF), 1), y, core)
    bias_ref[:HALF, :] = jnp.broadcast_to(jnp.where(zlo == 1, 0.0, -1e30), (HALF, HALF))
    bias_ref[HALF:, :] = jnp.where(key_at <= query_at, 0.0, -1e30)


def attention_kernel(place_ref, *refs):
    w_refs, query_ref, kv_ref, mixed_ref, log_ref = refs[:5], *refs[5:9]
    parts, w_out, bias_ref, weight, sems = refs[9:14], *refs[14:]
    columns = put_columns(place_ref, w_refs, weight, sems, 0)
    back = pltpu.make_async_copy(weight, w_out, sems.at[16])

    @pl.when(pl.program_id(0) == 0)
    def _():
        for copy in columns:
            copy.start()
        set_bias(place_ref, bias_ref)
        for copy in columns:
            copy.wait()
        back.start()

    key, value = kv_ref[0, :, :HD], kv_ref[0, :, HD:]
    for head in range(HEADS):
        scores = times_transposed(key, query_ref[0, head]) + bias_ref[...]
        top = jnp.max(scores, axis=0, keepdims=True)
        weights = jnp.exp(scores - top)
        total = jnp.sum(weights, axis=0, keepdims=True)
        low = (weights * (1.0 / total)).astype(BF16)
        mixed_ref[0, :, head * HD : (head + 1) * HD] = outer_sum(value, low).T.astype(BF16)
        log_ref[0, head] = top + jnp.log(total)
    put_rows(matmul(mixed_ref[0], weight[...]).astype(BF16), parts)

    @pl.when(pl.program_id(0) == 1)
    def _():
        back.wait()


def attention_back_kernel(place_ref, *refs):
    grad_refs, query_ref, kv_ref, log_ref, weight_ref = refs[:5], *refs[5:9]
    grad_query_ref, earlier_ref, own_ref, bias_ref, rows, sems = refs[9:]
    step = pl.program_id(0)
    copies = put_tokens(grad_refs, rows, sems, 0)

    @pl.when(step == 0)
    def _():
        for copy in copies:
            copy.start()
        set_bias(place_ref, bias_ref)
        for copy in copies:
            copy.wait()

    hidden = rows[pl.ds(pl.multiple_of(step * HALF, HALF), HALF), :]
    grads = times_transposed(hidden, weight_ref[...]).astype(BF16)
    key, value = kv_ref[0, :, :HD], kv_ref[0, :, HD:]
    grad_key = jnp.zeros((2 * HALF, HD), F32)
    grad_value = jnp.zeros((2 * HALF, HD), F32)
    for head in range(HEADS):
        lanes = slice(head * HD, (head + 1) * HD)
        query, grad = query_ref[0, head], grads[:, lanes]
        weights = jnp.exp(times_transposed(key, query) + bias_ref[...] - log_ref[0, head])
        grad_weights = times_transposed(value, grad)
        delta = jnp.sum(weights * grad_weights, axis=0, keepdims=True)
        grad_scores = (weights * (grad_weights - delta)).astype(BF16)
        grad_query_ref[0, :, lanes] = outer_sum(key, grad_scores).T * HD ** (-0.5)
        grad_key += matmul(grad_scores, query)
        grad_value += matmul(weights.astype(BF16), grad)
    total = jnp.concatenate([grad_key, grad_value], axis=1)
    earlier_ref[0] = total[:HALF].astype(BF16)
    own_ref[0] = total[HALF:]


def sequence_block(*tail):
    return pl.BlockSpec((1,) + tail, lambda s, place: (s,) + (0,) * len(tail))


def attention_call(kernel, in_specs, out_specs, out_shape, scratch, flops, name):
    return pl.pallas_call(
        kernel,
        grid_spec=pltpu.PrefetchScalarGridSpec(
            num_scalar_prefetch=1,
            grid=(2,),
            in_specs=in_specs,
            out_specs=out_specs,
            scratch_shapes=[pltpu.VMEM((2 * HALF, HALF), F32)] + scratch,
        ),
        out_shape=out_shape,
        compiler_params=params("arbitrary"),
        cost_estimate=cost(flops * 8 * 2 * HALF * HALF * HD * 2, 8),
        name=name,
    )


def attention(place, w_pieces, query, kv):
    return attention_call(
        attention_kernel,
        [ANYWHERE] * 5 + [sequence_block(HEADS, HALF, HD), sequence_block(2 * HALF, 2 * HD)],
        [sequence_block(HALF, HEADS * HD), sequence_block(HEADS, 1, HALF)]
        + part_specs(1)
        + [ANYWHERE],
        [shaped(2, HALF, HEADS * HD), shaped(2, HEADS, 1, HALF, kind=F32)] + PART_SHAPES + [shaped(HEADS * HD, D)],
        [pltpu.VMEM((HEADS * HD, D), BF16), pltpu.SemaphoreType.DMA((17,))],
        3,
        "attention",
    )(place, *w_pieces, query, kv)


def attention_back(place, grad_pieces, query, kv, log_total, weight):
    return attention_call(
        attention_back_kernel,
        [ANYWHERE] * 5
        + [
            sequence_block(HEADS, HALF, HD), sequence_block(2 * HALF, 2 * HD),
            sequence_block(HEADS, 1, HALF), pl.BlockSpec((HEADS * HD, D), lambda s, place: (0, 0)),
        ],
        [sequence_block(HALF, HEADS * HD), sequence_block(HALF, 2 * HD), sequence_block(HALF, 2 * HD)],
        [
            shaped(2, HALF, HEADS * HD, kind=F32),
            shaped(2, HALF, 2 * HD),
            shaped(2, HALF, 2 * HD, kind=F32),
        ],
        [pltpu.VMEM((2 * HALF, D), BF16), pltpu.SemaphoreType.DMA((10,))],
        6,
        "attention_back",
    )(place, *grad_pieces, query, kv, log_total, weight)


def finish_attention_kernel(place, *refs):
    piece_refs, w_query, w_key, w_value, gain_ref = refs[:4], *refs[4:8]
    query_out, key_out, value_out, gain_out, rows = refs[8:]
    for ref, by in zip(piece_refs, range(4)):
        at_y = (place[1] + by) % 4
        for c in range(2):
            piece = ref[c].astype(F32)
            rows[pl.ds(pl.multiple_of((2 * at_y + c) * HEADS * HD, HEADS * HD), HEADS * HD)] = piece[: HEADS * HD]
        both = ref[0].astype(F32) + ref[1].astype(F32)
        at = pl.multiple_of(H * HD + at_y * HD, HD)
        rows[pl.ds(at, HD)] = both[HEADS * HD : (HEADS + 1) * HD]
        rows[pl.ds(at + KV * HD, HD)] = both[(HEADS + 1) * HD :]
    gain = gain_ref[...]
    total = jnp.zeros((B, 1), F32)
    row = 0
    for weight, out in ((w_query, query_out), (w_key, key_out), (w_value, value_out)):
        for i in range(out.shape[1] // B):
            lanes = slice(i * B, (i + 1) * B)
            block = rows[row : row + B].T
            total = total + jnp.sum(block * weight[:, lanes].astype(F32), axis=1, keepdims=True)
            out[:, lanes] = block * gain
            row += B
    gain_out[...] = total


def finish_attention(place, pieces, w_query, w_key, w_value, gain):
    whole = lambda *shape: pl.BlockSpec(shape, lambda i, p: (0,) * len(shape))
    kv = KV * HD
    return pl.pallas_call(
        finish_attention_kernel,
        grid_spec=pltpu.PrefetchScalarGridSpec(
            num_scalar_prefetch=1,
            grid=(1,),
            in_specs=[whole(2, QKV, B)] * 4 + [whole(B, D), whole(B, kv), whole(B, kv), whole(B, 1)],
            out_specs=[whole(B, D), whole(B, kv), whole(B, kv), whole(B, 1)],
            scratch_shapes=[pltpu.VMEM((D + 2 * kv, B), F32)],
        ),
        out_shape=[
            shaped(B, D, kind=F32), shaped(B, kv, kind=F32), shaped(B, kv, kind=F32), shaped(B, 1, kind=F32),
        ],
        compiler_params=params("arbitrary"),
        cost_estimate=cost(0, 4),
        name="finish_attention",
    )(place, *pieces, w_query, w_key, w_value, gain)


def finish_output_kernel(blocks, out):
    for i in range(16):
        out[:, i * B : (i + 1) * B] = blocks[i].astype(F32)


def finish_output(blocks):
    return pl.pallas_call(
        finish_output_kernel,
        out_shape=shaped(B, D, kind=F32),
        compiler_params=params(),
        cost_estimate=cost(0, 2),
        name="finish_output",
    )(blocks)


def feed_forward_kernel(*refs):
    place, token_refs, grad_refs, ff_ref = refs[0], refs[1:6], refs[6:11], refs[11]
    act_ref, act_t, gate_t, up_t = refs[12:16]
    parts, down_out = refs[16:21], refs[21]
    rows_h, rows_g, gate_up, down, slabs, sems = refs[22:]
    step = pl.program_id(0)
    tokens = put_tokens(token_refs, rows_h, sems, 0)
    grads = put_tokens(grad_refs, rows_g, sems, 10)
    weights, loads = [], []
    for x in range(4):
        for by in range(4):
            z = (2 * place[4] + place[0] + by) % 4
            zhi, zlo = z // 2, z % 2
            for core in range(2):
                weights.append(
                    pltpu.make_async_copy(
                        ff_ref.at[x, by, pl.ds(core * FFL, FFL)],
                        gate_up.at[zlo, :, lane_block(zhi, x, core)],
                        sems.at[20 + len(weights)],
                    )
                )
            loads.append(
                pltpu.make_async_copy(
                    ff_ref.at[x, by, pl.ds(2 * FFL, FFL)], slabs.at[zlo, zhi * 4 + x], sems.at[52 + len(loads)]
                )
            )
    back = pltpu.make_async_copy(down, down_out, sems.at[68])

    @pl.when(step == 0)
    def _():
        for copy in tokens + weights + loads + grads:
            copy.start()
        for copy in tokens + weights:
            copy.wait()

    rows = pl.ds(pl.multiple_of(step * HALF, HALF), HALF)
    normed = rows_h[rows, :]
    gate_pre = times_transposed(normed, gate_up[0])
    upward = times_transposed(normed, gate_up[1])

    @pl.when(step == 0)
    def _():
        for copy in loads:
            copy.wait()

        def put(q, carry):
            for half in range(2):
                for p in range(4):
                    one = slabs[half, 2 * q, 2 * p * PIECE : 2 * (p + 1) * PIECE, :].astype(F32)
                    two = slabs[half, 2 * q + 1, 2 * p * PIECE : 2 * (p + 1) * PIECE, :].astype(F32)
                    lane = (half * 8 + 2 * p) * B
                    rows = pl.ds(pl.multiple_of(q * 2 * PIECE, 16), 2 * PIECE)
                    down[rows, lane : lane + B] = jnp.concatenate([one[:PIECE], two[:PIECE]], axis=0).astype(BF16)
                    down[rows, lane + B : lane + 2 * B] = jnp.concatenate(
                        [one[PIECE:], two[PIECE:]], axis=0
                    ).astype(BF16)
            return carry

        lax.fori_loop(0, 4, put, 0)
        back.start()
        for copy in grads:
            copy.wait()

    grad_act = times_transposed(rows_g[rows, :], down[...])
    sigmoid = 1.0 / (1.0 + jnp.exp(-gate_pre))
    silu = gate_pre * sigmoid
    activation = silu * upward
    grad_up = grad_act * silu
    grad_gate = grad_act * upward * (sigmoid * (1.0 + gate_pre * (1.0 - sigmoid)))
    part = matmul(grad_gate.astype(BF16), gate_up[0]) + matmul(grad_up.astype(BF16), gate_up[1])
    put_rows(part.astype(BF16), parts)
    act_ref[...] = activation.astype(BF16)
    act_t[...] = activation.T.astype(BF16)
    gate_t[...] = grad_gate.T.astype(BF16)
    up_t[...] = grad_up.T.astype(BF16)

    @pl.when(step == 1)
    def _():
        back.wait()


def feed_forward(place, tokens, grads, ff_all):
    turned_spec = pl.BlockSpec((FFL, HALF), lambda i, p: (0, i))
    turned_shape = shaped(FFL, 2 * HALF)
    return pl.pallas_call(
        feed_forward_kernel,
        grid_spec=pltpu.PrefetchScalarGridSpec(
            num_scalar_prefetch=1,
            grid=(2,),
            in_specs=[ANYWHERE] * 11,
            out_specs=[pl.BlockSpec((HALF, FFL), lambda i, p: (i, 0))]
            + [turned_spec] * 3
            + part_specs(1)
            + [ANYWHERE],
            scratch_shapes=[
                pltpu.VMEM((2 * HALF, D), BF16),
                pltpu.VMEM((2 * HALF, D), BF16),
                pltpu.VMEM((2, FFL, D), BF16),
                pltpu.VMEM((FFL, D), BF16),
                pltpu.VMEM((2, 8, FFL, B), BF16),
                pltpu.SemaphoreType.DMA((69,)),
            ],
        ),
        out_shape=[shaped(2 * HALF, FFL)] + [turned_shape] * 3 + PART_SHAPES + [shaped(FFL, D)],
        compiler_params=params("arbitrary"),
        cost_estimate=cost(2 * 5 * 2 * HALF * FFL * D, 32),
        name="feed_forward",
    )(place, *tokens, *grads, ff_all)


def along_z(place, zhi, zlo):
    return (2 * zhi + zlo + 4 - 2 * place[4] - place[0]) % 4


def load_tokens(step, refs, rows, sems):
    copies = put_tokens(refs, rows, sems, 0)

    @pl.when(step == 0)
    def _():
        for copy in copies:
            copy.start()
        for copy in copies:
            copy.wait()


def gate_up_kernel(*refs):
    place, token_refs, gate_t, up_t, out_ref, rows, terms, sems = refs[0], refs[1:6], *refs[6:]
    step = pl.program_id(0)
    load_tokens(step, token_refs, rows, sems)
    normed = rows[:, pl.ds(pl.multiple_of(step * 4 * B, 4 * B), 4 * B)]

    def out(i, matrix):
        xs, by = pl.ds(i % 2 * 2, 2), along_z(place, i // 2, matrix)
        return pltpu.make_async_copy(terms.at[xs, by], out_ref.at[xs, by], sems.at[10 + 2 * i + matrix])

    for matrix, left in ((0, gate_t), (1, up_t)):
        term = matmul(left[...], normed).astype(BF16)
        by = along_z(place, step // 2, matrix)
        for j in range(2):
            terms[step % 2 * 2 + j, by, 0:FFL, :] = term[:, 2 * j * B : (2 * j + 1) * B]
            terms[step % 2 * 2 + j, by, FFL:, :] = term[:, (2 * j + 1) * B : (2 * j + 2) * B]
        out(step, matrix).start()

    @pl.when(step == 3)
    def _():
        for i in range(4):
            for matrix in range(2):
                out(i, matrix).wait()


def down_kernel(*refs):
    place, grad_refs, act_t, out_ref, rows, terms, sems = refs[0], refs[1:6], *refs[6:]
    step = pl.program_id(0)
    load_tokens(step, grad_refs, rows, sems)
    term = matmul(act_t[...], rows[:, pl.ds(pl.multiple_of(step * 4 * B, 4 * B), 4 * B)])
    for j in range(2):
        p = (2 * step + j) % 4
        at = pl.ds(pl.multiple_of(p * 2 * PIECE, 16), 2 * PIECE)
        for zx in range(8):
            slab = term[zx * PIECE : (zx + 1) * PIECE]
            low, high = slab[:, 2 * j * B : (2 * j + 1) * B], slab[:, (2 * j + 1) * B : (2 * j + 2) * B]
            by = along_z(place, zx // 4, step // 2)
            terms[zx % 4, by, at, :] = jnp.concatenate([low, high], axis=0).astype(BF16)

    def out(half, zhi):
        by = along_z(place, zhi, half)
        return pltpu.make_async_copy(terms.at[:, by], out_ref.at[:, by], sems.at[10 + 2 * half + zhi])

    @pl.when(step % 2 == 1)
    def _():
        for zhi in range(2):
            out(step // 2, zhi).start()

    @pl.when(step == 3)
    def _():
        for half in range(2):
            for zhi in range(2):
                out(half, zhi).wait()


def ff_terms(kernel, place, pieces, lefts, rows, name):
    whole = pl.BlockSpec((FFL, 2 * HALF), lambda i, p: (0, 0))
    return pl.pallas_call(
        kernel,
        grid_spec=pltpu.PrefetchScalarGridSpec(
            num_scalar_prefetch=1,
            grid=(4,),
            in_specs=[ANYWHERE] * 5 + [whole] * len(lefts),
            out_specs=ANYWHERE,
            scratch_shapes=[
                pltpu.VMEM((2 * HALF, D), BF16),
                pltpu.VMEM((4, 4, rows, B), BF16),
                pltpu.SemaphoreType.DMA((18,)),
            ],
        ),
        out_shape=shaped(4, 4, rows, B),
        compiler_params=params("arbitrary"),
        cost_estimate=cost(2 * len(lefts) * 2 * HALF * FFL * D, 8 + 4 * len(lefts)),
        name=name,
    )(place, *pieces, *lefts)


def finish_hidden_kernel(*refs):
    place, piece_refs, weight_ref, gain_ref, out_ref, gain_out, rows = refs[0], refs[1:5], *refs[5:]
    for ref, by in zip(piece_refs, range(4)):
        at_y = (place[1] + by) % 4
        for core in range(2):
            slab = ref[0, core].astype(F32)
            for zx in range(8):
                at = pl.multiple_of((2 * zx + core) * 4 * PIECE + at_y * PIECE, 8)
                rows[pl.ds(at, PIECE)] = slab[zx * PIECE : (zx + 1) * PIECE]
    gain = gain_ref[...]
    total = jnp.zeros((B, 1), F32)
    for i in range(FF // B):
        lanes = slice(i * B, (i + 1) * B)
        block = rows[lanes].T
        total = total + jnp.sum(block * weight_ref[:, lanes].astype(F32), axis=1, keepdims=True)
        out_ref[:, lanes] = block * gain
    gain_out[...] = total


def finish_hidden(place, pieces, matrix, weight, gain):
    own, after, low, high, before = pieces
    at = lambda m: pl.BlockSpec((1, 2, FFL, B), lambda i, p: (m, 0, 0, 0))
    whole = lambda *shape: pl.BlockSpec(shape, lambda i, p: (0,) * len(shape))
    return pl.pallas_call(
        finish_hidden_kernel,
        grid_spec=pltpu.PrefetchScalarGridSpec(
            num_scalar_prefetch=1,
            grid=(1,),
            in_specs=[at(matrix), at(matrix), at(0), at(matrix), whole(B, FF), whole(B, 1)],
            out_specs=[whole(B, FF), whole(B, 1)],
            scratch_shapes=[pltpu.VMEM((FF, B), F32)],
        ),
        out_shape=[shaped(B, FF, kind=F32), shaped(B, 1, kind=F32)],
        compiler_params=params("arbitrary"),
        cost_estimate=cost(0, 6),
        name="finish_hidden",
    )(place, own, after, (low, high)[matrix], before, weight, gain)


def finish_down_kernel(place, own, after, low, high, before, out_ref):
    for refs, by in (((own, own), 0), ((after, after), 1), ((low, high), 2), ((before, before), 3)):
        rows = pl.ds(pl.multiple_of((place[1] + by) % 4 * PIECE, 8), PIECE)
        for half in range(2):
            slab = refs[half][half if by != 2 else 0].astype(F32)
            for t in range(8):
                lane = (half * 8 + t) * B
                out_ref[rows, lane : lane + B] = slab[t * PIECE : (t + 1) * PIECE]


def finish_down(place, pieces):
    halves = lambda n: pl.BlockSpec((n, FFL, B), lambda i, p: (0, 0, 0))
    return pl.pallas_call(
        finish_down_kernel,
        grid_spec=pltpu.PrefetchScalarGridSpec(
            num_scalar_prefetch=1,
            grid=(1,),
            in_specs=[halves(2), halves(2), halves(1), halves(1), halves(2)],
            out_specs=pl.BlockSpec((4 * PIECE, D), lambda i, p: (0, 0)),
        ),
        out_shape=shaped(4 * PIECE, D, kind=F32),
        compiler_params=params("arbitrary"),
        cost_estimate=cost(0, 5),
        name="finish_down",
    )(place, *pieces)


def own_rows(rows_all, y, core, per):
    return lax.dynamic_slice_in_dim(rows_all, (2 * y + core) * per, per, 0)


class Flow:
    def __init__(self, steps):
        self.steps, self.result, self.sent = steps, None, None
        self.move(None)

    def move(self, arrived):
        try:
            self.sent = self.steps.send(arrived)
        except StopIteration as end:
            self.sent, self.result = (), end.value


def stage(flows, *values):
    flows = [flow for flow in flows if flow.result is None]
    sizes = [len(flow.sent) for flow in flows]
    leaves, tree = jax.tree.flatten(values)
    tied = tie(*[v for flow in flows for v in flow.sent], *leaves)
    for flow, size in zip(flows, sizes):
        flow.move(tied[:size])
        tied = tied[size:]
    return jax.tree.unflatten(tree, tied)


def gather_steps(block):
    (other,) = yield (swap_core(block),)
    pair = jnp.stack([block, other])
    (got,) = yield (along_y(pair),)
    far, swapped = yield (along_y(send_half(got)), swap_core(got))
    (far_swapped,) = yield (swap_core(far),)
    return pair, got, swapped, far, far_swapped


def scatter_steps(parts):
    core = lax.axis_index("core")
    first, behind, ahead, far, far_other = parts
    (far_got,) = yield (swap_core(far_other),)
    far = add(far, far_got).astype(BF16)
    low, behind_got, first_got = yield (along_y(far), swap_core(behind), swap_core(first[1]))
    ahead = add(ahead, behind_got).astype(BF16)
    mine = add(lax.dynamic_slice_in_dim(ahead, core * (B // 2), B // 2, 1), low).astype(BF16)
    ahead = lax.dynamic_update_slice_in_dim(ahead, mine, core * (B // 2), 1)
    (got,) = yield (along_y(ahead),)
    (last,) = yield (swap_core(got[1]),)
    return add(first[0], first_got) + got[0].astype(F32) + last.astype(F32)


def ring_gather_steps(block, axis):
    half = block.shape[0] // 2
    before, after = yield (shift(block, axis, 1), shift(block, axis, -1))
    low, high = yield (shift(before[:half], axis, 1), shift(after[half:], axis, -1))
    return block, after, low, high, before


def ring_scatter_steps(parts, axis):
    half = parts[2].shape[0] // 2
    low, high = yield (shift(parts[2][:half], axis, 1), shift(parts[2][half:], axis, -1))
    after = jnp.concatenate([add(parts[1][:half], low).astype(BF16), parts[1][half:]], axis=0)
    before = jnp.concatenate([parts[3][:half], add(parts[3][half:], high).astype(BF16)], axis=0)
    from_before, from_after = yield (shift(after, axis, 1), shift(before, axis, -1))
    return add(parts[0], from_before) + from_after.astype(F32)


def on_device(
    layer_input,
    positions,
    attn_gain,
    w_query,
    w_key,
    w_value,
    w_output,
    mlp_gain,
    w_gate,
    w_up,
    w_down,
    out_grad,
):
    zlo, y, zhi, x, core = (lax.axis_index(axis) for axis in AXES)
    place = jnp.stack([zlo, y, core, x, zhi]).astype(jnp.int32)

    def by_core(mine, got):
        return jnp.where(core == 0, jnp.stack([mine, got]), jnp.stack([got, mine]))

    def by_zlo(mine, got):
        return jnp.where(zlo == 0, jnp.stack([mine, got]), jnp.stack([got, mine]))

    def by_zhi(mine, got):
        return jnp.where(zhi == 0, jnp.stack([mine, got]), jnp.stack([got, mine]))

    def trio(mine, other, axis):
        across = lax.ppermute(other, (axis, "core"), [(i, 3 - i) for i in range(4)])
        return shift(mine, axis, 1), swap_core(other), across

    def column_steps(mine, got):
        pair = by_core(mine, got)
        (got,) = yield (shift(pair, "zhi", 1),)
        return (yield from ring_gather_steps(by_zhi(pair, got), "x"))

    def output_steps(mine, other):
        there, here, across = yield trio(mine, other, "zhi")
        column = by_zhi(by_core(mine, here), by_core(there, across))
        return (yield from ring_gather_steps(column, "x"))

    def hidden_steps(mine, got, down):
        piece = jnp.concatenate([by_core(mine, got).reshape(2 * FFL, B), down], axis=0)
        pieces = yield from ring_gather_steps(piece, "z")
        return jnp.concatenate(pieces, axis=0).reshape(4, 3 * FFL, B)

    def of_core(pair, other=False):
        return lax.dynamic_index_in_dim(pair, 1 - core if other else core, 0, keepdims=False)

    def whole_ring(pieces):
        own, after, low, high, before = pieces
        return own, after, jnp.concatenate([low, high], axis=0), before

    def attention_steps(column):
        keep = lax.dynamic_index_in_dim(column, zhi, 0, keepdims=False)
        send = lax.dynamic_index_in_dim(column, 1 - zhi, 0, keepdims=False)
        (got,) = yield (shift(send, "zhi", 1),)
        pair = add(keep, got).astype(BF16)
        mine, other = of_core(pair), of_core(pair, True)
        there, here, across = yield trio(mine, other, "zlo")
        own = by_core(add(mine, there), add(here, across)).astype(BF16)
        return (yield from ring_gather_steps(own, "y"))

    def gate_up_steps(sums):
        own = yield from ring_scatter_steps([sums[i] for i in range(4)], "z")
        pair = own.astype(BF16).reshape(2, FFL, B)
        mine, other = of_core(pair), of_core(pair, True)
        there, here, across = yield trio(mine, other, "zlo")
        return (yield from ring_gather_steps(by_zlo(by_core(mine, here), by_core(there, across)), "y"))

    def down_steps(sums):
        own = yield from ring_scatter_steps([sums[i] for i in range(4)], "z")
        own = own.astype(BF16)
        (got,) = yield (shift(own, "zlo", 1),)
        return (yield from ring_gather_steps(by_zlo(own, got), "y"))

    x_low = layer_input[0]
    frequency = theta ** (-jnp.arange(0, HD, 2).astype(F32) / HD)
    angles = positions[0].astype(F32)[:, None] * frequency
    tables = []
    for table in (jnp.cos(angles), jnp.sin(angles)):
        high = lax.reduce_precision(table, 8, 7)
        tables += [high.astype(BF16), (table - high).astype(BF16)]
    tokens = Flow(gather_steps(jnp.concatenate([x_low, *tables], axis=1)))
    grads = Flow(gather_steps(out_grad[0]))
    qkv_mine, qkv_other = prepare_qkv(place, w_query, w_key, w_value, attn_gain[:, None])
    qkv_mine, qkv_got, gain_two, w_out = stage([tokens], qkv_mine, swap_core(qkv_other), mlp_gain[:, None], w_output)

    columns = Flow(column_steps(qkv_mine, qkv_got))
    o_rows = lax.all_to_all(w_out.reshape(B, 16, B).transpose(1, 0, 2), FSDP, 0, 0, tiled=True)
    ff_mine, ff_other, ff_down = prepare_ff(place, w_gate, w_up, w_down, gain_two)
    ff_mine, ff_got, ff_down, x_low, o_rows = stage(
        [tokens, columns], ff_mine, swap_core(ff_other), ff_down, x_low, o_rows
    )

    inputs = x_low.astype(F32)
    scale_one = lax.rsqrt(jnp.mean(inputs * inputs, axis=-1, keepdims=True) + eps)
    o_rows = o_rows.reshape(D, B)
    mine, other = own_rows(o_rows, y, core, HEADS * HD), own_rows(o_rows, y, 1 - core, HEADS * HD)
    scale_one, mine, other, ff_mine, ff_got, ff_down = stage(
        [tokens, columns, grads], scale_one, mine, other, ff_mine, ff_got, ff_down
    )

    outputs = Flow(output_steps(mine, other))
    ff_mine, ff_got, ff_down = stage([tokens, columns, outputs], ff_mine, ff_got, ff_down)

    hidden_rows = Flow(hidden_steps(ff_mine, ff_got, ff_down))
    x_pieces = tokens.result
    query, key_value, scale_all, cosine, sine, qkv_full = project_qkv(place, x_pieces, columns.result)
    query, key_value = stage([hidden_rows, outputs, grads], query, key_value)

    earlier = lax.ppermute(key_value, "zlo", [(0, 1)])
    query, key_value, earlier = stage([outputs, hidden_rows], query, key_value, earlier)
    ff_all = lax.all_gather(hidden_rows.result, "x", axis=0, tiled=False)

    key_value = jnp.concatenate([earlier, key_value], axis=1)
    mixed, log_total, *parts, o_full = attention(place, outputs.result, query, key_value)
    parts = stage([grads], *parts)
    sums = Flow(scatter_steps(parts))
    stage([sums, grads])
    grad_pieces = grads.result
    for _ in range(3):
        stage([sums])
    hidden = inputs + sums.result
    scale_two = lax.rsqrt(jnp.mean(hidden * hidden, axis=-1, keepdims=True) + eps)
    normed = Flow(gather_steps((hidden * scale_two).astype(BF16)))
    for _ in range(4):
        stage([normed])
    normed_pieces = normed.result

    activation, act_t, gate_t, up_t, *parts, down_full = feed_forward(place, normed_pieces, grad_pieces, ff_all)
    sums = Flow(scatter_steps(parts))
    (act_t,) = stage([sums], act_t)
    down_terms = ff_terms(down_kernel, place, grad_pieces, (act_t,), FFL, "down_terms")
    down_terms, gate_t = stage([sums], down_terms, gate_t)
    down_sum = lax.psum_scatter(down_terms, "x", scatter_dimension=0, tiled=True)[0]
    gate_up_terms = ff_terms(gate_up_kernel, place, normed_pieces, (gate_t, up_t), 2 * FFL, "gate_up_terms")
    (gate_up_terms,) = stage([sums], gate_up_terms)
    gate_up_sum = lax.psum_scatter(gate_up_terms, "x", scatter_dimension=0, tiled=True)[0]
    stage([sums])

    grad_normed_two = sums.result
    mean_two = jnp.mean(grad_normed_two * hidden, axis=-1, keepdims=True)
    grad_hidden = (
        out_grad[0].astype(F32)
        + scale_two * grad_normed_two
        - hidden * (scale_two * scale_two * scale_two) * mean_two
    )
    hidden_grads = Flow(gather_steps(grad_hidden.astype(BF16)))
    (activation,) = stage([hidden_grads], activation)
    down_parts = project(activation, down_full)
    down_parts = stage([hidden_grads], *down_parts)
    result = Flow(scatter_steps(down_parts))
    (down_sum,) = stage([hidden_grads], down_sum)
    down = Flow(down_steps(down_sum))
    stage([hidden_grads, result, down])

    hidden_grad_pieces = hidden_grads.result
    grad_query, grad_earlier, grad_own = attention_back(
        place, hidden_grad_pieces, query, key_value, log_total, o_full
    )
    grad_query, grad_earlier, grad_own, mixed = stage([result, down], grad_query, grad_earlier, grad_own, mixed)

    later = lax.ppermute(grad_earlier, "zlo", [(1, 0)])
    output_terms = attention_terms(
        place, hidden_grad_pieces, mixed.reshape(2 * HALF, HEADS * HD), "output_terms"
    )
    later, grad_query, output_terms, gate_up_sum = stage(
        [result, down], later, grad_query, output_terms, gate_up_sum
    )

    output_sum = lax.psum_scatter(output_terms, "x", scatter_dimension=0, tiled=True)[0]
    gate_up = Flow(gate_up_steps(gate_up_sum))
    grad_pre, terms = qkv_back(place, x_pieces, grad_query, grad_own, later, cosine, sine, scale_all)
    grad_pre, terms = stage([gate_up, down, result], grad_pre, terms)

    attention_sum = lax.psum_scatter(terms, "x", scatter_dimension=0, tiled=True)[0]
    parts = project(grad_pre, qkv_full)
    *parts, output_sum = stage([gate_up, down], *parts, output_sum)

    sums = Flow(scatter_steps(parts))
    output_sums = Flow(attention_steps(output_sum))
    (attention_sum,) = stage([sums, gate_up, output_sums], attention_sum)
    attention_sums = Flow(attention_steps(attention_sum))
    stage([sums, output_sums, attention_sums])
    stage([output_sums, attention_sums, gate_up])
    stage([sums, output_sums, attention_sums, gate_up])

    ring = jnp.roll(jnp.stack(whole_ring(output_sums.result)), y, axis=0).reshape(16, B, B)
    stage([attention_sums])
    output_grad = lax.all_to_all(ring, FSDP, 0, 0, tiled=True)
    stage([sums])
    grad_normed = sums.result
    mean_one = jnp.mean(grad_normed * inputs, axis=-1, keepdims=True)
    input_grad = (
        grad_hidden
        + scale_one * grad_normed
        - inputs * (scale_one * scale_one * scale_one) * mean_one
    )
    input_grad = input_grad.astype(BF16)
    gain_two = mlp_gain[:, None]
    gate_grad, gate_gain = finish_hidden(place, gate_up.result, 0, w_gate, gain_two)
    up_grad, up_gain = finish_hidden(place, gate_up.result, 1, w_up, gain_two)
    down_grad = finish_down(place, down.result)
    query_grad, key_grad, value_grad, attn_gain_grad = finish_attention(
        place, whole_ring(attention_sums.result), w_query, w_key, w_value, attn_gain[:, None]
    )
    output_grad, gate_grad, up_grad, down_grad, query_grad = tie(output_grad, gate_grad, up_grad, down_grad, query_grad)
    output_grad = finish_output(output_grad)
    return (
        (hidden + result.result).astype(BF16)[None],
        input_grad[None],
        attn_gain_grad[:, 0],
        query_grad,
        key_grad,
        value_grad,
        output_grad,
        (gate_gain + up_gain)[:, 0],
        gate_grad,
        up_grad,
        down_grad,
    )


def solution(mesh):
    split = Mesh(mesh.devices.reshape(2, 4, 2, 4, 2), AXES)
    tokens = P(FSDP, SEQ, None)
    rows = P(FSDP, None)
    gain = P(FSDP)
    in_specs = (
        tokens, P(FSDP, SEQ), gain, rows, rows, rows, rows, gain, rows, rows, rows, tokens,
    )
    out_specs = (tokens, tokens, gain, rows, rows, rows, rows, gain, rows, rows, rows)
    return jax.shard_map(
        on_device, mesh=split, in_specs=in_specs, out_specs=out_specs, check_vma=False
    )
```

```python
import jax
import jax.numpy as jnp
from jax import lax
from jax.experimental import pallas as pl
from jax.experimental.pallas import tpu as pltpu
from jax.sharding import Mesh
from jax.sharding import PartitionSpec as P

H = 32
KV = 4
HD = 64
D = 2048
FF = 5632
B = 128
HALF = 512
HEADS = 4
FFL = 704
PIECE = 88

eps = 1e-05
theta = 10000.0
F32 = jnp.float32
BF16 = jnp.bfloat16
AXES = ("zlo", "y", "zhi", "x", "core")
FSDP = ("zhi", "x", "core")
SEQ = ("zlo", "y")


def matmul(left, right):
    return jnp.dot(left, right, preferred_element_type=F32)


def times_transposed(left, right):
    return lax.dot_general(left, right, (((1,), (1,)), ((), ())), preferred_element_type=F32)


def outer_sum(left, right):
    return lax.dot_general(left, right, (((0,), (0,)), ((), ())), preferred_element_type=F32)


def shift(value, axis, by):
    if axis == "z":
        at = [2 * (z % 2) + z // 2 for z in range(4)]
        return lax.ppermute(value, ("zlo", "zhi"), [(at[z], at[(z + by) % 4]) for z in range(4)])
    size = lax.axis_size(axis)
    return lax.ppermute(value, axis, [(i, (i + by) % size) for i in range(size)])


def swap_core(value):
    return shift(value, "core", 1)


def small_gather(block, axis):
    return shift(block, axis, -1), shift(block, axis, 2), shift(block, axis, 1)


def tie(*values):
    return lax.optimization_barrier(values)


def add(left, right):
    return left.astype(F32) + right.astype(F32)


def along_y(value):
    pairs = []
    for i in range(4):
        pairs.append((2 * i, 2 * ((i + 1) % 4)))
        pairs.append((2 * i + 1, 2 * ((i + 3) % 4) + 1))
    return lax.ppermute(value, ("y", "core"), pairs)


def send_half(got):
    core = lax.axis_index("core")
    return lax.dynamic_slice_in_dim(got, core * (B // 2), B // 2, 1)


FLIPPED = (0, 0, 1, 0, 1)
LENGTHS = (B, B, B, B // 2, B // 2)


def put_tokens(refs, rows_ref, sems, start):
    lanes = pl.ds(0, rows_ref.shape[1])
    copies = []
    row = 0
    for s in range(2):
        for ref, flip, length in zip(refs, FLIPPED, LENGTHS):
            copies.append(
                pltpu.make_async_copy(
                    ref.at[s ^ flip, :, lanes], rows_ref.at[pl.ds(row, length)], sems.at[start + len(copies)]
                )
            )
            row += length
    return copies


TILE = 256
WIDE = D + B
VMEM_LIMIT = 56 * 2**20
ANYWHERE = pl.BlockSpec(memory_space=pl.ANY)


def params(*kinds):
    return pltpu.CompilerParams(dimension_semantics=kinds or None, vmem_limit_bytes=VMEM_LIMIT)


def cost(flops, megabytes):
    return pl.CostEstimate(flops=flops, bytes_accessed=int(megabytes * 2**20), transcendentals=0)


def shaped(*shape, kind=BF16):
    return jax.ShapeDtypeStruct(shape, kind)


PARTS = ((B, False), (B, True), (B, False), (B // 2, False), (B // 2, True))
PART_SHAPES = [jax.ShapeDtypeStruct((2, n, D), BF16) for n, _ in PARTS]


def part_specs(steps):
    def of(turn):
        return lambda i, *_: (1 - i // steps if turn else i // steps, 0, 0)

    return [pl.BlockSpec((1, n, D), of(turn)) for n, turn in PARTS]


def put_parts(step, tile, refs):
    @pl.when(step % 2 == 0)
    def _():
        refs[0][0] = tile[:B]
        refs[1][0] = tile[B:]

    @pl.when(step % 2 == 1)
    def _():
        refs[2][0] = tile[:B]
        refs[3][0] = tile[B : B + B // 2]
        refs[4][0] = tile[B + B // 2 :]


def put_rows(rows, refs):
    row = 0
    for ref, (length, _) in zip(refs, PARTS):
        ref[0] = rows[row : row + length]
        row += length


def turned(values):
    lane = lax.broadcasted_iota(jnp.int32, values.shape, 1) % HD
    return jnp.where(lane < HD // 2, -pltpu.roll(values, 2 * HD - HD // 2, 1), pltpu.roll(values, HD // 2, 1))


def lane_block(zhi, x, core):
    return pl.ds(pl.multiple_of((zhi * 8 + x * 2 + core) * B, B), B)


def put_columns(place, refs, into, sems, start):
    copies = []
    for ref, by, first in zip(refs, (0, 1, 2, 2, 3), (0, 0, 0, 1, 0)):
        for i in range(ref.shape[0]):
            for core in range(2):
                lanes = lane_block(first + i, (place[3] + by) % 4, core)
                copies.append(
                    pltpu.make_async_copy(ref.at[i, core], into.at[:, lanes], sems.at[start + len(copies)])
                )
    return copies


def prepare_qkv_kernel(place, q_mine, q_other, w_key, w_value, gain, mine_ref, other_ref, k_rows, v_rows):
    scale = gain[...]
    k_rows[...] = (w_key[...].astype(F32) * scale).T
    v_rows[...] = (w_value[...].astype(F32) * scale).T
    rows = pl.ds(pl.multiple_of(place[1] * HD, HD), HD)
    for source, out in ((q_mine, mine_ref), (q_other, other_ref)):
        out[: HEADS * HD] = (source[...].astype(F32) * scale).T.astype(BF16)
        out[HEADS * HD : (HEADS + 1) * HD] = k_rows[rows].astype(BF16)
        out[(HEADS + 1) * HD :] = v_rows[rows].astype(BF16)


QKV = (HEADS + 2) * HD


def prepare_qkv(place, w_query, w_key, w_value, gain):
    whole = lambda *shape: pl.BlockSpec(shape, lambda i, p: (0,) * len(shape))
    return pl.pallas_call(
        prepare_qkv_kernel,
        grid_spec=pltpu.PrefetchScalarGridSpec(
            num_scalar_prefetch=1,
            grid=(1,),
            in_specs=[
                pl.BlockSpec((B, HEADS * HD), lambda i, p: (0, 2 * p[1] + p[2])),
                pl.BlockSpec((B, HEADS * HD), lambda i, p: (0, 2 * p[1] + 1 - p[2])),
                whole(B, KV * HD), whole(B, KV * HD), whole(B, 1),
            ],
            out_specs=[whole(QKV, B), whole(QKV, B)],
            scratch_shapes=[pltpu.VMEM((KV * HD, B), F32), pltpu.VMEM((KV * HD, B), F32)],
        ),
        out_shape=[shaped(QKV, B), shaped(QKV, B)],
        compiler_params=params("arbitrary"),
        cost_estimate=cost(0, 1),
        name="prepare_qkv",
    )(place, w_query, w_query, w_key, w_value, gain)


def prepare_ff_kernel(place, w_gate, w_up, w_down, gain, mine_ref, other_ref, down_ref, picked, rows, down_rows, sems):
    zlo, y, core = place[0], place[1], place[2]
    down = pltpu.make_async_copy(
        w_down.at[:, pl.ds(pl.multiple_of(zlo * (D // 2), D // 2), D // 2)], down_rows, sems.at[1]
    )
    down.start()

    @pl.when(zlo == 0)
    def _():
        copy = pltpu.make_async_copy(w_gate, picked, sems.at[0])
        copy.start()
        copy.wait()

    @pl.when(zlo == 1)
    def _():
        copy = pltpu.make_async_copy(w_up, picked, sems.at[0])
        copy.start()
        copy.wait()

    scale = gain[...]
    for i in range(FF // B):
        rows[i * B : (i + 1) * B] = (picked[:, i * B : (i + 1) * B].astype(F32) * scale).T
    for which, out in ((core, mine_ref), (1 - core, other_ref)):
        slabs = []
        for zx in range(8):
            at = pl.multiple_of(zx * 2 * 4 * PIECE + which * 4 * PIECE + y * PIECE, 8)
            slabs.append(rows[pl.ds(at, PIECE)])
        out[...] = jnp.concatenate(slabs, axis=0).astype(BF16)
    down.wait()
    for t in range(8):
        rows[t * 4 * PIECE : (t + 1) * 4 * PIECE] = down_rows[:, t * B : (t + 1) * B].astype(F32)
    slabs = [rows[pl.ds(pl.multiple_of(t * 4 * PIECE + y * PIECE, 8), PIECE)] for t in range(8)]
    down_ref[...] = jnp.concatenate(slabs, axis=0).astype(BF16)


def prepare_ff(place, w_gate, w_up, w_down, gain):
    return pl.pallas_call(
        prepare_ff_kernel,
        grid_spec=pltpu.PrefetchScalarGridSpec(
            num_scalar_prefetch=1,
            grid=(1,),
            in_specs=[ANYWHERE, ANYWHERE, ANYWHERE, pl.BlockSpec((B, 1), lambda i, p: (0, 0))],
            out_specs=[pl.BlockSpec((FFL, B), lambda i, p: (0, 0))] * 3,
            scratch_shapes=[
                pltpu.VMEM((B, FF), BF16),
                pltpu.VMEM((FF, B), F32),
                pltpu.VMEM((4 * PIECE, D // 2), BF16),
                pltpu.SemaphoreType.DMA((2,)),
            ],
        ),
        out_shape=[shaped(FFL, B)] * 3,
        compiler_params=params("arbitrary"),
        cost_estimate=cost(0, 6),
        name="prepare_ff",
    )(place, w_gate, w_up, w_down, gain)


def project_qkv_kernel(*refs):
    place, x_refs, w_refs = refs[0], refs[1:6], refs[6:11]
    query_ref, kv_ref, scale_ref, cosine_ref, sine_ref, w_out, rows, weights, sems = refs[11:]
    step = pl.program_id(0)
    tokens = put_tokens(x_refs, rows, sems, 0)
    columns = put_columns(place, w_refs, weights, sems, 10)
    back = pltpu.make_async_copy(weights, w_out, sems.at[26])

    @pl.when(step == 0)
    def _():
        for copy in columns + tokens:
            copy.start()
        for copy in columns:
            copy.wait()
        back.start()
        for copy in tokens:
            copy.wait()

    at = pl.ds(pl.multiple_of(step * TILE, TILE), TILE)
    tile = rows[at, :D]
    wide = tile.astype(F32)
    scale = lax.rsqrt(jnp.mean(wide * wide, axis=-1, keepdims=True) + eps)
    scale_ref[...] = scale
    pre = times_transposed(tile, weights[...]) * scale
    tables = rows[at, D:].astype(F32)
    tables = tables + pltpu.roll(tables, B - HD // 2, 1)
    cosine = jnp.concatenate([tables[:, : HD // 2]] * 4, axis=1)
    sine = jnp.concatenate([tables[:, HD : HD + HD // 2]] * 4, axis=1)
    cosine_ref[...] = cosine
    sine_ref[...] = sine
    for i in range(2):
        part = pre[:, i * 2 * HD : (i + 1) * 2 * HD]
        part = (part * cosine + turned(part) * sine).astype(BF16) * HD ** (-0.5)
        query_ref[0, 2 * i] = part[:, :HD]
        query_ref[0, 2 * i + 1] = part[:, HD:]
    part = pre[:, HEADS * HD :]
    lane = lax.broadcasted_iota(jnp.int32, part.shape, 1)
    kv_ref[0] = jnp.where(lane < HD, part * cosine + turned(part) * sine, part).astype(BF16)

    @pl.when(step == 3)
    def _():
        back.wait()


def project_qkv(place, x_pieces, w_pieces):
    tile = lambda lanes: pl.BlockSpec((TILE, lanes), lambda i, p: (i, 0))
    return pl.pallas_call(
        project_qkv_kernel,
        grid_spec=pltpu.PrefetchScalarGridSpec(
            num_scalar_prefetch=1,
            grid=(4,),
            in_specs=[ANYWHERE] * 10,
            out_specs=[
                pl.BlockSpec((1, HEADS, TILE, HD), lambda i, p: (i // 2, 0, i % 2, 0)),
                pl.BlockSpec((1, TILE, 2 * HD), lambda i, p: (i // 2, i % 2, 0)),
                tile(1), tile(2 * HD), tile(2 * HD),
                ANYWHERE,
            ],
            scratch_shapes=[
                pltpu.VMEM((2 * HALF, WIDE), BF16),
                pltpu.VMEM((QKV, D), BF16),
                pltpu.SemaphoreType.DMA((27,)),
            ],
        ),
        out_shape=[
            shaped(2, HEADS, HALF, HD), shaped(2, HALF, 2 * HD), shaped(2 * HALF, 1, kind=F32),
            shaped(2 * HALF, 2 * HD, kind=F32), shaped(2 * HALF, 2 * HD, kind=F32), shaped(QKV, D),
        ],
        compiler_params=params("arbitrary"),
        cost_estimate=cost(2 * 2 * HALF * QKV * D, 8),
        name="project_qkv",
    )(place, *x_pieces, *w_pieces)


def project_kernel(left_ref, weight_ref, *parts):
    put_parts(pl.program_id(0), matmul(left_ref[...], weight_ref[...]).astype(BF16), parts)


def project(left, weight):
    depth = left.shape[1]
    return pl.pallas_call(
        project_kernel,
        grid=(4,),
        in_specs=[pl.BlockSpec((TILE, depth), lambda i: (i, 0)), pl.BlockSpec((depth, D), lambda i: (0, 0))],
        out_specs=part_specs(2),
        out_shape=PART_SHAPES,
        compiler_params=params("arbitrary"),
        cost_estimate=cost(2 * 2 * HALF * depth * D, 8),
        name="project",
    )(left, weight)


def put_term(left, rows, term_ref):
    def one(i, carry):
        term = matmul(left, rows[:, pl.ds(pl.multiple_of(i * 4 * B, 4 * B), 4 * B)]).astype(BF16)
        for j in range(2):
            zx = 2 * i + j
            term_ref[zx % 4, zx // 4, 0] = term[:, 2 * j * B : (2 * j + 1) * B]
            term_ref[zx % 4, zx // 4, 1] = term[:, (2 * j + 1) * B : (2 * j + 2) * B]
        return carry

    lax.fori_loop(0, 4, one, 0)


def qkv_back_kernel(*refs):
    x_refs, grad_q, own, later, cosine_ref, sine_ref, scale_ref = refs[1:6], *refs[6:12]
    grad_ref, term_ref, rows, left, sems = refs[12:]
    copies = put_tokens(x_refs, rows, sems, 0)
    for copy in copies:
        copy.start()
    for step in range(4):
        at, s = slice(step * TILE, (step + 1) * TILE), step // 2
        inner = slice(step % 2 * TILE, (step % 2 + 1) * TILE)
        cosine, sine = cosine_ref[at], sine_ref[at]
        pieces = []
        for i in range(2):
            part = grad_q[s, inner, i * 2 * HD : (i + 1) * 2 * HD]
            pieces.append(part * cosine - turned(part * sine))
        lane = lax.broadcasted_iota(jnp.int32, cosine.shape, 1)
        part = own[s, inner] + later[s, inner].astype(F32)
        pieces.append(jnp.where(lane < HD, part * cosine - turned(part * sine), part))
        grad_pre = jnp.concatenate(pieces, axis=1)
        grad_ref[at] = grad_pre.astype(BF16)
        left[:, at] = (grad_pre * scale_ref[at]).T.astype(BF16)
    for copy in copies:
        copy.wait()
    put_term(left[...], rows, term_ref)


def qkv_back(place, x_pieces, grad_query, own, later, cosine, sine, scale):
    whole = lambda *shape: pl.BlockSpec(shape, lambda i, p: (0,) * len(shape))
    tokens = 2 * HALF
    return pl.pallas_call(
        qkv_back_kernel,
        grid_spec=pltpu.PrefetchScalarGridSpec(
            num_scalar_prefetch=1,
            grid=(1,),
            in_specs=[ANYWHERE] * 5
            + [
                whole(2, HALF, HEADS * HD), whole(2, HALF, 2 * HD), whole(2, HALF, 2 * HD),
                whole(tokens, 2 * HD), whole(tokens, 2 * HD), whole(tokens, 1),
            ],
            out_specs=[whole(tokens, QKV), whole(4, 2, 2, QKV, B)],
            scratch_shapes=[
                pltpu.VMEM((tokens, D), BF16), pltpu.VMEM((QKV, tokens), BF16), pltpu.SemaphoreType.DMA((10,)),
            ],
        ),
        out_shape=[shaped(tokens, QKV), shaped(4, 2, 2, QKV, B)],
        compiler_params=params("arbitrary"),
        cost_estimate=cost(2 * tokens * QKV * D, 9),
        name="qkv_back",
    )(place, *x_pieces, grad_query, own, later, cosine, sine, scale)


def attention_term_kernel(*refs):
    token_refs, left_ref = refs[1:6], refs[6]
    term_ref, rows, sems = refs[-3:]
    copies = put_tokens(token_refs, rows, sems, 0)
    for copy in copies:
        copy.start()
    left = left_ref[...]
    if left.shape[0] == 2 * HALF:
        left = left.T
    for copy in copies:
        copy.wait()
    put_term(left, rows, term_ref)


def attention_terms(place, pieces, left, name):
    whole = lambda *shape: pl.BlockSpec(shape, lambda i, p: (0,) * len(shape))
    rows = min(left.shape)
    return pl.pallas_call(
        attention_term_kernel,
        grid_spec=pltpu.PrefetchScalarGridSpec(
            num_scalar_prefetch=1,
            grid=(1,),
            in_specs=[ANYWHERE] * 5 + [whole(*left.shape)],
            out_specs=whole(4, 2, 2, rows, B),
            scratch_shapes=[pltpu.VMEM((2 * HALF, D), BF16), pltpu.SemaphoreType.DMA((10,))],
        ),
        out_shape=shaped(4, 2, 2, rows, B),
        compiler_params=params("arbitrary"),
        cost_estimate=cost(2 * 2 * HALF * rows * D, 7),
        name=name,
    )(place, *pieces, left)


def token_places(at, y, core):
    step = 1 - 2 * core
    block = jnp.where(
        at < B, y, jnp.where(at < 2 * B, y + 4 - step, jnp.where(at < 3 * B, y + 4 + step, y + 2))
    )
    row = at % B
    row = jnp.where(at < 3 * B, row, (row + core * (B // 2)) % B)
    return (block % 4) * B + row


def set_bias(place_ref, bias_ref):
    zlo, y, core = place_ref[0], place_ref[1], place_ref[2]
    key_at = token_places(lax.broadcasted_iota(jnp.int32, (HALF, 1), 0), y, core)
    query_at = token_places(lax.broadcasted_iota(jnp.int32, (1, HALF), 1), y, core)
    bias_ref[:HALF, :] = jnp.broadcast_to(jnp.where(zlo == 1, 0.0, -1e30), (HALF, HALF))
    bias_ref[HALF:, :] = jnp.where(key_at <= query_at, 0.0, -1e30)


def attention_kernel(place_ref, *refs):
    w_refs, query_ref, kv_ref, mixed_ref, log_ref = refs[:5], *refs[5:9]
    parts, w_out, bias_ref, weight, sems = refs[9:14], *refs[14:]
    columns = put_columns(place_ref, w_refs, weight, sems, 0)
    back = pltpu.make_async_copy(weight, w_out, sems.at[16])

    @pl.when(pl.program_id(0) == 0)
    def _():
        for copy in columns:
            copy.start()
        set_bias(place_ref, bias_ref)
        for copy in columns:
            copy.wait()
        back.start()

    key, value = kv_ref[0, :, :HD], kv_ref[0, :, HD:]
    for head in range(HEADS):
        scores = times_transposed(key, query_ref[0, head]) + bias_ref[...]
        top = jnp.max(scores, axis=0, keepdims=True)
        weights = jnp.exp(scores - top)
        total = jnp.sum(weights, axis=0, keepdims=True)
        low = (weights * (1.0 / total)).astype(BF16)
        mixed_ref[0, :, head * HD : (head + 1) * HD] = outer_sum(value, low).T.astype(BF16)
        log_ref[0, head] = top + jnp.log(total)
    put_rows(matmul(mixed_ref[0], weight[...]).astype(BF16), parts)

    @pl.when(pl.program_id(0) == 1)
    def _():
        back.wait()


def attention_back_kernel(place_ref, *refs):
    grad_refs, query_ref, kv_ref, log_ref, weight_ref = refs[:5], *refs[5:9]
    grad_query_ref, earlier_ref, own_ref, bias_ref, rows, sems = refs[9:]
    step = pl.program_id(0)
    copies = put_tokens(grad_refs, rows, sems, 0)

    @pl.when(step == 0)
    def _():
        for copy in copies:
            copy.start()
        set_bias(place_ref, bias_ref)
        for copy in copies:
            copy.wait()

    hidden = rows[pl.ds(pl.multiple_of(step * HALF, HALF), HALF), :]
    grads = times_transposed(hidden, weight_ref[...]).astype(BF16)
    key, value = kv_ref[0, :, :HD], kv_ref[0, :, HD:]
    grad_key = jnp.zeros((2 * HALF, HD), F32)
    grad_value = jnp.zeros((2 * HALF, HD), F32)
    for head in range(HEADS):
        lanes = slice(head * HD, (head + 1) * HD)
        query, grad = query_ref[0, head], grads[:, lanes]
        weights = jnp.exp(times_transposed(key, query) + bias_ref[...] - log_ref[0, head])
        grad_weights = times_transposed(value, grad)
        delta = jnp.sum(weights * grad_weights, axis=0, keepdims=True)
        grad_scores = (weights * (grad_weights - delta)).astype(BF16)
        grad_query_ref[0, :, lanes] = outer_sum(key, grad_scores).T * HD ** (-0.5)
        grad_key += matmul(grad_scores, query)
        grad_value += matmul(weights.astype(BF16), grad)
    total = jnp.concatenate([grad_key, grad_value], axis=1)
    earlier_ref[0] = total[:HALF].astype(BF16)
    own_ref[0] = total[HALF:]


def sequence_block(*tail):
    return pl.BlockSpec((1,) + tail, lambda s, place: (s,) + (0,) * len(tail))


def attention_call(kernel, in_specs, out_specs, out_shape, scratch, flops, name):
    return pl.pallas_call(
        kernel,
        grid_spec=pltpu.PrefetchScalarGridSpec(
            num_scalar_prefetch=1,
            grid=(2,),
            in_specs=in_specs,
            out_specs=out_specs,
            scratch_shapes=[pltpu.VMEM((2 * HALF, HALF), F32)] + scratch,
        ),
        out_shape=out_shape,
        compiler_params=params("arbitrary"),
        cost_estimate=cost(flops * 8 * 2 * HALF * HALF * HD * 2, 8),
        name=name,
    )


def attention(place, w_pieces, query, kv):
    return attention_call(
        attention_kernel,
        [ANYWHERE] * 5 + [sequence_block(HEADS, HALF, HD), sequence_block(2 * HALF, 2 * HD)],
        [sequence_block(HALF, HEADS * HD), sequence_block(HEADS, 1, HALF)]
        + part_specs(1)
        + [ANYWHERE],
        [shaped(2, HALF, HEADS * HD), shaped(2, HEADS, 1, HALF, kind=F32)] + PART_SHAPES + [shaped(HEADS * HD, D)],
        [pltpu.VMEM((HEADS * HD, D), BF16), pltpu.SemaphoreType.DMA((17,))],
        3,
        "attention",
    )(place, *w_pieces, query, kv)


def attention_back(place, grad_pieces, query, kv, log_total, weight):
    return attention_call(
        attention_back_kernel,
        [ANYWHERE] * 5
        + [
            sequence_block(HEADS, HALF, HD), sequence_block(2 * HALF, 2 * HD),
            sequence_block(HEADS, 1, HALF), pl.BlockSpec((HEADS * HD, D), lambda s, place: (0, 0)),
        ],
        [sequence_block(HALF, HEADS * HD), sequence_block(HALF, 2 * HD), sequence_block(HALF, 2 * HD)],
        [
            shaped(2, HALF, HEADS * HD, kind=F32),
            shaped(2, HALF, 2 * HD),
            shaped(2, HALF, 2 * HD, kind=F32),
        ],
        [pltpu.VMEM((2 * HALF, D), BF16), pltpu.SemaphoreType.DMA((10,))],
        6,
        "attention_back",
    )(place, *grad_pieces, query, kv, log_total, weight)


def finish_attention_kernel(place, *refs):
    piece_refs, w_query, w_key, w_value, gain_ref = refs[:4], *refs[4:8]
    query_out, key_out, value_out, gain_out, rows = refs[8:]
    for ref, by in zip(piece_refs, range(4)):
        at_y = (place[1] + by) % 4
        for c in range(2):
            piece = ref[c].astype(F32)
            rows[pl.ds(pl.multiple_of((2 * at_y + c) * HEADS * HD, HEADS * HD), HEADS * HD)] = piece[: HEADS * HD]
        both = ref[0].astype(F32) + ref[1].astype(F32)
        at = pl.multiple_of(H * HD + at_y * HD, HD)
        rows[pl.ds(at, HD)] = both[HEADS * HD : (HEADS + 1) * HD]
        rows[pl.ds(at + KV * HD, HD)] = both[(HEADS + 1) * HD :]
    gain = gain_ref[...]
    total = jnp.zeros((B, 1), F32)
    row = 0
    for weight, out in ((w_query, query_out), (w_key, key_out), (w_value, value_out)):
        for i in range(out.shape[1] // B):
            lanes = slice(i * B, (i + 1) * B)
            block = rows[row : row + B].T
            total = total + jnp.sum(block * weight[:, lanes].astype(F32), axis=1, keepdims=True)
            out[:, lanes] = block * gain
            row += B
    gain_out[...] = total


def finish_attention(place, pieces, w_query, w_key, w_value, gain):
    whole = lambda *shape: pl.BlockSpec(shape, lambda i, p: (0,) * len(shape))
    kv = KV * HD
    return pl.pallas_call(
        finish_attention_kernel,
        grid_spec=pltpu.PrefetchScalarGridSpec(
            num_scalar_prefetch=1,
            grid=(1,),
            in_specs=[whole(2, QKV, B)] * 4 + [whole(B, D), whole(B, kv), whole(B, kv), whole(B, 1)],
            out_specs=[whole(B, D), whole(B, kv), whole(B, kv), whole(B, 1)],
            scratch_shapes=[pltpu.VMEM((D + 2 * kv, B), F32)],
        ),
        out_shape=[
            shaped(B, D, kind=F32), shaped(B, kv, kind=F32), shaped(B, kv, kind=F32), shaped(B, 1, kind=F32),
        ],
        compiler_params=params("arbitrary"),
        cost_estimate=cost(0, 4),
        name="finish_attention",
    )(place, *pieces, w_query, w_key, w_value, gain)


def finish_output_kernel(blocks, out):
    for i in range(16):
        out[:, i * B : (i + 1) * B] = blocks[i].astype(F32)


def finish_output(blocks):
    return pl.pallas_call(
        finish_output_kernel,
        out_shape=shaped(B, D, kind=F32),
        compiler_params=params(),
        cost_estimate=cost(0, 2),
        name="finish_output",
    )(blocks)


def feed_forward_kernel(*refs):
    place, token_refs, grad_refs, ff_ref = refs[0], refs[1:6], refs[6:11], refs[11]
    act_ref, act_t, gate_t, up_t = refs[12:16]
    parts, down_out = refs[16:21], refs[21]
    rows_h, rows_g, gate_up, down, slabs, sems = refs[22:]
    step = pl.program_id(0)
    tokens = put_tokens(token_refs, rows_h, sems, 0)
    grads = put_tokens(grad_refs, rows_g, sems, 10)
    weights, loads = [], []
    for x in range(4):
        for by in range(4):
            z = (2 * place[4] + place[0] + by) % 4
            zhi, zlo = z // 2, z % 2
            for core in range(2):
                weights.append(
                    pltpu.make_async_copy(
                        ff_ref.at[x, by, pl.ds(core * FFL, FFL)],
                        gate_up.at[zlo, :, lane_block(zhi, x, core)],
                        sems.at[20 + len(weights)],
                    )
                )
            loads.append(
                pltpu.make_async_copy(
                    ff_ref.at[x, by, pl.ds(2 * FFL, FFL)], slabs.at[zlo, zhi * 4 + x], sems.at[52 + len(loads)]
                )
            )
    back = pltpu.make_async_copy(down, down_out, sems.at[68])

    @pl.when(step == 0)
    def _():
        for copy in tokens + weights + loads + grads:
            copy.start()
        for copy in tokens + weights:
            copy.wait()

    rows = pl.ds(pl.multiple_of(step * HALF, HALF), HALF)
    normed = rows_h[rows, :]
    gate_pre = times_transposed(normed, gate_up[0])
    upward = times_transposed(normed, gate_up[1])

    @pl.when(step == 0)
    def _():
        for copy in loads:
            copy.wait()

        def put(q, carry):
            for half in range(2):
                for p in range(4):
                    one = slabs[half, 2 * q, 2 * p * PIECE : 2 * (p + 1) * PIECE, :].astype(F32)
                    two = slabs[half, 2 * q + 1, 2 * p * PIECE : 2 * (p + 1) * PIECE, :].astype(F32)
                    lane = (half * 8 + 2 * p) * B
                    rows = pl.ds(pl.multiple_of(q * 2 * PIECE, 16), 2 * PIECE)
                    down[rows, lane : lane + B] = jnp.concatenate([one[:PIECE], two[:PIECE]], axis=0).astype(BF16)
                    down[rows, lane + B : lane + 2 * B] = jnp.concatenate(
                        [one[PIECE:], two[PIECE:]], axis=0
                    ).astype(BF16)
            return carry

        lax.fori_loop(0, 4, put, 0)
        back.start()
        for copy in grads:
            copy.wait()

    grad_act = times_transposed(rows_g[rows, :], down[...])
    sigmoid = 1.0 / (1.0 + jnp.exp(-gate_pre))
    silu = gate_pre * sigmoid
    activation = silu * upward
    grad_up = grad_act * silu
    grad_gate = grad_act * upward * (sigmoid * (1.0 + gate_pre * (1.0 - sigmoid)))
    part = matmul(grad_gate.astype(BF16), gate_up[0]) + matmul(grad_up.astype(BF16), gate_up[1])
    put_rows(part.astype(BF16), parts)
    act_ref[...] = activation.astype(BF16)
    act_t[...] = activation.T.astype(BF16)
    gate_t[...] = grad_gate.T.astype(BF16)
    up_t[...] = grad_up.T.astype(BF16)

    @pl.when(step == 1)
    def _():
        back.wait()


def feed_forward(place, tokens, grads, ff_all):
    turned_spec = pl.BlockSpec((FFL, HALF), lambda i, p: (0, i))
    turned_shape = shaped(FFL, 2 * HALF)
    return pl.pallas_call(
        feed_forward_kernel,
        grid_spec=pltpu.PrefetchScalarGridSpec(
            num_scalar_prefetch=1,
            grid=(2,),
            in_specs=[ANYWHERE] * 11,
            out_specs=[pl.BlockSpec((HALF, FFL), lambda i, p: (i, 0))]
            + [turned_spec] * 3
            + part_specs(1)
            + [ANYWHERE],
            scratch_shapes=[
                pltpu.VMEM((2 * HALF, D), BF16),
                pltpu.VMEM((2 * HALF, D), BF16),
                pltpu.VMEM((2, FFL, D), BF16),
                pltpu.VMEM((FFL, D), BF16),
                pltpu.VMEM((2, 8, FFL, B), BF16),
                pltpu.SemaphoreType.DMA((69,)),
            ],
        ),
        out_shape=[shaped(2 * HALF, FFL)] + [turned_shape] * 3 + PART_SHAPES + [shaped(FFL, D)],
        compiler_params=params("arbitrary"),
        cost_estimate=cost(2 * 5 * 2 * HALF * FFL * D, 32),
        name="feed_forward",
    )(place, *tokens, *grads, ff_all)


def along_z(place, zhi, zlo):
    return (2 * zhi + zlo + 4 - 2 * place[4] - place[0]) % 4


def load_tokens(step, refs, rows, sems):
    copies = put_tokens(refs, rows, sems, 0)

    @pl.when(step == 0)
    def _():
        for copy in copies:
            copy.start()
        for copy in copies:
            copy.wait()


def gate_up_kernel(*refs):
    place, token_refs, gate_t, up_t, out_ref, rows, terms, sems = refs[0], refs[1:6], *refs[6:]
    step = pl.program_id(0)
    load_tokens(step, token_refs, rows, sems)
    normed = rows[:, pl.ds(pl.multiple_of(step * 4 * B, 4 * B), 4 * B)]

    def out(i, matrix):
        xs, by = pl.ds(i % 2 * 2, 2), along_z(place, i // 2, matrix)
        return pltpu.make_async_copy(terms.at[xs, by], out_ref.at[xs, by], sems.at[10 + 2 * i + matrix])

    for matrix, left in ((0, gate_t), (1, up_t)):
        term = matmul(left[...], normed).astype(BF16)
        by = along_z(place, step // 2, matrix)
        for j in range(2):
            terms[step % 2 * 2 + j, by, 0:FFL, :] = term[:, 2 * j * B : (2 * j + 1) * B]
            terms[step % 2 * 2 + j, by, FFL:, :] = term[:, (2 * j + 1) * B : (2 * j + 2) * B]
        out(step, matrix).start()

    @pl.when(step == 3)
    def _():
        for i in range(4):
            for matrix in range(2):
                out(i, matrix).wait()


def down_kernel(*refs):
    place, grad_refs, act_t, out_ref, rows, terms, sems = refs[0], refs[1:6], *refs[6:]
    step = pl.program_id(0)
    load_tokens(step, grad_refs, rows, sems)
    term = matmul(act_t[...], rows[:, pl.ds(pl.multiple_of(step * 4 * B, 4 * B), 4 * B)])
    for j in range(2):
        p = (2 * step + j) % 4
        at = pl.ds(pl.multiple_of(p * 2 * PIECE, 16), 2 * PIECE)
        for zx in range(8):
            slab = term[zx * PIECE : (zx + 1) * PIECE]
            low, high = slab[:, 2 * j * B : (2 * j + 1) * B], slab[:, (2 * j + 1) * B : (2 * j + 2) * B]
            by = along_z(place, zx // 4, step // 2)
            terms[zx % 4, by, at, :] = jnp.concatenate([low, high], axis=0).astype(BF16)

    def out(half, zhi):
        by = along_z(place, zhi, half)
        return pltpu.make_async_copy(terms.at[:, by], out_ref.at[:, by], sems.at[10 + 2 * half + zhi])

    @pl.when(step % 2 == 1)
    def _():
        for zhi in range(2):
            out(step // 2, zhi).start()

    @pl.when(step == 3)
    def _():
        for half in range(2):
            for zhi in range(2):
                out(half, zhi).wait()


def ff_terms(kernel, place, pieces, lefts, rows, name):
    whole = pl.BlockSpec((FFL, 2 * HALF), lambda i, p: (0, 0))
    return pl.pallas_call(
        kernel,
        grid_spec=pltpu.PrefetchScalarGridSpec(
            num_scalar_prefetch=1,
            grid=(4,),
            in_specs=[ANYWHERE] * 5 + [whole] * len(lefts),
            out_specs=ANYWHERE,
            scratch_shapes=[
                pltpu.VMEM((2 * HALF, D), BF16),
                pltpu.VMEM((4, 4, rows, B), BF16),
                pltpu.SemaphoreType.DMA((18,)),
            ],
        ),
        out_shape=shaped(4, 4, rows, B),
        compiler_params=params("arbitrary"),
        cost_estimate=cost(2 * len(lefts) * 2 * HALF * FFL * D, 8 + 4 * len(lefts)),
        name=name,
    )(place, *pieces, *lefts)


def finish_hidden_kernel(*refs):
    place, piece_refs, weight_ref, gain_ref, out_ref, gain_out, rows = refs[0], refs[1:5], *refs[5:]
    for ref, by in zip(piece_refs, range(4)):
        at_y = (place[1] + by) % 4
        for core in range(2):
            slab = ref[0, core].astype(F32)
            for zx in range(8):
                at = pl.multiple_of((2 * zx + core) * 4 * PIECE + at_y * PIECE, 8)
                rows[pl.ds(at, PIECE)] = slab[zx * PIECE : (zx + 1) * PIECE]
    gain = gain_ref[...]
    total = jnp.zeros((B, 1), F32)
    for i in range(FF // B):
        lanes = slice(i * B, (i + 1) * B)
        block = rows[lanes].T
        total = total + jnp.sum(block * weight_ref[:, lanes].astype(F32), axis=1, keepdims=True)
        out_ref[:, lanes] = block * gain
    gain_out[...] = total


def finish_hidden(place, pieces, matrix, weight, gain):
    own, after, low, high, before = pieces
    at = lambda m: pl.BlockSpec((1, 2, FFL, B), lambda i, p: (m, 0, 0, 0))
    whole = lambda *shape: pl.BlockSpec(shape, lambda i, p: (0,) * len(shape))
    return pl.pallas_call(
        finish_hidden_kernel,
        grid_spec=pltpu.PrefetchScalarGridSpec(
            num_scalar_prefetch=1,
            grid=(1,),
            in_specs=[at(matrix), at(matrix), at(0), at(matrix), whole(B, FF), whole(B, 1)],
            out_specs=[whole(B, FF), whole(B, 1)],
            scratch_shapes=[pltpu.VMEM((FF, B), F32)],
        ),
        out_shape=[shaped(B, FF, kind=F32), shaped(B, 1, kind=F32)],
        compiler_params=params("arbitrary"),
        cost_estimate=cost(0, 6),
        name="finish_hidden",
    )(place, own, after, (low, high)[matrix], before, weight, gain)


def finish_down_kernel(place, own, after, low, high, before, out_ref):
    for refs, by in (((own, own), 0), ((after, after), 1), ((low, high), 2), ((before, before), 3)):
        rows = pl.ds(pl.multiple_of((place[1] + by) % 4 * PIECE, 8), PIECE)
        for half in range(2):
            slab = refs[half][half if by != 2 else 0].astype(F32)
            for t in range(8):
                lane = (half * 8 + t) * B
                out_ref[rows, lane : lane + B] = slab[t * PIECE : (t + 1) * PIECE]


def finish_down(place, pieces):
    halves = lambda n: pl.BlockSpec((n, FFL, B), lambda i, p: (0, 0, 0))
    return pl.pallas_call(
        finish_down_kernel,
        grid_spec=pltpu.PrefetchScalarGridSpec(
            num_scalar_prefetch=1,
            grid=(1,),
            in_specs=[halves(2), halves(2), halves(1), halves(1), halves(2)],
            out_specs=pl.BlockSpec((4 * PIECE, D), lambda i, p: (0, 0)),
        ),
        out_shape=shaped(4 * PIECE, D, kind=F32),
        compiler_params=params("arbitrary"),
        cost_estimate=cost(0, 5),
        name="finish_down",
    )(place, *pieces)


def own_rows(rows_all, y, core, per):
    return lax.dynamic_slice_in_dim(rows_all, (2 * y + core) * per, per, 0)


class Flow:
    def __init__(self, steps):
        self.steps, self.result, self.sent = steps, None, None
        self.move(None)

    def move(self, arrived):
        try:
            self.sent = self.steps.send(arrived)
        except StopIteration as end:
            self.sent, self.result = (), end.value


def stage(flows, *values):
    flows = [flow for flow in flows if flow.result is None]
    sizes = [len(flow.sent) for flow in flows]
    leaves, tree = jax.tree.flatten(values)
    tied = tie(*[v for flow in flows for v in flow.sent], *leaves)
    for flow, size in zip(flows, sizes):
        flow.move(tied[:size])
        tied = tied[size:]
    return jax.tree.unflatten(tree, tied)


def gather_steps(block):
    (other,) = yield (swap_core(block),)
    pair = jnp.stack([block, other])
    (got,) = yield (along_y(pair),)
    far, swapped = yield (along_y(send_half(got)), swap_core(got))
    (far_swapped,) = yield (swap_core(far),)
    return pair, got, swapped, far, far_swapped


def scatter_steps(parts):
    core = lax.axis_index("core")
    first, behind, ahead, far, far_other = parts
    (far_got,) = yield (swap_core(far_other),)
    far = add(far, far_got).astype(BF16)
    low, behind_got, first_got = yield (along_y(far), swap_core(behind), swap_core(first[1]))
    ahead = add(ahead, behind_got).astype(BF16)
    mine = add(lax.dynamic_slice_in_dim(ahead, core * (B // 2), B // 2, 1), low).astype(BF16)
    ahead = lax.dynamic_update_slice_in_dim(ahead, mine, core * (B // 2), 1)
    (got,) = yield (along_y(ahead),)
    (last,) = yield (swap_core(got[1]),)
    return add(first[0], first_got) + got[0].astype(F32) + last.astype(F32)


def ring_gather_steps(block, axis):
    half = block.shape[0] // 2
    before, after = yield (shift(block, axis, 1), shift(block, axis, -1))
    low, high = yield (shift(before[:half], axis, 1), shift(after[half:], axis, -1))
    return block, after, low, high, before


def ring_scatter_steps(parts, axis):
    half = parts[2].shape[0] // 2
    low, high = yield (shift(parts[2][:half], axis, 1), shift(parts[2][half:], axis, -1))
    after = jnp.concatenate([add(parts[1][:half], low).astype(BF16), parts[1][half:]], axis=0)
    before = jnp.concatenate([parts[3][:half], add(parts[3][half:], high).astype(BF16)], axis=0)
    from_before, from_after = yield (shift(after, axis, 1), shift(before, axis, -1))
    return add(parts[0], from_before) + from_after.astype(F32)


def on_device(
    layer_input,
    positions,
    attn_gain,
    w_query,
    w_key,
    w_value,
    w_output,
    mlp_gain,
    w_gate,
    w_up,
    w_down,
    out_grad,
):
    zlo, y, zhi, x, core = (lax.axis_index(axis) for axis in AXES)
    place = jnp.stack([zlo, y, core, x, zhi]).astype(jnp.int32)

    def by_core(mine, got):
        return jnp.where(core == 0, jnp.stack([mine, got]), jnp.stack([got, mine]))

    def by_zlo(mine, got):
        return jnp.where(zlo == 0, jnp.stack([mine, got]), jnp.stack([got, mine]))

    def by_zhi(mine, got):
        return jnp.where(zhi == 0, jnp.stack([mine, got]), jnp.stack([got, mine]))

    def trio(mine, other, axis):
        across = lax.ppermute(other, (axis, "core"), [(i, 3 - i) for i in range(4)])
        return shift(mine, axis, 1), swap_core(other), across

    def column_steps(mine, got):
        pair = by_core(mine, got)
        (got,) = yield (shift(pair, "zhi", 1),)
        return (yield from ring_gather_steps(by_zhi(pair, got), "x"))

    def output_steps(mine, other):
        there, here, across = yield trio(mine, other, "zhi")
        column = by_zhi(by_core(mine, here), by_core(there, across))
        return (yield from ring_gather_steps(column, "x"))

    def hidden_steps(mine, got, down):
        piece = jnp.concatenate([by_core(mine, got).reshape(2 * FFL, B), down], axis=0)
        pieces = yield from ring_gather_steps(piece, "z")
        return jnp.concatenate(pieces, axis=0).reshape(4, 3 * FFL, B)

    def of_core(pair, other=False):
        return lax.dynamic_index_in_dim(pair, 1 - core if other else core, 0, keepdims=False)

    def whole_ring(pieces):
        own, after, low, high, before = pieces
        return own, after, jnp.concatenate([low, high], axis=0), before

    def attention_steps(column):
        keep = lax.dynamic_index_in_dim(column, zhi, 0, keepdims=False)
        send = lax.dynamic_index_in_dim(column, 1 - zhi, 0, keepdims=False)
        (got,) = yield (shift(send, "zhi", 1),)
        pair = add(keep, got).astype(BF16)
        mine, other = of_core(pair), of_core(pair, True)
        there, here, across = yield trio(mine, other, "zlo")
        own = by_core(add(mine, there), add(here, across)).astype(BF16)
        return (yield from ring_gather_steps(own, "y"))

    def gate_up_steps(sums):
        own = yield from ring_scatter_steps([sums[i] for i in range(4)], "z")
        pair = own.astype(BF16).reshape(2, FFL, B)
        mine, other = of_core(pair), of_core(pair, True)
        there, here, across = yield trio(mine, other, "zlo")
        block = by_zlo(by_core(mine, here), by_core(there, across))
        before, after = yield (shift(block, "y", 1), shift(block, "y", -1))
        yield ()
        low, high = yield (shift(before[:1], "y", 1), shift(after[1:], "y", -1))
        return block, after, low, high, before

    def down_steps(sums):
        own = yield from ring_scatter_steps([sums[i] for i in range(4)], "z")
        own = own.astype(BF16)
        (got,) = yield (shift(own, "zlo", 1),)
        return (yield from ring_gather_steps(by_zlo(own, got), "y"))

    x_low = layer_input[0]
    frequency = theta ** (-jnp.arange(0, HD, 2).astype(F32) / HD)
    angles = positions[0].astype(F32)[:, None] * frequency
    tables = []
    for table in (jnp.cos(angles), jnp.sin(angles)):
        high = lax.reduce_precision(table, 8, 7)
        tables += [high.astype(BF16), (table - high).astype(BF16)]
    tokens = Flow(gather_steps(jnp.concatenate([x_low, *tables], axis=1)))
    grads = Flow(gather_steps(out_grad[0]))
    qkv_mine, qkv_other = prepare_qkv(place, w_query, w_key, w_value, attn_gain[:, None])
    qkv_mine, qkv_got, gain_two, w_out = stage([tokens], qkv_mine, swap_core(qkv_other), mlp_gain[:, None], w_output)

    columns = Flow(column_steps(qkv_mine, qkv_got))
    o_rows = lax.all_to_all(w_out.reshape(B, 16, B).transpose(1, 0, 2), FSDP, 0, 0, tiled=True)
    ff_mine, ff_other, ff_down = prepare_ff(place, w_gate, w_up, w_down, gain_two)
    ff_mine, ff_got, ff_down, x_low, o_rows = stage(
        [tokens, columns], ff_mine, swap_core(ff_other), ff_down, x_low, o_rows
    )

    inputs = x_low.astype(F32)
    scale_one = lax.rsqrt(jnp.mean(inputs * inputs, axis=-1, keepdims=True) + eps)
    o_rows = o_rows.reshape(D, B)
    mine, other = own_rows(o_rows, y, core, HEADS * HD), own_rows(o_rows, y, 1 - core, HEADS * HD)
    scale_one, mine, other, ff_mine, ff_got, ff_down = stage(
        [tokens, columns, grads], scale_one, mine, other, ff_mine, ff_got, ff_down
    )

    outputs = Flow(output_steps(mine, other))
    ff_mine, ff_got, ff_down = stage([tokens, columns, outputs], ff_mine, ff_got, ff_down)

    hidden_rows = Flow(hidden_steps(ff_mine, ff_got, ff_down))
    x_pieces = tokens.result
    query, key_value, scale_all, cosine, sine, qkv_full = project_qkv(place, x_pieces, columns.result)
    query, key_value = stage([hidden_rows, outputs, grads], query, key_value)

    earlier = lax.ppermute(key_value, "zlo", [(0, 1)])
    query, key_value, earlier = stage([outputs, hidden_rows], query, key_value, earlier)
    ff_all = lax.all_gather(hidden_rows.result, "x", axis=0, tiled=False)

    key_value = jnp.concatenate([earlier, key_value], axis=1)
    mixed, log_total, *parts, o_full = attention(place, outputs.result, query, key_value)
    parts = stage([grads], *parts)
    sums = Flow(scatter_steps(parts))
    stage([sums, grads])
    grad_pieces = grads.result
    for _ in range(3):
        stage([sums])
    hidden = inputs + sums.result
    scale_two = lax.rsqrt(jnp.mean(hidden * hidden, axis=-1, keepdims=True) + eps)
    normed = Flow(gather_steps((hidden * scale_two).astype(BF16)))
    for _ in range(4):
        stage([normed])
    normed_pieces = normed.result

    activation, act_t, gate_t, up_t, *parts, down_full = feed_forward(place, normed_pieces, grad_pieces, ff_all)
    sums = Flow(scatter_steps(parts))
    (act_t,) = stage([sums], act_t)
    down_terms = ff_terms(down_kernel, place, grad_pieces, (act_t,), FFL, "down_terms")
    down_terms, gate_t = stage([sums], down_terms, gate_t)
    down_sum = lax.psum_scatter(down_terms, "x", scatter_dimension=0, tiled=True)[0]
    gate_up_terms = ff_terms(gate_up_kernel, place, normed_pieces, (gate_t, up_t), 2 * FFL, "gate_up_terms")
    (gate_up_terms,) = stage([sums], gate_up_terms)
    gate_up_sum = lax.psum_scatter(gate_up_terms, "x", scatter_dimension=0, tiled=True)[0]
    stage([sums])

    grad_normed_two = sums.result
    mean_two = jnp.mean(grad_normed_two * hidden, axis=-1, keepdims=True)
    grad_hidden = (
        out_grad[0].astype(F32)
        + scale_two * grad_normed_two
        - hidden * (scale_two * scale_two * scale_two) * mean_two
    )
    hidden_grads = Flow(gather_steps(grad_hidden.astype(BF16)))
    (activation,) = stage([hidden_grads], activation)
    down_parts = project(activation, down_full)
    down_parts = stage([hidden_grads], *down_parts)
    result = Flow(scatter_steps(down_parts))
    stage([hidden_grads])
    (down_sum,) = stage([hidden_grads, result], down_sum)

    down = Flow(down_steps(down_sum))
    hidden_grad_pieces = hidden_grads.result
    grad_query, grad_earlier, grad_own = attention_back(
        place, hidden_grad_pieces, query, key_value, log_total, o_full
    )
    grad_query, grad_earlier, grad_own, mixed = stage([result, down], grad_query, grad_earlier, grad_own, mixed)

    later = lax.ppermute(grad_earlier, "zlo", [(1, 0)])
    output_terms = attention_terms(
        place, hidden_grad_pieces, mixed.reshape(2 * HALF, HEADS * HD), "output_terms"
    )
    later, grad_query, output_terms, gate_up_sum = stage(
        [result, down], later, grad_query, output_terms, gate_up_sum
    )

    output_sum = lax.psum_scatter(output_terms, "x", scatter_dimension=0, tiled=True)[0]
    gate_up = Flow(gate_up_steps(gate_up_sum))
    grad_pre, terms = qkv_back(place, x_pieces, grad_query, grad_own, later, cosine, sine, scale_all)
    grad_pre, terms = stage([gate_up, down, result], grad_pre, terms)

    attention_sum = lax.psum_scatter(terms, "x", scatter_dimension=0, tiled=True)[0]
    parts = project(grad_pre, qkv_full)
    *parts, output_sum = stage([gate_up, down], *parts, output_sum)

    sums = Flow(scatter_steps(parts))
    output_sums = Flow(attention_steps(output_sum))
    (attention_sum,) = stage([sums, gate_up, output_sums, down], attention_sum)
    attention_sums = Flow(attention_steps(attention_sum))
    stage([sums, output_sums, attention_sums])
    down_grad = finish_down(place, down.result)
    (down_grad,) = stage([output_sums, attention_sums, gate_up], down_grad)
    stage([sums, output_sums, attention_sums, gate_up])

    ring = jnp.roll(jnp.stack(whole_ring(output_sums.result)), y, axis=0).reshape(16, B, B)
    output_grad = lax.all_to_all(ring, FSDP, 0, 0, tiled=True)
    stage([sums, attention_sums, gate_up])
    grad_normed = sums.result
    mean_one = jnp.mean(grad_normed * inputs, axis=-1, keepdims=True)
    input_grad = (
        grad_hidden
        + scale_one * grad_normed
        - inputs * (scale_one * scale_one * scale_one) * mean_one
    )
    input_grad = input_grad.astype(BF16)
    gain_two = mlp_gain[:, None]
    gate_grad, gate_gain = finish_hidden(place, gate_up.result, 0, w_gate, gain_two)
    up_grad, up_gain = finish_hidden(place, gate_up.result, 1, w_up, gain_two)
    query_grad, key_grad, value_grad, attn_gain_grad = finish_attention(
        place, whole_ring(attention_sums.result), w_query, w_key, w_value, attn_gain[:, None]
    )
    output_grad, gate_grad, up_grad, query_grad = tie(output_grad, gate_grad, up_grad, query_grad)
    output_grad = finish_output(output_grad)
    return (
        (hidden + result.result).astype(BF16)[None],
        input_grad[None],
        attn_gain_grad[:, 0],
        query_grad,
        key_grad,
        value_grad,
        output_grad,
        (gate_gain + up_gain)[:, 0],
        gate_grad,
        up_grad,
        down_grad,
    )


def solution(mesh):
    split = Mesh(mesh.devices.reshape(2, 4, 2, 4, 2), AXES)
    tokens = P(FSDP, SEQ, None)
    rows = P(FSDP, None)
    gain = P(FSDP)
    in_specs = (
        tokens, P(FSDP, SEQ), gain, rows, rows, rows, rows, gain, rows, rows, rows, tokens,
    )
    out_specs = (tokens, tokens, gain, rows, rows, rows, rows, gain, rows, rows, rows)
    return jax.shard_map(
        on_device, mesh=split, in_specs=in_specs, out_specs=out_specs, check_vma=False
    )
```

```python
import jax
import jax.numpy as jnp
from jax import lax
from jax.experimental import pallas as pl
from jax.experimental.pallas import tpu as pltpu
from jax.sharding import Mesh
from jax.sharding import PartitionSpec as P

H = 32
KV = 4
HD = 64
D = 2048
FF = 5632
B = 128
HALF = 512
HEADS = 4
FFL = 704
PIECE = 88

eps = 1e-05
theta = 10000.0
F32 = jnp.float32
BF16 = jnp.bfloat16
AXES = ("zlo", "y", "zhi", "x", "core")
FSDP = ("zhi", "x", "core")
SEQ = ("zlo", "y")


def matmul(left, right):
    return jnp.dot(left, right, preferred_element_type=F32)


def times_transposed(left, right):
    return lax.dot_general(left, right, (((1,), (1,)), ((), ())), preferred_element_type=F32)


def outer_sum(left, right):
    return lax.dot_general(left, right, (((0,), (0,)), ((), ())), preferred_element_type=F32)


def shift(value, axis, by):
    if axis == "z":
        at = [2 * (z % 2) + z // 2 for z in range(4)]
        return lax.ppermute(value, ("zlo", "zhi"), [(at[z], at[(z + by) % 4]) for z in range(4)])
    size = lax.axis_size(axis)
    return lax.ppermute(value, axis, [(i, (i + by) % size) for i in range(size)])


def swap_core(value):
    return shift(value, "core", 1)


def small_gather(block, axis):
    return shift(block, axis, -1), shift(block, axis, 2), shift(block, axis, 1)


def tie(*values):
    return lax.optimization_barrier(values)


def add(left, right):
    return left.astype(F32) + right.astype(F32)


def along_y(value):
    pairs = []
    for i in range(4):
        pairs.append((2 * i, 2 * ((i + 1) % 4)))
        pairs.append((2 * i + 1, 2 * ((i + 3) % 4) + 1))
    return lax.ppermute(value, ("y", "core"), pairs)


def send_half(got):
    core = lax.axis_index("core")
    return lax.dynamic_slice_in_dim(got, core * (B // 2), B // 2, 1)


FLIPPED = (0, 0, 1, 0, 1)
LENGTHS = (B, B, B, B // 2, B // 2)


def put_tokens(refs, rows_ref, sems, start):
    lanes = pl.ds(0, rows_ref.shape[1])
    copies = []
    row = 0
    for s in range(2):
        for ref, flip, length in zip(refs, FLIPPED, LENGTHS):
            copies.append(
                pltpu.make_async_copy(
                    ref.at[s ^ flip, :, lanes], rows_ref.at[pl.ds(row, length)], sems.at[start + len(copies)]
                )
            )
            row += length
    return copies


TILE = 256
WIDE = D + B
VMEM_LIMIT = 56 * 2**20
ANYWHERE = pl.BlockSpec(memory_space=pl.ANY)


def params(*kinds):
    return pltpu.CompilerParams(dimension_semantics=kinds or None, vmem_limit_bytes=VMEM_LIMIT)


def cost(flops, megabytes):
    return pl.CostEstimate(flops=flops, bytes_accessed=int(megabytes * 2**20), transcendentals=0)


def shaped(*shape, kind=BF16):
    return jax.ShapeDtypeStruct(shape, kind)


PARTS = ((B, False), (B, True), (B, False), (B // 2, False), (B // 2, True))
PART_SHAPES = [jax.ShapeDtypeStruct((2, n, D), BF16) for n, _ in PARTS]


def part_specs(steps):
    def of(turn):
        return lambda i, *_: (1 - i // steps if turn else i // steps, 0, 0)

    return [pl.BlockSpec((1, n, D), of(turn)) for n, turn in PARTS]


def put_parts(step, tile, refs):
    @pl.when(step % 2 == 0)
    def _():
        refs[0][0] = tile[:B]
        refs[1][0] = tile[B:]

    @pl.when(step % 2 == 1)
    def _():
        refs[2][0] = tile[:B]
        refs[3][0] = tile[B : B + B // 2]
        refs[4][0] = tile[B + B // 2 :]


def put_rows(rows, refs):
    row = 0
    for ref, (length, _) in zip(refs, PARTS):
        ref[0] = rows[row : row + length]
        row += length


def turned(values):
    lane = lax.broadcasted_iota(jnp.int32, values.shape, 1) % HD
    return jnp.where(lane < HD // 2, -pltpu.roll(values, 2 * HD - HD // 2, 1), pltpu.roll(values, HD // 2, 1))


def lane_block(zhi, x, core):
    return pl.ds(pl.multiple_of((zhi * 8 + x * 2 + core) * B, B), B)


def put_columns(place, refs, into, sems, start):
    copies = []
    for ref, by, first in zip(refs, (0, 1, 2, 2, 3), (0, 0, 0, 1, 0)):
        for i in range(ref.shape[0]):
            for core in range(2):
                lanes = lane_block(first + i, (place[3] + by) % 4, core)
                copies.append(
                    pltpu.make_async_copy(ref.at[i, core], into.at[:, lanes], sems.at[start + len(copies)])
                )
    return copies


def prepare_qkv_kernel(place, q_mine, q_other, w_key, w_value, gain, mine_ref, other_ref, k_rows, v_rows):
    scale = gain[...]
    k_rows[...] = (w_key[...].astype(F32) * scale).T
    v_rows[...] = (w_value[...].astype(F32) * scale).T
    rows = pl.ds(pl.multiple_of(place[1] * HD, HD), HD)
    for source, out in ((q_mine, mine_ref), (q_other, other_ref)):
        out[: HEADS * HD] = (source[...].astype(F32) * scale).T.astype(BF16)
        out[HEADS * HD : (HEADS + 1) * HD] = k_rows[rows].astype(BF16)
        out[(HEADS + 1) * HD :] = v_rows[rows].astype(BF16)


QKV = (HEADS + 2) * HD


def prepare_qkv(place, w_query, w_key, w_value, gain):
    whole = lambda *shape: pl.BlockSpec(shape, lambda i, p: (0,) * len(shape))
    return pl.pallas_call(
        prepare_qkv_kernel,
        grid_spec=pltpu.PrefetchScalarGridSpec(
            num_scalar_prefetch=1,
            grid=(1,),
            in_specs=[
                pl.BlockSpec((B, HEADS * HD), lambda i, p: (0, 2 * p[1] + p[2])),
                pl.BlockSpec((B, HEADS * HD), lambda i, p: (0, 2 * p[1] + 1 - p[2])),
                whole(B, KV * HD), whole(B, KV * HD), whole(B, 1),
            ],
            out_specs=[whole(QKV, B), whole(QKV, B)],
            scratch_shapes=[pltpu.VMEM((KV * HD, B), F32), pltpu.VMEM((KV * HD, B), F32)],
        ),
        out_shape=[shaped(QKV, B), shaped(QKV, B)],
        compiler_params=params("arbitrary"),
        cost_estimate=cost(0, 1),
        name="prepare_qkv",
    )(place, w_query, w_query, w_key, w_value, gain)


def prepare_ff_kernel(place, w_gate, w_up, w_down, gain, mine_ref, other_ref, down_ref, picked, rows, down_rows, sems):
    zlo, y, core = place[0], place[1], place[2]
    down = pltpu.make_async_copy(
        w_down.at[:, pl.ds(pl.multiple_of(zlo * (D // 2), D // 2), D // 2)], down_rows, sems.at[1]
    )
    down.start()

    @pl.when(zlo == 0)
    def _():
        copy = pltpu.make_async_copy(w_gate, picked, sems.at[0])
        copy.start()
        copy.wait()

    @pl.when(zlo == 1)
    def _():
        copy = pltpu.make_async_copy(w_up, picked, sems.at[0])
        copy.start()
        copy.wait()

    scale = gain[...]
    for i in range(FF // B):
        rows[i * B : (i + 1) * B] = (picked[:, i * B : (i + 1) * B].astype(F32) * scale).T
    for which, out in ((core, mine_ref), (1 - core, other_ref)):
        slabs = []
        for zx in range(8):
            at = pl.multiple_of(zx * 2 * 4 * PIECE + which * 4 * PIECE + y * PIECE, 8)
            slabs.append(rows[pl.ds(at, PIECE)])
        out[...] = jnp.concatenate(slabs, axis=0).astype(BF16)
    down.wait()
    for t in range(8):
        rows[t * 4 * PIECE : (t + 1) * 4 * PIECE] = down_rows[:, t * B : (t + 1) * B].astype(F32)
    slabs = [rows[pl.ds(pl.multiple_of(t * 4 * PIECE + y * PIECE, 8), PIECE)] for t in range(8)]
    down_ref[...] = jnp.concatenate(slabs, axis=0).astype(BF16)


def prepare_ff(place, w_gate, w_up, w_down, gain):
    return pl.pallas_call(
        prepare_ff_kernel,
        grid_spec=pltpu.PrefetchScalarGridSpec(
            num_scalar_prefetch=1,
            grid=(1,),
            in_specs=[ANYWHERE, ANYWHERE, ANYWHERE, pl.BlockSpec((B, 1), lambda i, p: (0, 0))],
            out_specs=[pl.BlockSpec((FFL, B), lambda i, p: (0, 0))] * 3,
            scratch_shapes=[
                pltpu.VMEM((B, FF), BF16),
                pltpu.VMEM((FF, B), F32),
                pltpu.VMEM((4 * PIECE, D // 2), BF16),
                pltpu.SemaphoreType.DMA((2,)),
            ],
        ),
        out_shape=[shaped(FFL, B)] * 3,
        compiler_params=params("arbitrary"),
        cost_estimate=cost(0, 6),
        name="prepare_ff",
    )(place, w_gate, w_up, w_down, gain)


def project_qkv_kernel(*refs):
    place, x_refs, w_refs = refs[0], refs[1:6], refs[6:11]
    query_ref, kv_ref, scale_ref, cosine_ref, sine_ref, w_out, rows, weights, sems = refs[11:]
    step = pl.program_id(0)
    tokens = put_tokens(x_refs, rows, sems, 0)
    columns = put_columns(place, w_refs, weights, sems, 10)
    back = pltpu.make_async_copy(weights, w_out, sems.at[26])

    @pl.when(step == 0)
    def _():
        for copy in columns + tokens:
            copy.start()
        for copy in columns:
            copy.wait()
        back.start()
        for copy in tokens:
            copy.wait()

    at = pl.ds(pl.multiple_of(step * TILE, TILE), TILE)
    tile = rows[at, :D]
    wide = tile.astype(F32)
    scale = lax.rsqrt(jnp.mean(wide * wide, axis=-1, keepdims=True) + eps)
    scale_ref[...] = scale
    pre = times_transposed(tile, weights[...]) * scale
    tables = rows[at, D:].astype(F32)
    tables = tables + pltpu.roll(tables, B - HD // 2, 1)
    cosine = jnp.concatenate([tables[:, : HD // 2]] * 4, axis=1)
    sine = jnp.concatenate([tables[:, HD : HD + HD // 2]] * 4, axis=1)
    cosine_ref[...] = cosine
    sine_ref[...] = sine
    for i in range(2):
        part = pre[:, i * 2 * HD : (i + 1) * 2 * HD]
        part = (part * cosine + turned(part) * sine).astype(BF16) * HD ** (-0.5)
        query_ref[0, 2 * i] = part[:, :HD]
        query_ref[0, 2 * i + 1] = part[:, HD:]
    part = pre[:, HEADS * HD :]
    lane = lax.broadcasted_iota(jnp.int32, part.shape, 1)
    kv_ref[0] = jnp.where(lane < HD, part * cosine + turned(part) * sine, part).astype(BF16)

    @pl.when(step == 3)
    def _():
        back.wait()


def project_qkv(place, x_pieces, w_pieces):
    tile = lambda lanes: pl.BlockSpec((TILE, lanes), lambda i, p: (i, 0))
    return pl.pallas_call(
        project_qkv_kernel,
        grid_spec=pltpu.PrefetchScalarGridSpec(
            num_scalar_prefetch=1,
            grid=(4,),
            in_specs=[ANYWHERE] * 10,
            out_specs=[
                pl.BlockSpec((1, HEADS, TILE, HD), lambda i, p: (i // 2, 0, i % 2, 0)),
                pl.BlockSpec((1, TILE, 2 * HD), lambda i, p: (i // 2, i % 2, 0)),
                tile(1), tile(2 * HD), tile(2 * HD),
                ANYWHERE,
            ],
            scratch_shapes=[
                pltpu.VMEM((2 * HALF, WIDE), BF16),
                pltpu.VMEM((QKV, D), BF16),
                pltpu.SemaphoreType.DMA((27,)),
            ],
        ),
        out_shape=[
            shaped(2, HEADS, HALF, HD), shaped(2, HALF, 2 * HD), shaped(2 * HALF, 1, kind=F32),
            shaped(2 * HALF, 2 * HD, kind=F32), shaped(2 * HALF, 2 * HD, kind=F32), shaped(QKV, D),
        ],
        compiler_params=params("arbitrary"),
        cost_estimate=cost(2 * 2 * HALF * QKV * D, 8),
        name="project_qkv",
    )(place, *x_pieces, *w_pieces)


def project_kernel(left_ref, weight_ref, *parts):
    put_parts(pl.program_id(0), matmul(left_ref[...], weight_ref[...]).astype(BF16), parts)


def project(left, weight):
    depth = left.shape[1]
    return pl.pallas_call(
        project_kernel,
        grid=(4,),
        in_specs=[pl.BlockSpec((TILE, depth), lambda i: (i, 0)), pl.BlockSpec((depth, D), lambda i: (0, 0))],
        out_specs=part_specs(2),
        out_shape=PART_SHAPES,
        compiler_params=params("arbitrary"),
        cost_estimate=cost(2 * 2 * HALF * depth * D, 8),
        name="project",
    )(left, weight)


def put_term(left, rows, term_ref):
    def one(i, carry):
        term = matmul(left, rows[:, pl.ds(pl.multiple_of(i * 4 * B, 4 * B), 4 * B)]).astype(BF16)
        for j in range(2):
            zx = 2 * i + j
            term_ref[zx % 4, zx // 4, 0] = term[:, 2 * j * B : (2 * j + 1) * B]
            term_ref[zx % 4, zx // 4, 1] = term[:, (2 * j + 1) * B : (2 * j + 2) * B]
        return carry

    lax.fori_loop(0, 4, one, 0)


def qkv_back_kernel(*refs):
    x_refs, grad_q, own, later, cosine_ref, sine_ref, scale_ref = refs[1:6], *refs[6:12]
    grad_ref, term_ref, rows, left, sems = refs[12:]
    copies = put_tokens(x_refs, rows, sems, 0)
    for copy in copies:
        copy.start()
    for step in range(4):
        at, s = slice(step * TILE, (step + 1) * TILE), step // 2
        inner = slice(step % 2 * TILE, (step % 2 + 1) * TILE)
        cosine, sine = cosine_ref[at], sine_ref[at]
        pieces = []
        for i in range(2):
            part = grad_q[s, inner, i * 2 * HD : (i + 1) * 2 * HD]
            pieces.append(part * cosine - turned(part * sine))
        lane = lax.broadcasted_iota(jnp.int32, cosine.shape, 1)
        part = own[s, inner] + later[s, inner].astype(F32)
        pieces.append(jnp.where(lane < HD, part * cosine - turned(part * sine), part))
        grad_pre = jnp.concatenate(pieces, axis=1)
        grad_ref[at] = grad_pre.astype(BF16)
        left[:, at] = (grad_pre * scale_ref[at]).T.astype(BF16)
    for copy in copies:
        copy.wait()
    put_term(left[...], rows, term_ref)


def qkv_back(place, x_pieces, grad_query, own, later, cosine, sine, scale):
    whole = lambda *shape: pl.BlockSpec(shape, lambda i, p: (0,) * len(shape))
    tokens = 2 * HALF
    return pl.pallas_call(
        qkv_back_kernel,
        grid_spec=pltpu.PrefetchScalarGridSpec(
            num_scalar_prefetch=1,
            grid=(1,),
            in_specs=[ANYWHERE] * 5
            + [
                whole(2, HALF, HEADS * HD), whole(2, HALF, 2 * HD), whole(2, HALF, 2 * HD),
                whole(tokens, 2 * HD), whole(tokens, 2 * HD), whole(tokens, 1),
            ],
            out_specs=[whole(tokens, QKV), whole(4, 2, 2, QKV, B)],
            scratch_shapes=[
                pltpu.VMEM((tokens, D), BF16), pltpu.VMEM((QKV, tokens), BF16), pltpu.SemaphoreType.DMA((10,)),
            ],
        ),
        out_shape=[shaped(tokens, QKV), shaped(4, 2, 2, QKV, B)],
        compiler_params=params("arbitrary"),
        cost_estimate=cost(2 * tokens * QKV * D, 9),
        name="qkv_back",
    )(place, *x_pieces, grad_query, own, later, cosine, sine, scale)


def attention_term_kernel(*refs):
    token_refs, left_ref = refs[1:6], refs[6]
    term_ref, rows, sems = refs[-3:]
    copies = put_tokens(token_refs, rows, sems, 0)
    for copy in copies:
        copy.start()
    left = left_ref[...]
    if left.shape[0] == 2 * HALF:
        left = left.T
    for copy in copies:
        copy.wait()
    put_term(left, rows, term_ref)


def attention_terms(place, pieces, left, name):
    whole = lambda *shape: pl.BlockSpec(shape, lambda i, p: (0,) * len(shape))
    rows = min(left.shape)
    return pl.pallas_call(
        attention_term_kernel,
        grid_spec=pltpu.PrefetchScalarGridSpec(
            num_scalar_prefetch=1,
            grid=(1,),
            in_specs=[ANYWHERE] * 5 + [whole(*left.shape)],
            out_specs=whole(4, 2, 2, rows, B),
            scratch_shapes=[pltpu.VMEM((2 * HALF, D), BF16), pltpu.SemaphoreType.DMA((10,))],
        ),
        out_shape=shaped(4, 2, 2, rows, B),
        compiler_params=params("arbitrary"),
        cost_estimate=cost(2 * 2 * HALF * rows * D, 7),
        name=name,
    )(place, *pieces, left)


def token_places(at, y, core):
    step = 1 - 2 * core
    block = jnp.where(
        at < B, y, jnp.where(at < 2 * B, y + 4 - step, jnp.where(at < 3 * B, y + 4 + step, y + 2))
    )
    row = at % B
    row = jnp.where(at < 3 * B, row, (row + core * (B // 2)) % B)
    return (block % 4) * B + row


def set_bias(place_ref, bias_ref):
    zlo, y, core = place_ref[0], place_ref[1], place_ref[2]
    key_at = token_places(lax.broadcasted_iota(jnp.int32, (HALF, 1), 0), y, core)
    query_at = token_places(lax.broadcasted_iota(jnp.int32, (1, HALF), 1), y, core)
    bias_ref[:HALF, :] = jnp.broadcast_to(jnp.where(zlo == 1, 0.0, -1e30), (HALF, HALF))
    bias_ref[HALF:, :] = jnp.where(key_at <= query_at, 0.0, -1e30)


def attention_kernel(place_ref, *refs):
    w_refs, query_ref, kv_ref, mixed_ref, log_ref = refs[:5], *refs[5:9]
    parts, w_out, bias_ref, weight, sems = refs[9:14], *refs[14:]
    columns = put_columns(place_ref, w_refs, weight, sems, 0)
    back = pltpu.make_async_copy(weight, w_out, sems.at[16])

    @pl.when(pl.program_id(0) == 0)
    def _():
        for copy in columns:
            copy.start()
        set_bias(place_ref, bias_ref)
        for copy in columns:
            copy.wait()
        back.start()

    key, value = kv_ref[0, :, :HD], kv_ref[0, :, HD:]
    for head in range(HEADS):
        scores = times_transposed(key, query_ref[0, head]) + bias_ref[...]
        top = jnp.max(scores, axis=0, keepdims=True)
        weights = jnp.exp(scores - top)
        total = jnp.sum(weights, axis=0, keepdims=True)
        low = (weights * (1.0 / total)).astype(BF16)
        mixed_ref[0, :, head * HD : (head + 1) * HD] = outer_sum(value, low).T.astype(BF16)
        log_ref[0, head] = top + jnp.log(total)
    put_rows(matmul(mixed_ref[0], weight[...]).astype(BF16), parts)

    @pl.when(pl.program_id(0) == 1)
    def _():
        back.wait()


def attention_back_kernel(place_ref, *refs):
    grad_refs, query_ref, kv_ref, log_ref, weight_ref = refs[:5], *refs[5:9]
    grad_query_ref, earlier_ref, own_ref, bias_ref, rows, sems = refs[9:]
    step = pl.program_id(0)
    copies = put_tokens(grad_refs, rows, sems, 0)

    @pl.when(step == 0)
    def _():
        for copy in copies:
            copy.start()
        set_bias(place_ref, bias_ref)
        for copy in copies:
            copy.wait()

    hidden = rows[pl.ds(pl.multiple_of(step * HALF, HALF), HALF), :]
    grads = times_transposed(hidden, weight_ref[...]).astype(BF16)
    key, value = kv_ref[0, :, :HD], kv_ref[0, :, HD:]
    grad_key = jnp.zeros((2 * HALF, HD), F32)
    grad_value = jnp.zeros((2 * HALF, HD), F32)
    for head in range(HEADS):
        lanes = slice(head * HD, (head + 1) * HD)
        query, grad = query_ref[0, head], grads[:, lanes]
        weights = jnp.exp(times_transposed(key, query) + bias_ref[...] - log_ref[0, head])
        grad_weights = times_transposed(value, grad)
        delta = jnp.sum(weights * grad_weights, axis=0, keepdims=True)
        grad_scores = (weights * (grad_weights - delta)).astype(BF16)
        grad_query_ref[0, :, lanes] = outer_sum(key, grad_scores).T * HD ** (-0.5)
        grad_key += matmul(grad_scores, query)
        grad_value += matmul(weights.astype(BF16), grad)
    total = jnp.concatenate([grad_key, grad_value], axis=1)
    earlier_ref[0] = total[:HALF].astype(BF16)
    own_ref[0] = total[HALF:]


def sequence_block(*tail):
    return pl.BlockSpec((1,) + tail, lambda s, place: (s,) + (0,) * len(tail))


def attention_call(kernel, in_specs, out_specs, out_shape, scratch, flops, name):
    return pl.pallas_call(
        kernel,
        grid_spec=pltpu.PrefetchScalarGridSpec(
            num_scalar_prefetch=1,
            grid=(2,),
            in_specs=in_specs,
            out_specs=out_specs,
            scratch_shapes=[pltpu.VMEM((2 * HALF, HALF), F32)] + scratch,
        ),
        out_shape=out_shape,
        compiler_params=params("arbitrary"),
        cost_estimate=cost(flops * 8 * 2 * HALF * HALF * HD * 2, 8),
        name=name,
    )


def attention(place, w_pieces, query, kv):
    return attention_call(
        attention_kernel,
        [ANYWHERE] * 5 + [sequence_block(HEADS, HALF, HD), sequence_block(2 * HALF, 2 * HD)],
        [sequence_block(HALF, HEADS * HD), sequence_block(HEADS, 1, HALF)]
        + part_specs(1)
        + [ANYWHERE],
        [shaped(2, HALF, HEADS * HD), shaped(2, HEADS, 1, HALF, kind=F32)] + PART_SHAPES + [shaped(HEADS * HD, D)],
        [pltpu.VMEM((HEADS * HD, D), BF16), pltpu.SemaphoreType.DMA((17,))],
        3,
        "attention",
    )(place, *w_pieces, query, kv)


def attention_back(place, grad_pieces, query, kv, log_total, weight):
    return attention_call(
        attention_back_kernel,
        [ANYWHERE] * 5
        + [
            sequence_block(HEADS, HALF, HD), sequence_block(2 * HALF, 2 * HD),
            sequence_block(HEADS, 1, HALF), pl.BlockSpec((HEADS * HD, D), lambda s, place: (0, 0)),
        ],
        [sequence_block(HALF, HEADS * HD), sequence_block(HALF, 2 * HD), sequence_block(HALF, 2 * HD)],
        [
            shaped(2, HALF, HEADS * HD, kind=F32),
            shaped(2, HALF, 2 * HD),
            shaped(2, HALF, 2 * HD, kind=F32),
        ],
        [pltpu.VMEM((2 * HALF, D), BF16), pltpu.SemaphoreType.DMA((10,))],
        6,
        "attention_back",
    )(place, *grad_pieces, query, kv, log_total, weight)


def finish_attention_kernel(place, *refs):
    piece_refs, w_query, w_key, w_value, gain_ref = refs[:4], *refs[4:8]
    query_out, key_out, value_out, gain_out, rows = refs[8:]
    for ref, by in zip(piece_refs, range(4)):
        at_y = (place[1] + by) % 4
        for c in range(2):
            piece = ref[c].astype(F32)
            rows[pl.ds(pl.multiple_of((2 * at_y + c) * HEADS * HD, HEADS * HD), HEADS * HD)] = piece[: HEADS * HD]
        both = ref[0].astype(F32) + ref[1].astype(F32)
        at = pl.multiple_of(H * HD + at_y * HD, HD)
        rows[pl.ds(at, HD)] = both[HEADS * HD : (HEADS + 1) * HD]
        rows[pl.ds(at + KV * HD, HD)] = both[(HEADS + 1) * HD :]
    gain = gain_ref[...]
    total = jnp.zeros((B, 1), F32)
    row = 0
    for weight, out in ((w_query, query_out), (w_key, key_out), (w_value, value_out)):
        for i in range(out.shape[1] // B):
            lanes = slice(i * B, (i + 1) * B)
            block = rows[row : row + B].T
            total = total + jnp.sum(block * weight[:, lanes].astype(F32), axis=1, keepdims=True)
            out[:, lanes] = block * gain
            row += B
    gain_out[...] = total


def finish_attention(place, pieces, w_query, w_key, w_value, gain):
    whole = lambda *shape: pl.BlockSpec(shape, lambda i, p: (0,) * len(shape))
    kv = KV * HD
    return pl.pallas_call(
        finish_attention_kernel,
        grid_spec=pltpu.PrefetchScalarGridSpec(
            num_scalar_prefetch=1,
            grid=(1,),
            in_specs=[whole(2, QKV, B)] * 4 + [whole(B, D), whole(B, kv), whole(B, kv), whole(B, 1)],
            out_specs=[whole(B, D), whole(B, kv), whole(B, kv), whole(B, 1)],
            scratch_shapes=[pltpu.VMEM((D + 2 * kv, B), F32)],
        ),
        out_shape=[
            shaped(B, D, kind=F32), shaped(B, kv, kind=F32), shaped(B, kv, kind=F32), shaped(B, 1, kind=F32),
        ],
        compiler_params=params("arbitrary"),
        cost_estimate=cost(0, 4),
        name="finish_attention",
    )(place, *pieces, w_query, w_key, w_value, gain)


def finish_output_kernel(blocks, out):
    for i in range(16):
        out[:, i * B : (i + 1) * B] = blocks[i].astype(F32)


def finish_output(blocks):
    return pl.pallas_call(
        finish_output_kernel,
        out_shape=shaped(B, D, kind=F32),
        compiler_params=params(),
        cost_estimate=cost(0, 2),
        name="finish_output",
    )(blocks)


def feed_forward_kernel(*refs):
    place, token_refs, grad_refs, ff_ref = refs[0], refs[1:6], refs[6:11], refs[11]
    act_ref, act_t, gate_t, up_t = refs[12:16]
    parts, down_out = refs[16:21], refs[21]
    rows_h, rows_g, gate_up, down, slabs, sems = refs[22:]
    step = pl.program_id(0)
    tokens = put_tokens(token_refs, rows_h, sems, 0)
    grads = put_tokens(grad_refs, rows_g, sems, 10)
    weights, loads = [], []
    for x in range(4):
        for by in range(4):
            z = (2 * place[4] + place[0] + by) % 4
            zhi, zlo = z // 2, z % 2
            for core in range(2):
                weights.append(
                    pltpu.make_async_copy(
                        ff_ref.at[x, by, pl.ds(core * FFL, FFL)],
                        gate_up.at[zlo, :, lane_block(zhi, x, core)],
                        sems.at[20 + len(weights)],
                    )
                )
            loads.append(
                pltpu.make_async_copy(
                    ff_ref.at[x, by, pl.ds(2 * FFL, FFL)], slabs.at[zlo, zhi * 4 + x], sems.at[52 + len(loads)]
                )
            )
    back = pltpu.make_async_copy(down, down_out, sems.at[68])

    @pl.when(step == 0)
    def _():
        for copy in tokens + weights + loads + grads:
            copy.start()
        for copy in tokens + weights:
            copy.wait()

    rows = pl.ds(pl.multiple_of(step * HALF, HALF), HALF)
    normed = rows_h[rows, :]
    gate_pre = times_transposed(normed, gate_up[0])
    upward = times_transposed(normed, gate_up[1])

    @pl.when(step == 0)
    def _():
        for copy in loads:
            copy.wait()

        def put(q, carry):
            for half in range(2):
                for p in range(4):
                    one = slabs[half, 2 * q, 2 * p * PIECE : 2 * (p + 1) * PIECE, :].astype(F32)
                    two = slabs[half, 2 * q + 1, 2 * p * PIECE : 2 * (p + 1) * PIECE, :].astype(F32)
                    lane = (half * 8 + 2 * p) * B
                    rows = pl.ds(pl.multiple_of(q * 2 * PIECE, 16), 2 * PIECE)
                    down[rows, lane : lane + B] = jnp.concatenate([one[:PIECE], two[:PIECE]], axis=0).astype(BF16)
                    down[rows, lane + B : lane + 2 * B] = jnp.concatenate(
                        [one[PIECE:], two[PIECE:]], axis=0
                    ).astype(BF16)
            return carry

        lax.fori_loop(0, 4, put, 0)
        back.start()
        for copy in grads:
            copy.wait()

    grad_act = times_transposed(rows_g[rows, :], down[...])
    sigmoid = 1.0 / (1.0 + jnp.exp(-gate_pre))
    silu = gate_pre * sigmoid
    activation = silu * upward
    grad_up = grad_act * silu
    grad_gate = grad_act * upward * (sigmoid * (1.0 + gate_pre * (1.0 - sigmoid)))
    part = matmul(grad_gate.astype(BF16), gate_up[0]) + matmul(grad_up.astype(BF16), gate_up[1])
    put_rows(part.astype(BF16), parts)
    act_ref[...] = activation.astype(BF16)
    act_t[...] = activation.T.astype(BF16)
    gate_t[...] = grad_gate.T.astype(BF16)
    up_t[...] = grad_up.T.astype(BF16)

    @pl.when(step == 1)
    def _():
        back.wait()


def feed_forward(place, tokens, grads, ff_all):
    turned_spec = pl.BlockSpec((FFL, HALF), lambda i, p: (0, i))
    turned_shape = shaped(FFL, 2 * HALF)
    return pl.pallas_call(
        feed_forward_kernel,
        grid_spec=pltpu.PrefetchScalarGridSpec(
            num_scalar_prefetch=1,
            grid=(2,),
            in_specs=[ANYWHERE] * 11,
            out_specs=[pl.BlockSpec((HALF, FFL), lambda i, p: (i, 0))]
            + [turned_spec] * 3
            + part_specs(1)
            + [ANYWHERE],
            scratch_shapes=[
                pltpu.VMEM((2 * HALF, D), BF16),
                pltpu.VMEM((2 * HALF, D), BF16),
                pltpu.VMEM((2, FFL, D), BF16),
                pltpu.VMEM((FFL, D), BF16),
                pltpu.VMEM((2, 8, FFL, B), BF16),
                pltpu.SemaphoreType.DMA((69,)),
            ],
        ),
        out_shape=[shaped(2 * HALF, FFL)] + [turned_shape] * 3 + PART_SHAPES + [shaped(FFL, D)],
        compiler_params=params("arbitrary"),
        cost_estimate=cost(2 * 5 * 2 * HALF * FFL * D, 32),
        name="feed_forward",
    )(place, *tokens, *grads, ff_all)


def along_z(place, zhi, zlo):
    return (2 * zhi + zlo + 4 - 2 * place[4] - place[0]) % 4


def load_tokens(step, refs, rows, sems):
    copies = put_tokens(refs, rows, sems, 0)

    @pl.when(step == 0)
    def _():
        for copy in copies:
            copy.start()
        for copy in copies:
            copy.wait()


def gate_up_kernel(*refs):
    place, token_refs, gate_t, up_t, out_ref, rows, terms, sems = refs[0], refs[1:6], *refs[6:]
    step = pl.program_id(0)
    load_tokens(step, token_refs, rows, sems)
    normed = rows[:, pl.ds(pl.multiple_of(step * 4 * B, 4 * B), 4 * B)]

    def out(i, matrix):
        xs, by = pl.ds(i % 2 * 2, 2), along_z(place, i // 2, matrix)
        return pltpu.make_async_copy(terms.at[xs, by], out_ref.at[xs, by], sems.at[10 + 2 * i + matrix])

    for matrix, left in ((0, gate_t), (1, up_t)):
        term = matmul(left[...], normed).astype(BF16)
        by = along_z(place, step // 2, matrix)
        for j in range(2):
            terms[step % 2 * 2 + j, by, 0:FFL, :] = term[:, 2 * j * B : (2 * j + 1) * B]
            terms[step % 2 * 2 + j, by, FFL:, :] = term[:, (2 * j + 1) * B : (2 * j + 2) * B]
        out(step, matrix).start()

    @pl.when(step == 3)
    def _():
        for i in range(4):
            for matrix in range(2):
                out(i, matrix).wait()


def down_kernel(*refs):
    place, grad_refs, act_t, out_ref, rows, terms, sems = refs[0], refs[1:6], *refs[6:]
    step = pl.program_id(0)
    load_tokens(step, grad_refs, rows, sems)
    term = matmul(act_t[...], rows[:, pl.ds(pl.multiple_of(step * 4 * B, 4 * B), 4 * B)])
    for j in range(2):
        p = (2 * step + j) % 4
        at = pl.ds(pl.multiple_of(p * 2 * PIECE, 16), 2 * PIECE)
        for zx in range(8):
            slab = term[zx * PIECE : (zx + 1) * PIECE]
            low, high = slab[:, 2 * j * B : (2 * j + 1) * B], slab[:, (2 * j + 1) * B : (2 * j + 2) * B]
            by = along_z(place, zx // 4, step // 2)
            terms[zx % 4, by, at, :] = jnp.concatenate([low, high], axis=0).astype(BF16)

    def out(half, zhi):
        by = along_z(place, zhi, half)
        return pltpu.make_async_copy(terms.at[:, by], out_ref.at[:, by], sems.at[10 + 2 * half + zhi])

    @pl.when(step % 2 == 1)
    def _():
        for zhi in range(2):
            out(step // 2, zhi).start()

    @pl.when(step == 3)
    def _():
        for half in range(2):
            for zhi in range(2):
                out(half, zhi).wait()


def ff_terms(kernel, place, pieces, lefts, rows, name):
    whole = pl.BlockSpec((FFL, 2 * HALF), lambda i, p: (0, 0))
    return pl.pallas_call(
        kernel,
        grid_spec=pltpu.PrefetchScalarGridSpec(
            num_scalar_prefetch=1,
            grid=(4,),
            in_specs=[ANYWHERE] * 5 + [whole] * len(lefts),
            out_specs=ANYWHERE,
            scratch_shapes=[
                pltpu.VMEM((2 * HALF, D), BF16),
                pltpu.VMEM((4, 4, rows, B), BF16),
                pltpu.SemaphoreType.DMA((18,)),
            ],
        ),
        out_shape=shaped(4, 4, rows, B),
        compiler_params=params("arbitrary"),
        cost_estimate=cost(2 * len(lefts) * 2 * HALF * FFL * D, 8 + 4 * len(lefts)),
        name=name,
    )(place, *pieces, *lefts)


def finish_hidden_kernel(*refs):
    place, piece_refs, weight_ref, gain_ref, out_ref, gain_out, rows = refs[0], refs[1:5], *refs[5:]
    for ref, by in zip(piece_refs, range(4)):
        at_y = (place[1] + by) % 4
        for core in range(2):
            slab = ref[0, core].astype(F32)
            for zx in range(8):
                at = pl.multiple_of((2 * zx + core) * 4 * PIECE + at_y * PIECE, 8)
                rows[pl.ds(at, PIECE)] = slab[zx * PIECE : (zx + 1) * PIECE]
    gain = gain_ref[...]
    total = jnp.zeros((B, 1), F32)
    for i in range(FF // B):
        lanes = slice(i * B, (i + 1) * B)
        block = rows[lanes].T
        total = total + jnp.sum(block * weight_ref[:, lanes].astype(F32), axis=1, keepdims=True)
        out_ref[:, lanes] = block * gain
    gain_out[...] = total


def finish_hidden(place, pieces, matrix, weight, gain):
    own, after, low, high, before = pieces
    at = lambda m: pl.BlockSpec((1, 2, FFL, B), lambda i, p: (m, 0, 0, 0))
    whole = lambda *shape: pl.BlockSpec(shape, lambda i, p: (0,) * len(shape))
    return pl.pallas_call(
        finish_hidden_kernel,
        grid_spec=pltpu.PrefetchScalarGridSpec(
            num_scalar_prefetch=1,
            grid=(1,),
            in_specs=[at(matrix), at(matrix), at(0), at(matrix), whole(B, FF), whole(B, 1)],
            out_specs=[whole(B, FF), whole(B, 1)],
            scratch_shapes=[pltpu.VMEM((FF, B), F32)],
        ),
        out_shape=[shaped(B, FF, kind=F32), shaped(B, 1, kind=F32)],
        compiler_params=params("arbitrary"),
        cost_estimate=cost(3 * 10**9, 6),
        name="finish_hidden",
    )(place, own, after, (low, high)[matrix], before, weight, gain)


def finish_down_kernel(place, own, after, low, high, before, out_ref):
    for refs, by in (((own, own), 0), ((after, after), 1), ((low, high), 2), ((before, before), 3)):
        rows = pl.ds(pl.multiple_of((place[1] + by) % 4 * PIECE, 8), PIECE)
        for half in range(2):
            slab = refs[half][half if by != 2 else 0].astype(F32)
            for t in range(8):
                lane = (half * 8 + t) * B
                out_ref[rows, lane : lane + B] = slab[t * PIECE : (t + 1) * PIECE]


def finish_down(place, pieces):
    halves = lambda n: pl.BlockSpec((n, FFL, B), lambda i, p: (0, 0, 0))
    return pl.pallas_call(
        finish_down_kernel,
        grid_spec=pltpu.PrefetchScalarGridSpec(
            num_scalar_prefetch=1,
            grid=(1,),
            in_specs=[halves(2), halves(2), halves(1), halves(1), halves(2)],
            out_specs=pl.BlockSpec((4 * PIECE, D), lambda i, p: (0, 0)),
        ),
        out_shape=shaped(4 * PIECE, D, kind=F32),
        compiler_params=params("arbitrary"),
        cost_estimate=cost(2 * 10**9, 5),
        name="finish_down",
    )(place, *pieces)


def own_rows(rows_all, y, core, per):
    return lax.dynamic_slice_in_dim(rows_all, (2 * y + core) * per, per, 0)


class Flow:
    def __init__(self, steps):
        self.steps, self.result, self.sent = steps, None, None
        self.move(None)

    def move(self, arrived):
        try:
            self.sent = self.steps.send(arrived)
        except StopIteration as end:
            self.sent, self.result = (), end.value


def stage(flows, *values):
    flows = [flow for flow in flows if flow.result is None]
    sizes = [len(flow.sent) for flow in flows]
    leaves, tree = jax.tree.flatten(values)
    tied = tie(*[v for flow in flows for v in flow.sent], *leaves)
    for flow, size in zip(flows, sizes):
        flow.move(tied[:size])
        tied = tied[size:]
    return jax.tree.unflatten(tree, tied)


def gather_steps(block):
    (other,) = yield (swap_core(block),)
    pair = jnp.stack([block, other])
    (got,) = yield (along_y(pair),)
    far, swapped = yield (along_y(send_half(got)), swap_core(got))
    (far_swapped,) = yield (swap_core(far),)
    return pair, got, swapped, far, far_swapped


def scatter_steps(parts):
    core = lax.axis_index("core")
    first, behind, ahead, far, far_other = parts
    (far_got,) = yield (swap_core(far_other),)
    far = add(far, far_got).astype(BF16)
    low, behind_got, first_got = yield (along_y(far), swap_core(behind), swap_core(first[1]))
    ahead = add(ahead, behind_got).astype(BF16)
    mine = add(lax.dynamic_slice_in_dim(ahead, core * (B // 2), B // 2, 1), low).astype(BF16)
    ahead = lax.dynamic_update_slice_in_dim(ahead, mine, core * (B // 2), 1)
    (got,) = yield (along_y(ahead),)
    (last,) = yield (swap_core(got[1]),)
    return add(first[0], first_got) + got[0].astype(F32) + last.astype(F32)


def ring_gather_steps(block, axis):
    half = block.shape[0] // 2
    before, after = yield (shift(block, axis, 1), shift(block, axis, -1))
    low, high = yield (shift(before[:half], axis, 1), shift(after[half:], axis, -1))
    return block, after, low, high, before


def ring_scatter_steps(parts, axis):
    half = parts[2].shape[0] // 2
    low, high = yield (shift(parts[2][:half], axis, 1), shift(parts[2][half:], axis, -1))
    after = jnp.concatenate([add(parts[1][:half], low).astype(BF16), parts[1][half:]], axis=0)
    before = jnp.concatenate([parts[3][:half], add(parts[3][half:], high).astype(BF16)], axis=0)
    from_before, from_after = yield (shift(after, axis, 1), shift(before, axis, -1))
    return add(parts[0], from_before) + from_after.astype(F32)


def on_device(
    layer_input,
    positions,
    attn_gain,
    w_query,
    w_key,
    w_value,
    w_output,
    mlp_gain,
    w_gate,
    w_up,
    w_down,
    out_grad,
):
    zlo, y, zhi, x, core = (lax.axis_index(axis) for axis in AXES)
    place = jnp.stack([zlo, y, core, x, zhi]).astype(jnp.int32)

    def by_core(mine, got):
        return jnp.where(core == 0, jnp.stack([mine, got]), jnp.stack([got, mine]))

    def by_zlo(mine, got):
        return jnp.where(zlo == 0, jnp.stack([mine, got]), jnp.stack([got, mine]))

    def by_zhi(mine, got):
        return jnp.where(zhi == 0, jnp.stack([mine, got]), jnp.stack([got, mine]))

    def trio(mine, other, axis):
        across = lax.ppermute(other, (axis, "core"), [(i, 3 - i) for i in range(4)])
        return shift(mine, axis, 1), swap_core(other), across

    def column_steps(mine, got):
        pair = by_core(mine, got)
        (got,) = yield (shift(pair, "zhi", 1),)
        return (yield from ring_gather_steps(by_zhi(pair, got), "x"))

    def output_steps(mine, other):
        there, here, across = yield trio(mine, other, "zhi")
        column = by_zhi(by_core(mine, here), by_core(there, across))
        return (yield from ring_gather_steps(column, "x"))

    def hidden_steps(mine, got, down):
        piece = jnp.concatenate([by_core(mine, got).reshape(2 * FFL, B), down], axis=0)
        pieces = yield from ring_gather_steps(piece, "z")
        return jnp.concatenate(pieces, axis=0).reshape(4, 3 * FFL, B)

    def of_core(pair, other=False):
        return lax.dynamic_index_in_dim(pair, 1 - core if other else core, 0, keepdims=False)

    def whole_ring(pieces):
        own, after, low, high, before = pieces
        return own, after, jnp.concatenate([low, high], axis=0), before

    def attention_steps(column):
        keep = lax.dynamic_index_in_dim(column, zhi, 0, keepdims=False)
        send = lax.dynamic_index_in_dim(column, 1 - zhi, 0, keepdims=False)
        (got,) = yield (shift(send, "zhi", 1),)
        pair = add(keep, got).astype(BF16)
        mine, other = of_core(pair), of_core(pair, True)
        there, here, across = yield trio(mine, other, "zlo")
        own = by_core(add(mine, there), add(here, across)).astype(BF16)
        return (yield from ring_gather_steps(own, "y"))

    def gate_up_steps(sums):
        own = yield from ring_scatter_steps([sums[i] for i in range(4)], "z")
        pair = own.astype(BF16).reshape(2, FFL, B)
        mine, other = of_core(pair), of_core(pair, True)
        there, here, across = yield trio(mine, other, "zlo")
        block = by_zlo(by_core(mine, here), by_core(there, across))
        before, after = yield (shift(block, "y", 1), shift(block, "y", -1))
        low, high = yield (shift(before[:1], "y", 1), shift(after[1:], "y", -1))
        return block, after, low, high, before

    def down_steps(sums):
        own = yield from ring_scatter_steps([sums[i] for i in range(4)], "z")
        own = own.astype(BF16)
        yield ()
        (got,) = yield (shift(own, "zlo", 1),)
        return (yield from ring_gather_steps(by_zlo(own, got), "y"))

    x_low = layer_input[0]
    frequency = theta ** (-jnp.arange(0, HD, 2).astype(F32) / HD)
    angles = positions[0].astype(F32)[:, None] * frequency
    tables = []
    for table in (jnp.cos(angles), jnp.sin(angles)):
        high = lax.reduce_precision(table, 8, 7)
        tables += [high.astype(BF16), (table - high).astype(BF16)]
    tokens = Flow(gather_steps(jnp.concatenate([x_low, *tables], axis=1)))
    grads = Flow(gather_steps(out_grad[0]))
    qkv_mine, qkv_other = prepare_qkv(place, w_query, w_key, w_value, attn_gain[:, None])
    qkv_mine, qkv_got, gain_two, w_out = stage([tokens], qkv_mine, swap_core(qkv_other), mlp_gain[:, None], w_output)

    columns = Flow(column_steps(qkv_mine, qkv_got))
    o_rows = lax.all_to_all(w_out.reshape(B, 16, B).transpose(1, 0, 2), FSDP, 0, 0, tiled=True)
    ff_mine, ff_other, ff_down = prepare_ff(place, w_gate, w_up, w_down, gain_two)
    ff_mine, ff_got, ff_down, x_low, o_rows = stage(
        [tokens, columns], ff_mine, swap_core(ff_other), ff_down, x_low, o_rows
    )

    inputs = x_low.astype(F32)
    scale_one = lax.rsqrt(jnp.mean(inputs * inputs, axis=-1, keepdims=True) + eps)
    o_rows = o_rows.reshape(D, B)
    mine, other = own_rows(o_rows, y, core, HEADS * HD), own_rows(o_rows, y, 1 - core, HEADS * HD)
    scale_one, mine, other, ff_mine, ff_got, ff_down = stage(
        [tokens, columns, grads], scale_one, mine, other, ff_mine, ff_got, ff_down
    )

    outputs = Flow(output_steps(mine, other))
    ff_mine, ff_got, ff_down = stage([tokens, columns, outputs], ff_mine, ff_got, ff_down)

    hidden_rows = Flow(hidden_steps(ff_mine, ff_got, ff_down))
    x_pieces = tokens.result
    query, key_value, scale_all, cosine, sine, qkv_full = project_qkv(place, x_pieces, columns.result)
    query, key_value = stage([hidden_rows, outputs, grads], query, key_value)

    earlier = lax.ppermute(key_value, "zlo", [(0, 1)])
    query, key_value, earlier = stage([outputs, hidden_rows], query, key_value, earlier)
    ff_all = lax.all_gather(hidden_rows.result, "x", axis=0, tiled=False)

    key_value = jnp.concatenate([earlier, key_value], axis=1)
    mixed, log_total, *parts, o_full = attention(place, outputs.result, query, key_value)
    parts = stage([grads], *parts)
    sums = Flow(scatter_steps(parts))
    stage([sums, grads])
    grad_pieces = grads.result
    for _ in range(3):
        stage([sums])
    hidden = inputs + sums.result
    scale_two = lax.rsqrt(jnp.mean(hidden * hidden, axis=-1, keepdims=True) + eps)
    normed = Flow(gather_steps((hidden * scale_two).astype(BF16)))
    for _ in range(4):
        stage([normed])
    normed_pieces = normed.result

    activation, act_t, gate_t, up_t, *parts, down_full = feed_forward(place, normed_pieces, grad_pieces, ff_all)
    sums = Flow(scatter_steps(parts))
    (act_t,) = stage([sums], act_t)
    down_terms = ff_terms(down_kernel, place, grad_pieces, (act_t,), FFL, "down_terms")
    down_terms, gate_t = stage([sums], down_terms, gate_t)
    down_sum = lax.psum_scatter(down_terms, "x", scatter_dimension=0, tiled=True)[0]
    gate_up_terms = ff_terms(gate_up_kernel, place, normed_pieces, (gate_t, up_t), 2 * FFL, "gate_up_terms")
    (gate_up_terms,) = stage([sums], gate_up_terms)
    gate_up_sum = lax.psum_scatter(gate_up_terms, "x", scatter_dimension=0, tiled=True)[0]
    stage([sums])

    grad_normed_two = sums.result
    mean_two = jnp.mean(grad_normed_two * hidden, axis=-1, keepdims=True)
    grad_hidden = (
        out_grad[0].astype(F32)
        + scale_two * grad_normed_two
        - hidden * (scale_two * scale_two * scale_two) * mean_two
    )
    hidden_grads = Flow(gather_steps(grad_hidden.astype(BF16)))
    (activation,) = stage([hidden_grads], activation)
    down_parts = project(activation, down_full)
    *down_parts, down_sum = stage([hidden_grads], *down_parts, down_sum)
    result = Flow(scatter_steps(down_parts))
    down = Flow(down_steps(down_sum))
    stage([hidden_grads, down])
    stage([hidden_grads, result])

    hidden_grad_pieces = hidden_grads.result
    grad_query, grad_earlier, grad_own = attention_back(
        place, hidden_grad_pieces, query, key_value, log_total, o_full
    )
    grad_query, grad_earlier, grad_own, mixed = stage([result, down], grad_query, grad_earlier, grad_own, mixed)

    later = lax.ppermute(grad_earlier, "zlo", [(1, 0)])
    output_terms = attention_terms(
        place, hidden_grad_pieces, mixed.reshape(2 * HALF, HEADS * HD), "output_terms"
    )
    later, grad_query, output_terms, gate_up_sum = stage(
        [result, down], later, grad_query, output_terms, gate_up_sum
    )

    output_sum = lax.psum_scatter(output_terms, "x", scatter_dimension=0, tiled=True)[0]
    gate_up = Flow(gate_up_steps(gate_up_sum))
    grad_pre, terms = qkv_back(place, x_pieces, grad_query, grad_own, later, cosine, sine, scale_all)
    grad_pre, terms = stage([gate_up, down, result], grad_pre, terms)

    attention_sum = lax.psum_scatter(terms, "x", scatter_dimension=0, tiled=True)[0]
    parts = project(grad_pre, qkv_full)
    *parts, output_sum = stage([gate_up, down], *parts, output_sum)

    sums = Flow(scatter_steps(parts))
    output_sums = Flow(attention_steps(output_sum))
    (attention_sum,) = stage([sums, gate_up, output_sums, down], attention_sum)
    attention_sums = Flow(attention_steps(attention_sum))
    stage([output_sums, attention_sums])
    down_grad = finish_down(place, down.result)
    (down_grad,) = stage([output_sums, attention_sums, gate_up], down_grad)
    stage([sums, output_sums, attention_sums, gate_up])

    ring = jnp.roll(jnp.stack(whole_ring(output_sums.result)), y, axis=0).reshape(16, B, B)
    output_grad = lax.all_to_all(ring, FSDP, 0, 0, tiled=True)
    gain_two = mlp_gain[:, None]
    gate_grad, gate_gain = finish_hidden(place, gate_up.result, 0, w_gate, gain_two)
    up_grad, up_gain = finish_hidden(place, gate_up.result, 1, w_up, gain_two)
    gate_grad, up_grad = stage([sums, attention_sums], gate_grad, up_grad)
    stage([sums])
    grad_normed = sums.result
    mean_one = jnp.mean(grad_normed * inputs, axis=-1, keepdims=True)
    input_grad = (
        grad_hidden
        + scale_one * grad_normed
        - inputs * (scale_one * scale_one * scale_one) * mean_one
    )
    input_grad = input_grad.astype(BF16)
    query_grad, key_grad, value_grad, attn_gain_grad = finish_attention(
        place, whole_ring(attention_sums.result), w_query, w_key, w_value, attn_gain[:, None]
    )
    output_grad, query_grad = tie(output_grad, query_grad)
    output_grad = finish_output(output_grad)
    return (
        (hidden + result.result).astype(BF16)[None],
        input_grad[None],
        attn_gain_grad[:, 0],
        query_grad,
        key_grad,
        value_grad,
        output_grad,
        (gate_gain + up_gain)[:, 0],
        gate_grad,
        up_grad,
        down_grad,
    )


def solution(mesh):
    split = Mesh(mesh.devices.reshape(2, 4, 2, 4, 2), AXES)
    tokens = P(FSDP, SEQ, None)
    rows = P(FSDP, None)
    gain = P(FSDP)
    in_specs = (
        tokens, P(FSDP, SEQ), gain, rows, rows, rows, rows, gain, rows, rows, rows, tokens,
    )
    out_specs = (tokens, tokens, gain, rows, rows, rows, rows, gain, rows, rows, rows)
    return jax.shard_map(
        on_device, mesh=split, in_specs=in_specs, out_specs=out_specs, check_vma=False
    )
```

```python
import jax
import jax.numpy as jnp
from jax import lax
from jax.experimental import pallas as pl
from jax.experimental.pallas import tpu as pltpu
from jax.sharding import Mesh
from jax.sharding import PartitionSpec as P

H = 32
KV = 4
HD = 64
D = 2048
FF = 5632
B = 128
HALF = 512
HEADS = 4
FFL = 704
PIECE = 88

eps = 1e-05
theta = 10000.0
F32 = jnp.float32
BF16 = jnp.bfloat16
AXES = ("zlo", "y", "zhi", "x", "core")
FSDP = ("zhi", "x", "core")
SEQ = ("zlo", "y")


def matmul(left, right):
    return jnp.dot(left, right, preferred_element_type=F32)


def times_transposed(left, right):
    return lax.dot_general(left, right, (((1,), (1,)), ((), ())), preferred_element_type=F32)


def outer_sum(left, right):
    return lax.dot_general(left, right, (((0,), (0,)), ((), ())), preferred_element_type=F32)


def shift(value, axis, by):
    if axis == "z":
        at = [2 * (z % 2) + z // 2 for z in range(4)]
        return lax.ppermute(value, ("zlo", "zhi"), [(at[z], at[(z + by) % 4]) for z in range(4)])
    size = lax.axis_size(axis)
    return lax.ppermute(value, axis, [(i, (i + by) % size) for i in range(size)])


def swap_core(value):
    return shift(value, "core", 1)


def small_gather(block, axis):
    return shift(block, axis, -1), shift(block, axis, 2), shift(block, axis, 1)


def tie(*values):
    return lax.optimization_barrier(values)


def add(left, right):
    return left.astype(F32) + right.astype(F32)


def along_y(value):
    pairs = []
    for i in range(4):
        pairs.append((2 * i, 2 * ((i + 1) % 4)))
        pairs.append((2 * i + 1, 2 * ((i + 3) % 4) + 1))
    return lax.ppermute(value, ("y", "core"), pairs)


def send_half(got):
    core = lax.axis_index("core")
    return lax.dynamic_slice_in_dim(got, core * (B // 2), B // 2, 1)


FLIPPED = (0, 0, 1, 0, 1)
LENGTHS = (B, B, B, B // 2, B // 2)


def put_tokens(refs, rows_ref, sems, start):
    lanes = pl.ds(0, rows_ref.shape[1])
    copies = []
    row = 0
    for s in range(2):
        for ref, flip, length in zip(refs, FLIPPED, LENGTHS):
            copies.append(
                pltpu.make_async_copy(
                    ref.at[s ^ flip, :, lanes], rows_ref.at[pl.ds(row, length)], sems.at[start + len(copies)]
                )
            )
            row += length
    return copies


TILE = 256
WIDE = D + B
VMEM_LIMIT = 56 * 2**20
ANYWHERE = pl.BlockSpec(memory_space=pl.ANY)


def params(*kinds):
    return pltpu.CompilerParams(dimension_semantics=kinds or None, vmem_limit_bytes=VMEM_LIMIT)


def cost(flops, megabytes):
    return pl.CostEstimate(flops=flops, bytes_accessed=int(megabytes * 2**20), transcendentals=0)


def shaped(*shape, kind=BF16):
    return jax.ShapeDtypeStruct(shape, kind)


PARTS = ((B, False), (B, True), (B, False), (B // 2, False), (B // 2, True))
PART_SHAPES = [jax.ShapeDtypeStruct((2, n, D), BF16) for n, _ in PARTS]


def part_specs(steps):
    def of(turn):
        return lambda i, *_: (1 - i // steps if turn else i // steps, 0, 0)

    return [pl.BlockSpec((1, n, D), of(turn)) for n, turn in PARTS]


def put_parts(step, tile, refs):
    @pl.when(step % 2 == 0)
    def _():
        refs[0][0] = tile[:B]
        refs[1][0] = tile[B:]

    @pl.when(step % 2 == 1)
    def _():
        refs[2][0] = tile[:B]
        refs[3][0] = tile[B : B + B // 2]
        refs[4][0] = tile[B + B // 2 :]


def put_rows(rows, refs):
    row = 0
    for ref, (length, _) in zip(refs, PARTS):
        ref[0] = rows[row : row + length]
        row += length


def turned(values):
    lane = lax.broadcasted_iota(jnp.int32, values.shape, 1) % HD
    return jnp.where(lane < HD // 2, -pltpu.roll(values, 2 * HD - HD // 2, 1), pltpu.roll(values, HD // 2, 1))


def lane_block(zhi, x, core):
    return pl.ds(pl.multiple_of((zhi * 8 + x * 2 + core) * B, B), B)


def put_columns(place, refs, into, sems, start):
    copies = []
    for ref, by, first in zip(refs, (0, 1, 2, 2, 3), (0, 0, 0, 1, 0)):
        for i in range(ref.shape[0]):
            for core in range(2):
                lanes = lane_block(first + i, (place[3] + by) % 4, core)
                copies.append(
                    pltpu.make_async_copy(ref.at[i, core], into.at[:, lanes], sems.at[start + len(copies)])
                )
    return copies


def prepare_qkv_kernel(place, q_mine, q_other, w_key, w_value, gain, mine_ref, other_ref, k_rows, v_rows):
    scale = gain[...]
    k_rows[...] = (w_key[...].astype(F32) * scale).T
    v_rows[...] = (w_value[...].astype(F32) * scale).T
    rows = pl.ds(pl.multiple_of(place[1] * HD, HD), HD)
    for source, out in ((q_mine, mine_ref), (q_other, other_ref)):
        out[: HEADS * HD] = (source[...].astype(F32) * scale).T.astype(BF16)
        out[HEADS * HD : (HEADS + 1) * HD] = k_rows[rows].astype(BF16)
        out[(HEADS + 1) * HD :] = v_rows[rows].astype(BF16)


QKV = (HEADS + 2) * HD


def prepare_qkv(place, w_query, w_key, w_value, gain):
    whole = lambda *shape: pl.BlockSpec(shape, lambda i, p: (0,) * len(shape))
    return pl.pallas_call(
        prepare_qkv_kernel,
        grid_spec=pltpu.PrefetchScalarGridSpec(
            num_scalar_prefetch=1,
            grid=(1,),
            in_specs=[
                pl.BlockSpec((B, HEADS * HD), lambda i, p: (0, 2 * p[1] + p[2])),
                pl.BlockSpec((B, HEADS * HD), lambda i, p: (0, 2 * p[1] + 1 - p[2])),
                whole(B, KV * HD), whole(B, KV * HD), whole(B, 1),
            ],
            out_specs=[whole(QKV, B), whole(QKV, B)],
            scratch_shapes=[pltpu.VMEM((KV * HD, B), F32), pltpu.VMEM((KV * HD, B), F32)],
        ),
        out_shape=[shaped(QKV, B), shaped(QKV, B)],
        compiler_params=params("arbitrary"),
        cost_estimate=cost(0, 1),
        name="prepare_qkv",
    )(place, w_query, w_query, w_key, w_value, gain)


def prepare_ff_kernel(place, w_gate, w_up, w_down, gain, mine_ref, other_ref, down_ref, picked, rows, down_rows, sems):
    zlo, y, core = place[0], place[1], place[2]
    down = pltpu.make_async_copy(
        w_down.at[:, pl.ds(pl.multiple_of(zlo * (D // 2), D // 2), D // 2)], down_rows, sems.at[1]
    )
    down.start()

    @pl.when(zlo == 0)
    def _():
        copy = pltpu.make_async_copy(w_gate, picked, sems.at[0])
        copy.start()
        copy.wait()

    @pl.when(zlo == 1)
    def _():
        copy = pltpu.make_async_copy(w_up, picked, sems.at[0])
        copy.start()
        copy.wait()

    scale = gain[...]
    for i in range(FF // B):
        rows[i * B : (i + 1) * B] = (picked[:, i * B : (i + 1) * B].astype(F32) * scale).T
    for which, out in ((core, mine_ref), (1 - core, other_ref)):
        slabs = []
        for zx in range(8):
            at = pl.multiple_of(zx * 2 * 4 * PIECE + which * 4 * PIECE + y * PIECE, 8)
            slabs.append(rows[pl.ds(at, PIECE)])
        out[...] = jnp.concatenate(slabs, axis=0).astype(BF16)
    down.wait()
    for t in range(8):
        rows[t * 4 * PIECE : (t + 1) * 4 * PIECE] = down_rows[:, t * B : (t + 1) * B].astype(F32)
    slabs = [rows[pl.ds(pl.multiple_of(t * 4 * PIECE + y * PIECE, 8), PIECE)] for t in range(8)]
    down_ref[...] = jnp.concatenate(slabs, axis=0).astype(BF16)


def prepare_ff(place, w_gate, w_up, w_down, gain):
    return pl.pallas_call(
        prepare_ff_kernel,
        grid_spec=pltpu.PrefetchScalarGridSpec(
            num_scalar_prefetch=1,
            grid=(1,),
            in_specs=[ANYWHERE, ANYWHERE, ANYWHERE, pl.BlockSpec((B, 1), lambda i, p: (0, 0))],
            out_specs=[pl.BlockSpec((FFL, B), lambda i, p: (0, 0))] * 3,
            scratch_shapes=[
                pltpu.VMEM((B, FF), BF16),
                pltpu.VMEM((FF, B), F32),
                pltpu.VMEM((4 * PIECE, D // 2), BF16),
                pltpu.SemaphoreType.DMA((2,)),
            ],
        ),
        out_shape=[shaped(FFL, B)] * 3,
        compiler_params=params("arbitrary"),
        cost_estimate=cost(0, 6),
        name="prepare_ff",
    )(place, w_gate, w_up, w_down, gain)


def project_qkv_kernel(*refs):
    place, x_refs, w_refs = refs[0], refs[1:6], refs[6:11]
    query_ref, kv_ref, scale_ref, cosine_ref, sine_ref, w_out, rows, weights, sems = refs[11:]
    step = pl.program_id(0)
    tokens = put_tokens(x_refs, rows, sems, 0)
    columns = put_columns(place, w_refs, weights, sems, 10)
    back = pltpu.make_async_copy(weights, w_out, sems.at[26])

    @pl.when(step == 0)
    def _():
        for copy in columns + tokens:
            copy.start()
        for copy in columns:
            copy.wait()
        back.start()
        for copy in tokens:
            copy.wait()

    at = pl.ds(pl.multiple_of(step * TILE, TILE), TILE)
    tile = rows[at, :D]
    wide = tile.astype(F32)
    scale = lax.rsqrt(jnp.mean(wide * wide, axis=-1, keepdims=True) + eps)
    scale_ref[...] = scale
    pre = times_transposed(tile, weights[...]) * scale
    tables = rows[at, D:].astype(F32)
    tables = tables + pltpu.roll(tables, B - HD // 2, 1)
    cosine = jnp.concatenate([tables[:, : HD // 2]] * 4, axis=1)
    sine = jnp.concatenate([tables[:, HD : HD + HD // 2]] * 4, axis=1)
    cosine_ref[...] = cosine
    sine_ref[...] = sine
    for i in range(2):
        part = pre[:, i * 2 * HD : (i + 1) * 2 * HD]
        part = (part * cosine + turned(part) * sine).astype(BF16) * HD ** (-0.5)
        query_ref[0, 2 * i] = part[:, :HD]
        query_ref[0, 2 * i + 1] = part[:, HD:]
    part = pre[:, HEADS * HD :]
    lane = lax.broadcasted_iota(jnp.int32, part.shape, 1)
    kv_ref[0] = jnp.where(lane < HD, part * cosine + turned(part) * sine, part).astype(BF16)

    @pl.when(step == 3)
    def _():
        back.wait()


def project_qkv(place, x_pieces, w_pieces):
    tile = lambda lanes: pl.BlockSpec((TILE, lanes), lambda i, p: (i, 0))
    return pl.pallas_call(
        project_qkv_kernel,
        grid_spec=pltpu.PrefetchScalarGridSpec(
            num_scalar_prefetch=1,
            grid=(4,),
            in_specs=[ANYWHERE] * 10,
            out_specs=[
                pl.BlockSpec((1, HEADS, TILE, HD), lambda i, p: (i // 2, 0, i % 2, 0)),
                pl.BlockSpec((1, TILE, 2 * HD), lambda i, p: (i // 2, i % 2, 0)),
                tile(1), tile(2 * HD), tile(2 * HD),
                ANYWHERE,
            ],
            scratch_shapes=[
                pltpu.VMEM((2 * HALF, WIDE), BF16),
                pltpu.VMEM((QKV, D), BF16),
                pltpu.SemaphoreType.DMA((27,)),
            ],
        ),
        out_shape=[
            shaped(2, HEADS, HALF, HD), shaped(2, HALF, 2 * HD), shaped(2 * HALF, 1, kind=F32),
            shaped(2 * HALF, 2 * HD, kind=F32), shaped(2 * HALF, 2 * HD, kind=F32), shaped(QKV, D),
        ],
        compiler_params=params("arbitrary"),
        cost_estimate=cost(2 * 2 * HALF * QKV * D, 8),
        name="project_qkv",
    )(place, *x_pieces, *w_pieces)


def project_kernel(left_ref, weight_ref, *parts):
    put_parts(pl.program_id(0), matmul(left_ref[...], weight_ref[...]).astype(BF16), parts)


def project(left, weight):
    depth = left.shape[1]
    return pl.pallas_call(
        project_kernel,
        grid=(4,),
        in_specs=[pl.BlockSpec((TILE, depth), lambda i: (i, 0)), pl.BlockSpec((depth, D), lambda i: (0, 0))],
        out_specs=part_specs(2),
        out_shape=PART_SHAPES,
        compiler_params=params("arbitrary"),
        cost_estimate=cost(2 * 2 * HALF * depth * D, 8),
        name="project",
    )(left, weight)


def put_term(left, rows, term_ref):
    def one(i, carry):
        term = matmul(left, rows[:, pl.ds(pl.multiple_of(i * 4 * B, 4 * B), 4 * B)]).astype(BF16)
        for j in range(2):
            zx = 2 * i + j
            term_ref[zx % 4, zx // 4, 0] = term[:, 2 * j * B : (2 * j + 1) * B]
            term_ref[zx % 4, zx // 4, 1] = term[:, (2 * j + 1) * B : (2 * j + 2) * B]
        return carry

    lax.fori_loop(0, 4, one, 0)


def qkv_back_kernel(*refs):
    x_refs, grad_q, own, later, cosine_ref, sine_ref, scale_ref = refs[1:6], *refs[6:12]
    grad_ref, term_ref, rows, left, sems = refs[12:]
    copies = put_tokens(x_refs, rows, sems, 0)
    for copy in copies:
        copy.start()
    for step in range(4):
        at, s = slice(step * TILE, (step + 1) * TILE), step // 2
        inner = slice(step % 2 * TILE, (step % 2 + 1) * TILE)
        cosine, sine = cosine_ref[at], sine_ref[at]
        pieces = []
        for i in range(2):
            part = grad_q[s, inner, i * 2 * HD : (i + 1) * 2 * HD]
            pieces.append(part * cosine - turned(part * sine))
        lane = lax.broadcasted_iota(jnp.int32, cosine.shape, 1)
        part = own[s, inner] + later[s, inner].astype(F32)
        pieces.append(jnp.where(lane < HD, part * cosine - turned(part * sine), part))
        grad_pre = jnp.concatenate(pieces, axis=1)
        grad_ref[at] = grad_pre.astype(BF16)
        left[:, at] = (grad_pre * scale_ref[at]).T.astype(BF16)
    for copy in copies:
        copy.wait()
    put_term(left[...], rows, term_ref)


def qkv_back(place, x_pieces, grad_query, own, later, cosine, sine, scale):
    whole = lambda *shape: pl.BlockSpec(shape, lambda i, p: (0,) * len(shape))
    tokens = 2 * HALF
    return pl.pallas_call(
        qkv_back_kernel,
        grid_spec=pltpu.PrefetchScalarGridSpec(
            num_scalar_prefetch=1,
            grid=(1,),
            in_specs=[ANYWHERE] * 5
            + [
                whole(2, HALF, HEADS * HD), whole(2, HALF, 2 * HD), whole(2, HALF, 2 * HD),
                whole(tokens, 2 * HD), whole(tokens, 2 * HD), whole(tokens, 1),
            ],
            out_specs=[whole(tokens, QKV), whole(4, 2, 2, QKV, B)],
            scratch_shapes=[
                pltpu.VMEM((tokens, D), BF16), pltpu.VMEM((QKV, tokens), BF16), pltpu.SemaphoreType.DMA((10,)),
            ],
        ),
        out_shape=[shaped(tokens, QKV), shaped(4, 2, 2, QKV, B)],
        compiler_params=params("arbitrary"),
        cost_estimate=cost(2 * tokens * QKV * D, 9),
        name="qkv_back",
    )(place, *x_pieces, grad_query, own, later, cosine, sine, scale)


def attention_term_kernel(*refs):
    token_refs, left_ref = refs[1:6], refs[6]
    term_ref, rows, sems = refs[-3:]
    copies = put_tokens(token_refs, rows, sems, 0)
    for copy in copies:
        copy.start()
    left = left_ref[...]
    if left.shape[0] == 2 * HALF:
        left = left.T
    for copy in copies:
        copy.wait()
    put_term(left, rows, term_ref)


def attention_terms(place, pieces, left, name):
    whole = lambda *shape: pl.BlockSpec(shape, lambda i, p: (0,) * len(shape))
    rows = min(left.shape)
    return pl.pallas_call(
        attention_term_kernel,
        grid_spec=pltpu.PrefetchScalarGridSpec(
            num_scalar_prefetch=1,
            grid=(1,),
            in_specs=[ANYWHERE] * 5 + [whole(*left.shape)],
            out_specs=whole(4, 2, 2, rows, B),
            scratch_shapes=[pltpu.VMEM((2 * HALF, D), BF16), pltpu.SemaphoreType.DMA((10,))],
        ),
        out_shape=shaped(4, 2, 2, rows, B),
        compiler_params=params("arbitrary"),
        cost_estimate=cost(2 * 2 * HALF * rows * D, 7),
        name=name,
    )(place, *pieces, left)


def token_places(at, y, core):
    step = 1 - 2 * core
    block = jnp.where(
        at < B, y, jnp.where(at < 2 * B, y + 4 - step, jnp.where(at < 3 * B, y + 4 + step, y + 2))
    )
    row = at % B
    row = jnp.where(at < 3 * B, row, (row + core * (B // 2)) % B)
    return (block % 4) * B + row


def set_bias(place_ref, bias_ref):
    zlo, y, core = place_ref[0], place_ref[1], place_ref[2]
    key_at = token_places(lax.broadcasted_iota(jnp.int32, (HALF, 1), 0), y, core)
    query_at = token_places(lax.broadcasted_iota(jnp.int32, (1, HALF), 1), y, core)
    bias_ref[:HALF, :] = jnp.broadcast_to(jnp.where(zlo == 1, 0.0, -1e30), (HALF, HALF))
    bias_ref[HALF:, :] = jnp.where(key_at <= query_at, 0.0, -1e30)


def attention_kernel(place_ref, *refs):
    w_refs, query_ref, kv_ref, mixed_ref, log_ref = refs[:5], *refs[5:9]
    parts, w_out, bias_ref, weight, sems = refs[9:14], *refs[14:]
    columns = put_columns(place_ref, w_refs, weight, sems, 0)
    back = pltpu.make_async_copy(weight, w_out, sems.at[16])

    @pl.when(pl.program_id(0) == 0)
    def _():
        for copy in columns:
            copy.start()
        set_bias(place_ref, bias_ref)
        for copy in columns:
            copy.wait()
        back.start()

    key, value = kv_ref[0, :, :HD], kv_ref[0, :, HD:]
    for head in range(HEADS):
        scores = times_transposed(key, query_ref[0, head]) + bias_ref[...]
        top = jnp.max(scores, axis=0, keepdims=True)
        weights = jnp.exp(scores - top)
        total = jnp.sum(weights, axis=0, keepdims=True)
        low = (weights * (1.0 / total)).astype(BF16)
        mixed_ref[0, :, head * HD : (head + 1) * HD] = outer_sum(value, low).T.astype(BF16)
        log_ref[0, head] = top + jnp.log(total)
    put_rows(matmul(mixed_ref[0], weight[...]).astype(BF16), parts)

    @pl.when(pl.program_id(0) == 1)
    def _():
        back.wait()


def attention_back_kernel(place_ref, *refs):
    grad_refs, query_ref, kv_ref, log_ref, weight_ref = refs[:5], *refs[5:9]
    grad_query_ref, earlier_ref, own_ref, bias_ref, rows, sems = refs[9:]
    step = pl.program_id(0)
    copies = put_tokens(grad_refs, rows, sems, 0)

    @pl.when(step == 0)
    def _():
        for copy in copies:
            copy.start()
        set_bias(place_ref, bias_ref)
        for copy in copies:
            copy.wait()

    hidden = rows[pl.ds(pl.multiple_of(step * HALF, HALF), HALF), :]
    grads = times_transposed(hidden, weight_ref[...]).astype(BF16)
    key, value = kv_ref[0, :, :HD], kv_ref[0, :, HD:]
    grad_key = jnp.zeros((2 * HALF, HD), F32)
    grad_value = jnp.zeros((2 * HALF, HD), F32)
    for head in range(HEADS):
        lanes = slice(head * HD, (head + 1) * HD)
        query, grad = query_ref[0, head], grads[:, lanes]
        weights = jnp.exp(times_transposed(key, query) + bias_ref[...] - log_ref[0, head])
        grad_weights = times_transposed(value, grad)
        delta = jnp.sum(weights * grad_weights, axis=0, keepdims=True)
        grad_scores = (weights * (grad_weights - delta)).astype(BF16)
        grad_query_ref[0, :, lanes] = outer_sum(key, grad_scores).T * HD ** (-0.5)
        grad_key += matmul(grad_scores, query)
        grad_value += matmul(weights.astype(BF16), grad)
    total = jnp.concatenate([grad_key, grad_value], axis=1)
    earlier_ref[0] = total[:HALF].astype(BF16)
    own_ref[0] = total[HALF:]


def sequence_block(*tail):
    return pl.BlockSpec((1,) + tail, lambda s, place: (s,) + (0,) * len(tail))


def attention_call(kernel, in_specs, out_specs, out_shape, scratch, flops, name):
    return pl.pallas_call(
        kernel,
        grid_spec=pltpu.PrefetchScalarGridSpec(
            num_scalar_prefetch=1,
            grid=(2,),
            in_specs=in_specs,
            out_specs=out_specs,
            scratch_shapes=[pltpu.VMEM((2 * HALF, HALF), F32)] + scratch,
        ),
        out_shape=out_shape,
        compiler_params=params("arbitrary"),
        cost_estimate=cost(flops * 8 * 2 * HALF * HALF * HD * 2, 8),
        name=name,
    )


def attention(place, w_pieces, query, kv):
    return attention_call(
        attention_kernel,
        [ANYWHERE] * 5 + [sequence_block(HEADS, HALF, HD), sequence_block(2 * HALF, 2 * HD)],
        [sequence_block(HALF, HEADS * HD), sequence_block(HEADS, 1, HALF)]
        + part_specs(1)
        + [ANYWHERE],
        [shaped(2, HALF, HEADS * HD), shaped(2, HEADS, 1, HALF, kind=F32)] + PART_SHAPES + [shaped(HEADS * HD, D)],
        [pltpu.VMEM((HEADS * HD, D), BF16), pltpu.SemaphoreType.DMA((17,))],
        3,
        "attention",
    )(place, *w_pieces, query, kv)


def attention_back(place, grad_pieces, query, kv, log_total, weight):
    return attention_call(
        attention_back_kernel,
        [ANYWHERE] * 5
        + [
            sequence_block(HEADS, HALF, HD), sequence_block(2 * HALF, 2 * HD),
            sequence_block(HEADS, 1, HALF), pl.BlockSpec((HEADS * HD, D), lambda s, place: (0, 0)),
        ],
        [sequence_block(HALF, HEADS * HD), sequence_block(HALF, 2 * HD), sequence_block(HALF, 2 * HD)],
        [
            shaped(2, HALF, HEADS * HD, kind=F32),
            shaped(2, HALF, 2 * HD),
            shaped(2, HALF, 2 * HD, kind=F32),
        ],
        [pltpu.VMEM((2 * HALF, D), BF16), pltpu.SemaphoreType.DMA((10,))],
        6,
        "attention_back",
    )(place, *grad_pieces, query, kv, log_total, weight)


def finish_attention_kernel(place, *refs):
    piece_refs, w_query, w_key, w_value, gain_ref = refs[:4], *refs[4:8]
    query_out, key_out, value_out, gain_out, rows = refs[8:]
    for ref, by in zip(piece_refs, range(4)):
        at_y = (place[1] + by) % 4
        for c in range(2):
            piece = ref[c].astype(F32)
            rows[pl.ds(pl.multiple_of((2 * at_y + c) * HEADS * HD, HEADS * HD), HEADS * HD)] = piece[: HEADS * HD]
        both = ref[0].astype(F32) + ref[1].astype(F32)
        at = pl.multiple_of(H * HD + at_y * HD, HD)
        rows[pl.ds(at, HD)] = both[HEADS * HD : (HEADS + 1) * HD]
        rows[pl.ds(at + KV * HD, HD)] = both[(HEADS + 1) * HD :]
    gain = gain_ref[...]
    total = jnp.zeros((B, 1), F32)
    row = 0
    for weight, out in ((w_query, query_out), (w_key, key_out), (w_value, value_out)):
        for i in range(out.shape[1] // B):
            lanes = slice(i * B, (i + 1) * B)
            block = rows[row : row + B].T
            total = total + jnp.sum(block * weight[:, lanes].astype(F32), axis=1, keepdims=True)
            out[:, lanes] = block * gain
            row += B
    gain_out[...] = total


def finish_attention(place, pieces, w_query, w_key, w_value, gain):
    whole = lambda *shape: pl.BlockSpec(shape, lambda i, p: (0,) * len(shape))
    kv = KV * HD
    return pl.pallas_call(
        finish_attention_kernel,
        grid_spec=pltpu.PrefetchScalarGridSpec(
            num_scalar_prefetch=1,
            grid=(1,),
            in_specs=[whole(2, QKV, B)] * 4 + [whole(B, D), whole(B, kv), whole(B, kv), whole(B, 1)],
            out_specs=[whole(B, D), whole(B, kv), whole(B, kv), whole(B, 1)],
            scratch_shapes=[pltpu.VMEM((D + 2 * kv, B), F32)],
        ),
        out_shape=[
            shaped(B, D, kind=F32), shaped(B, kv, kind=F32), shaped(B, kv, kind=F32), shaped(B, 1, kind=F32),
        ],
        compiler_params=params("arbitrary"),
        cost_estimate=cost(0, 4),
        name="finish_attention",
    )(place, *pieces, w_query, w_key, w_value, gain)


def finish_output_kernel(blocks, out):
    for i in range(16):
        out[:, i * B : (i + 1) * B] = blocks[i].astype(F32)


def finish_output(blocks):
    return pl.pallas_call(
        finish_output_kernel,
        out_shape=shaped(B, D, kind=F32),
        compiler_params=params(),
        cost_estimate=cost(0, 2),
        name="finish_output",
    )(blocks)


def feed_forward_kernel(*refs):
    place, token_refs, grad_refs, ff_ref = refs[0], refs[1:6], refs[6:11], refs[11]
    act_ref, act_t, gate_t, up_t = refs[12:16]
    parts, down_out = refs[16:21], refs[21]
    rows_h, rows_g, gate_up, down, slabs, sems = refs[22:]
    step = pl.program_id(0)
    tokens = put_tokens(token_refs, rows_h, sems, 0)
    grads = put_tokens(grad_refs, rows_g, sems, 10)
    weights, loads = [], []
    for x in range(4):
        for by in range(4):
            z = (2 * place[4] + place[0] + by) % 4
            zhi, zlo = z // 2, z % 2
            for core in range(2):
                weights.append(
                    pltpu.make_async_copy(
                        ff_ref.at[x, by, pl.ds(core * FFL, FFL)],
                        gate_up.at[zlo, :, lane_block(zhi, x, core)],
                        sems.at[20 + len(weights)],
                    )
                )
            loads.append(
                pltpu.make_async_copy(
                    ff_ref.at[x, by, pl.ds(2 * FFL, FFL)], slabs.at[zlo, zhi * 4 + x], sems.at[52 + len(loads)]
                )
            )
    back = pltpu.make_async_copy(down, down_out, sems.at[68])

    @pl.when(step == 0)
    def _():
        for copy in tokens + weights + loads + grads:
            copy.start()
        for copy in tokens + weights:
            copy.wait()

    rows = pl.ds(pl.multiple_of(step * HALF, HALF), HALF)
    normed = rows_h[rows, :]
    gate_pre = times_transposed(normed, gate_up[0])
    upward = times_transposed(normed, gate_up[1])

    @pl.when(step == 0)
    def _():
        for copy in loads:
            copy.wait()

        def put(q, carry):
            for half in range(2):
                for p in range(4):
                    one = slabs[half, 2 * q, 2 * p * PIECE : 2 * (p + 1) * PIECE, :].astype(F32)
                    two = slabs[half, 2 * q + 1, 2 * p * PIECE : 2 * (p + 1) * PIECE, :].astype(F32)
                    lane = (half * 8 + 2 * p) * B
                    rows = pl.ds(pl.multiple_of(q * 2 * PIECE, 16), 2 * PIECE)
                    down[rows, lane : lane + B] = jnp.concatenate([one[:PIECE], two[:PIECE]], axis=0).astype(BF16)
                    down[rows, lane + B : lane + 2 * B] = jnp.concatenate(
                        [one[PIECE:], two[PIECE:]], axis=0
                    ).astype(BF16)
            return carry

        lax.fori_loop(0, 4, put, 0)
        back.start()
        for copy in grads:
            copy.wait()

    grad_act = times_transposed(rows_g[rows, :], down[...])
    sigmoid = 1.0 / (1.0 + jnp.exp(-gate_pre))
    silu = gate_pre * sigmoid
    activation = silu * upward
    grad_up = grad_act * silu
    grad_gate = grad_act * upward * (sigmoid * (1.0 + gate_pre * (1.0 - sigmoid)))
    part = matmul(grad_gate.astype(BF16), gate_up[0]) + matmul(grad_up.astype(BF16), gate_up[1])
    put_rows(part.astype(BF16), parts)
    act_ref[...] = activation.astype(BF16)
    act_t[...] = activation.T.astype(BF16)
    gate_t[...] = grad_gate.T.astype(BF16)
    up_t[...] = grad_up.T.astype(BF16)

    @pl.when(step == 1)
    def _():
        back.wait()


def feed_forward(place, tokens, grads, ff_all):
    turned_spec = pl.BlockSpec((FFL, HALF), lambda i, p: (0, i))
    turned_shape = shaped(FFL, 2 * HALF)
    return pl.pallas_call(
        feed_forward_kernel,
        grid_spec=pltpu.PrefetchScalarGridSpec(
            num_scalar_prefetch=1,
            grid=(2,),
            in_specs=[ANYWHERE] * 11,
            out_specs=[pl.BlockSpec((HALF, FFL), lambda i, p: (i, 0))]
            + [turned_spec] * 3
            + part_specs(1)
            + [ANYWHERE],
            scratch_shapes=[
                pltpu.VMEM((2 * HALF, D), BF16),
                pltpu.VMEM((2 * HALF, D), BF16),
                pltpu.VMEM((2, FFL, D), BF16),
                pltpu.VMEM((FFL, D), BF16),
                pltpu.VMEM((2, 8, FFL, B), BF16),
                pltpu.SemaphoreType.DMA((69,)),
            ],
        ),
        out_shape=[shaped(2 * HALF, FFL)] + [turned_shape] * 3 + PART_SHAPES + [shaped(FFL, D)],
        compiler_params=params("arbitrary"),
        cost_estimate=cost(2 * 5 * 2 * HALF * FFL * D, 32),
        name="feed_forward",
    )(place, *tokens, *grads, ff_all)


def along_z(place, zhi, zlo):
    return (2 * zhi + zlo + 4 - 2 * place[4] - place[0]) % 4


def load_tokens(step, refs, rows, sems):
    copies = put_tokens(refs, rows, sems, 0)

    @pl.when(step == 0)
    def _():
        for copy in copies:
            copy.start()
        for copy in copies:
            copy.wait()


def gate_up_kernel(*refs):
    place, token_refs, gate_t, up_t, out_ref, rows, terms, sems = refs[0], refs[1:6], *refs[6:]
    step = pl.program_id(0)
    load_tokens(step, token_refs, rows, sems)
    normed = rows[:, pl.ds(pl.multiple_of(step * 4 * B, 4 * B), 4 * B)]

    def out(i, matrix):
        xs, by = pl.ds(i % 2 * 2, 2), along_z(place, i // 2, matrix)
        return pltpu.make_async_copy(terms.at[xs, by], out_ref.at[xs, by], sems.at[10 + 2 * i + matrix])

    for matrix, left in ((0, gate_t), (1, up_t)):
        term = matmul(left[...], normed).astype(BF16)
        by = along_z(place, step // 2, matrix)
        for j in range(2):
            terms[step % 2 * 2 + j, by, 0:FFL, :] = term[:, 2 * j * B : (2 * j + 1) * B]
            terms[step % 2 * 2 + j, by, FFL:, :] = term[:, (2 * j + 1) * B : (2 * j + 2) * B]
        out(step, matrix).start()

    @pl.when(step == 3)
    def _():
        for i in range(4):
            for matrix in range(2):
                out(i, matrix).wait()


def down_kernel(*refs):
    place, grad_refs, act_t, out_ref, rows, terms, sems = refs[0], refs[1:6], *refs[6:]
    step = pl.program_id(0)
    load_tokens(step, grad_refs, rows, sems)
    term = matmul(act_t[...], rows[:, pl.ds(pl.multiple_of(step * 4 * B, 4 * B), 4 * B)])
    for j in range(2):
        p = (2 * step + j) % 4
        at = pl.ds(pl.multiple_of(p * 2 * PIECE, 16), 2 * PIECE)
        for zx in range(8):
            slab = term[zx * PIECE : (zx + 1) * PIECE]
            low, high = slab[:, 2 * j * B : (2 * j + 1) * B], slab[:, (2 * j + 1) * B : (2 * j + 2) * B]
            by = along_z(place, zx // 4, step // 2)
            terms[zx % 4, by, at, :] = jnp.concatenate([low, high], axis=0).astype(BF16)

    def out(half, zhi):
        by = along_z(place, zhi, half)
        return pltpu.make_async_copy(terms.at[:, by], out_ref.at[:, by], sems.at[10 + 2 * half + zhi])

    @pl.when(step % 2 == 1)
    def _():
        for zhi in range(2):
            out(step // 2, zhi).start()

    @pl.when(step == 3)
    def _():
        for half in range(2):
            for zhi in range(2):
                out(half, zhi).wait()


def ff_terms(kernel, place, pieces, lefts, rows, name):
    whole = pl.BlockSpec((FFL, 2 * HALF), lambda i, p: (0, 0))
    return pl.pallas_call(
        kernel,
        grid_spec=pltpu.PrefetchScalarGridSpec(
            num_scalar_prefetch=1,
            grid=(4,),
            in_specs=[ANYWHERE] * 5 + [whole] * len(lefts),
            out_specs=ANYWHERE,
            scratch_shapes=[
                pltpu.VMEM((2 * HALF, D), BF16),
                pltpu.VMEM((4, 4, rows, B), BF16),
                pltpu.SemaphoreType.DMA((18,)),
            ],
        ),
        out_shape=shaped(4, 4, rows, B),
        compiler_params=params("arbitrary"),
        cost_estimate=cost(2 * len(lefts) * 2 * HALF * FFL * D, 8 + 4 * len(lefts)),
        name=name,
    )(place, *pieces, *lefts)


def finish_hidden_kernel(*refs):
    place, piece_refs, weight_ref, gain_ref, out_ref, gain_out, rows = refs[0], refs[1:5], *refs[5:]
    for ref, by in zip(piece_refs, range(4)):
        at_y = (place[1] + by) % 4
        for core in range(2):
            slab = ref[0, core].astype(F32)
            for zx in range(8):
                at = pl.multiple_of((2 * zx + core) * 4 * PIECE + at_y * PIECE, 8)
                rows[pl.ds(at, PIECE)] = slab[zx * PIECE : (zx + 1) * PIECE]
    gain = gain_ref[...]
    total = jnp.zeros((B, 1), F32)
    for i in range(FF // B):
        lanes = slice(i * B, (i + 1) * B)
        block = rows[lanes].T
        total = total + jnp.sum(block * weight_ref[:, lanes].astype(F32), axis=1, keepdims=True)
        out_ref[:, lanes] = block * gain
    gain_out[...] = total


def finish_hidden(place, pieces, matrix, weight, gain):
    own, after, low, high, before = pieces
    at = lambda m: pl.BlockSpec((1, 2, FFL, B), lambda i, p: (m, 0, 0, 0))
    whole = lambda *shape: pl.BlockSpec(shape, lambda i, p: (0,) * len(shape))
    return pl.pallas_call(
        finish_hidden_kernel,
        grid_spec=pltpu.PrefetchScalarGridSpec(
            num_scalar_prefetch=1,
            grid=(1,),
            in_specs=[at(matrix), at(matrix), at(0), at(matrix), whole(B, FF), whole(B, 1)],
            out_specs=[whole(B, FF), whole(B, 1)],
            scratch_shapes=[pltpu.VMEM((FF, B), F32)],
        ),
        out_shape=[shaped(B, FF, kind=F32), shaped(B, 1, kind=F32)],
        compiler_params=params("arbitrary"),
        cost_estimate=cost(3 * 10**9, 6),
        name="finish_hidden",
    )(place, own, after, (low, high)[matrix], before, weight, gain)


def finish_down_kernel(place, own, after, low, high, before, out_ref):
    for refs, by in (((own, own), 0), ((after, after), 1), ((low, high), 2), ((before, before), 3)):
        rows = pl.ds(pl.multiple_of((place[1] + by) % 4 * PIECE, 8), PIECE)
        for half in range(2):
            slab = refs[half][half if by != 2 else 0].astype(F32)
            for t in range(8):
                lane = (half * 8 + t) * B
                out_ref[rows, lane : lane + B] = slab[t * PIECE : (t + 1) * PIECE]


def finish_down(place, pieces):
    halves = lambda n: pl.BlockSpec((n, FFL, B), lambda i, p: (0, 0, 0))
    return pl.pallas_call(
        finish_down_kernel,
        grid_spec=pltpu.PrefetchScalarGridSpec(
            num_scalar_prefetch=1,
            grid=(1,),
            in_specs=[halves(2), halves(2), halves(1), halves(1), halves(2)],
            out_specs=pl.BlockSpec((4 * PIECE, D), lambda i, p: (0, 0)),
        ),
        out_shape=shaped(4 * PIECE, D, kind=F32),
        compiler_params=params("arbitrary"),
        cost_estimate=cost(2 * 10**9, 5),
        name="finish_down",
    )(place, *pieces)


def own_rows(rows_all, y, core, per):
    return lax.dynamic_slice_in_dim(rows_all, (2 * y + core) * per, per, 0)


def resumed(steps, arrived):
    try:
        while True:
            arrived = yield steps.send(arrived)
    except StopIteration as end:
        return end.value


class Flow:
    def __init__(self, steps):
        self.steps, self.result, self.sent = steps, None, None
        self.move(None)

    def move(self, arrived):
        try:
            self.sent = self.steps.send(arrived)
        except StopIteration as end:
            self.sent, self.result = (), end.value


def stage(flows, *values):
    flows = [flow for flow in flows if flow.result is None]
    sizes = [len(flow.sent) for flow in flows]
    leaves, tree = jax.tree.flatten(values)
    tied = tie(*[v for flow in flows for v in flow.sent], *leaves)
    for flow, size in zip(flows, sizes):
        flow.move(tied[:size])
        tied = tied[size:]
    return jax.tree.unflatten(tree, tied)


def gather_steps(block):
    (other,) = yield (swap_core(block),)
    pair = jnp.stack([block, other])
    (got,) = yield (along_y(pair),)
    far, swapped = yield (along_y(send_half(got)), swap_core(got))
    (far_swapped,) = yield (swap_core(far),)
    return pair, got, swapped, far, far_swapped


def scatter_steps(parts):
    core = lax.axis_index("core")
    first, behind, ahead, far, far_other = parts
    (far_got,) = yield (swap_core(far_other),)
    far = add(far, far_got).astype(BF16)
    low, behind_got, first_got = yield (along_y(far), swap_core(behind), swap_core(first[1]))
    ahead = add(ahead, behind_got).astype(BF16)
    mine = add(lax.dynamic_slice_in_dim(ahead, core * (B // 2), B // 2, 1), low).astype(BF16)
    ahead = lax.dynamic_update_slice_in_dim(ahead, mine, core * (B // 2), 1)
    (got,) = yield (along_y(ahead),)
    (last,) = yield (swap_core(got[1]),)
    return add(first[0], first_got) + got[0].astype(F32) + last.astype(F32)


def ring_gather_steps(block, axis):
    half = block.shape[0] // 2
    before, after = yield (shift(block, axis, 1), shift(block, axis, -1))
    low, high = yield (shift(before[:half], axis, 1), shift(after[half:], axis, -1))
    return block, after, low, high, before


def ring_scatter_steps(parts, axis):
    half = parts[2].shape[0] // 2
    low, high = yield (shift(parts[2][:half], axis, 1), shift(parts[2][half:], axis, -1))
    after = jnp.concatenate([add(parts[1][:half], low).astype(BF16), parts[1][half:]], axis=0)
    before = jnp.concatenate([parts[3][:half], add(parts[3][half:], high).astype(BF16)], axis=0)
    from_before, from_after = yield (shift(after, axis, 1), shift(before, axis, -1))
    return add(parts[0], from_before) + from_after.astype(F32)


def on_device(
    layer_input,
    positions,
    attn_gain,
    w_query,
    w_key,
    w_value,
    w_output,
    mlp_gain,
    w_gate,
    w_up,
    w_down,
    out_grad,
):
    zlo, y, zhi, x, core = (lax.axis_index(axis) for axis in AXES)
    place = jnp.stack([zlo, y, core, x, zhi]).astype(jnp.int32)

    def by_core(mine, got):
        return jnp.where(core == 0, jnp.stack([mine, got]), jnp.stack([got, mine]))

    def by_zlo(mine, got):
        return jnp.where(zlo == 0, jnp.stack([mine, got]), jnp.stack([got, mine]))

    def by_zhi(mine, got):
        return jnp.where(zhi == 0, jnp.stack([mine, got]), jnp.stack([got, mine]))

    def trio(mine, other, axis):
        across = lax.ppermute(other, (axis, "core"), [(i, 3 - i) for i in range(4)])
        return shift(mine, axis, 1), swap_core(other), across

    def column_steps(mine, got):
        pair = by_core(mine, got)
        (got,) = yield (shift(pair, "zhi", 1),)
        return (yield from ring_gather_steps(by_zhi(pair, got), "x"))

    def output_steps(mine, other):
        there, here, across = yield trio(mine, other, "zhi")
        column = by_zhi(by_core(mine, here), by_core(there, across))
        return (yield from ring_gather_steps(column, "x"))

    def hidden_steps(mine, got, down):
        piece = jnp.concatenate([by_core(mine, got).reshape(2 * FFL, B), down], axis=0)
        pieces = yield from ring_gather_steps(piece, "z")
        return jnp.concatenate(pieces, axis=0).reshape(4, 3 * FFL, B)

    def of_core(pair, other=False):
        return lax.dynamic_index_in_dim(pair, 1 - core if other else core, 0, keepdims=False)

    def whole_ring(pieces):
        own, after, low, high, before = pieces
        return own, after, jnp.concatenate([low, high], axis=0), before

    def attention_steps(column):
        keep = lax.dynamic_index_in_dim(column, zhi, 0, keepdims=False)
        send = lax.dynamic_index_in_dim(column, 1 - zhi, 0, keepdims=False)
        (got,) = yield (shift(send, "zhi", 1),)
        pair = add(keep, got).astype(BF16)
        mine, other = of_core(pair), of_core(pair, True)
        there, here, across = yield trio(mine, other, "zlo")
        own = by_core(add(mine, there), add(here, across)).astype(BF16)
        return (yield from ring_gather_steps(own, "y"))

    def gate_up_steps(sums):
        own = yield from ring_scatter_steps([sums[i] for i in range(4)], "z")
        pair = own.astype(BF16).reshape(2, FFL, B)
        mine, other = of_core(pair), of_core(pair, True)
        there, here, across = yield trio(mine, other, "zlo")
        block = by_zlo(by_core(mine, here), by_core(there, across))
        before, after = yield (shift(block, "y", 1), shift(block, "y", -1))
        low, high = yield (shift(before[:1], "y", 1), shift(after[1:], "y", -1))
        return block, after, low, high, before

    def down_steps(sums):
        steps = ring_scatter_steps([sums[i] for i in range(4)], "z")
        arrived = yield next(steps)
        yield ()
        own = yield from resumed(steps, arrived)
        own = own.astype(BF16)
        (got,) = yield (shift(own, "zlo", 1),)
        return (yield from ring_gather_steps(by_zlo(own, got), "y"))

    x_low = layer_input[0]
    frequency = theta ** (-jnp.arange(0, HD, 2).astype(F32) / HD)
    angles = positions[0].astype(F32)[:, None] * frequency
    tables = []
    for table in (jnp.cos(angles), jnp.sin(angles)):
        high = lax.reduce_precision(table, 8, 7)
        tables += [high.astype(BF16), (table - high).astype(BF16)]
    tokens = Flow(gather_steps(jnp.concatenate([x_low, *tables], axis=1)))
    grads = Flow(gather_steps(out_grad[0]))
    qkv_mine, qkv_other = prepare_qkv(place, w_query, w_key, w_value, attn_gain[:, None])
    qkv_mine, qkv_got, gain_two, w_out = stage([tokens], qkv_mine, swap_core(qkv_other), mlp_gain[:, None], w_output)

    columns = Flow(column_steps(qkv_mine, qkv_got))
    o_rows = lax.all_to_all(w_out.reshape(B, 16, B).transpose(1, 0, 2), FSDP, 0, 0, tiled=True)
    ff_mine, ff_other, ff_down = prepare_ff(place, w_gate, w_up, w_down, gain_two)
    ff_mine, ff_got, ff_down, x_low, o_rows = stage(
        [tokens, columns], ff_mine, swap_core(ff_other), ff_down, x_low, o_rows
    )

    inputs = x_low.astype(F32)
    scale_one = lax.rsqrt(jnp.mean(inputs * inputs, axis=-1, keepdims=True) + eps)
    o_rows = o_rows.reshape(D, B)
    mine, other = own_rows(o_rows, y, core, HEADS * HD), own_rows(o_rows, y, 1 - core, HEADS * HD)
    scale_one, mine, other, ff_mine, ff_got, ff_down = stage(
        [tokens, columns, grads], scale_one, mine, other, ff_mine, ff_got, ff_down
    )

    outputs = Flow(output_steps(mine, other))
    ff_mine, ff_got, ff_down = stage([tokens, columns, outputs], ff_mine, ff_got, ff_down)

    hidden_rows = Flow(hidden_steps(ff_mine, ff_got, ff_down))
    x_pieces = tokens.result
    query, key_value, scale_all, cosine, sine, qkv_full = project_qkv(place, x_pieces, columns.result)
    query, key_value = stage([hidden_rows, outputs, grads], query, key_value)

    earlier = lax.ppermute(key_value, "zlo", [(0, 1)])
    query, key_value, earlier = stage([outputs, hidden_rows], query, key_value, earlier)
    ff_all = lax.all_gather(hidden_rows.result, "x", axis=0, tiled=False)

    key_value = jnp.concatenate([earlier, key_value], axis=1)
    mixed, log_total, *parts, o_full = attention(place, outputs.result, query, key_value)
    parts = stage([grads], *parts)
    sums = Flow(scatter_steps(parts))
    stage([sums, grads])
    grad_pieces = grads.result
    for _ in range(3):
        stage([sums])
    hidden = inputs + sums.result
    scale_two = lax.rsqrt(jnp.mean(hidden * hidden, axis=-1, keepdims=True) + eps)
    normed = Flow(gather_steps((hidden * scale_two).astype(BF16)))
    for _ in range(4):
        stage([normed])
    normed_pieces = normed.result

    activation, act_t, gate_t, up_t, *parts, down_full = feed_forward(place, normed_pieces, grad_pieces, ff_all)
    sums = Flow(scatter_steps(parts))
    (act_t,) = stage([sums], act_t)
    down_terms = ff_terms(down_kernel, place, grad_pieces, (act_t,), FFL, "down_terms")
    down_terms, gate_t = stage([sums], down_terms, gate_t)
    down_sum = lax.psum_scatter(down_terms, "x", scatter_dimension=0, tiled=True)[0]
    gate_up_terms = ff_terms(gate_up_kernel, place, normed_pieces, (gate_t, up_t), 2 * FFL, "gate_up_terms")
    (gate_up_terms,) = stage([sums], gate_up_terms)
    gate_up_sum = lax.psum_scatter(gate_up_terms, "x", scatter_dimension=0, tiled=True)[0]
    stage([sums])

    grad_normed_two = sums.result
    mean_two = jnp.mean(grad_normed_two * hidden, axis=-1, keepdims=True)
    grad_hidden = (
        out_grad[0].astype(F32)
        + scale_two * grad_normed_two
        - hidden * (scale_two * scale_two * scale_two) * mean_two
    )
    hidden_grads = Flow(gather_steps(grad_hidden.astype(BF16)))
    (activation,) = stage([hidden_grads], activation)
    down_parts = project(activation, down_full)
    *down_parts, down_sum = stage([hidden_grads], *down_parts, down_sum)
    result = Flow(scatter_steps(down_parts))
    down = Flow(down_steps(down_sum))
    stage([hidden_grads, down])
    stage([hidden_grads, result])

    hidden_grad_pieces = hidden_grads.result
    grad_query, grad_earlier, grad_own = attention_back(
        place, hidden_grad_pieces, query, key_value, log_total, o_full
    )
    grad_query, grad_earlier, grad_own, mixed = stage([result, down], grad_query, grad_earlier, grad_own, mixed)

    later = lax.ppermute(grad_earlier, "zlo", [(1, 0)])
    output_terms = attention_terms(
        place, hidden_grad_pieces, mixed.reshape(2 * HALF, HEADS * HD), "output_terms"
    )
    later, grad_query, output_terms, gate_up_sum = stage(
        [down], later, grad_query, output_terms, gate_up_sum
    )

    output_sum = lax.psum_scatter(output_terms, "x", scatter_dimension=0, tiled=True)[0]
    gate_up = Flow(gate_up_steps(gate_up_sum))
    grad_pre, terms = qkv_back(place, x_pieces, grad_query, grad_own, later, cosine, sine, scale_all)
    grad_pre, terms = stage([gate_up, down, result], grad_pre, terms)

    attention_sum = lax.psum_scatter(terms, "x", scatter_dimension=0, tiled=True)[0]
    parts = project(grad_pre, qkv_full)
    *parts, output_sum = stage([gate_up, down, result], *parts, output_sum)

    sums = Flow(scatter_steps(parts))
    output_sums = Flow(attention_steps(output_sum))
    (attention_sum,) = stage([sums, gate_up, output_sums, down], attention_sum)
    attention_sums = Flow(attention_steps(attention_sum))
    stage([output_sums, attention_sums])
    down_grad = finish_down(place, down.result)
    (down_grad,) = stage([output_sums, attention_sums, gate_up], down_grad)
    stage([sums, output_sums, attention_sums, gate_up])

    ring = jnp.roll(jnp.stack(whole_ring(output_sums.result)), y, axis=0).reshape(16, B, B)
    output_grad = lax.all_to_all(ring, FSDP, 0, 0, tiled=True)
    gain_two = mlp_gain[:, None]
    gate_grad, gate_gain = finish_hidden(place, gate_up.result, 0, w_gate, gain_two)
    up_grad, up_gain = finish_hidden(place, gate_up.result, 1, w_up, gain_two)
    gate_grad, up_grad, output_grad = stage([sums, attention_sums], gate_grad, up_grad, output_grad)
    stage([sums])
    grad_normed = sums.result
    mean_one = jnp.mean(grad_normed * inputs, axis=-1, keepdims=True)
    input_grad = (
        grad_hidden
        + scale_one * grad_normed
        - inputs * (scale_one * scale_one * scale_one) * mean_one
    )
    input_grad = input_grad.astype(BF16)
    query_grad, key_grad, value_grad, attn_gain_grad = finish_attention(
        place, whole_ring(attention_sums.result), w_query, w_key, w_value, attn_gain[:, None]
    )
    output_grad = finish_output(output_grad)
    return (
        (hidden + result.result).astype(BF16)[None],
        input_grad[None],
        attn_gain_grad[:, 0],
        query_grad,
        key_grad,
        value_grad,
        output_grad,
        (gate_gain + up_gain)[:, 0],
        gate_grad,
        up_grad,
        down_grad,
    )


def solution(mesh):
    split = Mesh(mesh.devices.reshape(2, 4, 2, 4, 2), AXES)
    tokens = P(FSDP, SEQ, None)
    rows = P(FSDP, None)
    gain = P(FSDP)
    in_specs = (
        tokens, P(FSDP, SEQ), gain, rows, rows, rows, rows, gain, rows, rows, rows, tokens,
    )
    out_specs = (tokens, tokens, gain, rows, rows, rows, rows, gain, rows, rows, rows)
    return jax.shard_map(
        on_device, mesh=split, in_specs=in_specs, out_specs=out_specs, check_vma=False
    )
```

```python
import jax
import jax.numpy as jnp
from jax import lax
from jax.experimental import pallas as pl
from jax.experimental.pallas import tpu as pltpu
from jax.sharding import Mesh
from jax.sharding import PartitionSpec as P

H = 32
KV = 4
HD = 64
D = 2048
FF = 5632
B = 128
HALF = 512
HEADS = 4
FFL = 704
PIECE = 88

eps = 1e-05
theta = 10000.0
F32 = jnp.float32
BF16 = jnp.bfloat16
AXES = ("zlo", "y", "zhi", "x", "core")
FSDP = ("zhi", "x", "core")
SEQ = ("zlo", "y")


def matmul(left, right):
    return jnp.dot(left, right, preferred_element_type=F32)


def times_transposed(left, right):
    return lax.dot_general(left, right, (((1,), (1,)), ((), ())), preferred_element_type=F32)


def outer_sum(left, right):
    return lax.dot_general(left, right, (((0,), (0,)), ((), ())), preferred_element_type=F32)


def shift(value, axis, by):
    if axis == "z":
        at = [2 * (z % 2) + z // 2 for z in range(4)]
        return lax.ppermute(value, ("zlo", "zhi"), [(at[z], at[(z + by) % 4]) for z in range(4)])
    size = lax.axis_size(axis)
    return lax.ppermute(value, axis, [(i, (i + by) % size) for i in range(size)])


def swap_core(value):
    return shift(value, "core", 1)


def small_gather(block, axis):
    return shift(block, axis, -1), shift(block, axis, 2), shift(block, axis, 1)


def tie(*values):
    return lax.optimization_barrier(values)


def add(left, right):
    return left.astype(F32) + right.astype(F32)


def along_y(value):
    pairs = []
    for i in range(4):
        pairs.append((2 * i, 2 * ((i + 1) % 4)))
        pairs.append((2 * i + 1, 2 * ((i + 3) % 4) + 1))
    return lax.ppermute(value, ("y", "core"), pairs)


def send_half(got):
    core = lax.axis_index("core")
    return lax.dynamic_slice_in_dim(got, core * (B // 2), B // 2, 1)


FLIPPED = (0, 0, 1, 0, 1)
LENGTHS = (B, B, B, B // 2, B // 2)


def put_tokens(refs, rows_ref, sems, start):
    lanes = pl.ds(0, rows_ref.shape[1])
    copies = []
    row = 0
    for s in range(2):
        for ref, flip, length in zip(refs, FLIPPED, LENGTHS):
            copies.append(
                pltpu.make_async_copy(
                    ref.at[s ^ flip, :, lanes], rows_ref.at[pl.ds(row, length)], sems.at[start + len(copies)]
                )
            )
            row += length
    return copies


TILE = 256
WIDE = D + B
VMEM_LIMIT = 56 * 2**20
ANYWHERE = pl.BlockSpec(memory_space=pl.ANY)


def params(*kinds):
    return pltpu.CompilerParams(dimension_semantics=kinds or None, vmem_limit_bytes=VMEM_LIMIT)


def cost(flops, megabytes):
    return pl.CostEstimate(flops=flops, bytes_accessed=int(megabytes * 2**20), transcendentals=0)


def shaped(*shape, kind=BF16):
    return jax.ShapeDtypeStruct(shape, kind)


PARTS = ((B, False), (B, True), (B, False), (B // 2, False), (B // 2, True))
PART_SHAPES = [jax.ShapeDtypeStruct((2, n, D), BF16) for n, _ in PARTS]


def part_specs(steps):
    def of(turn):
        return lambda i, *_: (1 - i // steps if turn else i // steps, 0, 0)

    return [pl.BlockSpec((1, n, D), of(turn)) for n, turn in PARTS]


def put_parts(step, tile, refs):
    @pl.when(step % 2 == 0)
    def _():
        refs[0][0] = tile[:B]
        refs[1][0] = tile[B:]

    @pl.when(step % 2 == 1)
    def _():
        refs[2][0] = tile[:B]
        refs[3][0] = tile[B : B + B // 2]
        refs[4][0] = tile[B + B // 2 :]


def put_rows(rows, refs):
    row = 0
    for ref, (length, _) in zip(refs, PARTS):
        ref[0] = rows[row : row + length]
        row += length


def turned(values):
    lane = lax.broadcasted_iota(jnp.int32, values.shape, 1) % HD
    return jnp.where(lane < HD // 2, -pltpu.roll(values, 2 * HD - HD // 2, 1), pltpu.roll(values, HD // 2, 1))


def lane_block(zhi, x, core):
    return pl.ds(pl.multiple_of((zhi * 8 + x * 2 + core) * B, B), B)


def put_columns(place, refs, into, sems, start):
    copies = []
    for ref, by, first in zip(refs, (0, 1, 2, 2, 3), (0, 0, 0, 1, 0)):
        for i in range(ref.shape[0]):
            for core in range(2):
                lanes = lane_block(first + i, (place[3] + by) % 4, core)
                copies.append(
                    pltpu.make_async_copy(ref.at[i, core], into.at[:, lanes], sems.at[start + len(copies)])
                )
    return copies


def prepare_qkv_kernel(place, q_mine, q_other, w_key, w_value, gain, mine_ref, other_ref, k_rows, v_rows):
    scale = gain[...]
    k_rows[...] = (w_key[...].astype(F32) * scale).T
    v_rows[...] = (w_value[...].astype(F32) * scale).T
    rows = pl.ds(pl.multiple_of(place[1] * HD, HD), HD)
    for source, out in ((q_mine, mine_ref), (q_other, other_ref)):
        out[: HEADS * HD] = (source[...].astype(F32) * scale).T.astype(BF16)
        out[HEADS * HD : (HEADS + 1) * HD] = k_rows[rows].astype(BF16)
        out[(HEADS + 1) * HD :] = v_rows[rows].astype(BF16)


QKV = (HEADS + 2) * HD


def prepare_qkv(place, w_query, w_key, w_value, gain):
    whole = lambda *shape: pl.BlockSpec(shape, lambda i, p: (0,) * len(shape))
    return pl.pallas_call(
        prepare_qkv_kernel,
        grid_spec=pltpu.PrefetchScalarGridSpec(
            num_scalar_prefetch=1,
            grid=(1,),
            in_specs=[
                pl.BlockSpec((B, HEADS * HD), lambda i, p: (0, 2 * p[1] + p[2])),
                pl.BlockSpec((B, HEADS * HD), lambda i, p: (0, 2 * p[1] + 1 - p[2])),
                whole(B, KV * HD), whole(B, KV * HD), whole(B, 1),
            ],
            out_specs=[whole(QKV, B), whole(QKV, B)],
            scratch_shapes=[pltpu.VMEM((KV * HD, B), F32), pltpu.VMEM((KV * HD, B), F32)],
        ),
        out_shape=[shaped(QKV, B), shaped(QKV, B)],
        compiler_params=params("arbitrary"),
        cost_estimate=cost(0, 1),
        name="prepare_qkv",
    )(place, w_query, w_query, w_key, w_value, gain)


def prepare_ff_kernel(place, w_gate, w_up, w_down, gain, mine_ref, other_ref, down_ref, picked, rows, down_rows, sems):
    zlo, y, core = place[0], place[1], place[2]
    down = pltpu.make_async_copy(
        w_down.at[:, pl.ds(pl.multiple_of(zlo * (D // 2), D // 2), D // 2)], down_rows, sems.at[1]
    )
    down.start()

    @pl.when(zlo == 0)
    def _():
        copy = pltpu.make_async_copy(w_gate, picked, sems.at[0])
        copy.start()
        copy.wait()

    @pl.when(zlo == 1)
    def _():
        copy = pltpu.make_async_copy(w_up, picked, sems.at[0])
        copy.start()
        copy.wait()

    scale = gain[...]
    for i in range(FF // B):
        rows[i * B : (i + 1) * B] = (picked[:, i * B : (i + 1) * B].astype(F32) * scale).T
    for which, out in ((core, mine_ref), (1 - core, other_ref)):
        slabs = []
        for zx in range(8):
            at = pl.multiple_of(zx * 2 * 4 * PIECE + which * 4 * PIECE + y * PIECE, 8)
            slabs.append(rows[pl.ds(at, PIECE)])
        out[...] = jnp.concatenate(slabs, axis=0).astype(BF16)
    down.wait()
    for t in range(8):
        rows[t * 4 * PIECE : (t + 1) * 4 * PIECE] = down_rows[:, t * B : (t + 1) * B].astype(F32)
    slabs = [rows[pl.ds(pl.multiple_of(t * 4 * PIECE + y * PIECE, 8), PIECE)] for t in range(8)]
    down_ref[...] = jnp.concatenate(slabs, axis=0).astype(BF16)


def prepare_ff(place, w_gate, w_up, w_down, gain):
    return pl.pallas_call(
        prepare_ff_kernel,
        grid_spec=pltpu.PrefetchScalarGridSpec(
            num_scalar_prefetch=1,
            grid=(1,),
            in_specs=[ANYWHERE, ANYWHERE, ANYWHERE, pl.BlockSpec((B, 1), lambda i, p: (0, 0))],
            out_specs=[pl.BlockSpec((FFL, B), lambda i, p: (0, 0))] * 3,
            scratch_shapes=[
                pltpu.VMEM((B, FF), BF16),
                pltpu.VMEM((FF, B), F32),
                pltpu.VMEM((4 * PIECE, D // 2), BF16),
                pltpu.SemaphoreType.DMA((2,)),
            ],
        ),
        out_shape=[shaped(FFL, B)] * 3,
        compiler_params=params("arbitrary"),
        cost_estimate=cost(0, 6),
        name="prepare_ff",
    )(place, w_gate, w_up, w_down, gain)


def project_qkv_kernel(*refs):
    place, x_refs, w_refs = refs[0], refs[1:6], refs[6:11]
    query_ref, kv_ref, scale_ref, cosine_ref, sine_ref, w_out, rows, weights, sems = refs[11:]
    step = pl.program_id(0)
    tokens = put_tokens(x_refs, rows, sems, 0)
    columns = put_columns(place, w_refs, weights, sems, 10)
    back = pltpu.make_async_copy(weights, w_out, sems.at[26])

    @pl.when(step == 0)
    def _():
        for copy in columns + tokens:
            copy.start()
        for copy in columns:
            copy.wait()
        back.start()
        for copy in tokens:
            copy.wait()

    at = pl.ds(pl.multiple_of(step * TILE, TILE), TILE)
    tile = rows[at, :D]
    wide = tile.astype(F32)
    scale = lax.rsqrt(jnp.mean(wide * wide, axis=-1, keepdims=True) + eps)
    scale_ref[...] = scale
    pre = times_transposed(tile, weights[...]) * scale
    tables = rows[at, D:].astype(F32)
    tables = tables + pltpu.roll(tables, B - HD // 2, 1)
    cosine = jnp.concatenate([tables[:, : HD // 2]] * 4, axis=1)
    sine = jnp.concatenate([tables[:, HD : HD + HD // 2]] * 4, axis=1)
    cosine_ref[...] = cosine
    sine_ref[...] = sine
    for i in range(2):
        part = pre[:, i * 2 * HD : (i + 1) * 2 * HD]
        part = (part * cosine + turned(part) * sine).astype(BF16) * HD ** (-0.5)
        query_ref[0, 2 * i] = part[:, :HD]
        query_ref[0, 2 * i + 1] = part[:, HD:]
    part = pre[:, HEADS * HD :]
    lane = lax.broadcasted_iota(jnp.int32, part.shape, 1)
    kv_ref[0] = jnp.where(lane < HD, part * cosine + turned(part) * sine, part).astype(BF16)

    @pl.when(step == 3)
    def _():
        back.wait()


def project_qkv(place, x_pieces, w_pieces):
    tile = lambda lanes: pl.BlockSpec((TILE, lanes), lambda i, p: (i, 0))
    return pl.pallas_call(
        project_qkv_kernel,
        grid_spec=pltpu.PrefetchScalarGridSpec(
            num_scalar_prefetch=1,
            grid=(4,),
            in_specs=[ANYWHERE] * 10,
            out_specs=[
                pl.BlockSpec((1, HEADS, TILE, HD), lambda i, p: (i // 2, 0, i % 2, 0)),
                pl.BlockSpec((1, TILE, 2 * HD), lambda i, p: (i // 2, i % 2, 0)),
                tile(1), tile(2 * HD), tile(2 * HD),
                ANYWHERE,
            ],
            scratch_shapes=[
                pltpu.VMEM((2 * HALF, WIDE), BF16),
                pltpu.VMEM((QKV, D), BF16),
                pltpu.SemaphoreType.DMA((27,)),
            ],
        ),
        out_shape=[
            shaped(2, HEADS, HALF, HD), shaped(2, HALF, 2 * HD), shaped(2 * HALF, 1, kind=F32),
            shaped(2 * HALF, 2 * HD, kind=F32), shaped(2 * HALF, 2 * HD, kind=F32), shaped(QKV, D),
        ],
        compiler_params=params("arbitrary"),
        cost_estimate=cost(2 * 2 * HALF * QKV * D, 8),
        name="project_qkv",
    )(place, *x_pieces, *w_pieces)


def project_kernel(left_ref, weight_ref, *parts):
    put_parts(pl.program_id(0), matmul(left_ref[...], weight_ref[...]).astype(BF16), parts)


def project(left, weight):
    depth = left.shape[1]
    return pl.pallas_call(
        project_kernel,
        grid=(4,),
        in_specs=[pl.BlockSpec((TILE, depth), lambda i: (i, 0)), pl.BlockSpec((depth, D), lambda i: (0, 0))],
        out_specs=part_specs(2),
        out_shape=PART_SHAPES,
        compiler_params=params("arbitrary"),
        cost_estimate=cost(2 * 2 * HALF * depth * D, 8),
        name="project",
    )(left, weight)


def put_term(left, rows, term_ref):
    def one(i, carry):
        term = matmul(left, rows[:, pl.ds(pl.multiple_of(i * 4 * B, 4 * B), 4 * B)]).astype(BF16)
        for j in range(2):
            zx = 2 * i + j
            term_ref[zx % 4, zx // 4, 0] = term[:, 2 * j * B : (2 * j + 1) * B]
            term_ref[zx % 4, zx // 4, 1] = term[:, (2 * j + 1) * B : (2 * j + 2) * B]
        return carry

    lax.fori_loop(0, 4, one, 0)


def qkv_back_kernel(*refs):
    x_refs, grad_q, own, later, cosine_ref, sine_ref, scale_ref = refs[1:6], *refs[6:12]
    grad_ref, term_ref, rows, left, sems = refs[12:]
    copies = put_tokens(x_refs, rows, sems, 0)
    for copy in copies:
        copy.start()
    for step in range(4):
        at, s = slice(step * TILE, (step + 1) * TILE), step // 2
        inner = slice(step % 2 * TILE, (step % 2 + 1) * TILE)
        cosine, sine = cosine_ref[at], sine_ref[at]
        pieces = []
        for i in range(2):
            part = grad_q[s, inner, i * 2 * HD : (i + 1) * 2 * HD]
            pieces.append(part * cosine - turned(part * sine))
        lane = lax.broadcasted_iota(jnp.int32, cosine.shape, 1)
        part = own[s, inner] + later[s, inner].astype(F32)
        pieces.append(jnp.where(lane < HD, part * cosine - turned(part * sine), part))
        grad_pre = jnp.concatenate(pieces, axis=1)
        grad_ref[at] = grad_pre.astype(BF16)
        left[:, at] = (grad_pre * scale_ref[at]).T.astype(BF16)
    for copy in copies:
        copy.wait()
    put_term(left[...], rows, term_ref)


def qkv_back(place, x_pieces, grad_query, own, later, cosine, sine, scale):
    whole = lambda *shape: pl.BlockSpec(shape, lambda i, p: (0,) * len(shape))
    tokens = 2 * HALF
    return pl.pallas_call(
        qkv_back_kernel,
        grid_spec=pltpu.PrefetchScalarGridSpec(
            num_scalar_prefetch=1,
            grid=(1,),
            in_specs=[ANYWHERE] * 5
            + [
                whole(2, HALF, HEADS * HD), whole(2, HALF, 2 * HD), whole(2, HALF, 2 * HD),
                whole(tokens, 2 * HD), whole(tokens, 2 * HD), whole(tokens, 1),
            ],
            out_specs=[whole(tokens, QKV), whole(4, 2, 2, QKV, B)],
            scratch_shapes=[
                pltpu.VMEM((tokens, D), BF16), pltpu.VMEM((QKV, tokens), BF16), pltpu.SemaphoreType.DMA((10,)),
            ],
        ),
        out_shape=[shaped(tokens, QKV), shaped(4, 2, 2, QKV, B)],
        compiler_params=params("arbitrary"),
        cost_estimate=cost(2 * tokens * QKV * D, 9),
        name="qkv_back",
    )(place, *x_pieces, grad_query, own, later, cosine, sine, scale)


def attention_term_kernel(*refs):
    token_refs, left_ref = refs[1:6], refs[6]
    term_ref, rows, sems = refs[-3:]
    copies = put_tokens(token_refs, rows, sems, 0)
    for copy in copies:
        copy.start()
    left = left_ref[...]
    if left.shape[0] == 2 * HALF:
        left = left.T
    for copy in copies:
        copy.wait()
    put_term(left, rows, term_ref)


def attention_terms(place, pieces, left, name):
    whole = lambda *shape: pl.BlockSpec(shape, lambda i, p: (0,) * len(shape))
    rows = min(left.shape)
    return pl.pallas_call(
        attention_term_kernel,
        grid_spec=pltpu.PrefetchScalarGridSpec(
            num_scalar_prefetch=1,
            grid=(1,),
            in_specs=[ANYWHERE] * 5 + [whole(*left.shape)],
            out_specs=whole(4, 2, 2, rows, B),
            scratch_shapes=[pltpu.VMEM((2 * HALF, D), BF16), pltpu.SemaphoreType.DMA((10,))],
        ),
        out_shape=shaped(4, 2, 2, rows, B),
        compiler_params=params("arbitrary"),
        cost_estimate=cost(2 * 2 * HALF * rows * D, 7),
        name=name,
    )(place, *pieces, left)


def token_places(at, y, core):
    step = 1 - 2 * core
    block = jnp.where(
        at < B, y, jnp.where(at < 2 * B, y + 4 - step, jnp.where(at < 3 * B, y + 4 + step, y + 2))
    )
    row = at % B
    row = jnp.where(at < 3 * B, row, (row + core * (B // 2)) % B)
    return (block % 4) * B + row


def set_bias(place_ref, bias_ref):
    zlo, y, core = place_ref[0], place_ref[1], place_ref[2]
    key_at = token_places(lax.broadcasted_iota(jnp.int32, (HALF, 1), 0), y, core)
    query_at = token_places(lax.broadcasted_iota(jnp.int32, (1, HALF), 1), y, core)
    bias_ref[:HALF, :] = jnp.broadcast_to(jnp.where(zlo == 1, 0.0, -1e30), (HALF, HALF))
    bias_ref[HALF:, :] = jnp.where(key_at <= query_at, 0.0, -1e30)


def attention_kernel(place_ref, *refs):
    w_refs, query_ref, kv_ref, mixed_ref, log_ref = refs[:5], *refs[5:9]
    parts, w_out, bias_ref, weight, sems = refs[9:14], *refs[14:]
    columns = put_columns(place_ref, w_refs, weight, sems, 0)
    back = pltpu.make_async_copy(weight, w_out, sems.at[16])

    @pl.when(pl.program_id(0) == 0)
    def _():
        for copy in columns:
            copy.start()
        set_bias(place_ref, bias_ref)
        for copy in columns:
            copy.wait()
        back.start()

    key, value = kv_ref[0, :, :HD], kv_ref[0, :, HD:]
    for head in range(HEADS):
        scores = times_transposed(key, query_ref[0, head]) + bias_ref[...]
        top = jnp.max(scores, axis=0, keepdims=True)
        weights = jnp.exp(scores - top)
        total = jnp.sum(weights, axis=0, keepdims=True)
        low = (weights * (1.0 / total)).astype(BF16)
        mixed_ref[0, :, head * HD : (head + 1) * HD] = outer_sum(value, low).T.astype(BF16)
        log_ref[0, head] = top + jnp.log(total)
    put_rows(matmul(mixed_ref[0], weight[...]).astype(BF16), parts)

    @pl.when(pl.program_id(0) == 1)
    def _():
        back.wait()


def attention_back_kernel(place_ref, *refs):
    grad_refs, query_ref, kv_ref, log_ref, weight_ref = refs[:5], *refs[5:9]
    grad_query_ref, earlier_ref, own_ref, bias_ref, rows, sems = refs[9:]
    step = pl.program_id(0)
    copies = put_tokens(grad_refs, rows, sems, 0)

    @pl.when(step == 0)
    def _():
        for copy in copies:
            copy.start()
        set_bias(place_ref, bias_ref)
        for copy in copies:
            copy.wait()

    hidden = rows[pl.ds(pl.multiple_of(step * HALF, HALF), HALF), :]
    grads = times_transposed(hidden, weight_ref[...]).astype(BF16)
    key, value = kv_ref[0, :, :HD], kv_ref[0, :, HD:]
    grad_key = jnp.zeros((2 * HALF, HD), F32)
    grad_value = jnp.zeros((2 * HALF, HD), F32)
    for head in range(HEADS):
        lanes = slice(head * HD, (head + 1) * HD)
        query, grad = query_ref[0, head], grads[:, lanes]
        weights = jnp.exp(times_transposed(key, query) + bias_ref[...] - log_ref[0, head])
        grad_weights = times_transposed(value, grad)
        delta = jnp.sum(weights * grad_weights, axis=0, keepdims=True)
        grad_scores = (weights * (grad_weights - delta)).astype(BF16)
        grad_query_ref[0, :, lanes] = outer_sum(key, grad_scores).T * HD ** (-0.5)
        grad_key += matmul(grad_scores, query)
        grad_value += matmul(weights.astype(BF16), grad)
    total = jnp.concatenate([grad_key, grad_value], axis=1)
    earlier_ref[0] = total[:HALF].astype(BF16)
    own_ref[0] = total[HALF:]


def sequence_block(*tail):
    return pl.BlockSpec((1,) + tail, lambda s, place: (s,) + (0,) * len(tail))


def attention_call(kernel, in_specs, out_specs, out_shape, scratch, flops, name):
    return pl.pallas_call(
        kernel,
        grid_spec=pltpu.PrefetchScalarGridSpec(
            num_scalar_prefetch=1,
            grid=(2,),
            in_specs=in_specs,
            out_specs=out_specs,
            scratch_shapes=[pltpu.VMEM((2 * HALF, HALF), F32)] + scratch,
        ),
        out_shape=out_shape,
        compiler_params=params("arbitrary"),
        cost_estimate=cost(flops * 8 * 2 * HALF * HALF * HD * 2, 8),
        name=name,
    )


def attention(place, w_pieces, query, kv):
    return attention_call(
        attention_kernel,
        [ANYWHERE] * 5 + [sequence_block(HEADS, HALF, HD), sequence_block(2 * HALF, 2 * HD)],
        [sequence_block(HALF, HEADS * HD), sequence_block(HEADS, 1, HALF)]
        + part_specs(1)
        + [ANYWHERE],
        [shaped(2, HALF, HEADS * HD), shaped(2, HEADS, 1, HALF, kind=F32)] + PART_SHAPES + [shaped(HEADS * HD, D)],
        [pltpu.VMEM((HEADS * HD, D), BF16), pltpu.SemaphoreType.DMA((17,))],
        3,
        "attention",
    )(place, *w_pieces, query, kv)


def attention_back(place, grad_pieces, query, kv, log_total, weight):
    return attention_call(
        attention_back_kernel,
        [ANYWHERE] * 5
        + [
            sequence_block(HEADS, HALF, HD), sequence_block(2 * HALF, 2 * HD),
            sequence_block(HEADS, 1, HALF), pl.BlockSpec((HEADS * HD, D), lambda s, place: (0, 0)),
        ],
        [sequence_block(HALF, HEADS * HD), sequence_block(HALF, 2 * HD), sequence_block(HALF, 2 * HD)],
        [
            shaped(2, HALF, HEADS * HD, kind=F32),
            shaped(2, HALF, 2 * HD),
            shaped(2, HALF, 2 * HD, kind=F32),
        ],
        [pltpu.VMEM((2 * HALF, D), BF16), pltpu.SemaphoreType.DMA((10,))],
        6,
        "attention_back",
    )(place, *grad_pieces, query, kv, log_total, weight)


def finish_attention_kernel(place, *refs):
    piece_refs, w_query, w_key, w_value, gain_ref = refs[:4], *refs[4:8]
    query_out, key_out, value_out, gain_out, rows = refs[8:]
    for ref, by in zip(piece_refs, range(4)):
        at_y = (place[1] + by) % 4
        for c in range(2):
            piece = ref[c].astype(F32)
            rows[pl.ds(pl.multiple_of((2 * at_y + c) * HEADS * HD, HEADS * HD), HEADS * HD)] = piece[: HEADS * HD]
        both = ref[0].astype(F32) + ref[1].astype(F32)
        at = pl.multiple_of(H * HD + at_y * HD, HD)
        rows[pl.ds(at, HD)] = both[HEADS * HD : (HEADS + 1) * HD]
        rows[pl.ds(at + KV * HD, HD)] = both[(HEADS + 1) * HD :]
    gain = gain_ref[...]
    total = jnp.zeros((B, 1), F32)
    row = 0
    for weight, out in ((w_query, query_out), (w_key, key_out), (w_value, value_out)):
        for i in range(out.shape[1] // B):
            lanes = slice(i * B, (i + 1) * B)
            block = rows[row : row + B].T
            total = total + jnp.sum(block * weight[:, lanes].astype(F32), axis=1, keepdims=True)
            out[:, lanes] = block * gain
            row += B
    gain_out[...] = total


def finish_attention(place, pieces, w_query, w_key, w_value, gain):
    whole = lambda *shape: pl.BlockSpec(shape, lambda i, p: (0,) * len(shape))
    kv = KV * HD
    return pl.pallas_call(
        finish_attention_kernel,
        grid_spec=pltpu.PrefetchScalarGridSpec(
            num_scalar_prefetch=1,
            grid=(1,),
            in_specs=[whole(2, QKV, B)] * 4 + [whole(B, D), whole(B, kv), whole(B, kv), whole(B, 1)],
            out_specs=[whole(B, D), whole(B, kv), whole(B, kv), whole(B, 1)],
            scratch_shapes=[pltpu.VMEM((D + 2 * kv, B), F32)],
        ),
        out_shape=[
            shaped(B, D, kind=F32), shaped(B, kv, kind=F32), shaped(B, kv, kind=F32), shaped(B, 1, kind=F32),
        ],
        compiler_params=params("arbitrary"),
        cost_estimate=cost(0, 4),
        name="finish_attention",
    )(place, *pieces, w_query, w_key, w_value, gain)


def finish_output_kernel(blocks, out):
    for i in range(16):
        out[:, i * B : (i + 1) * B] = blocks[i].astype(F32)


def finish_output(blocks):
    return pl.pallas_call(
        finish_output_kernel,
        out_shape=shaped(B, D, kind=F32),
        compiler_params=params(),
        cost_estimate=cost(0, 2),
        name="finish_output",
    )(blocks)


def feed_forward_kernel(*refs):
    place, token_refs, grad_refs, ff_ref = refs[0], refs[1:6], refs[6:11], refs[11]
    act_ref, act_t, gate_t, up_t = refs[12:16]
    parts, down_out = refs[16:21], refs[21]
    rows_h, rows_g, gate_up, down, slabs, sems = refs[22:]
    step = pl.program_id(0)
    tokens = put_tokens(token_refs, rows_h, sems, 0)
    grads = put_tokens(grad_refs, rows_g, sems, 10)
    weights, loads = [], []
    for x in range(4):
        for by in range(4):
            z = (2 * place[4] + place[0] + by) % 4
            zhi, zlo = z // 2, z % 2
            for core in range(2):
                weights.append(
                    pltpu.make_async_copy(
                        ff_ref.at[x, by, pl.ds(core * FFL, FFL)],
                        gate_up.at[zlo, :, lane_block(zhi, x, core)],
                        sems.at[20 + len(weights)],
                    )
                )
            loads.append(
                pltpu.make_async_copy(
                    ff_ref.at[x, by, pl.ds(2 * FFL, FFL)], slabs.at[zlo, zhi * 4 + x], sems.at[52 + len(loads)]
                )
            )
    back = pltpu.make_async_copy(down, down_out, sems.at[68])

    @pl.when(step == 0)
    def _():
        for copy in tokens + weights + loads + grads:
            copy.start()
        for copy in tokens + weights:
            copy.wait()

    rows = pl.ds(pl.multiple_of(step * HALF, HALF), HALF)
    normed = rows_h[rows, :]
    gate_pre = times_transposed(normed, gate_up[0])
    upward = times_transposed(normed, gate_up[1])

    @pl.when(step == 0)
    def _():
        for copy in loads:
            copy.wait()

        def put(q, carry):
            for half in range(2):
                for p in range(4):
                    one = slabs[half, 2 * q, 2 * p * PIECE : 2 * (p + 1) * PIECE, :].astype(F32)
                    two = slabs[half, 2 * q + 1, 2 * p * PIECE : 2 * (p + 1) * PIECE, :].astype(F32)
                    lane = (half * 8 + 2 * p) * B
                    rows = pl.ds(pl.multiple_of(q * 2 * PIECE, 16), 2 * PIECE)
                    down[rows, lane : lane + B] = jnp.concatenate([one[:PIECE], two[:PIECE]], axis=0).astype(BF16)
                    down[rows, lane + B : lane + 2 * B] = jnp.concatenate(
                        [one[PIECE:], two[PIECE:]], axis=0
                    ).astype(BF16)
            return carry

        lax.fori_loop(0, 4, put, 0)
        back.start()
        for copy in grads:
            copy.wait()

    grad_act = times_transposed(rows_g[rows, :], down[...])
    sigmoid = 1.0 / (1.0 + jnp.exp(-gate_pre))
    silu = gate_pre * sigmoid
    activation = silu * upward
    grad_up = grad_act * silu
    grad_gate = grad_act * upward * (sigmoid * (1.0 + gate_pre * (1.0 - sigmoid)))
    part = matmul(grad_gate.astype(BF16), gate_up[0]) + matmul(grad_up.astype(BF16), gate_up[1])
    put_rows(part.astype(BF16), parts)
    act_ref[...] = activation.astype(BF16)
    act_t[...] = activation.T.astype(BF16)
    gate_t[...] = grad_gate.T.astype(BF16)
    up_t[...] = grad_up.T.astype(BF16)

    @pl.when(step == 1)
    def _():
        back.wait()


def feed_forward(place, tokens, grads, ff_all):
    turned_spec = pl.BlockSpec((FFL, HALF), lambda i, p: (0, i))
    turned_shape = shaped(FFL, 2 * HALF)
    return pl.pallas_call(
        feed_forward_kernel,
        grid_spec=pltpu.PrefetchScalarGridSpec(
            num_scalar_prefetch=1,
            grid=(2,),
            in_specs=[ANYWHERE] * 11,
            out_specs=[pl.BlockSpec((HALF, FFL), lambda i, p: (i, 0))]
            + [turned_spec] * 3
            + part_specs(1)
            + [ANYWHERE],
            scratch_shapes=[
                pltpu.VMEM((2 * HALF, D), BF16),
                pltpu.VMEM((2 * HALF, D), BF16),
                pltpu.VMEM((2, FFL, D), BF16),
                pltpu.VMEM((FFL, D), BF16),
                pltpu.VMEM((2, 8, FFL, B), BF16),
                pltpu.SemaphoreType.DMA((69,)),
            ],
        ),
        out_shape=[shaped(2 * HALF, FFL)] + [turned_shape] * 3 + PART_SHAPES + [shaped(FFL, D)],
        compiler_params=params("arbitrary"),
        cost_estimate=cost(2 * 5 * 2 * HALF * FFL * D, 32),
        name="feed_forward",
    )(place, *tokens, *grads, ff_all)


def along_z(place, zhi, zlo):
    return (2 * zhi + zlo + 4 - 2 * place[4] - place[0]) % 4


def load_tokens(step, refs, rows, sems):
    copies = put_tokens(refs, rows, sems, 0)

    @pl.when(step == 0)
    def _():
        for copy in copies:
            copy.start()
        for copy in copies:
            copy.wait()


def gate_up_kernel(*refs):
    place, token_refs, gate_t, up_t, out_ref, rows, terms, sems = refs[0], refs[1:6], *refs[6:]
    step = pl.program_id(0)
    load_tokens(step, token_refs, rows, sems)
    normed = rows[:, pl.ds(pl.multiple_of(step * 4 * B, 4 * B), 4 * B)]

    def out(i, matrix):
        xs, by = pl.ds(i % 2 * 2, 2), along_z(place, i // 2, matrix)
        return pltpu.make_async_copy(terms.at[xs, by], out_ref.at[xs, by], sems.at[10 + 2 * i + matrix])

    for matrix, left in ((0, gate_t), (1, up_t)):
        term = matmul(left[...], normed).astype(BF16)
        by = along_z(place, step // 2, matrix)
        for j in range(2):
            terms[step % 2 * 2 + j, by, 0:FFL, :] = term[:, 2 * j * B : (2 * j + 1) * B]
            terms[step % 2 * 2 + j, by, FFL:, :] = term[:, (2 * j + 1) * B : (2 * j + 2) * B]
        out(step, matrix).start()

    @pl.when(step == 3)
    def _():
        for i in range(4):
            for matrix in range(2):
                out(i, matrix).wait()


def down_kernel(*refs):
    place, grad_refs, act_t, out_ref, rows, terms, sems = refs[0], refs[1:6], *refs[6:]
    step = pl.program_id(0)
    load_tokens(step, grad_refs, rows, sems)
    term = matmul(act_t[...], rows[:, pl.ds(pl.multiple_of(step * 4 * B, 4 * B), 4 * B)])
    for j in range(2):
        p = (2 * step + j) % 4
        at = pl.ds(pl.multiple_of(p * 2 * PIECE, 16), 2 * PIECE)
        for zx in range(8):
            slab = term[zx * PIECE : (zx + 1) * PIECE]
            low, high = slab[:, 2 * j * B : (2 * j + 1) * B], slab[:, (2 * j + 1) * B : (2 * j + 2) * B]
            by = along_z(place, zx // 4, step // 2)
            terms[zx % 4, by, at, :] = jnp.concatenate([low, high], axis=0).astype(BF16)

    def out(half, zhi):
        by = along_z(place, zhi, half)
        return pltpu.make_async_copy(terms.at[:, by], out_ref.at[:, by], sems.at[10 + 2 * half + zhi])

    @pl.when(step % 2 == 1)
    def _():
        for zhi in range(2):
            out(step // 2, zhi).start()

    @pl.when(step == 3)
    def _():
        for half in range(2):
            for zhi in range(2):
                out(half, zhi).wait()


def ff_terms(kernel, place, pieces, lefts, rows, name):
    whole = pl.BlockSpec((FFL, 2 * HALF), lambda i, p: (0, 0))
    return pl.pallas_call(
        kernel,
        grid_spec=pltpu.PrefetchScalarGridSpec(
            num_scalar_prefetch=1,
            grid=(4,),
            in_specs=[ANYWHERE] * 5 + [whole] * len(lefts),
            out_specs=ANYWHERE,
            scratch_shapes=[
                pltpu.VMEM((2 * HALF, D), BF16),
                pltpu.VMEM((4, 4, rows, B), BF16),
                pltpu.SemaphoreType.DMA((18,)),
            ],
        ),
        out_shape=shaped(4, 4, rows, B),
        compiler_params=params("arbitrary"),
        cost_estimate=cost(2 * len(lefts) * 2 * HALF * FFL * D, 8 + 4 * len(lefts)),
        name=name,
    )(place, *pieces, *lefts)


def finish_hidden_kernel(*refs):
    place, piece_refs, weight_ref, gain_ref, out_ref, gain_out, rows = refs[0], refs[1:5], *refs[5:]
    for ref, by in zip(piece_refs, range(4)):
        at_y = (place[1] + by) % 4
        for core in range(2):
            slab = ref[0, core].astype(F32)
            for zx in range(8):
                at = pl.multiple_of((2 * zx + core) * 4 * PIECE + at_y * PIECE, 8)
                rows[pl.ds(at, PIECE)] = slab[zx * PIECE : (zx + 1) * PIECE]
    gain = gain_ref[...]
    total = jnp.zeros((B, 1), F32)
    for i in range(FF // B):
        lanes = slice(i * B, (i + 1) * B)
        block = rows[lanes].T
        total = total + jnp.sum(block * weight_ref[:, lanes].astype(F32), axis=1, keepdims=True)
        out_ref[:, lanes] = block * gain
    gain_out[...] = total


def finish_hidden(place, pieces, matrix, weight, gain):
    own, after, low, high, before = pieces
    at = lambda m: pl.BlockSpec((1, 2, FFL, B), lambda i, p: (m, 0, 0, 0))
    whole = lambda *shape: pl.BlockSpec(shape, lambda i, p: (0,) * len(shape))
    return pl.pallas_call(
        finish_hidden_kernel,
        grid_spec=pltpu.PrefetchScalarGridSpec(
            num_scalar_prefetch=1,
            grid=(1,),
            in_specs=[at(matrix), at(matrix), at(0), at(matrix), whole(B, FF), whole(B, 1)],
            out_specs=[whole(B, FF), whole(B, 1)],
            scratch_shapes=[pltpu.VMEM((FF, B), F32)],
        ),
        out_shape=[shaped(B, FF, kind=F32), shaped(B, 1, kind=F32)],
        compiler_params=params("arbitrary"),
        cost_estimate=cost(3 * 10**9, 6),
        name="finish_hidden",
    )(place, own, after, (low, high)[matrix], before, weight, gain)


def finish_down_kernel(place, own, after, low, high, before, out_ref):
    for refs, by in (((own, own), 0), ((after, after), 1), ((low, high), 2), ((before, before), 3)):
        rows = pl.ds(pl.multiple_of((place[1] + by) % 4 * PIECE, 8), PIECE)
        for half in range(2):
            slab = refs[half][half if by != 2 else 0].astype(F32)
            for t in range(8):
                lane = (half * 8 + t) * B
                out_ref[rows, lane : lane + B] = slab[t * PIECE : (t + 1) * PIECE]


def finish_down(place, pieces):
    halves = lambda n: pl.BlockSpec((n, FFL, B), lambda i, p: (0, 0, 0))
    return pl.pallas_call(
        finish_down_kernel,
        grid_spec=pltpu.PrefetchScalarGridSpec(
            num_scalar_prefetch=1,
            grid=(1,),
            in_specs=[halves(2), halves(2), halves(1), halves(1), halves(2)],
            out_specs=pl.BlockSpec((4 * PIECE, D), lambda i, p: (0, 0)),
        ),
        out_shape=shaped(4 * PIECE, D, kind=F32),
        compiler_params=params("arbitrary"),
        cost_estimate=cost(2 * 10**9, 5),
        name="finish_down",
    )(place, *pieces)


def own_rows(rows_all, y, core, per):
    return lax.dynamic_slice_in_dim(rows_all, (2 * y + core) * per, per, 0)


def resumed(steps, arrived):
    try:
        while True:
            arrived = yield steps.send(arrived)
    except StopIteration as end:
        return end.value


class Flow:
    def __init__(self, steps):
        self.steps, self.result, self.sent = steps, None, None
        self.move(None)

    def move(self, arrived):
        try:
            self.sent = self.steps.send(arrived)
        except StopIteration as end:
            self.sent, self.result = (), end.value


def stage(flows, *values):
    flows = [flow for flow in flows if flow.result is None]
    sizes = [len(flow.sent) for flow in flows]
    leaves, tree = jax.tree.flatten(values)
    tied = tie(*[v for flow in flows for v in flow.sent], *leaves)
    for flow, size in zip(flows, sizes):
        flow.move(tied[:size])
        tied = tied[size:]
    return jax.tree.unflatten(tree, tied)


def gather_steps(block):
    (other,) = yield (swap_core(block),)
    pair = jnp.stack([block, other])
    (got,) = yield (along_y(pair),)
    far, swapped = yield (along_y(send_half(got)), swap_core(got))
    (far_swapped,) = yield (swap_core(far),)
    return pair, got, swapped, far, far_swapped


def scatter_steps(parts, held=0):
    core = lax.axis_index("core")
    first, behind, ahead, far, far_other = parts
    (far_got,) = yield (swap_core(far_other),)
    far = add(far, far_got).astype(BF16)
    low, behind_got, first_got = yield (along_y(far), swap_core(behind), swap_core(first[1]))
    ahead = add(ahead, behind_got).astype(BF16)
    mine = add(lax.dynamic_slice_in_dim(ahead, core * (B // 2), B // 2, 1), low).astype(BF16)
    ahead = lax.dynamic_update_slice_in_dim(ahead, mine, core * (B // 2), 1)
    for _ in range(held):
        yield ()
    (got,) = yield (along_y(ahead),)
    (last,) = yield (swap_core(got[1]),)
    return add(first[0], first_got) + got[0].astype(F32) + last.astype(F32)


def ring_gather_steps(block, axis):
    half = block.shape[0] // 2
    before, after = yield (shift(block, axis, 1), shift(block, axis, -1))
    low, high = yield (shift(before[:half], axis, 1), shift(after[half:], axis, -1))
    return block, after, low, high, before


def ring_scatter_steps(parts, axis):
    half = parts[2].shape[0] // 2
    low, high = yield (shift(parts[2][:half], axis, 1), shift(parts[2][half:], axis, -1))
    after = jnp.concatenate([add(parts[1][:half], low).astype(BF16), parts[1][half:]], axis=0)
    before = jnp.concatenate([parts[3][:half], add(parts[3][half:], high).astype(BF16)], axis=0)
    from_before, from_after = yield (shift(after, axis, 1), shift(before, axis, -1))
    return add(parts[0], from_before) + from_after.astype(F32)


def on_device(
    layer_input,
    positions,
    attn_gain,
    w_query,
    w_key,
    w_value,
    w_output,
    mlp_gain,
    w_gate,
    w_up,
    w_down,
    out_grad,
):
    zlo, y, zhi, x, core = (lax.axis_index(axis) for axis in AXES)
    place = jnp.stack([zlo, y, core, x, zhi]).astype(jnp.int32)

    def by_core(mine, got):
        return jnp.where(core == 0, jnp.stack([mine, got]), jnp.stack([got, mine]))

    def by_zlo(mine, got):
        return jnp.where(zlo == 0, jnp.stack([mine, got]), jnp.stack([got, mine]))

    def by_zhi(mine, got):
        return jnp.where(zhi == 0, jnp.stack([mine, got]), jnp.stack([got, mine]))

    def trio(mine, other, axis):
        across = lax.ppermute(other, (axis, "core"), [(i, 3 - i) for i in range(4)])
        return shift(mine, axis, 1), swap_core(other), across

    def column_steps(mine, got):
        pair = by_core(mine, got)
        (got,) = yield (shift(pair, "zhi", 1),)
        return (yield from ring_gather_steps(by_zhi(pair, got), "x"))

    def output_steps(mine, other):
        there, here, across = yield trio(mine, other, "zhi")
        column = by_zhi(by_core(mine, here), by_core(there, across))
        return (yield from ring_gather_steps(column, "x"))

    def hidden_steps(mine, got, down):
        piece = jnp.concatenate([by_core(mine, got).reshape(2 * FFL, B), down], axis=0)
        pieces = yield from ring_gather_steps(piece, "z")
        return jnp.concatenate(pieces, axis=0).reshape(4, 3 * FFL, B)

    def of_core(pair, other=False):
        return lax.dynamic_index_in_dim(pair, 1 - core if other else core, 0, keepdims=False)

    def whole_ring(pieces):
        own, after, low, high, before = pieces
        return own, after, jnp.concatenate([low, high], axis=0), before

    def attention_steps(column):
        keep = lax.dynamic_index_in_dim(column, zhi, 0, keepdims=False)
        send = lax.dynamic_index_in_dim(column, 1 - zhi, 0, keepdims=False)
        (got,) = yield (shift(send, "zhi", 1),)
        pair = add(keep, got).astype(BF16)
        mine, other = of_core(pair), of_core(pair, True)
        there, here, across = yield trio(mine, other, "zlo")
        own = by_core(add(mine, there), add(here, across)).astype(BF16)
        return (yield from ring_gather_steps(own, "y"))

    def gate_up_steps(sums):
        own = yield from ring_scatter_steps([sums[i] for i in range(4)], "z")
        pair = own.astype(BF16).reshape(2, FFL, B)
        mine, other = of_core(pair), of_core(pair, True)
        there, here, across = yield trio(mine, other, "zlo")
        block = by_zlo(by_core(mine, here), by_core(there, across))
        before, after = yield (shift(block, "y", 1), shift(block, "y", -1))
        low, high = yield (shift(before[:1], "y", 1), shift(after[1:], "y", -1))
        return block, after, low, high, before

    def down_steps(sums):
        steps = ring_scatter_steps([sums[i] for i in range(4)], "z")
        arrived = yield next(steps)
        yield ()
        own = yield from resumed(steps, arrived)
        own = own.astype(BF16)
        (got,) = yield (shift(own, "zlo", 1),)
        return (yield from ring_gather_steps(by_zlo(own, got), "y"))

    x_low = layer_input[0]
    frequency = theta ** (-jnp.arange(0, HD, 2).astype(F32) / HD)
    angles = positions[0].astype(F32)[:, None] * frequency
    tables = []
    for table in (jnp.cos(angles), jnp.sin(angles)):
        high = lax.reduce_precision(table, 8, 7)
        tables += [high.astype(BF16), (table - high).astype(BF16)]
    tokens = Flow(gather_steps(jnp.concatenate([x_low, *tables], axis=1)))
    grads = Flow(gather_steps(out_grad[0]))
    qkv_mine, qkv_other = prepare_qkv(place, w_query, w_key, w_value, attn_gain[:, None])
    qkv_mine, qkv_got, gain_two, w_out = stage([tokens], qkv_mine, swap_core(qkv_other), mlp_gain[:, None], w_output)

    columns = Flow(column_steps(qkv_mine, qkv_got))
    o_rows = lax.all_to_all(w_out.reshape(B, 16, B).transpose(1, 0, 2), FSDP, 0, 0, tiled=True)
    ff_mine, ff_other, ff_down = prepare_ff(place, w_gate, w_up, w_down, gain_two)
    ff_mine, ff_got, ff_down, x_low, o_rows = stage(
        [tokens, columns], ff_mine, swap_core(ff_other), ff_down, x_low, o_rows
    )

    inputs = x_low.astype(F32)
    scale_one = lax.rsqrt(jnp.mean(inputs * inputs, axis=-1, keepdims=True) + eps)
    o_rows = o_rows.reshape(D, B)
    mine, other = own_rows(o_rows, y, core, HEADS * HD), own_rows(o_rows, y, 1 - core, HEADS * HD)
    scale_one, mine, other, ff_mine, ff_got, ff_down = stage(
        [tokens, columns, grads], scale_one, mine, other, ff_mine, ff_got, ff_down
    )

    outputs = Flow(output_steps(mine, other))
    ff_mine, ff_got, ff_down = stage([tokens, columns, outputs], ff_mine, ff_got, ff_down)

    hidden_rows = Flow(hidden_steps(ff_mine, ff_got, ff_down))
    x_pieces = tokens.result
    query, key_value, scale_all, cosine, sine, qkv_full = project_qkv(place, x_pieces, columns.result)
    query, key_value = stage([hidden_rows, outputs, grads], query, key_value)

    earlier = lax.ppermute(key_value, "zlo", [(0, 1)])
    query, key_value, earlier = stage([outputs, hidden_rows], query, key_value, earlier)
    ff_all = lax.all_gather(hidden_rows.result, "x", axis=0, tiled=False)

    key_value = jnp.concatenate([earlier, key_value], axis=1)
    mixed, log_total, *parts, o_full = attention(place, outputs.result, query, key_value)
    parts = stage([grads], *parts)
    sums = Flow(scatter_steps(parts))
    stage([sums, grads])
    grad_pieces = grads.result
    for _ in range(3):
        stage([sums])
    hidden = inputs + sums.result
    scale_two = lax.rsqrt(jnp.mean(hidden * hidden, axis=-1, keepdims=True) + eps)
    normed = Flow(gather_steps((hidden * scale_two).astype(BF16)))
    for _ in range(4):
        stage([normed])
    normed_pieces = normed.result

    activation, act_t, gate_t, up_t, *parts, down_full = feed_forward(place, normed_pieces, grad_pieces, ff_all)
    sums = Flow(scatter_steps(parts))
    (act_t,) = stage([sums], act_t)
    down_terms = ff_terms(down_kernel, place, grad_pieces, (act_t,), FFL, "down_terms")
    down_terms, gate_t = stage([sums], down_terms, gate_t)
    down_sum = lax.psum_scatter(down_terms, "x", scatter_dimension=0, tiled=True)[0]
    gate_up_terms = ff_terms(gate_up_kernel, place, normed_pieces, (gate_t, up_t), 2 * FFL, "gate_up_terms")
    (gate_up_terms,) = stage([sums], gate_up_terms)
    gate_up_sum = lax.psum_scatter(gate_up_terms, "x", scatter_dimension=0, tiled=True)[0]
    stage([sums])

    grad_normed_two = sums.result
    mean_two = jnp.mean(grad_normed_two * hidden, axis=-1, keepdims=True)
    grad_hidden = (
        out_grad[0].astype(F32)
        + scale_two * grad_normed_two
        - hidden * (scale_two * scale_two * scale_two) * mean_two
    )
    hidden_grads = Flow(gather_steps(grad_hidden.astype(BF16)))
    (activation,) = stage([hidden_grads], activation)
    down_parts = project(activation, down_full)
    *down_parts, down_sum = stage([hidden_grads], *down_parts, down_sum)
    result = Flow(scatter_steps(down_parts))
    down = Flow(down_steps(down_sum))
    stage([hidden_grads, down])
    stage([hidden_grads, result])

    hidden_grad_pieces = hidden_grads.result
    grad_query, grad_earlier, grad_own = attention_back(
        place, hidden_grad_pieces, query, key_value, log_total, o_full
    )
    grad_query, grad_earlier, grad_own, mixed = stage([result, down], grad_query, grad_earlier, grad_own, mixed)

    later = lax.ppermute(grad_earlier, "zlo", [(1, 0)])
    output_terms = attention_terms(
        place, hidden_grad_pieces, mixed.reshape(2 * HALF, HEADS * HD), "output_terms"
    )
    later, grad_query, output_terms, gate_up_sum = stage(
        [down], later, grad_query, output_terms, gate_up_sum
    )

    output_sum = lax.psum_scatter(output_terms, "x", scatter_dimension=0, tiled=True)[0]
    gate_up = Flow(gate_up_steps(gate_up_sum))
    grad_pre, terms = qkv_back(place, x_pieces, grad_query, grad_own, later, cosine, sine, scale_all)
    grad_pre, terms, output_sum = stage([gate_up, down, result], grad_pre, terms, output_sum)

    attention_sum = lax.psum_scatter(terms, "x", scatter_dimension=0, tiled=True)[0]
    parts = project(grad_pre, qkv_full)
    output_sums = Flow(attention_steps(output_sum))
    parts = stage([gate_up, down, result, output_sums], *parts)

    sums = Flow(scatter_steps(parts, 2))
    (attention_sum,) = stage([sums, gate_up, output_sums, down], attention_sum)
    attention_sums = Flow(attention_steps(attention_sum))
    stage([sums, output_sums, attention_sums])
    down_grad = finish_down(place, down.result)
    (down_grad,) = stage([sums, output_sums, attention_sums, gate_up], down_grad)

    ring = jnp.roll(jnp.stack(whole_ring(output_sums.result)), y, axis=0).reshape(16, B, B)
    output_grad = lax.all_to_all(ring, FSDP, 0, 0, tiled=True)
    (output_grad,) = stage([sums, attention_sums, gate_up], output_grad)

    gain_two = mlp_gain[:, None]
    gate_grad, gate_gain = finish_hidden(place, gate_up.result, 0, w_gate, gain_two)
    up_grad, up_gain = finish_hidden(place, gate_up.result, 1, w_up, gain_two)
    output_grad = finish_output(output_grad)
    gate_grad, up_grad, output_grad = stage([sums, attention_sums], gate_grad, up_grad, output_grad)
    stage([sums])
    grad_normed = sums.result
    mean_one = jnp.mean(grad_normed * inputs, axis=-1, keepdims=True)
    input_grad = (
        grad_hidden
        + scale_one * grad_normed
        - inputs * (scale_one * scale_one * scale_one) * mean_one
    )
    input_grad = input_grad.astype(BF16)
    query_grad, key_grad, value_grad, attn_gain_grad = finish_attention(
        place, whole_ring(attention_sums.result), w_query, w_key, w_value, attn_gain[:, None]
    )
    return (
        (hidden + result.result).astype(BF16)[None],
        input_grad[None],
        attn_gain_grad[:, 0],
        query_grad,
        key_grad,
        value_grad,
        output_grad,
        (gate_gain + up_gain)[:, 0],
        gate_grad,
        up_grad,
        down_grad,
    )


def solution(mesh):
    split = Mesh(mesh.devices.reshape(2, 4, 2, 4, 2), AXES)
    tokens = P(FSDP, SEQ, None)
    rows = P(FSDP, None)
    gain = P(FSDP)
    in_specs = (
        tokens, P(FSDP, SEQ), gain, rows, rows, rows, rows, gain, rows, rows, rows, tokens,
    )
    out_specs = (tokens, tokens, gain, rows, rows, rows, rows, gain, rows, rows, rows)
    return jax.shard_map(
        on_device, mesh=split, in_specs=in_specs, out_specs=out_specs, check_vma=False
    )
```

```python
import jax
import jax.numpy as jnp
from jax import lax
from jax.experimental import pallas as pl
from jax.experimental.pallas import tpu as pltpu
from jax.sharding import Mesh
from jax.sharding import PartitionSpec as P

H = 32
KV = 4
HD = 64
D = 2048
FF = 5632
B = 128
HALF = 512
HEADS = 4
FFL = 704
PIECE = 88

eps = 1e-05
theta = 10000.0
F32 = jnp.float32
BF16 = jnp.bfloat16
AXES = ("zlo", "y", "zhi", "x", "core")
FSDP = ("zhi", "x", "core")
SEQ = ("zlo", "y")


def matmul(left, right):
    return jnp.dot(left, right, preferred_element_type=F32)


def times_transposed(left, right):
    return lax.dot_general(left, right, (((1,), (1,)), ((), ())), preferred_element_type=F32)


def outer_sum(left, right):
    return lax.dot_general(left, right, (((0,), (0,)), ((), ())), preferred_element_type=F32)


def shift(value, axis, by):
    if axis == "z":
        at = [2 * (z % 2) + z // 2 for z in range(4)]
        return lax.ppermute(value, ("zlo", "zhi"), [(at[z], at[(z + by) % 4]) for z in range(4)])
    size = lax.axis_size(axis)
    return lax.ppermute(value, axis, [(i, (i + by) % size) for i in range(size)])


def swap_core(value):
    return shift(value, "core", 1)


def small_gather(block, axis):
    return shift(block, axis, -1), shift(block, axis, 2), shift(block, axis, 1)


def tie(*values):
    return lax.optimization_barrier(values)


def add(left, right):
    return left.astype(F32) + right.astype(F32)


def along_y(value):
    pairs = []
    for i in range(4):
        pairs.append((2 * i, 2 * ((i + 1) % 4)))
        pairs.append((2 * i + 1, 2 * ((i + 3) % 4) + 1))
    return lax.ppermute(value, ("y", "core"), pairs)


def send_half(got):
    core = lax.axis_index("core")
    return lax.dynamic_slice_in_dim(got, core * (B // 2), B // 2, 1)


FLIPPED = (0, 0, 1, 0, 1)
LENGTHS = (B, B, B, B // 2, B // 2)


def put_tokens(refs, rows_ref, sems, start):
    lanes = pl.ds(0, rows_ref.shape[1])
    copies = []
    row = 0
    for s in range(2):
        for ref, flip, length in zip(refs, FLIPPED, LENGTHS):
            copies.append(
                pltpu.make_async_copy(
                    ref.at[s ^ flip, :, lanes], rows_ref.at[pl.ds(row, length)], sems.at[start + len(copies)]
                )
            )
            row += length
    return copies


TILE = 256
WIDE = D + B
VMEM_LIMIT = 56 * 2**20
ANYWHERE = pl.BlockSpec(memory_space=pl.ANY)


def params(*kinds):
    return pltpu.CompilerParams(dimension_semantics=kinds or None, vmem_limit_bytes=VMEM_LIMIT)


def cost(flops, megabytes):
    return pl.CostEstimate(flops=flops, bytes_accessed=int(megabytes * 2**20), transcendentals=0)


def shaped(*shape, kind=BF16):
    return jax.ShapeDtypeStruct(shape, kind)


PARTS = ((B, False), (B, True), (B, False), (B // 2, False), (B // 2, True))
PART_SHAPES = [jax.ShapeDtypeStruct((2, n, D), BF16) for n, _ in PARTS]


def part_specs(steps):
    def of(turn):
        return lambda i, *_: (1 - i // steps if turn else i // steps, 0, 0)

    return [pl.BlockSpec((1, n, D), of(turn)) for n, turn in PARTS]


def put_parts(step, tile, refs):
    @pl.when(step % 2 == 0)
    def _():
        refs[0][0] = tile[:B]
        refs[1][0] = tile[B:]

    @pl.when(step % 2 == 1)
    def _():
        refs[2][0] = tile[:B]
        refs[3][0] = tile[B : B + B // 2]
        refs[4][0] = tile[B + B // 2 :]


def put_rows(rows, refs):
    row = 0
    for ref, (length, _) in zip(refs, PARTS):
        ref[0] = rows[row : row + length]
        row += length


def turned(values):
    lane = lax.broadcasted_iota(jnp.int32, values.shape, 1) % HD
    return jnp.where(lane < HD // 2, -pltpu.roll(values, 2 * HD - HD // 2, 1), pltpu.roll(values, HD // 2, 1))


def lane_block(zhi, x, core):
    return pl.ds(pl.multiple_of((zhi * 8 + x * 2 + core) * B, B), B)


def put_columns(place, refs, into, sems, start):
    copies = []
    for ref, by, first in zip(refs, (0, 1, 2, 2, 3), (0, 0, 0, 1, 0)):
        for i in range(ref.shape[0]):
            for core in range(2):
                lanes = lane_block(first + i, (place[3] + by) % 4, core)
                copies.append(
                    pltpu.make_async_copy(ref.at[i, core], into.at[:, lanes], sems.at[start + len(copies)])
                )
    return copies


def prepare_qkv_kernel(place, q_mine, q_other, w_key, w_value, gain, mine_ref, other_ref, k_rows, v_rows):
    scale = gain[...]
    k_rows[...] = (w_key[...].astype(F32) * scale).T
    v_rows[...] = (w_value[...].astype(F32) * scale).T
    rows = pl.ds(pl.multiple_of(place[1] * HD, HD), HD)
    for source, out in ((q_mine, mine_ref), (q_other, other_ref)):
        out[: HEADS * HD] = (source[...].astype(F32) * scale).T.astype(BF16)
        out[HEADS * HD : (HEADS + 1) * HD] = k_rows[rows].astype(BF16)
        out[(HEADS + 1) * HD :] = v_rows[rows].astype(BF16)


QKV = (HEADS + 2) * HD


def prepare_qkv(place, w_query, w_key, w_value, gain):
    whole = lambda *shape: pl.BlockSpec(shape, lambda i, p: (0,) * len(shape))
    return pl.pallas_call(
        prepare_qkv_kernel,
        grid_spec=pltpu.PrefetchScalarGridSpec(
            num_scalar_prefetch=1,
            grid=(1,),
            in_specs=[
                pl.BlockSpec((B, HEADS * HD), lambda i, p: (0, 2 * p[1] + p[2])),
                pl.BlockSpec((B, HEADS * HD), lambda i, p: (0, 2 * p[1] + 1 - p[2])),
                whole(B, KV * HD), whole(B, KV * HD), whole(B, 1),
            ],
            out_specs=[whole(QKV, B), whole(QKV, B)],
            scratch_shapes=[pltpu.VMEM((KV * HD, B), F32), pltpu.VMEM((KV * HD, B), F32)],
        ),
        out_shape=[shaped(QKV, B), shaped(QKV, B)],
        compiler_params=params("arbitrary"),
        cost_estimate=cost(0, 1),
        name="prepare_qkv",
    )(place, w_query, w_query, w_key, w_value, gain)


def prepare_ff_kernel(place, w_gate, w_up, w_down, gain, mine_ref, other_ref, down_ref, picked, rows, down_rows, sems):
    zlo, y, core = place[0], place[1], place[2]
    down = pltpu.make_async_copy(
        w_down.at[:, pl.ds(pl.multiple_of(zlo * (D // 2), D // 2), D // 2)], down_rows, sems.at[1]
    )
    down.start()

    @pl.when(zlo == 0)
    def _():
        copy = pltpu.make_async_copy(w_gate, picked, sems.at[0])
        copy.start()
        copy.wait()

    @pl.when(zlo == 1)
    def _():
        copy = pltpu.make_async_copy(w_up, picked, sems.at[0])
        copy.start()
        copy.wait()

    scale = gain[...]
    for i in range(FF // B):
        rows[i * B : (i + 1) * B] = (picked[:, i * B : (i + 1) * B].astype(F32) * scale).T
    for which, out in ((core, mine_ref), (1 - core, other_ref)):
        slabs = []
        for zx in range(8):
            at = pl.multiple_of(zx * 2 * 4 * PIECE + which * 4 * PIECE + y * PIECE, 8)
            slabs.append(rows[pl.ds(at, PIECE)])
        out[...] = jnp.concatenate(slabs, axis=0).astype(BF16)
    down.wait()
    for t in range(8):
        rows[t * 4 * PIECE : (t + 1) * 4 * PIECE] = down_rows[:, t * B : (t + 1) * B].astype(F32)
    slabs = [rows[pl.ds(pl.multiple_of(t * 4 * PIECE + y * PIECE, 8), PIECE)] for t in range(8)]
    down_ref[...] = jnp.concatenate(slabs, axis=0).astype(BF16)


def prepare_ff(place, w_gate, w_up, w_down, gain):
    return pl.pallas_call(
        prepare_ff_kernel,
        grid_spec=pltpu.PrefetchScalarGridSpec(
            num_scalar_prefetch=1,
            grid=(1,),
            in_specs=[ANYWHERE, ANYWHERE, ANYWHERE, pl.BlockSpec((B, 1), lambda i, p: (0, 0))],
            out_specs=[pl.BlockSpec((FFL, B), lambda i, p: (0, 0))] * 3,
            scratch_shapes=[
                pltpu.VMEM((B, FF), BF16),
                pltpu.VMEM((FF, B), F32),
                pltpu.VMEM((4 * PIECE, D // 2), BF16),
                pltpu.SemaphoreType.DMA((2,)),
            ],
        ),
        out_shape=[shaped(FFL, B)] * 3,
        compiler_params=params("arbitrary"),
        cost_estimate=cost(0, 6),
        name="prepare_ff",
    )(place, w_gate, w_up, w_down, gain)


def project_qkv_kernel(*refs):
    place, x_refs, w_refs = refs[0], refs[1:6], refs[6:11]
    query_ref, kv_ref, scale_ref, cosine_ref, sine_ref, w_out, rows, weights, sems = refs[11:]
    step = pl.program_id(0)
    tokens = put_tokens(x_refs, rows, sems, 0)
    columns = put_columns(place, w_refs, weights, sems, 10)
    back = pltpu.make_async_copy(weights, w_out, sems.at[26])

    @pl.when(step == 0)
    def _():
        for copy in columns + tokens:
            copy.start()
        for copy in columns:
            copy.wait()
        back.start()
        for copy in tokens:
            copy.wait()

    at = pl.ds(pl.multiple_of(step * TILE, TILE), TILE)
    tile = rows[at, :D]
    wide = tile.astype(F32)
    scale = lax.rsqrt(jnp.mean(wide * wide, axis=-1, keepdims=True) + eps)
    scale_ref[...] = scale
    pre = times_transposed(tile, weights[...]) * scale
    tables = rows[at, D:].astype(F32)
    tables = tables + pltpu.roll(tables, B - HD // 2, 1)
    cosine = jnp.concatenate([tables[:, : HD // 2]] * 4, axis=1)
    sine = jnp.concatenate([tables[:, HD : HD + HD // 2]] * 4, axis=1)
    cosine_ref[...] = cosine
    sine_ref[...] = sine
    for i in range(2):
        part = pre[:, i * 2 * HD : (i + 1) * 2 * HD]
        part = (part * cosine + turned(part) * sine).astype(BF16) * HD ** (-0.5)
        query_ref[0, 2 * i] = part[:, :HD]
        query_ref[0, 2 * i + 1] = part[:, HD:]
    part = pre[:, HEADS * HD :]
    lane = lax.broadcasted_iota(jnp.int32, part.shape, 1)
    kv_ref[0] = jnp.where(lane < HD, part * cosine + turned(part) * sine, part).astype(BF16)

    @pl.when(step == 3)
    def _():
        back.wait()


def project_qkv(place, x_pieces, w_pieces):
    tile = lambda lanes: pl.BlockSpec((TILE, lanes), lambda i, p: (i, 0))
    return pl.pallas_call(
        project_qkv_kernel,
        grid_spec=pltpu.PrefetchScalarGridSpec(
            num_scalar_prefetch=1,
            grid=(4,),
            in_specs=[ANYWHERE] * 10,
            out_specs=[
                pl.BlockSpec((1, HEADS, TILE, HD), lambda i, p: (i // 2, 0, i % 2, 0)),
                pl.BlockSpec((1, TILE, 2 * HD), lambda i, p: (i // 2, i % 2, 0)),
                tile(1), tile(2 * HD), tile(2 * HD),
                ANYWHERE,
            ],
            scratch_shapes=[
                pltpu.VMEM((2 * HALF, WIDE), BF16),
                pltpu.VMEM((QKV, D), BF16),
                pltpu.SemaphoreType.DMA((27,)),
            ],
        ),
        out_shape=[
            shaped(2, HEADS, HALF, HD), shaped(2, HALF, 2 * HD), shaped(2 * HALF, 1, kind=F32),
            shaped(2 * HALF, 2 * HD, kind=F32), shaped(2 * HALF, 2 * HD, kind=F32), shaped(QKV, D),
        ],
        compiler_params=params("arbitrary"),
        cost_estimate=cost(2 * 2 * HALF * QKV * D, 8),
        name="project_qkv",
    )(place, *x_pieces, *w_pieces)


def project_kernel(left_ref, weight_ref, *parts):
    put_parts(pl.program_id(0), matmul(left_ref[...], weight_ref[...]).astype(BF16), parts)


def project(left, weight):
    depth = left.shape[1]
    return pl.pallas_call(
        project_kernel,
        grid=(4,),
        in_specs=[pl.BlockSpec((TILE, depth), lambda i: (i, 0)), pl.BlockSpec((depth, D), lambda i: (0, 0))],
        out_specs=part_specs(2),
        out_shape=PART_SHAPES,
        compiler_params=params("arbitrary"),
        cost_estimate=cost(2 * 2 * HALF * depth * D, 8),
        name="project",
    )(left, weight)


def put_term(left, rows, term_ref):
    def one(i, carry):
        term = matmul(left, rows[:, pl.ds(pl.multiple_of(i * 4 * B, 4 * B), 4 * B)]).astype(BF16)
        for j in range(2):
            zx = 2 * i + j
            term_ref[zx % 4, zx // 4, 0] = term[:, 2 * j * B : (2 * j + 1) * B]
            term_ref[zx % 4, zx // 4, 1] = term[:, (2 * j + 1) * B : (2 * j + 2) * B]
        return carry

    lax.fori_loop(0, 4, one, 0)


def qkv_back_kernel(*refs):
    x_refs, grad_q, own, later, cosine_ref, sine_ref, scale_ref = refs[1:6], *refs[6:12]
    grad_ref, term_ref, rows, left, sems = refs[12:]
    copies = put_tokens(x_refs, rows, sems, 0)
    for copy in copies:
        copy.start()
    for step in range(4):
        at, s = slice(step * TILE, (step + 1) * TILE), step // 2
        inner = slice(step % 2 * TILE, (step % 2 + 1) * TILE)
        cosine, sine = cosine_ref[at], sine_ref[at]
        pieces = []
        for i in range(2):
            part = grad_q[s, inner, i * 2 * HD : (i + 1) * 2 * HD]
            pieces.append(part * cosine - turned(part * sine))
        lane = lax.broadcasted_iota(jnp.int32, cosine.shape, 1)
        part = own[s, inner] + later[s, inner].astype(F32)
        pieces.append(jnp.where(lane < HD, part * cosine - turned(part * sine), part))
        grad_pre = jnp.concatenate(pieces, axis=1)
        grad_ref[at] = grad_pre.astype(BF16)
        left[:, at] = (grad_pre * scale_ref[at]).T.astype(BF16)
    for copy in copies:
        copy.wait()
    put_term(left[...], rows, term_ref)


def qkv_back(place, x_pieces, grad_query, own, later, cosine, sine, scale):
    whole = lambda *shape: pl.BlockSpec(shape, lambda i, p: (0,) * len(shape))
    tokens = 2 * HALF
    return pl.pallas_call(
        qkv_back_kernel,
        grid_spec=pltpu.PrefetchScalarGridSpec(
            num_scalar_prefetch=1,
            grid=(1,),
            in_specs=[ANYWHERE] * 5
            + [
                whole(2, HALF, HEADS * HD), whole(2, HALF, 2 * HD), whole(2, HALF, 2 * HD),
                whole(tokens, 2 * HD), whole(tokens, 2 * HD), whole(tokens, 1),
            ],
            out_specs=[whole(tokens, QKV), whole(4, 2, 2, QKV, B)],
            scratch_shapes=[
                pltpu.VMEM((tokens, D), BF16), pltpu.VMEM((QKV, tokens), BF16), pltpu.SemaphoreType.DMA((10,)),
            ],
        ),
        out_shape=[shaped(tokens, QKV), shaped(4, 2, 2, QKV, B)],
        compiler_params=params("arbitrary"),
        cost_estimate=cost(2 * tokens * QKV * D, 9),
        name="qkv_back",
    )(place, *x_pieces, grad_query, own, later, cosine, sine, scale)


def attention_term_kernel(*refs):
    token_refs, left_ref = refs[1:6], refs[6]
    term_ref, rows, sems = refs[-3:]
    copies = put_tokens(token_refs, rows, sems, 0)
    for copy in copies:
        copy.start()
    left = left_ref[...]
    if left.shape[0] == 2 * HALF:
        left = left.T
    for copy in copies:
        copy.wait()
    put_term(left, rows, term_ref)


def attention_terms(place, pieces, left, name):
    whole = lambda *shape: pl.BlockSpec(shape, lambda i, p: (0,) * len(shape))
    rows = min(left.shape)
    return pl.pallas_call(
        attention_term_kernel,
        grid_spec=pltpu.PrefetchScalarGridSpec(
            num_scalar_prefetch=1,
            grid=(1,),
            in_specs=[ANYWHERE] * 5 + [whole(*left.shape)],
            out_specs=whole(4, 2, 2, rows, B),
            scratch_shapes=[pltpu.VMEM((2 * HALF, D), BF16), pltpu.SemaphoreType.DMA((10,))],
        ),
        out_shape=shaped(4, 2, 2, rows, B),
        compiler_params=params("arbitrary"),
        cost_estimate=cost(2 * 2 * HALF * rows * D, 7),
        name=name,
    )(place, *pieces, left)


def token_places(at, y, core):
    step = 1 - 2 * core
    block = jnp.where(
        at < B, y, jnp.where(at < 2 * B, y + 4 - step, jnp.where(at < 3 * B, y + 4 + step, y + 2))
    )
    row = at % B
    row = jnp.where(at < 3 * B, row, (row + core * (B // 2)) % B)
    return (block % 4) * B + row


def set_bias(place_ref, bias_ref):
    zlo, y, core = place_ref[0], place_ref[1], place_ref[2]
    key_at = token_places(lax.broadcasted_iota(jnp.int32, (HALF, 1), 0), y, core)
    query_at = token_places(lax.broadcasted_iota(jnp.int32, (1, HALF), 1), y, core)
    bias_ref[:HALF, :] = jnp.broadcast_to(jnp.where(zlo == 1, 0.0, -1e30), (HALF, HALF))
    bias_ref[HALF:, :] = jnp.where(key_at <= query_at, 0.0, -1e30)


def attention_kernel(place_ref, *refs):
    w_refs, query_ref, kv_ref, mixed_ref, log_ref = refs[:5], *refs[5:9]
    parts, w_out, bias_ref, weight, sems = refs[9:14], *refs[14:]
    columns = put_columns(place_ref, w_refs, weight, sems, 0)
    back = pltpu.make_async_copy(weight, w_out, sems.at[16])

    @pl.when(pl.program_id(0) == 0)
    def _():
        for copy in columns:
            copy.start()
        set_bias(place_ref, bias_ref)
        for copy in columns:
            copy.wait()
        back.start()

    key, value = kv_ref[0, :, :HD], kv_ref[0, :, HD:]
    for head in range(HEADS):
        scores = times_transposed(key, query_ref[0, head]) + bias_ref[...]
        top = jnp.max(scores, axis=0, keepdims=True)
        weights = jnp.exp(scores - top)
        total = jnp.sum(weights, axis=0, keepdims=True)
        low = (weights * (1.0 / total)).astype(BF16)
        mixed_ref[0, :, head * HD : (head + 1) * HD] = outer_sum(value, low).T.astype(BF16)
        log_ref[0, head] = top + jnp.log(total)
    put_rows(matmul(mixed_ref[0], weight[...]).astype(BF16), parts)

    @pl.when(pl.program_id(0) == 1)
    def _():
        back.wait()


def attention_back_kernel(place_ref, *refs):
    grad_refs, query_ref, kv_ref, log_ref, weight_ref = refs[:5], *refs[5:9]
    grad_query_ref, earlier_ref, own_ref, bias_ref, rows, sems = refs[9:]
    step = pl.program_id(0)
    copies = put_tokens(grad_refs, rows, sems, 0)

    @pl.when(step == 0)
    def _():
        for copy in copies:
            copy.start()
        set_bias(place_ref, bias_ref)
        for copy in copies:
            copy.wait()

    hidden = rows[pl.ds(pl.multiple_of(step * HALF, HALF), HALF), :]
    grads = times_transposed(hidden, weight_ref[...]).astype(BF16)
    key, value = kv_ref[0, :, :HD], kv_ref[0, :, HD:]
    grad_key = jnp.zeros((2 * HALF, HD), F32)
    grad_value = jnp.zeros((2 * HALF, HD), F32)
    for head in range(HEADS):
        lanes = slice(head * HD, (head + 1) * HD)
        query, grad = query_ref[0, head], grads[:, lanes]
        weights = jnp.exp(times_transposed(key, query) + bias_ref[...] - log_ref[0, head])
        grad_weights = times_transposed(value, grad)
        delta = jnp.sum(weights * grad_weights, axis=0, keepdims=True)
        grad_scores = (weights * (grad_weights - delta)).astype(BF16)
        grad_query_ref[0, :, lanes] = outer_sum(key, grad_scores).T * HD ** (-0.5)
        grad_key += matmul(grad_scores, query)
        grad_value += matmul(weights.astype(BF16), grad)
    total = jnp.concatenate([grad_key, grad_value], axis=1)
    earlier_ref[0] = total[:HALF].astype(BF16)
    own_ref[0] = total[HALF:]


def sequence_block(*tail):
    return pl.BlockSpec((1,) + tail, lambda s, place: (s,) + (0,) * len(tail))


def attention_call(kernel, in_specs, out_specs, out_shape, scratch, flops, name):
    return pl.pallas_call(
        kernel,
        grid_spec=pltpu.PrefetchScalarGridSpec(
            num_scalar_prefetch=1,
            grid=(2,),
            in_specs=in_specs,
            out_specs=out_specs,
            scratch_shapes=[pltpu.VMEM((2 * HALF, HALF), F32)] + scratch,
        ),
        out_shape=out_shape,
        compiler_params=params("arbitrary"),
        cost_estimate=cost(flops * 8 * 2 * HALF * HALF * HD * 2, 8),
        name=name,
    )


def attention(place, w_pieces, query, kv):
    return attention_call(
        attention_kernel,
        [ANYWHERE] * 5 + [sequence_block(HEADS, HALF, HD), sequence_block(2 * HALF, 2 * HD)],
        [sequence_block(HALF, HEADS * HD), sequence_block(HEADS, 1, HALF)]
        + part_specs(1)
        + [ANYWHERE],
        [shaped(2, HALF, HEADS * HD), shaped(2, HEADS, 1, HALF, kind=F32)] + PART_SHAPES + [shaped(HEADS * HD, D)],
        [pltpu.VMEM((HEADS * HD, D), BF16), pltpu.SemaphoreType.DMA((17,))],
        3,
        "attention",
    )(place, *w_pieces, query, kv)


def attention_back(place, grad_pieces, query, kv, log_total, weight):
    return attention_call(
        attention_back_kernel,
        [ANYWHERE] * 5
        + [
            sequence_block(HEADS, HALF, HD), sequence_block(2 * HALF, 2 * HD),
            sequence_block(HEADS, 1, HALF), pl.BlockSpec((HEADS * HD, D), lambda s, place: (0, 0)),
        ],
        [sequence_block(HALF, HEADS * HD), sequence_block(HALF, 2 * HD), sequence_block(HALF, 2 * HD)],
        [
            shaped(2, HALF, HEADS * HD, kind=F32),
            shaped(2, HALF, 2 * HD),
            shaped(2, HALF, 2 * HD, kind=F32),
        ],
        [pltpu.VMEM((2 * HALF, D), BF16), pltpu.SemaphoreType.DMA((10,))],
        6,
        "attention_back",
    )(place, *grad_pieces, query, kv, log_total, weight)


def finish_attention_kernel(place, *refs):
    piece_refs, w_query, w_key, w_value, gain_ref = refs[:4], *refs[4:8]
    query_out, key_out, value_out, gain_out, rows = refs[8:]
    for ref, by in zip(piece_refs, range(4)):
        at_y = (place[1] + by) % 4
        for c in range(2):
            piece = ref[c].astype(F32)
            rows[pl.ds(pl.multiple_of((2 * at_y + c) * HEADS * HD, HEADS * HD), HEADS * HD)] = piece[: HEADS * HD]
        both = ref[0].astype(F32) + ref[1].astype(F32)
        at = pl.multiple_of(H * HD + at_y * HD, HD)
        rows[pl.ds(at, HD)] = both[HEADS * HD : (HEADS + 1) * HD]
        rows[pl.ds(at + KV * HD, HD)] = both[(HEADS + 1) * HD :]
    gain = gain_ref[...]
    total = jnp.zeros((B, 1), F32)
    row = 0
    for weight, out in ((w_query, query_out), (w_key, key_out), (w_value, value_out)):
        for i in range(out.shape[1] // B):
            lanes = slice(i * B, (i + 1) * B)
            block = rows[row : row + B].T
            total = total + jnp.sum(block * weight[:, lanes].astype(F32), axis=1, keepdims=True)
            out[:, lanes] = block * gain
            row += B
    gain_out[...] = total


def finish_attention(place, pieces, w_query, w_key, w_value, gain):
    whole = lambda *shape: pl.BlockSpec(shape, lambda i, p: (0,) * len(shape))
    kv = KV * HD
    return pl.pallas_call(
        finish_attention_kernel,
        grid_spec=pltpu.PrefetchScalarGridSpec(
            num_scalar_prefetch=1,
            grid=(1,),
            in_specs=[whole(2, QKV, B)] * 4 + [whole(B, D), whole(B, kv), whole(B, kv), whole(B, 1)],
            out_specs=[whole(B, D), whole(B, kv), whole(B, kv), whole(B, 1)],
            scratch_shapes=[pltpu.VMEM((D + 2 * kv, B), F32)],
        ),
        out_shape=[
            shaped(B, D, kind=F32), shaped(B, kv, kind=F32), shaped(B, kv, kind=F32), shaped(B, 1, kind=F32),
        ],
        compiler_params=params("arbitrary"),
        cost_estimate=cost(0, 4),
        name="finish_attention",
    )(place, *pieces, w_query, w_key, w_value, gain)


def finish_output_kernel(blocks, out):
    for i in range(16):
        out[:, i * B : (i + 1) * B] = blocks[i].astype(F32)


def finish_output(blocks):
    return pl.pallas_call(
        finish_output_kernel,
        out_shape=shaped(B, D, kind=F32),
        compiler_params=params(),
        cost_estimate=cost(0, 2),
        name="finish_output",
    )(blocks)


def feed_forward_kernel(*refs):
    place, token_refs, grad_refs, ff_ref = refs[0], refs[1:6], refs[6:11], refs[11]
    act_ref, act_t, gate_t, up_t = refs[12:16]
    parts, down_out = refs[16:21], refs[21]
    rows_h, rows_g, gate_up, down, slabs, sems = refs[22:]
    step = pl.program_id(0)
    tokens = put_tokens(token_refs, rows_h, sems, 0)
    grads = put_tokens(grad_refs, rows_g, sems, 10)
    weights, loads = [], []
    for x in range(4):
        for by in range(4):
            z = (2 * place[4] + place[0] + by) % 4
            zhi, zlo = z // 2, z % 2
            for core in range(2):
                weights.append(
                    pltpu.make_async_copy(
                        ff_ref.at[x, by, pl.ds(core * FFL, FFL)],
                        gate_up.at[zlo, :, lane_block(zhi, x, core)],
                        sems.at[20 + len(weights)],
                    )
                )
            loads.append(
                pltpu.make_async_copy(
                    ff_ref.at[x, by, pl.ds(2 * FFL, FFL)], slabs.at[zlo, zhi * 4 + x], sems.at[52 + len(loads)]
                )
            )
    back = pltpu.make_async_copy(down, down_out, sems.at[68])

    @pl.when(step == 0)
    def _():
        for copy in tokens + weights + loads + grads:
            copy.start()
        for copy in tokens + weights:
            copy.wait()

    rows = pl.ds(pl.multiple_of(step * HALF, HALF), HALF)
    normed = rows_h[rows, :]
    gate_pre = times_transposed(normed, gate_up[0])
    upward = times_transposed(normed, gate_up[1])

    @pl.when(step == 0)
    def _():
        for copy in loads:
            copy.wait()

        def put(q, carry):
            for half in range(2):
                for p in range(4):
                    one = slabs[half, 2 * q, 2 * p * PIECE : 2 * (p + 1) * PIECE, :].astype(F32)
                    two = slabs[half, 2 * q + 1, 2 * p * PIECE : 2 * (p + 1) * PIECE, :].astype(F32)
                    lane = (half * 8 + 2 * p) * B
                    rows = pl.ds(pl.multiple_of(q * 2 * PIECE, 16), 2 * PIECE)
                    down[rows, lane : lane + B] = jnp.concatenate([one[:PIECE], two[:PIECE]], axis=0).astype(BF16)
                    down[rows, lane + B : lane + 2 * B] = jnp.concatenate(
                        [one[PIECE:], two[PIECE:]], axis=0
                    ).astype(BF16)
            return carry

        lax.fori_loop(0, 4, put, 0)
        back.start()
        for copy in grads:
            copy.wait()

    grad_act = times_transposed(rows_g[rows, :], down[...])
    sigmoid = 1.0 / (1.0 + jnp.exp(-gate_pre))
    silu = gate_pre * sigmoid
    activation = silu * upward
    grad_up = grad_act * silu
    grad_gate = grad_act * upward * (sigmoid * (1.0 + gate_pre * (1.0 - sigmoid)))
    part = matmul(grad_gate.astype(BF16), gate_up[0]) + matmul(grad_up.astype(BF16), gate_up[1])
    put_rows(part.astype(BF16), parts)
    act_ref[...] = activation.astype(BF16)
    act_t[...] = activation.T.astype(BF16)
    gate_t[...] = grad_gate.T.astype(BF16)
    up_t[...] = grad_up.T.astype(BF16)

    @pl.when(step == 1)
    def _():
        back.wait()


def feed_forward(place, tokens, grads, ff_all):
    turned_spec = pl.BlockSpec((FFL, HALF), lambda i, p: (0, i))
    turned_shape = shaped(FFL, 2 * HALF)
    return pl.pallas_call(
        feed_forward_kernel,
        grid_spec=pltpu.PrefetchScalarGridSpec(
            num_scalar_prefetch=1,
            grid=(2,),
            in_specs=[ANYWHERE] * 11,
            out_specs=[pl.BlockSpec((HALF, FFL), lambda i, p: (i, 0))]
            + [turned_spec] * 3
            + part_specs(1)
            + [ANYWHERE],
            scratch_shapes=[
                pltpu.VMEM((2 * HALF, D), BF16),
                pltpu.VMEM((2 * HALF, D), BF16),
                pltpu.VMEM((2, FFL, D), BF16),
                pltpu.VMEM((FFL, D), BF16),
                pltpu.VMEM((2, 8, FFL, B), BF16),
                pltpu.SemaphoreType.DMA((69,)),
            ],
        ),
        out_shape=[shaped(2 * HALF, FFL)] + [turned_shape] * 3 + PART_SHAPES + [shaped(FFL, D)],
        compiler_params=params("arbitrary"),
        cost_estimate=cost(2 * 5 * 2 * HALF * FFL * D, 32),
        name="feed_forward",
    )(place, *tokens, *grads, ff_all)


def along_z(place, zhi, zlo):
    return (2 * zhi + zlo + 4 - 2 * place[4] - place[0]) % 4


def load_tokens(step, refs, rows, sems):
    copies = put_tokens(refs, rows, sems, 0)

    @pl.when(step == 0)
    def _():
        for copy in copies:
            copy.start()
        for copy in copies:
            copy.wait()


def gate_up_kernel(*refs):
    place, token_refs, gate_t, up_t, out_ref, rows, terms, sems = refs[0], refs[1:6], *refs[6:]
    step = pl.program_id(0)
    load_tokens(step, token_refs, rows, sems)
    normed = rows[:, pl.ds(pl.multiple_of(step * 4 * B, 4 * B), 4 * B)]

    def out(i, matrix):
        xs, by = pl.ds(i % 2 * 2, 2), along_z(place, i // 2, matrix)
        return pltpu.make_async_copy(terms.at[xs, by], out_ref.at[xs, by], sems.at[10 + 2 * i + matrix])

    for matrix, left in ((0, gate_t), (1, up_t)):
        term = matmul(left[...], normed).astype(BF16)
        by = along_z(place, step // 2, matrix)
        for j in range(2):
            terms[step % 2 * 2 + j, by, 0:FFL, :] = term[:, 2 * j * B : (2 * j + 1) * B]
            terms[step % 2 * 2 + j, by, FFL:, :] = term[:, (2 * j + 1) * B : (2 * j + 2) * B]
        out(step, matrix).start()

    @pl.when(step == 3)
    def _():
        for i in range(4):
            for matrix in range(2):
                out(i, matrix).wait()


def down_kernel(*refs):
    place, grad_refs, act_t, out_ref, rows, terms, sems = refs[0], refs[1:6], *refs[6:]
    step = pl.program_id(0)
    load_tokens(step, grad_refs, rows, sems)
    term = matmul(act_t[...], rows[:, pl.ds(pl.multiple_of(step * 4 * B, 4 * B), 4 * B)])
    for j in range(2):
        p = (2 * step + j) % 4
        at = pl.ds(pl.multiple_of(p * 2 * PIECE, 16), 2 * PIECE)
        for zx in range(8):
            slab = term[zx * PIECE : (zx + 1) * PIECE]
            low, high = slab[:, 2 * j * B : (2 * j + 1) * B], slab[:, (2 * j + 1) * B : (2 * j + 2) * B]
            by = along_z(place, zx // 4, step // 2)
            terms[zx % 4, by, at, :] = jnp.concatenate([low, high], axis=0).astype(BF16)

    def out(half, zhi):
        by = along_z(place, zhi, half)
        return pltpu.make_async_copy(terms.at[:, by], out_ref.at[:, by], sems.at[10 + 2 * half + zhi])

    @pl.when(step % 2 == 1)
    def _():
        for zhi in range(2):
            out(step // 2, zhi).start()

    @pl.when(step == 3)
    def _():
        for half in range(2):
            for zhi in range(2):
                out(half, zhi).wait()


def ff_terms(kernel, place, pieces, lefts, rows, name):
    whole = pl.BlockSpec((FFL, 2 * HALF), lambda i, p: (0, 0))
    return pl.pallas_call(
        kernel,
        grid_spec=pltpu.PrefetchScalarGridSpec(
            num_scalar_prefetch=1,
            grid=(4,),
            in_specs=[ANYWHERE] * 5 + [whole] * len(lefts),
            out_specs=ANYWHERE,
            scratch_shapes=[
                pltpu.VMEM((2 * HALF, D), BF16),
                pltpu.VMEM((4, 4, rows, B), BF16),
                pltpu.SemaphoreType.DMA((18,)),
            ],
        ),
        out_shape=shaped(4, 4, rows, B),
        compiler_params=params("arbitrary"),
        cost_estimate=cost(2 * len(lefts) * 2 * HALF * FFL * D, 8 + 4 * len(lefts)),
        name=name,
    )(place, *pieces, *lefts)


def finish_hidden_kernel(*refs):
    place, piece_refs, weight_ref, gain_ref, out_ref, gain_out, rows = refs[0], refs[1:5], *refs[5:]
    for ref, by in zip(piece_refs, range(4)):
        at_y = (place[1] + by) % 4
        for core in range(2):
            slab = ref[0, core].astype(F32)
            for zx in range(8):
                at = pl.multiple_of((2 * zx + core) * 4 * PIECE + at_y * PIECE, 8)
                rows[pl.ds(at, PIECE)] = slab[zx * PIECE : (zx + 1) * PIECE]
    gain = gain_ref[...]
    total = jnp.zeros((B, 1), F32)
    for i in range(FF // B):
        lanes = slice(i * B, (i + 1) * B)
        block = rows[lanes].T
        total = total + jnp.sum(block * weight_ref[:, lanes].astype(F32), axis=1, keepdims=True)
        out_ref[:, lanes] = block * gain
    gain_out[...] = total


def finish_hidden(place, pieces, matrix, weight, gain):
    own, after, low, high, before = pieces
    at = lambda m: pl.BlockSpec((1, 2, FFL, B), lambda i, p: (m, 0, 0, 0))
    whole = lambda *shape: pl.BlockSpec(shape, lambda i, p: (0,) * len(shape))
    return pl.pallas_call(
        finish_hidden_kernel,
        grid_spec=pltpu.PrefetchScalarGridSpec(
            num_scalar_prefetch=1,
            grid=(1,),
            in_specs=[at(matrix), at(matrix), at(0), at(matrix), whole(B, FF), whole(B, 1)],
            out_specs=[whole(B, FF), whole(B, 1)],
            scratch_shapes=[pltpu.VMEM((FF, B), F32)],
        ),
        out_shape=[shaped(B, FF, kind=F32), shaped(B, 1, kind=F32)],
        compiler_params=params("arbitrary"),
        cost_estimate=cost(3 * 10**9, 6),
        name="finish_hidden",
    )(place, own, after, (low, high)[matrix], before, weight, gain)


def finish_down_kernel(place, own, after, low, high, before, out_ref):
    for refs, by in (((own, own), 0), ((after, after), 1), ((low, high), 2), ((before, before), 3)):
        rows = pl.ds(pl.multiple_of((place[1] + by) % 4 * PIECE, 8), PIECE)
        for half in range(2):
            slab = refs[half][half if by != 2 else 0].astype(F32)
            for t in range(8):
                lane = (half * 8 + t) * B
                out_ref[rows, lane : lane + B] = slab[t * PIECE : (t + 1) * PIECE]


def finish_down(place, pieces):
    halves = lambda n: pl.BlockSpec((n, FFL, B), lambda i, p: (0, 0, 0))
    return pl.pallas_call(
        finish_down_kernel,
        grid_spec=pltpu.PrefetchScalarGridSpec(
            num_scalar_prefetch=1,
            grid=(1,),
            in_specs=[halves(2), halves(2), halves(1), halves(1), halves(2)],
            out_specs=pl.BlockSpec((4 * PIECE, D), lambda i, p: (0, 0)),
        ),
        out_shape=shaped(4 * PIECE, D, kind=F32),
        compiler_params=params("arbitrary"),
        cost_estimate=cost(2 * 10**9, 5),
        name="finish_down",
    )(place, *pieces)


def own_rows(rows_all, y, core, per):
    return lax.dynamic_slice_in_dim(rows_all, (2 * y + core) * per, per, 0)


def resumed(steps, arrived):
    try:
        while True:
            arrived = yield steps.send(arrived)
    except StopIteration as end:
        return end.value


class Flow:
    def __init__(self, steps):
        self.steps, self.result, self.sent = steps, None, None
        self.move(None)

    def move(self, arrived):
        try:
            self.sent = self.steps.send(arrived)
        except StopIteration as end:
            self.sent, self.result = (), end.value


def stage(flows, *values):
    flows = [flow for flow in flows if flow.result is None]
    sizes = [len(flow.sent) for flow in flows]
    leaves, tree = jax.tree.flatten(values)
    tied = tie(*[v for flow in flows for v in flow.sent], *leaves)
    for flow, size in zip(flows, sizes):
        flow.move(tied[:size])
        tied = tied[size:]
    return jax.tree.unflatten(tree, tied)


def gather_steps(block):
    (other,) = yield (swap_core(block),)
    pair = jnp.stack([block, other])
    (got,) = yield (along_y(pair),)
    far, swapped = yield (along_y(send_half(got)), swap_core(got))
    (far_swapped,) = yield (swap_core(far),)
    return pair, got, swapped, far, far_swapped


def scatter_steps(parts, held=0):
    core = lax.axis_index("core")
    first, behind, ahead, far, far_other = parts
    (far_got,) = yield (swap_core(far_other),)
    far = add(far, far_got).astype(BF16)
    low, behind_got, first_got = yield (along_y(far), swap_core(behind), swap_core(first))
    ahead = add(ahead, behind_got).astype(BF16)
    mine = add(lax.dynamic_slice_in_dim(ahead, core * (B // 2), B // 2, 1), low).astype(BF16)
    ahead = lax.dynamic_update_slice_in_dim(ahead, mine, core * (B // 2), 1)
    for _ in range(held):
        yield ()
    (got,) = yield (along_y(ahead),)
    (last,) = yield (swap_core(got),)
    return add(first[0], first_got[1]) + add(got[0], last[1])


def ring_gather_steps(block, axis):
    half = block.shape[0] // 2
    before, after = yield (shift(block, axis, 1), shift(block, axis, -1))
    low, high = yield (shift(before[:half], axis, 1), shift(after[half:], axis, -1))
    return block, after, low, high, before


def ring_scatter_steps(parts, axis):
    half = parts[2].shape[0] // 2
    low, high = yield (shift(parts[2][:half], axis, 1), shift(parts[2][half:], axis, -1))
    after = jnp.concatenate([add(parts[1][:half], low).astype(BF16), parts[1][half:]], axis=0)
    before = jnp.concatenate([parts[3][:half], add(parts[3][half:], high).astype(BF16)], axis=0)
    from_before, from_after = yield (shift(after, axis, 1), shift(before, axis, -1))
    return add(parts[0], from_before) + from_after.astype(F32)


def on_device(
    layer_input,
    positions,
    attn_gain,
    w_query,
    w_key,
    w_value,
    w_output,
    mlp_gain,
    w_gate,
    w_up,
    w_down,
    out_grad,
):
    zlo, y, zhi, x, core = (lax.axis_index(axis) for axis in AXES)
    place = jnp.stack([zlo, y, core, x, zhi]).astype(jnp.int32)

    def by_core(mine, got):
        return jnp.where(core == 0, jnp.stack([mine, got]), jnp.stack([got, mine]))

    def by_zlo(mine, got):
        return jnp.where(zlo == 0, jnp.stack([mine, got]), jnp.stack([got, mine]))

    def by_zhi(mine, got):
        return jnp.where(zhi == 0, jnp.stack([mine, got]), jnp.stack([got, mine]))

    def trio(mine, other, axis):
        across = lax.ppermute(other, (axis, "core"), [(i, 3 - i) for i in range(4)])
        return shift(mine, axis, 1), swap_core(other), across

    def column_steps(mine, got):
        pair = by_core(mine, got)
        (got,) = yield (shift(pair, "zhi", 1),)
        return (yield from ring_gather_steps(by_zhi(pair, got), "x"))

    def output_steps(mine, other):
        there, here, across = yield trio(mine, other, "zhi")
        column = by_zhi(by_core(mine, here), by_core(there, across))
        return (yield from ring_gather_steps(column, "x"))

    def hidden_steps(mine, got, down):
        piece = jnp.concatenate([by_core(mine, got).reshape(2 * FFL, B), down], axis=0)
        pieces = yield from ring_gather_steps(piece, "z")
        return jnp.concatenate(pieces, axis=0).reshape(4, 3 * FFL, B)

    def of_core(pair, other=False):
        return lax.dynamic_index_in_dim(pair, 1 - core if other else core, 0, keepdims=False)

    def whole_ring(pieces):
        own, after, low, high, before = pieces
        return own, after, jnp.concatenate([low, high], axis=0), before

    def attention_steps(column):
        keep = lax.dynamic_index_in_dim(column, zhi, 0, keepdims=False)
        send = lax.dynamic_index_in_dim(column, 1 - zhi, 0, keepdims=False)
        (got,) = yield (shift(send, "zhi", 1),)
        pair = add(keep, got).astype(BF16)
        mine, other = of_core(pair), of_core(pair, True)
        there, here, across = yield trio(mine, other, "zlo")
        own = by_core(add(mine, there), add(here, across)).astype(BF16)
        return (yield from ring_gather_steps(own, "y"))

    def gate_up_steps(sums):
        own = yield from ring_scatter_steps([sums[i] for i in range(4)], "z")
        pair = own.astype(BF16).reshape(2, FFL, B)
        mine, other = of_core(pair), of_core(pair, True)
        there, here, across = yield trio(mine, other, "zlo")
        block = by_zlo(by_core(mine, here), by_core(there, across))
        before, after = yield (shift(block, "y", 1), shift(block, "y", -1))
        low, high = yield (shift(before[:1], "y", 1), shift(after[1:], "y", -1))
        return block, after, low, high, before

    def down_steps(sums):
        steps = ring_scatter_steps([sums[i] for i in range(4)], "z")
        arrived = yield next(steps)
        yield ()
        own = yield from resumed(steps, arrived)
        own = own.astype(BF16)
        (got,) = yield (shift(own, "zlo", 1),)
        return (yield from ring_gather_steps(by_zlo(own, got), "y"))

    x_low = layer_input[0]
    frequency = theta ** (-jnp.arange(0, HD, 2).astype(F32) / HD)
    angles = positions[0].astype(F32)[:, None] * frequency
    tables = []
    for table in (jnp.cos(angles), jnp.sin(angles)):
        high = lax.reduce_precision(table, 8, 7)
        tables += [high.astype(BF16), (table - high).astype(BF16)]
    tokens = Flow(gather_steps(jnp.concatenate([x_low, *tables], axis=1)))
    grads = Flow(gather_steps(out_grad[0]))
    qkv_mine, qkv_other = prepare_qkv(place, w_query, w_key, w_value, attn_gain[:, None])
    qkv_mine, qkv_got, gain_two, w_out = stage([tokens], qkv_mine, swap_core(qkv_other), mlp_gain[:, None], w_output)

    columns = Flow(column_steps(qkv_mine, qkv_got))
    o_rows = lax.all_to_all(w_out.reshape(B, 16, B).transpose(1, 0, 2), FSDP, 0, 0, tiled=True)
    ff_mine, ff_other, ff_down = prepare_ff(place, w_gate, w_up, w_down, gain_two)
    ff_mine, ff_got, ff_down, x_low, o_rows = stage(
        [tokens, columns], ff_mine, swap_core(ff_other), ff_down, x_low, o_rows
    )

    inputs = x_low.astype(F32)
    scale_one = lax.rsqrt(jnp.mean(inputs * inputs, axis=-1, keepdims=True) + eps)
    o_rows = o_rows.reshape(D, B)
    mine, other = own_rows(o_rows, y, core, HEADS * HD), own_rows(o_rows, y, 1 - core, HEADS * HD)
    scale_one, mine, other, ff_mine, ff_got, ff_down = stage(
        [tokens, columns, grads], scale_one, mine, other, ff_mine, ff_got, ff_down
    )

    outputs = Flow(output_steps(mine, other))
    ff_mine, ff_got, ff_down = stage([tokens, columns, outputs], ff_mine, ff_got, ff_down)

    hidden_rows = Flow(hidden_steps(ff_mine, ff_got, ff_down))
    x_pieces = tokens.result
    query, key_value, scale_all, cosine, sine, qkv_full = project_qkv(place, x_pieces, columns.result)
    query, key_value = stage([hidden_rows, outputs, grads], query, key_value)

    earlier = lax.ppermute(key_value, "zlo", [(0, 1)])
    query, key_value, earlier = stage([outputs, hidden_rows], query, key_value, earlier)
    ff_all = lax.all_gather(hidden_rows.result, "x", axis=0, tiled=False)

    key_value = jnp.concatenate([earlier, key_value], axis=1)
    mixed, log_total, *parts, o_full = attention(place, outputs.result, query, key_value)
    parts = stage([grads], *parts)
    sums = Flow(scatter_steps(parts))
    stage([sums, grads])
    grad_pieces = grads.result
    for _ in range(3):
        stage([sums])
    hidden = inputs + sums.result
    scale_two = lax.rsqrt(jnp.mean(hidden * hidden, axis=-1, keepdims=True) + eps)
    normed = Flow(gather_steps((hidden * scale_two).astype(BF16)))
    for _ in range(4):
        stage([normed])
    normed_pieces = normed.result

    activation, act_t, gate_t, up_t, *parts, down_full = feed_forward(place, normed_pieces, grad_pieces, ff_all)
    sums = Flow(scatter_steps(parts))
    (act_t,) = stage([sums], act_t)
    down_terms = ff_terms(down_kernel, place, grad_pieces, (act_t,), FFL, "down_terms")
    down_terms, gate_t = stage([sums], down_terms, gate_t)
    down_sum = lax.psum_scatter(down_terms, "x", scatter_dimension=0, tiled=True)[0]
    gate_up_terms = ff_terms(gate_up_kernel, place, normed_pieces, (gate_t, up_t), 2 * FFL, "gate_up_terms")
    (gate_up_terms,) = stage([sums], gate_up_terms)
    gate_up_sum = lax.psum_scatter(gate_up_terms, "x", scatter_dimension=0, tiled=True)[0]
    stage([sums])

    grad_normed_two = sums.result
    mean_two = jnp.mean(grad_normed_two * hidden, axis=-1, keepdims=True)
    grad_hidden = (
        out_grad[0].astype(F32)
        + scale_two * grad_normed_two
        - hidden * (scale_two * scale_two * scale_two) * mean_two
    )
    hidden_grads = Flow(gather_steps(grad_hidden.astype(BF16)))
    (activation,) = stage([hidden_grads], activation)
    down_parts = project(activation, down_full)
    *down_parts, down_sum = stage([hidden_grads], *down_parts, down_sum)
    result = Flow(scatter_steps(down_parts))
    down = Flow(down_steps(down_sum))
    stage([hidden_grads, down])
    stage([hidden_grads, result])

    hidden_grad_pieces = hidden_grads.result
    grad_query, grad_earlier, grad_own = attention_back(
        place, hidden_grad_pieces, query, key_value, log_total, o_full
    )
    grad_query, grad_earlier, grad_own, mixed = stage([result, down], grad_query, grad_earlier, grad_own, mixed)

    later = lax.ppermute(grad_earlier, "zlo", [(1, 0)])
    output_terms = attention_terms(
        place, hidden_grad_pieces, mixed.reshape(2 * HALF, HEADS * HD), "output_terms"
    )
    later, grad_query, output_terms, gate_up_sum = stage(
        [down], later, grad_query, output_terms, gate_up_sum
    )

    output_sum = lax.psum_scatter(output_terms, "x", scatter_dimension=0, tiled=True)[0]
    gate_up = Flow(gate_up_steps(gate_up_sum))
    grad_pre, terms = qkv_back(place, x_pieces, grad_query, grad_own, later, cosine, sine, scale_all)
    grad_pre, terms = stage([gate_up, down, result], grad_pre, terms)

    attention_sum = lax.psum_scatter(terms, "x", scatter_dimension=0, tiled=True)[0]
    parts = project(grad_pre, qkv_full)
    *parts, output_sum = stage([gate_up, down, result], *parts, output_sum)

    sums = Flow(scatter_steps(parts, 2))
    output_sums = Flow(attention_steps(output_sum))
    (attention_sum,) = stage([sums, gate_up, output_sums, down], attention_sum)
    attention_sums = Flow(attention_steps(attention_sum))
    stage([sums, output_sums, attention_sums])
    down_grad = finish_down(place, down.result)
    layer_output = (hidden + result.result).astype(BF16)
    down_grad, layer_output = stage([sums, output_sums, attention_sums, gate_up], down_grad, layer_output)
    stage([sums, output_sums, attention_sums, gate_up])

    ring = jnp.roll(jnp.stack(whole_ring(output_sums.result)), y, axis=0).reshape(16, B, B)
    output_grad = lax.all_to_all(ring, FSDP, 0, 0, tiled=True)
    gain_two = mlp_gain[:, None]
    gate_grad, gate_gain = finish_hidden(place, gate_up.result, 0, w_gate, gain_two)
    up_grad, up_gain = finish_hidden(place, gate_up.result, 1, w_up, gain_two)
    gate_grad, up_grad, output_grad = stage([sums, attention_sums], gate_grad, up_grad, output_grad)
    stage([sums])
    grad_normed = sums.result
    mean_one = jnp.mean(grad_normed * inputs, axis=-1, keepdims=True)
    input_grad = (
        grad_hidden
        + scale_one * grad_normed
        - inputs * (scale_one * scale_one * scale_one) * mean_one
    )
    input_grad = input_grad.astype(BF16)
    query_grad, key_grad, value_grad, attn_gain_grad = finish_attention(
        place, whole_ring(attention_sums.result), w_query, w_key, w_value, attn_gain[:, None]
    )
    output_grad = finish_output(output_grad)
    return (
        layer_output[None],
        input_grad[None],
        attn_gain_grad[:, 0],
        query_grad,
        key_grad,
        value_grad,
        output_grad,
        (gate_gain + up_gain)[:, 0],
        gate_grad,
        up_grad,
        down_grad,
    )


def solution(mesh):
    split = Mesh(mesh.devices.reshape(2, 4, 2, 4, 2), AXES)
    tokens = P(FSDP, SEQ, None)
    rows = P(FSDP, None)
    gain = P(FSDP)
    in_specs = (
        tokens, P(FSDP, SEQ), gain, rows, rows, rows, rows, gain, rows, rows, rows, tokens,
    )
    out_specs = (tokens, tokens, gain, rows, rows, rows, rows, gain, rows, rows, rows)
    return jax.shard_map(
        on_device, mesh=split, in_specs=in_specs, out_specs=out_specs, check_vma=False
    )
```

```python
import jax
import jax.numpy as jnp
from jax import lax
from jax.experimental import pallas as pl
from jax.experimental.pallas import tpu as pltpu
from jax.sharding import Mesh
from jax.sharding import PartitionSpec as P

H = 32
KV = 4
HD = 64
D = 2048
FF = 5632
B = 128
HALF = 512
HEADS = 4
FFL = 704
PIECE = 88

eps = 1e-05
theta = 10000.0
F32 = jnp.float32
BF16 = jnp.bfloat16
AXES = ("zlo", "y", "zhi", "x", "core")
FSDP = ("zhi", "x", "core")
SEQ = ("zlo", "y")


def matmul(left, right):
    return jnp.dot(left, right, preferred_element_type=F32)


def times_transposed(left, right):
    return lax.dot_general(left, right, (((1,), (1,)), ((), ())), preferred_element_type=F32)


def outer_sum(left, right):
    return lax.dot_general(left, right, (((0,), (0,)), ((), ())), preferred_element_type=F32)


def shift(value, axis, by):
    if axis == "z":
        at = [2 * (z % 2) + z // 2 for z in range(4)]
        return lax.ppermute(value, ("zlo", "zhi"), [(at[z], at[(z + by) % 4]) for z in range(4)])
    size = lax.axis_size(axis)
    return lax.ppermute(value, axis, [(i, (i + by) % size) for i in range(size)])


def swap_core(value):
    return shift(value, "core", 1)


def small_gather(block, axis):
    return shift(block, axis, -1), shift(block, axis, 2), shift(block, axis, 1)


def tie(*values):
    return lax.optimization_barrier(values)


def add(left, right):
    return left.astype(F32) + right.astype(F32)


def along_y(value):
    pairs = []
    for i in range(4):
        pairs.append((2 * i, 2 * ((i + 1) % 4)))
        pairs.append((2 * i + 1, 2 * ((i + 3) % 4) + 1))
    return lax.ppermute(value, ("y", "core"), pairs)


def send_half(got):
    core = lax.axis_index("core")
    return lax.dynamic_slice_in_dim(got, core * (B // 2), B // 2, 1)


FLIPPED = (0, 0, 1, 0, 1)
LENGTHS = (B, B, B, B // 2, B // 2)


def put_tokens(refs, rows_ref, sems, start):
    lanes = pl.ds(0, rows_ref.shape[1])
    copies = []
    row = 0
    for s in range(2):
        for ref, flip, length in zip(refs, FLIPPED, LENGTHS):
            copies.append(
                pltpu.make_async_copy(
                    ref.at[s ^ flip, :, lanes], rows_ref.at[pl.ds(row, length)], sems.at[start + len(copies)]
                )
            )
            row += length
    return copies


TILE = 256
WIDE = D + B
VMEM_LIMIT = 56 * 2**20
ANYWHERE = pl.BlockSpec(memory_space=pl.ANY)


def params(*kinds):
    return pltpu.CompilerParams(dimension_semantics=kinds or None, vmem_limit_bytes=VMEM_LIMIT)


def cost(flops, megabytes):
    return pl.CostEstimate(flops=flops, bytes_accessed=int(megabytes * 2**20), transcendentals=0)


def shaped(*shape, kind=BF16):
    return jax.ShapeDtypeStruct(shape, kind)


PARTS = ((B, False), (B, True), (B, False), (B // 2, False), (B // 2, True))
PART_SHAPES = [jax.ShapeDtypeStruct((2, n, D), BF16) for n, _ in PARTS]


def part_specs(steps):
    def of(turn):
        return lambda i, *_: (1 - i // steps if turn else i // steps, 0, 0)

    return [pl.BlockSpec((1, n, D), of(turn)) for n, turn in PARTS]


def put_parts(step, tile, refs):
    @pl.when(step % 2 == 0)
    def _():
        refs[0][0] = tile[:B]
        refs[1][0] = tile[B:]

    @pl.when(step % 2 == 1)
    def _():
        refs[2][0] = tile[:B]
        refs[3][0] = tile[B : B + B // 2]
        refs[4][0] = tile[B + B // 2 :]


def put_rows(rows, refs):
    row = 0
    for ref, (length, _) in zip(refs, PARTS):
        ref[0] = rows[row : row + length]
        row += length


def turned(values):
    lane = lax.broadcasted_iota(jnp.int32, values.shape, 1) % HD
    return jnp.where(lane < HD // 2, -pltpu.roll(values, 2 * HD - HD // 2, 1), pltpu.roll(values, HD // 2, 1))


def lane_block(zhi, x, core):
    return pl.ds(pl.multiple_of((zhi * 8 + x * 2 + core) * B, B), B)


def put_columns(place, refs, into, sems, start):
    copies = []
    for ref, by, first in zip(refs, (0, 1, 2, 2, 3), (0, 0, 0, 1, 0)):
        for i in range(ref.shape[0]):
            for core in range(2):
                lanes = lane_block(first + i, (place[3] + by) % 4, core)
                copies.append(
                    pltpu.make_async_copy(ref.at[i, core], into.at[:, lanes], sems.at[start + len(copies)])
                )
    return copies


def prepare_qkv_kernel(place, q_mine, q_other, w_key, w_value, gain, mine_ref, other_ref, k_rows, v_rows):
    scale = gain[...]
    k_rows[...] = (w_key[...].astype(F32) * scale).T
    v_rows[...] = (w_value[...].astype(F32) * scale).T
    rows = pl.ds(pl.multiple_of(place[1] * HD, HD), HD)
    for source, out in ((q_mine, mine_ref), (q_other, other_ref)):
        out[: HEADS * HD] = (source[...].astype(F32) * scale).T.astype(BF16)
        out[HEADS * HD : (HEADS + 1) * HD] = k_rows[rows].astype(BF16)
        out[(HEADS + 1) * HD :] = v_rows[rows].astype(BF16)


QKV = (HEADS + 2) * HD


def prepare_qkv(place, w_query, w_key, w_value, gain):
    whole = lambda *shape: pl.BlockSpec(shape, lambda i, p: (0,) * len(shape))
    return pl.pallas_call(
        prepare_qkv_kernel,
        grid_spec=pltpu.PrefetchScalarGridSpec(
            num_scalar_prefetch=1,
            grid=(1,),
            in_specs=[
                pl.BlockSpec((B, HEADS * HD), lambda i, p: (0, 2 * p[1] + p[2])),
                pl.BlockSpec((B, HEADS * HD), lambda i, p: (0, 2 * p[1] + 1 - p[2])),
                whole(B, KV * HD), whole(B, KV * HD), whole(B, 1),
            ],
            out_specs=[whole(QKV, B), whole(QKV, B)],
            scratch_shapes=[pltpu.VMEM((KV * HD, B), F32), pltpu.VMEM((KV * HD, B), F32)],
        ),
        out_shape=[shaped(QKV, B), shaped(QKV, B)],
        compiler_params=params("arbitrary"),
        cost_estimate=cost(0, 1),
        name="prepare_qkv",
    )(place, w_query, w_query, w_key, w_value, gain)


def prepare_ff_kernel(place, w_gate, w_up, w_down, gain, mine_ref, other_ref, down_ref, picked, rows, down_rows, sems):
    zlo, y, core = place[0], place[1], place[2]
    down = pltpu.make_async_copy(
        w_down.at[:, pl.ds(pl.multiple_of(zlo * (D // 2), D // 2), D // 2)], down_rows, sems.at[1]
    )
    down.start()

    @pl.when(zlo == 0)
    def _():
        copy = pltpu.make_async_copy(w_gate, picked, sems.at[0])
        copy.start()
        copy.wait()

    @pl.when(zlo == 1)
    def _():
        copy = pltpu.make_async_copy(w_up, picked, sems.at[0])
        copy.start()
        copy.wait()

    scale = gain[...]
    for i in range(FF // B):
        rows[i * B : (i + 1) * B] = (picked[:, i * B : (i + 1) * B].astype(F32) * scale).T
    for which, out in ((core, mine_ref), (1 - core, other_ref)):
        slabs = []
        for zx in range(8):
            at = pl.multiple_of(zx * 2 * 4 * PIECE + which * 4 * PIECE + y * PIECE, 8)
            slabs.append(rows[pl.ds(at, PIECE)])
        out[...] = jnp.concatenate(slabs, axis=0).astype(BF16)
    down.wait()
    for t in range(8):
        rows[t * 4 * PIECE : (t + 1) * 4 * PIECE] = down_rows[:, t * B : (t + 1) * B].astype(F32)
    slabs = [rows[pl.ds(pl.multiple_of(t * 4 * PIECE + y * PIECE, 8), PIECE)] for t in range(8)]
    down_ref[...] = jnp.concatenate(slabs, axis=0).astype(BF16)


def prepare_ff(place, w_gate, w_up, w_down, gain):
    return pl.pallas_call(
        prepare_ff_kernel,
        grid_spec=pltpu.PrefetchScalarGridSpec(
            num_scalar_prefetch=1,
            grid=(1,),
            in_specs=[ANYWHERE, ANYWHERE, ANYWHERE, pl.BlockSpec((B, 1), lambda i, p: (0, 0))],
            out_specs=[pl.BlockSpec((FFL, B), lambda i, p: (0, 0))] * 3,
            scratch_shapes=[
                pltpu.VMEM((B, FF), BF16),
                pltpu.VMEM((FF, B), F32),
                pltpu.VMEM((4 * PIECE, D // 2), BF16),
                pltpu.SemaphoreType.DMA((2,)),
            ],
        ),
        out_shape=[shaped(FFL, B)] * 3,
        compiler_params=params("arbitrary"),
        cost_estimate=cost(0, 6),
        name="prepare_ff",
    )(place, w_gate, w_up, w_down, gain)


def project_qkv_kernel(*refs):
    place, x_refs, w_refs = refs[0], refs[1:6], refs[6:11]
    query_ref, kv_ref, scale_ref, cosine_ref, sine_ref, w_out, rows, weights, sems = refs[11:]
    step = pl.program_id(0)
    tokens = put_tokens(x_refs, rows, sems, 0)
    columns = put_columns(place, w_refs, weights, sems, 10)
    back = pltpu.make_async_copy(weights, w_out, sems.at[26])

    @pl.when(step == 0)
    def _():
        for copy in columns + tokens:
            copy.start()
        for copy in columns:
            copy.wait()
        back.start()
        for copy in tokens:
            copy.wait()

    at = pl.ds(pl.multiple_of(step * TILE, TILE), TILE)
    tile = rows[at, :D]
    wide = tile.astype(F32)
    scale = lax.rsqrt(jnp.mean(wide * wide, axis=-1, keepdims=True) + eps)
    scale_ref[...] = scale
    pre = times_transposed(tile, weights[...]) * scale
    tables = rows[at, D:].astype(F32)
    tables = tables + pltpu.roll(tables, B - HD // 2, 1)
    cosine = jnp.concatenate([tables[:, : HD // 2]] * 4, axis=1)
    sine = jnp.concatenate([tables[:, HD : HD + HD // 2]] * 4, axis=1)
    cosine_ref[...] = cosine
    sine_ref[...] = sine
    for i in range(2):
        part = pre[:, i * 2 * HD : (i + 1) * 2 * HD]
        part = (part * cosine + turned(part) * sine).astype(BF16) * HD ** (-0.5)
        query_ref[0, 2 * i] = part[:, :HD]
        query_ref[0, 2 * i + 1] = part[:, HD:]
    part = pre[:, HEADS * HD :]
    lane = lax.broadcasted_iota(jnp.int32, part.shape, 1)
    kv_ref[0] = jnp.where(lane < HD, part * cosine + turned(part) * sine, part).astype(BF16)

    @pl.when(step == 3)
    def _():
        back.wait()


def project_qkv(place, x_pieces, w_pieces):
    tile = lambda lanes: pl.BlockSpec((TILE, lanes), lambda i, p: (i, 0))
    return pl.pallas_call(
        project_qkv_kernel,
        grid_spec=pltpu.PrefetchScalarGridSpec(
            num_scalar_prefetch=1,
            grid=(4,),
            in_specs=[ANYWHERE] * 10,
            out_specs=[
                pl.BlockSpec((1, HEADS, TILE, HD), lambda i, p: (i // 2, 0, i % 2, 0)),
                pl.BlockSpec((1, TILE, 2 * HD), lambda i, p: (i // 2, i % 2, 0)),
                tile(1), tile(2 * HD), tile(2 * HD),
                ANYWHERE,
            ],
            scratch_shapes=[
                pltpu.VMEM((2 * HALF, WIDE), BF16),
                pltpu.VMEM((QKV, D), BF16),
                pltpu.SemaphoreType.DMA((27,)),
            ],
        ),
        out_shape=[
            shaped(2, HEADS, HALF, HD), shaped(2, HALF, 2 * HD), shaped(2 * HALF, 1, kind=F32),
            shaped(2 * HALF, 2 * HD, kind=F32), shaped(2 * HALF, 2 * HD, kind=F32), shaped(QKV, D),
        ],
        compiler_params=params("arbitrary"),
        cost_estimate=cost(2 * 2 * HALF * QKV * D, 8),
        name="project_qkv",
    )(place, *x_pieces, *w_pieces)


def project_kernel(left_ref, weight_ref, *parts):
    put_parts(pl.program_id(0), matmul(left_ref[...], weight_ref[...]).astype(BF16), parts)


def project(left, weight):
    depth = left.shape[1]
    return pl.pallas_call(
        project_kernel,
        grid=(4,),
        in_specs=[pl.BlockSpec((TILE, depth), lambda i: (i, 0)), pl.BlockSpec((depth, D), lambda i: (0, 0))],
        out_specs=part_specs(2),
        out_shape=PART_SHAPES,
        compiler_params=params("arbitrary"),
        cost_estimate=cost(2 * 2 * HALF * depth * D, 8),
        name="project",
    )(left, weight)


def put_term(left, rows, term_ref):
    def one(i, carry):
        term = matmul(left, rows[:, pl.ds(pl.multiple_of(i * 4 * B, 4 * B), 4 * B)]).astype(BF16)
        for j in range(2):
            zx = 2 * i + j
            term_ref[zx % 4, zx // 4, 0] = term[:, 2 * j * B : (2 * j + 1) * B]
            term_ref[zx % 4, zx // 4, 1] = term[:, (2 * j + 1) * B : (2 * j + 2) * B]
        return carry

    lax.fori_loop(0, 4, one, 0)


def qkv_back_kernel(*refs):
    x_refs, grad_q, own, later, cosine_ref, sine_ref, scale_ref = refs[1:6], *refs[6:12]
    grad_ref, term_ref, rows, left, sems = refs[12:]
    copies = put_tokens(x_refs, rows, sems, 0)
    for copy in copies:
        copy.start()
    for step in range(4):
        at, s = slice(step * TILE, (step + 1) * TILE), step // 2
        inner = slice(step % 2 * TILE, (step % 2 + 1) * TILE)
        cosine, sine = cosine_ref[at], sine_ref[at]
        pieces = []
        for i in range(2):
            part = grad_q[s, inner, i * 2 * HD : (i + 1) * 2 * HD]
            pieces.append(part * cosine - turned(part * sine))
        lane = lax.broadcasted_iota(jnp.int32, cosine.shape, 1)
        part = own[s, inner] + later[s, inner].astype(F32)
        pieces.append(jnp.where(lane < HD, part * cosine - turned(part * sine), part))
        grad_pre = jnp.concatenate(pieces, axis=1)
        grad_ref[at] = grad_pre.astype(BF16)
        left[:, at] = (grad_pre * scale_ref[at]).T.astype(BF16)
    for copy in copies:
        copy.wait()
    put_term(left[...], rows, term_ref)


def qkv_back(place, x_pieces, grad_query, own, later, cosine, sine, scale):
    whole = lambda *shape: pl.BlockSpec(shape, lambda i, p: (0,) * len(shape))
    tokens = 2 * HALF
    return pl.pallas_call(
        qkv_back_kernel,
        grid_spec=pltpu.PrefetchScalarGridSpec(
            num_scalar_prefetch=1,
            grid=(1,),
            in_specs=[ANYWHERE] * 5
            + [
                whole(2, HALF, HEADS * HD), whole(2, HALF, 2 * HD), whole(2, HALF, 2 * HD),
                whole(tokens, 2 * HD), whole(tokens, 2 * HD), whole(tokens, 1),
            ],
            out_specs=[whole(tokens, QKV), whole(4, 2, 2, QKV, B)],
            scratch_shapes=[
                pltpu.VMEM((tokens, D), BF16), pltpu.VMEM((QKV, tokens), BF16), pltpu.SemaphoreType.DMA((10,)),
            ],
        ),
        out_shape=[shaped(tokens, QKV), shaped(4, 2, 2, QKV, B)],
        compiler_params=params("arbitrary"),
        cost_estimate=cost(2 * tokens * QKV * D, 9),
        name="qkv_back",
    )(place, *x_pieces, grad_query, own, later, cosine, sine, scale)


def attention_term_kernel(*refs):
    token_refs, left_ref = refs[1:6], refs[6]
    term_ref, rows, sems = refs[-3:]
    copies = put_tokens(token_refs, rows, sems, 0)
    for copy in copies:
        copy.start()
    left = left_ref[...]
    if left.shape[0] == 2 * HALF:
        left = left.T
    for copy in copies:
        copy.wait()
    put_term(left, rows, term_ref)


def attention_terms(place, pieces, left, name):
    whole = lambda *shape: pl.BlockSpec(shape, lambda i, p: (0,) * len(shape))
    rows = min(left.shape)
    return pl.pallas_call(
        attention_term_kernel,
        grid_spec=pltpu.PrefetchScalarGridSpec(
            num_scalar_prefetch=1,
            grid=(1,),
            in_specs=[ANYWHERE] * 5 + [whole(*left.shape)],
            out_specs=whole(4, 2, 2, rows, B),
            scratch_shapes=[pltpu.VMEM((2 * HALF, D), BF16), pltpu.SemaphoreType.DMA((10,))],
        ),
        out_shape=shaped(4, 2, 2, rows, B),
        compiler_params=params("arbitrary"),
        cost_estimate=cost(2 * 2 * HALF * rows * D, 7),
        name=name,
    )(place, *pieces, left)


def token_places(at, y, core):
    step = 1 - 2 * core
    block = jnp.where(
        at < B, y, jnp.where(at < 2 * B, y + 4 - step, jnp.where(at < 3 * B, y + 4 + step, y + 2))
    )
    row = at % B
    row = jnp.where(at < 3 * B, row, (row + core * (B // 2)) % B)
    return (block % 4) * B + row


def set_bias(place_ref, bias_ref):
    zlo, y, core = place_ref[0], place_ref[1], place_ref[2]
    key_at = token_places(lax.broadcasted_iota(jnp.int32, (HALF, 1), 0), y, core)
    query_at = token_places(lax.broadcasted_iota(jnp.int32, (1, HALF), 1), y, core)
    bias_ref[:HALF, :] = jnp.broadcast_to(jnp.where(zlo == 1, 0.0, -1e30), (HALF, HALF))
    bias_ref[HALF:, :] = jnp.where(key_at <= query_at, 0.0, -1e30)


def attention_kernel(place_ref, *refs):
    w_refs, query_ref, kv_ref, mixed_ref, log_ref = refs[:5], *refs[5:9]
    parts, w_out, bias_ref, weight, sems = refs[9:14], *refs[14:]
    columns = put_columns(place_ref, w_refs, weight, sems, 0)
    back = pltpu.make_async_copy(weight, w_out, sems.at[16])

    @pl.when(pl.program_id(0) == 0)
    def _():
        for copy in columns:
            copy.start()
        set_bias(place_ref, bias_ref)
        for copy in columns:
            copy.wait()
        back.start()

    key, value = kv_ref[0, :, :HD], kv_ref[0, :, HD:]
    for head in range(HEADS):
        scores = times_transposed(key, query_ref[0, head]) + bias_ref[...]
        top = jnp.max(scores, axis=0, keepdims=True)
        weights = jnp.exp(scores - top)
        total = jnp.sum(weights, axis=0, keepdims=True)
        low = (weights * (1.0 / total)).astype(BF16)
        mixed_ref[0, :, head * HD : (head + 1) * HD] = outer_sum(value, low).T.astype(BF16)
        log_ref[0, head] = top + jnp.log(total)
    put_rows(matmul(mixed_ref[0], weight[...]).astype(BF16), parts)

    @pl.when(pl.program_id(0) == 1)
    def _():
        back.wait()


def attention_back_kernel(place_ref, *refs):
    grad_refs, query_ref, kv_ref, log_ref, weight_ref = refs[:5], *refs[5:9]
    grad_query_ref, earlier_ref, own_ref, bias_ref, rows, sems = refs[9:]
    step = pl.program_id(0)
    copies = put_tokens(grad_refs, rows, sems, 0)

    @pl.when(step == 0)
    def _():
        for copy in copies:
            copy.start()
        set_bias(place_ref, bias_ref)
        for copy in copies:
            copy.wait()

    hidden = rows[pl.ds(pl.multiple_of(step * HALF, HALF), HALF), :]
    grads = times_transposed(hidden, weight_ref[...]).astype(BF16)
    key, value = kv_ref[0, :, :HD], kv_ref[0, :, HD:]
    grad_key = jnp.zeros((2 * HALF, HD), F32)
    grad_value = jnp.zeros((2 * HALF, HD), F32)
    for head in range(HEADS):
        lanes = slice(head * HD, (head + 1) * HD)
        query, grad = query_ref[0, head], grads[:, lanes]
        weights = jnp.exp(times_transposed(key, query) + bias_ref[...] - log_ref[0, head])
        grad_weights = times_transposed(value, grad)
        delta = jnp.sum(weights * grad_weights, axis=0, keepdims=True)
        grad_scores = (weights * (grad_weights - delta)).astype(BF16)
        grad_query_ref[0, :, lanes] = outer_sum(key, grad_scores).T * HD ** (-0.5)
        grad_key += matmul(grad_scores, query)
        grad_value += matmul(weights.astype(BF16), grad)
    total = jnp.concatenate([grad_key, grad_value], axis=1)
    earlier_ref[0] = total[:HALF].astype(BF16)
    own_ref[0] = total[HALF:]


def sequence_block(*tail):
    return pl.BlockSpec((1,) + tail, lambda s, place: (s,) + (0,) * len(tail))


def attention_call(kernel, in_specs, out_specs, out_shape, scratch, flops, name):
    return pl.pallas_call(
        kernel,
        grid_spec=pltpu.PrefetchScalarGridSpec(
            num_scalar_prefetch=1,
            grid=(2,),
            in_specs=in_specs,
            out_specs=out_specs,
            scratch_shapes=[pltpu.VMEM((2 * HALF, HALF), F32)] + scratch,
        ),
        out_shape=out_shape,
        compiler_params=params("arbitrary"),
        cost_estimate=cost(flops * 8 * 2 * HALF * HALF * HD * 2, 8),
        name=name,
    )


def attention(place, w_pieces, query, kv):
    return attention_call(
        attention_kernel,
        [ANYWHERE] * 5 + [sequence_block(HEADS, HALF, HD), sequence_block(2 * HALF, 2 * HD)],
        [sequence_block(HALF, HEADS * HD), sequence_block(HEADS, 1, HALF)]
        + part_specs(1)
        + [ANYWHERE],
        [shaped(2, HALF, HEADS * HD), shaped(2, HEADS, 1, HALF, kind=F32)] + PART_SHAPES + [shaped(HEADS * HD, D)],
        [pltpu.VMEM((HEADS * HD, D), BF16), pltpu.SemaphoreType.DMA((17,))],
        3,
        "attention",
    )(place, *w_pieces, query, kv)


def attention_back(place, grad_pieces, query, kv, log_total, weight):
    return attention_call(
        attention_back_kernel,
        [ANYWHERE] * 5
        + [
            sequence_block(HEADS, HALF, HD), sequence_block(2 * HALF, 2 * HD),
            sequence_block(HEADS, 1, HALF), pl.BlockSpec((HEADS * HD, D), lambda s, place: (0, 0)),
        ],
        [sequence_block(HALF, HEADS * HD), sequence_block(HALF, 2 * HD), sequence_block(HALF, 2 * HD)],
        [
            shaped(2, HALF, HEADS * HD, kind=F32),
            shaped(2, HALF, 2 * HD),
            shaped(2, HALF, 2 * HD, kind=F32),
        ],
        [pltpu.VMEM((2 * HALF, D), BF16), pltpu.SemaphoreType.DMA((10,))],
        6,
        "attention_back",
    )(place, *grad_pieces, query, kv, log_total, weight)


def finish_attention_kernel(place, *refs):
    piece_refs, w_query, w_key, w_value, gain_ref = refs[:4], *refs[4:8]
    query_out, key_out, value_out, gain_out, rows = refs[8:]
    for ref, by in zip(piece_refs, range(4)):
        at_y = (place[1] + by) % 4
        for c in range(2):
            piece = ref[c].astype(F32)
            rows[pl.ds(pl.multiple_of((2 * at_y + c) * HEADS * HD, HEADS * HD), HEADS * HD)] = piece[: HEADS * HD]
        both = ref[0].astype(F32) + ref[1].astype(F32)
        at = pl.multiple_of(H * HD + at_y * HD, HD)
        rows[pl.ds(at, HD)] = both[HEADS * HD : (HEADS + 1) * HD]
        rows[pl.ds(at + KV * HD, HD)] = both[(HEADS + 1) * HD :]
    gain = gain_ref[...]
    total = jnp.zeros((B, 1), F32)
    row = 0
    for weight, out in ((w_query, query_out), (w_key, key_out), (w_value, value_out)):
        for i in range(out.shape[1] // B):
            lanes = slice(i * B, (i + 1) * B)
            block = rows[row : row + B].T
            total = total + jnp.sum(block * weight[:, lanes].astype(F32), axis=1, keepdims=True)
            out[:, lanes] = block * gain
            row += B
    gain_out[...] = total


def finish_attention(place, pieces, w_query, w_key, w_value, gain):
    whole = lambda *shape: pl.BlockSpec(shape, lambda i, p: (0,) * len(shape))
    kv = KV * HD
    return pl.pallas_call(
        finish_attention_kernel,
        grid_spec=pltpu.PrefetchScalarGridSpec(
            num_scalar_prefetch=1,
            grid=(1,),
            in_specs=[whole(2, QKV, B)] * 4 + [whole(B, D), whole(B, kv), whole(B, kv), whole(B, 1)],
            out_specs=[whole(B, D), whole(B, kv), whole(B, kv), whole(B, 1)],
            scratch_shapes=[pltpu.VMEM((D + 2 * kv, B), F32)],
        ),
        out_shape=[
            shaped(B, D, kind=F32), shaped(B, kv, kind=F32), shaped(B, kv, kind=F32), shaped(B, 1, kind=F32),
        ],
        compiler_params=params("arbitrary"),
        cost_estimate=cost(0, 4),
        name="finish_attention",
    )(place, *pieces, w_query, w_key, w_value, gain)


def finish_output_kernel(blocks, out):
    for i in range(16):
        out[:, i * B : (i + 1) * B] = blocks[i].astype(F32)


def finish_output(blocks):
    return pl.pallas_call(
        finish_output_kernel,
        out_shape=shaped(B, D, kind=F32),
        compiler_params=params(),
        cost_estimate=cost(0, 2),
        name="finish_output",
    )(blocks)


def feed_forward_kernel(*refs):
    place, token_refs, grad_refs, ff_ref = refs[0], refs[1:6], refs[6:11], refs[11]
    act_ref, act_t, gate_t, up_t = refs[12:16]
    parts, down_out = refs[16:21], refs[21]
    rows_h, rows_g, gate_up, down, slabs, sems = refs[22:]
    step = pl.program_id(0)
    tokens = put_tokens(token_refs, rows_h, sems, 0)
    grads = put_tokens(grad_refs, rows_g, sems, 10)
    weights, loads = [], []
    for x in range(4):
        for by in range(4):
            z = (2 * place[4] + place[0] + by) % 4
            zhi, zlo = z // 2, z % 2
            for core in range(2):
                weights.append(
                    pltpu.make_async_copy(
                        ff_ref.at[x, by, pl.ds(core * FFL, FFL)],
                        gate_up.at[zlo, :, lane_block(zhi, x, core)],
                        sems.at[20 + len(weights)],
                    )
                )
            loads.append(
                pltpu.make_async_copy(
                    ff_ref.at[x, by, pl.ds(2 * FFL, FFL)], slabs.at[zlo, zhi * 4 + x], sems.at[52 + len(loads)]
                )
            )
    back = pltpu.make_async_copy(down, down_out, sems.at[68])

    @pl.when(step == 0)
    def _():
        for copy in tokens + weights + loads + grads:
            copy.start()
        for copy in tokens + weights:
            copy.wait()

    rows = pl.ds(pl.multiple_of(step * HALF, HALF), HALF)
    normed = rows_h[rows, :]
    gate_pre = times_transposed(normed, gate_up[0])
    upward = times_transposed(normed, gate_up[1])

    @pl.when(step == 0)
    def _():
        for copy in loads:
            copy.wait()

        def put(q, carry):
            for half in range(2):
                for p in range(4):
                    one = slabs[half, 2 * q, 2 * p * PIECE : 2 * (p + 1) * PIECE, :].astype(F32)
                    two = slabs[half, 2 * q + 1, 2 * p * PIECE : 2 * (p + 1) * PIECE, :].astype(F32)
                    lane = (half * 8 + 2 * p) * B
                    rows = pl.ds(pl.multiple_of(q * 2 * PIECE, 16), 2 * PIECE)
                    down[rows, lane : lane + B] = jnp.concatenate([one[:PIECE], two[:PIECE]], axis=0).astype(BF16)
                    down[rows, lane + B : lane + 2 * B] = jnp.concatenate(
                        [one[PIECE:], two[PIECE:]], axis=0
                    ).astype(BF16)
            return carry

        lax.fori_loop(0, 4, put, 0)
        back.start()
        for copy in grads:
            copy.wait()

    grad_act = times_transposed(rows_g[rows, :], down[...])
    sigmoid = 1.0 / (1.0 + jnp.exp(-gate_pre))
    silu = gate_pre * sigmoid
    activation = silu * upward
    grad_up = grad_act * silu
    grad_gate = grad_act * upward * (sigmoid * (1.0 + gate_pre * (1.0 - sigmoid)))
    part = matmul(grad_gate.astype(BF16), gate_up[0]) + matmul(grad_up.astype(BF16), gate_up[1])
    put_rows(part.astype(BF16), parts)
    act_ref[...] = activation.astype(BF16)
    act_t[...] = activation.T.astype(BF16)
    gate_t[...] = grad_gate.T.astype(BF16)
    up_t[...] = grad_up.T.astype(BF16)

    @pl.when(step == 1)
    def _():
        back.wait()


def feed_forward(place, tokens, grads, ff_all):
    turned_spec = pl.BlockSpec((FFL, HALF), lambda i, p: (0, i))
    turned_shape = shaped(FFL, 2 * HALF)
    return pl.pallas_call(
        feed_forward_kernel,
        grid_spec=pltpu.PrefetchScalarGridSpec(
            num_scalar_prefetch=1,
            grid=(2,),
            in_specs=[ANYWHERE] * 11,
            out_specs=[pl.BlockSpec((HALF, FFL), lambda i, p: (i, 0))]
            + [turned_spec] * 3
            + part_specs(1)
            + [ANYWHERE],
            scratch_shapes=[
                pltpu.VMEM((2 * HALF, D), BF16),
                pltpu.VMEM((2 * HALF, D), BF16),
                pltpu.VMEM((2, FFL, D), BF16),
                pltpu.VMEM((FFL, D), BF16),
                pltpu.VMEM((2, 8, FFL, B), BF16),
                pltpu.SemaphoreType.DMA((69,)),
            ],
        ),
        out_shape=[shaped(2 * HALF, FFL)] + [turned_shape] * 3 + PART_SHAPES + [shaped(FFL, D)],
        compiler_params=params("arbitrary"),
        cost_estimate=cost(2 * 5 * 2 * HALF * FFL * D, 32),
        name="feed_forward",
    )(place, *tokens, *grads, ff_all)


def along_z(place, zhi, zlo):
    return (2 * zhi + zlo + 4 - 2 * place[4] - place[0]) % 4


def load_tokens(step, refs, rows, sems):
    copies = put_tokens(refs, rows, sems, 0)

    @pl.when(step == 0)
    def _():
        for copy in copies:
            copy.start()
        for copy in copies:
            copy.wait()


def gate_up_kernel(*refs):
    place, token_refs, gate_t, up_t, out_ref, rows, terms, sems = refs[0], refs[1:6], *refs[6:]
    step = pl.program_id(0)
    load_tokens(step, token_refs, rows, sems)
    normed = rows[:, pl.ds(pl.multiple_of(step * 4 * B, 4 * B), 4 * B)]

    def out(i, matrix):
        xs, by = pl.ds(i % 2 * 2, 2), along_z(place, i // 2, matrix)
        return pltpu.make_async_copy(terms.at[xs, by], out_ref.at[xs, by], sems.at[10 + 2 * i + matrix])

    for matrix, left in ((0, gate_t), (1, up_t)):
        term = matmul(left[...], normed).astype(BF16)
        by = along_z(place, step // 2, matrix)
        for j in range(2):
            terms[step % 2 * 2 + j, by, 0:FFL, :] = term[:, 2 * j * B : (2 * j + 1) * B]
            terms[step % 2 * 2 + j, by, FFL:, :] = term[:, (2 * j + 1) * B : (2 * j + 2) * B]
        out(step, matrix).start()

    @pl.when(step == 3)
    def _():
        for i in range(4):
            for matrix in range(2):
                out(i, matrix).wait()


def down_kernel(*refs):
    place, grad_refs, act_t, out_ref, rows, terms, sems = refs[0], refs[1:6], *refs[6:]
    step = pl.program_id(0)
    load_tokens(step, grad_refs, rows, sems)
    term = matmul(act_t[...], rows[:, pl.ds(pl.multiple_of(step * 4 * B, 4 * B), 4 * B)])
    for j in range(2):
        p = (2 * step + j) % 4
        at = pl.ds(pl.multiple_of(p * 2 * PIECE, 16), 2 * PIECE)
        for zx in range(8):
            slab = term[zx * PIECE : (zx + 1) * PIECE]
            low, high = slab[:, 2 * j * B : (2 * j + 1) * B], slab[:, (2 * j + 1) * B : (2 * j + 2) * B]
            by = along_z(place, zx // 4, step // 2)
            terms[zx % 4, by, at, :] = jnp.concatenate([low, high], axis=0).astype(BF16)

    def out(half, zhi):
        by = along_z(place, zhi, half)
        return pltpu.make_async_copy(terms.at[:, by], out_ref.at[:, by], sems.at[10 + 2 * half + zhi])

    @pl.when(step % 2 == 1)
    def _():
        for zhi in range(2):
            out(step // 2, zhi).start()

    @pl.when(step == 3)
    def _():
        for half in range(2):
            for zhi in range(2):
                out(half, zhi).wait()


def ff_terms(kernel, place, pieces, lefts, rows, name):
    whole = pl.BlockSpec((FFL, 2 * HALF), lambda i, p: (0, 0))
    return pl.pallas_call(
        kernel,
        grid_spec=pltpu.PrefetchScalarGridSpec(
            num_scalar_prefetch=1,
            grid=(4,),
            in_specs=[ANYWHERE] * 5 + [whole] * len(lefts),
            out_specs=ANYWHERE,
            scratch_shapes=[
                pltpu.VMEM((2 * HALF, D), BF16),
                pltpu.VMEM((4, 4, rows, B), BF16),
                pltpu.SemaphoreType.DMA((18,)),
            ],
        ),
        out_shape=shaped(4, 4, rows, B),
        compiler_params=params("arbitrary"),
        cost_estimate=cost(2 * len(lefts) * 2 * HALF * FFL * D, 8 + 4 * len(lefts)),
        name=name,
    )(place, *pieces, *lefts)


def finish_hidden_kernel(*refs):
    place, piece_refs, weight_ref, gain_ref, out_ref, gain_out, rows = refs[0], refs[1:5], *refs[5:]
    for ref, by in zip(piece_refs, range(4)):
        at_y = (place[1] + by) % 4
        for core in range(2):
            slab = ref[0, core].astype(F32)
            for zx in range(8):
                at = pl.multiple_of((2 * zx + core) * 4 * PIECE + at_y * PIECE, 8)
                rows[pl.ds(at, PIECE)] = slab[zx * PIECE : (zx + 1) * PIECE]
    gain = gain_ref[...]
    total = jnp.zeros((B, 1), F32)
    for i in range(FF // B):
        lanes = slice(i * B, (i + 1) * B)
        block = rows[lanes].T
        total = total + jnp.sum(block * weight_ref[:, lanes].astype(F32), axis=1, keepdims=True)
        out_ref[:, lanes] = block * gain
    gain_out[...] = total


def finish_hidden(place, pieces, matrix, weight, gain):
    own, after, low, high, before = pieces
    at = lambda m: pl.BlockSpec((1, 2, FFL, B), lambda i, p: (m, 0, 0, 0))
    whole = lambda *shape: pl.BlockSpec(shape, lambda i, p: (0,) * len(shape))
    return pl.pallas_call(
        finish_hidden_kernel,
        grid_spec=pltpu.PrefetchScalarGridSpec(
            num_scalar_prefetch=1,
            grid=(1,),
            in_specs=[at(matrix), at(matrix), at(0), at(matrix), whole(B, FF), whole(B, 1)],
            out_specs=[whole(B, FF), whole(B, 1)],
            scratch_shapes=[pltpu.VMEM((FF, B), F32)],
        ),
        out_shape=[shaped(B, FF, kind=F32), shaped(B, 1, kind=F32)],
        compiler_params=params("arbitrary"),
        cost_estimate=cost(3 * 10**9, 6),
        name="finish_hidden",
    )(place, own, after, (low, high)[matrix], before, weight, gain)


def finish_down_kernel(place, own, after, low, high, before, out_ref):
    for refs, by in (((own, own), 0), ((after, after), 1), ((low, high), 2), ((before, before), 3)):
        rows = pl.ds(pl.multiple_of((place[1] + by) % 4 * PIECE, 8), PIECE)
        for half in range(2):
            slab = refs[half][half if by != 2 else 0].astype(F32)
            for t in range(8):
                lane = (half * 8 + t) * B
                out_ref[rows, lane : lane + B] = slab[t * PIECE : (t + 1) * PIECE]


def finish_down(place, pieces):
    halves = lambda n: pl.BlockSpec((n, FFL, B), lambda i, p: (0, 0, 0))
    return pl.pallas_call(
        finish_down_kernel,
        grid_spec=pltpu.PrefetchScalarGridSpec(
            num_scalar_prefetch=1,
            grid=(1,),
            in_specs=[halves(2), halves(2), halves(1), halves(1), halves(2)],
            out_specs=pl.BlockSpec((4 * PIECE, D), lambda i, p: (0, 0)),
        ),
        out_shape=shaped(4 * PIECE, D, kind=F32),
        compiler_params=params("arbitrary"),
        cost_estimate=cost(2 * 10**9, 5),
        name="finish_down",
    )(place, *pieces)


def own_rows(rows_all, y, core, per):
    return lax.dynamic_slice_in_dim(rows_all, (2 * y + core) * per, per, 0)


def resumed(steps, arrived):
    try:
        while True:
            arrived = yield steps.send(arrived)
    except StopIteration as end:
        return end.value


class Flow:
    def __init__(self, steps):
        self.steps, self.result, self.sent = steps, None, None
        self.move(None)

    def move(self, arrived):
        try:
            self.sent = self.steps.send(arrived)
        except StopIteration as end:
            self.sent, self.result = (), end.value


def stage(flows, *values):
    flows = [flow for flow in flows if flow.result is None]
    sizes = [len(flow.sent) for flow in flows]
    leaves, tree = jax.tree.flatten(values)
    tied = tie(*[v for flow in flows for v in flow.sent], *leaves)
    for flow, size in zip(flows, sizes):
        flow.move(tied[:size])
        tied = tied[size:]
    return jax.tree.unflatten(tree, tied)


def gather_steps(block):
    (other,) = yield (swap_core(block),)
    pair = jnp.stack([block, other])
    (got,) = yield (along_y(pair),)
    far, swapped = yield (along_y(send_half(got)), swap_core(got))
    (far_swapped,) = yield (swap_core(far),)
    return pair, got, swapped, far, far_swapped


def scatter_steps(parts, held=0):
    core = lax.axis_index("core")
    first, behind, ahead, far, far_other = parts
    (far_got,) = yield (swap_core(far_other),)
    far = add(far, far_got).astype(BF16)
    low, behind_got, first_got = yield (along_y(far), swap_core(behind), swap_core(first))
    ahead = add(ahead, behind_got).astype(BF16)
    mine = add(lax.dynamic_slice_in_dim(ahead, core * (B // 2), B // 2, 1), low).astype(BF16)
    ahead = lax.dynamic_update_slice_in_dim(ahead, mine, core * (B // 2), 1)
    for _ in range(held):
        yield ()
    (got,) = yield (along_y(ahead),)
    (last,) = yield (swap_core(got),)
    return add(first[0], first_got[1]) + add(got[0], last[1])


def ring_gather_steps(block, axis):
    half = block.shape[0] // 2
    before, after = yield (shift(block, axis, 1), shift(block, axis, -1))
    low, high = yield (shift(before[:half], axis, 1), shift(after[half:], axis, -1))
    return block, after, low, high, before


def ring_scatter_steps(parts, axis):
    half = parts[2].shape[0] // 2
    low, high = yield (shift(parts[2][:half], axis, 1), shift(parts[2][half:], axis, -1))
    after = jnp.concatenate([add(parts[1][:half], low).astype(BF16), parts[1][half:]], axis=0)
    before = jnp.concatenate([parts[3][:half], add(parts[3][half:], high).astype(BF16)], axis=0)
    from_before, from_after = yield (shift(after, axis, 1), shift(before, axis, -1))
    return add(parts[0], from_before) + from_after.astype(F32)


def on_device(
    layer_input,
    positions,
    attn_gain,
    w_query,
    w_key,
    w_value,
    w_output,
    mlp_gain,
    w_gate,
    w_up,
    w_down,
    out_grad,
):
    zlo, y, zhi, x, core = (lax.axis_index(axis) for axis in AXES)
    place = jnp.stack([zlo, y, core, x, zhi]).astype(jnp.int32)

    def by_core(mine, got):
        return jnp.where(core == 0, jnp.stack([mine, got]), jnp.stack([got, mine]))

    def by_zlo(mine, got):
        return jnp.where(zlo == 0, jnp.stack([mine, got]), jnp.stack([got, mine]))

    def by_zhi(mine, got):
        return jnp.where(zhi == 0, jnp.stack([mine, got]), jnp.stack([got, mine]))

    def trio(mine, other, axis):
        across = lax.ppermute(other, (axis, "core"), [(i, 3 - i) for i in range(4)])
        return shift(mine, axis, 1), swap_core(other), across

    def column_steps(mine, got):
        pair = by_core(mine, got)
        (got,) = yield (shift(pair, "zhi", 1),)
        return (yield from ring_gather_steps(by_zhi(pair, got), "x"))

    def output_steps(mine, other):
        there, here, across = yield trio(mine, other, "zhi")
        column = by_zhi(by_core(mine, here), by_core(there, across))
        return (yield from ring_gather_steps(column, "x"))

    def hidden_steps(mine, got, down):
        piece = jnp.concatenate([by_core(mine, got).reshape(2 * FFL, B), down], axis=0)
        pieces = yield from ring_gather_steps(piece, "z")
        return jnp.concatenate(pieces, axis=0).reshape(4, 3 * FFL, B)

    def of_core(pair, other=False):
        return lax.dynamic_index_in_dim(pair, 1 - core if other else core, 0, keepdims=False)

    def whole_ring(pieces):
        own, after, low, high, before = pieces
        return own, after, jnp.concatenate([low, high], axis=0), before

    def attention_steps(column):
        keep = lax.dynamic_index_in_dim(column, zhi, 0, keepdims=False)
        send = lax.dynamic_index_in_dim(column, 1 - zhi, 0, keepdims=False)
        (got,) = yield (shift(send, "zhi", 1),)
        pair = add(keep, got).astype(BF16)
        mine, other = of_core(pair), of_core(pair, True)
        there, here, across = yield trio(mine, other, "zlo")
        own = by_core(add(mine, there), add(here, across)).astype(BF16)
        return (yield from ring_gather_steps(own, "y"))

    def gate_up_steps(sums):
        own = yield from ring_scatter_steps([sums[i] for i in range(4)], "z")
        pair = own.astype(BF16).reshape(2, FFL, B)
        mine, other = of_core(pair), of_core(pair, True)
        there, here, across = yield trio(mine, other, "zlo")
        block = by_zlo(by_core(mine, here), by_core(there, across))
        before, after = yield (shift(block, "y", 1), shift(block, "y", -1))
        low, high = yield (shift(before[:1], "y", 1), shift(after[1:], "y", -1))
        return block, after, low, high, before

    def down_steps(sums):
        steps = ring_scatter_steps([sums[i] for i in range(4)], "z")
        arrived = yield next(steps)
        yield ()
        own = yield from resumed(steps, arrived)
        own = own.astype(BF16)
        (got,) = yield (shift(own, "zlo", 1),)
        return (yield from ring_gather_steps(by_zlo(own, got), "y"))

    x_low = layer_input[0]
    frequency = theta ** (-jnp.arange(0, HD, 2).astype(F32) / HD)
    angles = positions[0].astype(F32)[:, None] * frequency
    tables = []
    for table in (jnp.cos(angles), jnp.sin(angles)):
        high = lax.reduce_precision(table, 8, 7)
        tables += [high.astype(BF16), (table - high).astype(BF16)]
    tokens = Flow(gather_steps(jnp.concatenate([x_low, *tables], axis=1)))
    grads = Flow(gather_steps(out_grad[0]))
    qkv_mine, qkv_other = prepare_qkv(place, w_query, w_key, w_value, attn_gain[:, None])
    qkv_mine, qkv_got, gain_two, w_out = stage([tokens], qkv_mine, swap_core(qkv_other), mlp_gain[:, None], w_output)

    columns = Flow(column_steps(qkv_mine, qkv_got))
    o_rows = lax.all_to_all(w_out.reshape(B, 16, B).transpose(1, 0, 2), FSDP, 0, 0, tiled=True)
    ff_mine, ff_other, ff_down = prepare_ff(place, w_gate, w_up, w_down, gain_two)
    ff_mine, ff_got, ff_down, x_low, o_rows = stage(
        [tokens, columns], ff_mine, swap_core(ff_other), ff_down, x_low, o_rows
    )

    inputs = x_low.astype(F32)
    scale_one = lax.rsqrt(jnp.mean(inputs * inputs, axis=-1, keepdims=True) + eps)
    o_rows = o_rows.reshape(D, B)
    mine, other = own_rows(o_rows, y, core, HEADS * HD), own_rows(o_rows, y, 1 - core, HEADS * HD)
    scale_one, mine, other, ff_mine, ff_got, ff_down = stage(
        [tokens, columns, grads], scale_one, mine, other, ff_mine, ff_got, ff_down
    )

    outputs = Flow(output_steps(mine, other))
    ff_mine, ff_got, ff_down = stage([tokens, columns, outputs], ff_mine, ff_got, ff_down)

    hidden_rows = Flow(hidden_steps(ff_mine, ff_got, ff_down))
    x_pieces = tokens.result
    query, key_value, scale_all, cosine, sine, qkv_full = project_qkv(place, x_pieces, columns.result)
    query, key_value = stage([hidden_rows, outputs, grads], query, key_value)

    earlier = lax.ppermute(key_value, "zlo", [(0, 1)])
    query, key_value, earlier = stage([outputs, hidden_rows], query, key_value, earlier)
    ff_all = lax.all_gather(hidden_rows.result, "x", axis=0, tiled=False)

    key_value = jnp.concatenate([earlier, key_value], axis=1)
    mixed, log_total, *parts, o_full = attention(place, outputs.result, query, key_value)
    parts = stage([grads], *parts)
    sums = Flow(scatter_steps(parts))
    stage([sums, grads])
    grad_pieces = grads.result
    for _ in range(3):
        stage([sums])
    hidden = inputs + sums.result
    scale_two = lax.rsqrt(jnp.mean(hidden * hidden, axis=-1, keepdims=True) + eps)
    normed = Flow(gather_steps((hidden * scale_two).astype(BF16)))
    for _ in range(4):
        stage([normed])
    normed_pieces = normed.result

    activation, act_t, gate_t, up_t, *parts, down_full = feed_forward(place, normed_pieces, grad_pieces, ff_all)
    sums = Flow(scatter_steps(parts))
    (act_t,) = stage([sums], act_t)
    down_terms = ff_terms(down_kernel, place, grad_pieces, (act_t,), FFL, "down_terms")
    down_terms, gate_t = stage([sums], down_terms, gate_t)
    down_sum = lax.psum_scatter(down_terms, "x", scatter_dimension=0, tiled=True)[0]
    gate_up_terms = ff_terms(gate_up_kernel, place, normed_pieces, (gate_t, up_t), 2 * FFL, "gate_up_terms")
    (gate_up_terms,) = stage([sums], gate_up_terms)
    gate_up_sum = lax.psum_scatter(gate_up_terms, "x", scatter_dimension=0, tiled=True)[0]
    stage([sums])

    grad_normed_two = sums.result
    mean_two = jnp.mean(grad_normed_two * hidden, axis=-1, keepdims=True)
    grad_hidden = (
        out_grad[0].astype(F32)
        + scale_two * grad_normed_two
        - hidden * (scale_two * scale_two * scale_two) * mean_two
    )
    hidden_grads = Flow(gather_steps(grad_hidden.astype(BF16)))
    (activation,) = stage([hidden_grads], activation)
    down_parts = project(activation, down_full)
    *down_parts, down_sum = stage([hidden_grads], *down_parts, down_sum)
    result = Flow(scatter_steps(down_parts))
    down = Flow(down_steps(down_sum))
    stage([hidden_grads, down])
    stage([hidden_grads, result])

    hidden_grad_pieces = hidden_grads.result
    grad_query, grad_earlier, grad_own = attention_back(
        place, hidden_grad_pieces, query, key_value, log_total, o_full
    )
    grad_query, grad_earlier, grad_own, mixed = stage([result, down], grad_query, grad_earlier, grad_own, mixed)

    later = lax.ppermute(grad_earlier, "zlo", [(1, 0)])
    output_terms = attention_terms(
        place, hidden_grad_pieces, mixed.reshape(2 * HALF, HEADS * HD), "output_terms"
    )
    later, grad_query, output_terms, gate_up_sum = stage(
        [down], later, grad_query, output_terms, gate_up_sum
    )

    output_sum = lax.psum_scatter(output_terms, "x", scatter_dimension=0, tiled=True)[0]
    gate_up = Flow(gate_up_steps(gate_up_sum))
    grad_pre, terms = qkv_back(place, x_pieces, grad_query, grad_own, later, cosine, sine, scale_all)
    grad_pre, terms = stage([gate_up, down, result], grad_pre, terms)

    attention_sum = lax.psum_scatter(terms, "x", scatter_dimension=0, tiled=True)[0]
    parts = project(grad_pre, qkv_full)
    *parts, output_sum = stage([gate_up, down, result], *parts, output_sum)

    sums = Flow(scatter_steps(parts, 2))
    output_sums = Flow(attention_steps(output_sum))
    (attention_sum,) = stage([sums, gate_up, output_sums, down], attention_sum)
    attention_sums = Flow(attention_steps(attention_sum))
    down_pieces = stage([sums, output_sums, attention_sums], *down.result)
    down_grad = finish_down(place, down_pieces)
    layer_output = (hidden + result.result).astype(BF16)
    down_grad, layer_output = stage([sums, output_sums, attention_sums, gate_up], down_grad, layer_output)
    stage([sums, output_sums, attention_sums, gate_up])

    ring = jnp.roll(jnp.stack(whole_ring(output_sums.result)), y, axis=0).reshape(16, B, B)
    output_grad = lax.all_to_all(ring, FSDP, 0, 0, tiled=True)
    gain_two = mlp_gain[:, None]
    gate_grad, gate_gain = finish_hidden(place, gate_up.result, 0, w_gate, gain_two)
    up_grad, up_gain = finish_hidden(place, gate_up.result, 1, w_up, gain_two)
    gate_grad, up_grad, output_grad = stage([sums, attention_sums], gate_grad, up_grad, output_grad)
    stage([sums])
    grad_normed = sums.result
    mean_one = jnp.mean(grad_normed * inputs, axis=-1, keepdims=True)
    input_grad = (
        grad_hidden
        + scale_one * grad_normed
        - inputs * (scale_one * scale_one * scale_one) * mean_one
    )
    input_grad = input_grad.astype(BF16)
    query_grad, key_grad, value_grad, attn_gain_grad = finish_attention(
        place, whole_ring(attention_sums.result), w_query, w_key, w_value, attn_gain[:, None]
    )
    output_grad = finish_output(output_grad)
    return (
        layer_output[None],
        input_grad[None],
        attn_gain_grad[:, 0],
        query_grad,
        key_grad,
        value_grad,
        output_grad,
        (gate_gain + up_gain)[:, 0],
        gate_grad,
        up_grad,
        down_grad,
    )


def solution(mesh):
    split = Mesh(mesh.devices.reshape(2, 4, 2, 4, 2), AXES)
    tokens = P(FSDP, SEQ, None)
    rows = P(FSDP, None)
    gain = P(FSDP)
    in_specs = (
        tokens, P(FSDP, SEQ), gain, rows, rows, rows, rows, gain, rows, rows, rows, tokens,
    )
    out_specs = (tokens, tokens, gain, rows, rows, rows, rows, gain, rows, rows, rows)
    return jax.shard_map(
        on_device, mesh=split, in_specs=in_specs, out_specs=out_specs, check_vma=False
    )
```
